32 devices in a mesh: groups: 2 (over y), lon: 16 (over z, x, core).
Axes of the slice: x: 2, y: 2, z: 4, core: 2. Of those that a mesh axis runs over, the one named last changes fastest.
Arguments:
- right_side: float32 [2048, 8192], P(('groups', 'lon')), parts along dimension 0, may hold values from -6 to 6
- texel_weight: bfloat16 [2048, 8192], P(('groups', 'lon')), parts along dimension 0, may hold values from 0.049804688 to 2
- seam_flags: int32 [64, 256], P(('groups', 'lon')), parts along dimension 0, may hold values 0 or 1
Outputs:
- fine_residual: float32 [2048, 8192], P(('groups', 'lon')), parts along dimension 0
- coarse_solution: float32 [512, 2048], P(('groups', 'lon')), parts along dimension 0
- coarse_residual: float32 [512, 2048], P(('groups', 'lon')), parts along dimension 0
The draws below stay inside these ranges and needn't reach their ends.
There are 2 independent parts, one for each index of `groups`. The reference program is written for one: setup_inputs(seed, part) draws one part's arguments, and reference() takes and returns one part's arrays. A program takes and returns all parts, laid end to end along the dimension named above; each array names one. Nothing has to cross between parts.
Inputs may be any that keep to these rules, and one draw needn't show every extreme that they name: `seam_flags`: 1 marks a seam tile, 0 any other tile.
All inputs are finite; a program needn't handle non-finite values. No bound on the sum of `seam_flags` on one device may be relied on, other than what follows from the above.
Results may differ from the reference program's by a relative error of at most 0.0003.
Values sent between devices are 32-bit elements; how exact they have to be, the bound alone decides.
No kernel may reach another device: no remote copies, remote signals or barrier semaphores. Data moves between devices by JAX's collectives and lax.ppermute only.
A program may use at most 128 MiB of HBM per device.

```python
import math
import jax
import jax.numpy as jnp
from jax import lax

NLAT = 8192
TILE = 32
NU = 2
NLON = 1024


def place_ends(result, key, low, largest):
    shape = result.shape
    spot = [jax.random.randint(jax.random.fold_in(key, axis), (), 0, shape[axis]) for axis in range(len(shape))]
    result = result.at[tuple(spot)].set(low)
    longest = shape.index(max(shape))
    spot[longest] = (spot[longest] + 1) % shape[longest]
    return result.at[tuple(spot)].set(largest)


def levels(key, shape, pieces, smallest, top_value):
    gain, own = 1.0, jax.random.fold_in(key, 6)
    for dim, shards_of in pieces:
        draws = jnp.exp(jax.random.uniform(jax.random.fold_in(own, dim), (shards_of,), jnp.float32, smallest / len(pieces), top_value / len(pieces)))
        gain = gain * jnp.repeat(draws, shape[dim] // shards_of).reshape([-1 if axis == dim else 1 for axis in range(len(shape))])
    return gain


def bell_draw(stream_key, shape, width, most, cuts=(), kind=jnp.bfloat16):
    factor_of = levels(stream_key, shape, cuts, -0.22, 0.18) if cuts else 1.0
    result = jax.random.normal(stream_key, shape, jnp.float32) * width * factor_of
    return jnp.minimum(jnp.maximum(result, -most), most).astype(kind)


def setup_inputs(seed: int = 0, part: int = 0) -> dict:
    key_list = jax.random.split(jax.random.key(seed), 4)
    own_keys = jax.random.split(jax.random.fold_in(key_list[3], part), 4)
    right_side = bell_draw(own_keys[0], (NLON, NLAT), 1.0, 6.0, ((0, 16),), jnp.float32)
    texel_weight = jnp.clip(jnp.exp(math.log(2.0) - 3.6927934 * jax.random.uniform(own_keys[1], (NLON, NLAT), jnp.float32) ** levels(own_keys[1], (NLON, NLAT), ((0, 16),), -0.2, 0.2)), 0.049804688, 2.0).astype(jnp.bfloat16)
    seam_flags = place_ends((jax.random.randint(own_keys[2], (NLON // TILE, NLAT // TILE), 0, 3) < 1).astype(jnp.int32), jax.random.fold_in(own_keys[2], 1), 0, 1)
    return {"right_side": right_side, "texel_weight": texel_weight, "seam_flags": seam_flags}


seam_scale = 0.1


def colour_mask(lon_count, lat_count, lon_start, lat_start):
    lon_ids = lon_start + lax.iota(jnp.int32, lon_count)
    lat_ids = lat_start + lax.iota(jnp.int32, lat_count)
    return (lon_ids[:, None] + lat_ids[None, :]) % 2 == 0


def polar_pair(field):
    half_turn = field.shape[0] // 2
    return jnp.roll(field[:, :1], half_turn, 0), jnp.roll(field[:, -1:], half_turn, 0)


def sides(field):
    height = field.shape[1]
    lat_ids = lax.iota(jnp.int32, height)[None, :]
    north_pole, south_pole = polar_pair(field)
    north = jnp.where(lat_ids == 0, north_pole, jnp.roll(field, 1, 1))
    south = jnp.where(lat_ids == height - 1, south_pole, jnp.roll(field, -1, 1))
    return jnp.roll(field, 1, 0), jnp.roll(field, -1, 0), north, south


def relax_colour(field, parts, source, screen, update_mask):
    beside_all = (parts[0] + parts[1]) + (parts[2] + parts[3])
    return jnp.where(update_mask, (source + beside_all) / (4.0 + screen), field)


def residual_of(field, parts, source, screen):
    beside_all = (parts[0] + parts[1]) + (parts[2] + parts[3])
    return source - ((4.0 + screen) * field - beside_all)


def restrict(field):
    height = field.shape[1]
    lat_ids = lax.iota(jnp.int32, height)[None, :]
    north_pole, south_pole = polar_pair(field)
    north = jnp.where(lat_ids == 0, north_pole, jnp.roll(field, 1, 1))
    south = jnp.where(lat_ids == height - 1, south_pole, jnp.roll(field, -1, 1))
    twice = jnp.where(lat_ids == height - 2, south_pole, jnp.roll(field, -2, 1))
    lat_sum = north + 3.0 * field + 3.0 * south + twice
    halved = lat_sum[:, 0::2]
    lon_sum = jnp.roll(halved, 1, 0)[0::2] + 3.0 * halved[0::2] + 3.0 * halved[1::2] + jnp.roll(halved, -1, 0)[1::2]
    return lon_sum / 16.0


def coarsen(screen):
    paired = screen + jnp.roll(screen, -1, 1)
    paired = paired[:, 0::2]
    return paired[0::2] + paired[1::2]


def smooth(source, screen, red_cells):
    black_cells = jnp.logical_not(red_cells)
    field = jnp.where(red_cells, source / (4.0 + screen), 0.0)
    field = relax_colour(field, sides(field), source, screen, black_cells)
    for sweep_index in range(1, NU):
        field = relax_colour(field, sides(field), source, screen, red_cells)
        field = relax_colour(field, sides(field), source, screen, black_cells)
    return field


def reference(right_side, texel_weight, seam_flags):
    tile_flags = jnp.repeat(jnp.repeat(seam_flags, TILE, 0), TILE, 1)
    screen = texel_weight.astype(jnp.float32) * jnp.where(tile_flags == 1, seam_scale, 1.0)
    source = right_side
    fine_residual = source
    for depth_level in range(3):
        red_cells = colour_mask(source.shape[0], source.shape[1], 0, 0)
        field = smooth(source, screen, red_cells)
        misfit = residual_of(field, sides(field), source, screen)
        if depth_level == 0:
            fine_residual = misfit
        if depth_level < 2:
            source = restrict(misfit)
            screen = coarsen(screen)
    return fine_residual, field, misfit
```

```python
import functools

import jax
import jax.numpy as jnp
from jax import lax
from jax.experimental import pallas as pl
from jax.experimental.pallas import tpu as pltpu
from jax.sharding import PartitionSpec as P

TILE = 32
SEAM_SCALE = 0.1
LANES = 128
F32 = jnp.float32
BF16 = jnp.bfloat16


def lane_ids(rows):
    return lax.broadcasted_iota(jnp.int32, (rows, LANES), 1)


def row_ids(rows):
    return lax.broadcasted_iota(jnp.int32, (rows, LANES), 0)


def roll_up(x):
    return pltpu.roll(x, 1, 1)


def roll_down(x):
    return pltpu.roll(x, LANES - 1, 1)


def col_prev(x):
    return pltpu.roll(x, 1, 0)


def col_next(x):
    return pltpu.roll(x, x.shape[0] - 1, 0)


def splitter():
    a = lax.broadcasted_iota(jnp.int32, (256, 256), 0)
    b = lax.broadcasted_iota(jnp.int32, (256, 256), 1)
    return jnp.where(a == 2 * (b % LANES) + b // LANES, 1.0, 0.0).astype(BF16)


def merger():
    a = lax.broadcasted_iota(jnp.int32, (256, 256), 0)
    b = lax.broadcasted_iota(jnp.int32, (256, 256), 1)
    return jnp.where(b == 2 * (a % LANES) + a // LANES, 1.0, 0.0).astype(BF16)


def virtual_splitter():
    a = lax.broadcasted_iota(jnp.int32, (LANES, 256), 0)
    b = lax.broadcasted_iota(jnp.int32, (LANES, 256), 1)
    place = a // 2 + jnp.where(a >= 64, 64, 0) + LANES * (a % 2)
    return jnp.where(place == b, 1.0, 0.0).astype(BF16)


def moved(x, matrix):
    high = x.astype(BF16)
    low = (x - high.astype(F32)).astype(BF16)
    return jnp.dot(high, matrix, preferred_element_type=F32) + jnp.dot(
        low, matrix, preferred_element_type=F32
    )


def quarters_of(parts, temp):
    count = parts.shape[0] // 2
    temp[0] = parts[:, :LANES]
    temp[1] = parts[:, LANES:]
    return [temp[pr, pl.ds(pc, count, 2), :] for pc in (0, 1) for pr in (0, 1)]


def prepare_kernel(
    right_ref, weight_ref, flag_ref,
    s_ref, d_ref, low_ref, high_ref, to_left, to_right, polar_ref, corner_low, corner_high,
    temp_s, temp_d, scale_ref,
):
    tiles, rows = s_ref.shape[1], s_ref.shape[2]
    flag_cols = flag_ref.shape[0]
    flag_lats = flag_ref.shape[1]
    per_tile = rows // flag_cols
    matrix = splitter()
    flags = jnp.concatenate(
        [flag_ref[...].astype(F32), jnp.zeros((8 - flag_cols, flag_lats), F32)], 0
    )
    lat = lax.broadcasted_iota(jnp.int32, (8, flag_lats), 1)
    stacked = jnp.concatenate(
        [jnp.where(lat // 8 == c, flags, 0.0) for c in range(tiles)], 0
    ).astype(BF16)
    a = lax.broadcasted_iota(jnp.int32, (flag_lats, LANES), 0)
    b = lax.broadcasted_iota(jnp.int32, (flag_lats, LANES), 1)
    spread = jnp.where(a % 8 == b // (TILE // 2), 1.0, 0.0).astype(BF16)
    spread_flags = jnp.dot(stacked, spread, preferred_element_type=F32)
    scale_ref[...] = jnp.where(spread_flags > 0.5, SEAM_SCALE, 1.0).reshape(tiles, 8, LANES)

    sub = row_ids(8)

    def edge(group, first, shift_of):
        packed = group[0] if shift_of(0) == 0 else pltpu.roll(group[0], shift_of(0), 0)
        for q in range(1, 4):
            shift = shift_of(q) % 8
            moved_q = group[q] if shift == 0 else pltpu.roll(group[q], shift, 0)
            packed = jnp.where(sub // 2 == q, moved_q, packed)
        return packed

    def body(c, _):
        where = pl.ds(pl.multiple_of(c * 256, 256), 256)
        source = quarters_of(moved(right_ref[:, where], matrix), temp_s)
        weight = quarters_of(
            jnp.dot(weight_ref[:, where], matrix, preferred_element_type=F32), temp_d
        )
        scales = scale_ref[c]
        scale = jnp.concatenate(
            [jnp.broadcast_to(scales[i : i + 1], (per_tile, LANES)) for i in range(flag_cols)], 0
        )
        screen = [w * scale for w in weight]
        coarse = (screen[0] + screen[1]) + (screen[2] + screen[3])
        half = rows // 2
        low_ref[c] = coarse[:half]
        high_ref[c] = coarse[half:]
        diag = [4.0 + s for s in screen]
        for q in range(4):
            s_ref[q, c] = source[q]
            d_ref[q, c] = diag[q]
        gs = [x[rows - 8 :] for x in source]
        gd = [x[rows - 8 :] for x in diag]
        first = pltpu.roll(gs[0] / gd[0], 2, 0)
        second = pltpu.roll(gs[3] / gd[3], 3, 0)
        to_right[0, c] = jnp.where(sub == 0, first, edge(gs, 0, lambda q: 2 * q + 2))
        to_right[1, c] = jnp.where(sub == 0, second, edge(gd, 0, lambda q: 2 * q + 2))
        gs = [x[:8] for x in source]
        gd = [x[:8] for x in diag]
        first = pltpu.roll(gs[3] / gd[3], 6, 0)
        second = pltpu.roll(gs[0] / gd[0], 5, 0)
        to_left[0, c] = jnp.where(sub == 7, first, edge(gs, 0, lambda q: 2 * q))
        to_left[1, c] = jnp.where(sub == 7, second, edge(gd, 0, lambda q: 2 * q))
        return 0

    lax.fori_loop(0, tiles, body, 0)

    a = lax.broadcasted_iota(jnp.int32, (LANES, LANES), 0)
    b = lax.broadcasted_iota(jnp.int32, (LANES, LANES), 1)
    mirror = jnp.where(a + b == LANES - 1, 1.0, 0.0).astype(BF16)
    lane = lane_ids(rows)
    for pc in (0, 1):
        for pr in (0, 1):
            q, from_q = 2 * pc + pr, 2 * pc + 1 - pr
            both = jnp.where(lane >= 64, s_ref[from_q, tiles - 1], s_ref[from_q, 0])
            diag = jnp.where(lane >= 64, d_ref[from_q, tiles - 1], d_ref[from_q, 0])
            both = jnp.where((lane >= 32) & (lane < 96), pltpu.roll(diag, 64, 1), both)
            both = moved(both, mirror)
            polar_ref[q] = both
            corner_low[q] = both[: rows // 2]
            corner_high[q] = both[rows // 2 :]


def inverse_kernel(d_ref, i_ref):
    def body(t, _):
        for q in range(4):
            i_ref[q, t] = 1.0 / d_ref[q, t]
        return 0

    lax.fori_loop(0, d_ref.shape[1], body, 0)


def half_sweep(v, load_s, load_i, tiles, red):
    rows = v.shape[2]
    lane = lane_ids(rows)
    y, z, qa, qb = (1, 2, 0, 3) if red else (3, 0, 2, 1)
    col_a, col_b = (col_prev, col_next) if red else (col_next, col_prev)

    def beside_virtual(q):
        ns, we = q ^ 1, q ^ 2
        here = v[ns, tiles]
        if q % 2 == 0:
            lat = jnp.where(lane == 0, roll_up(v[ns, tiles - 1]), roll_up(here))
        else:
            lat = jnp.where(lane == LANES - 1, roll_down(v[ns, 0]), roll_down(here))
        cols = v[we, tiles]
        return (here + lat) + (cols + (col_prev if q < 2 else col_next)(cols))

    held = [
        (q, (load_s(q, tiles) + beside_virtual(q)) * load_i(q, tiles)) for q in (y, z)
    ]

    def body(t, carry):
        y_before, z_here = carry
        vy, vz = v[y, t], v[z, t]
        y_here = roll_up(vy)
        z_after = roll_down(v[z, t + 1])
        lat_a = vy + jnp.where(lane == 0, y_before, y_here)
        lat_b = vz + jnp.where(lane == LANES - 1, z_after, z_here)
        v[qa, t] = (load_s(qa, t) + (lat_a + (vz + col_a(vz)))) * load_i(qa, t)
        v[qb, t] = (load_s(qb, t) + (lat_b + (vy + col_b(vy)))) * load_i(qb, t)
        return y_here, z_after

    lax.fori_loop(0, tiles, body, (roll_up(v[y, tiles]), roll_down(v[z, 0])))
    for q, value in held:
        v[q, tiles] = value


def smooth(v, load_s, load_i, tiles):
    rows = v.shape[2]
    zeros = jnp.zeros((rows, LANES), F32)

    def first(t, _):
        for q in (0, 3):
            v[q, t] = load_s(q, t) * load_i(q, t)
        return 0

    lax.fori_loop(0, tiles, first, 0)
    for q in (1, 2):
        v[q, 0] = zeros
        v[q, tiles - 1] = zeros
        v[q, tiles] = load_s(q, tiles) * load_i(q, tiles)
        v[3 * (q - 1), tiles] = zeros
    half_sweep(v, load_s, load_i, tiles, False)
    half_sweep(v, load_s, load_i, tiles, True)
    half_sweep(v, load_s, load_i, tiles, False)


def residual_and_columns(v, load_s, load_d, tiles, c_ref, keep):
    rows = v.shape[2]
    lane = lane_ids(rows)

    def body(t, _):
        before = jnp.where(t == 0, tiles, t - 1)
        after = jnp.where(t == tiles, 0, t + 1)
        x = [v[q, t] for q in range(4)]

        def north(q):
            return jnp.where(lane == 0, roll_up(v[q, before]), roll_up(x[q]))

        def south(q):
            return jnp.where(lane == LANES - 1, roll_down(v[q, after]), roll_down(x[q]))

        beside = [
            (x[1] + north(1)) + (x[2] + col_prev(x[2])),
            (x[0] + south(0)) + (x[3] + col_prev(x[3])),
            (x[3] + north(3)) + (x[0] + col_next(x[0])),
            (x[2] + south(2)) + (x[1] + col_next(x[1])),
        ]
        r = [load_s(q, t) - (load_d(q, t) * x[q] - beside[q]) for q in range(4)]
        keep(t, r)
        c_ref[0, t] = (col_prev(r[2]) + col_next(r[0])) + 3.0 * (r[0] + r[2])
        c_ref[1, t] = (col_prev(r[3]) + col_next(r[1])) + 3.0 * (r[1] + r[3])
        return 0

    lax.fori_loop(0, tiles + 1, body, 0)


def restricted(c_ref, t, tiles):
    lane = lane_ids(c_ref.shape[2])
    before = jnp.where(t == 0, tiles, t - 1)
    after = jnp.where(t == tiles, 0, t + 1)
    c0, c1 = c_ref[0, t], c_ref[1, t]
    north = jnp.where(lane == 0, roll_up(c_ref[1, before]), roll_up(c1))
    south = jnp.where(lane == LANES - 1, roll_down(c_ref[0, after]), roll_down(c0))
    return ((north + south) + 3.0 * (c0 + c1)) * (1.0 / 16.0)


def fine_kernel(
    s_ref, d_ref, i_ref, from_left, from_right, polar_ref, corner_left, corner_right,
    r_ref, low_ref, high_ref, screen_virtual,
    v, c_ref, hs, hd, hi, ps, pd, pi,
):
    tiles, rows = s_ref.shape[1], s_ref.shape[2]
    sub = row_ids(8)

    def rolled(x, shift):
        return x if shift % 8 == 0 else pltpu.roll(x, shift % 8, 0)

    def halo(t, _):
        al, bl, ar, br = from_left[0, t], from_left[1, t], from_right[0, t], from_right[1, t]
        for q in range(4):
            source = jnp.where(
                sub >= 6, rolled(al, 6 - 2 * q), jnp.where(sub <= 1, rolled(ar, -2 * q), 0.0)
            )
            diag = jnp.where(
                sub >= 6, rolled(bl, 6 - 2 * q), jnp.where(sub <= 1, rolled(br, -2 * q), 4.0)
            )
            if q == 0:
                source = jnp.where(sub == 2, rolled(br, 3), source)
                diag = jnp.where((sub == 2) | (sub == 6), 1.0, diag)
            if q == 3:
                source = jnp.where(sub == 5, rolled(bl, 5), source)
                diag = jnp.where((sub == 5) | (sub == 1), 1.0, diag)
            hs[q, t] = source
            hd[q, t] = diag
            hi[q, t] = 1.0 / diag
        return 0

    lax.fori_loop(0, tiles, halo, 0)

    def unpacked(x):
        lane = lane_ids(x.shape[0])
        used = (lane < 32) | (lane >= 96)
        return jnp.where(used, x, 0.0), jnp.where(used, pltpu.roll(x, 64, 1), 4.0)

    half = rows // 2
    totals = [0.0, 0.0, 0.0]
    for q in range(4):
        left_s, left_d = unpacked(corner_left[q])
        own_s, own_d = unpacked(polar_ref[q])
        right_s, right_d = unpacked(corner_right[q])
        totals = [totals[0] + left_d, totals[1] + own_d, totals[2] + right_d]
        ps[q] = own_s
        pd[q] = own_d
        pi[q] = 1.0 / own_d
        source = jnp.where(sub >= 5, left_s[half - 8 :], jnp.where(sub <= 2, right_s[:8], 0.0))
        diag = jnp.where(sub >= 5, left_d[half - 8 :], jnp.where(sub <= 2, right_d[:8], 4.0))
        hs[q, tiles] = source
        hd[q, tiles] = diag
        hi[q, tiles] = 1.0 / diag
    screen_virtual[:half] = totals[0] - 16.0
    screen_virtual[half : half + rows] = totals[1] - 16.0
    screen_virtual[half + rows :] = totals[2] - 16.0

    def loader(own, halo_ref, virtual):
        def load(q, t):
            if isinstance(t, int) and t == tiles:
                return jnp.concatenate([virtual[q], halo_ref[q, t]], 0)
            return jnp.concatenate([own[q, t], halo_ref[q, t]], 0)

        return load

    smooth(v, loader(s_ref, hs, ps), loader(i_ref, hi, pi), tiles)

    def residual(t, before, after, own_s, own_d):
        lane = lane_ids(v.shape[2])
        x = [v[q, t] for q in range(4)]

        def north(q):
            return jnp.where(lane == 0, roll_up(v[q, before]), roll_up(x[q]))

        def south(q):
            return jnp.where(lane == LANES - 1, roll_down(v[q, after]), roll_down(x[q]))

        beside = [
            (x[1] + north(1)) + (x[2] + col_prev(x[2])),
            (x[0] + south(0)) + (x[3] + col_prev(x[3])),
            (x[3] + north(3)) + (x[0] + col_next(x[0])),
            (x[2] + south(2)) + (x[1] + col_next(x[1])),
        ]
        r = [
            jnp.concatenate([own_s[q], hs[q, t]], 0)
            - (jnp.concatenate([own_d[q], hd[q, t]], 0) * x[q] - beside[q])
            for q in range(4)
        ]
        c_ref[0, t] = (col_prev(r[2]) + col_next(r[0])) + 3.0 * (r[0] + r[2])
        c_ref[1, t] = (col_prev(r[3]) + col_next(r[1])) + 3.0 * (r[1] + r[3])
        return r

    def main(t, _):
        before = jnp.where(t == 0, tiles, t - 1)
        r = residual(
            t, before, t + 1, [s_ref[q, t] for q in range(4)], [d_ref[q, t] for q in range(4)]
        )
        for q in range(4):
            r_ref[q, t] = r[q][:rows]
        return 0

    lax.fori_loop(0, tiles, main, 0)
    residual(tiles, tiles - 1, 0, [ps[q] for q in range(4)], [pd[q] for q in range(4)])

    def coarse(t, _):
        value = restricted(c_ref, t, tiles)
        low_ref[t] = value[:half]
        high_ref[t] = value[half:rows]
        return 0

    lax.fori_loop(0, tiles + 1, coarse, 0)


def merge_kernel(r_ref, out_ref, temp):
    tiles = r_ref.shape[1]
    rows = r_ref.shape[2]
    matrix = merger()

    def body(c, _):
        for pr in (0, 1):
            for pc in (0, 1):
                temp[pr, pl.ds(pc, rows, 2), :] = r_ref[2 * pc + pr, c]
        both = jnp.concatenate([temp[0], temp[1]], 1)
        out_ref[:, pl.ds(pl.multiple_of(c * 256, 256), 256)] = moved(both, matrix)
        return 0

    lax.fori_loop(0, tiles, body, 0)


def coarse_kernel(
    s_left, s_low, s_high, s_right, e_left, e_low, e_high, e_right, e_virtual,
    solution_ref, residual_ref,
    s, d, inv, v, c_ref, temp, s2, d2, i2, v2,
):
    tiles = s.shape[1] - 1
    rows = s.shape[2]
    matrix = splitter()

    def fill(t, source, screen):
        for q, value in enumerate(source):
            s[q, t] = value
        for q, value in enumerate(screen):
            diag = 4.0 + value
            d[q, t] = diag
            inv[q, t] = 1.0 / diag
        total = (screen[0] + screen[1]) + (screen[2] + screen[3])
        d2[t] = 4.0 + total
        i2[t] = 1.0 / (4.0 + total)

    def split(c, _):
        def wide(refs):
            return jnp.concatenate(
                [jnp.concatenate([ref[2 * c + h] for ref in refs], 0) for h in (0, 1)], 1
            )

        source = quarters_of(moved(wide((s_left, s_low, s_high, s_right)), matrix), temp)
        screen = quarters_of(moved(wide((e_left, e_low, e_high, e_right)), matrix), temp)
        fill(c, source, screen)
        return 0

    lax.fori_loop(0, tiles, split, 0)
    last = 2 * tiles
    matrix = virtual_splitter()
    source = jnp.concatenate([s_left[last], s_low[last], s_high[last], s_right[last]], 0)
    source = quarters_of(moved(source, matrix), temp)
    screen = quarters_of(moved(e_virtual[...], matrix), temp)
    fill(tiles, source, screen)

    smooth(v, lambda q, t: s[q, t], lambda q, t: inv[q, t], tiles)
    residual_and_columns(
        v, lambda q, t: s[q, t], lambda q, t: d[q, t], tiles, c_ref, lambda t, r: None
    )

    lane, sub = lane_ids(rows), row_ids(rows)
    even = (lane + sub) % 2 == 0

    def start(t, _):
        value = restricted(c_ref, t, tiles)
        s2[t] = value
        v2[t] = jnp.where(even, value * i2[t], 0.0)
        return 0

    lax.fori_loop(0, tiles, start, 0)
    value = restricted(c_ref, tiles, tiles)
    s2[tiles] = value
    v2[tiles] = jnp.where(even, 0.0, value * i2[tiles])

    def beside(t, before, after):
        x = v2[t]
        north = jnp.where(lane == 0, roll_up(v2[before]), roll_up(x))
        south = jnp.where(lane == LANES - 1, roll_down(v2[after]), roll_down(x))
        return (col_prev(x) + col_next(x)) + (north + south)

    def relaxed(t, before, after, mask):
        return jnp.where(mask, (s2[t] + beside(t, before, after)) * i2[t], v2[t])

    for mask, other in ((~even, even), (even, ~even), (~even, even)):
        held = relaxed(tiles, tiles - 1, 0, other)

        def sweep(t, _, mask=mask):
            v2[t] = relaxed(t, jnp.where(t == 0, tiles, t - 1), t + 1, mask)
            return 0

        lax.fori_loop(0, tiles, sweep, 0)
        v2[tiles] = held

    own = solution_ref.shape[0]
    skip = (rows - own) // 2

    def finish(t, _):
        x = v2[t]
        r = s2[t] - (d2[t] * x - beside(t, jnp.where(t == 0, tiles, t - 1), t + 1))
        where = pl.ds(pl.multiple_of(t * LANES, LANES), LANES)
        solution_ref[:, where] = x[skip : skip + own]
        residual_ref[:, where] = r[skip : skip + own]
        return 0

    lax.fori_loop(0, tiles, finish, 0)


def call(kernel, out_shapes, scratch, *args):
    vmem = pl.BlockSpec(memory_space=pltpu.VMEM)
    return pl.pallas_call(
        kernel,
        out_shape=[jax.ShapeDtypeStruct(shape, F32) for shape in out_shapes],
        in_specs=[vmem] * len(args),
        out_specs=[vmem] * len(out_shapes),
        scratch_shapes=[pltpu.VMEM(shape, F32) for shape in scratch],
        compiler_params=pltpu.CompilerParams(vmem_limit_bytes=40 * 2**20),
    )(*args)


def shifted(x, by):
    count = lax.axis_size("lon")
    return lax.ppermute(x, "lon", [(i, (i + by) % count) for i in range(count)])


def body(right_side, texel_weight, seam_flags):
    columns, height = right_side.shape
    half_turn = lax.axis_size("lon") // 2
    tiles, rows = height // 256, columns // 2
    half = rows // 2
    quarters = (4, tiles, rows, LANES)
    part = (tiles, half, LANES)
    s, d, e_low, e_high, to_left, to_right, polar, corner_low, corner_high = call(
        prepare_kernel,
        [quarters, quarters, part, part, (2, tiles, 8, LANES), (2, tiles, 8, LANES)]
        + [(4, rows, LANES), (4, half, LANES), (4, half, LANES)],
        [(2, columns, LANES), (2, columns, LANES), (tiles, 8, LANES)],
        right_side, texel_weight, seam_flags,
    )
    from_left = shifted(to_right, 1)
    from_right = shifted(to_left, -1)
    polar = shifted(polar, half_turn)
    corner_left = shifted(corner_high, half_turn + 1)
    corner_right = shifted(corner_low, half_turn - 1)
    e_left = shifted(e_high, 1)
    e_right = shifted(e_low, -1)
    (inverse,) = call(inverse_kernel, [quarters], [], d)
    wide = rows + 8
    halo = (4, tiles + 1, 8, LANES)
    own = (4, rows, LANES)
    part = (tiles + 1, half, LANES)
    r, s_low, s_high, e_virtual = call(
        fine_kernel,
        [quarters, part, part, (2 * rows, LANES)],
        [(4, tiles + 1, wide, LANES), (2, tiles + 1, wide, LANES), halo, halo, halo, own, own, own],
        s, d, inverse, from_left, from_right, polar, corner_left, corner_right,
    )
    s_left = shifted(s_high, 1)
    s_right = shifted(s_low, -1)
    (fine_residual,) = call(merge_kernel, [(columns, height)], [(2, columns, LANES)], r)
    coarse = (4, tiles // 2 + 1, rows, LANES)
    single = coarse[1:]
    solution_2, residual_2 = call(
        coarse_kernel,
        [(columns // 4, height // 4)] * 2,
        [coarse, coarse, coarse, coarse, (2,) + single, (2, columns, LANES)]
        + [single, single, single, single],
        s_left, s_low, s_high, s_right, e_left, e_low, e_high, e_right, e_virtual,
    )
    return fine_residual, solution_2, residual_2


def solution(mesh):
    spec = P(("groups", "lon"), None)
    return jax.shard_map(
        body, mesh=mesh, in_specs=(spec,) * 3, out_specs=(spec,) * 3, check_vma=False
    )
```

```python
import functools

import jax
import jax.numpy as jnp
from jax import lax
from jax.experimental import pallas as pl
from jax.experimental.pallas import tpu as pltpu
from jax.sharding import PartitionSpec as P

TILE = 32
SEAM_SCALE = 0.1
LANES = 128
GROUPS = 4
BATCH = 4
F32 = jnp.float32
BF16 = jnp.bfloat16


def lane_ids(rows):
    return lax.broadcasted_iota(jnp.int32, (rows, LANES), 1)


def row_ids(rows):
    return lax.broadcasted_iota(jnp.int32, (rows, LANES), 0)


def roll_up(x):
    return pltpu.roll(x, 1, 1)


def roll_down(x):
    return pltpu.roll(x, LANES - 1, 1)


def col_prev(x):
    return pltpu.roll(x, 1, 0)


def col_next(x):
    return pltpu.roll(x, x.shape[0] - 1, 0)


def loop(count, body, carry=0, unroll=4):
    def steps(block, carry):
        for i in range(unroll):
            carry = body(block * unroll + i, carry)
        return carry

    carry = lax.fori_loop(0, count // unroll, steps, carry)
    for t in range(count - count % unroll, count):
        carry = body(t, carry)
    return carry


def splitter():
    a = lax.broadcasted_iota(jnp.int32, (256, 256), 0)
    b = lax.broadcasted_iota(jnp.int32, (256, 256), 1)
    return jnp.where(a == 2 * (b % LANES) + b // LANES, 1.0, 0.0).astype(BF16)


def merger():
    a = lax.broadcasted_iota(jnp.int32, (256, 256), 0)
    b = lax.broadcasted_iota(jnp.int32, (256, 256), 1)
    return jnp.where(b == 2 * (a % LANES) + a // LANES, 1.0, 0.0).astype(BF16)


def virtual_splitter():
    a = lax.broadcasted_iota(jnp.int32, (LANES, 256), 0)
    b = lax.broadcasted_iota(jnp.int32, (LANES, 256), 1)
    place = a // 2 + jnp.where(a >= 64, 64, 0) + LANES * (a % 2)
    return jnp.where(place == b, 1.0, 0.0).astype(BF16)


def moved(x, matrix, exact=None):
    rows = x.shape[0]
    high = x.astype(BF16)
    low = (x - high.astype(F32)).astype(BF16)
    terms = [high, low] if exact is None else [high, low, exact]
    out = jnp.dot(jnp.concatenate(terms, 0), matrix, preferred_element_type=F32)
    both = out[:rows] + out[rows : 2 * rows]
    return both if exact is None else (both, out[2 * rows :])


def quarters_of(parts, temp):
    count = parts.shape[0] // 2
    temp[0] = parts[:, :LANES]
    temp[1] = parts[:, LANES:]
    return [temp[pr, pl.ds(pc, count, 2), :] for pc in (0, 1) for pr in (0, 1)]


def prepare_kernel(
    right_ref, weight_ref, flag_ref,
    s_ref, d_ref, low_ref, high_ref, to_left, to_right, polar_ref, corner_low, corner_high,
    right_buf, weight_buf, temp_s, temp_d, scale_ref, sems,
):
    tiles, rows = s_ref.shape[1], s_ref.shape[2]
    chunk = right_ref.shape[1] // GROUPS
    copies = []
    for group in range(GROUPS):
        part = pl.ds(group * chunk, chunk)
        copies.append(
            [
                pltpu.make_async_copy(src.at[:, part], dst.at[:, part], sems.at[i, group])
                for i, (src, dst) in enumerate(((right_ref, right_buf), (weight_ref, weight_buf)))
            ]
        )
        for copy in copies[group]:
            copy.start()
    flag_cols = flag_ref.shape[0]
    flag_lats = flag_ref.shape[1]
    per_tile = rows // flag_cols
    matrix = splitter()
    flags = jnp.concatenate(
        [flag_ref[...].astype(F32), jnp.zeros((8 - flag_cols, flag_lats), F32)], 0
    )
    lat = lax.broadcasted_iota(jnp.int32, (8, flag_lats), 1)
    stacked = jnp.concatenate(
        [jnp.where(lat // 8 == c, flags, 0.0) for c in range(tiles)], 0
    ).astype(BF16)
    a = lax.broadcasted_iota(jnp.int32, (flag_lats, LANES), 0)
    b = lax.broadcasted_iota(jnp.int32, (flag_lats, LANES), 1)
    spread = jnp.where(a % 8 == b // (TILE // 2), 1.0, 0.0).astype(BF16)
    spread_flags = jnp.dot(stacked, spread, preferred_element_type=F32)
    scale_ref[...] = jnp.where(spread_flags > 0.5, SEAM_SCALE, 1.0).reshape(tiles, 8, LANES)

    sub = row_ids(8)

    def edge(group, first, shift_of):
        packed = group[0] if shift_of(0) == 0 else pltpu.roll(group[0], shift_of(0), 0)
        for q in range(1, 4):
            shift = shift_of(q) % 8
            moved_q = group[q] if shift == 0 else pltpu.roll(group[q], shift, 0)
            packed = jnp.where(sub // 2 == q, moved_q, packed)
        return packed

    def piece(c, source, weight):
        scales = scale_ref[c]
        scale = jnp.concatenate(
            [jnp.broadcast_to(scales[i : i + 1], (per_tile, LANES)) for i in range(flag_cols)], 0
        )
        screen = [w * scale for w in weight]
        coarse = (screen[0] + screen[1]) + (screen[2] + screen[3])
        half = rows // 2
        low_ref[c] = coarse[:half]
        high_ref[c] = coarse[half:]
        diag = [4.0 + s for s in screen]
        for q in range(4):
            s_ref[q, c] = source[q]
            d_ref[q, c] = diag[q]
        gs = [x[rows - 8 :] for x in source]
        gd = [x[rows - 8 :] for x in diag]
        first = pltpu.roll(gs[0] / gd[0], 2, 0)
        second = pltpu.roll(gs[3] / gd[3], 3, 0)
        to_right[0, c] = jnp.where(sub == 0, first, edge(gs, 0, lambda q: 2 * q + 2))
        to_right[1, c] = jnp.where(sub == 0, second, edge(gd, 0, lambda q: 2 * q + 2))
        gs = [x[:8] for x in source]
        gd = [x[:8] for x in diag]
        first = pltpu.roll(gs[3] / gd[3], 6, 0)
        second = pltpu.roll(gs[0] / gd[0], 5, 0)
        to_left[0, c] = jnp.where(sub == 7, first, edge(gs, 0, lambda q: 2 * q))
        to_left[1, c] = jnp.where(sub == 7, second, edge(gd, 0, lambda q: 2 * q))

    columns = right_ref.shape[0]
    for group in range(GROUPS):
        for copy in copies[group]:
            copy.wait()
        for batch in range(tiles // GROUPS // BATCH):
            start = group * (tiles // GROUPS) + batch * BATCH
            lanes = [slice((start + i) * 256, (start + i + 1) * 256) for i in range(BATCH)]
            source = jnp.concatenate([right_buf[:, w] for w in lanes], 0)
            weight = jnp.concatenate([weight_buf[:, w] for w in lanes], 0)
            source, weight = moved(source, matrix, weight)
            for i in range(BATCH):
                here = slice(i * columns, (i + 1) * columns)
                piece(
                    start + i,
                    quarters_of(source[here], temp_s.at[i]),
                    quarters_of(weight[here], temp_d.at[i]),
                )

    a = lax.broadcasted_iota(jnp.int32, (LANES, LANES), 0)
    b = lax.broadcasted_iota(jnp.int32, (LANES, LANES), 1)
    mirror = jnp.where(a + b == LANES - 1, 1.0, 0.0).astype(BF16)
    lane = lane_ids(rows)
    for pc in (0, 1):
        for pr in (0, 1):
            q, from_q = 2 * pc + pr, 2 * pc + 1 - pr
            both = jnp.where(lane >= 64, s_ref[from_q, tiles - 1], s_ref[from_q, 0])
            diag = jnp.where(lane >= 64, d_ref[from_q, tiles - 1], d_ref[from_q, 0])
            both = jnp.where((lane >= 32) & (lane < 96), pltpu.roll(diag, 64, 1), both)
            both = moved(both, mirror)
            polar_ref[q] = both
            corner_low[q] = both[: rows // 2]
            corner_high[q] = both[rows // 2 :]


def inverse_kernel(d_ref, i_ref):
    def body(t, _):
        for q in range(4):
            i_ref[q, t] = 1.0 / d_ref[q, t]
        return 0

    loop(d_ref.shape[1], body)


def half_sweep(v, load_s, load_i, tiles, red):
    rows = v[0].shape[1]
    lane = lane_ids(rows)
    y, z, qa, qb = (1, 2, 0, 3) if red else (3, 0, 2, 1)
    col_a, col_b = (col_prev, col_next) if red else (col_next, col_prev)

    def beside_virtual(q):
        ns, we = q ^ 1, q ^ 2
        here = v[ns][tiles]
        if q % 2 == 0:
            lat = jnp.where(lane == 0, roll_up(v[ns][tiles - 1]), roll_up(here))
        else:
            lat = jnp.where(lane == LANES - 1, roll_down(v[ns][0]), roll_down(here))
        cols = v[we][tiles]
        return (here + lat) + (cols + (col_prev if q < 2 else col_next)(cols))

    held = [
        (q, (load_s(q, tiles) + beside_virtual(q)) * load_i(q, tiles)) for q in (y, z)
    ]

    def body(t, carry):
        y_before, z_here = carry
        vy, vz = v[y][t], v[z][t]
        y_here = roll_up(vy)
        z_after = roll_down(v[z][t + 1])
        lat_a = vy + jnp.where(lane == 0, y_before, y_here)
        lat_b = vz + jnp.where(lane == LANES - 1, z_after, z_here)
        v[qa][t] = (load_s(qa, t) + (lat_a + (vz + col_a(vz)))) * load_i(qa, t)
        v[qb][t] = (load_s(qb, t) + (lat_b + (vy + col_b(vy)))) * load_i(qb, t)
        return y_here, z_after

    loop(tiles, body, (roll_up(v[y][tiles]), roll_down(v[z][0])))
    for q, value in held:
        v[q][tiles] = value


def smooth(v, load_s, load_i, tiles):
    rows = v[0].shape[1]
    zeros = jnp.zeros((rows, LANES), F32)

    def first(t, _):
        for q in (0, 3):
            v[q][t] = load_s(q, t) * load_i(q, t)
        return 0

    loop(tiles, first)
    for q in (1, 2):
        v[q][0] = zeros
        v[q][tiles - 1] = zeros
        v[q][tiles] = load_s(q, tiles) * load_i(q, tiles)
        v[3 * (q - 1)][tiles] = zeros
    half_sweep(v, load_s, load_i, tiles, False)
    half_sweep(v, load_s, load_i, tiles, True)
    half_sweep(v, load_s, load_i, tiles, False)


def residual_and_columns(v, load_s, load_d, tiles, c_ref, keep):
    rows = v[0].shape[1]
    lane = lane_ids(rows)

    def body(t, _):
        before = jnp.where(t == 0, tiles, t - 1)
        after = jnp.where(t == tiles, 0, t + 1)
        x = [v[q][t] for q in range(4)]

        def north(q):
            return jnp.where(lane == 0, roll_up(v[q][before]), roll_up(x[q]))

        def south(q):
            return jnp.where(lane == LANES - 1, roll_down(v[q][after]), roll_down(x[q]))

        beside = [
            (x[1] + north(1)) + (x[2] + col_prev(x[2])),
            (x[0] + south(0)) + (x[3] + col_prev(x[3])),
            (x[3] + north(3)) + (x[0] + col_next(x[0])),
            (x[2] + south(2)) + (x[1] + col_next(x[1])),
        ]
        r = [load_s(q, t) - (load_d(q, t) * x[q] - beside[q]) for q in range(4)]
        keep(t, r)
        c_ref[0, t] = (col_prev(r[2]) + col_next(r[0])) + 3.0 * (r[0] + r[2])
        c_ref[1, t] = (col_prev(r[3]) + col_next(r[1])) + 3.0 * (r[1] + r[3])
        return 0

    loop(tiles + 1, body)


def restricted(c_ref, t, tiles):
    lane = lane_ids(c_ref.shape[2])
    before = jnp.where(t == 0, tiles, t - 1)
    after = jnp.where(t == tiles, 0, t + 1)
    c0, c1 = c_ref[0, t], c_ref[1, t]
    north = jnp.where(lane == 0, roll_up(c_ref[1, before]), roll_up(c1))
    south = jnp.where(lane == LANES - 1, roll_down(c_ref[0, after]), roll_down(c0))
    return ((north + south) + 3.0 * (c0 + c1)) * (1.0 / 16.0)


def fine_kernel(
    s_ref, d_ref, i_ref, from_left, from_right, polar_ref, corner_left, corner_right,
    r_ref, low_ref, high_ref, screen_virtual,
    v0, v1, v2, v3, c_ref, hs, hd, hi, ps, pd, pi,
):
    v = [v0, v1, v2, v3]
    tiles, rows = s_ref.shape[1], s_ref.shape[2]
    sub = row_ids(8)

    def rolled(x, shift):
        return x if shift % 8 == 0 else pltpu.roll(x, shift % 8, 0)

    def halo(t, _):
        al, bl, ar, br = from_left[0, t], from_left[1, t], from_right[0, t], from_right[1, t]
        for q in range(4):
            source = jnp.where(
                sub >= 6, rolled(al, 6 - 2 * q), jnp.where(sub <= 1, rolled(ar, -2 * q), 0.0)
            )
            diag = jnp.where(
                sub >= 6, rolled(bl, 6 - 2 * q), jnp.where(sub <= 1, rolled(br, -2 * q), 4.0)
            )
            if q == 0:
                source = jnp.where(sub == 2, rolled(br, 3), source)
                diag = jnp.where((sub == 2) | (sub == 6), 1.0, diag)
            if q == 3:
                source = jnp.where(sub == 5, rolled(bl, 5), source)
                diag = jnp.where((sub == 5) | (sub == 1), 1.0, diag)
            hs[q, t] = source
            hd[q, t] = diag
            hi[q, t] = 1.0 / diag
        return 0

    loop(tiles, halo)

    def unpacked(x):
        lane = lane_ids(x.shape[0])
        used = (lane < 32) | (lane >= 96)
        return jnp.where(used, x, 0.0), jnp.where(used, pltpu.roll(x, 64, 1), 4.0)

    half = rows // 2
    totals = [0.0, 0.0, 0.0]
    for q in range(4):
        left_s, left_d = unpacked(corner_left[q])
        own_s, own_d = unpacked(polar_ref[q])
        right_s, right_d = unpacked(corner_right[q])
        totals = [totals[0] + left_d, totals[1] + own_d, totals[2] + right_d]
        ps[q] = own_s
        pd[q] = own_d
        pi[q] = 1.0 / own_d
        source = jnp.where(sub >= 5, left_s[half - 8 :], jnp.where(sub <= 2, right_s[:8], 0.0))
        diag = jnp.where(sub >= 5, left_d[half - 8 :], jnp.where(sub <= 2, right_d[:8], 4.0))
        hs[q, tiles] = source
        hd[q, tiles] = diag
        hi[q, tiles] = 1.0 / diag
    screen_virtual[:half] = totals[0] - 16.0
    screen_virtual[half : half + rows] = totals[1] - 16.0
    screen_virtual[half + rows :] = totals[2] - 16.0

    def loader(own, halo_ref, virtual):
        def load(q, t):
            if isinstance(t, int) and t == tiles:
                return jnp.concatenate([virtual[q], halo_ref[q, t]], 0)
            return jnp.concatenate([own[q, t], halo_ref[q, t]], 0)

        return load

    smooth(v, loader(s_ref, hs, ps), loader(i_ref, hi, pi), tiles)

    def residual(t, before, after, own_s, own_d):
        lane = lane_ids(v[0].shape[1])
        x = [v[q][t] for q in range(4)]

        def north(q):
            return jnp.where(lane == 0, roll_up(v[q][before]), roll_up(x[q]))

        def south(q):
            return jnp.where(lane == LANES - 1, roll_down(v[q][after]), roll_down(x[q]))

        beside = [
            (x[1] + north(1)) + (x[2] + col_prev(x[2])),
            (x[0] + south(0)) + (x[3] + col_prev(x[3])),
            (x[3] + north(3)) + (x[0] + col_next(x[0])),
            (x[2] + south(2)) + (x[1] + col_next(x[1])),
        ]
        r = [
            jnp.concatenate([own_s[q], hs[q, t]], 0)
            - (jnp.concatenate([own_d[q], hd[q, t]], 0) * x[q] - beside[q])
            for q in range(4)
        ]
        c_ref[0, t] = (col_prev(r[2]) + col_next(r[0])) + 3.0 * (r[0] + r[2])
        c_ref[1, t] = (col_prev(r[3]) + col_next(r[1])) + 3.0 * (r[1] + r[3])
        return r

    def main(t, _):
        before = jnp.where(t == 0, tiles, t - 1)
        r = residual(
            t, before, t + 1, [s_ref[q, t] for q in range(4)], [d_ref[q, t] for q in range(4)]
        )
        for q in range(4):
            r_ref[q, t] = r[q][:rows]
        return 0

    loop(tiles, main)
    residual(tiles, tiles - 1, 0, [ps[q] for q in range(4)], [pd[q] for q in range(4)])

    def coarse(t, _):
        value = restricted(c_ref, t, tiles)
        low_ref[t] = value[:half]
        high_ref[t] = value[half:rows]
        return 0

    loop(tiles + 1, coarse)


def merge_kernel(r_ref, out_ref, temp, out_buf, sems):
    tiles = r_ref.shape[1]
    rows = r_ref.shape[2]
    matrix = merger()
    chunk = out_ref.shape[1] // GROUPS
    copies = []
    for group in range(GROUPS):
        for batch in range(tiles // GROUPS // BATCH):
            start = group * (tiles // GROUPS) + batch * BATCH
            both = []
            for i in range(BATCH):
                for pr in (0, 1):
                    for pc in (0, 1):
                        temp[i, pr, pl.ds(pc, rows, 2), :] = r_ref[2 * pc + pr, start + i]
                both.append(jnp.concatenate([temp[i, 0], temp[i, 1]], 1))
            out = moved(jnp.concatenate(both, 0), matrix)
            for i in range(BATCH):
                where = slice((start + i) * 256, (start + i + 1) * 256)
                out_buf[:, where] = out[2 * rows * i : 2 * rows * (i + 1)]
        part = pl.ds(group * chunk, chunk)
        copy = pltpu.make_async_copy(out_buf.at[:, part], out_ref.at[:, part], sems.at[group])
        copy.start()
        copies.append(copy)
    for copy in copies:
        copy.wait()


def coarse_kernel(
    s_left, s_low, s_high, s_right, e_left, e_low, e_high, e_right, e_virtual,
    solution_ref, residual_ref,
    s, d, inv, qv0, qv1, qv2, qv3, c_ref, temp, s2, d2, i2, v2,
):
    v = [qv0, qv1, qv2, qv3]
    tiles = s.shape[1] - 1
    rows = s.shape[2]
    matrix = splitter()

    def fill(t, source, screen):
        for q, value in enumerate(source):
            s[q, t] = value
        for q, value in enumerate(screen):
            diag = 4.0 + value
            d[q, t] = diag
            inv[q, t] = 1.0 / diag
        total = (screen[0] + screen[1]) + (screen[2] + screen[3])
        d2[t] = 4.0 + total
        i2[t] = 1.0 / (4.0 + total)

    def split(batch, _):
        def wide(refs, c):
            return jnp.concatenate(
                [jnp.concatenate([ref[2 * c + h] for ref in refs], 0) for h in (0, 1)], 1
            )

        both = []
        for i in range(BATCH):
            both.append(wide((s_left, s_low, s_high, s_right), batch * BATCH + i))
            both.append(wide((e_left, e_low, e_high, e_right), batch * BATCH + i))
        out = moved(jnp.concatenate(both, 0), matrix)
        size = 2 * rows
        for i in range(BATCH):
            at = 2 * i * size
            source = quarters_of(out[at : at + size], temp.at[2 * i])
            screen = quarters_of(out[at + size : at + 2 * size], temp.at[2 * i + 1])
            fill(batch * BATCH + i, source, screen)
        return 0

    loop(tiles // BATCH, split, unroll=1)
    last = 2 * tiles
    matrix = virtual_splitter()
    source = jnp.concatenate([s_left[last], s_low[last], s_high[last], s_right[last]], 0)
    source = quarters_of(moved(source, matrix), temp.at[0])
    screen = quarters_of(moved(e_virtual[...], matrix), temp.at[1])
    fill(tiles, source, screen)

    smooth(v, lambda q, t: s[q, t], lambda q, t: inv[q, t], tiles)
    residual_and_columns(
        v, lambda q, t: s[q, t], lambda q, t: d[q, t], tiles, c_ref, lambda t, r: None
    )

    lane, sub = lane_ids(rows), row_ids(rows)
    even = (lane + sub) % 2 == 0

    def start(t, _):
        value = restricted(c_ref, t, tiles)
        s2[t] = value
        v2[t] = jnp.where(even, value * i2[t], 0.0)
        return 0

    loop(tiles, start)
    value = restricted(c_ref, tiles, tiles)
    s2[tiles] = value
    v2[tiles] = jnp.where(even, 0.0, value * i2[tiles])

    def beside(t, before, after):
        x = v2[t]
        north = jnp.where(lane == 0, roll_up(v2[before]), roll_up(x))
        south = jnp.where(lane == LANES - 1, roll_down(v2[after]), roll_down(x))
        return (col_prev(x) + col_next(x)) + (north + south)

    def relaxed(t, before, after, mask):
        return jnp.where(mask, (s2[t] + beside(t, before, after)) * i2[t], v2[t])

    for mask, other in ((~even, even), (even, ~even), (~even, even)):
        held = relaxed(tiles, tiles - 1, 0, other)

        def sweep(t, _, mask=mask):
            v2[t] = relaxed(t, jnp.where(t == 0, tiles, t - 1), t + 1, mask)
            return 0

        loop(tiles, sweep)
        v2[tiles] = held

    own = solution_ref.shape[0]
    skip = (rows - own) // 2

    def finish(t, _):
        x = v2[t]
        r = s2[t] - (d2[t] * x - beside(t, jnp.where(t == 0, tiles, t - 1), t + 1))
        where = pl.ds(pl.multiple_of(t * LANES, LANES), LANES)
        solution_ref[:, where] = x[skip : skip + own]
        residual_ref[:, where] = r[skip : skip + own]
        return 0

    loop(tiles, finish)


VMEM = pl.BlockSpec(memory_space=pltpu.VMEM)
HBM = pl.BlockSpec(memory_space=pltpu.HBM)


def call(kernel, out_shapes, scratch, *args, sems=None, far_in=0, far_out=0):
    scratch = [pltpu.VMEM(x, F32) if isinstance(x, tuple) else x for x in scratch]
    if sems is not None:
        scratch.append(pltpu.SemaphoreType.DMA(sems))
    return pl.pallas_call(
        kernel,
        out_shape=[jax.ShapeDtypeStruct(shape, F32) for shape in out_shapes],
        in_specs=[HBM] * far_in + [VMEM] * (len(args) - far_in),
        out_specs=[HBM] * far_out + [VMEM] * (len(out_shapes) - far_out),
        scratch_shapes=scratch,
        compiler_params=pltpu.CompilerParams(vmem_limit_bytes=40 * 2**20),
    )(*args)


def shifted(x, by):
    count = lax.axis_size("lon")
    return lax.ppermute(x, "lon", [(i, (i + by) % count) for i in range(count)])


def body(right_side, texel_weight, seam_flags):
    columns, height = right_side.shape
    half_turn = lax.axis_size("lon") // 2
    tiles, rows = height // 256, columns // 2
    half = rows // 2
    quarters = (4, tiles, rows, LANES)
    part = (tiles, half, LANES)
    s, d, e_low, e_high, to_left, to_right, polar, corner_low, corner_high = call(
        prepare_kernel,
        [quarters, quarters, part, part, (2, tiles, 8, LANES), (2, tiles, 8, LANES)]
        + [(4, rows, LANES), (4, half, LANES), (4, half, LANES)],
        [(columns, height), pltpu.VMEM((columns, height), BF16)]
        + [(BATCH, 2, columns, LANES)] * 2
        + [(tiles, 8, LANES)],
        right_side, texel_weight, seam_flags,
        sems=(2, GROUPS), far_in=2,
    )
    from_left = shifted(to_right, 1)
    from_right = shifted(to_left, -1)
    polar = shifted(polar, half_turn)
    corner_left = shifted(corner_high, half_turn + 1)
    corner_right = shifted(corner_low, half_turn - 1)
    e_left = shifted(e_high, 1)
    e_right = shifted(e_low, -1)
    (inverse,) = call(inverse_kernel, [quarters], [], d)
    wide = rows + 8
    halo = (4, tiles + 1, 8, LANES)
    own = (4, rows, LANES)
    part = (tiles + 1, half, LANES)
    r, s_low, s_high, e_virtual = call(
        fine_kernel,
        [quarters, part, part, (2 * rows, LANES)],
        [(tiles + 1, wide, LANES)] * 4 + [(2, tiles + 1, wide, LANES), halo, halo, halo, own, own, own],
        s, d, inverse, from_left, from_right, polar, corner_left, corner_right,
    )
    s_left = shifted(s_high, 1)
    s_right = shifted(s_low, -1)
    (fine_residual,) = call(
        merge_kernel,
        [(columns, height)],
        [(BATCH, 2, columns, LANES), (columns, height)],
        r,
        sems=(GROUPS,), far_out=1,
    )
    coarse = (4, tiles // 2 + 1, rows, LANES)
    single = coarse[1:]
    solution_2, residual_2 = call(
        coarse_kernel,
        [(columns // 4, height // 4)] * 2,
        [coarse, coarse, coarse, single, single, single, single, (2,) + single, (2 * BATCH, 2, columns, LANES)]
        + [single, single, single, single],
        s_left, s_low, s_high, s_right, e_left, e_low, e_high, e_right, e_virtual,
    )
    return fine_residual, solution_2, residual_2


def solution(mesh):
    spec = P(("groups", "lon"), None)
    return jax.shard_map(
        body, mesh=mesh, in_specs=(spec,) * 3, out_specs=(spec,) * 3, check_vma=False
    )
```

```python
import jax
import jax.numpy as jnp
from jax import lax
from jax.experimental import pallas as pl
from jax.experimental.pallas import tpu as pltpu
from jax.sharding import PartitionSpec as P

TILE = 32
SEAM_SCALE = 0.1
LANES = 128
GROUPS = 4
BATCH = 4
F32 = jnp.float32
BF16 = jnp.bfloat16


def loop(count, body, carry=0, unroll=4):
    unroll = min(unroll, count)

    def steps(block, carry):
        for i in range(unroll):
            carry = body(block * unroll + i, carry)
        return carry

    whole = count // unroll
    carry = steps(0, carry) if whole == 1 else lax.fori_loop(0, whole, steps, carry)
    for t in range(whole * unroll, count):
        carry = body(t, carry)
    return carry


def before(t, tiles):
    return (tiles if t == 0 else t - 1) if isinstance(t, int) else jnp.where(t == 0, tiles, t - 1)


def after(t, tiles):
    return (0 if t == tiles else t + 1) if isinstance(t, int) else t + 1


def lane_ids(rows):
    return lax.broadcasted_iota(jnp.int32, (rows, LANES), 1)


def row_ids(rows):
    return lax.broadcasted_iota(jnp.int32, (rows, LANES), 0)


def roll_up(x):
    return pltpu.roll(x, 1, 1)


def roll_down(x):
    return pltpu.roll(x, LANES - 1, 1)


def roll_rows(x, by):
    by %= x.shape[0]
    return x if by == 0 else pltpu.roll(x, by, 0)


def roll_lanes(x, by):
    by %= LANES
    return x if by == 0 else pltpu.roll(x, by, 1)


def col_prev(x):
    return pltpu.roll(x, 1, 0)


def col_next(x):
    return pltpu.roll(x, x.shape[0] - 1, 0)


def selector(shape, rule):
    a = lax.broadcasted_iota(jnp.int32, shape, 0)
    b = lax.broadcasted_iota(jnp.int32, shape, 1)
    return jnp.where(rule(a, b), 1.0, 0.0).astype(BF16)


def splitter():
    return selector((256, 256), lambda a, b: a == 2 * (b % LANES) + b // LANES)


def merger():
    return selector((256, 256), lambda a, b: b == 2 * (a % LANES) + a // LANES)


def virtual_splitter():
    return selector(
        (LANES, 256),
        lambda a, b: a // 2 + jnp.where(a >= 64, 64, 0) + LANES * (a % 2) == b,
    )


def moved(x, matrix, exact=None):
    rows = x.shape[0]
    high = x.astype(BF16)
    low = (x - high.astype(F32)).astype(BF16)
    terms = [high, low] if exact is None else [high, low, exact]
    out = jnp.dot(jnp.concatenate(terms, 0), matrix, preferred_element_type=F32)
    both = out[:rows] + out[rows : 2 * rows]
    return both if exact is None else (both, out[2 * rows :])


def quarters_of(parts, temp):
    count = parts.shape[0] // 2
    temp[0] = parts[:, :LANES]
    temp[1] = parts[:, LANES:]
    return [temp[pr, pl.ds(pc, count, 2), :] for pc in (0, 1) for pr in (0, 1)]


def reds(swapped):
    return (1, 2) if swapped else (0, 3)


def interleaved(group, offset):
    sub = row_ids(8)
    packed = roll_rows(group[0], offset)
    for q in range(1, 4):
        packed = jnp.where(sub // 2 == q, roll_rows(group[q], 2 * q + offset), packed)
    return packed


def edge_packs(source, diag, swapped):
    sub = row_ids(8)
    even, odd = reds(swapped)
    rows = source[0].shape[0]
    packs = []
    for here, first, second, row, step in (
        (slice(rows - 8, rows), even, odd, 6, 1),
        (slice(0, 8), odd, even, 1, -1),
    ):
        gs = [x[here] for x in source]
        gd = [x[here] for x in diag]
        near = gs[first] / gd[first]
        far = roll_rows(gs[second] / gd[second], step)
        gs[first] = jnp.where(sub == row, near, gs[first])
        gd[first] = jnp.where(sub == row, far, gd[first])
        offset = 2 if row == 6 else 0
        packs.append((interleaved(gs, offset), interleaved(gd, offset)))
    return packs


def unpacked_halo(left, right, swapped):
    sub = row_ids(8)
    even, odd = reds(swapped)
    (al, bl), (ar, br) = left, right
    source, diag = [], []
    for q in range(4):
        s = jnp.where(
            sub >= 6,
            roll_rows(al, 6 - 2 * q),
            jnp.where(sub <= 1, roll_rows(ar, -2 * q), 0.0),
        )
        d = jnp.where(
            sub >= 6,
            roll_rows(bl, 6 - 2 * q),
            jnp.where(sub <= 1, roll_rows(br, -2 * q), 4.0),
        )
        if q == even:
            s = jnp.where(sub == 2, roll_rows(br, 1 - 2 * odd), s)
            d = jnp.where((sub == 2) | (sub == 6), 1.0, d)
        if q == odd:
            s = jnp.where(sub == 5, roll_rows(bl, 5 - 2 * even), s)
            d = jnp.where((sub == 5) | (sub == 1), 1.0, d)
        source.append(s)
        diag.append(d)
    return source, diag


def fill_halo(t, left, right, swapped, hs, hd, hi):
    source, diag = unpacked_halo(
        (left[0, t], left[1, t]), (right[0, t], right[1, t]), swapped
    )
    for q in range(4):
        hs[q, t] = source[q]
        hd[q, t] = diag[q]
        hi[q, t] = 1.0 / diag[q]


def loader(own, halo, virtual, tiles):
    def load(q, t):
        if isinstance(t, int) and t == tiles:
            return jnp.concatenate([virtual[q], halo[q, t]], 0)
        return jnp.concatenate([own[q, t], halo[q, t]], 0)

    return load


def polar_packs(tiles_of):
    lane = lane_ids(tiles_of[0][0].shape[0])
    packs = []
    for pc in (0, 1):
        parts = [*tiles_of[2 * pc], *tiles_of[2 * pc + 1]]
        packed = parts[0]
        for m in range(1, 4):
            mine = (lane + (16 - 32 * m) % LANES) % LANES < 32
            packed = jnp.where(mine, roll_lanes(parts[m], 32 * m), packed)
        packs.append(packed)
    return packs


def polar_unpacked(x, q):
    lane = lane_ids(x.shape[1])
    used = (lane < 16) | (lane >= LANES - 16)
    m = 2 * (q % 2)
    return (
        jnp.where(used, roll_lanes(x[q // 2], 32 * m), 0.0),
        jnp.where(used, roll_lanes(x[q // 2], 32 * (m + 1)), 4.0),
    )


def prepare_kernel(
    right_ref, weight_ref, flag_ref,
    s_ref, d_ref, e_ref, to_left, to_right, polar_ref, corner_low, corner_high,
    right_buf, weight_buf, temp_s, temp_d, scale_ref, sems,
):
    tiles, rows = s_ref.shape[1], s_ref.shape[2]
    chunk = right_ref.shape[1] // GROUPS
    copies = []
    for group in range(GROUPS):
        part = pl.ds(group * chunk, chunk)
        copies.append(
            [
                pltpu.make_async_copy(src.at[:, part], dst.at[:, part], sems.at[i, group])
                for i, (src, dst) in enumerate(((right_ref, right_buf), (weight_ref, weight_buf)))
            ]
        )
        for copy in copies[group]:
            copy.start()
    flag_cols = flag_ref.shape[0]
    flag_lats = flag_ref.shape[1]
    per_tile = rows // flag_cols
    matrix = splitter()
    flags = jnp.concatenate(
        [flag_ref[...].astype(F32), jnp.zeros((8 - flag_cols, flag_lats), F32)], 0
    )
    lat = lax.broadcasted_iota(jnp.int32, (8, flag_lats), 1)
    stacked = jnp.concatenate(
        [jnp.where(lat // 8 == c, flags, 0.0) for c in range(tiles)], 0
    ).astype(BF16)
    spread = selector((flag_lats, LANES), lambda a, b: a % 8 == b // (TILE // 2))
    spread_flags = jnp.dot(stacked, spread, preferred_element_type=F32)
    scale_ref[...] = jnp.where(spread_flags > 0.5, SEAM_SCALE, 1.0).reshape(tiles, 8, LANES)

    def piece(c, source, weight):
        scales = scale_ref[c]
        scale = jnp.concatenate(
            [jnp.broadcast_to(scales[i : i + 1], (per_tile, LANES)) for i in range(flag_cols)], 0
        )
        screen = [w * scale for w in weight]
        e_ref[c] = (screen[0] + screen[1]) + (screen[2] + screen[3])
        diag = [4.0 + s for s in screen]
        for q in range(4):
            s_ref[q, c] = source[q]
            d_ref[q, c] = diag[q]
        right, left = edge_packs(source, diag, False)
        to_right[0, c], to_right[1, c] = right
        to_left[0, c], to_left[1, c] = left

    columns = right_ref.shape[0]
    for group in range(GROUPS):
        for copy in copies[group]:
            copy.wait()
        for batch in range(tiles // GROUPS // BATCH):
            start = group * (tiles // GROUPS) + batch * BATCH
            lanes = [slice((start + i) * 256, (start + i + 1) * 256) for i in range(BATCH)]
            source = jnp.concatenate([right_buf[:, w] for w in lanes], 0)
            weight = jnp.concatenate([weight_buf[:, w] for w in lanes], 0)
            source, weight = moved(source, matrix, weight)
            for i in range(BATCH):
                here = slice(i * columns, (i + 1) * columns)
                piece(
                    start + i,
                    quarters_of(source[here], temp_s.at[i]),
                    quarters_of(weight[here], temp_d.at[i]),
                )

    mirror = selector((LANES, LANES), lambda a, b: a + b == LANES - 1)
    lane = lane_ids(rows)
    ends = [
        [jnp.where(lane >= 64, ref[q ^ 1, tiles - 1], ref[q ^ 1, 0]) for ref in (s_ref, d_ref)]
        for q in range(4)
    ]
    both = moved(jnp.concatenate(polar_packs(ends), 0), mirror)
    for pc in (0, 1):
        pack = both[pc * rows : (pc + 1) * rows]
        polar_ref[pc] = pack
        corner_low[pc] = pack[:8]
        corner_high[pc] = pack[rows - 8 :]


def split_tiles(load, tiles, rows, matrix, temp, use):
    for start in range(0, tiles, BATCH):
        wide = [
            jnp.concatenate([load(2 * c), load(2 * c + 1)], 1)
            for c in range(start, start + BATCH)
        ]
        out = moved(jnp.concatenate(wide, 0), matrix)
        for i in range(BATCH):
            use(start + i, quarters_of(out[i * rows : (i + 1) * rows], temp.at[i]))


def screens_kernel(d_ref, e_ref, i_ref, d1_ref, i1_ref, d2_ref, temp):
    def inverse(t, _):
        for q in range(4):
            i_ref[q, t] = 1.0 / d_ref[q, t]
        return 0

    loop(d_ref.shape[1], inverse)

    def use(c, screen):
        for q in range(4):
            d1_ref[q, c] = 4.0 + screen[q]
            i1_ref[q, c] = 1.0 / (4.0 + screen[q])
        d2_ref[c] = 4.0 + ((screen[0] + screen[1]) + (screen[2] + screen[3]))

    tiles, rows = d1_ref.shape[1], e_ref.shape[1]
    split_tiles(lambda t: e_ref[t], tiles, rows, splitter(), temp, use)


def half_sweep(v, load_s, load_i, tiles, red, unroll):
    rows = v[0].shape[1]
    lane = lane_ids(rows)
    y, z, qa, qb = (1, 2, 0, 3) if red else (3, 0, 2, 1)
    col_a, col_b = (col_prev, col_next) if red else (col_next, col_prev)

    def beside_virtual(q):
        ns, we = q ^ 1, q ^ 2
        here = v[ns][tiles]
        if q % 2 == 0:
            lat = jnp.where(lane == 0, roll_up(v[ns][tiles - 1]), roll_up(here))
        else:
            lat = jnp.where(lane == LANES - 1, roll_down(v[ns][0]), roll_down(here))
        cols = v[we][tiles]
        return (here + lat) + (cols + (col_prev if q < 2 else col_next)(cols))

    held = [
        (q, (load_s(q, tiles) + beside_virtual(q)) * load_i(q, tiles)) for q in (y, z)
    ]

    def body(t, carry):
        y_before, z_here = carry
        vy, vz = v[y][t], v[z][t]
        y_here = roll_up(vy)
        z_after = roll_down(v[z][t + 1])
        lat_a = vy + jnp.where(lane == 0, y_before, y_here)
        lat_b = vz + jnp.where(lane == LANES - 1, z_after, z_here)
        v[qa][t] = (load_s(qa, t) + (lat_a + (vz + col_a(vz)))) * load_i(qa, t)
        v[qb][t] = (load_s(qb, t) + (lat_b + (vy + col_b(vy)))) * load_i(qb, t)
        return y_here, z_after

    loop(tiles, body, (roll_up(v[y][tiles]), roll_down(v[z][0])), unroll)
    for q, value in held:
        v[q][tiles] = value


def smooth(v, load_s, load_i, tiles, unroll):
    zeros = jnp.zeros(v[0].shape[1:], F32)

    def first(t, _):
        for q in (0, 3):
            v[q][t] = load_s(q, t) * load_i(q, t)
        return 0

    loop(tiles, first, 0, unroll)
    for q in (1, 2):
        v[q][0] = zeros
        v[q][tiles - 1] = zeros
        v[q][tiles] = load_s(q, tiles) * load_i(q, tiles)
        v[3 * (q - 1)][tiles] = zeros
    half_sweep(v, load_s, load_i, tiles, False, unroll)
    half_sweep(v, load_s, load_i, tiles, True, unroll)
    half_sweep(v, load_s, load_i, tiles, False, unroll)


def residuals(v, load_s, load_d, tiles, c0, c1, keep, unroll):
    lane = lane_ids(v[0].shape[1])

    def body(t, _):
        x = [v[q][t] for q in range(4)]

        def north(q):
            return jnp.where(lane == 0, roll_up(v[q][before(t, tiles)]), roll_up(x[q]))

        def south(q):
            return jnp.where(
                lane == LANES - 1, roll_down(v[q][after(t, tiles)]), roll_down(x[q])
            )

        beside = [
            (x[1] + north(1)) + (x[2] + col_prev(x[2])),
            (x[0] + south(0)) + (x[3] + col_prev(x[3])),
            (x[3] + north(3)) + (x[0] + col_next(x[0])),
            (x[2] + south(2)) + (x[1] + col_next(x[1])),
        ]
        r = [load_s(q, t) - (load_d(q, t) * x[q] - beside[q]) for q in range(4)]
        keep(t, r)
        c0[t] = (col_prev(r[2]) + col_next(r[0])) + 3.0 * (r[0] + r[2])
        c1[t] = (col_prev(r[3]) + col_next(r[1])) + 3.0 * (r[1] + r[3])
        return 0

    loop(tiles, body, 0, unroll)
    body(tiles, 0)


def restricted(c0, c1, t, tiles, rows):
    lane = lane_ids(rows)
    here, other = c0[t, :rows], c1[t, :rows]
    north = jnp.where(lane == 0, roll_up(c1[before(t, tiles), :rows]), roll_up(other))
    south = jnp.where(
        lane == LANES - 1, roll_down(c0[after(t, tiles), :rows]), roll_down(here)
    )
    return ((north + south) + 3.0 * (here + other)) * (1.0 / 16.0)


def fine_kernel(
    s_ref, d_ref, i_ref, d1_ref, from_left, from_right, polar_ref, corner_left, corner_right,
    r_ref, s1_ref, d1_virtual, d2_virtual, to_left, to_right,
    v0, v1, v2, v3, c0, c1, hs, hd, hi, ps, pd, pi, n1, temp,
):
    v = [v0, v1, v2, v3]
    tiles, rows = s_ref.shape[1], s_ref.shape[2]
    sub = row_ids(8)

    def halo(t, _):
        fill_halo(t, from_left, from_right, False, hs, hd, hi)
        return 0

    loop(tiles, halo)
    total = -16.0
    for q in range(4):
        left_s, left_d = polar_unpacked(corner_left, q)
        own_s, own_d = polar_unpacked(polar_ref, q)
        right_s, right_d = polar_unpacked(corner_right, q)
        total = total + own_d
        ps[q] = own_s
        pd[q] = own_d
        pi[q] = 1.0 / own_d
        source = jnp.where(sub >= 5, left_s, jnp.where(sub <= 2, right_s, 0.0))
        diag = jnp.where(sub >= 5, left_d, jnp.where(sub <= 2, right_d, 4.0))
        hs[q, tiles] = source
        hd[q, tiles] = diag
        hi[q, tiles] = 1.0 / diag

    load_s = loader(s_ref, hs, ps, tiles)
    smooth(v, load_s, loader(i_ref, hi, pi, tiles), tiles, 8)

    def keep(t, r):
        if not (isinstance(t, int) and t == tiles):
            for q in range(4):
                r_ref[q, t] = r[q][:rows]

    residuals(v, load_s, loader(d_ref, hd, pd, tiles), tiles, c0, c1, keep, 4)

    def coarse(t, _):
        n1[t] = restricted(c0, c1, t, tiles, rows)
        return 0

    loop(tiles, coarse, 0, 8)
    coarse(tiles, 0)

    def edges(t, source, diag, swapped):
        right, left = edge_packs(source, diag, swapped)
        to_right[0, t], to_right[1, t] = right
        to_left[0, t], to_left[1, t] = left

    def use(c, source):
        for q in range(4):
            s1_ref[q, c] = source[q]
        edges(c, source, [d1_ref[q, c] for q in range(4)], False)

    tiles1 = tiles // 2
    split_tiles(lambda t: n1[t], tiles1, rows, splitter(), temp, use)
    out = moved(jnp.concatenate([n1[tiles], total], 0), virtual_splitter())
    source = quarters_of(out[:rows], temp.at[0])
    screen = quarters_of(out[rows:], temp.at[1])
    diag = [4.0 + x for x in screen]
    for q in range(4):
        s1_ref[q, tiles1] = source[q]
        d1_virtual[q] = diag[q]
    d2_virtual[...] = 4.0 + ((screen[0] + screen[1]) + (screen[2] + screen[3]))
    edges(tiles1, source, diag, True)


def merge_kernel(r_ref, out_ref, temp, out_buf, sems):
    tiles = r_ref.shape[1]
    rows = r_ref.shape[2]
    matrix = merger()
    chunk = out_ref.shape[1] // GROUPS
    copies = []
    for group in range(GROUPS):
        for batch in range(tiles // GROUPS // BATCH):
            start = group * (tiles // GROUPS) + batch * BATCH
            both = []
            for i in range(BATCH):
                for pr in (0, 1):
                    for pc in (0, 1):
                        temp[i, pr, pl.ds(pc, rows, 2), :] = r_ref[2 * pc + pr, start + i]
                both.append(jnp.concatenate([temp[i, 0], temp[i, 1]], 1))
            out = moved(jnp.concatenate(both, 0), matrix)
            for i in range(BATCH):
                where = slice((start + i) * 256, (start + i + 1) * 256)
                out_buf[:, where] = out[2 * rows * i : 2 * rows * (i + 1)]
        part = pl.ds(group * chunk, chunk)
        copy = pltpu.make_async_copy(out_buf.at[:, part], out_ref.at[:, part], sems.at[group])
        copy.start()
        copies.append(copy)
    for copy in copies:
        copy.wait()


def middle_kernel(
    s_ref, d_ref, i_ref, d_virtual, d2_ref, d2_virtual, from_left, from_right,
    s2_ref, to_left, to_right,
    v0, v1, v2, v3, c0, c1, hs, hd, hi, pi,
):
    v = [v0, v1, v2, v3]
    tiles, rows = d_ref.shape[1], d_ref.shape[2]
    for t in range(tiles + 1):
        fill_halo(t, from_left, from_right, t == tiles, hs, hd, hi)
    for q in range(4):
        pi[q] = 1.0 / d_virtual[q]

    def load_s(q, t):
        return jnp.concatenate([s_ref[q, t], hs[q, t]], 0)

    smooth(v, load_s, loader(i_ref, hi, pi, tiles), tiles, 16)
    residuals(
        v, load_s, loader(d_ref, hd, d_virtual, tiles), tiles, c0, c1, lambda t, r: None, 16
    )
    sub = row_ids(8)
    for t in range(tiles + 1):
        value = restricted(c0, c1, t, tiles, rows)
        diag = d2_virtual[...] if t == tiles else d2_ref[t]
        s2_ref[t] = value
        to_right[t] = jnp.where(sub < 4, roll_rows(value[rows - 8 :], 4), diag[rows - 8 :])
        to_left[t] = jnp.where(sub < 4, value[:8], roll_rows(diag[:8], 4))


def last_kernel(
    s_ref, d_ref, d_virtual, from_left, from_right,
    solution_ref, residual_ref,
    s, d, inv, va, vb,
):
    tiles, own = d_ref.shape[0], d_ref.shape[1]
    rows = own + 8
    sub = row_ids(8)
    lane, row = lane_ids(rows), row_ids(rows)
    even = (lane + row) % 2 == 0
    odd = jnp.logical_not(even)
    for t in range(tiles + 1):
        left, right = from_left[t], from_right[t]
        diag = d_virtual[...] if t == tiles else d_ref[t]
        source = jnp.concatenate(
            [s_ref[t], jnp.where(sub < 4, right, roll_rows(left, 4))], 0
        )
        diag = jnp.concatenate([diag, jnp.where(sub < 4, roll_rows(right, 4), left)], 0)
        inverse = 1.0 / diag
        s[t] = source
        d[t] = diag
        inv[t] = inverse
        va[t] = jnp.where(odd if t == tiles else even, source * inverse, 0.0)

    def beside(v, t):
        x = v[t]
        north = jnp.where(lane == 0, roll_up(v[before(t, tiles)]), roll_up(x))
        south = jnp.where(lane == LANES - 1, roll_down(v[after(t, tiles)]), roll_down(x))
        return (col_prev(x) + col_next(x)) + (north + south)

    old, new = va, vb
    for mask, other in ((odd, even), (even, odd), (odd, even)):
        for t in range(tiles + 1):
            value = (s[t] + beside(old, t)) * inv[t]
            new[t] = jnp.where(other if t == tiles else mask, value, old[t])
        old, new = new, old
    for t in range(tiles):
        x = old[t]
        r = s[t] - (d[t] * x - beside(old, t))
        where = slice(t * LANES, (t + 1) * LANES)
        solution_ref[:, where] = x[:own]
        residual_ref[:, where] = r[:own]


VMEM = pl.BlockSpec(memory_space=pltpu.VMEM)
HBM = pl.BlockSpec(memory_space=pltpu.HBM)


def call(kernel, out_shapes, scratch, *args, sems=None, far_in=0, far_out=0):
    scratch = [pltpu.VMEM(x, F32) if isinstance(x, tuple) else x for x in scratch]
    if sems is not None:
        scratch.append(pltpu.SemaphoreType.DMA(sems))
    return pl.pallas_call(
        kernel,
        out_shape=[jax.ShapeDtypeStruct(shape, F32) for shape in out_shapes],
        in_specs=[HBM] * far_in + [VMEM] * (len(args) - far_in),
        out_specs=[HBM] * far_out + [VMEM] * (len(out_shapes) - far_out),
        scratch_shapes=scratch,
        compiler_params=pltpu.CompilerParams(vmem_limit_bytes=40 * 2**20),
    )(*args)


def shifted(x, by):
    count = lax.axis_size("lon")
    return lax.ppermute(x, "lon", [(i, (i + by) % count) for i in range(count)])


def body(right_side, texel_weight, seam_flags):
    columns, height = right_side.shape
    half_turn = lax.axis_size("lon") // 2
    tiles, rows = height // 256, columns // 2
    tiles1, rows1 = tiles // 2, rows // 2
    temp = (BATCH, 2, columns, LANES)
    right_side = pltpu.with_memory_space_constraint(right_side, pltpu.HBM)
    texel_weight = pltpu.with_memory_space_constraint(texel_weight, pltpu.HBM)

    quarters = (4, tiles, rows, LANES)
    s, d, e, to_left, to_right, polar, corner_low, corner_high = call(
        prepare_kernel,
        [quarters, quarters, quarters[1:], (2, tiles, 8, LANES), (2, tiles, 8, LANES)]
        + [(2, rows, LANES), (2, 8, LANES), (2, 8, LANES)],
        [(columns, height), pltpu.VMEM((columns, height), BF16), temp, temp, (tiles, 8, LANES)],
        right_side, texel_weight, seam_flags,
        sems=(2, GROUPS), far_in=2,
    )
    from_left = shifted(to_right, 1)
    from_right = shifted(to_left, -1)
    polar = shifted(polar, half_turn)
    corner_left = shifted(corner_high, half_turn + 1)
    corner_right = shifted(corner_low, half_turn - 1)
    quarters1 = (4, tiles1, rows1, LANES)
    inverse, d1, i1, d2 = call(
        screens_kernel,
        [quarters, quarters1, quarters1, quarters1[1:]],
        [(BATCH, 2, rows, LANES)],
        d, e,
    )

    def level_scratch(tiles, rows):
        halo = (4, tiles + 1, 8, LANES)
        return [(tiles + 1, rows + 8, LANES)] * 6 + [halo] * 3

    pack1 = (2, tiles1 + 1, 8, LANES)
    r, s1, d1_virtual, d2_virtual, to_left, to_right = call(
        fine_kernel,
        [quarters, (4, tiles1 + 1, rows1, LANES), (4, rows1, LANES), (rows1, LANES), pack1, pack1],
        level_scratch(tiles, rows)
        + [(4, rows, LANES)] * 3
        + [(tiles + 1, rows, LANES), (BATCH, 2, rows, LANES)],
        s, d, inverse, d1, from_left, from_right, polar, corner_left, corner_right,
    )
    from_left = shifted(to_right, 1)
    from_right = shifted(to_left, -1)
    (fine_residual,) = call(
        merge_kernel, [(columns, height)], [temp, (columns, height)], r,
        sems=(GROUPS,), far_out=1,
    )
    pack2 = (tiles1 + 1, 8, LANES)
    s2, to_left, to_right = call(
        middle_kernel,
        [(tiles1 + 1, rows1, LANES), pack2, pack2],
        level_scratch(tiles1, rows1) + [(4, rows1, LANES)],
        s1, d1, i1, d1_virtual, d2, d2_virtual, from_left, from_right,
    )
    from_left = shifted(to_right, 1)
    from_right = shifted(to_left, -1)
    solution_2, residual_2 = call(
        last_kernel,
        [(columns // 4, height // 4)] * 2,
        [(tiles1 + 1, rows1 + 8, LANES)] * 5,
        s2, d2, d2_virtual, from_left, from_right,
    )
    return fine_residual, solution_2, residual_2


def solution(mesh):
    spec = P(("groups", "lon"), None)
    return jax.shard_map(
        body, mesh=mesh, in_specs=(spec,) * 3, out_specs=(spec,) * 3, check_vma=False
    )
```

```python
import jax
import jax.numpy as jnp
from jax import lax
from jax.experimental import pallas as pl
from jax.experimental.pallas import tpu as pltpu
from jax.sharding import PartitionSpec as P

TILE = 32
SEAM_SCALE = 0.1
LANES = 128
GROUPS = 4
BATCH = 4
F32 = jnp.float32
BF16 = jnp.bfloat16


def loop(count, body, carry=0, unroll=4):
    unroll = min(unroll, count)

    def steps(block, carry):
        for i in range(unroll):
            carry = body(block * unroll + i, carry)
        return carry

    whole = count // unroll
    carry = steps(0, carry) if whole == 1 else lax.fori_loop(0, whole, steps, carry)
    for t in range(whole * unroll, count):
        carry = body(t, carry)
    return carry


def before(t, tiles):
    return (tiles if t == 0 else t - 1) if isinstance(t, int) else jnp.where(t == 0, tiles, t - 1)


def after(t, tiles):
    return (0 if t == tiles else t + 1) if isinstance(t, int) else t + 1


def lane_ids(rows):
    return lax.broadcasted_iota(jnp.int32, (rows, LANES), 1)


def row_ids(rows):
    return lax.broadcasted_iota(jnp.int32, (rows, LANES), 0)


def roll_up(x):
    return pltpu.roll(x, 1, 1)


def roll_down(x):
    return pltpu.roll(x, LANES - 1, 1)


def roll_rows(x, by):
    by %= x.shape[0]
    return x if by == 0 else pltpu.roll(x, by, 0)


def roll_lanes(x, by):
    by %= LANES
    return x if by == 0 else pltpu.roll(x, by, 1)


def col_prev(x):
    return pltpu.roll(x, 1, 0)


def col_next(x):
    return pltpu.roll(x, x.shape[0] - 1, 0)


def selector(shape, rule):
    a = lax.broadcasted_iota(jnp.int32, shape, 0)
    b = lax.broadcasted_iota(jnp.int32, shape, 1)
    return jnp.where(rule(a, b), 1.0, 0.0).astype(BF16)


def splitter():
    return selector((256, 256), lambda a, b: a == 2 * (b % LANES) + b // LANES)


def merger():
    return selector((256, 256), lambda a, b: b == 2 * (a % LANES) + a // LANES)


def virtual_splitter():
    return selector(
        (LANES, 256),
        lambda a, b: a // 2 + jnp.where(a >= 64, 64, 0) + LANES * (a % 2) == b,
    )


def moved(x, matrix, exact=None):
    rows = x.shape[0]
    high = x.astype(BF16)
    low = (x - high.astype(F32)).astype(BF16)
    terms = [high, low] if exact is None else [high, low, exact]
    out = jnp.dot(jnp.concatenate(terms, 0), matrix, preferred_element_type=F32)
    both = out[:rows] + out[rows : 2 * rows]
    return both if exact is None else (both, out[2 * rows :])


def quarters_of(parts, temp):
    count = parts.shape[0] // 2
    temp[0] = parts[:, :LANES]
    temp[1] = parts[:, LANES:]
    return [temp[pr, pl.ds(pc, count, 2), :] for pc in (0, 1) for pr in (0, 1)]


def reds(swapped):
    return (1, 2) if swapped else (0, 3)


def interleaved(group, offset):
    sub = row_ids(8)
    packed = roll_rows(group[0], offset)
    for q in range(1, 4):
        packed = jnp.where(sub // 2 == q, roll_rows(group[q], 2 * q + offset), packed)
    return packed


def edge_packs(source, diag, swapped):
    sub = row_ids(8)
    even, odd = reds(swapped)
    rows = source[0].shape[0]
    packs = []
    for here, first, second, row, step in (
        (slice(rows - 8, rows), even, odd, 6, 1),
        (slice(0, 8), odd, even, 1, -1),
    ):
        gs = [x[here] for x in source]
        gd = [x[here] for x in diag]
        near = gs[first] / gd[first]
        far = roll_rows(gs[second] / gd[second], step)
        gs[first] = jnp.where(sub == row, near, gs[first])
        gd[first] = jnp.where(sub == row, far, gd[first])
        offset = 2 if row == 6 else 0
        packs.append((interleaved(gs, offset), interleaved(gd, offset)))
    return packs


def unpacked_halo(left, right, swapped):
    sub = row_ids(8)
    even, odd = reds(swapped)
    (al, bl), (ar, br) = left, right
    source, diag = [], []
    for q in range(4):
        s = jnp.where(
            sub >= 6,
            roll_rows(al, 6 - 2 * q),
            jnp.where(sub <= 1, roll_rows(ar, -2 * q), 0.0),
        )
        d = jnp.where(
            sub >= 6,
            roll_rows(bl, 6 - 2 * q),
            jnp.where(sub <= 1, roll_rows(br, -2 * q), 4.0),
        )
        if q == even:
            s = jnp.where(sub == 2, roll_rows(br, 1 - 2 * odd), s)
            d = jnp.where((sub == 2) | (sub == 6), 1.0, d)
        if q == odd:
            s = jnp.where(sub == 5, roll_rows(bl, 5 - 2 * even), s)
            d = jnp.where((sub == 5) | (sub == 1), 1.0, d)
        source.append(s)
        diag.append(d)
    return source, diag


def fill_halo(t, left, right, swapped, hs, hd, hi):
    source, diag = unpacked_halo(
        (left[0, t], left[1, t]), (right[0, t], right[1, t]), swapped
    )
    for q in range(4):
        hs[q, t] = source[q]
        hd[q, t] = diag[q]
        hi[q, t] = 1.0 / diag[q]


def loader(own, halo, virtual, tiles):
    def load(q, t):
        if isinstance(t, int) and t == tiles:
            return jnp.concatenate([virtual[q], halo[q, t]], 0)
        return jnp.concatenate([own[q, t], halo[q, t]], 0)

    return load


def polar_packs(tiles_of):
    lane = lane_ids(tiles_of[0][0].shape[0])
    packs = []
    for pc in (0, 1):
        parts = [*tiles_of[2 * pc], *tiles_of[2 * pc + 1]]
        packed = parts[0]
        for m in range(1, 4):
            mine = (lane + (16 - 32 * m) % LANES) % LANES < 32
            packed = jnp.where(mine, roll_lanes(parts[m], 32 * m), packed)
        packs.append(packed)
    return packs


def polar_unpacked(x, q):
    lane = lane_ids(x.shape[1])
    used = (lane < 16) | (lane >= LANES - 16)
    m = 2 * (q % 2)
    return (
        jnp.where(used, roll_lanes(x[q // 2], 32 * m), 0.0),
        jnp.where(used, roll_lanes(x[q // 2], 32 * (m + 1)), 4.0),
    )


def seam_scales(flag_ref, chunks):
    flag_cols, flag_lats = flag_ref.shape
    flags = jnp.concatenate(
        [flag_ref[...].astype(F32), jnp.zeros((8 - flag_cols, flag_lats), F32)], 0
    )
    lat = lax.broadcasted_iota(jnp.int32, (8, flag_lats), 1)
    stacked = jnp.concatenate([jnp.where(lat // 8 == c, flags, 0.0) for c in chunks], 0)
    spread = selector((flag_lats, LANES), lambda a, b: a % 8 == b // (TILE // 2))
    spread_flags = jnp.dot(stacked.astype(BF16), spread, preferred_element_type=F32)
    scale = jnp.where(spread_flags > 0.5, SEAM_SCALE, 1.0)
    return scale.reshape(len(chunks), 8, LANES)


def seam_rows(scales, flag_cols, rows):
    size = (rows // flag_cols, LANES)
    return jnp.concatenate(
        [jnp.broadcast_to(scales[i : i + 1], size) for i in range(flag_cols)], 0
    )


def polar_kernel(
    right_ref, weight_ref, flag_ref, polar_ref, corner_ref, right_buf, weight_buf, temp_s, temp_d, sems
):
    columns, height = right_ref.shape
    rows = columns // 2
    copies = []
    for end, start in enumerate((0, height - 256)):
        for i, (src, dst) in enumerate(((right_ref, right_buf), (weight_ref, weight_buf))):
            copies.append(
                pltpu.make_async_copy(src.at[:, pl.ds(start, 256)], dst.at[end], sems.at[i, end])
            )
    for copy in copies:
        copy.start()
    scales = seam_scales(flag_ref, (0, height // 256 - 1))
    mirror = selector((LANES, LANES), lambda a, b: a + b == LANES - 1)
    matrix = splitter()
    lane = lane_ids(rows)
    for copy in copies:
        copy.wait()
    source, weight = moved(
        jnp.concatenate([right_buf[0], right_buf[1]], 0),
        matrix,
        jnp.concatenate([weight_buf[0], weight_buf[1]], 0),
    )
    found = []
    for end in (0, 1):
        here = slice(end * columns, (end + 1) * columns)
        scale = seam_rows(scales[end], flag_ref.shape[0], rows)
        found.append(
            (
                quarters_of(source[here], temp_s.at[end]),
                [4.0 + w * scale for w in quarters_of(weight[here], temp_d.at[end])],
            )
        )
    ends = [
        [jnp.where(lane >= 64, found[1][i][q ^ 1], found[0][i][q ^ 1]) for i in (0, 1)]
        for q in range(4)
    ]
    both = moved(jnp.concatenate(polar_packs(ends), 0), mirror)
    for pc in (0, 1):
        pack = both[pc * rows : (pc + 1) * rows]
        polar_ref[pc] = pack
        corner_ref[pc, :8] = pack[:8]
        corner_ref[pc, 8:] = pack[rows - 8 :]


def prepare_kernel(
    right_ref, weight_ref, polar_first, flag_ref,
    s_ref, d_ref, e_ref, to_left, to_right,
    right_buf, weight_buf, temp_s, temp_d, scale_ref, sems,
):
    tiles, rows = s_ref.shape[1], s_ref.shape[2]
    chunk = right_ref.shape[1] // GROUPS
    copies = []
    for group in range(GROUPS):
        part = pl.ds(group * chunk, chunk)
        copies.append(
            [
                pltpu.make_async_copy(src.at[:, part], dst.at[:, part], sems.at[i, group])
                for i, (src, dst) in enumerate(((right_ref, right_buf), (weight_ref, weight_buf)))
            ]
        )
        for copy in copies[group]:
            copy.start()
    matrix = splitter()
    scale_ref[...] = seam_scales(flag_ref, range(tiles))

    def piece(c, source, weight):
        scale = seam_rows(scale_ref[c], flag_ref.shape[0], rows)
        screen = [w * scale for w in weight]
        e_ref[c] = (screen[0] + screen[1]) + (screen[2] + screen[3])
        diag = [4.0 + s for s in screen]
        for q in range(4):
            s_ref[q, c] = source[q]
            d_ref[q, c] = diag[q]
        right, left = edge_packs(source, diag, False)
        to_right[0, c], to_right[1, c] = right
        to_left[0, c], to_left[1, c] = left

    columns = right_ref.shape[0]
    for group in range(GROUPS):
        for copy in copies[group]:
            copy.wait()
        for batch in range(tiles // GROUPS // BATCH):
            start = group * (tiles // GROUPS) + batch * BATCH
            lanes = [slice((start + i) * 256, (start + i + 1) * 256) for i in range(BATCH)]
            source = jnp.concatenate([right_buf[:, w] for w in lanes], 0)
            weight = jnp.concatenate([weight_buf[:, w] for w in lanes], 0)
            source, weight = moved(source, matrix, weight)
            for i in range(BATCH):
                here = slice(i * columns, (i + 1) * columns)
                piece(
                    start + i,
                    quarters_of(source[here], temp_s.at[i]),
                    quarters_of(weight[here], temp_d.at[i]),
                )


def split_tiles(load, tiles, rows, matrix, temp, use):
    for start in range(0, tiles, BATCH):
        wide = [
            jnp.concatenate([load(2 * c), load(2 * c + 1)], 1)
            for c in range(start, start + BATCH)
        ]
        out = moved(jnp.concatenate(wide, 0), matrix)
        for i in range(BATCH):
            use(start + i, quarters_of(out[i * rows : (i + 1) * rows], temp.at[i]))


def screens_kernel(d_ref, e_ref, i_ref, d1_ref, i1_ref, d2_ref, temp):
    def inverse(t, _):
        for q in range(4):
            i_ref[q, t] = 1.0 / d_ref[q, t]
        return 0

    loop(d_ref.shape[1], inverse)

    def use(c, screen):
        for q in range(4):
            d1_ref[q, c] = 4.0 + screen[q]
            i1_ref[q, c] = 1.0 / (4.0 + screen[q])
        d2_ref[c] = 4.0 + ((screen[0] + screen[1]) + (screen[2] + screen[3]))

    tiles, rows = d1_ref.shape[1], e_ref.shape[1]
    split_tiles(lambda t: e_ref[t], tiles, rows, splitter(), temp, use)


def half_sweep(v, load_s, load_i, tiles, red, unroll):
    rows = v[0].shape[1]
    lane = lane_ids(rows)
    y, z, qa, qb = (1, 2, 0, 3) if red else (3, 0, 2, 1)
    col_a, col_b = (col_prev, col_next) if red else (col_next, col_prev)

    def beside_virtual(q):
        ns, we = q ^ 1, q ^ 2
        here = v[ns][tiles]
        if q % 2 == 0:
            lat = jnp.where(lane == 0, roll_up(v[ns][tiles - 1]), roll_up(here))
        else:
            lat = jnp.where(lane == LANES - 1, roll_down(v[ns][0]), roll_down(here))
        cols = v[we][tiles]
        return (here + lat) + (cols + (col_prev if q < 2 else col_next)(cols))

    held = [
        (q, (load_s(q, tiles) + beside_virtual(q)) * load_i(q, tiles)) for q in (y, z)
    ]

    def body(t, carry):
        y_before, z_here = carry
        vy, vz = v[y][t], v[z][t]
        y_here = roll_up(vy)
        z_after = roll_down(v[z][t + 1])
        lat_a = vy + jnp.where(lane == 0, y_before, y_here)
        lat_b = vz + jnp.where(lane == LANES - 1, z_after, z_here)
        v[qa][t] = (load_s(qa, t) + (lat_a + (vz + col_a(vz)))) * load_i(qa, t)
        v[qb][t] = (load_s(qb, t) + (lat_b + (vy + col_b(vy)))) * load_i(qb, t)
        return y_here, z_after

    loop(tiles, body, (roll_up(v[y][tiles]), roll_down(v[z][0])), unroll)
    for q, value in held:
        v[q][tiles] = value


def smooth(v, load_s, load_i, tiles, unroll):
    zeros = jnp.zeros(v[0].shape[1:], F32)

    def first(t, _):
        for q in (0, 3):
            v[q][t] = load_s(q, t) * load_i(q, t)
        return 0

    loop(tiles, first, 0, unroll)
    for q in (1, 2):
        v[q][0] = zeros
        v[q][tiles - 1] = zeros
        v[q][tiles] = load_s(q, tiles) * load_i(q, tiles)
        v[3 * (q - 1)][tiles] = zeros
    half_sweep(v, load_s, load_i, tiles, False, unroll)
    half_sweep(v, load_s, load_i, tiles, True, unroll)
    half_sweep(v, load_s, load_i, tiles, False, unroll)


def residuals(v, load_s, load_d, tiles, c0, c1, keep, unroll):
    lane = lane_ids(v[0].shape[1])

    def body(t, _):
        x = [v[q][t] for q in range(4)]

        def north(q):
            return jnp.where(lane == 0, roll_up(v[q][before(t, tiles)]), roll_up(x[q]))

        def south(q):
            return jnp.where(
                lane == LANES - 1, roll_down(v[q][after(t, tiles)]), roll_down(x[q])
            )

        beside = [
            (x[1] + north(1)) + (x[2] + col_prev(x[2])),
            (x[0] + south(0)) + (x[3] + col_prev(x[3])),
            (x[3] + north(3)) + (x[0] + col_next(x[0])),
            (x[2] + south(2)) + (x[1] + col_next(x[1])),
        ]
        r = [load_s(q, t) - (load_d(q, t) * x[q] - beside[q]) for q in range(4)]
        keep(t, r)
        c0[t] = (col_prev(r[2]) + col_next(r[0])) + 3.0 * (r[0] + r[2])
        c1[t] = (col_prev(r[3]) + col_next(r[1])) + 3.0 * (r[1] + r[3])
        return 0

    loop(tiles, body, 0, unroll)
    body(tiles, 0)


def restricted(c0, c1, t, tiles, rows):
    lane = lane_ids(rows)
    here, other = c0[t, :rows], c1[t, :rows]
    north = jnp.where(lane == 0, roll_up(c1[before(t, tiles), :rows]), roll_up(other))
    south = jnp.where(
        lane == LANES - 1, roll_down(c0[after(t, tiles), :rows]), roll_down(here)
    )
    return ((north + south) + 3.0 * (here + other)) * (1.0 / 16.0)


def fine_kernel(
    s_ref, d_ref, i_ref, d1_ref, from_left, from_right, mates, others,
    r_ref, s1_ref, d1_virtual, d2_virtual, to_left, to_right,
    v0, v1, v2, v3, c0, c1, hs, hd, hi, ps, pd, pi, n1, temp,
):
    v = [v0, v1, v2, v3]
    tiles, rows = s_ref.shape[1], s_ref.shape[2]
    sub = row_ids(8)
    count = lax.axis_size("lon")
    me = lax.axis_index("lon")
    odd = lax.rem(me, 2)
    across = 2 * (1 - me // (count // 2))
    polar_ref = mates.at[odd + across]
    beside = mates.at[1 - odd + across]
    behind = lax.rem(me + count - 1 + odd, count) // (count // 2)
    far = others.at[2 * (1 - behind) + odd]

    def halo(t, _):
        fill_halo(t, from_left, from_right, False, hs, hd, hi)
        return 0

    loop(tiles, halo)
    total = -16.0
    for q in range(4):
        own_s, own_d = polar_unpacked(polar_ref, q)
        beside_s, beside_d = polar_unpacked(beside, q)
        low_s, low_d = polar_unpacked(far.at[:, :8], q)
        high_s, high_d = polar_unpacked(far.at[:, 8:], q)
        left_s = jnp.where(odd == 1, beside_s[rows - 8 :], high_s)
        left_d = jnp.where(odd == 1, beside_d[rows - 8 :], high_d)
        right_s = jnp.where(odd == 1, low_s, beside_s[:8])
        right_d = jnp.where(odd == 1, low_d, beside_d[:8])
        total = total + own_d
        ps[q] = own_s
        pd[q] = own_d
        pi[q] = 1.0 / own_d
        source = jnp.where(sub >= 5, left_s, jnp.where(sub <= 2, right_s, 0.0))
        diag = jnp.where(sub >= 5, left_d, jnp.where(sub <= 2, right_d, 4.0))
        hs[q, tiles] = source
        hd[q, tiles] = diag
        hi[q, tiles] = 1.0 / diag

    load_s = loader(s_ref, hs, ps, tiles)
    smooth(v, load_s, loader(i_ref, hi, pi, tiles), tiles, 8)

    def keep(t, r):
        if not (isinstance(t, int) and t == tiles):
            for q in range(4):
                r_ref[q, t] = r[q][:rows]

    residuals(v, load_s, loader(d_ref, hd, pd, tiles), tiles, c0, c1, keep, 4)

    def coarse(t, _):
        n1[t] = restricted(c0, c1, t, tiles, rows)
        return 0

    loop(tiles, coarse, 0, 8)
    coarse(tiles, 0)

    def edges(t, source, diag, swapped):
        right, left = edge_packs(source, diag, swapped)
        to_right[0, t], to_right[1, t] = right
        to_left[0, t], to_left[1, t] = left

    def use(c, source):
        for q in range(4):
            s1_ref[q, c] = source[q]
        edges(c, source, [d1_ref[q, c] for q in range(4)], False)

    tiles1 = tiles // 2
    split_tiles(lambda t: n1[t], tiles1, rows, splitter(), temp, use)
    out = moved(jnp.concatenate([n1[tiles], total], 0), virtual_splitter())
    source = quarters_of(out[:rows], temp.at[0])
    screen = quarters_of(out[rows:], temp.at[1])
    diag = [4.0 + x for x in screen]
    for q in range(4):
        s1_ref[q, tiles1] = source[q]
        d1_virtual[q] = diag[q]
    d2_virtual[...] = 4.0 + ((screen[0] + screen[1]) + (screen[2] + screen[3]))
    edges(tiles1, source, diag, True)


def merge_kernel(r_ref, out_ref, temp, out_buf, sems):
    tiles = r_ref.shape[1]
    rows = r_ref.shape[2]
    matrix = merger()
    chunk = out_ref.shape[1] // GROUPS
    copies = []
    for group in range(GROUPS):
        for batch in range(tiles // GROUPS // BATCH):
            start = group * (tiles // GROUPS) + batch * BATCH
            both = []
            for i in range(BATCH):
                for pr in (0, 1):
                    for pc in (0, 1):
                        temp[i, pr, pl.ds(pc, rows, 2), :] = r_ref[2 * pc + pr, start + i]
                both.append(jnp.concatenate([temp[i, 0], temp[i, 1]], 1))
            out = moved(jnp.concatenate(both, 0), matrix)
            for i in range(BATCH):
                where = slice((start + i) * 256, (start + i + 1) * 256)
                out_buf[:, where] = out[2 * rows * i : 2 * rows * (i + 1)]
        part = pl.ds(group * chunk, chunk)
        copy = pltpu.make_async_copy(out_buf.at[:, part], out_ref.at[:, part], sems.at[group])
        copy.start()
        copies.append(copy)
    for copy in copies:
        copy.wait()


def middle_kernel(
    merged_first, s_ref, d_ref, i_ref, d_virtual, d2_ref, d2_virtual, from_left, from_right,
    s2_ref, to_left, to_right,
    v0, v1, v2, v3, c0, c1, hs, hd, hi, pi,
):
    v = [v0, v1, v2, v3]
    tiles, rows = d_ref.shape[1], d_ref.shape[2]
    for t in range(tiles + 1):
        fill_halo(t, from_left, from_right, t == tiles, hs, hd, hi)
    for q in range(4):
        pi[q] = 1.0 / d_virtual[q]

    def load_s(q, t):
        return jnp.concatenate([s_ref[q, t], hs[q, t]], 0)

    smooth(v, load_s, loader(i_ref, hi, pi, tiles), tiles, 16)
    residuals(
        v, load_s, loader(d_ref, hd, d_virtual, tiles), tiles, c0, c1, lambda t, r: None, 16
    )
    sub = row_ids(8)
    for t in range(tiles + 1):
        value = restricted(c0, c1, t, tiles, rows)
        diag = d2_virtual[...] if t == tiles else d2_ref[t]
        s2_ref[t] = value
        to_right[t] = jnp.where(sub < 4, roll_rows(value[rows - 8 :], 4), diag[rows - 8 :])
        to_left[t] = jnp.where(sub < 4, value[:8], roll_rows(diag[:8], 4))


def last_kernel(
    s_ref, d_ref, d_virtual, from_left, from_right,
    solution_ref, residual_ref,
    s, d, inv, va, vb,
):
    tiles, own = d_ref.shape[0], d_ref.shape[1]
    rows = own + 8
    sub = row_ids(8)
    lane, row = lane_ids(rows), row_ids(rows)
    even = (lane + row) % 2 == 0
    odd = jnp.logical_not(even)
    for t in range(tiles + 1):
        left, right = from_left[t], from_right[t]
        diag = d_virtual[...] if t == tiles else d_ref[t]
        source = jnp.concatenate(
            [s_ref[t], jnp.where(sub < 4, right, roll_rows(left, 4))], 0
        )
        diag = jnp.concatenate([diag, jnp.where(sub < 4, roll_rows(right, 4), left)], 0)
        inverse = 1.0 / diag
        s[t] = source
        d[t] = diag
        inv[t] = inverse
        va[t] = jnp.where(odd if t == tiles else even, source * inverse, 0.0)

    def beside(v, t):
        x = v[t]
        north = jnp.where(lane == 0, roll_up(v[before(t, tiles)]), roll_up(x))
        south = jnp.where(lane == LANES - 1, roll_down(v[after(t, tiles)]), roll_down(x))
        return (col_prev(x) + col_next(x)) + (north + south)

    old, new = va, vb
    for mask, other in ((odd, even), (even, odd), (odd, even)):
        for t in range(tiles + 1):
            value = (s[t] + beside(old, t)) * inv[t]
            new[t] = jnp.where(other if t == tiles else mask, value, old[t])
        old, new = new, old
    for t in range(tiles):
        x = old[t]
        r = s[t] - (d[t] * x - beside(old, t))
        where = slice(t * LANES, (t + 1) * LANES)
        solution_ref[:, where] = x[:own]
        residual_ref[:, where] = r[:own]


VMEM = pl.BlockSpec(memory_space=pltpu.VMEM)
HBM = pl.BlockSpec(memory_space=pltpu.HBM)


def call(kernel, out_shapes, scratch, *args, sems=None, far_in=0, far_out=0):
    scratch = [pltpu.VMEM(x, F32) if isinstance(x, tuple) else x for x in scratch]
    if sems is not None:
        scratch.append(pltpu.SemaphoreType.DMA(sems))
    return pl.pallas_call(
        kernel,
        out_shape=[jax.ShapeDtypeStruct(shape, F32) for shape in out_shapes],
        in_specs=[HBM] * far_in + [VMEM] * (len(args) - far_in),
        out_specs=[HBM] * far_out + [VMEM] * (len(out_shapes) - far_out),
        scratch_shapes=scratch,
        compiler_params=pltpu.CompilerParams(vmem_limit_bytes=40 * 2**20),
        cost_estimate=pl.CostEstimate(flops=2**10, bytes_accessed=2**10, transcendentals=0),
    )(*args)


def shifted(x, by):
    count = lax.axis_size("lon")
    return lax.ppermute(x, "lon", [(i, (i + by) % count) for i in range(count)])


def body(right_side, texel_weight, seam_flags):
    columns, height = right_side.shape
    half_turn = lax.axis_size("lon") // 2
    tiles, rows = height // 256, columns // 2
    tiles1, rows1 = tiles // 2, rows // 2
    temp = (BATCH, 2, columns, LANES)
    right_side = pltpu.with_memory_space_constraint(right_side, pltpu.HBM)
    texel_weight = pltpu.with_memory_space_constraint(texel_weight, pltpu.HBM)

    polar, corners = call(
        polar_kernel,
        [(2, rows, LANES), (2, 16, LANES)],
        [(2, columns, 256), pltpu.VMEM((2, columns, 256), BF16)] + [(2, 2, columns, LANES)] * 2,
        right_side, texel_weight, seam_flags,
        sems=(2, 2), far_in=2,
    )
    count = lax.axis_size("lon")
    pairs = [(i, i + 1, i + half_turn, i + half_turn + 1) for i in range(half_turn)]
    groups = [[i % count for i in pair] for pair in pairs]
    mates = lax.all_gather(polar, "lon", axis_index_groups=groups[0::2])
    others = lax.all_gather(corners, "lon", axis_index_groups=groups[1::2])

    quarters = (4, tiles, rows, LANES)
    s, d, e, to_left, to_right = call(
        prepare_kernel,
        [quarters, quarters, quarters[1:], (2, tiles, 8, LANES), (2, tiles, 8, LANES)],
        [(columns, height), pltpu.VMEM((columns, height), BF16), temp, temp, (tiles, 8, LANES)],
        right_side, texel_weight, polar, seam_flags,
        sems=(2, GROUPS), far_in=3,
    )
    from_left = shifted(to_right, 1)
    from_right = shifted(to_left, -1)
    quarters1 = (4, tiles1, rows1, LANES)
    inverse, d1, i1, d2 = call(
        screens_kernel,
        [quarters, quarters1, quarters1, quarters1[1:]],
        [(BATCH, 2, rows, LANES)],
        d, e,
    )

    def level_scratch(tiles, rows):
        halo = (4, tiles + 1, 8, LANES)
        return [(tiles + 1, rows + 8, LANES)] * 6 + [halo] * 3

    pack1 = (2, tiles1 + 1, 8, LANES)
    r, s1, d1_virtual, d2_virtual, to_left, to_right = call(
        fine_kernel,
        [quarters, (4, tiles1 + 1, rows1, LANES), (4, rows1, LANES), (rows1, LANES), pack1, pack1],
        level_scratch(tiles, rows)
        + [(4, rows, LANES)] * 3
        + [(tiles + 1, rows, LANES), (BATCH, 2, rows, LANES)],
        s, d, inverse, d1, from_left, from_right, mates, others,
    )
    from_left = shifted(to_right, 1)
    from_right = shifted(to_left, -1)
    (fine_residual,) = call(
        merge_kernel, [(columns, height)], [temp, (columns, height)], r,
        sems=(GROUPS,), far_out=1,
    )
    pack2 = (tiles1 + 1, 8, LANES)
    s2, to_left, to_right = call(
        middle_kernel,
        [(tiles1 + 1, rows1, LANES), pack2, pack2],
        level_scratch(tiles1, rows1) + [(4, rows1, LANES)],
        fine_residual, s1, d1, i1, d1_virtual, d2, d2_virtual, from_left, from_right,
        far_in=1,
    )
    from_left = shifted(to_right, 1)
    from_right = shifted(to_left, -1)
    solution_2, residual_2 = call(
        last_kernel,
        [(columns // 4, height // 4)] * 2,
        [(tiles1 + 1, rows1 + 8, LANES)] * 5,
        s2, d2, d2_virtual, from_left, from_right,
    )
    return fine_residual, solution_2, residual_2


def solution(mesh):
    spec = P(("groups", "lon"), None)
    return jax.shard_map(
        body, mesh=mesh, in_specs=(spec,) * 3, out_specs=(spec,) * 3, check_vma=False
    )
```

```python
import jax
import jax.numpy as jnp
from jax import lax
from jax.experimental import pallas as pl
from jax.experimental.pallas import tpu as pltpu
from jax.sharding import PartitionSpec as P

TILE = 32
SEAM_SCALE = 0.1
LANES = 128
GROUPS = 4
BATCH = 4
F32 = jnp.float32
BF16 = jnp.bfloat16


def loop(count, body, carry=0, unroll=4):
    unroll = min(unroll, count)

    def steps(block, carry):
        for i in range(unroll):
            carry = body(block * unroll + i, carry)
        return carry

    whole = count // unroll
    carry = steps(0, carry) if whole == 1 else lax.fori_loop(0, whole, steps, carry)
    for t in range(whole * unroll, count):
        carry = body(t, carry)
    return carry


def before(t, tiles):
    return (tiles if t == 0 else t - 1) if isinstance(t, int) else jnp.where(t == 0, tiles, t - 1)


def after(t, tiles):
    return (0 if t == tiles else t + 1) if isinstance(t, int) else t + 1


def lane_ids(rows):
    return lax.broadcasted_iota(jnp.int32, (rows, LANES), 1)


def row_ids(rows):
    return lax.broadcasted_iota(jnp.int32, (rows, LANES), 0)


def roll_up(x):
    return pltpu.roll(x, 1, 1)


def roll_down(x):
    return pltpu.roll(x, LANES - 1, 1)


def roll_rows(x, by):
    by %= x.shape[0]
    return x if by == 0 else pltpu.roll(x, by, 0)


def roll_lanes(x, by):
    by %= LANES
    return x if by == 0 else pltpu.roll(x, by, 1)


def col_prev(x):
    return pltpu.roll(x, 1, 0)


def col_next(x):
    return pltpu.roll(x, x.shape[0] - 1, 0)


def selector(shape, rule):
    a = lax.broadcasted_iota(jnp.int32, shape, 0)
    b = lax.broadcasted_iota(jnp.int32, shape, 1)
    return jnp.where(rule(a, b), 1.0, 0.0).astype(BF16)


def splitter():
    return selector((256, 256), lambda a, b: a == 2 * (b % LANES) + b // LANES)


def merger():
    return selector((256, 256), lambda a, b: b == 2 * (a % LANES) + a // LANES)


def virtual_splitter():
    return selector(
        (LANES, 256),
        lambda a, b: a // 2 + jnp.where(a >= 64, 64, 0) + LANES * (a % 2) == b,
    )


def moved(x, matrix, exact=None):
    rows = x.shape[0]
    high = x.astype(BF16)
    low = (x - high.astype(F32)).astype(BF16)
    terms = [high, low] if exact is None else [high, low, exact]
    out = jnp.dot(jnp.concatenate(terms, 0), matrix, preferred_element_type=F32)
    both = out[:rows] + out[rows : 2 * rows]
    return both if exact is None else (both, out[2 * rows :])


def quarters_of(parts, temp):
    count = parts.shape[0] // 2
    temp[0] = parts[:, :LANES]
    temp[1] = parts[:, LANES:]
    return [temp[pr, pl.ds(pc, count, 2), :] for pc in (0, 1) for pr in (0, 1)]


def reds(swapped):
    return (1, 2) if swapped else (0, 3)


def interleaved(group, offset):
    sub = row_ids(8)
    packed = roll_rows(group[0], offset)
    for q in range(1, 4):
        packed = jnp.where(sub // 2 == q, roll_rows(group[q], 2 * q + offset), packed)
    return packed


def edge_packs(source, diag, swapped):
    sub = row_ids(8)
    even, odd = reds(swapped)
    rows = source[0].shape[0]
    packs = []
    for here, first, second, row, step in (
        (slice(rows - 8, rows), even, odd, 6, 1),
        (slice(0, 8), odd, even, 1, -1),
    ):
        gs = [x[here] for x in source]
        gd = [x[here] for x in diag]
        near = gs[first] / gd[first]
        far = roll_rows(gs[second] / gd[second], step)
        gs[first] = jnp.where(sub == row, near, gs[first])
        gd[first] = jnp.where(sub == row, far, gd[first])
        offset = 2 if row == 6 else 0
        packs.append((interleaved(gs, offset), interleaved(gd, offset)))
    return packs


def unpacked_halo(left, right, swapped):
    sub = row_ids(8)
    even, odd = reds(swapped)
    (al, bl), (ar, br) = left, right
    source, diag = [], []
    for q in range(4):
        s = jnp.where(
            sub >= 6,
            roll_rows(al, 6 - 2 * q),
            jnp.where(sub <= 1, roll_rows(ar, -2 * q), 0.0),
        )
        d = jnp.where(
            sub >= 6,
            roll_rows(bl, 6 - 2 * q),
            jnp.where(sub <= 1, roll_rows(br, -2 * q), 4.0),
        )
        if q == even:
            s = jnp.where(sub == 2, roll_rows(br, 1 - 2 * odd), s)
            d = jnp.where((sub == 2) | (sub == 6), 1.0, d)
        if q == odd:
            s = jnp.where(sub == 5, roll_rows(bl, 5 - 2 * even), s)
            d = jnp.where((sub == 5) | (sub == 1), 1.0, d)
        source.append(s)
        diag.append(d)
    return source, diag


def is_odd():
    return lax.rem(lax.axis_index("lon"), 2) == 1


def chosen(odd, a, b):
    return jnp.where(odd, a, b), jnp.where(odd, b, a)


def store_edges(t, packs, odd, to_mate, to_other):
    right, left = packs
    for i in (0, 1):
        to_mate[i, t], to_other[i, t] = chosen(odd, left[i], right[i])


def fill_halo(t, from_mate, from_other, odd, swapped, hs, hd, hi):
    al, ar = chosen(odd, from_mate[0, t], from_other[0, t])
    bl, br = chosen(odd, from_mate[1, t], from_other[1, t])
    source, diag = unpacked_halo((al, bl), (ar, br), swapped)
    for q in range(4):
        hs[q, t] = source[q]
        hd[q, t] = diag[q]
        hi[q, t] = 1.0 / diag[q]


def loader(own, halo, virtual, tiles):
    def load(q, t):
        if isinstance(t, int) and t == tiles:
            return jnp.concatenate([virtual[q], halo[q, t]], 0)
        return jnp.concatenate([own[q, t], halo[q, t]], 0)

    return load


def polar_packs(tiles_of):
    lane = lane_ids(tiles_of[0][0].shape[0])
    packs = []
    for pc in (0, 1):
        parts = [*tiles_of[2 * pc], *tiles_of[2 * pc + 1]]
        packed = parts[0]
        for m in range(1, 4):
            mine = (lane + (16 - 32 * m) % LANES) % LANES < 32
            packed = jnp.where(mine, roll_lanes(parts[m], 32 * m), packed)
        packs.append(packed)
    return packs


def polar_unpacked(x, q):
    lane = lane_ids(x.shape[1])
    used = (lane < 16) | (lane >= LANES - 16)
    m = 2 * (q % 2)
    return (
        jnp.where(used, roll_lanes(x[q // 2], 32 * m), 0.0),
        jnp.where(used, roll_lanes(x[q // 2], 32 * (m + 1)), 4.0),
    )


def prepare_kernel(
    right_ref, weight_ref, flag_ref,
    s_ref, d_ref, e_ref, to_mate, to_other, polar_ref, corner_near, corner_far,
    right_buf, weight_buf, flag_buf, temp_s, temp_d, scale_ref, sems,
):
    flag_copy = pltpu.make_async_copy(flag_ref, flag_buf, sems.at[0, GROUPS])
    flag_copy.start()
    odd = is_odd()
    tiles, rows = s_ref.shape[1], s_ref.shape[2]
    chunk = right_ref.shape[1] // GROUPS
    copies = []
    for group in range(GROUPS):
        part = pl.ds(group * chunk, chunk)
        copies.append(
            [
                pltpu.make_async_copy(src.at[:, part], dst.at[:, part], sems.at[i, group])
                for i, (src, dst) in enumerate(((right_ref, right_buf), (weight_ref, weight_buf)))
            ]
        )
        for copy in copies[group]:
            copy.start()
    flag_copy.wait()
    flag_cols = flag_ref.shape[0]
    flag_lats = flag_ref.shape[1]
    per_tile = rows // flag_cols
    matrix = splitter()
    flags = jnp.concatenate(
        [flag_buf[...].astype(F32), jnp.zeros((8 - flag_cols, flag_lats), F32)], 0
    )
    lat = lax.broadcasted_iota(jnp.int32, (8, flag_lats), 1)
    stacked = jnp.concatenate(
        [jnp.where(lat // 8 == c, flags, 0.0) for c in range(tiles)], 0
    ).astype(BF16)
    spread = selector((flag_lats, LANES), lambda a, b: a % 8 == b // (TILE // 2))
    spread_flags = jnp.dot(stacked, spread, preferred_element_type=F32)
    scale_ref[...] = jnp.where(spread_flags > 0.5, SEAM_SCALE, 1.0).reshape(tiles, 8, LANES)

    def piece(c, source, weight):
        scales = scale_ref[c]
        scale = jnp.concatenate(
            [jnp.broadcast_to(scales[i : i + 1], (per_tile, LANES)) for i in range(flag_cols)], 0
        )
        screen = [w * scale for w in weight]
        e_ref[c] = (screen[0] + screen[1]) + (screen[2] + screen[3])
        diag = [4.0 + s for s in screen]
        for q in range(4):
            s_ref[q, c] = source[q]
            d_ref[q, c] = diag[q]
        store_edges(c, edge_packs(source, diag, False), odd, to_mate, to_other)

    columns = right_ref.shape[0]
    for group in range(GROUPS):
        for copy in copies[group]:
            copy.wait()
        for batch in range(tiles // GROUPS // BATCH):
            start = group * (tiles // GROUPS) + batch * BATCH
            lanes = [slice((start + i) * 256, (start + i + 1) * 256) for i in range(BATCH)]
            source = jnp.concatenate([right_buf[:, w] for w in lanes], 0)
            weight = jnp.concatenate([weight_buf[:, w] for w in lanes], 0)
            source, weight = moved(source, matrix, weight)
            for i in range(BATCH):
                here = slice(i * columns, (i + 1) * columns)
                piece(
                    start + i,
                    quarters_of(source[here], temp_s.at[i]),
                    quarters_of(weight[here], temp_d.at[i]),
                )

    mirror = selector((LANES, LANES), lambda a, b: a + b == LANES - 1)
    lane = lane_ids(rows)
    ends = [
        [jnp.where(lane >= 64, ref[q ^ 1, tiles - 1], ref[q ^ 1, 0]) for ref in (s_ref, d_ref)]
        for q in range(4)
    ]
    both = moved(jnp.concatenate(polar_packs(ends), 0), mirror)
    for pc in (0, 1):
        pack = both[pc * rows : (pc + 1) * rows]
        polar_ref[pc] = pack
        corner_near[pc], corner_far[pc] = chosen(odd, pack[:8], pack[rows - 8 :])


def split_tiles(load, tiles, rows, matrix, temp, use):
    for start in range(0, tiles, BATCH):
        wide = [
            jnp.concatenate([load(2 * c), load(2 * c + 1)], 1)
            for c in range(start, start + BATCH)
        ]
        out = moved(jnp.concatenate(wide, 0), matrix)
        for i in range(BATCH):
            use(start + i, quarters_of(out[i * rows : (i + 1) * rows], temp.at[i]))


def screens_kernel(d_ref, e_ref, i_ref, d1_ref, i1_ref, d2_ref, temp):
    def inverse(t, _):
        for q in range(4):
            i_ref[q, t] = 1.0 / d_ref[q, t]
        return 0

    loop(d_ref.shape[1], inverse)

    def use(c, screen):
        for q in range(4):
            d1_ref[q, c] = 4.0 + screen[q]
            i1_ref[q, c] = 1.0 / (4.0 + screen[q])
        d2_ref[c] = 4.0 + ((screen[0] + screen[1]) + (screen[2] + screen[3]))

    tiles, rows = d1_ref.shape[1], e_ref.shape[1]
    split_tiles(lambda t: e_ref[t], tiles, rows, splitter(), temp, use)


def half_sweep(v, load_s, load_i, tiles, red, unroll):
    rows = v[0].shape[1]
    lane = lane_ids(rows)
    y, z, qa, qb = (1, 2, 0, 3) if red else (3, 0, 2, 1)
    col_a, col_b = (col_prev, col_next) if red else (col_next, col_prev)

    def beside_virtual(q):
        ns, we = q ^ 1, q ^ 2
        here = v[ns][tiles]
        if q % 2 == 0:
            lat = jnp.where(lane == 0, roll_up(v[ns][tiles - 1]), roll_up(here))
        else:
            lat = jnp.where(lane == LANES - 1, roll_down(v[ns][0]), roll_down(here))
        cols = v[we][tiles]
        return (here + lat) + (cols + (col_prev if q < 2 else col_next)(cols))

    held = [
        (q, (load_s(q, tiles) + beside_virtual(q)) * load_i(q, tiles)) for q in (y, z)
    ]

    def body(t, carry):
        y_before, z_here = carry
        vy, vz = v[y][t], v[z][t]
        y_here = roll_up(vy)
        z_after = roll_down(v[z][t + 1])
        lat_a = vy + jnp.where(lane == 0, y_before, y_here)
        lat_b = vz + jnp.where(lane == LANES - 1, z_after, z_here)
        v[qa][t] = (load_s(qa, t) + (lat_a + (vz + col_a(vz)))) * load_i(qa, t)
        v[qb][t] = (load_s(qb, t) + (lat_b + (vy + col_b(vy)))) * load_i(qb, t)
        return y_here, z_after

    loop(tiles, body, (roll_up(v[y][tiles]), roll_down(v[z][0])), unroll)
    for q, value in held:
        v[q][tiles] = value


def smooth(v, load_s, load_i, tiles, unroll):
    zeros = jnp.zeros(v[0].shape[1:], F32)

    def first(t, _):
        for q in (0, 3):
            v[q][t] = load_s(q, t) * load_i(q, t)
        return 0

    loop(tiles, first, 0, unroll)
    for q in (1, 2):
        v[q][0] = zeros
        v[q][tiles - 1] = zeros
        v[q][tiles] = load_s(q, tiles) * load_i(q, tiles)
        v[3 * (q - 1)][tiles] = zeros
    half_sweep(v, load_s, load_i, tiles, False, unroll)
    half_sweep(v, load_s, load_i, tiles, True, unroll)
    half_sweep(v, load_s, load_i, tiles, False, unroll)


def residuals(v, load_s, load_d, tiles, c0, c1, keep, unroll):
    lane = lane_ids(v[0].shape[1])

    def body(t, _):
        x = [v[q][t] for q in range(4)]

        def north(q):
            return jnp.where(lane == 0, roll_up(v[q][before(t, tiles)]), roll_up(x[q]))

        def south(q):
            return jnp.where(
                lane == LANES - 1, roll_down(v[q][after(t, tiles)]), roll_down(x[q])
            )

        beside = [
            (x[1] + north(1)) + (x[2] + col_prev(x[2])),
            (x[0] + south(0)) + (x[3] + col_prev(x[3])),
            (x[3] + north(3)) + (x[0] + col_next(x[0])),
            (x[2] + south(2)) + (x[1] + col_next(x[1])),
        ]
        r = [load_s(q, t) - (load_d(q, t) * x[q] - beside[q]) for q in range(4)]
        keep(t, r)
        c0[t] = (col_prev(r[2]) + col_next(r[0])) + 3.0 * (r[0] + r[2])
        c1[t] = (col_prev(r[3]) + col_next(r[1])) + 3.0 * (r[1] + r[3])
        return 0

    loop(tiles, body, 0, unroll)
    body(tiles, 0)


def restricted(c0, c1, t, tiles, rows):
    lane = lane_ids(rows)
    here, other = c0[t, :rows], c1[t, :rows]
    north = jnp.where(lane == 0, roll_up(c1[before(t, tiles), :rows]), roll_up(other))
    south = jnp.where(
        lane == LANES - 1, roll_down(c0[after(t, tiles), :rows]), roll_down(here)
    )
    return ((north + south) + 3.0 * (here + other)) * (1.0 / 16.0)


def fine_kernel(
    s_ref, d_ref, i_ref, d1_ref, from_mate, from_other, polar_ref, corner_near, corner_far,
    r_ref, s1_ref, d1_virtual, d2_virtual, to_mate, to_other,
    v0, v1, v2, v3, c0, c1, hs, hd, hi, ps, pd, pi, n1, temp,
):
    v = [v0, v1, v2, v3]
    tiles, rows = s_ref.shape[1], s_ref.shape[2]
    sub = row_ids(8)
    odd = is_odd()

    def halo(t, _):
        fill_halo(t, from_mate, from_other, odd, False, hs, hd, hi)
        return 0

    loop(tiles, halo)
    total = -16.0
    for q in range(4):
        own_s, own_d = polar_unpacked(polar_ref, q)
        near_s, near_d = polar_unpacked(corner_near, q)
        far_s, far_d = polar_unpacked(corner_far, q)
        left_s, right_s = chosen(odd, near_s, far_s)
        left_d, right_d = chosen(odd, near_d, far_d)
        total = total + own_d
        ps[q] = own_s
        pd[q] = own_d
        pi[q] = 1.0 / own_d
        source = jnp.where(sub >= 5, left_s, jnp.where(sub <= 2, right_s, 0.0))
        diag = jnp.where(sub >= 5, left_d, jnp.where(sub <= 2, right_d, 4.0))
        hs[q, tiles] = source
        hd[q, tiles] = diag
        hi[q, tiles] = 1.0 / diag

    load_s = loader(s_ref, hs, ps, tiles)
    smooth(v, load_s, loader(i_ref, hi, pi, tiles), tiles, 16)

    def keep(t, r):
        if not (isinstance(t, int) and t == tiles):
            for q in range(4):
                r_ref[q, t] = r[q][:rows]

    residuals(v, load_s, loader(d_ref, hd, pd, tiles), tiles, c0, c1, keep, 8)

    def coarse(t, _):
        n1[t] = restricted(c0, c1, t, tiles, rows)
        return 0

    loop(tiles, coarse, 0, 8)
    coarse(tiles, 0)

    def edges(t, source, diag, swapped):
        store_edges(t, edge_packs(source, diag, swapped), odd, to_mate, to_other)

    def use(c, source):
        for q in range(4):
            s1_ref[q, c] = source[q]
        edges(c, source, [d1_ref[q, c] for q in range(4)], False)

    tiles1 = tiles // 2
    split_tiles(lambda t: n1[t], tiles1, rows, splitter(), temp, use)
    out = moved(jnp.concatenate([n1[tiles], total], 0), virtual_splitter())
    source = quarters_of(out[:rows], temp.at[0])
    screen = quarters_of(out[rows:], temp.at[1])
    diag = [4.0 + x for x in screen]
    for q in range(4):
        s1_ref[q, tiles1] = source[q]
        d1_virtual[q] = diag[q]
    d2_virtual[...] = 4.0 + ((screen[0] + screen[1]) + (screen[2] + screen[3]))
    edges(tiles1, source, diag, True)


def merge_kernel(r_ref, out_ref, temp, out_buf, sems):
    tiles = r_ref.shape[1]
    rows = r_ref.shape[2]
    matrix = merger()
    chunk = out_ref.shape[1] // GROUPS
    copies = []
    for group in range(GROUPS):
        for batch in range(tiles // GROUPS // BATCH):
            start = group * (tiles // GROUPS) + batch * BATCH
            both = []
            for i in range(BATCH):
                for pr in (0, 1):
                    for pc in (0, 1):
                        temp[i, pr, pl.ds(pc, rows, 2), :] = r_ref[2 * pc + pr, start + i]
                both.append(jnp.concatenate([temp[i, 0], temp[i, 1]], 1))
            out = moved(jnp.concatenate(both, 0), matrix)
            for i in range(BATCH):
                where = slice((start + i) * 256, (start + i + 1) * 256)
                out_buf[:, where] = out[2 * rows * i : 2 * rows * (i + 1)]
        part = pl.ds(group * chunk, chunk)
        copy = pltpu.make_async_copy(out_buf.at[:, part], out_ref.at[:, part], sems.at[group])
        copy.start()
        copies.append(copy)
    for copy in copies:
        copy.wait()


def middle_kernel(
    merged_first, s_ref, d_ref, i_ref, d_virtual, d2_ref, d2_virtual, from_mate, from_other,
    s2_ref, to_mate, to_other,
    v0, v1, v2, v3, c0, c1, hs, hd, hi, pi,
):
    v = [v0, v1, v2, v3]
    tiles, rows = d_ref.shape[1], d_ref.shape[2]
    odd = is_odd()
    for t in range(tiles + 1):
        fill_halo(t, from_mate, from_other, odd, t == tiles, hs, hd, hi)
    for q in range(4):
        pi[q] = 1.0 / d_virtual[q]

    def load_s(q, t):
        return jnp.concatenate([s_ref[q, t], hs[q, t]], 0)

    smooth(v, load_s, loader(i_ref, hi, pi, tiles), tiles, 16)
    residuals(
        v, load_s, loader(d_ref, hd, d_virtual, tiles), tiles, c0, c1, lambda t, r: None, 16
    )
    sub = row_ids(8)
    for t in range(tiles + 1):
        value = restricted(c0, c1, t, tiles, rows)
        diag = d2_virtual[...] if t == tiles else d2_ref[t]
        s2_ref[t] = value
        right = jnp.where(sub < 4, roll_rows(value[rows - 8 :], 4), diag[rows - 8 :])
        left = jnp.where(sub < 4, value[:8], roll_rows(diag[:8], 4))
        to_mate[t], to_other[t] = chosen(odd, left, right)


def last_kernel(
    s_ref, d_ref, d_virtual, from_mate, from_other,
    solution_ref, residual_ref,
    s, d, inv, va, vb,
):
    tiles, own = d_ref.shape[0], d_ref.shape[1]
    rows = own + 8
    sub = row_ids(8)
    lane, row = lane_ids(rows), row_ids(rows)
    even = (lane + row) % 2 == 0
    odd = jnp.logical_not(even)
    odd_band = is_odd()
    for t in range(tiles + 1):
        left, right = chosen(odd_band, from_mate[t], from_other[t])
        diag = d_virtual[...] if t == tiles else d_ref[t]
        source = jnp.concatenate(
            [s_ref[t], jnp.where(sub < 4, right, roll_rows(left, 4))], 0
        )
        diag = jnp.concatenate([diag, jnp.where(sub < 4, roll_rows(right, 4), left)], 0)
        inverse = 1.0 / diag
        s[t] = source
        d[t] = diag
        inv[t] = inverse
        va[t] = jnp.where(odd if t == tiles else even, source * inverse, 0.0)

    def beside(v, t):
        x = v[t]
        north = jnp.where(lane == 0, roll_up(v[before(t, tiles)]), roll_up(x))
        south = jnp.where(lane == LANES - 1, roll_down(v[after(t, tiles)]), roll_down(x))
        return (col_prev(x) + col_next(x)) + (north + south)

    old, new = va, vb
    for mask, other in ((odd, even), (even, odd), (odd, even)):
        for t in range(tiles + 1):
            value = (s[t] + beside(old, t)) * inv[t]
            new[t] = jnp.where(other if t == tiles else mask, value, old[t])
        old, new = new, old
    for t in range(tiles):
        x = old[t]
        r = s[t] - (d[t] * x - beside(old, t))
        where = slice(t * LANES, (t + 1) * LANES)
        solution_ref[:, where] = x[:own]
        residual_ref[:, where] = r[:own]


VMEM = pl.BlockSpec(memory_space=pltpu.VMEM)
HBM = pl.BlockSpec(memory_space=pltpu.HBM)


def call(kernel, out_shapes, scratch, *args, sems=None, far_in=0, far_out=0):
    scratch = [pltpu.VMEM(x, F32) if isinstance(x, tuple) else x for x in scratch]
    if sems is not None:
        scratch.append(pltpu.SemaphoreType.DMA(sems))
    return pl.pallas_call(
        kernel,
        out_shape=[jax.ShapeDtypeStruct(shape, F32) for shape in out_shapes],
        in_specs=[HBM] * far_in + [VMEM] * (len(args) - far_in),
        out_specs=[HBM] * far_out + [VMEM] * (len(out_shapes) - far_out),
        scratch_shapes=scratch,
        compiler_params=pltpu.CompilerParams(vmem_limit_bytes=40 * 2**20),
    )(*args)


def swapped_with(x, by):
    count = lax.axis_size("lon")
    pairs = [(i, (i + by) % count) for i in range(0, count, 2)]
    return lax.ppermute(x, "lon", pairs + [(b, a) for a, b in pairs])


def swapped_edges(to_mate, to_other):
    from_other = swapped_with(to_other, -1)
    return swapped_with(to_mate, 1), from_other


def body(right_side, texel_weight, seam_flags):
    columns, height = right_side.shape
    half_turn = lax.axis_size("lon") // 2
    tiles, rows = height // 256, columns // 2
    tiles1, rows1 = tiles // 2, rows // 2
    temp = (BATCH, 2, columns, LANES)
    right_side = pltpu.with_memory_space_constraint(right_side, pltpu.HBM)
    texel_weight = pltpu.with_memory_space_constraint(texel_weight, pltpu.HBM)
    seam_flags = pltpu.with_memory_space_constraint(seam_flags, pltpu.HBM)

    quarters = (4, tiles, rows, LANES)
    s, d, e, to_mate, to_other, polar, corner_near, corner_far = call(
        prepare_kernel,
        [quarters, quarters, quarters[1:], (2, tiles, 8, LANES), (2, tiles, 8, LANES)]
        + [(2, rows, LANES), (2, 8, LANES), (2, 8, LANES)],
        [(columns, height), pltpu.VMEM((columns, height), BF16)]
        + [pltpu.VMEM(seam_flags.shape, jnp.int32), temp, temp, (tiles, 8, LANES)],
        right_side, texel_weight, seam_flags,
        sems=(2, GROUPS + 1), far_in=3,
    )
    from_mate, from_other = swapped_edges(to_mate, to_other)
    polar = lax.ppermute(
        polar, "lon", [(i, (i + half_turn) % (2 * half_turn)) for i in range(2 * half_turn)]
    )
    corner_far = swapped_with(corner_far, half_turn - 1)
    corner_near = swapped_with(corner_near, half_turn + 1)
    quarters1 = (4, tiles1, rows1, LANES)
    inverse, d1, i1, d2 = call(
        screens_kernel,
        [quarters, quarters1, quarters1, quarters1[1:]],
        [(BATCH, 2, rows, LANES)],
        d, e,
    )

    def level_scratch(tiles, rows):
        halo = (4, tiles + 1, 8, LANES)
        return [(tiles + 1, rows + 8, LANES)] * 6 + [halo] * 3

    pack1 = (2, tiles1 + 1, 8, LANES)
    r, s1, d1_virtual, d2_virtual, to_mate, to_other = call(
        fine_kernel,
        [quarters, (4, tiles1 + 1, rows1, LANES), (4, rows1, LANES), (rows1, LANES), pack1, pack1],
        level_scratch(tiles, rows)
        + [(4, rows, LANES)] * 3
        + [(tiles + 1, rows, LANES), (BATCH, 2, rows, LANES)],
        s, d, inverse, d1, from_mate, from_other, polar, corner_near, corner_far,
    )
    from_mate, from_other = swapped_edges(to_mate, to_other)
    (fine_residual,) = call(
        merge_kernel, [(columns, height)], [temp, (columns, height)], r,
        sems=(GROUPS,), far_out=1,
    )
    pack2 = (tiles1 + 1, 8, LANES)
    s2, to_mate, to_other = call(
        middle_kernel,
        [(tiles1 + 1, rows1, LANES), pack2, pack2],
        level_scratch(tiles1, rows1) + [(4, rows1, LANES)],
        pltpu.with_memory_space_constraint(fine_residual, pltpu.HBM),
        s1, d1, i1, d1_virtual, d2, d2_virtual, from_mate, from_other,
        far_in=1,
    )
    from_mate, from_other = swapped_edges(to_mate, to_other)
    solution_2, residual_2 = call(
        last_kernel,
        [(columns // 4, height // 4)] * 2,
        [(tiles1 + 1, rows1 + 8, LANES)] * 5,
        s2, d2, d2_virtual, from_mate, from_other,
    )
    return fine_residual, solution_2, residual_2


def solution(mesh):
    spec = P(("groups", "lon"), None)
    return jax.shard_map(
        body, mesh=mesh, in_specs=(spec,) * 3, out_specs=(spec,) * 3, check_vma=False
    )
```

```python
import jax
import jax.numpy as jnp
from jax import lax
from jax.experimental import pallas as pl
from jax.experimental.pallas import tpu as pltpu
from jax.sharding import PartitionSpec as P

TILE = 32
SEAM_SCALE = 0.1
LANES = 128
GROUPS = 4
BATCH = 4
F32 = jnp.float32
BF16 = jnp.bfloat16


def loop(count, body, carry=0, unroll=4):
    unroll = min(unroll, count)

    def steps(block, carry):
        for i in range(unroll):
            carry = body(block * unroll + i, carry)
        return carry

    whole = count // unroll
    carry = steps(0, carry) if whole == 1 else lax.fori_loop(0, whole, steps, carry)
    for t in range(whole * unroll, count):
        carry = body(t, carry)
    return carry


def before(t, tiles):
    return (tiles if t == 0 else t - 1) if isinstance(t, int) else jnp.where(t == 0, tiles, t - 1)


def after(t, tiles):
    return (0 if t == tiles else t + 1) if isinstance(t, int) else t + 1


def lane_ids(rows):
    return lax.broadcasted_iota(jnp.int32, (rows, LANES), 1)


def row_ids(rows):
    return lax.broadcasted_iota(jnp.int32, (rows, LANES), 0)


def roll_up(x):
    return pltpu.roll(x, 1, 1)


def roll_down(x):
    return pltpu.roll(x, LANES - 1, 1)


def roll_rows(x, by):
    by %= x.shape[0]
    return x if by == 0 else pltpu.roll(x, by, 0)


def roll_lanes(x, by):
    by %= LANES
    return x if by == 0 else pltpu.roll(x, by, 1)


def col_prev(x):
    return pltpu.roll(x, 1, 0)


def col_next(x):
    return pltpu.roll(x, x.shape[0] - 1, 0)


def selector(shape, rule):
    a = lax.broadcasted_iota(jnp.int32, shape, 0)
    b = lax.broadcasted_iota(jnp.int32, shape, 1)
    return jnp.where(rule(a, b), 1.0, 0.0).astype(BF16)


def splitter():
    return selector((256, 256), lambda a, b: a == 2 * (b % LANES) + b // LANES)


def merger():
    return selector((256, 256), lambda a, b: b == 2 * (a % LANES) + a // LANES)


def virtual_splitter():
    return selector(
        (LANES, 256),
        lambda a, b: a // 2 + jnp.where(a >= 64, 64, 0) + LANES * (a % 2) == b,
    )


def moved(x, matrix, exact=None):
    rows = x.shape[0]
    high = x.astype(BF16)
    low = (x - high.astype(F32)).astype(BF16)
    terms = [high, low] if exact is None else [high, low, exact]
    out = jnp.dot(jnp.concatenate(terms, 0), matrix, preferred_element_type=F32)
    both = out[:rows] + out[rows : 2 * rows]
    return both if exact is None else (both, out[2 * rows :])


def quarters_of(parts, temp):
    count = parts.shape[0] // 2
    temp[0] = parts[:, :LANES]
    temp[1] = parts[:, LANES:]
    return [temp[pr, pl.ds(pc, count, 2), :] for pc in (0, 1) for pr in (0, 1)]


def reds(swapped):
    return (1, 2) if swapped else (0, 3)


def interleaved(group, offset):
    sub = row_ids(8)
    packed = roll_rows(group[0], offset)
    for q in range(1, 4):
        packed = jnp.where(sub // 2 == q, roll_rows(group[q], 2 * q + offset), packed)
    return packed


def edge_packs(source, diag, swapped):
    sub = row_ids(8)
    even, odd = reds(swapped)
    rows = source[0].shape[0]
    packs = []
    for here, first, second, row, step in (
        (slice(rows - 8, rows), even, odd, 6, 1),
        (slice(0, 8), odd, even, 1, -1),
    ):
        gs = [x[here] for x in source]
        gd = [x[here] for x in diag]
        near = gs[first] / gd[first]
        far = roll_rows(gs[second] / gd[second], step)
        gs[first] = jnp.where(sub == row, near, gs[first])
        gd[first] = jnp.where(sub == row, far, gd[first])
        offset = 2 if row == 6 else 0
        packs.append((interleaved(gs, offset), interleaved(gd, offset)))
    return packs


def unpacked_halo(left, right, swapped):
    sub = row_ids(8)
    even, odd = reds(swapped)
    (al, bl), (ar, br) = left, right
    source, diag = [], []
    for q in range(4):
        s = jnp.where(
            sub >= 6,
            roll_rows(al, 6 - 2 * q),
            jnp.where(sub <= 1, roll_rows(ar, -2 * q), 0.0),
        )
        d = jnp.where(
            sub >= 6,
            roll_rows(bl, 6 - 2 * q),
            jnp.where(sub <= 1, roll_rows(br, -2 * q), 4.0),
        )
        if q == even:
            s = jnp.where(sub == 2, roll_rows(br, 1 - 2 * odd), s)
            d = jnp.where((sub == 2) | (sub == 6), 1.0, d)
        if q == odd:
            s = jnp.where(sub == 5, roll_rows(bl, 5 - 2 * even), s)
            d = jnp.where((sub == 5) | (sub == 1), 1.0, d)
        source.append(s)
        diag.append(d)
    return source, diag


def is_odd():
    return lax.rem(lax.axis_index("lon"), 2) == 1


def chosen(odd, a, b):
    return jnp.where(odd, a, b), jnp.where(odd, b, a)


def store_edges(t, packs, odd, to_mate, to_other):
    right, left = packs
    for i in (0, 1):
        to_mate[i, t], to_other[i, t] = chosen(odd, left[i], right[i])


def fill_halo(t, from_mate, from_other, odd, swapped, hs, hd, hi):
    al, ar = chosen(odd, from_mate[0, t], from_other[0, t])
    bl, br = chosen(odd, from_mate[1, t], from_other[1, t])
    source, diag = unpacked_halo((al, bl), (ar, br), swapped)
    for q in range(4):
        hs[q, t] = source[q]
        hd[q, t] = diag[q]
        hi[q, t] = 1.0 / diag[q]


def loader(own, halo, virtual, tiles):
    def load(q, t):
        if isinstance(t, int) and t == tiles:
            return jnp.concatenate([virtual[q], halo[q, t]], 0)
        return jnp.concatenate([own[q, t], halo[q, t]], 0)

    return load


def polar_packs(tiles_of):
    lane = lane_ids(tiles_of[0][0].shape[0])
    packs = []
    for pc in (0, 1):
        parts = [*tiles_of[2 * pc], *tiles_of[2 * pc + 1]]
        packed = parts[0]
        for m in range(1, 4):
            mine = (lane + (16 - 32 * m) % LANES) % LANES < 32
            packed = jnp.where(mine, roll_lanes(parts[m], 32 * m), packed)
        packs.append(packed)
    return packs


def polar_unpacked(x, q):
    lane = lane_ids(x.shape[1])
    used = (lane < 16) | (lane >= LANES - 16)
    m = 2 * (q % 2)
    return (
        jnp.where(used, roll_lanes(x[q // 2], 32 * m), 0.0),
        jnp.where(used, roll_lanes(x[q // 2], 32 * (m + 1)), 4.0),
    )


def seam_scales(flags, chunks):
    flag_cols, flag_lats = flags.shape
    flags = jnp.concatenate(
        [flags.astype(F32), jnp.zeros((8 - flag_cols, flag_lats), F32)], 0
    )
    lat = lax.broadcasted_iota(jnp.int32, (8, flag_lats), 1)
    stacked = jnp.concatenate([jnp.where(lat // 8 == c, flags, 0.0) for c in chunks], 0)
    spread = selector((flag_lats, LANES), lambda a, b: a % 8 == b // (TILE // 2))
    spread_flags = jnp.dot(stacked.astype(BF16), spread, preferred_element_type=F32)
    scale = jnp.where(spread_flags > 0.5, SEAM_SCALE, 1.0)
    return scale.reshape(len(chunks), 8, LANES)


def seam_rows(scales, flag_cols, rows):
    size = (rows // flag_cols, LANES)
    return jnp.concatenate(
        [jnp.broadcast_to(scales[i : i + 1], size) for i in range(flag_cols)], 0
    )


def edge_kernel(
    right_ref, weight_ref, flag_ref,
    to_mate, to_other, polar_ref, corner_near, corner_far,
    edge_s, edge_w, end_s, end_w, flags, temp_s, temp_w, temp_p, temp_q, scale_ref, sems,
):
    columns, height = right_ref.shape
    rows, tiles = columns // 2, height // 256
    pairs = [(flag_ref, flags)]
    for i, (src, dst, size) in enumerate(
        ((right_ref, edge_s, 8), (weight_ref, edge_w, 16))
    ):
        pairs.append((src.at[pl.ds(0, size)], dst.at[pl.ds(0, size)]))
        pairs.append((src.at[pl.ds(columns - size, size)], dst.at[pl.ds(size, size)]))
    for src, dst in ((right_ref, end_s), (weight_ref, end_w)):
        for end, start in enumerate((0, height - 256)):
            pairs.append((src.at[:, pl.ds(start, 256)], dst.at[end]))
    copies = [
        pltpu.make_async_copy(src, dst, sems.at[i]) for i, (src, dst) in enumerate(pairs)
    ]
    for copy in copies:
        copy.start()
    odd = is_odd()
    matrix = splitter()
    flag_cols = flag_ref.shape[0]
    copies[0].wait()
    scale_ref[...] = seam_scales(flags[...], range(tiles))
    for copy in copies[1:5]:
        copy.wait()
    sub = row_ids(8)
    lanes = [slice(c * 256, (c + 1) * 256) for c in range(tiles)]
    source, weight = moved(
        jnp.concatenate([edge_s[:, w] for w in lanes], 0),
        matrix,
        jnp.concatenate([edge_w[:, w] for w in lanes], 0),
    )
    weight = weight.reshape(tiles, 32, 256)
    weight = jnp.concatenate([weight[:, :8], weight[:, 24:]], 1).reshape(tiles * 16, 256)
    source = quarters_of(source, temp_s)
    weight = quarters_of(weight, temp_w)
    for c in range(tiles):
        here = slice(c * 8, (c + 1) * 8)
        scales = scale_ref[c]
        scale = jnp.where(sub < 4, scales[:1], scales[flag_cols - 1 : flag_cols])
        diag = [4.0 + w[here] * scale for w in weight]
        store_edges(
            c, edge_packs([x[here] for x in source], diag, False), odd, to_mate, to_other
        )

    for copy in copies[5:]:
        copy.wait()
    mirror = selector((LANES, LANES), lambda a, b: a + b == LANES - 1)
    lane = lane_ids(rows)
    source, weight = moved(
        jnp.concatenate([end_s[0], end_s[1]], 0),
        matrix,
        jnp.concatenate([end_w[0], end_w[1]], 0),
    )
    found = []
    for end, c in enumerate((0, tiles - 1)):
        here = slice(end * columns, (end + 1) * columns)
        scale = seam_rows(scale_ref[c], flag_cols, rows)
        found.append(
            (
                quarters_of(source[here], temp_p.at[end]),
                [4.0 + w * scale for w in quarters_of(weight[here], temp_q.at[end])],
            )
        )
    ends = [
        [jnp.where(lane >= 64, found[1][i][q ^ 1], found[0][i][q ^ 1]) for i in (0, 1)]
        for q in range(4)
    ]
    both = moved(jnp.concatenate(polar_packs(ends), 0), mirror)
    for pc in (0, 1):
        pack = both[pc * rows : (pc + 1) * rows]
        polar_ref[pc] = pack
        corner_near[pc], corner_far[pc] = chosen(odd, pack[:8], pack[rows - 8 :])


def bulk_kernel(
    right_ref, weight_ref, flag_ref, edges_first,
    s_ref, d_ref, i_ref, d1_ref, i1_ref, d2_ref,
    temp_s, temp_d, scale_ref, e_ref,
):
    tiles, rows = s_ref.shape[1], s_ref.shape[2]
    columns = 2 * rows
    matrix = splitter()
    scale_ref[...] = seam_scales(flag_ref[...], range(tiles))
    for start in range(0, tiles, BATCH):
        lanes = [slice((start + i) * 256, (start + i + 1) * 256) for i in range(BATCH)]
        source, weight = moved(
            jnp.concatenate([right_ref[:, w] for w in lanes], 0),
            matrix,
            jnp.concatenate([weight_ref[:, w] for w in lanes], 0),
        )
        for i in range(BATCH):
            c = start + i
            here = slice(i * columns, (i + 1) * columns)
            scale = seam_rows(scale_ref[c], flag_ref.shape[0], rows)
            for q, value in enumerate(quarters_of(source[here], temp_s.at[i])):
                s_ref[q, c] = value
            screen = [w * scale for w in quarters_of(weight[here], temp_d.at[i])]
            e_ref[c] = (screen[0] + screen[1]) + (screen[2] + screen[3])
            for q in range(4):
                diag = 4.0 + screen[q]
                d_ref[q, c] = diag
                i_ref[q, c] = 1.0 / diag

    def use(c, screen):
        for q in range(4):
            d1_ref[q, c] = 4.0 + screen[q]
            i1_ref[q, c] = 1.0 / (4.0 + screen[q])
        d2_ref[c] = 4.0 + ((screen[0] + screen[1]) + (screen[2] + screen[3]))

    split_tiles(lambda t: e_ref[t], tiles // 2, rows, matrix, temp_s, use)


def split_tiles(load, tiles, rows, matrix, temp, use):
    for start in range(0, tiles, BATCH):
        wide = [
            jnp.concatenate([load(2 * c), load(2 * c + 1)], 1)
            for c in range(start, start + BATCH)
        ]
        out = moved(jnp.concatenate(wide, 0), matrix)
        for i in range(BATCH):
            use(start + i, quarters_of(out[i * rows : (i + 1) * rows], temp.at[i, :, :rows]))


def half_sweep(v, load_s, load_i, tiles, red, unroll):
    rows = v[0].shape[1]
    lane = lane_ids(rows)
    y, z, qa, qb = (1, 2, 0, 3) if red else (3, 0, 2, 1)
    col_a, col_b = (col_prev, col_next) if red else (col_next, col_prev)

    def beside_virtual(q):
        ns, we = q ^ 1, q ^ 2
        here = v[ns][tiles]
        if q % 2 == 0:
            lat = jnp.where(lane == 0, roll_up(v[ns][tiles - 1]), roll_up(here))
        else:
            lat = jnp.where(lane == LANES - 1, roll_down(v[ns][0]), roll_down(here))
        cols = v[we][tiles]
        return (here + lat) + (cols + (col_prev if q < 2 else col_next)(cols))

    held = [
        (q, (load_s(q, tiles) + beside_virtual(q)) * load_i(q, tiles)) for q in (y, z)
    ]

    def body(t, carry):
        y_before, z_here = carry
        vy, vz = v[y][t], v[z][t]
        y_here = roll_up(vy)
        z_after = roll_down(v[z][t + 1])
        lat_a = vy + jnp.where(lane == 0, y_before, y_here)
        lat_b = vz + jnp.where(lane == LANES - 1, z_after, z_here)
        v[qa][t] = (load_s(qa, t) + (lat_a + (vz + col_a(vz)))) * load_i(qa, t)
        v[qb][t] = (load_s(qb, t) + (lat_b + (vy + col_b(vy)))) * load_i(qb, t)
        return y_here, z_after

    loop(tiles, body, (roll_up(v[y][tiles]), roll_down(v[z][0])), unroll)
    for q, value in held:
        v[q][tiles] = value


def smooth(v, load_s, load_i, tiles, unroll):
    zeros = jnp.zeros(v[0].shape[1:], F32)

    def first(t, _):
        for q in (0, 3):
            v[q][t] = load_s(q, t) * load_i(q, t)
        return 0

    loop(tiles, first, 0, unroll)
    for q in (1, 2):
        v[q][0] = zeros
        v[q][tiles - 1] = zeros
        v[q][tiles] = load_s(q, tiles) * load_i(q, tiles)
        v[3 * (q - 1)][tiles] = zeros
    half_sweep(v, load_s, load_i, tiles, False, unroll)
    half_sweep(v, load_s, load_i, tiles, True, unroll)
    half_sweep(v, load_s, load_i, tiles, False, unroll)


def residuals(v, load_s, load_d, tiles, c0, c1, keep, unroll):
    lane = lane_ids(v[0].shape[1])

    def body(t, _):
        x = [v[q][t] for q in range(4)]

        def north(q):
            return jnp.where(lane == 0, roll_up(v[q][before(t, tiles)]), roll_up(x[q]))

        def south(q):
            return jnp.where(
                lane == LANES - 1, roll_down(v[q][after(t, tiles)]), roll_down(x[q])
            )

        beside = [
            (x[1] + north(1)) + (x[2] + col_prev(x[2])),
            (x[0] + south(0)) + (x[3] + col_prev(x[3])),
            (x[3] + north(3)) + (x[0] + col_next(x[0])),
            (x[2] + south(2)) + (x[1] + col_next(x[1])),
        ]
        r = [load_s(q, t) - (load_d(q, t) * x[q] - beside[q]) for q in range(4)]
        keep(t, r)
        c0[t] = (col_prev(r[2]) + col_next(r[0])) + 3.0 * (r[0] + r[2])
        c1[t] = (col_prev(r[3]) + col_next(r[1])) + 3.0 * (r[1] + r[3])
        return 0

    loop(tiles, body, 0, unroll)
    body(tiles, 0)


def restricted(c0, c1, t, tiles, rows):
    lane = lane_ids(rows)
    here, other = c0[t, :rows], c1[t, :rows]
    north = jnp.where(lane == 0, roll_up(c1[before(t, tiles), :rows]), roll_up(other))
    south = jnp.where(
        lane == LANES - 1, roll_down(c0[after(t, tiles), :rows]), roll_down(here)
    )
    return ((north + south) + 3.0 * (here + other)) * (1.0 / 16.0)


def fine_kernel(
    s_ref, d_ref, i_ref, d1_ref, from_mate, from_other, polar_ref, corner_near, corner_far,
    r_ref, s1_ref, d1_virtual, d2_virtual, to_mate, to_other,
    v0, v1, v2, v3, c0, c1, hs, hd, hi, ps, pd, pi, n1, temp,
):
    v = [v0, v1, v2, v3]
    tiles, rows = s_ref.shape[1], s_ref.shape[2]
    sub = row_ids(8)
    odd = is_odd()

    def halo(t, _):
        fill_halo(t, from_mate, from_other, odd, False, hs, hd, hi)
        return 0

    loop(tiles, halo)
    total = -16.0
    for q in range(4):
        own_s, own_d = polar_unpacked(polar_ref, q)
        near_s, near_d = polar_unpacked(corner_near, q)
        far_s, far_d = polar_unpacked(corner_far, q)
        left_s, right_s = chosen(odd, near_s, far_s)
        left_d, right_d = chosen(odd, near_d, far_d)
        total = total + own_d
        ps[q] = own_s
        pd[q] = own_d
        pi[q] = 1.0 / own_d
        source = jnp.where(sub >= 5, left_s, jnp.where(sub <= 2, right_s, 0.0))
        diag = jnp.where(sub >= 5, left_d, jnp.where(sub <= 2, right_d, 4.0))
        hs[q, tiles] = source
        hd[q, tiles] = diag
        hi[q, tiles] = 1.0 / diag

    load_s = loader(s_ref, hs, ps, tiles)
    smooth(v, load_s, loader(i_ref, hi, pi, tiles), tiles, 16)

    def keep(t, r):
        if not (isinstance(t, int) and t == tiles):
            for q in range(4):
                r_ref[q, t] = r[q][:rows]

    residuals(v, load_s, loader(d_ref, hd, pd, tiles), tiles, c0, c1, keep, 8)

    def coarse(t, _):
        n1[t] = restricted(c0, c1, t, tiles, rows)
        return 0

    loop(tiles, coarse, 0, 8)
    coarse(tiles, 0)

    def edges(t, source, diag, swapped):
        store_edges(t, edge_packs(source, diag, swapped), odd, to_mate, to_other)

    def use(c, source):
        for q in range(4):
            s1_ref[q, c] = source[q]
        edges(c, source, [d1_ref[q, c] for q in range(4)], False)

    tiles1 = tiles // 2
    split_tiles(lambda t: n1[t], tiles1, rows, splitter(), temp, use)
    out = moved(jnp.concatenate([n1[tiles], total], 0), virtual_splitter())
    source = quarters_of(out[:rows], temp.at[0])
    screen = quarters_of(out[rows:], temp.at[1])
    diag = [4.0 + x for x in screen]
    for q in range(4):
        s1_ref[q, tiles1] = source[q]
        d1_virtual[q] = diag[q]
    d2_virtual[...] = 4.0 + ((screen[0] + screen[1]) + (screen[2] + screen[3]))
    edges(tiles1, source, diag, True)


def merge_kernel(r_ref, out_ref, temp, out_buf, sems):
    tiles = r_ref.shape[1]
    rows = r_ref.shape[2]
    matrix = merger()
    chunk = out_ref.shape[1] // GROUPS
    copies = []
    for group in range(GROUPS):
        for batch in range(tiles // GROUPS // BATCH):
            start = group * (tiles // GROUPS) + batch * BATCH
            both = []
            for i in range(BATCH):
                for pr in (0, 1):
                    for pc in (0, 1):
                        temp[i, pr, pl.ds(pc, rows, 2), :] = r_ref[2 * pc + pr, start + i]
                both.append(jnp.concatenate([temp[i, 0], temp[i, 1]], 1))
            out = moved(jnp.concatenate(both, 0), matrix)
            for i in range(BATCH):
                where = slice((start + i) * 256, (start + i + 1) * 256)
                out_buf[:, where] = out[2 * rows * i : 2 * rows * (i + 1)]
        part = pl.ds(group * chunk, chunk)
        copy = pltpu.make_async_copy(out_buf.at[:, part], out_ref.at[:, part], sems.at[group])
        copy.start()
        copies.append(copy)
    for copy in copies:
        copy.wait()


def middle_kernel(
    merged_first, s_ref, d_ref, i_ref, d_virtual, d2_ref, d2_virtual, from_mate, from_other,
    s2_ref, to_mate, to_other,
    v0, v1, v2, v3, c0, c1, hs, hd, hi, pi,
):
    v = [v0, v1, v2, v3]
    tiles, rows = d_ref.shape[1], d_ref.shape[2]
    odd = is_odd()
    for t in range(tiles + 1):
        fill_halo(t, from_mate, from_other, odd, t == tiles, hs, hd, hi)
    for q in range(4):
        pi[q] = 1.0 / d_virtual[q]

    def load_s(q, t):
        return jnp.concatenate([s_ref[q, t], hs[q, t]], 0)

    smooth(v, load_s, loader(i_ref, hi, pi, tiles), tiles, 16)
    residuals(
        v, load_s, loader(d_ref, hd, d_virtual, tiles), tiles, c0, c1, lambda t, r: None, 16
    )
    sub = row_ids(8)
    for t in range(tiles + 1):
        value = restricted(c0, c1, t, tiles, rows)
        diag = d2_virtual[...] if t == tiles else d2_ref[t]
        s2_ref[t] = value
        right = jnp.where(sub < 4, roll_rows(value[rows - 8 :], 4), diag[rows - 8 :])
        left = jnp.where(sub < 4, value[:8], roll_rows(diag[:8], 4))
        to_mate[t], to_other[t] = chosen(odd, left, right)


def last_kernel(
    s_ref, d_ref, d_virtual, from_mate, from_other,
    solution_ref, residual_ref,
    s, d, inv, va, vb,
):
    tiles, own = d_ref.shape[0], d_ref.shape[1]
    rows = own + 8
    sub = row_ids(8)
    lane, row = lane_ids(rows), row_ids(rows)
    even = (lane + row) % 2 == 0
    odd = jnp.logical_not(even)
    odd_band = is_odd()
    for t in range(tiles + 1):
        left, right = chosen(odd_band, from_mate[t], from_other[t])
        diag = d_virtual[...] if t == tiles else d_ref[t]
        source = jnp.concatenate(
            [s_ref[t], jnp.where(sub < 4, right, roll_rows(left, 4))], 0
        )
        diag = jnp.concatenate([diag, jnp.where(sub < 4, roll_rows(right, 4), left)], 0)
        inverse = 1.0 / diag
        s[t] = source
        d[t] = diag
        inv[t] = inverse
        va[t] = jnp.where(odd if t == tiles else even, source * inverse, 0.0)

    def beside(v, t):
        x = v[t]
        north = jnp.where(lane == 0, roll_up(v[before(t, tiles)]), roll_up(x))
        south = jnp.where(lane == LANES - 1, roll_down(v[after(t, tiles)]), roll_down(x))
        return (col_prev(x) + col_next(x)) + (north + south)

    old, new = va, vb
    for mask, other in ((odd, even), (even, odd), (odd, even)):
        for t in range(tiles + 1):
            value = (s[t] + beside(old, t)) * inv[t]
            new[t] = jnp.where(other if t == tiles else mask, value, old[t])
        old, new = new, old
    for t in range(tiles):
        x = old[t]
        r = s[t] - (d[t] * x - beside(old, t))
        where = slice(t * LANES, (t + 1) * LANES)
        solution_ref[:, where] = x[:own]
        residual_ref[:, where] = r[:own]


VMEM = pl.BlockSpec(memory_space=pltpu.VMEM)
HBM = pl.BlockSpec(memory_space=pltpu.HBM)


def call(kernel, out_shapes, scratch, *args, sems=None, far_in=0, far_out=0):
    scratch = [pltpu.VMEM(x, F32) if isinstance(x, tuple) else x for x in scratch]
    if sems is not None:
        scratch.append(pltpu.SemaphoreType.DMA(sems))
    return pl.pallas_call(
        kernel,
        out_shape=[jax.ShapeDtypeStruct(shape, F32) for shape in out_shapes],
        in_specs=[HBM] * far_in + [VMEM] * (len(args) - far_in),
        out_specs=[HBM] * far_out + [VMEM] * (len(out_shapes) - far_out),
        scratch_shapes=scratch,
        compiler_params=pltpu.CompilerParams(vmem_limit_bytes=40 * 2**20),
    )(*args)


def swapped_with(x, by):
    count = lax.axis_size("lon")
    pairs = [(i, (i + by) % count) for i in range(0, count, 2)]
    return lax.ppermute(x, "lon", pairs + [(b, a) for a, b in pairs])


def swapped_edges(to_mate, to_other):
    from_other = swapped_with(to_other, -1)
    return swapped_with(to_mate, 1), from_other


def body(right_side, texel_weight, seam_flags):
    columns, height = right_side.shape
    half_turn = lax.axis_size("lon") // 2
    tiles, rows = height // 256, columns // 2
    tiles1, rows1 = tiles // 2, rows // 2
    temp = (BATCH, 2, columns, LANES)
    quarters = (4, tiles, rows, LANES)
    quarters1 = (4, tiles1, rows1, LANES)
    pack = (2, tiles, 8, LANES)
    corner = (2, 8, LANES)
    split = (2, 16 * tiles, LANES)
    to_mate, to_other, polar, corner_near, corner_far = call(
        edge_kernel,
        [pack, pack, (2, rows, LANES), corner, corner],
        [(16, height), pltpu.VMEM((32, height), BF16)]
        + [(2, columns, 256), pltpu.VMEM((2, columns, 256), BF16)]
        + [pltpu.VMEM(seam_flags.shape, jnp.int32), split, split]
        + [(2, 2, columns, LANES)] * 2
        + [(tiles, 8, LANES)],
        *[
            pltpu.with_memory_space_constraint(x, pltpu.HBM)
            for x in (right_side, texel_weight, seam_flags)
        ],
        sems=(9,), far_in=3,
    )
    from_mate, from_other = swapped_edges(to_mate, to_other)
    polar = lax.ppermute(
        polar, "lon", [(i, (i + half_turn) % (2 * half_turn)) for i in range(2 * half_turn)]
    )
    corner_near_own = corner_near
    corner_far = swapped_with(corner_far, half_turn - 1)
    corner_near = swapped_with(corner_near, half_turn + 1)
    s, d, inverse, d1, i1, d2 = call(
        bulk_kernel,
        [quarters] * 3 + [quarters1, quarters1, quarters1[1:]],
        [temp, temp, (tiles, 8, LANES), quarters[1:]],
        right_side, texel_weight, seam_flags, corner_near_own,
    )

    def level_scratch(tiles, rows):
        halo = (4, tiles + 1, 8, LANES)
        return [(tiles + 1, rows + 8, LANES)] * 6 + [halo] * 3

    pack1 = (2, tiles1 + 1, 8, LANES)
    r, s1, d1_virtual, d2_virtual, to_mate, to_other = call(
        fine_kernel,
        [quarters, (4, tiles1 + 1, rows1, LANES), (4, rows1, LANES), (rows1, LANES), pack1, pack1],
        level_scratch(tiles, rows)
        + [(4, rows, LANES)] * 3
        + [(tiles + 1, rows, LANES), (BATCH, 2, rows, LANES)],
        s, d, inverse, d1, from_mate, from_other, polar, corner_near, corner_far,
    )
    from_mate, from_other = swapped_edges(to_mate, to_other)
    (fine_residual,) = call(
        merge_kernel, [(columns, height)], [temp, (columns, height)], r,
        sems=(GROUPS,), far_out=1,
    )
    pack2 = (tiles1 + 1, 8, LANES)
    s2, to_mate, to_other = call(
        middle_kernel,
        [(tiles1 + 1, rows1, LANES), pack2, pack2],
        level_scratch(tiles1, rows1) + [(4, rows1, LANES)],
        pltpu.with_memory_space_constraint(fine_residual, pltpu.HBM),
        s1, d1, i1, d1_virtual, d2, d2_virtual, from_mate, from_other,
        far_in=1,
    )
    from_mate, from_other = swapped_edges(to_mate, to_other)
    solution_2, residual_2 = call(
        last_kernel,
        [(columns // 4, height // 4)] * 2,
        [(tiles1 + 1, rows1 + 8, LANES)] * 5,
        s2, d2, d2_virtual, from_mate, from_other,
    )
    return fine_residual, solution_2, residual_2


def solution(mesh):
    spec = P(("groups", "lon"), None)
    return jax.shard_map(
        body, mesh=mesh, in_specs=(spec,) * 3, out_specs=(spec,) * 3, check_vma=False
    )
```

```python
import jax
import jax.numpy as jnp
from jax import lax
from jax.experimental import pallas as pl
from jax.experimental.pallas import tpu as pltpu
from jax.sharding import PartitionSpec as P

TILE = 32
SEAM_SCALE = 0.1
LANES = 128
GROUPS = 4
BATCH = 4
F32 = jnp.float32
BF16 = jnp.bfloat16


def loop(count, body, carry=0, unroll=4):
    unroll = min(unroll, count)

    def steps(block, carry):
        for i in range(unroll):
            carry = body(block * unroll + i, carry)
        return carry

    whole = count // unroll
    carry = steps(0, carry) if whole == 1 else lax.fori_loop(0, whole, steps, carry)
    for t in range(whole * unroll, count):
        carry = body(t, carry)
    return carry


def before(t, tiles):
    return (tiles if t == 0 else t - 1) if isinstance(t, int) else jnp.where(t == 0, tiles, t - 1)


def after(t, tiles):
    return (0 if t == tiles else t + 1) if isinstance(t, int) else t + 1


def lane_ids(rows):
    return lax.broadcasted_iota(jnp.int32, (rows, LANES), 1)


def row_ids(rows):
    return lax.broadcasted_iota(jnp.int32, (rows, LANES), 0)


def roll_up(x):
    return pltpu.roll(x, 1, 1)


def roll_down(x):
    return pltpu.roll(x, LANES - 1, 1)


def roll_rows(x, by):
    by %= x.shape[0]
    return x if by == 0 else pltpu.roll(x, by, 0)


def roll_lanes(x, by):
    by %= LANES
    return x if by == 0 else pltpu.roll(x, by, 1)


def col_prev(x):
    return pltpu.roll(x, 1, 0)


def col_next(x):
    return pltpu.roll(x, x.shape[0] - 1, 0)


def selector(shape, rule):
    a = lax.broadcasted_iota(jnp.int32, shape, 0)
    b = lax.broadcasted_iota(jnp.int32, shape, 1)
    return jnp.where(rule(a, b), 1.0, 0.0).astype(BF16)


def splitter():
    return selector((256, 256), lambda a, b: a == 2 * (b % LANES) + b // LANES)


def merger():
    return selector((256, 256), lambda a, b: b == 2 * (a % LANES) + a // LANES)


def virtual_splitter():
    return selector(
        (LANES, 256),
        lambda a, b: a // 2 + jnp.where(a >= 64, 64, 0) + LANES * (a % 2) == b,
    )


def moved(x, matrix, exact=None):
    rows = x.shape[0]
    high = x.astype(BF16)
    low = (x - high.astype(F32)).astype(BF16)
    terms = [high, low] if exact is None else [high, low, exact]
    out = jnp.dot(jnp.concatenate(terms, 0), matrix, preferred_element_type=F32)
    both = out[:rows] + out[rows : 2 * rows]
    return both if exact is None else (both, out[2 * rows :])


def quarters_of(parts, temp):
    count = parts.shape[0] // 2
    temp[0] = parts[:, :LANES]
    temp[1] = parts[:, LANES:]
    return [temp[pr, pl.ds(pc, count, 2), :] for pc in (0, 1) for pr in (0, 1)]


def reds(swapped):
    return (1, 2) if swapped else (0, 3)


def interleaved(group, offset):
    sub = row_ids(8)
    packed = roll_rows(group[0], offset)
    for q in range(1, 4):
        packed = jnp.where(sub // 2 == q, roll_rows(group[q], 2 * q + offset), packed)
    return packed


def edge_packs(source, diag, swapped):
    sub = row_ids(8)
    even, odd = reds(swapped)
    rows = source[0].shape[0]
    packs = []
    for here, first, second, row, step in (
        (slice(rows - 8, rows), even, odd, 6, 1),
        (slice(0, 8), odd, even, 1, -1),
    ):
        gs = [x[here] for x in source]
        gd = [x[here] for x in diag]
        near = gs[first] / gd[first]
        far = roll_rows(gs[second] / gd[second], step)
        gs[first] = jnp.where(sub == row, near, gs[first])
        gd[first] = jnp.where(sub == row, far, gd[first])
        offset = 2 if row == 6 else 0
        packs.append((interleaved(gs, offset), interleaved(gd, offset)))
    return packs


def unpacked_halo(left, right, swapped):
    sub = row_ids(8)
    even, odd = reds(swapped)
    (al, bl), (ar, br) = left, right
    source, diag = [], []
    for q in range(4):
        s = jnp.where(
            sub >= 6,
            roll_rows(al, 6 - 2 * q),
            jnp.where(sub <= 1, roll_rows(ar, -2 * q), 0.0),
        )
        d = jnp.where(
            sub >= 6,
            roll_rows(bl, 6 - 2 * q),
            jnp.where(sub <= 1, roll_rows(br, -2 * q), 4.0),
        )
        if q == even:
            s = jnp.where(sub == 2, roll_rows(br, 1 - 2 * odd), s)
            d = jnp.where((sub == 2) | (sub == 6), 1.0, d)
        if q == odd:
            s = jnp.where(sub == 5, roll_rows(bl, 5 - 2 * even), s)
            d = jnp.where((sub == 5) | (sub == 1), 1.0, d)
        source.append(s)
        diag.append(d)
    return source, diag


def is_odd():
    return lax.rem(lax.axis_index("lon"), 2) == 1


def chosen(odd, a, b):
    return jnp.where(odd, a, b), jnp.where(odd, b, a)


def store_edges(t, packs, odd, to_mate, to_other):
    right, left = packs
    for i in (0, 1):
        to_mate[i, t], to_other[i, t] = chosen(odd, left[i], right[i])


def fill_halo(t, from_mate, from_other, odd, swapped, hs, hd, hi):
    al, ar = chosen(odd, from_mate[0, t], from_other[0, t])
    bl, br = chosen(odd, from_mate[1, t], from_other[1, t])
    source, diag = unpacked_halo((al, bl), (ar, br), swapped)
    for q in range(4):
        hs[q, t] = source[q]
        hd[q, t] = diag[q]
        hi[q, t] = 1.0 / diag[q]


def loader(own, halo, virtual, tiles):
    def load(q, t):
        if isinstance(t, int) and t == tiles:
            return jnp.concatenate([virtual[q], halo[q, t]], 0)
        return jnp.concatenate([own[q, t], halo[q, t]], 0)

    return load


def polar_packs(tiles_of):
    lane = lane_ids(tiles_of[0][0].shape[0])
    packs = []
    for pc in (0, 1):
        parts = [*tiles_of[2 * pc], *tiles_of[2 * pc + 1]]
        packed = parts[0]
        for m in range(1, 4):
            mine = (lane + (16 - 32 * m) % LANES) % LANES < 32
            packed = jnp.where(mine, roll_lanes(parts[m], 32 * m), packed)
        packs.append(packed)
    return packs


def polar_unpacked(x, q):
    lane = lane_ids(x.shape[1])
    used = (lane < 16) | (lane >= LANES - 16)
    m = 2 * (q % 2)
    return (
        jnp.where(used, roll_lanes(x[q // 2], 32 * m), 0.0),
        jnp.where(used, roll_lanes(x[q // 2], 32 * (m + 1)), 4.0),
    )


def seam_scales(flags, chunks):
    flag_cols, flag_lats = flags.shape
    flags = jnp.concatenate(
        [flags.astype(F32), jnp.zeros((8 - flag_cols, flag_lats), F32)], 0
    )
    lat = lax.broadcasted_iota(jnp.int32, (8, flag_lats), 1)
    stacked = jnp.concatenate([jnp.where(lat // 8 == c, flags, 0.0) for c in chunks], 0)
    spread = selector((flag_lats, LANES), lambda a, b: a % 8 == b // (TILE // 2))
    spread_flags = jnp.dot(stacked.astype(BF16), spread, preferred_element_type=F32)
    scale = jnp.where(spread_flags > 0.5, SEAM_SCALE, 1.0)
    return scale.reshape(len(chunks), 8, LANES)


def seam_rows(scales, flag_cols, rows):
    size = (rows // flag_cols, LANES)
    return jnp.concatenate(
        [jnp.broadcast_to(scales[i : i + 1], size) for i in range(flag_cols)], 0
    )


def edge_kernel(
    right_ref, weight_ref, flag_ref,
    to_mate, to_other, polar_ref, corner_near, corner_far,
    edge_s, edge_w, end_s, end_w, flags, temp_s, temp_w, temp_p, temp_q, scale_ref, sems,
):
    columns, height = right_ref.shape
    rows, tiles = columns // 2, height // 256
    pairs = [(flag_ref, flags)]
    for i, (src, dst, size) in enumerate(
        ((right_ref, edge_s, 8), (weight_ref, edge_w, 16))
    ):
        pairs.append((src.at[pl.ds(0, size)], dst.at[pl.ds(0, size)]))
        pairs.append((src.at[pl.ds(columns - size, size)], dst.at[pl.ds(size, size)]))
    for src, dst in ((right_ref, end_s), (weight_ref, end_w)):
        for end, start in enumerate((0, height - 256)):
            pairs.append((src.at[:, pl.ds(start, 256)], dst.at[end]))
    copies = [
        pltpu.make_async_copy(src, dst, sems.at[i]) for i, (src, dst) in enumerate(pairs)
    ]
    for copy in copies:
        copy.start()
    odd = is_odd()
    matrix = splitter()
    flag_cols = flag_ref.shape[0]
    copies[0].wait()
    scale_ref[...] = seam_scales(flags[...], range(tiles))
    for copy in copies[1:5]:
        copy.wait()
    sub = row_ids(8)
    lanes = [slice(c * 256, (c + 1) * 256) for c in range(tiles)]
    source, weight = moved(
        jnp.concatenate([edge_s[:, w] for w in lanes], 0),
        matrix,
        jnp.concatenate([edge_w[:, w] for w in lanes], 0),
    )
    weight = weight.reshape(tiles, 32, 256)
    weight = jnp.concatenate([weight[:, :8], weight[:, 24:]], 1).reshape(tiles * 16, 256)
    source = quarters_of(source, temp_s)
    weight = quarters_of(weight, temp_w)
    for c in range(tiles):
        here = slice(c * 8, (c + 1) * 8)
        scales = scale_ref[c]
        scale = jnp.where(sub < 4, scales[:1], scales[flag_cols - 1 : flag_cols])
        diag = [4.0 + w[here] * scale for w in weight]
        store_edges(
            c, edge_packs([x[here] for x in source], diag, False), odd, to_mate, to_other
        )

    for copy in copies[5:]:
        copy.wait()
    mirror = selector((LANES, LANES), lambda a, b: a + b == LANES - 1)
    lane = lane_ids(rows)
    source, weight = moved(
        jnp.concatenate([end_s[0], end_s[1]], 0),
        matrix,
        jnp.concatenate([end_w[0], end_w[1]], 0),
    )
    found = []
    for end, c in enumerate((0, tiles - 1)):
        here = slice(end * columns, (end + 1) * columns)
        scale = seam_rows(scale_ref[c], flag_cols, rows)
        found.append(
            (
                quarters_of(source[here], temp_p.at[end]),
                [4.0 + w * scale for w in quarters_of(weight[here], temp_q.at[end])],
            )
        )
    ends = [
        [jnp.where(lane >= 64, found[1][i][q ^ 1], found[0][i][q ^ 1]) for i in (0, 1)]
        for q in range(4)
    ]
    both = moved(jnp.concatenate(polar_packs(ends), 0), mirror)
    for pc in (0, 1):
        pack = both[pc * rows : (pc + 1) * rows]
        polar_ref[pc] = pack
        corner_near[pc], corner_far[pc] = chosen(odd, pack[:8], pack[rows - 8 :])


def bulk_kernel(
    right_ref, weight_ref, flag_ref, edges_first,
    s_ref, d_ref, i_ref, d1_ref, i1_ref, d2_ref,
    temp_s, temp_d, scale_ref, e_ref,
):
    tiles, rows = s_ref.shape[1], s_ref.shape[2]
    columns = 2 * rows
    matrix = splitter()
    scale_ref[...] = seam_scales(flag_ref[...], range(tiles))
    for start in range(0, tiles, BATCH):
        lanes = [slice((start + i) * 256, (start + i + 1) * 256) for i in range(BATCH)]
        source, weight = moved(
            jnp.concatenate([right_ref[:, w] for w in lanes], 0),
            matrix,
            jnp.concatenate([weight_ref[:, w] for w in lanes], 0),
        )
        for i in range(BATCH):
            c = start + i
            here = slice(i * columns, (i + 1) * columns)
            scale = seam_rows(scale_ref[c], flag_ref.shape[0], rows)
            for q, value in enumerate(quarters_of(source[here], temp_s.at[i])):
                s_ref[q, c] = value
            screen = [w * scale for w in quarters_of(weight[here], temp_d.at[i])]
            e_ref[c] = (screen[0] + screen[1]) + (screen[2] + screen[3])
            for q in range(4):
                diag = 4.0 + screen[q]
                d_ref[q, c] = diag
                i_ref[q, c] = 1.0 / diag

    def use(c, screen):
        for q in range(4):
            d1_ref[q, c] = 4.0 + screen[q]
            i1_ref[q, c] = 1.0 / (4.0 + screen[q])
        d2_ref[c] = 4.0 + ((screen[0] + screen[1]) + (screen[2] + screen[3]))

    split_tiles(lambda t: e_ref[t], tiles // 2, rows, matrix, temp_s, use)


def split_tiles(load, tiles, rows, matrix, temp, use):
    for start in range(0, tiles, BATCH):
        wide = [
            jnp.concatenate([load(2 * c), load(2 * c + 1)], 1)
            for c in range(start, start + BATCH)
        ]
        out = moved(jnp.concatenate(wide, 0), matrix)
        for i in range(BATCH):
            use(start + i, quarters_of(out[i * rows : (i + 1) * rows], temp.at[i, :, :rows]))


def half_sweep(v, load_s, load_i, tiles, red, unroll):
    rows = v[0].shape[1]
    lane = lane_ids(rows)
    y, z, qa, qb = (1, 2, 0, 3) if red else (3, 0, 2, 1)
    col_a, col_b = (col_prev, col_next) if red else (col_next, col_prev)

    def beside_virtual(q):
        ns, we = q ^ 1, q ^ 2
        here = v[ns][tiles]
        if q % 2 == 0:
            lat = jnp.where(lane == 0, roll_up(v[ns][tiles - 1]), roll_up(here))
        else:
            lat = jnp.where(lane == LANES - 1, roll_down(v[ns][0]), roll_down(here))
        cols = v[we][tiles]
        return (here + lat) + (cols + (col_prev if q < 2 else col_next)(cols))

    held = [
        (q, (load_s(q, tiles) + beside_virtual(q)) * load_i(q, tiles)) for q in (y, z)
    ]

    def body(t, carry):
        y_before, z_here = carry
        vy, vz = v[y][t], v[z][t]
        y_here = roll_up(vy)
        z_after = roll_down(v[z][t + 1])
        lat_a = vy + jnp.where(lane == 0, y_before, y_here)
        lat_b = vz + jnp.where(lane == LANES - 1, z_after, z_here)
        v[qa][t] = (load_s(qa, t) + (lat_a + (vz + col_a(vz)))) * load_i(qa, t)
        v[qb][t] = (load_s(qb, t) + (lat_b + (vy + col_b(vy)))) * load_i(qb, t)
        return y_here, z_after

    loop(tiles, body, (roll_up(v[y][tiles]), roll_down(v[z][0])), unroll)
    for q, value in held:
        v[q][tiles] = value


def smooth(v, load_s, load_i, tiles, unroll):
    zeros = jnp.zeros(v[0].shape[1:], F32)

    def first(t, _):
        for q in (0, 3):
            v[q][t] = load_s(q, t) * load_i(q, t)
        return 0

    loop(tiles, first, 0, unroll)
    for q in (1, 2):
        v[q][0] = zeros
        v[q][tiles - 1] = zeros
        v[q][tiles] = load_s(q, tiles) * load_i(q, tiles)
        v[3 * (q - 1)][tiles] = zeros
    half_sweep(v, load_s, load_i, tiles, False, unroll)
    half_sweep(v, load_s, load_i, tiles, True, unroll)
    half_sweep(v, load_s, load_i, tiles, False, unroll)


def residuals(v, load_s, load_d, tiles, c0, c1, keep, unroll):
    lane = lane_ids(v[0].shape[1])

    def body(t, carry):
        up1, up3, down0, down2 = carry
        x = [v[q][t] for q in range(4)]
        here1, here3 = roll_up(x[1]), roll_up(x[3])
        next0, next2 = (roll_down(v[q][after(t, tiles)]) for q in (0, 2))
        beside = [
            (x[1] + jnp.where(lane == 0, up1, here1)) + (x[2] + col_prev(x[2])),
            (x[0] + jnp.where(lane == LANES - 1, next0, down0)) + (x[3] + col_prev(x[3])),
            (x[3] + jnp.where(lane == 0, up3, here3)) + (x[0] + col_next(x[0])),
            (x[2] + jnp.where(lane == LANES - 1, next2, down2)) + (x[1] + col_next(x[1])),
        ]
        r = [load_s(q, t) - (load_d(q, t) * x[q] - beside[q]) for q in range(4)]
        keep(t, r)
        c0[t] = (col_prev(r[2]) + col_next(r[0])) + 3.0 * (r[0] + r[2])
        c1[t] = (col_prev(r[3]) + col_next(r[1])) + 3.0 * (r[1] + r[3])
        return here1, here3, next0, next2

    start = (
        roll_up(v[1][tiles]), roll_up(v[3][tiles]), roll_down(v[0][0]), roll_down(v[2][0])
    )
    body(tiles, loop(tiles, body, start, unroll))


def restrict(c0, c1, tiles, rows, use, unroll):
    lane = lane_ids(rows)

    def body(t, carry):
        up, down = carry
        here, other = c0[t, :rows], c1[t, :rows]
        up_here = roll_up(other)
        down_next = roll_down(c0[after(t, tiles), :rows])
        north = jnp.where(lane == 0, up, up_here)
        south = jnp.where(lane == LANES - 1, down_next, down)
        use(t, ((north + south) + 3.0 * (here + other)) * (1.0 / 16.0))
        return up_here, down_next

    start = roll_up(c1[tiles, :rows]), roll_down(c0[0, :rows])
    body(tiles, loop(tiles, body, start, unroll))


def fine_kernel(
    s_ref, d_ref, i_ref, d1_ref, from_other, from_mate, polar_ref, corner_near, corner_far,
    r_ref, s1_ref, d1_virtual, d2_virtual, to_mate, to_other,
    v0, v1, v2, v3, c0, c1, hs, hd, hi, ps, pd, pi, n1, temp,
):
    v = [v0, v1, v2, v3]
    tiles, rows = s_ref.shape[1], s_ref.shape[2]
    sub = row_ids(8)
    odd = is_odd()

    def halo(t, _):
        fill_halo(t, from_mate, from_other, odd, False, hs, hd, hi)
        return 0

    loop(tiles, halo, 0, 8)
    total = -16.0
    for q in range(4):
        own_s, own_d = polar_unpacked(polar_ref, q)
        near_s, near_d = polar_unpacked(corner_near, q)
        far_s, far_d = polar_unpacked(corner_far, q)
        left_s, right_s = chosen(odd, near_s, far_s)
        left_d, right_d = chosen(odd, near_d, far_d)
        total = total + own_d
        ps[q] = own_s
        pd[q] = own_d
        pi[q] = 1.0 / own_d
        source = jnp.where(sub >= 5, left_s, jnp.where(sub <= 2, right_s, 0.0))
        diag = jnp.where(sub >= 5, left_d, jnp.where(sub <= 2, right_d, 4.0))
        hs[q, tiles] = source
        hd[q, tiles] = diag
        hi[q, tiles] = 1.0 / diag

    load_s = loader(s_ref, hs, ps, tiles)
    smooth(v, load_s, loader(i_ref, hi, pi, tiles), tiles, 32)

    def keep(t, r):
        if not (isinstance(t, int) and t == tiles):
            for q in range(4):
                r_ref[q, t] = r[q][:rows]

    residuals(v, load_s, loader(d_ref, hd, pd, tiles), tiles, c0, c1, keep, 16)

    def coarse(t, value):
        n1[t] = value

    restrict(c0, c1, tiles, rows, coarse, 16)

    def edges(t, source, diag, swapped):
        store_edges(t, edge_packs(source, diag, swapped), odd, to_mate, to_other)

    def use(c, source):
        for q in range(4):
            s1_ref[q, c] = source[q]
        edges(c, source, [d1_ref[q, c] for q in range(4)], False)

    tiles1 = tiles // 2
    split_tiles(lambda t: n1[t], tiles1, rows, splitter(), temp, use)
    out = moved(jnp.concatenate([n1[tiles], total], 0), virtual_splitter())
    source = quarters_of(out[:rows], temp.at[0])
    screen = quarters_of(out[rows:], temp.at[1])
    diag = [4.0 + x for x in screen]
    for q in range(4):
        s1_ref[q, tiles1] = source[q]
        d1_virtual[q] = diag[q]
    d2_virtual[...] = 4.0 + ((screen[0] + screen[1]) + (screen[2] + screen[3]))
    edges(tiles1, source, diag, True)


def merge_kernel(r_ref, out_ref, temp, out_buf, sems):
    tiles = r_ref.shape[1]
    rows = r_ref.shape[2]
    matrix = merger()
    chunk = out_ref.shape[1] // GROUPS
    copies = []
    for group in range(GROUPS):
        for batch in range(tiles // GROUPS // BATCH):
            start = group * (tiles // GROUPS) + batch * BATCH
            both = []
            for i in range(BATCH):
                for pr in (0, 1):
                    for pc in (0, 1):
                        temp[i, pr, pl.ds(pc, rows, 2), :] = r_ref[2 * pc + pr, start + i]
                both.append(jnp.concatenate([temp[i, 0], temp[i, 1]], 1))
            out = moved(jnp.concatenate(both, 0), matrix)
            for i in range(BATCH):
                where = slice((start + i) * 256, (start + i + 1) * 256)
                out_buf[:, where] = out[2 * rows * i : 2 * rows * (i + 1)]
        part = pl.ds(group * chunk, chunk)
        copy = pltpu.make_async_copy(out_buf.at[:, part], out_ref.at[:, part], sems.at[group])
        copy.start()
        copies.append(copy)
    for copy in copies:
        copy.wait()


def middle_kernel(
    merged_first, s_ref, d_ref, i_ref, d_virtual, d2_ref, d2_virtual, from_other, from_mate,
    s2_ref, to_mate, to_other,
    v0, v1, v2, v3, c0, c1, hs, hd, hi, pi,
):
    v = [v0, v1, v2, v3]
    tiles, rows = d_ref.shape[1], d_ref.shape[2]
    odd = is_odd()
    for t in range(tiles + 1):
        fill_halo(t, from_mate, from_other, odd, t == tiles, hs, hd, hi)
    for q in range(4):
        pi[q] = 1.0 / d_virtual[q]

    def load_s(q, t):
        return jnp.concatenate([s_ref[q, t], hs[q, t]], 0)

    smooth(v, load_s, loader(i_ref, hi, pi, tiles), tiles, 16)
    residuals(
        v, load_s, loader(d_ref, hd, d_virtual, tiles), tiles, c0, c1, lambda t, r: None, 16
    )
    sub = row_ids(8)

    def coarse(t, value):
        diag = d2_virtual[...] if t == tiles else d2_ref[t]
        s2_ref[t] = value
        right = jnp.where(sub < 4, roll_rows(value[rows - 8 :], 4), diag[rows - 8 :])
        left = jnp.where(sub < 4, value[:8], roll_rows(diag[:8], 4))
        to_mate[t], to_other[t] = chosen(odd, left, right)

    restrict(c0, c1, tiles, rows, coarse, 16)


def last_kernel(
    s_ref, d_ref, d_virtual, from_other, from_mate,
    solution_ref, residual_ref,
    s, d, inv, va, vb,
):
    tiles, own = d_ref.shape[0], d_ref.shape[1]
    rows = own + 8
    sub = row_ids(8)
    lane, row = lane_ids(rows), row_ids(rows)
    even = (lane + row) % 2 == 0
    odd = jnp.logical_not(even)
    odd_band = is_odd()
    for t in range(tiles + 1):
        left, right = chosen(odd_band, from_mate[t], from_other[t])
        diag = d_virtual[...] if t == tiles else d_ref[t]
        source = jnp.concatenate(
            [s_ref[t], jnp.where(sub < 4, right, roll_rows(left, 4))], 0
        )
        diag = jnp.concatenate([diag, jnp.where(sub < 4, roll_rows(right, 4), left)], 0)
        inverse = 1.0 / diag
        s[t] = source
        d[t] = diag
        inv[t] = inverse
        va[t] = jnp.where(odd if t == tiles else even, source * inverse, 0.0)

    def scan(v, use):
        up, down = roll_up(v[tiles]), roll_down(v[0])
        for t in range(tiles + 1):
            x = v[t]
            up_here, down_next = roll_up(x), roll_down(v[after(t, tiles)])
            north = jnp.where(lane == 0, up, up_here)
            south = jnp.where(lane == LANES - 1, down_next, down)
            use(t, x, (col_prev(x) + col_next(x)) + (north + south))
            up, down = up_here, down_next

    for old, new, mask, other in ((va, vb, odd, even), (vb, va, even, odd), (va, vb, odd, even)):

        def relax(t, x, beside):
            update = other if t == tiles else mask
            new[t] = jnp.where(update, (s[t] + beside) * inv[t], x)

        scan(old, relax)

    def finish(t, x, beside):
        if t < tiles:
            where = slice(t * LANES, (t + 1) * LANES)
            solution_ref[:, where] = x[:own]
            residual_ref[:, where] = (s[t] - (d[t] * x - beside))[:own]

    scan(vb, finish)


VMEM = pl.BlockSpec(memory_space=pltpu.VMEM)
HBM = pl.BlockSpec(memory_space=pltpu.HBM)


def call(kernel, out_shapes, scratch, *args, sems=None, far_in=0, far_out=0):
    scratch = [pltpu.VMEM(x, F32) if isinstance(x, tuple) else x for x in scratch]
    if sems is not None:
        scratch.append(pltpu.SemaphoreType.DMA(sems))
    return pl.pallas_call(
        kernel,
        out_shape=[jax.ShapeDtypeStruct(shape, F32) for shape in out_shapes],
        in_specs=[HBM] * far_in + [VMEM] * (len(args) - far_in),
        out_specs=[HBM] * far_out + [VMEM] * (len(out_shapes) - far_out),
        scratch_shapes=scratch,
        compiler_params=pltpu.CompilerParams(vmem_limit_bytes=40 * 2**20),
    )(*args)


def swapped_with(x, by):
    count = lax.axis_size("lon")
    pairs = [(i, (i + by) % count) for i in range(0, count, 2)]
    return lax.ppermute(x, "lon", pairs + [(b, a) for a, b in pairs])


def swapped_edges(to_mate, to_other):
    from_mate = swapped_with(to_mate, 1)
    return from_mate, swapped_with(to_other, -1)


def body(right_side, texel_weight, seam_flags):
    columns, height = right_side.shape
    half_turn = lax.axis_size("lon") // 2
    tiles, rows = height // 256, columns // 2
    tiles1, rows1 = tiles // 2, rows // 2
    temp = (BATCH, 2, columns, LANES)
    quarters = (4, tiles, rows, LANES)
    quarters1 = (4, tiles1, rows1, LANES)
    pack = (2, tiles, 8, LANES)
    corner = (2, 8, LANES)
    split = (2, 16 * tiles, LANES)
    to_mate, to_other, polar, corner_near, corner_far = call(
        edge_kernel,
        [pack, pack, (2, rows, LANES), corner, corner],
        [(16, height), pltpu.VMEM((32, height), BF16)]
        + [(2, columns, 256), pltpu.VMEM((2, columns, 256), BF16)]
        + [pltpu.VMEM(seam_flags.shape, jnp.int32), split, split]
        + [(2, 2, columns, LANES)] * 2
        + [(tiles, 8, LANES)],
        *[
            pltpu.with_memory_space_constraint(x, pltpu.HBM)
            for x in (right_side, texel_weight, seam_flags)
        ],
        sems=(9,), far_in=3,
    )
    from_mate, from_other = swapped_edges(to_mate, to_other)
    polar = lax.ppermute(
        polar, "lon", [(i, (i + half_turn) % (2 * half_turn)) for i in range(2 * half_turn)]
    )
    corner_near_own = corner_near
    corner_far = swapped_with(corner_far, half_turn - 1)
    corner_near = swapped_with(corner_near, half_turn + 1)
    s, d, inverse, d1, i1, d2 = call(
        bulk_kernel,
        [quarters] * 3 + [quarters1, quarters1, quarters1[1:]],
        [temp, temp, (tiles, 8, LANES), quarters[1:]],
        right_side, texel_weight, seam_flags, corner_near_own,
    )

    def level_scratch(tiles, rows):
        halo = (4, tiles + 1, 8, LANES)
        return [(tiles + 1, rows + 8, LANES)] * 6 + [halo] * 3

    pack1 = (2, tiles1 + 1, 8, LANES)
    r, s1, d1_virtual, d2_virtual, to_mate, to_other = call(
        fine_kernel,
        [quarters, (4, tiles1 + 1, rows1, LANES), (4, rows1, LANES), (rows1, LANES), pack1, pack1],
        level_scratch(tiles, rows)
        + [(4, rows, LANES)] * 3
        + [(tiles + 1, rows, LANES), (BATCH, 2, rows, LANES)],
        s, d, inverse, d1, from_other, from_mate, polar, corner_near, corner_far,
    )
    from_mate, from_other = swapped_edges(to_mate, to_other)
    (fine_residual,) = call(
        merge_kernel, [(columns, height)], [temp, (columns, height)], r,
        sems=(GROUPS,), far_out=1,
    )
    pack2 = (tiles1 + 1, 8, LANES)
    s2, to_mate, to_other = call(
        middle_kernel,
        [(tiles1 + 1, rows1, LANES), pack2, pack2],
        level_scratch(tiles1, rows1) + [(4, rows1, LANES)],
        pltpu.with_memory_space_constraint(fine_residual, pltpu.HBM),
        s1, d1, i1, d1_virtual, d2, d2_virtual, from_other, from_mate,
        far_in=1,
    )
    from_mate, from_other = swapped_edges(to_mate, to_other)
    solution_2, residual_2 = call(
        last_kernel,
        [(columns // 4, height // 4)] * 2,
        [(tiles1 + 1, rows1 + 8, LANES)] * 5,
        s2, d2, d2_virtual, from_other, from_mate,
    )
    return fine_residual, solution_2, residual_2


def solution(mesh):
    spec = P(("groups", "lon"), None)
    return jax.shard_map(
        body, mesh=mesh, in_specs=(spec,) * 3, out_specs=(spec,) * 3, check_vma=False
    )
```

```python
import jax
import jax.numpy as jnp
from jax import lax
from jax.experimental import pallas as pl
from jax.experimental.pallas import tpu as pltpu
from jax.sharding import PartitionSpec as P

TILE = 32
SEAM_SCALE = 0.1
LANES = 128
GROUPS = 4
BATCH = 4
F32 = jnp.float32
BF16 = jnp.bfloat16


def loop(count, body, carry=0, unroll=4):
    unroll = min(unroll, count)

    def steps(block, carry):
        for i in range(unroll):
            carry = body(block * unroll + i, carry)
        return carry

    whole = count // unroll
    carry = steps(0, carry) if whole == 1 else lax.fori_loop(0, whole, steps, carry)
    for t in range(whole * unroll, count):
        carry = body(t, carry)
    return carry


def before(t, tiles):
    return (tiles if t == 0 else t - 1) if isinstance(t, int) else jnp.where(t == 0, tiles, t - 1)


def after(t, tiles):
    return (0 if t == tiles else t + 1) if isinstance(t, int) else t + 1


def lane_ids(rows):
    return lax.broadcasted_iota(jnp.int32, (rows, LANES), 1)


def row_ids(rows):
    return lax.broadcasted_iota(jnp.int32, (rows, LANES), 0)


def roll_up(x):
    return pltpu.roll(x, 1, 1)


def roll_down(x):
    return pltpu.roll(x, LANES - 1, 1)


def roll_rows(x, by):
    by %= x.shape[0]
    return x if by == 0 else pltpu.roll(x, by, 0)


def roll_lanes(x, by):
    by %= LANES
    return x if by == 0 else pltpu.roll(x, by, 1)


def col_prev(x):
    return pltpu.roll(x, 1, 0)


def col_next(x):
    return pltpu.roll(x, x.shape[0] - 1, 0)


def selector(shape, rule):
    a = lax.broadcasted_iota(jnp.int32, shape, 0)
    b = lax.broadcasted_iota(jnp.int32, shape, 1)
    return jnp.where(rule(a, b), 1.0, 0.0).astype(BF16)


def splitter():
    return selector((256, 256), lambda a, b: a == 2 * (b % LANES) + b // LANES)


def merger():
    return selector((256, 256), lambda a, b: b == 2 * (a % LANES) + a // LANES)


def virtual_splitter():
    return selector(
        (LANES, 256),
        lambda a, b: a // 2 + jnp.where(a >= 64, 64, 0) + LANES * (a % 2) == b,
    )


def moved(x, matrix, exact=None):
    rows = x.shape[0]
    high = x.astype(BF16)
    low = (x - high.astype(F32)).astype(BF16)
    terms = [high, low] if exact is None else [high, low, exact]
    out = jnp.dot(jnp.concatenate(terms, 0), matrix, preferred_element_type=F32)
    both = out[:rows] + out[rows : 2 * rows]
    return both if exact is None else (both, out[2 * rows :])


def quarters_of(parts, temp):
    count = parts.shape[0] // 2
    temp[0] = parts[:, :LANES]
    temp[1] = parts[:, LANES:]
    return [temp[pr, pl.ds(pc, count, 2), :] for pc in (0, 1) for pr in (0, 1)]


def reds(swapped):
    return (1, 2) if swapped else (0, 3)


def interleaved(group, offset):
    sub = row_ids(8)
    packed = roll_rows(group[0], offset)
    for q in range(1, 4):
        packed = jnp.where(sub // 2 == q, roll_rows(group[q], 2 * q + offset), packed)
    return packed


def edge_packs(source, diag, swapped):
    sub = row_ids(8)
    even, odd = reds(swapped)
    rows = source[0].shape[0]
    packs = []
    for here, first, second, row, step in (
        (slice(rows - 8, rows), even, odd, 6, 1),
        (slice(0, 8), odd, even, 1, -1),
    ):
        gs = [x[here] for x in source]
        gd = [x[here] for x in diag]
        near = gs[first] / gd[first]
        far = roll_rows(gs[second] / gd[second], step)
        gs[first] = jnp.where(sub == row, near, gs[first])
        gd[first] = jnp.where(sub == row, far, gd[first])
        offset = 2 if row == 6 else 0
        packs.append((interleaved(gs, offset), interleaved(gd, offset)))
    return packs


def unpacked_halo(left, right, swapped):
    sub = row_ids(8)
    even, odd = reds(swapped)
    (al, bl), (ar, br) = left, right
    source, diag = [], []
    for q in range(4):
        s = jnp.where(
            sub >= 6,
            roll_rows(al, 6 - 2 * q),
            jnp.where(sub <= 1, roll_rows(ar, -2 * q), 0.0),
        )
        d = jnp.where(
            sub >= 6,
            roll_rows(bl, 6 - 2 * q),
            jnp.where(sub <= 1, roll_rows(br, -2 * q), 4.0),
        )
        if q == even:
            s = jnp.where(sub == 2, roll_rows(br, 1 - 2 * odd), s)
            d = jnp.where((sub == 2) | (sub == 6), 1.0, d)
        if q == odd:
            s = jnp.where(sub == 5, roll_rows(bl, 5 - 2 * even), s)
            d = jnp.where((sub == 5) | (sub == 1), 1.0, d)
        source.append(s)
        diag.append(d)
    return source, diag


def is_odd():
    return lax.rem(lax.axis_index("lon"), 2) == 1


def chosen(odd, a, b):
    return jnp.where(odd, a, b), jnp.where(odd, b, a)


def store_edges(t, packs, odd, to_mate, to_other):
    right, left = packs
    for i in (0, 1):
        to_mate[i, t], to_other[i, t] = chosen(odd, left[i], right[i])


def fill_halo(t, from_mate, from_other, odd, swapped, hs, hd, hi):
    al, ar = chosen(odd, from_mate[0, t], from_other[0, t])
    bl, br = chosen(odd, from_mate[1, t], from_other[1, t])
    source, diag = unpacked_halo((al, bl), (ar, br), swapped)
    for q in range(4):
        hs[q, t] = source[q]
        hd[q, t] = diag[q]
        hi[q, t] = 1.0 / diag[q]


def loader(own, halo, virtual, tiles):
    def load(q, t):
        if isinstance(t, int) and t == tiles:
            return jnp.concatenate([virtual[q], halo[q, t]], 0)
        return jnp.concatenate([own[q, t], halo[q, t]], 0)

    return load


def polar_packs(tiles_of):
    lane = lane_ids(tiles_of[0][0].shape[0])
    packs = []
    for pc in (0, 1):
        parts = [*tiles_of[2 * pc], *tiles_of[2 * pc + 1]]
        packed = parts[0]
        for m in range(1, 4):
            mine = (lane + (16 - 32 * m) % LANES) % LANES < 32
            packed = jnp.where(mine, roll_lanes(parts[m], 32 * m), packed)
        packs.append(packed)
    return packs


def polar_unpacked(x, q):
    lane = lane_ids(x.shape[1])
    used = (lane < 16) | (lane >= LANES - 16)
    m = 2 * (q % 2)
    return (
        jnp.where(used, roll_lanes(x[q // 2], 32 * m), 0.0),
        jnp.where(used, roll_lanes(x[q // 2], 32 * (m + 1)), 4.0),
    )


def seam_scales(flags, chunks):
    flag_cols, flag_lats = flags.shape
    flags = jnp.concatenate(
        [flags.astype(F32), jnp.zeros((8 - flag_cols, flag_lats), F32)], 0
    )
    lat = lax.broadcasted_iota(jnp.int32, (8, flag_lats), 1)
    stacked = jnp.concatenate([jnp.where(lat // 8 == c, flags, 0.0) for c in chunks], 0)
    spread = selector((flag_lats, LANES), lambda a, b: a % 8 == b // (TILE // 2))
    spread_flags = jnp.dot(stacked.astype(BF16), spread, preferred_element_type=F32)
    scale = jnp.where(spread_flags > 0.5, SEAM_SCALE, 1.0)
    return scale.reshape(len(chunks), 8, LANES)


def seam_rows(scales, flag_cols, rows):
    size = (rows // flag_cols, LANES)
    return jnp.concatenate(
        [jnp.broadcast_to(scales[i : i + 1], size) for i in range(flag_cols)], 0
    )


def edge_kernel(
    right_ref, weight_ref, flag_ref,
    to_mate, to_other, polar_ref, corner_near, corner_far,
    edge_s, edge_w, end_s, end_w, flags, temp_s, temp_w, temp_p, temp_q, scale_ref, sems,
):
    columns, height = right_ref.shape
    rows, tiles = columns // 2, height // 256
    pairs = [(flag_ref, flags)]
    for i, (src, dst, size) in enumerate(
        ((right_ref, edge_s, 8), (weight_ref, edge_w, 16))
    ):
        pairs.append((src.at[pl.ds(0, size)], dst.at[pl.ds(0, size)]))
        pairs.append((src.at[pl.ds(columns - size, size)], dst.at[pl.ds(size, size)]))
    for src, dst in ((right_ref, end_s), (weight_ref, end_w)):
        for end, start in enumerate((0, height - 256)):
            pairs.append((src.at[:, pl.ds(start, 256)], dst.at[end]))
    copies = [
        pltpu.make_async_copy(src, dst, sems.at[i]) for i, (src, dst) in enumerate(pairs)
    ]
    for copy in copies:
        copy.start()
    odd = is_odd()
    matrix = splitter()
    flag_cols = flag_ref.shape[0]
    copies[0].wait()
    scale_ref[...] = seam_scales(flags[...], range(tiles))
    for copy in copies[1:5]:
        copy.wait()
    sub = row_ids(8)
    lanes = [slice(c * 256, (c + 1) * 256) for c in range(tiles)]
    source, weight = moved(
        jnp.concatenate([edge_s[:, w] for w in lanes], 0),
        matrix,
        jnp.concatenate([edge_w[:, w] for w in lanes], 0),
    )
    weight = weight.reshape(tiles, 32, 256)
    weight = jnp.concatenate([weight[:, :8], weight[:, 24:]], 1).reshape(tiles * 16, 256)
    source = quarters_of(source, temp_s)
    weight = quarters_of(weight, temp_w)
    for c in range(tiles):
        here = slice(c * 8, (c + 1) * 8)
        scales = scale_ref[c]
        scale = jnp.where(sub < 4, scales[:1], scales[flag_cols - 1 : flag_cols])
        diag = [4.0 + w[here] * scale for w in weight]
        store_edges(
            c, edge_packs([x[here] for x in source], diag, False), odd, to_mate, to_other
        )

    for copy in copies[5:]:
        copy.wait()
    mirror = selector((LANES, LANES), lambda a, b: a + b == LANES - 1)
    lane = lane_ids(rows)
    source, weight = moved(
        jnp.concatenate([end_s[0], end_s[1]], 0),
        matrix,
        jnp.concatenate([end_w[0], end_w[1]], 0),
    )
    found = []
    for end, c in enumerate((0, tiles - 1)):
        here = slice(end * columns, (end + 1) * columns)
        scale = seam_rows(scale_ref[c], flag_cols, rows)
        found.append(
            (
                quarters_of(source[here], temp_p.at[end]),
                [4.0 + w * scale for w in quarters_of(weight[here], temp_q.at[end])],
            )
        )
    ends = [
        [jnp.where(lane >= 64, found[1][i][q ^ 1], found[0][i][q ^ 1]) for i in (0, 1)]
        for q in range(4)
    ]
    both = moved(jnp.concatenate(polar_packs(ends), 0), mirror)
    for pc in (0, 1):
        pack = both[pc * rows : (pc + 1) * rows]
        polar_ref[pc] = pack
        corner_near[pc], corner_far[pc] = chosen(odd, pack[:8], pack[rows - 8 :])


def bulk_kernel(
    right_ref, weight_ref, flag_ref, edges_first,
    s_ref, d_ref, i_ref, d1_ref, i1_ref, d2_ref,
    temp_s, temp_d, scale_ref, e_ref,
):
    tiles, rows = s_ref.shape[1], s_ref.shape[2]
    columns = 2 * rows
    matrix = splitter()
    scale_ref[...] = seam_scales(flag_ref[...], range(tiles))
    for start in range(0, tiles, BATCH):
        lanes = [slice((start + i) * 256, (start + i + 1) * 256) for i in range(BATCH)]
        source, weight = moved(
            jnp.concatenate([right_ref[:, w] for w in lanes], 0),
            matrix,
            jnp.concatenate([weight_ref[:, w] for w in lanes], 0),
        )
        for i in range(BATCH):
            c = start + i
            here = slice(i * columns, (i + 1) * columns)
            scale = seam_rows(scale_ref[c], flag_ref.shape[0], rows)
            for q, value in enumerate(quarters_of(source[here], temp_s.at[i])):
                s_ref[q, c] = value
            screen = [w * scale for w in quarters_of(weight[here], temp_d.at[i])]
            e_ref[c] = (screen[0] + screen[1]) + (screen[2] + screen[3])
            for q in range(4):
                diag = 4.0 + screen[q]
                d_ref[q, c] = diag
                i_ref[q, c] = 1.0 / diag

    def use(c, screen):
        for q in range(4):
            d1_ref[q, c] = 4.0 + screen[q]
            i1_ref[q, c] = 1.0 / (4.0 + screen[q])
        d2_ref[c] = 4.0 + ((screen[0] + screen[1]) + (screen[2] + screen[3]))

    split_tiles(lambda t: e_ref[t], tiles // 2, rows, matrix, temp_s, use)


def split_tiles(load, tiles, rows, matrix, temp, use):
    for start in range(0, tiles, BATCH):
        wide = [
            jnp.concatenate([load(2 * c), load(2 * c + 1)], 1)
            for c in range(start, start + BATCH)
        ]
        out = moved(jnp.concatenate(wide, 0), matrix)
        for i in range(BATCH):
            use(start + i, quarters_of(out[i * rows : (i + 1) * rows], temp.at[i, :, :rows]))


def half_sweep(v, load_s, load_i, tiles, red, unroll):
    rows = v[0].shape[1]
    lane = lane_ids(rows)
    y, z, qa, qb = (1, 2, 0, 3) if red else (3, 0, 2, 1)
    col_a, col_b = (col_prev, col_next) if red else (col_next, col_prev)

    def beside_virtual(q):
        ns, we = q ^ 1, q ^ 2
        here = v[ns][tiles]
        if q % 2 == 0:
            lat = jnp.where(lane == 0, roll_up(v[ns][tiles - 1]), roll_up(here))
        else:
            lat = jnp.where(lane == LANES - 1, roll_down(v[ns][0]), roll_down(here))
        cols = v[we][tiles]
        return (here + lat) + (cols + (col_prev if q < 2 else col_next)(cols))

    held = [
        (q, (load_s(q, tiles) + beside_virtual(q)) * load_i(q, tiles)) for q in (y, z)
    ]

    def body(t, carry):
        y_before, z_here = carry
        vy, vz = v[y][t], v[z][t]
        y_here = roll_up(vy)
        z_after = roll_down(v[z][t + 1])
        lat_a = vy + jnp.where(lane == 0, y_before, y_here)
        lat_b = vz + jnp.where(lane == LANES - 1, z_after, z_here)
        v[qa][t] = (load_s(qa, t) + (lat_a + (vz + col_a(vz)))) * load_i(qa, t)
        v[qb][t] = (load_s(qb, t) + (lat_b + (vy + col_b(vy)))) * load_i(qb, t)
        return y_here, z_after

    loop(tiles, body, (roll_up(v[y][tiles]), roll_down(v[z][0])), unroll)
    for q, value in held:
        v[q][tiles] = value


def smooth(v, load_s, load_i, tiles, unroll):
    zeros = jnp.zeros(v[0].shape[1:], F32)

    def first(t, _):
        for q in (0, 3):
            v[q][t] = load_s(q, t) * load_i(q, t)
        return 0

    loop(tiles, first, 0, unroll)
    for q in (1, 2):
        v[q][0] = zeros
        v[q][tiles - 1] = zeros
        v[q][tiles] = load_s(q, tiles) * load_i(q, tiles)
        v[3 * (q - 1)][tiles] = zeros
    half_sweep(v, load_s, load_i, tiles, False, unroll)
    half_sweep(v, load_s, load_i, tiles, True, unroll)
    half_sweep(v, load_s, load_i, tiles, False, unroll)


def residuals(v, load_s, load_d, tiles, c0, c1, keep, unroll):
    lane = lane_ids(v[0].shape[1])

    def body(t, carry):
        up1, up3, down0, down2 = carry
        x = [v[q][t] for q in range(4)]
        here1, here3 = roll_up(x[1]), roll_up(x[3])
        next0, next2 = (roll_down(v[q][after(t, tiles)]) for q in (0, 2))
        beside = [
            (x[1] + jnp.where(lane == 0, up1, here1)) + (x[2] + col_prev(x[2])),
            (x[0] + jnp.where(lane == LANES - 1, next0, down0)) + (x[3] + col_prev(x[3])),
            (x[3] + jnp.where(lane == 0, up3, here3)) + (x[0] + col_next(x[0])),
            (x[2] + jnp.where(lane == LANES - 1, next2, down2)) + (x[1] + col_next(x[1])),
        ]
        r = [load_s(q, t) - (load_d(q, t) * x[q] - beside[q]) for q in range(4)]
        keep(t, r)
        c0[t] = (col_prev(r[2]) + col_next(r[0])) + 3.0 * (r[0] + r[2])
        c1[t] = (col_prev(r[3]) + col_next(r[1])) + 3.0 * (r[1] + r[3])
        return here1, here3, next0, next2

    start = (
        roll_up(v[1][tiles]), roll_up(v[3][tiles]), roll_down(v[0][0]), roll_down(v[2][0])
    )
    body(tiles, loop(tiles, body, start, unroll))


def restrict(c0, c1, tiles, rows, use, unroll):
    lane = lane_ids(rows)

    def body(t, carry):
        up, down = carry
        here, other = c0[t, :rows], c1[t, :rows]
        up_here = roll_up(other)
        down_next = roll_down(c0[after(t, tiles), :rows])
        north = jnp.where(lane == 0, up, up_here)
        south = jnp.where(lane == LANES - 1, down_next, down)
        use(t, ((north + south) + 3.0 * (here + other)) * (1.0 / 16.0))
        return up_here, down_next

    start = roll_up(c1[tiles, :rows]), roll_down(c0[0, :rows])
    body(tiles, loop(tiles, body, start, unroll))


def ends_of(x, rows):
    return x[rows - 8 : rows], x[:8]


def virtual_tiles(polar_ref, ps, pd, pi):
    total = -16.0
    for q in range(4):
        source, diag = polar_unpacked(polar_ref, q)
        total = total + diag
        ps[q] = source
        pd[q] = diag
        pi[q] = 1.0 / diag
    return total


def rim_kernel(
    s_ref, d_ref, i_ref, d1_ref, from_other, from_mate, polar_ref, corner_near, corner_far,
    r_ref, n_ref, to_mate, to_other,
    v0, v1, v2, v3, c0, c1, hs, hd, hi, ps, pd, pi, temp,
):
    v = [v0, v1, v2, v3]
    tiles, rows = s_ref.shape[1], s_ref.shape[2]
    sub = row_ids(8)
    odd = is_odd()

    def halo(t, _):
        fill_halo(t, from_mate, from_other, odd, False, hs, hd, hi)
        return 0

    loop(tiles, halo, 0, 8)
    total = virtual_tiles(polar_ref, ps, pd, pi)
    for q in range(4):
        near_s, near_d = polar_unpacked(corner_near, q)
        far_s, far_d = polar_unpacked(corner_far, q)
        left_s, right_s = chosen(odd, near_s, far_s)
        left_d, right_d = chosen(odd, near_d, far_d)
        source = jnp.where(sub >= 5, left_s, jnp.where(sub <= 2, right_s, 0.0))
        diag = jnp.where(sub >= 5, left_d, jnp.where(sub <= 2, right_d, 4.0))
        hs[q, tiles] = source
        hd[q, tiles] = diag
        hi[q, tiles] = 1.0 / diag

    def rim(own, halo, virtual):
        def load(q, t):
            if isinstance(t, int) and t == tiles:
                last, first = virtual[q, rows - 8 :], virtual[q, :8]
            else:
                last, first = own[q, t, rows - 8 :], own[q, t, :8]
            return jnp.concatenate([last, halo[q, t], first], 0)

        return load

    load_s = rim(s_ref, hs, ps)
    smooth(v, load_s, rim(i_ref, hi, pi), tiles, 32)

    def keep(t, r):
        if not (isinstance(t, int) and t == tiles):
            for q in range(4):
                r_ref[q, t] = jnp.concatenate([r[q][16:], r[q][:8]], 0)

    residuals(v, load_s, rim(d_ref, hd, pd), tiles, c0, c1, keep, 16)

    def coarse(t, value):
        n_ref[t] = jnp.concatenate([value[16:], value[:8]], 0)

    restrict(c0, c1, tiles, 24, coarse, 16)

    rows1 = rows // 2

    def use(c, source):
        diag = [
            jnp.where(sub < 4, d1_ref[q, c, :8], d1_ref[q, c, rows1 - 8 :]) for q in range(4)
        ]
        store_edges(c, edge_packs(source, diag, False), odd, to_mate, to_other)

    tiles1 = tiles // 2
    split_tiles(lambda t: n_ref[t], tiles1, 16, splitter(), temp, use)
    out = moved(
        jnp.concatenate([n_ref[tiles], total[:8], total[rows - 8 :]], 0), virtual_splitter()
    )
    source = quarters_of(out[:16], temp.at[0])
    diag = [4.0 + x for x in quarters_of(out[16:], temp.at[1])]
    store_edges(tiles1, edge_packs(source, diag, True), odd, to_mate, to_other)


def core_kernel(
    s_ref, d_ref, i_ref, polar_ref, rim_r, rim_n,
    r_ref, s1_ref, d1_virtual, d2_virtual,
    v0, v1, v2, v3, c0, c1, ps, pd, pi, n1, temp,
):
    v = [v0, v1, v2, v3]
    tiles, rows = s_ref.shape[1], s_ref.shape[2]
    sub = row_ids(8)
    total = virtual_tiles(polar_ref, ps, pd, pi)

    def core(own, virtual):
        def load(q, t):
            return virtual[q] if isinstance(t, int) and t == tiles else own[q, t]

        return load

    def stitched(first, value, last):
        return jnp.concatenate(
            [
                jnp.where(sub < 3, first, value[:8]),
                value[8 : rows - 8],
                jnp.where(sub > 4, last, value[rows - 8 :]),
            ],
            0,
        )

    load_s = core(s_ref, ps)
    smooth(v, load_s, core(i_ref, pi), tiles, 32)

    def keep(t, r):
        if not (isinstance(t, int) and t == tiles):
            for q in range(4):
                r_ref[q, t] = stitched(rim_r[q, t, :8], r[q], rim_r[q, t, 8:])

    residuals(v, load_s, core(d_ref, pd), tiles, c0, c1, keep, 16)

    def coarse(t, value):
        n1[t] = stitched(rim_n[t, :8], value, rim_n[t, 8:])

    restrict(c0, c1, tiles, rows, coarse, 16)

    def use(c, source):
        for q in range(4):
            s1_ref[q, c] = source[q]

    tiles1 = tiles // 2
    split_tiles(lambda t: n1[t], tiles1, rows, splitter(), temp, use)
    out = moved(jnp.concatenate([n1[tiles], total], 0), virtual_splitter())
    source = quarters_of(out[:rows], temp.at[0])
    screen = quarters_of(out[rows:], temp.at[1])
    for q in range(4):
        s1_ref[q, tiles1] = source[q]
        d1_virtual[q] = 4.0 + screen[q]
    d2_virtual[...] = 4.0 + ((screen[0] + screen[1]) + (screen[2] + screen[3]))


def merge_kernel(r_ref, out_ref, temp, out_buf, sems):
    tiles = r_ref.shape[1]
    rows = r_ref.shape[2]
    matrix = merger()
    chunk = out_ref.shape[1] // GROUPS
    copies = []
    for group in range(GROUPS):
        for batch in range(tiles // GROUPS // BATCH):
            start = group * (tiles // GROUPS) + batch * BATCH
            both = []
            for i in range(BATCH):
                for pr in (0, 1):
                    for pc in (0, 1):
                        temp[i, pr, pl.ds(pc, rows, 2), :] = r_ref[2 * pc + pr, start + i]
                both.append(jnp.concatenate([temp[i, 0], temp[i, 1]], 1))
            out = moved(jnp.concatenate(both, 0), matrix)
            for i in range(BATCH):
                where = slice((start + i) * 256, (start + i + 1) * 256)
                out_buf[:, where] = out[2 * rows * i : 2 * rows * (i + 1)]
        part = pl.ds(group * chunk, chunk)
        copy = pltpu.make_async_copy(out_buf.at[:, part], out_ref.at[:, part], sems.at[group])
        copy.start()
        copies.append(copy)
    for copy in copies:
        copy.wait()


def middle_kernel(
    s_ref, d_ref, i_ref, d_virtual, d2_ref, d2_virtual, from_other, from_mate,
    s2_ref, to_mate, to_other,
    v0, v1, v2, v3, c0, c1, hs, hd, hi, pi,
):
    v = [v0, v1, v2, v3]
    tiles, rows = d_ref.shape[1], d_ref.shape[2]
    odd = is_odd()
    for t in range(tiles + 1):
        fill_halo(t, from_mate, from_other, odd, t == tiles, hs, hd, hi)
    for q in range(4):
        pi[q] = 1.0 / d_virtual[q]

    def load_s(q, t):
        return jnp.concatenate([s_ref[q, t], hs[q, t]], 0)

    smooth(v, load_s, loader(i_ref, hi, pi, tiles), tiles, 16)
    residuals(
        v, load_s, loader(d_ref, hd, d_virtual, tiles), tiles, c0, c1, lambda t, r: None, 16
    )
    sub = row_ids(8)

    def coarse(t, value):
        diag = d2_virtual[...] if t == tiles else d2_ref[t]
        s2_ref[t] = value
        right = jnp.where(sub < 4, roll_rows(value[rows - 8 :], 4), diag[rows - 8 :])
        left = jnp.where(sub < 4, value[:8], roll_rows(diag[:8], 4))
        to_mate[t], to_other[t] = chosen(odd, left, right)

    restrict(c0, c1, tiles, rows, coarse, 16)


def last_kernel(
    s_ref, d_ref, d_virtual, from_other, from_mate,
    solution_ref, residual_ref,
    s, d, inv, va, vb,
):
    tiles, own = d_ref.shape[0], d_ref.shape[1]
    rows = own + 8
    sub = row_ids(8)
    lane, row = lane_ids(rows), row_ids(rows)
    even = (lane + row) % 2 == 0
    odd = jnp.logical_not(even)
    odd_band = is_odd()
    for t in range(tiles + 1):
        left, right = chosen(odd_band, from_mate[t], from_other[t])
        diag = d_virtual[...] if t == tiles else d_ref[t]
        source = jnp.concatenate(
            [s_ref[t], jnp.where(sub < 4, right, roll_rows(left, 4))], 0
        )
        diag = jnp.concatenate([diag, jnp.where(sub < 4, roll_rows(right, 4), left)], 0)
        inverse = 1.0 / diag
        s[t] = source
        d[t] = diag
        inv[t] = inverse
        va[t] = jnp.where(odd if t == tiles else even, source * inverse, 0.0)

    def scan(v, use):
        up, down = roll_up(v[tiles]), roll_down(v[0])
        for t in range(tiles + 1):
            x = v[t]
            up_here, down_next = roll_up(x), roll_down(v[after(t, tiles)])
            north = jnp.where(lane == 0, up, up_here)
            south = jnp.where(lane == LANES - 1, down_next, down)
            use(t, x, (col_prev(x) + col_next(x)) + (north + south))
            up, down = up_here, down_next

    for old, new, mask, other in ((va, vb, odd, even), (vb, va, even, odd), (va, vb, odd, even)):

        def relax(t, x, beside):
            update = other if t == tiles else mask
            new[t] = jnp.where(update, (s[t] + beside) * inv[t], x)

        scan(old, relax)

    def finish(t, x, beside):
        if t < tiles:
            where = slice(t * LANES, (t + 1) * LANES)
            solution_ref[:, where] = x[:own]
            residual_ref[:, where] = (s[t] - (d[t] * x - beside))[:own]

    scan(vb, finish)


VMEM = pl.BlockSpec(memory_space=pltpu.VMEM)
HBM = pl.BlockSpec(memory_space=pltpu.HBM)


def call(kernel, out_shapes, scratch, *args, sems=None, far_in=0, far_out=0):
    scratch = [pltpu.VMEM(x, F32) if isinstance(x, tuple) else x for x in scratch]
    if sems is not None:
        scratch.append(pltpu.SemaphoreType.DMA(sems))
    return pl.pallas_call(
        kernel,
        out_shape=[jax.ShapeDtypeStruct(shape, F32) for shape in out_shapes],
        in_specs=[HBM] * far_in + [VMEM] * (len(args) - far_in),
        out_specs=[HBM] * far_out + [VMEM] * (len(out_shapes) - far_out),
        scratch_shapes=scratch,
        compiler_params=pltpu.CompilerParams(vmem_limit_bytes=40 * 2**20),
    )(*args)


def swapped_with(x, by):
    count = lax.axis_size("lon")
    pairs = [(i, (i + by) % count) for i in range(0, count, 2)]
    return lax.ppermute(x, "lon", pairs + [(b, a) for a, b in pairs])


def swapped_edges(to_mate, to_other):
    from_mate = swapped_with(to_mate, 1)
    return from_mate, swapped_with(to_other, -1)


def body(right_side, texel_weight, seam_flags):
    columns, height = right_side.shape
    half_turn = lax.axis_size("lon") // 2
    tiles, rows = height // 256, columns // 2
    tiles1, rows1 = tiles // 2, rows // 2
    temp = (BATCH, 2, columns, LANES)
    quarters = (4, tiles, rows, LANES)
    quarters1 = (4, tiles1, rows1, LANES)
    pack = (2, tiles, 8, LANES)
    corner = (2, 8, LANES)
    split = (2, 16 * tiles, LANES)
    to_mate, to_other, polar, corner_near, corner_far = call(
        edge_kernel,
        [pack, pack, (2, rows, LANES), corner, corner],
        [(16, height), pltpu.VMEM((32, height), BF16)]
        + [(2, columns, 256), pltpu.VMEM((2, columns, 256), BF16)]
        + [pltpu.VMEM(seam_flags.shape, jnp.int32), split, split]
        + [(2, 2, columns, LANES)] * 2
        + [(tiles, 8, LANES)],
        *[
            pltpu.with_memory_space_constraint(x, pltpu.HBM)
            for x in (right_side, texel_weight, seam_flags)
        ],
        sems=(9,), far_in=3,
    )
    from_mate, from_other = swapped_edges(to_mate, to_other)
    polar = lax.ppermute(
        polar, "lon", [(i, (i + half_turn) % (2 * half_turn)) for i in range(2 * half_turn)]
    )
    corner_near_own = corner_near
    corner_far = swapped_with(corner_far, half_turn - 1)
    corner_near = swapped_with(corner_near, half_turn + 1)
    s, d, inverse, d1, i1, d2 = call(
        bulk_kernel,
        [quarters] * 3 + [quarters1, quarters1, quarters1[1:]],
        [temp, temp, (tiles, 8, LANES), quarters[1:]],
        right_side, texel_weight, seam_flags, corner_near_own,
    )

    def level_scratch(tiles, rows):
        return [(tiles + 1, rows, LANES)] * 6

    def halo_scratch(tiles):
        return [(4, tiles + 1, 8, LANES)] * 3

    pack1 = (2, tiles1 + 1, 8, LANES)
    virtual = [(4, rows, LANES)] * 3
    rim_r, rim_n, to_mate, to_other = call(
        rim_kernel,
        [(4, tiles, 16, LANES), (tiles + 1, 16, LANES), pack1, pack1],
        level_scratch(tiles, 24) + halo_scratch(tiles) + virtual + [(BATCH, 2, 16, LANES)],
        s, d, inverse, d1, from_other, from_mate, polar, corner_near, corner_far,
    )
    from_mate, from_other = swapped_edges(to_mate, to_other)
    r, s1, d1_virtual, d2_virtual = call(
        core_kernel,
        [quarters, (4, tiles1 + 1, rows1, LANES), (4, rows1, LANES), (rows1, LANES)],
        level_scratch(tiles, rows)
        + virtual
        + [(tiles + 1, rows, LANES), (BATCH, 2, rows, LANES)],
        s, d, inverse, polar, rim_r, rim_n,
    )
    (fine_residual,) = call(
        merge_kernel, [(columns, height)], [temp, (columns, height)], r,
        sems=(GROUPS,), far_out=1,
    )
    pack2 = (tiles1 + 1, 8, LANES)
    s2, to_mate, to_other = call(
        middle_kernel,
        [(tiles1 + 1, rows1, LANES), pack2, pack2],
        level_scratch(tiles1, rows1 + 8) + halo_scratch(tiles1) + [(4, rows1, LANES)],
        s1, d1, i1, d1_virtual, d2, d2_virtual, from_other, from_mate,
    )
    from_mate, from_other = swapped_edges(to_mate, to_other)
    solution_2, residual_2 = call(
        last_kernel,
        [(columns // 4, height // 4)] * 2,
        [(tiles1 + 1, rows1 + 8, LANES)] * 5,
        s2, d2, d2_virtual, from_other, from_mate,
    )
    return fine_residual, solution_2, residual_2


def solution(mesh):
    spec = P(("groups", "lon"), None)
    return jax.shard_map(
        body, mesh=mesh, in_specs=(spec,) * 3, out_specs=(spec,) * 3, check_vma=False
    )
```

```python
import jax
import jax.numpy as jnp
from jax import lax
from jax.experimental import pallas as pl
from jax.experimental.pallas import tpu as pltpu
from jax.sharding import PartitionSpec as P

TILE = 32
SEAM_SCALE = 0.1
LANES = 128
GROUPS = 4
BATCH = 4
F32 = jnp.float32
BF16 = jnp.bfloat16


def loop(count, body, carry=0, unroll=4):
    unroll = min(unroll, count)

    def steps(block, carry):
        for i in range(unroll):
            carry = body(block * unroll + i, carry)
        return carry

    whole = count // unroll
    carry = steps(0, carry) if whole == 1 else lax.fori_loop(0, whole, steps, carry)
    for t in range(whole * unroll, count):
        carry = body(t, carry)
    return carry


def before(t, tiles):
    return (tiles if t == 0 else t - 1) if isinstance(t, int) else jnp.where(t == 0, tiles, t - 1)


def after(t, tiles):
    return (0 if t == tiles else t + 1) if isinstance(t, int) else t + 1


def lane_ids(rows):
    return lax.broadcasted_iota(jnp.int32, (rows, LANES), 1)


def row_ids(rows):
    return lax.broadcasted_iota(jnp.int32, (rows, LANES), 0)


def roll_up(x):
    return pltpu.roll(x, 1, 1)


def roll_down(x):
    return pltpu.roll(x, LANES - 1, 1)


def roll_rows(x, by):
    by %= x.shape[0]
    return x if by == 0 else pltpu.roll(x, by, 0)


def roll_lanes(x, by):
    by %= LANES
    return x if by == 0 else pltpu.roll(x, by, 1)


def col_prev(x):
    return pltpu.roll(x, 1, 0)


def col_next(x):
    return pltpu.roll(x, x.shape[0] - 1, 0)


def selector(shape, rule):
    a = lax.broadcasted_iota(jnp.int32, shape, 0)
    b = lax.broadcasted_iota(jnp.int32, shape, 1)
    return jnp.where(rule(a, b), 1.0, 0.0).astype(BF16)


def splitter():
    return selector((256, 256), lambda a, b: a == 2 * (b % LANES) + b // LANES)


def merger():
    return selector((256, 256), lambda a, b: b == 2 * (a % LANES) + a // LANES)


def virtual_splitter():
    return selector(
        (LANES, 256),
        lambda a, b: a // 2 + jnp.where(a >= 64, 64, 0) + LANES * (a % 2) == b,
    )


def moved(x, matrix, exact=None):
    rows = x.shape[0]
    high = x.astype(BF16)
    low = (x - high.astype(F32)).astype(BF16)
    terms = [high, low] if exact is None else [high, low, exact]
    out = jnp.dot(jnp.concatenate(terms, 0), matrix, preferred_element_type=F32)
    both = out[:rows] + out[rows : 2 * rows]
    return both if exact is None else (both, out[2 * rows :])


def quarters_of(parts, temp):
    count = parts.shape[0] // 2
    temp[0] = parts[:, :LANES]
    temp[1] = parts[:, LANES:]
    return [temp[pr, pl.ds(pc, count, 2), :] for pc in (0, 1) for pr in (0, 1)]


def reds(swapped):
    return (1, 2) if swapped else (0, 3)


def interleaved(group, offset):
    sub = row_ids(8)
    packed = roll_rows(group[0], offset)
    for q in range(1, 4):
        packed = jnp.where(sub // 2 == q, roll_rows(group[q], 2 * q + offset), packed)
    return packed


def edge_packs(source, diag, swapped):
    sub = row_ids(8)
    even, odd = reds(swapped)
    rows = source[0].shape[0]
    packs = []
    for here, first, second, row, step in (
        (slice(rows - 8, rows), even, odd, 6, 1),
        (slice(0, 8), odd, even, 1, -1),
    ):
        gs = [x[here] for x in source]
        gd = [x[here] for x in diag]
        near = gs[first] / gd[first]
        far = roll_rows(gs[second] / gd[second], step)
        gs[first] = jnp.where(sub == row, near, gs[first])
        gd[first] = jnp.where(sub == row, far, gd[first])
        offset = 2 if row == 6 else 0
        packs.append((interleaved(gs, offset), interleaved(gd, offset)))
    return packs


def unpacked_halo(left, right, swapped):
    sub = row_ids(8)
    even, odd = reds(swapped)
    (al, bl), (ar, br) = left, right
    source, diag = [], []
    for q in range(4):
        s = jnp.where(
            sub >= 6,
            roll_rows(al, 6 - 2 * q),
            jnp.where(sub <= 1, roll_rows(ar, -2 * q), 0.0),
        )
        d = jnp.where(
            sub >= 6,
            roll_rows(bl, 6 - 2 * q),
            jnp.where(sub <= 1, roll_rows(br, -2 * q), 4.0),
        )
        if q == even:
            s = jnp.where(sub == 2, roll_rows(br, 1 - 2 * odd), s)
            d = jnp.where((sub == 2) | (sub == 6), 1.0, d)
        if q == odd:
            s = jnp.where(sub == 5, roll_rows(bl, 5 - 2 * even), s)
            d = jnp.where((sub == 5) | (sub == 1), 1.0, d)
        source.append(s)
        diag.append(d)
    return source, diag


def is_odd():
    return lax.rem(lax.axis_index("lon"), 2) == 1


def chosen(odd, a, b):
    return jnp.where(odd, a, b), jnp.where(odd, b, a)


def store_edges(t, packs, odd, to_mate, to_other):
    right, left = packs
    for i in (0, 1):
        to_mate[i, t], to_other[i, t] = chosen(odd, left[i], right[i])


def fill_halo(t, from_mate, from_other, odd, swapped, hs, hd, hi):
    al, ar = chosen(odd, from_mate[0, t], from_other[0, t])
    bl, br = chosen(odd, from_mate[1, t], from_other[1, t])
    source, diag = unpacked_halo((al, bl), (ar, br), swapped)
    for q in range(4):
        hs[q, t] = source[q]
        hd[q, t] = diag[q]
        hi[q, t] = 1.0 / diag[q]


def loader(own, halo, virtual, tiles):
    def load(q, t):
        if isinstance(t, int) and t == tiles:
            return jnp.concatenate([virtual[q], halo[q, t]], 0)
        return jnp.concatenate([own[q, t], halo[q, t]], 0)

    return load


def polar_packs(tiles_of):
    lane = lane_ids(tiles_of[0][0].shape[0])
    packs = []
    for pc in (0, 1):
        parts = [*tiles_of[2 * pc], *tiles_of[2 * pc + 1]]
        packed = parts[0]
        for m in range(1, 4):
            mine = (lane + (16 - 32 * m) % LANES) % LANES < 32
            packed = jnp.where(mine, roll_lanes(parts[m], 32 * m), packed)
        packs.append(packed)
    return packs


def polar_unpacked(x, q):
    lane = lane_ids(x.shape[1])
    used = (lane < 16) | (lane >= LANES - 16)
    m = 2 * (q % 2)
    return (
        jnp.where(used, roll_lanes(x[q // 2], 32 * m), 0.0),
        jnp.where(used, roll_lanes(x[q // 2], 32 * (m + 1)), 4.0),
    )


def seam_scales(flags, chunks):
    flag_cols, flag_lats = flags.shape
    flags = jnp.concatenate(
        [flags.astype(F32), jnp.zeros((8 - flag_cols, flag_lats), F32)], 0
    )
    lat = lax.broadcasted_iota(jnp.int32, (8, flag_lats), 1)
    stacked = jnp.concatenate([jnp.where(lat // 8 == c, flags, 0.0) for c in chunks], 0)
    spread = selector((flag_lats, LANES), lambda a, b: a % 8 == b // (TILE // 2))
    spread_flags = jnp.dot(stacked.astype(BF16), spread, preferred_element_type=F32)
    scale = jnp.where(spread_flags > 0.5, SEAM_SCALE, 1.0)
    return scale.reshape(len(chunks), 8, LANES)


def seam_rows(scales, flag_cols, rows):
    size = (rows // flag_cols, LANES)
    return jnp.concatenate(
        [jnp.broadcast_to(scales[i : i + 1], size) for i in range(flag_cols)], 0
    )


def edge_kernel(
    right_ref, weight_ref, flag_ref,
    to_mate, to_other, corner_ref,
    edge_s, edge_w, flags, temp_s, temp_w, scale_ref, sems,
):
    columns, height = right_ref.shape
    tiles = height // 256
    pairs = [(flag_ref, flags)]
    for i, (src, dst, size) in enumerate(
        ((right_ref, edge_s, 8), (weight_ref, edge_w, 16))
    ):
        pairs.append((src.at[pl.ds(0, size)], dst.at[pl.ds(0, size)]))
        pairs.append((src.at[pl.ds(columns - size, size)], dst.at[pl.ds(size, size)]))
    copies = [
        pltpu.make_async_copy(src, dst, sems.at[i]) for i, (src, dst) in enumerate(pairs)
    ]
    for copy in copies:
        copy.start()
    odd = is_odd()
    matrix = splitter()
    flag_cols = flag_ref.shape[0]
    copies[0].wait()
    scale_ref[...] = seam_scales(flags[...], range(tiles))
    for copy in copies[1:]:
        copy.wait()
    sub = row_ids(8)
    lanes = [slice(c * 256, (c + 1) * 256) for c in range(tiles)]
    source, weight = moved(
        jnp.concatenate([edge_s[:, w] for w in lanes], 0),
        matrix,
        jnp.concatenate([edge_w[:, w] for w in lanes], 0),
    )
    weight = weight.reshape(tiles, 32, 256)
    weight = jnp.concatenate([weight[:, :8], weight[:, 24:]], 1).reshape(tiles * 16, 256)
    source = quarters_of(source, temp_s)
    weight = quarters_of(weight, temp_w)
    found = []
    for c in range(tiles):
        here = slice(c * 8, (c + 1) * 8)
        scales = scale_ref[c]
        scale = jnp.where(sub < 4, scales[:1], scales[flag_cols - 1 : flag_cols])
        pair = [x[here] for x in source], [4.0 + w[here] * scale for w in weight]
        store_edges(c, edge_packs(*pair, False), odd, to_mate, to_other)
        if c in (0, tiles - 1):
            found.append(pair)
    both = mirrored_ends(*found)
    for pc in (0, 1):
        corner = both[8 * pc : 8 * (pc + 1)]
        corner_ref[pc] = corner
        to_mate[pc, tiles] = corner


def mirrored_ends(first, last):
    mirror = selector((LANES, LANES), lambda a, b: a + b == LANES - 1)
    lane = lane_ids(first[0][0].shape[0])
    ends = [
        [jnp.where(lane >= 64, last[i][q ^ 1], first[i][q ^ 1]) for i in (0, 1)]
        for q in range(4)
    ]
    return moved(jnp.concatenate(polar_packs(ends), 0), mirror)


def polar_kernel(right_ref, weight_ref, flag_ref, from_mate, polar_ref, temp_s, temp_w):
    columns, height = right_ref.shape
    rows, tiles = columns // 2, height // 256
    scales = seam_scales(flag_ref[...], (0, tiles - 1))
    lanes = slice(0, 256), slice(height - 256, height)
    source, weight = moved(
        jnp.concatenate([right_ref[:, w] for w in lanes], 0),
        splitter(),
        jnp.concatenate([weight_ref[:, w] for w in lanes], 0),
    )
    found = []
    for end in (0, 1):
        here = slice(end * columns, (end + 1) * columns)
        scale = seam_rows(scales[end], flag_ref.shape[0], rows)
        found.append(
            (
                quarters_of(source[here], temp_s.at[end]),
                [4.0 + w * scale for w in quarters_of(weight[here], temp_w.at[end])],
            )
        )
    both = mirrored_ends(*found)
    for pc in (0, 1):
        polar_ref[pc, :rows] = both[pc * rows : (pc + 1) * rows]
        polar_ref[pc, rows:] = from_mate[pc, tiles]


def bulk_kernel(
    right_ref, weight_ref, flag_ref, polar_first,
    s_ref, d_ref, i_ref, d1_ref, i1_ref, d2_ref,
    temp_s, temp_d, scale_ref, e_ref,
):
    tiles, rows = s_ref.shape[1], s_ref.shape[2]
    columns = 2 * rows
    matrix = splitter()
    scale_ref[...] = seam_scales(flag_ref[...], range(tiles))
    for start in range(0, tiles, BATCH):
        lanes = [slice((start + i) * 256, (start + i + 1) * 256) for i in range(BATCH)]
        source, weight = moved(
            jnp.concatenate([right_ref[:, w] for w in lanes], 0),
            matrix,
            jnp.concatenate([weight_ref[:, w] for w in lanes], 0),
        )
        for i in range(BATCH):
            c = start + i
            here = slice(i * columns, (i + 1) * columns)
            scale = seam_rows(scale_ref[c], flag_ref.shape[0], rows)
            for q, value in enumerate(quarters_of(source[here], temp_s.at[i])):
                s_ref[q, c] = value
            screen = [w * scale for w in quarters_of(weight[here], temp_d.at[i])]
            e_ref[c] = (screen[0] + screen[1]) + (screen[2] + screen[3])
            for q in range(4):
                diag = 4.0 + screen[q]
                d_ref[q, c] = diag
                i_ref[q, c] = 1.0 / diag

    def use(c, screen):
        for q in range(4):
            d1_ref[q, c] = 4.0 + screen[q]
            i1_ref[q, c] = 1.0 / (4.0 + screen[q])
        d2_ref[c] = 4.0 + ((screen[0] + screen[1]) + (screen[2] + screen[3]))

    split_tiles(lambda t: e_ref[t], tiles // 2, rows, matrix, temp_s, use)


def split_tiles(load, tiles, rows, matrix, temp, use):
    for start in range(0, tiles, BATCH):
        wide = [
            jnp.concatenate([load(2 * c), load(2 * c + 1)], 1)
            for c in range(start, start + BATCH)
        ]
        out = moved(jnp.concatenate(wide, 0), matrix)
        for i in range(BATCH):
            use(start + i, quarters_of(out[i * rows : (i + 1) * rows], temp.at[i, :, :rows]))


def half_sweep(v, load_s, load_i, tiles, red, unroll):
    rows = v[0].shape[1]
    lane = lane_ids(rows)
    y, z, qa, qb = (1, 2, 0, 3) if red else (3, 0, 2, 1)
    col_a, col_b = (col_prev, col_next) if red else (col_next, col_prev)

    def beside_virtual(q):
        ns, we = q ^ 1, q ^ 2
        here = v[ns][tiles]
        if q % 2 == 0:
            lat = jnp.where(lane == 0, roll_up(v[ns][tiles - 1]), roll_up(here))
        else:
            lat = jnp.where(lane == LANES - 1, roll_down(v[ns][0]), roll_down(here))
        cols = v[we][tiles]
        return (here + lat) + (cols + (col_prev if q < 2 else col_next)(cols))

    held = [
        (q, (load_s(q, tiles) + beside_virtual(q)) * load_i(q, tiles)) for q in (y, z)
    ]

    def body(t, carry):
        y_before, z_here = carry
        vy, vz = v[y][t], v[z][t]
        y_here = roll_up(vy)
        z_after = roll_down(v[z][t + 1])
        lat_a = vy + jnp.where(lane == 0, y_before, y_here)
        lat_b = vz + jnp.where(lane == LANES - 1, z_after, z_here)
        v[qa][t] = (load_s(qa, t) + (lat_a + (vz + col_a(vz)))) * load_i(qa, t)
        v[qb][t] = (load_s(qb, t) + (lat_b + (vy + col_b(vy)))) * load_i(qb, t)
        return y_here, z_after

    loop(tiles, body, (roll_up(v[y][tiles]), roll_down(v[z][0])), unroll)
    for q, value in held:
        v[q][tiles] = value


def smooth(v, load_s, load_i, tiles, unroll):
    zeros = jnp.zeros(v[0].shape[1:], F32)

    def first(t, _):
        for q in (0, 3):
            v[q][t] = load_s(q, t) * load_i(q, t)
        return 0

    loop(tiles, first, 0, unroll)
    for q in (1, 2):
        v[q][0] = zeros
        v[q][tiles - 1] = zeros
        v[q][tiles] = load_s(q, tiles) * load_i(q, tiles)
        v[3 * (q - 1)][tiles] = zeros
    half_sweep(v, load_s, load_i, tiles, False, unroll)
    half_sweep(v, load_s, load_i, tiles, True, unroll)
    half_sweep(v, load_s, load_i, tiles, False, unroll)


def residuals(v, load_s, load_d, tiles, c0, c1, keep, unroll):
    lane = lane_ids(v[0].shape[1])

    def body(t, carry):
        up1, up3, down0, down2 = carry
        x = [v[q][t] for q in range(4)]
        here1, here3 = roll_up(x[1]), roll_up(x[3])
        next0, next2 = (roll_down(v[q][after(t, tiles)]) for q in (0, 2))
        beside = [
            (x[1] + jnp.where(lane == 0, up1, here1)) + (x[2] + col_prev(x[2])),
            (x[0] + jnp.where(lane == LANES - 1, next0, down0)) + (x[3] + col_prev(x[3])),
            (x[3] + jnp.where(lane == 0, up3, here3)) + (x[0] + col_next(x[0])),
            (x[2] + jnp.where(lane == LANES - 1, next2, down2)) + (x[1] + col_next(x[1])),
        ]
        r = [load_s(q, t) - (load_d(q, t) * x[q] - beside[q]) for q in range(4)]
        keep(t, r)
        c0[t] = (col_prev(r[2]) + col_next(r[0])) + 3.0 * (r[0] + r[2])
        c1[t] = (col_prev(r[3]) + col_next(r[1])) + 3.0 * (r[1] + r[3])
        return here1, here3, next0, next2

    start = (
        roll_up(v[1][tiles]), roll_up(v[3][tiles]), roll_down(v[0][0]), roll_down(v[2][0])
    )
    body(tiles, loop(tiles, body, start, unroll))


def restrict(c0, c1, tiles, rows, use, unroll):
    lane = lane_ids(rows)

    def body(t, carry):
        up, down = carry
        here, other = c0[t, :rows], c1[t, :rows]
        up_here = roll_up(other)
        down_next = roll_down(c0[after(t, tiles), :rows])
        north = jnp.where(lane == 0, up, up_here)
        south = jnp.where(lane == LANES - 1, down_next, down)
        use(t, ((north + south) + 3.0 * (here + other)) * (1.0 / 16.0))
        return up_here, down_next

    start = roll_up(c1[tiles, :rows]), roll_down(c0[0, :rows])
    body(tiles, loop(tiles, body, start, unroll))


def ends_of(x, rows):
    return x[rows - 8 : rows], x[:8]


def virtual_tiles(polar_ref, ps, pd, pi):
    total = -16.0
    for q in range(4):
        source, diag = polar_unpacked(polar_ref.at[:, : ps.shape[1]], q)
        total = total + diag
        ps[q] = source
        pd[q] = diag
        pi[q] = 1.0 / diag
    return total


def rim_kernel(
    s_ref, d_ref, i_ref, d1_ref, from_other, from_mate, polar_ref, corner_far,
    r_ref, n_ref, to_mate, to_other,
    v0, v1, v2, v3, c0, c1, hs, hd, hi, ps, pd, pi, temp,
):
    v = [v0, v1, v2, v3]
    tiles, rows = s_ref.shape[1], s_ref.shape[2]
    sub = row_ids(8)
    odd = is_odd()

    def halo(t, _):
        fill_halo(t, from_mate, from_other, odd, False, hs, hd, hi)
        return 0

    loop(tiles, halo, 0, 8)
    total = virtual_tiles(polar_ref, ps, pd, pi)
    for q in range(4):
        near_s, near_d = polar_unpacked(polar_ref.at[:, rows:], q)
        far_s, far_d = polar_unpacked(corner_far, q)
        left_s, right_s = chosen(odd, near_s, far_s)
        left_d, right_d = chosen(odd, near_d, far_d)
        source = jnp.where(sub >= 5, left_s, jnp.where(sub <= 2, right_s, 0.0))
        diag = jnp.where(sub >= 5, left_d, jnp.where(sub <= 2, right_d, 4.0))
        hs[q, tiles] = source
        hd[q, tiles] = diag
        hi[q, tiles] = 1.0 / diag

    def rim(own, halo, virtual):
        def load(q, t):
            if isinstance(t, int) and t == tiles:
                last, first = virtual[q, rows - 8 :], virtual[q, :8]
            else:
                last, first = own[q, t, rows - 8 :], own[q, t, :8]
            return jnp.concatenate([last, halo[q, t], first], 0)

        return load

    load_s = rim(s_ref, hs, ps)
    smooth(v, load_s, rim(i_ref, hi, pi), tiles, 32)

    def keep(t, r):
        if not (isinstance(t, int) and t == tiles):
            for q in range(4):
                r_ref[q, t] = jnp.concatenate([r[q][16:], r[q][:8]], 0)

    residuals(v, load_s, rim(d_ref, hd, pd), tiles, c0, c1, keep, 16)

    def coarse(t, value):
        n_ref[t] = jnp.concatenate([value[16:], value[:8]], 0)

    restrict(c0, c1, tiles, 24, coarse, 16)

    rows1 = rows // 2

    def use(c, source):
        diag = [
            jnp.where(sub < 4, d1_ref[q, c, :8], d1_ref[q, c, rows1 - 8 :]) for q in range(4)
        ]
        store_edges(c, edge_packs(source, diag, False), odd, to_mate, to_other)

    tiles1 = tiles // 2
    split_tiles(lambda t: n_ref[t], tiles1, 16, splitter(), temp, use)
    out = moved(
        jnp.concatenate([n_ref[tiles], total[:8], total[rows - 8 :]], 0), virtual_splitter()
    )
    source = quarters_of(out[:16], temp.at[0])
    diag = [4.0 + x for x in quarters_of(out[16:], temp.at[1])]
    store_edges(tiles1, edge_packs(source, diag, True), odd, to_mate, to_other)


def core_kernel(
    s_ref, d_ref, i_ref, polar_ref, rim_r, rim_n,
    r_ref, s1_ref, d1_virtual, d2_virtual,
    v0, v1, v2, v3, c0, c1, ps, pd, pi, n1, temp,
):
    v = [v0, v1, v2, v3]
    tiles, rows = s_ref.shape[1], s_ref.shape[2]
    sub = row_ids(8)
    total = virtual_tiles(polar_ref, ps, pd, pi)

    def core(own, virtual):
        def load(q, t):
            return virtual[q] if isinstance(t, int) and t == tiles else own[q, t]

        return load

    def stitched(first, value, last):
        return jnp.concatenate(
            [
                jnp.where(sub < 3, first, value[:8]),
                value[8 : rows - 8],
                jnp.where(sub > 4, last, value[rows - 8 :]),
            ],
            0,
        )

    load_s = core(s_ref, ps)
    smooth(v, load_s, core(i_ref, pi), tiles, 32)

    def keep(t, r):
        if not (isinstance(t, int) and t == tiles):
            for q in range(4):
                r_ref[q, t] = stitched(rim_r[q, t, :8], r[q], rim_r[q, t, 8:])

    residuals(v, load_s, core(d_ref, pd), tiles, c0, c1, keep, 16)

    def coarse(t, value):
        n1[t] = stitched(rim_n[t, :8], value, rim_n[t, 8:])

    restrict(c0, c1, tiles, rows, coarse, 16)

    def use(c, source):
        for q in range(4):
            s1_ref[q, c] = source[q]

    tiles1 = tiles // 2
    split_tiles(lambda t: n1[t], tiles1, rows, splitter(), temp, use)
    out = moved(jnp.concatenate([n1[tiles], total], 0), virtual_splitter())
    source = quarters_of(out[:rows], temp.at[0])
    screen = quarters_of(out[rows:], temp.at[1])
    for q in range(4):
        s1_ref[q, tiles1] = source[q]
        d1_virtual[q] = 4.0 + screen[q]
    d2_virtual[...] = 4.0 + ((screen[0] + screen[1]) + (screen[2] + screen[3]))


def merge_kernel(r_ref, out_ref, temp, out_buf, sems):
    tiles = r_ref.shape[1]
    rows = r_ref.shape[2]
    matrix = merger()
    chunk = out_ref.shape[1] // GROUPS
    copies = []
    for group in range(GROUPS):
        for batch in range(tiles // GROUPS // BATCH):
            start = group * (tiles // GROUPS) + batch * BATCH
            both = []
            for i in range(BATCH):
                for pr in (0, 1):
                    for pc in (0, 1):
                        temp[i, pr, pl.ds(pc, rows, 2), :] = r_ref[2 * pc + pr, start + i]
                both.append(jnp.concatenate([temp[i, 0], temp[i, 1]], 1))
            out = moved(jnp.concatenate(both, 0), matrix)
            for i in range(BATCH):
                where = slice((start + i) * 256, (start + i + 1) * 256)
                out_buf[:, where] = out[2 * rows * i : 2 * rows * (i + 1)]
        part = pl.ds(group * chunk, chunk)
        copy = pltpu.make_async_copy(out_buf.at[:, part], out_ref.at[:, part], sems.at[group])
        copy.start()
        copies.append(copy)
    for copy in copies:
        copy.wait()


def middle_kernel(
    s_ref, d_ref, i_ref, d_virtual, d2_ref, d2_virtual, from_other, from_mate,
    s2_ref, to_mate, to_other,
    v0, v1, v2, v3, c0, c1, hs, hd, hi, pi,
):
    v = [v0, v1, v2, v3]
    tiles, rows = d_ref.shape[1], d_ref.shape[2]
    odd = is_odd()
    for t in range(tiles + 1):
        fill_halo(t, from_mate, from_other, odd, t == tiles, hs, hd, hi)
    for q in range(4):
        pi[q] = 1.0 / d_virtual[q]

    def load_s(q, t):
        return jnp.concatenate([s_ref[q, t], hs[q, t]], 0)

    smooth(v, load_s, loader(i_ref, hi, pi, tiles), tiles, 16)
    residuals(
        v, load_s, loader(d_ref, hd, d_virtual, tiles), tiles, c0, c1, lambda t, r: None, 16
    )
    sub = row_ids(8)

    def coarse(t, value):
        diag = d2_virtual[...] if t == tiles else d2_ref[t]
        s2_ref[t] = value
        right = jnp.where(sub < 4, roll_rows(value[rows - 8 :], 4), diag[rows - 8 :])
        left = jnp.where(sub < 4, value[:8], roll_rows(diag[:8], 4))
        to_mate[t], to_other[t] = chosen(odd, left, right)

    restrict(c0, c1, tiles, rows, coarse, 16)


def last_kernel(
    s_ref, d_ref, d_virtual, from_other, from_mate,
    solution_ref, residual_ref,
    s, d, inv, va, vb,
):
    tiles, own = d_ref.shape[0], d_ref.shape[1]
    rows = own + 8
    sub = row_ids(8)
    lane, row = lane_ids(rows), row_ids(rows)
    even = (lane + row) % 2 == 0
    odd = jnp.logical_not(even)
    odd_band = is_odd()
    for t in range(tiles + 1):
        left, right = chosen(odd_band, from_mate[t], from_other[t])
        diag = d_virtual[...] if t == tiles else d_ref[t]
        source = jnp.concatenate(
            [s_ref[t], jnp.where(sub < 4, right, roll_rows(left, 4))], 0
        )
        diag = jnp.concatenate([diag, jnp.where(sub < 4, roll_rows(right, 4), left)], 0)
        inverse = 1.0 / diag
        s[t] = source
        d[t] = diag
        inv[t] = inverse
        va[t] = jnp.where(odd if t == tiles else even, source * inverse, 0.0)

    def scan(v, use):
        up, down = roll_up(v[tiles]), roll_down(v[0])
        for t in range(tiles + 1):
            x = v[t]
            up_here, down_next = roll_up(x), roll_down(v[after(t, tiles)])
            north = jnp.where(lane == 0, up, up_here)
            south = jnp.where(lane == LANES - 1, down_next, down)
            use(t, x, (col_prev(x) + col_next(x)) + (north + south))
            up, down = up_here, down_next

    for old, new, mask, other in ((va, vb, odd, even), (vb, va, even, odd), (va, vb, odd, even)):

        def relax(t, x, beside):
            update = other if t == tiles else mask
            new[t] = jnp.where(update, (s[t] + beside) * inv[t], x)

        scan(old, relax)

    def finish(t, x, beside):
        if t < tiles:
            where = slice(t * LANES, (t + 1) * LANES)
            solution_ref[:, where] = x[:own]
            residual_ref[:, where] = (s[t] - (d[t] * x - beside))[:own]

    scan(vb, finish)


VMEM = pl.BlockSpec(memory_space=pltpu.VMEM)
HBM = pl.BlockSpec(memory_space=pltpu.HBM)


def call(kernel, out_shapes, scratch, *args, sems=None, far_in=0, far_out=0):
    scratch = [pltpu.VMEM(x, F32) if isinstance(x, tuple) else x for x in scratch]
    if sems is not None:
        scratch.append(pltpu.SemaphoreType.DMA(sems))
    return pl.pallas_call(
        kernel,
        out_shape=[jax.ShapeDtypeStruct(shape, F32) for shape in out_shapes],
        in_specs=[HBM] * far_in + [VMEM] * (len(args) - far_in),
        out_specs=[HBM] * far_out + [VMEM] * (len(out_shapes) - far_out),
        scratch_shapes=scratch,
        compiler_params=pltpu.CompilerParams(vmem_limit_bytes=40 * 2**20),
    )(*args)


def swapped_with(x, by):
    count = lax.axis_size("lon")
    pairs = [(i, (i + by) % count) for i in range(0, count, 2)]
    return lax.ppermute(x, "lon", pairs + [(b, a) for a, b in pairs])


def swapped_edges(to_mate, to_other):
    from_mate = swapped_with(to_mate, 1)
    return from_mate, swapped_with(to_other, -1)


def body(right_side, texel_weight, seam_flags):
    columns, height = right_side.shape
    half_turn = lax.axis_size("lon") // 2
    tiles, rows = height // 256, columns // 2
    tiles1, rows1 = tiles // 2, rows // 2
    temp = (BATCH, 2, columns, LANES)
    quarters = (4, tiles, rows, LANES)
    quarters1 = (4, tiles1, rows1, LANES)
    split = (2, 16 * tiles, LANES)
    to_mate, to_other, corner = call(
        edge_kernel,
        [(2, tiles + 1, 8, LANES), (2, tiles, 8, LANES), (2, 8, LANES)],
        [(16, height), pltpu.VMEM((32, height), BF16)]
        + [pltpu.VMEM(seam_flags.shape, jnp.int32), split, split, (tiles, 8, LANES)],
        *[
            pltpu.with_memory_space_constraint(x, pltpu.HBM)
            for x in (right_side, texel_weight, seam_flags)
        ],
        sems=(5,), far_in=3,
    )
    from_mate, from_other = swapped_edges(to_mate, to_other)
    corner_far = swapped_with(corner, half_turn - 1)
    ends = (2, 2, columns, LANES)
    (polar_own,) = call(
        polar_kernel, [(2, rows + 8, LANES)], [ends, ends],
        right_side, texel_weight, seam_flags, from_mate,
    )
    polar = lax.ppermute(
        polar_own, "lon", [(i, (i + half_turn) % (2 * half_turn)) for i in range(2 * half_turn)]
    )
    s, d, inverse, d1, i1, d2 = call(
        bulk_kernel,
        [quarters] * 3 + [quarters1, quarters1, quarters1[1:]],
        [temp, temp, (tiles, 8, LANES), quarters[1:]],
        right_side, texel_weight, seam_flags, polar_own,
    )

    def level_scratch(tiles, rows):
        return [(tiles + 1, rows, LANES)] * 6

    def halo_scratch(tiles):
        return [(4, tiles + 1, 8, LANES)] * 3

    pack1 = (2, tiles1 + 1, 8, LANES)
    virtual = [(4, rows, LANES)] * 3
    rim_r, rim_n, to_mate, to_other = call(
        rim_kernel,
        [(4, tiles, 16, LANES), (tiles + 1, 16, LANES), pack1, pack1],
        level_scratch(tiles, 24) + halo_scratch(tiles) + virtual + [(BATCH, 2, 16, LANES)],
        s, d, inverse, d1, from_other, from_mate, polar, corner_far,
    )
    from_mate, from_other = swapped_edges(to_mate, to_other)
    r, s1, d1_virtual, d2_virtual = call(
        core_kernel,
        [quarters, (4, tiles1 + 1, rows1, LANES), (4, rows1, LANES), (rows1, LANES)],
        level_scratch(tiles, rows)
        + virtual
        + [(tiles + 1, rows, LANES), (BATCH, 2, rows, LANES)],
        s, d, inverse, polar, rim_r, rim_n,
    )
    (fine_residual,) = call(
        merge_kernel, [(columns, height)], [temp, (columns, height)], r,
        sems=(GROUPS,), far_out=1,
    )
    pack2 = (tiles1 + 1, 8, LANES)
    s2, to_mate, to_other = call(
        middle_kernel,
        [(tiles1 + 1, rows1, LANES), pack2, pack2],
        level_scratch(tiles1, rows1 + 8) + halo_scratch(tiles1) + [(4, rows1, LANES)],
        s1, d1, i1, d1_virtual, d2, d2_virtual, from_other, from_mate,
    )
    from_mate, from_other = swapped_edges(to_mate, to_other)
    solution_2, residual_2 = call(
        last_kernel,
        [(columns // 4, height // 4)] * 2,
        [(tiles1 + 1, rows1 + 8, LANES)] * 5,
        s2, d2, d2_virtual, from_other, from_mate,
    )
    return fine_residual, solution_2, residual_2


def solution(mesh):
    spec = P(("groups", "lon"), None)
    return jax.shard_map(
        body, mesh=mesh, in_specs=(spec,) * 3, out_specs=(spec,) * 3, check_vma=False
    )
```

```python
import jax
import jax.numpy as jnp
from jax import lax
from jax.experimental import pallas as pl
from jax.experimental.pallas import tpu as pltpu
from jax.sharding import PartitionSpec as P

TILE = 32
SEAM_SCALE = 0.1
LANES = 128
GROUPS = 4
BATCH = 4
F32 = jnp.float32
BF16 = jnp.bfloat16


def loop(count, body, carry=0, unroll=4):
    unroll = min(unroll, count)

    def steps(block, carry):
        for i in range(unroll):
            carry = body(block * unroll + i, carry)
        return carry

    whole = count // unroll
    carry = steps(0, carry) if whole == 1 else lax.fori_loop(0, whole, steps, carry)
    for t in range(whole * unroll, count):
        carry = body(t, carry)
    return carry


def before(t, tiles):
    return (tiles if t == 0 else t - 1) if isinstance(t, int) else jnp.where(t == 0, tiles, t - 1)


def after(t, tiles):
    return (0 if t == tiles else t + 1) if isinstance(t, int) else t + 1


def lane_ids(rows):
    return lax.broadcasted_iota(jnp.int32, (rows, LANES), 1)


def row_ids(rows):
    return lax.broadcasted_iota(jnp.int32, (rows, LANES), 0)


def roll_up(x):
    return pltpu.roll(x, 1, 1)


def roll_down(x):
    return pltpu.roll(x, LANES - 1, 1)


def roll_rows(x, by):
    by %= x.shape[0]
    return x if by == 0 else pltpu.roll(x, by, 0)


def roll_lanes(x, by):
    by %= LANES
    return x if by == 0 else pltpu.roll(x, by, 1)


def col_prev(x):
    return pltpu.roll(x, 1, 0)


def col_next(x):
    return pltpu.roll(x, x.shape[0] - 1, 0)


def selector(shape, rule):
    a = lax.broadcasted_iota(jnp.int32, shape, 0)
    b = lax.broadcasted_iota(jnp.int32, shape, 1)
    return jnp.where(rule(a, b), 1.0, 0.0).astype(BF16)


def splitter():
    return selector((256, 256), lambda a, b: a == 2 * (b % LANES) + b // LANES)


def merger():
    return selector((256, 256), lambda a, b: b == 2 * (a % LANES) + a // LANES)


def virtual_splitter():
    return selector(
        (LANES, 256),
        lambda a, b: a // 2 + jnp.where(a >= 64, 64, 0) + LANES * (a % 2) == b,
    )


def moved(x, matrix, exact=None):
    rows = x.shape[0]
    high = x.astype(BF16)
    low = (x - high.astype(F32)).astype(BF16)
    terms = [high, low] if exact is None else [high, low, exact]
    out = jnp.dot(jnp.concatenate(terms, 0), matrix, preferred_element_type=F32)
    both = out[:rows] + out[rows : 2 * rows]
    return both if exact is None else (both, out[2 * rows :])


def quarters_of(parts, temp):
    count = parts.shape[0] // 2
    temp[0] = parts[:, :LANES]
    temp[1] = parts[:, LANES:]
    return [temp[pr, pl.ds(pc, count, 2), :] for pc in (0, 1) for pr in (0, 1)]


def reds(swapped):
    return (1, 2) if swapped else (0, 3)


def interleaved(group, offset):
    sub = row_ids(8)
    packed = roll_rows(group[0], offset)
    for q in range(1, 4):
        packed = jnp.where(sub // 2 == q, roll_rows(group[q], 2 * q + offset), packed)
    return packed


def edge_packs(source, diag, swapped):
    sub = row_ids(8)
    even, odd = reds(swapped)
    rows = source[0].shape[0]
    packs = []
    for here, first, second, row, step in (
        (slice(rows - 8, rows), even, odd, 6, 1),
        (slice(0, 8), odd, even, 1, -1),
    ):
        gs = [x[here] for x in source]
        gd = [x[here] for x in diag]
        near = gs[first] / gd[first]
        far = roll_rows(gs[second] / gd[second], step)
        gs[first] = jnp.where(sub == row, near, gs[first])
        gd[first] = jnp.where(sub == row, far, gd[first])
        offset = 2 if row == 6 else 0
        packs.append((interleaved(gs, offset), interleaved(gd, offset)))
    return packs


def unpacked_halo(left, right, swapped):
    sub = row_ids(8)
    even, odd = reds(swapped)
    (al, bl), (ar, br) = left, right
    source, diag = [], []
    for q in range(4):
        s = jnp.where(
            sub >= 6,
            roll_rows(al, 6 - 2 * q),
            jnp.where(sub <= 1, roll_rows(ar, -2 * q), 0.0),
        )
        d = jnp.where(
            sub >= 6,
            roll_rows(bl, 6 - 2 * q),
            jnp.where(sub <= 1, roll_rows(br, -2 * q), 4.0),
        )
        if q == even:
            s = jnp.where(sub == 2, roll_rows(br, 1 - 2 * odd), s)
            d = jnp.where((sub == 2) | (sub == 6), 1.0, d)
        if q == odd:
            s = jnp.where(sub == 5, roll_rows(bl, 5 - 2 * even), s)
            d = jnp.where((sub == 5) | (sub == 1), 1.0, d)
        source.append(s)
        diag.append(d)
    return source, diag


def is_odd():
    return lax.rem(lax.axis_index("lon"), 2) == 1


def chosen(odd, a, b):
    return jnp.where(odd, a, b), jnp.where(odd, b, a)


def store_edges(t, packs, odd, to_mate, to_other):
    right, left = packs
    for i in (0, 1):
        to_mate[i, t], to_other[i, t] = chosen(odd, left[i], right[i])


def wide_packs(source, diag, partial, diag2, swapped):
    sub = row_ids(8)
    even, odd = reds(swapped)
    rows = source[0].shape[0]
    packs = []
    for here, far, near, row, step in (
        (slice(rows - 8, rows), even, odd, 4, -1),
        (slice(0, 8), odd, even, 3, 1),
    ):
        gs = [x[here] for x in source]
        gd = [x[here] for x in diag]
        part = partial[here]
        at = sub == row
        for q in (far, near):
            gs[q] = jnp.where(at, gs[q] / gd[q], gs[q])
        gd[far] = jnp.where(at, part / diag2[here], gd[far])
        gs[far ^ 1] = jnp.where(at, roll_rows(part, step), gs[far ^ 1])
        gd[far ^ 1] = jnp.where(at, roll_rows(part, 2 * step), gd[far ^ 1])
        shift = 4 if row == 4 else 0
        packs.append(
            [
                jnp.where(sub < 4, roll_rows(g[q], shift), roll_rows(g[q + 1], 4 - shift))
                for g in (gs, gd)
                for q in (0, 2)
            ]
        )
    return packs


def wide_unpacked(left, right, swapped):
    sub = row_ids(8)
    even, odd = reds(swapped)
    groups = []
    for k in (0, 2):
        group = []
        for l, r in zip(left[k : k + 2], right[k : k + 2]):
            group.append(jnp.where(sub < 4, r, roll_rows(l, 4)))
            group.append(jnp.where(sub < 4, roll_rows(r, 4), l))
        groups.append(group)
    source, diag = groups
    partial = jnp.zeros_like(sub, F32)
    for far, near, row, step in ((even, odd, 4, 1), (odd, even, 3, -1)):
        at = sub == row
        for i, part in enumerate((diag[far], source[far ^ 1], diag[far ^ 1])):
            partial = jnp.where(sub == row + i * step, roll_rows(part, i * step), partial)
        source[far ^ 1] = jnp.where(at, 0.0, source[far ^ 1])
        diag[far ^ 1] = jnp.where(at, 4.0, diag[far ^ 1])
        for q in (far, near):
            diag[q] = jnp.where(at, 1.0, diag[q])
    return source, diag, partial


def fill_halo(t, from_mate, from_other, odd, swapped, hs, hd, hi):
    al, ar = chosen(odd, from_mate[0, t], from_other[0, t])
    bl, br = chosen(odd, from_mate[1, t], from_other[1, t])
    source, diag = unpacked_halo((al, bl), (ar, br), swapped)
    for q in range(4):
        hs[q, t] = source[q]
        hd[q, t] = diag[q]
        hi[q, t] = 1.0 / diag[q]


def loader(own, halo, virtual, tiles):
    def load(q, t):
        if isinstance(t, int) and t == tiles:
            return jnp.concatenate([virtual[q], halo[q, t]], 0)
        return jnp.concatenate([own[q, t], halo[q, t]], 0)

    return load


def polar_packs(tiles_of):
    lane = lane_ids(tiles_of[0][0].shape[0])
    packs = []
    for pc in (0, 1):
        parts = [*tiles_of[2 * pc], *tiles_of[2 * pc + 1]]
        packed = parts[0]
        for m in range(1, 4):
            mine = (lane + (16 - 32 * m) % LANES) % LANES < 32
            packed = jnp.where(mine, roll_lanes(parts[m], 32 * m), packed)
        packs.append(packed)
    return packs


def polar_unpacked(x, q):
    lane = lane_ids(x.shape[1])
    used = (lane < 16) | (lane >= LANES - 16)
    m = 2 * (q % 2)
    return (
        jnp.where(used, roll_lanes(x[q // 2], 32 * m), 0.0),
        jnp.where(used, roll_lanes(x[q // 2], 32 * (m + 1)), 4.0),
    )


def seam_scales(flags, chunks):
    flag_cols, flag_lats = flags.shape
    flags = jnp.concatenate(
        [flags.astype(F32), jnp.zeros((8 - flag_cols, flag_lats), F32)], 0
    )
    lat = lax.broadcasted_iota(jnp.int32, (8, flag_lats), 1)
    stacked = jnp.concatenate([jnp.where(lat // 8 == c, flags, 0.0) for c in chunks], 0)
    spread = selector((flag_lats, LANES), lambda a, b: a % 8 == b // (TILE // 2))
    spread_flags = jnp.dot(stacked.astype(BF16), spread, preferred_element_type=F32)
    scale = jnp.where(spread_flags > 0.5, SEAM_SCALE, 1.0)
    return scale.reshape(len(chunks), 8, LANES)


def seam_rows(scales, flag_cols, rows):
    size = (rows // flag_cols, LANES)
    return jnp.concatenate(
        [jnp.broadcast_to(scales[i : i + 1], size) for i in range(flag_cols)], 0
    )


def edge_kernel(
    right_ref, weight_ref, flag_ref,
    to_mate, to_other, polar_ref, corner_near, corner_far,
    edge_s, edge_w, end_s, end_w, flags, temp_s, temp_w, temp_p, temp_q, scale_ref, sems,
):
    columns, height = right_ref.shape
    rows, tiles = columns // 2, height // 256
    pairs = [(flag_ref, flags)]
    for i, (src, dst, size) in enumerate(
        ((right_ref, edge_s, 8), (weight_ref, edge_w, 16))
    ):
        pairs.append((src.at[pl.ds(0, size)], dst.at[pl.ds(0, size)]))
        pairs.append((src.at[pl.ds(columns - size, size)], dst.at[pl.ds(size, size)]))
    for src, dst in ((right_ref, end_s), (weight_ref, end_w)):
        for end, start in enumerate((0, height - 256)):
            pairs.append((src.at[:, pl.ds(start, 256)], dst.at[end]))
    copies = [
        pltpu.make_async_copy(src, dst, sems.at[i]) for i, (src, dst) in enumerate(pairs)
    ]
    for copy in copies:
        copy.start()
    odd = is_odd()
    matrix = splitter()
    flag_cols = flag_ref.shape[0]
    copies[0].wait()
    scale_ref[...] = seam_scales(flags[...], range(tiles))
    for copy in copies[1:5]:
        copy.wait()
    sub = row_ids(8)
    lanes = [slice(c * 256, (c + 1) * 256) for c in range(tiles)]
    source, weight = moved(
        jnp.concatenate([edge_s[:, w] for w in lanes], 0),
        matrix,
        jnp.concatenate([edge_w[:, w] for w in lanes], 0),
    )
    weight = weight.reshape(tiles, 32, 256)
    weight = jnp.concatenate([weight[:, :8], weight[:, 24:]], 1).reshape(tiles * 16, 256)
    source = quarters_of(source, temp_s)
    weight = quarters_of(weight, temp_w)
    for c in range(tiles):
        here = slice(c * 8, (c + 1) * 8)
        scales = scale_ref[c]
        scale = jnp.where(sub < 4, scales[:1], scales[flag_cols - 1 : flag_cols])
        diag = [4.0 + w[here] * scale for w in weight]
        store_edges(
            c, edge_packs([x[here] for x in source], diag, False), odd, to_mate, to_other
        )

    for copy in copies[5:]:
        copy.wait()
    mirror = selector((LANES, LANES), lambda a, b: a + b == LANES - 1)
    lane = lane_ids(rows)
    source, weight = moved(
        jnp.concatenate([end_s[0], end_s[1]], 0),
        matrix,
        jnp.concatenate([end_w[0], end_w[1]], 0),
    )
    found = []
    for end, c in enumerate((0, tiles - 1)):
        here = slice(end * columns, (end + 1) * columns)
        scale = seam_rows(scale_ref[c], flag_cols, rows)
        found.append(
            (
                quarters_of(source[here], temp_p.at[end]),
                [4.0 + w * scale for w in quarters_of(weight[here], temp_q.at[end])],
            )
        )
    ends = [
        [jnp.where(lane >= 64, found[1][i][q ^ 1], found[0][i][q ^ 1]) for i in (0, 1)]
        for q in range(4)
    ]
    both = moved(jnp.concatenate(polar_packs(ends), 0), mirror)
    for pc in (0, 1):
        pack = both[pc * rows : (pc + 1) * rows]
        polar_ref[pc] = pack
        corner_near[pc], corner_far[pc] = chosen(odd, pack[:8], pack[rows - 8 :])


def bulk_kernel(
    right_ref, weight_ref, flag_ref, edges_first,
    s_ref, d_ref, i_ref, d1_ref, i1_ref, d2_ref,
    temp_s, temp_d, scale_ref, e_ref,
):
    tiles, rows = s_ref.shape[1], s_ref.shape[2]
    columns = 2 * rows
    matrix = splitter()
    scale_ref[...] = seam_scales(flag_ref[...], range(tiles))
    for start in range(0, tiles, BATCH):
        lanes = [slice((start + i) * 256, (start + i + 1) * 256) for i in range(BATCH)]
        source, weight = moved(
            jnp.concatenate([right_ref[:, w] for w in lanes], 0),
            matrix,
            jnp.concatenate([weight_ref[:, w] for w in lanes], 0),
        )
        for i in range(BATCH):
            c = start + i
            here = slice(i * columns, (i + 1) * columns)
            scale = seam_rows(scale_ref[c], flag_ref.shape[0], rows)
            for q, value in enumerate(quarters_of(source[here], temp_s.at[i])):
                s_ref[q, c] = value
            screen = [w * scale for w in quarters_of(weight[here], temp_d.at[i])]
            e_ref[c] = (screen[0] + screen[1]) + (screen[2] + screen[3])
            for q in range(4):
                diag = 4.0 + screen[q]
                d_ref[q, c] = diag
                i_ref[q, c] = 1.0 / diag

    def use(c, screen):
        for q in range(4):
            d1_ref[q, c] = 4.0 + screen[q]
            i1_ref[q, c] = 1.0 / (4.0 + screen[q])
        d2_ref[c] = 4.0 + ((screen[0] + screen[1]) + (screen[2] + screen[3]))

    split_tiles(lambda t: e_ref[t], tiles // 2, rows, matrix, temp_s, use)


def split_tiles(load, tiles, rows, matrix, temp, use):
    for start in range(0, tiles, BATCH):
        wide = [
            jnp.concatenate([load(2 * c), load(2 * c + 1)], 1)
            for c in range(start, start + BATCH)
        ]
        out = moved(jnp.concatenate(wide, 0), matrix)
        for i in range(BATCH):
            use(start + i, quarters_of(out[i * rows : (i + 1) * rows], temp.at[i, :, :rows]))


def half_sweep(v, load_s, load_i, tiles, red, unroll):
    rows = v[0].shape[1]
    lane = lane_ids(rows)
    y, z, qa, qb = (1, 2, 0, 3) if red else (3, 0, 2, 1)
    col_a, col_b = (col_prev, col_next) if red else (col_next, col_prev)

    def beside_virtual(q):
        ns, we = q ^ 1, q ^ 2
        here = v[ns][tiles]
        if q % 2 == 0:
            lat = jnp.where(lane == 0, roll_up(v[ns][tiles - 1]), roll_up(here))
        else:
            lat = jnp.where(lane == LANES - 1, roll_down(v[ns][0]), roll_down(here))
        cols = v[we][tiles]
        return (here + lat) + (cols + (col_prev if q < 2 else col_next)(cols))

    held = [
        (q, (load_s(q, tiles) + beside_virtual(q)) * load_i(q, tiles)) for q in (y, z)
    ]

    def body(t, carry):
        y_before, z_here = carry
        vy, vz = v[y][t], v[z][t]
        y_here = roll_up(vy)
        z_after = roll_down(v[z][t + 1])
        lat_a = vy + jnp.where(lane == 0, y_before, y_here)
        lat_b = vz + jnp.where(lane == LANES - 1, z_after, z_here)
        v[qa][t] = (load_s(qa, t) + (lat_a + (vz + col_a(vz)))) * load_i(qa, t)
        v[qb][t] = (load_s(qb, t) + (lat_b + (vy + col_b(vy)))) * load_i(qb, t)
        return y_here, z_after

    loop(tiles, body, (roll_up(v[y][tiles]), roll_down(v[z][0])), unroll)
    for q, value in held:
        v[q][tiles] = value


def smooth(v, load_s, load_i, tiles, unroll):
    zeros = jnp.zeros(v[0].shape[1:], F32)

    def first(t, _):
        for q in (0, 3):
            v[q][t] = load_s(q, t) * load_i(q, t)
        return 0

    loop(tiles, first, 0, unroll)
    for q in (1, 2):
        v[q][0] = zeros
        v[q][tiles - 1] = zeros
        v[q][tiles] = load_s(q, tiles) * load_i(q, tiles)
        v[3 * (q - 1)][tiles] = zeros
    half_sweep(v, load_s, load_i, tiles, False, unroll)
    half_sweep(v, load_s, load_i, tiles, True, unroll)
    half_sweep(v, load_s, load_i, tiles, False, unroll)


def residuals(v, load_s, load_d, tiles, c0, c1, keep, unroll, valid=None):
    lane = lane_ids(v[0].shape[1])

    def body(t, carry):
        up1, up3, down0, down2 = carry
        x = [v[q][t] for q in range(4)]
        here1, here3 = roll_up(x[1]), roll_up(x[3])
        next0, next2 = (roll_down(v[q][after(t, tiles)]) for q in (0, 2))
        beside = [
            (x[1] + jnp.where(lane == 0, up1, here1)) + (x[2] + col_prev(x[2])),
            (x[0] + jnp.where(lane == LANES - 1, next0, down0)) + (x[3] + col_prev(x[3])),
            (x[3] + jnp.where(lane == 0, up3, here3)) + (x[0] + col_next(x[0])),
            (x[2] + jnp.where(lane == LANES - 1, next2, down2)) + (x[1] + col_next(x[1])),
        ]
        r = [load_s(q, t) - (load_d(q, t) * x[q] - beside[q]) for q in range(4)]
        keep(t, r)
        if valid is not None:
            r = [jnp.where(valid, x, 0.0) for x in r]
        c0[t] = (col_prev(r[2]) + col_next(r[0])) + 3.0 * (r[0] + r[2])
        c1[t] = (col_prev(r[3]) + col_next(r[1])) + 3.0 * (r[1] + r[3])
        return here1, here3, next0, next2

    start = (
        roll_up(v[1][tiles]), roll_up(v[3][tiles]), roll_down(v[0][0]), roll_down(v[2][0])
    )
    body(tiles, loop(tiles, body, start, unroll))


def restrict(c0, c1, tiles, rows, use, unroll):
    lane = lane_ids(rows)

    def body(t, carry):
        up, down = carry
        here, other = c0[t, :rows], c1[t, :rows]
        up_here = roll_up(other)
        down_next = roll_down(c0[after(t, tiles), :rows])
        north = jnp.where(lane == 0, up, up_here)
        south = jnp.where(lane == LANES - 1, down_next, down)
        use(t, ((north + south) + 3.0 * (here + other)) * (1.0 / 16.0))
        return up_here, down_next

    start = roll_up(c1[tiles, :rows]), roll_down(c0[0, :rows])
    body(tiles, loop(tiles, body, start, unroll))


def fine_kernel(
    s_ref, d_ref, i_ref, d1_ref, i1_ref, d2_ref,
    from_other, from_mate, polar_ref, corner_near, corner_far,
    r_ref, s1_ref, d1_virtual, d2_virtual, to_mate, to_other,
    v0, v1, v2, v3, c0, c1, hs, hd, hi, ps, pd, pi, n1, temp,
    w0, w1, w2, w3, e0, e1, pi1,
):
    v = [v0, v1, v2, v3]
    tiles, rows = s_ref.shape[1], s_ref.shape[2]
    sub = row_ids(8)
    odd = is_odd()

    def halo(t, _):
        fill_halo(t, from_mate, from_other, odd, False, hs, hd, hi)
        return 0

    loop(tiles, halo, 0, 8)
    total = -16.0
    for q in range(4):
        own_s, own_d = polar_unpacked(polar_ref, q)
        near_s, near_d = polar_unpacked(corner_near, q)
        far_s, far_d = polar_unpacked(corner_far, q)
        left_s, right_s = chosen(odd, near_s, far_s)
        left_d, right_d = chosen(odd, near_d, far_d)
        total = total + own_d
        ps[q] = own_s
        pd[q] = own_d
        pi[q] = 1.0 / own_d
        source = jnp.where(sub >= 5, left_s, jnp.where(sub <= 2, right_s, 0.0))
        diag = jnp.where(sub >= 5, left_d, jnp.where(sub <= 2, right_d, 4.0))
        hs[q, tiles] = source
        hd[q, tiles] = diag
        hi[q, tiles] = 1.0 / diag

    load_s = loader(s_ref, hs, ps, tiles)
    smooth(v, load_s, loader(i_ref, hi, pi, tiles), tiles, 32)

    def keep(t, r):
        if not (isinstance(t, int) and t == tiles):
            for q in range(4):
                r_ref[q, t] = r[q][:rows]

    residuals(v, load_s, loader(d_ref, hd, pd, tiles), tiles, c0, c1, keep, 16)

    def coarse(t, value):
        n1[t] = value

    restrict(c0, c1, tiles, rows, coarse, 16)

    def use(c, source):
        for q in range(4):
            s1_ref[q, c] = source[q]

    tiles1 = tiles // 2
    split_tiles(lambda t: n1[t], tiles1, rows, splitter(), temp, use)
    out = moved(jnp.concatenate([n1[tiles], total], 0), virtual_splitter())
    source = quarters_of(out[:rows], temp.at[0])
    screen = quarters_of(out[rows:], temp.at[1])
    for q in range(4):
        s1_ref[q, tiles1] = source[q]
        d1_virtual[q] = 4.0 + screen[q]
        pi1[q] = 1.0 / (4.0 + screen[q])
    d2_virtual[...] = 4.0 + ((screen[0] + screen[1]) + (screen[2] + screen[3]))

    def own(main, virtual):
        return lambda q, t: virtual[q] if isinstance(t, int) and t == tiles1 else main[q, t]

    w = [w0, w1, w2, w3]
    rows1 = rows // 2
    row = row_ids(rows1)
    load_s, load_d = own(s1_ref, s1_ref.at[:, tiles1]), own(d1_ref, d1_virtual)
    smooth(w, load_s, own(i1_ref, pi1), tiles1, 16)
    valid = (row >= 2) & (row < rows1 - 2)
    residuals(w, load_s, load_d, tiles1, e0, e1, lambda t, r: None, 16, valid)

    def edges(t, partial):
        virtual = isinstance(t, int) and t == tiles1
        source = [s1_ref[q, t] for q in range(4)]
        diag = [load_d(q, t) for q in range(4)]
        diag2 = d2_virtual[...] if virtual else d2_ref[t]
        right, left = wide_packs(source, diag, partial, diag2, virtual)
        for i in range(4):
            to_mate[i, t], to_other[i, t] = chosen(odd, left[i], right[i])

    restrict(e0, e1, tiles1, rows1, edges, 16)


def merge_kernel(r_ref, out_ref, temp, out_buf, sems):
    tiles = r_ref.shape[1]
    rows = r_ref.shape[2]
    matrix = merger()
    chunk = out_ref.shape[1] // GROUPS
    copies = []
    for group in range(GROUPS):
        for batch in range(tiles // GROUPS // BATCH):
            start = group * (tiles // GROUPS) + batch * BATCH
            both = []
            for i in range(BATCH):
                for pr in (0, 1):
                    for pc in (0, 1):
                        temp[i, pr, pl.ds(pc, rows, 2), :] = r_ref[2 * pc + pr, start + i]
                both.append(jnp.concatenate([temp[i, 0], temp[i, 1]], 1))
            out = moved(jnp.concatenate(both, 0), matrix)
            for i in range(BATCH):
                where = slice((start + i) * 256, (start + i + 1) * 256)
                out_buf[:, where] = out[2 * rows * i : 2 * rows * (i + 1)]
        part = pl.ds(group * chunk, chunk)
        copy = pltpu.make_async_copy(out_buf.at[:, part], out_ref.at[:, part], sems.at[group])
        copy.start()
        copies.append(copy)
    for copy in copies:
        copy.wait()


def coarse_kernel(
    s_ref, d_ref, i_ref, d_virtual, d2_ref, d2_virtual, from_other, from_mate,
    solution_ref, residual_ref,
    v0, v1, v2, v3, c0, c1, hs, hd, hi, pi, part, s, d, inv, va, vb,
):
    v = [v0, v1, v2, v3]
    tiles, own = d_ref.shape[1], d_ref.shape[2]
    rows = own + 8
    sub = row_ids(8)
    odd_band = is_odd()
    for t in range(tiles + 1):
        pairs = [chosen(odd_band, from_mate[i, t], from_other[i, t]) for i in range(4)]
        left, right = zip(*pairs)
        source, diag, part[t] = wide_unpacked(left, right, t == tiles)
        for q in range(4):
            hs[q, t] = source[q]
            hd[q, t] = diag[q]
            hi[q, t] = 1.0 / diag[q]
        total = (diag[0] + diag[1]) + (diag[2] + diag[3]) - 12.0
        total = jnp.where((sub == 3) | (sub == 4), 1.0, total)
        here = d2_virtual[...] if t == tiles else d2_ref[t]
        d[t] = jnp.concatenate([here, total], 0)
    for q in range(4):
        pi[q] = 1.0 / d_virtual[q]

    def load_s(q, t):
        return jnp.concatenate([s_ref[q, t], hs[q, t]], 0)

    smooth(v, load_s, loader(i_ref, hi, pi, tiles), tiles, 16)
    lane, row = lane_ids(rows), row_ids(rows)
    valid = (row < own + 2) | (row >= own + 6)
    load_d = loader(d_ref, hd, d_virtual, tiles)
    residuals(v, load_s, load_d, tiles, c0, c1, lambda t, r: None, 16, valid)

    even = (lane + row) % 2 == 0
    odd = jnp.logical_not(even)

    def start(t, value):
        source = jnp.concatenate([value[:own], value[own:] + part[t]], 0)
        inverse = 1.0 / d[t]
        s[t] = source
        inv[t] = inverse
        virtual = isinstance(t, int) and t == tiles
        va[t] = jnp.where(odd if virtual else even, source * inverse, 0.0)

    restrict(c0, c1, tiles, rows, start, 16)

    def scan(v, use):
        up, down = roll_up(v[tiles]), roll_down(v[0])
        for t in range(tiles + 1):
            x = v[t]
            up_here, down_next = roll_up(x), roll_down(v[after(t, tiles)])
            north = jnp.where(lane == 0, up, up_here)
            south = jnp.where(lane == LANES - 1, down_next, down)
            use(t, x, (col_prev(x) + col_next(x)) + (north + south))
            up, down = up_here, down_next

    for old, new, mask, other in ((va, vb, odd, even), (vb, va, even, odd), (va, vb, odd, even)):

        def relax(t, x, beside):
            update = other if t == tiles else mask
            new[t] = jnp.where(update, (s[t] + beside) * inv[t], x)

        scan(old, relax)

    def finish(t, x, beside):
        if t < tiles:
            where = slice(t * LANES, (t + 1) * LANES)
            solution_ref[:, where] = x[:own]
            residual_ref[:, where] = (s[t] - (d[t] * x - beside))[:own]

    scan(vb, finish)


VMEM = pl.BlockSpec(memory_space=pltpu.VMEM)
HBM = pl.BlockSpec(memory_space=pltpu.HBM)


def call(kernel, out_shapes, scratch, *args, sems=None, far_in=0, far_out=0):
    scratch = [pltpu.VMEM(x, F32) if isinstance(x, tuple) else x for x in scratch]
    if sems is not None:
        scratch.append(pltpu.SemaphoreType.DMA(sems))
    return pl.pallas_call(
        kernel,
        out_shape=[jax.ShapeDtypeStruct(shape, F32) for shape in out_shapes],
        in_specs=[HBM] * far_in + [VMEM] * (len(args) - far_in),
        out_specs=[HBM] * far_out + [VMEM] * (len(out_shapes) - far_out),
        scratch_shapes=scratch,
        compiler_params=pltpu.CompilerParams(vmem_limit_bytes=40 * 2**20),
    )(*args)


def swapped_with(x, by):
    count = lax.axis_size("lon")
    pairs = [(i, (i + by) % count) for i in range(0, count, 2)]
    return lax.ppermute(x, "lon", pairs + [(b, a) for a, b in pairs])


def swapped_edges(to_mate, to_other):
    from_mate = swapped_with(to_mate, 1)
    return from_mate, swapped_with(to_other, -1)


def body(right_side, texel_weight, seam_flags):
    columns, height = right_side.shape
    half_turn = lax.axis_size("lon") // 2
    tiles, rows = height // 256, columns // 2
    tiles1, rows1 = tiles // 2, rows // 2
    temp = (BATCH, 2, columns, LANES)
    quarters = (4, tiles, rows, LANES)
    quarters1 = (4, tiles1, rows1, LANES)
    pack = (2, tiles, 8, LANES)
    corner = (2, 8, LANES)
    split = (2, 16 * tiles, LANES)
    to_mate, to_other, polar, corner_near, corner_far = call(
        edge_kernel,
        [pack, pack, (2, rows, LANES), corner, corner],
        [(16, height), pltpu.VMEM((32, height), BF16)]
        + [(2, columns, 256), pltpu.VMEM((2, columns, 256), BF16)]
        + [pltpu.VMEM(seam_flags.shape, jnp.int32), split, split]
        + [(2, 2, columns, LANES)] * 2
        + [(tiles, 8, LANES)],
        *[
            pltpu.with_memory_space_constraint(x, pltpu.HBM)
            for x in (right_side, texel_weight, seam_flags)
        ],
        sems=(9,), far_in=3,
    )
    from_mate, from_other = swapped_edges(to_mate, to_other)
    polar = lax.ppermute(
        polar, "lon", [(i, (i + half_turn) % (2 * half_turn)) for i in range(2 * half_turn)]
    )
    corner_near_own = corner_near
    corner_far = swapped_with(corner_far, half_turn - 1)
    corner_near = swapped_with(corner_near, half_turn + 1)
    s, d, inverse, d1, i1, d2 = call(
        bulk_kernel,
        [quarters] * 3 + [quarters1, quarters1, quarters1[1:]],
        [temp, temp, (tiles, 8, LANES), quarters[1:]],
        right_side, texel_weight, seam_flags, corner_near_own,
    )

    def level_scratch(tiles, rows):
        return [(tiles + 1, rows, LANES)] * 6

    def halo_scratch(tiles):
        return [(4, tiles + 1, 8, LANES)] * 3

    pack1 = (4, tiles1 + 1, 8, LANES)
    r, s1, d1_virtual, d2_virtual, to_mate, to_other = call(
        fine_kernel,
        [quarters, (4, tiles1 + 1, rows1, LANES), (4, rows1, LANES), (rows1, LANES), pack1, pack1],
        level_scratch(tiles, rows + 8)
        + halo_scratch(tiles)
        + [(4, rows, LANES)] * 3
        + [(tiles + 1, rows, LANES), (BATCH, 2, rows, LANES)]
        + level_scratch(tiles1, rows1)
        + [(4, rows1, LANES)],
        s, d, inverse, d1, i1, d2, from_other, from_mate, polar, corner_near, corner_far,
    )
    from_mate, from_other = swapped_edges(to_mate, to_other)
    (fine_residual,) = call(
        merge_kernel, [(columns, height)], [temp, (columns, height)], r,
        sems=(GROUPS,), far_out=1,
    )
    wide = (tiles1 + 1, rows1 + 8, LANES)
    solution_2, residual_2 = call(
        coarse_kernel,
        [(columns // 4, height // 4)] * 2,
        level_scratch(tiles1, rows1 + 8)
        + halo_scratch(tiles1)
        + [(4, rows1, LANES), (tiles1 + 1, 8, LANES)]
        + [wide] * 5,
        s1, d1, i1, d1_virtual, d2, d2_virtual, from_other, from_mate,
    )
    return fine_residual, solution_2, residual_2


def solution(mesh):
    spec = P(("groups", "lon"), None)
    return jax.shard_map(
        body, mesh=mesh, in_specs=(spec,) * 3, out_specs=(spec,) * 3, check_vma=False
    )
```

```python
import jax
import jax.numpy as jnp
from jax import lax
from jax.experimental import pallas as pl
from jax.experimental.pallas import tpu as pltpu
from jax.sharding import PartitionSpec as P

TILE = 32
SEAM_SCALE = 0.1
LANES = 128
GROUPS = 4
BATCH = 4
F32 = jnp.float32
BF16 = jnp.bfloat16


def loop(count, body, carry=0, unroll=4):
    unroll = min(unroll, count)

    def steps(block, carry):
        for i in range(unroll):
            carry = body(block * unroll + i, carry)
        return carry

    whole = count // unroll
    carry = steps(0, carry) if whole == 1 else lax.fori_loop(0, whole, steps, carry)
    for t in range(whole * unroll, count):
        carry = body(t, carry)
    return carry


def before(t, tiles):
    return (tiles if t == 0 else t - 1) if isinstance(t, int) else jnp.where(t == 0, tiles, t - 1)


def after(t, tiles):
    return (0 if t == tiles else t + 1) if isinstance(t, int) else t + 1


def lane_ids(rows):
    return lax.broadcasted_iota(jnp.int32, (rows, LANES), 1)


def row_ids(rows):
    return lax.broadcasted_iota(jnp.int32, (rows, LANES), 0)


def roll_up(x):
    return pltpu.roll(x, 1, 1)


def roll_down(x):
    return pltpu.roll(x, LANES - 1, 1)


def roll_rows(x, by):
    by %= x.shape[0]
    return x if by == 0 else pltpu.roll(x, by, 0)


def roll_lanes(x, by):
    by %= LANES
    return x if by == 0 else pltpu.roll(x, by, 1)


def col_prev(x):
    return pltpu.roll(x, 1, 0)


def col_next(x):
    return pltpu.roll(x, x.shape[0] - 1, 0)


def selector(shape, rule):
    a = lax.broadcasted_iota(jnp.int32, shape, 0)
    b = lax.broadcasted_iota(jnp.int32, shape, 1)
    return jnp.where(rule(a, b), 1.0, 0.0).astype(BF16)


def splitter():
    return selector((256, 256), lambda a, b: a == 2 * (b % LANES) + b // LANES)


def merger():
    return selector((256, 256), lambda a, b: b == 2 * (a % LANES) + a // LANES)


def virtual_splitter():
    return selector(
        (LANES, 256),
        lambda a, b: a // 2 + jnp.where(a >= 64, 64, 0) + LANES * (a % 2) == b,
    )


def moved(x, matrix, exact=None):
    rows = x.shape[0]
    high = x.astype(BF16)
    low = (x - high.astype(F32)).astype(BF16)
    terms = [high, low] if exact is None else [high, low, exact]
    out = jnp.dot(jnp.concatenate(terms, 0), matrix, preferred_element_type=F32)
    both = out[:rows] + out[rows : 2 * rows]
    return both if exact is None else (both, out[2 * rows :])


def quarters_of(parts, temp):
    count = parts.shape[0] // 2
    temp[0] = parts[:, :LANES]
    temp[1] = parts[:, LANES:]
    return [temp[pr, pl.ds(pc, count, 2), :] for pc in (0, 1) for pr in (0, 1)]


def reds(swapped):
    return (1, 2) if swapped else (0, 3)


def interleaved(group, offset):
    sub = row_ids(8)
    packed = roll_rows(group[0], offset)
    for q in range(1, 4):
        packed = jnp.where(sub // 2 == q, roll_rows(group[q], 2 * q + offset), packed)
    return packed


def edge_packs(source, diag, swapped):
    sub = row_ids(8)
    even, odd = reds(swapped)
    rows = source[0].shape[0]
    packs = []
    for here, first, second, row, step in (
        (slice(rows - 8, rows), even, odd, 6, 1),
        (slice(0, 8), odd, even, 1, -1),
    ):
        gs = [x[here] for x in source]
        gd = [x[here] for x in diag]
        near = gs[first] / gd[first]
        far = roll_rows(gs[second] / gd[second], step)
        gs[first] = jnp.where(sub == row, near, gs[first])
        gd[first] = jnp.where(sub == row, far, gd[first])
        offset = 2 if row == 6 else 0
        packs.append((interleaved(gs, offset), interleaved(gd, offset)))
    return packs


def unpacked_halo(left, right, swapped):
    sub = row_ids(8)
    even, odd = reds(swapped)
    (al, bl), (ar, br) = left, right
    source, diag = [], []
    for q in range(4):
        s = jnp.where(
            sub >= 6,
            roll_rows(al, 6 - 2 * q),
            jnp.where(sub <= 1, roll_rows(ar, -2 * q), 0.0),
        )
        d = jnp.where(
            sub >= 6,
            roll_rows(bl, 6 - 2 * q),
            jnp.where(sub <= 1, roll_rows(br, -2 * q), 4.0),
        )
        if q == even:
            s = jnp.where(sub == 2, roll_rows(br, 1 - 2 * odd), s)
            d = jnp.where((sub == 2) | (sub == 6), 1.0, d)
        if q == odd:
            s = jnp.where(sub == 5, roll_rows(bl, 5 - 2 * even), s)
            d = jnp.where((sub == 5) | (sub == 1), 1.0, d)
        source.append(s)
        diag.append(d)
    return source, diag


def is_odd():
    return lax.rem(lax.axis_index("lon"), 2) == 1


def chosen(odd, a, b):
    return jnp.where(odd, a, b), jnp.where(odd, b, a)


def store_edges(t, packs, odd, to_mate, to_other):
    right, left = packs
    for i in (0, 1):
        to_mate[i, t], to_other[i, t] = chosen(odd, left[i], right[i])


def placed(rows):
    sub = row_ids(8)
    packed = roll_rows(rows[0][0], -rows[0][1])
    for i, (x, at) in enumerate(rows):
        if i:
            packed = jnp.where(sub == i, roll_rows(x, i - at), packed)
    return packed


def sides(swapped):
    even, odd = reds(swapped)
    return (even, even ^ 1, odd, odd ^ 1), (odd, odd ^ 1, even, even ^ 1)


def state_packs(source, diag, last, first_black, residual, partial, diag2, swapped):
    rows = source[0].shape[0]
    packs = []
    for (a, ab, b, bb), here, near, far, ends in zip(
        sides(swapped),
        (slice(rows - 8, rows), slice(0, 8)),
        (7, 0),
        (6, 1),
        ((4, 5, 6), (3, 2, 1)),
    ):
        s, d, v = ([x[here] for x in group] for group in (source, diag, last))
        part, d2 = partial[here], diag2[here]
        pack0 = [(x, near) for x in s + d]
        pack1 = [
            (first_black[ab][here], near),
            (s[bb] + v[a], far),
            (d[bb], far),
            (first_black[bb][here], far),
            (v[b], far),
            (s[b] - d[b] * v[b] + v[ab], far),
            (residual[a][here] - v[bb], far),
            (part / d2, ends[0]),
        ]
        pack2 = [(part, ends[1]), (part, ends[2]), (d2, ends[1]), (d2, ends[2])]
        packs.append((placed(pack0), placed(pack1), placed(pack2)))
    return packs


def fill_halo(t, from_mate, from_other, odd, swapped, hs, hd, hi):
    al, ar = chosen(odd, from_mate[0, t], from_other[0, t])
    bl, br = chosen(odd, from_mate[1, t], from_other[1, t])
    source, diag = unpacked_halo((al, bl), (ar, br), swapped)
    for q in range(4):
        hs[q, t] = source[q]
        hd[q, t] = diag[q]
        hi[q, t] = 1.0 / diag[q]


def loader(own, halo, virtual, tiles):
    def load(q, t):
        if isinstance(t, int) and t == tiles:
            return jnp.concatenate([virtual[q], halo[q, t]], 0)
        return jnp.concatenate([own[q, t], halo[q, t]], 0)

    return load


def polar_packs(tiles_of):
    lane = lane_ids(tiles_of[0][0].shape[0])
    packs = []
    for pc in (0, 1):
        parts = [*tiles_of[2 * pc], *tiles_of[2 * pc + 1]]
        packed = parts[0]
        for m in range(1, 4):
            mine = (lane + (16 - 32 * m) % LANES) % LANES < 32
            packed = jnp.where(mine, roll_lanes(parts[m], 32 * m), packed)
        packs.append(packed)
    return packs


def polar_unpacked(x, q):
    lane = lane_ids(x.shape[1])
    used = (lane < 16) | (lane >= LANES - 16)
    m = 2 * (q % 2)
    return (
        jnp.where(used, roll_lanes(x[q // 2], 32 * m), 0.0),
        jnp.where(used, roll_lanes(x[q // 2], 32 * (m + 1)), 4.0),
    )


def seam_scales(flags, chunks):
    flag_cols, flag_lats = flags.shape
    flags = jnp.concatenate(
        [flags.astype(F32), jnp.zeros((8 - flag_cols, flag_lats), F32)], 0
    )
    lat = lax.broadcasted_iota(jnp.int32, (8, flag_lats), 1)
    stacked = jnp.concatenate([jnp.where(lat // 8 == c, flags, 0.0) for c in chunks], 0)
    spread = selector((flag_lats, LANES), lambda a, b: a % 8 == b // (TILE // 2))
    spread_flags = jnp.dot(stacked.astype(BF16), spread, preferred_element_type=F32)
    scale = jnp.where(spread_flags > 0.5, SEAM_SCALE, 1.0)
    return scale.reshape(len(chunks), 8, LANES)


def seam_rows(scales, flag_cols, rows):
    size = (rows // flag_cols, LANES)
    return jnp.concatenate(
        [jnp.broadcast_to(scales[i : i + 1], size) for i in range(flag_cols)], 0
    )


def edge_kernel(
    right_ref, weight_ref, flag_ref,
    to_mate, to_other, polar_ref, corner_near, corner_far,
    edge_s, edge_w, end_s, end_w, flags, temp_s, temp_w, temp_p, temp_q, scale_ref, sems,
):
    columns, height = right_ref.shape
    rows, tiles = columns // 2, height // 256
    pairs = [(flag_ref, flags)]
    for i, (src, dst, size) in enumerate(
        ((right_ref, edge_s, 8), (weight_ref, edge_w, 16))
    ):
        pairs.append((src.at[pl.ds(0, size)], dst.at[pl.ds(0, size)]))
        pairs.append((src.at[pl.ds(columns - size, size)], dst.at[pl.ds(size, size)]))
    for src, dst in ((right_ref, end_s), (weight_ref, end_w)):
        for end, start in enumerate((0, height - 256)):
            pairs.append((src.at[:, pl.ds(start, 256)], dst.at[end]))
    copies = [
        pltpu.make_async_copy(src, dst, sems.at[i]) for i, (src, dst) in enumerate(pairs)
    ]
    for copy in copies:
        copy.start()
    odd = is_odd()
    matrix = splitter()
    flag_cols = flag_ref.shape[0]
    copies[0].wait()
    scale_ref[...] = seam_scales(flags[...], range(tiles))
    for copy in copies[1:5]:
        copy.wait()
    sub = row_ids(8)
    lanes = [slice(c * 256, (c + 1) * 256) for c in range(tiles)]
    source, weight = moved(
        jnp.concatenate([edge_s[:, w] for w in lanes], 0),
        matrix,
        jnp.concatenate([edge_w[:, w] for w in lanes], 0),
    )
    weight = weight.reshape(tiles, 32, 256)
    weight = jnp.concatenate([weight[:, :8], weight[:, 24:]], 1).reshape(tiles * 16, 256)
    source = quarters_of(source, temp_s)
    weight = quarters_of(weight, temp_w)
    for c in range(tiles):
        here = slice(c * 8, (c + 1) * 8)
        scales = scale_ref[c]
        scale = jnp.where(sub < 4, scales[:1], scales[flag_cols - 1 : flag_cols])
        diag = [4.0 + w[here] * scale for w in weight]
        store_edges(
            c, edge_packs([x[here] for x in source], diag, False), odd, to_mate, to_other
        )

    for copy in copies[5:]:
        copy.wait()
    mirror = selector((LANES, LANES), lambda a, b: a + b == LANES - 1)
    lane = lane_ids(rows)
    source, weight = moved(
        jnp.concatenate([end_s[0], end_s[1]], 0),
        matrix,
        jnp.concatenate([end_w[0], end_w[1]], 0),
    )
    found = []
    for end, c in enumerate((0, tiles - 1)):
        here = slice(end * columns, (end + 1) * columns)
        scale = seam_rows(scale_ref[c], flag_cols, rows)
        found.append(
            (
                quarters_of(source[here], temp_p.at[end]),
                [4.0 + w * scale for w in quarters_of(weight[here], temp_q.at[end])],
            )
        )
    ends = [
        [jnp.where(lane >= 64, found[1][i][q ^ 1], found[0][i][q ^ 1]) for i in (0, 1)]
        for q in range(4)
    ]
    both = moved(jnp.concatenate(polar_packs(ends), 0), mirror)
    for pc in (0, 1):
        pack = both[pc * rows : (pc + 1) * rows]
        polar_ref[pc] = pack
        corner_near[pc], corner_far[pc] = chosen(odd, pack[:8], pack[rows - 8 :])


def bulk_kernel(
    right_ref, weight_ref, flag_ref, edges_first,
    s_ref, d_ref, i_ref, d1_ref, i1_ref, d2_ref,
    temp_s, temp_d, scale_ref, e_ref,
):
    tiles, rows = s_ref.shape[1], s_ref.shape[2]
    columns = 2 * rows
    matrix = splitter()
    scale_ref[...] = seam_scales(flag_ref[...], range(tiles))
    for start in range(0, tiles, BATCH):
        lanes = [slice((start + i) * 256, (start + i + 1) * 256) for i in range(BATCH)]
        source, weight = moved(
            jnp.concatenate([right_ref[:, w] for w in lanes], 0),
            matrix,
            jnp.concatenate([weight_ref[:, w] for w in lanes], 0),
        )
        for i in range(BATCH):
            c = start + i
            here = slice(i * columns, (i + 1) * columns)
            scale = seam_rows(scale_ref[c], flag_ref.shape[0], rows)
            for q, value in enumerate(quarters_of(source[here], temp_s.at[i])):
                s_ref[q, c] = value
            screen = [w * scale for w in quarters_of(weight[here], temp_d.at[i])]
            e_ref[c] = (screen[0] + screen[1]) + (screen[2] + screen[3])
            for q in range(4):
                diag = 4.0 + screen[q]
                d_ref[q, c] = diag
                i_ref[q, c] = 1.0 / diag

    def use(c, screen):
        for q in range(4):
            d1_ref[q, c] = 4.0 + screen[q]
            i1_ref[q, c] = 1.0 / (4.0 + screen[q])
        d2_ref[c] = 4.0 + ((screen[0] + screen[1]) + (screen[2] + screen[3]))

    split_tiles(lambda t: e_ref[t], tiles // 2, rows, matrix, temp_s, use)


def split_tiles(load, tiles, rows, matrix, temp, use):
    for start in range(0, tiles, BATCH):
        wide = [
            jnp.concatenate([load(2 * c), load(2 * c + 1)], 1)
            for c in range(start, start + BATCH)
        ]
        out = moved(jnp.concatenate(wide, 0), matrix)
        for i in range(BATCH):
            use(start + i, quarters_of(out[i * rows : (i + 1) * rows], temp.at[i, :, :rows]))


def half_sweep(v, load_s, load_i, tiles, red, unroll):
    rows = v[0].shape[1]
    lane = lane_ids(rows)
    y, z, qa, qb = (1, 2, 0, 3) if red else (3, 0, 2, 1)
    col_a, col_b = (col_prev, col_next) if red else (col_next, col_prev)

    def beside_virtual(q):
        ns, we = q ^ 1, q ^ 2
        here = v[ns][tiles]
        if q % 2 == 0:
            lat = jnp.where(lane == 0, roll_up(v[ns][tiles - 1]), roll_up(here))
        else:
            lat = jnp.where(lane == LANES - 1, roll_down(v[ns][0]), roll_down(here))
        cols = v[we][tiles]
        return (here + lat) + (cols + (col_prev if q < 2 else col_next)(cols))

    held = [
        (q, (load_s(q, tiles) + beside_virtual(q)) * load_i(q, tiles)) for q in (y, z)
    ]

    def body(t, carry):
        y_before, z_here = carry
        vy, vz = v[y][t], v[z][t]
        y_here = roll_up(vy)
        z_after = roll_down(v[z][t + 1])
        lat_a = vy + jnp.where(lane == 0, y_before, y_here)
        lat_b = vz + jnp.where(lane == LANES - 1, z_after, z_here)
        v[qa][t] = (load_s(qa, t) + (lat_a + (vz + col_a(vz)))) * load_i(qa, t)
        v[qb][t] = (load_s(qb, t) + (lat_b + (vy + col_b(vy)))) * load_i(qb, t)
        return y_here, z_after

    loop(tiles, body, (roll_up(v[y][tiles]), roll_down(v[z][0])), unroll)
    for q, value in held:
        v[q][tiles] = value


def smooth(v, load_s, load_i, tiles, unroll, after_sweep=None):
    zeros = jnp.zeros(v[0].shape[1:], F32)

    def first(t, _):
        for q in (0, 3):
            v[q][t] = load_s(q, t) * load_i(q, t)
        return 0

    loop(tiles, first, 0, unroll)
    for q in (1, 2):
        v[q][0] = zeros
        v[q][tiles - 1] = zeros
        v[q][tiles] = load_s(q, tiles) * load_i(q, tiles)
        v[3 * (q - 1)][tiles] = zeros
    for sweep, red in enumerate((False, True, False)):
        half_sweep(v, load_s, load_i, tiles, red, unroll)
        if after_sweep is not None:
            after_sweep(sweep)


def residuals(v, load_s, load_d, tiles, c0, c1, keep, unroll, valid=None):
    lane = lane_ids(v[0].shape[1])

    def body(t, carry):
        up1, up3, down0, down2 = carry
        x = [v[q][t] for q in range(4)]
        here1, here3 = roll_up(x[1]), roll_up(x[3])
        next0, next2 = (roll_down(v[q][after(t, tiles)]) for q in (0, 2))
        beside = [
            (x[1] + jnp.where(lane == 0, up1, here1)) + (x[2] + col_prev(x[2])),
            (x[0] + jnp.where(lane == LANES - 1, next0, down0)) + (x[3] + col_prev(x[3])),
            (x[3] + jnp.where(lane == 0, up3, here3)) + (x[0] + col_next(x[0])),
            (x[2] + jnp.where(lane == LANES - 1, next2, down2)) + (x[1] + col_next(x[1])),
        ]
        r = [load_s(q, t) - (load_d(q, t) * x[q] - beside[q]) for q in range(4)]
        keep(t, r)
        if valid is not None:
            virtual = isinstance(t, int) and t == tiles
            r = [jnp.where(valid(q, virtual), r[q], 0.0) for q in range(4)]
        c0[t] = (col_prev(r[2]) + col_next(r[0])) + 3.0 * (r[0] + r[2])
        c1[t] = (col_prev(r[3]) + col_next(r[1])) + 3.0 * (r[1] + r[3])
        return here1, here3, next0, next2

    start = (
        roll_up(v[1][tiles]), roll_up(v[3][tiles]), roll_down(v[0][0]), roll_down(v[2][0])
    )
    body(tiles, loop(tiles, body, start, unroll))


def restrict(c0, c1, tiles, rows, use, unroll):
    lane = lane_ids(rows)

    def body(t, carry):
        up, down = carry
        here, other = c0[t, :rows], c1[t, :rows]
        up_here = roll_up(other)
        down_next = roll_down(c0[after(t, tiles), :rows])
        north = jnp.where(lane == 0, up, up_here)
        south = jnp.where(lane == LANES - 1, down_next, down)
        use(t, ((north + south) + 3.0 * (here + other)) * (1.0 / 16.0))
        return up_here, down_next

    start = roll_up(c1[tiles, :rows]), roll_down(c0[0, :rows])
    body(tiles, loop(tiles, body, start, unroll))


def fine_kernel(
    s_ref, d_ref, i_ref, d1_ref, i1_ref, d2_ref,
    from_other, from_mate, polar_ref, corner_near, corner_far,
    r_ref, s1_ref, d1_virtual, d2_virtual, to_mate, to_other,
    v0, v1, v2, v3, c0, c1, hs, hd, hi, ps, pd, pi, n1, temp,
    w0, w1, w2, w3, e0, e1, pi1, black_even, black_odd, red_even, red_odd,
):
    v = [v0, v1, v2, v3]
    tiles, rows = s_ref.shape[1], s_ref.shape[2]
    sub = row_ids(8)
    odd = is_odd()

    def halo(t, _):
        fill_halo(t, from_mate, from_other, odd, False, hs, hd, hi)
        return 0

    loop(tiles, halo, 0, 8)
    total = -16.0
    for q in range(4):
        own_s, own_d = polar_unpacked(polar_ref, q)
        near_s, near_d = polar_unpacked(corner_near, q)
        far_s, far_d = polar_unpacked(corner_far, q)
        left_s, right_s = chosen(odd, near_s, far_s)
        left_d, right_d = chosen(odd, near_d, far_d)
        total = total + own_d
        ps[q] = own_s
        pd[q] = own_d
        pi[q] = 1.0 / own_d
        source = jnp.where(sub >= 5, left_s, jnp.where(sub <= 2, right_s, 0.0))
        diag = jnp.where(sub >= 5, left_d, jnp.where(sub <= 2, right_d, 4.0))
        hs[q, tiles] = source
        hd[q, tiles] = diag
        hi[q, tiles] = 1.0 / diag

    load_s = loader(s_ref, hs, ps, tiles)
    smooth(v, load_s, loader(i_ref, hi, pi, tiles), tiles, 32)

    def keep(t, r):
        if not (isinstance(t, int) and t == tiles):
            for q in range(4):
                r_ref[q, t] = r[q][:rows]

    residuals(v, load_s, loader(d_ref, hd, pd, tiles), tiles, c0, c1, keep, 16)

    def coarse(t, value):
        n1[t] = value

    restrict(c0, c1, tiles, rows, coarse, 16)

    def use(c, source):
        for q in range(4):
            s1_ref[q, c] = source[q]

    tiles1 = tiles // 2
    split_tiles(lambda t: n1[t], tiles1, rows, splitter(), temp, use)
    out = moved(jnp.concatenate([n1[tiles], total], 0), virtual_splitter())
    source = quarters_of(out[:rows], temp.at[0])
    screen = quarters_of(out[rows:], temp.at[1])
    for q in range(4):
        s1_ref[q, tiles1] = source[q]
        d1_virtual[q] = 4.0 + screen[q]
        pi1[q] = 1.0 / (4.0 + screen[q])
    d2_virtual[...] = 4.0 + ((screen[0] + screen[1]) + (screen[2] + screen[3]))

    def own(main, virtual):
        return lambda q, t: virtual[q] if isinstance(t, int) and t == tiles1 else main[q, t]

    w = [w0, w1, w2, w3]
    rows1 = rows // 2
    row = row_ids(rows1)
    load_s, load_d = own(s1_ref, s1_ref.at[:, tiles1]), own(d1_ref, d1_virtual)

    def after_sweep(sweep):
        if sweep == 0:
            for t in range(tiles1 + 1):
                even, odd_red = reds(t == tiles1)
                black_even[t] = w[even ^ 1][t]
                black_odd[t] = w[odd_red ^ 1][t]

    smooth(w, load_s, own(i1_ref, pi1), tiles1, 16, after_sweep)

    def valid(q, virtual):
        even, odd_red = reds(virtual)
        first = 1 if q == odd_red ^ 1 else 2
        last = rows1 - 2 if q == even ^ 1 else rows1 - 3
        return (row >= first) & (row <= last)

    def keep_red(t, r):
        even, odd_red = reds(isinstance(t, int) and t == tiles1)
        red_even[t] = r[even]
        red_odd[t] = r[odd_red]

    residuals(w, load_s, load_d, tiles1, e0, e1, keep_red, 16, valid)
    shared = {}

    def edges(t, partial):
        virtual = t == tiles1
        even, odd_red = reds(virtual)
        packs = state_packs(
            [s1_ref[q, t] for q in range(4)],
            [load_d(q, t) for q in range(4)],
            [w[q][t] for q in range(4)],
            {even ^ 1: black_even[t], odd_red ^ 1: black_odd[t]},
            {even: red_even[t], odd_red: red_odd[t]},
            partial,
            d2_virtual[...] if virtual else d2_ref[t],
            virtual,
        )
        right, left = packs
        count = tiles1 + 1
        for i in (0, 1):
            to_mate[i * count + t], to_other[i * count + t] = chosen(odd, left[i], right[i])
        pair = chosen(odd, left[2], right[2])
        if t % 2 == 0:
            shared[0] = pair
        if t % 2 == 1 or virtual:
            if t % 2 == 1:
                pair = [
                    jnp.where(sub < 4, x, roll_rows(y, 4)) for x, y in zip(shared[0], pair)
                ]
            to_mate[2 * count + t // 2], to_other[2 * count + t // 2] = pair

    restrict(e0, e1, tiles1, rows1, edges, 16)


def merge_kernel(r_ref, out_ref, temp, out_buf, sems):
    tiles = r_ref.shape[1]
    rows = r_ref.shape[2]
    matrix = merger()
    chunk = out_ref.shape[1] // GROUPS
    copies = []
    for group in range(GROUPS):
        for batch in range(tiles // GROUPS // BATCH):
            start = group * (tiles // GROUPS) + batch * BATCH
            both = []
            for i in range(BATCH):
                for pr in (0, 1):
                    for pc in (0, 1):
                        temp[i, pr, pl.ds(pc, rows, 2), :] = r_ref[2 * pc + pr, start + i]
                both.append(jnp.concatenate([temp[i, 0], temp[i, 1]], 1))
            out = moved(jnp.concatenate(both, 0), matrix)
            for i in range(BATCH):
                where = slice((start + i) * 256, (start + i + 1) * 256)
                out_buf[:, where] = out[2 * rows * i : 2 * rows * (i + 1)]
        part = pl.ds(group * chunk, chunk)
        copy = pltpu.make_async_copy(out_buf.at[:, part], out_ref.at[:, part], sems.at[group])
        copy.start()
        copies.append(copy)
    for copy in copies:
        copy.wait()


def coarse_kernel(
    s_ref, d_ref, i_ref, d_virtual, d2_ref, d2_virtual, from_other, from_mate,
    solution_ref, residual_ref,
    v0, v1, v2, v3, c0, c1, hs, hd, hi, pi, part, fixes, s, d, inv, va, vb,
):
    v = [v0, v1, v2, v3]
    tiles, own = d_ref.shape[1], d_ref.shape[2]
    rows = own + 8
    count = tiles + 1
    sub = row_ids(8)
    odd_band = is_odd()
    for t in range(count):
        places = t, count + t, 2 * count + t // 2
        packs = [chosen(odd_band, from_mate[i], from_other[i]) for i in places]
        source = [jnp.zeros((8, LANES), F32)] * 4
        diag = [jnp.full((8, LANES), 4.0, F32)] * 4
        inverse = [jnp.zeros((8, LANES), F32)] * 4
        fixed = [jnp.zeros((8, LANES), F32)] * 4
        more = jnp.zeros((8, LANES), F32)
        total = jnp.ones((8, LANES), F32)
        third = 4 * (t % 2)
        for side, (a, ab, b, bb) in enumerate(sides(t == tiles)):
            near, far, step = (7, 6, -1) if side == 0 else (0, 1, 1)
            pack0, pack1, pack2 = (pair[side] for pair in packs)

            def put(group, q, at, pack, row):
                group[q] = jnp.where(sub == at, roll_rows(pack, at - row), group[q])

            for q in range(4):
                put(source, q, near, pack0, q)
                put(diag, q, near, pack0, 4 + q)
            put(source, bb, far, pack1, 1)
            put(diag, bb, far, pack1, 2)
            put(source, b, far, pack1, 5)
            diag[b] = jnp.where(sub == far, 0.0, diag[b])
            put(source, a, far, pack1, 6)
            put(fixed, ab, near, pack1, 0)
            put(fixed, bb, far, pack1, 3)
            put(fixed, b, far, pack1, 4)
            for at, pack, row in (
                (far + 2 * step, pack1, 7), (far + step, pack2, third), (far, pack2, third + 1)
            ):
                more = jnp.where(sub == at, roll_rows(pack, at - row), more)
            for at, row in ((far + step, third + 2), (far, third + 3)):
                total = jnp.where(sub == at, roll_rows(pack2, at - row), total)
            for q in range(4):
                known = (sub == near) | (sub == far) if q == bb else sub == near
                inverse[q] = jnp.where(known, 1.0 / diag[q], inverse[q])
        for q in range(4):
            hs[q, t] = source[q]
            hd[q, t] = diag[q]
            hi[q, t] = inverse[q]
            fixes[q, t] = fixed[q]
        part[t] = more
        near_total = (diag[0] + diag[1]) + (diag[2] + diag[3]) - 12.0
        total = jnp.where((sub == 0) | (sub == 7), near_total, total)
        here = d2_virtual[...] if t == tiles else d2_ref[t]
        d[t] = jnp.concatenate([here, total], 0)
    for q in range(4):
        pi[q] = 1.0 / d_virtual[q]

    def load_s(q, t):
        return jnp.concatenate([s_ref[q, t], hs[q, t]], 0)

    def after_sweep(sweep):
        if sweep == 2:
            return
        for t in range(count):
            (a, ab, b, bb), (_, _, other_b, other_bb) = sides(t == tiles)
            todo = {}
            if sweep == 0:
                todo = {ab: (sub == 7) | (sub == 1), bb: (sub == 6) | (sub == 0)}
            else:
                todo = {b: sub == 6, other_b: sub == 1}
            for q, mask in todo.items():
                v[q][t, own:] = jnp.where(mask, fixes[q, t], v[q][t, own:])

    smooth(v, load_s, loader(i_ref, hi, pi, tiles), tiles, 16, after_sweep)
    lane, row = lane_ids(rows), row_ids(rows)

    def valid(q, virtual):
        even, odd_red = reds(virtual)
        last = own if q == odd_red ^ 1 else own + 1
        first = rows - 1 if q == even ^ 1 else rows - 2
        return (row <= last) | (row >= first)

    load_d = loader(d_ref, hd, d_virtual, tiles)
    residuals(v, load_s, load_d, tiles, c0, c1, lambda t, r: None, 16, valid)

    even = (lane + row) % 2 == 0
    odd = jnp.logical_not(even)

    def start(t, value):
        source = jnp.concatenate([value[:own], value[own:] + part[t]], 0)
        inverse = 1.0 / d[t]
        s[t] = source
        inv[t] = inverse
        virtual = isinstance(t, int) and t == tiles
        va[t] = jnp.where(odd if virtual else even, source * inverse, 0.0)

    restrict(c0, c1, tiles, rows, start, 16)

    def scan(v, use):
        up, down = roll_up(v[tiles]), roll_down(v[0])
        for t in range(tiles + 1):
            x = v[t]
            up_here, down_next = roll_up(x), roll_down(v[after(t, tiles)])
            north = jnp.where(lane == 0, up, up_here)
            south = jnp.where(lane == LANES - 1, down_next, down)
            use(t, x, (col_prev(x) + col_next(x)) + (north + south))
            up, down = up_here, down_next

    for old, new, mask, other in ((va, vb, odd, even), (vb, va, even, odd), (va, vb, odd, even)):

        def relax(t, x, beside):
            update = other if t == tiles else mask
            new[t] = jnp.where(update, (s[t] + beside) * inv[t], x)

        scan(old, relax)

    def finish(t, x, beside):
        if t < tiles:
            where = slice(t * LANES, (t + 1) * LANES)
            solution_ref[:, where] = x[:own]
            residual_ref[:, where] = (s[t] - (d[t] * x - beside))[:own]

    scan(vb, finish)


VMEM = pl.BlockSpec(memory_space=pltpu.VMEM)
HBM = pl.BlockSpec(memory_space=pltpu.HBM)


def call(kernel, out_shapes, scratch, *args, sems=None, far_in=0, far_out=0):
    scratch = [pltpu.VMEM(x, F32) if isinstance(x, tuple) else x for x in scratch]
    if sems is not None:
        scratch.append(pltpu.SemaphoreType.DMA(sems))
    return pl.pallas_call(
        kernel,
        out_shape=[jax.ShapeDtypeStruct(shape, F32) for shape in out_shapes],
        in_specs=[HBM] * far_in + [VMEM] * (len(args) - far_in),
        out_specs=[HBM] * far_out + [VMEM] * (len(out_shapes) - far_out),
        scratch_shapes=scratch,
        compiler_params=pltpu.CompilerParams(vmem_limit_bytes=40 * 2**20),
    )(*args)


def swapped_with(x, by):
    count = lax.axis_size("lon")
    pairs = [(i, (i + by) % count) for i in range(0, count, 2)]
    return lax.ppermute(x, "lon", pairs + [(b, a) for a, b in pairs])


def swapped_edges(to_mate, to_other):
    from_mate = swapped_with(to_mate, 1)
    return from_mate, swapped_with(to_other, -1)


def body(right_side, texel_weight, seam_flags):
    columns, height = right_side.shape
    half_turn = lax.axis_size("lon") // 2
    tiles, rows = height // 256, columns // 2
    tiles1, rows1 = tiles // 2, rows // 2
    temp = (BATCH, 2, columns, LANES)
    quarters = (4, tiles, rows, LANES)
    quarters1 = (4, tiles1, rows1, LANES)
    pack = (2, tiles, 8, LANES)
    corner = (2, 8, LANES)
    split = (2, 16 * tiles, LANES)
    to_mate, to_other, polar, corner_near, corner_far = call(
        edge_kernel,
        [pack, pack, (2, rows, LANES), corner, corner],
        [(16, height), pltpu.VMEM((32, height), BF16)]
        + [(2, columns, 256), pltpu.VMEM((2, columns, 256), BF16)]
        + [pltpu.VMEM(seam_flags.shape, jnp.int32), split, split]
        + [(2, 2, columns, LANES)] * 2
        + [(tiles, 8, LANES)],
        *[
            pltpu.with_memory_space_constraint(x, pltpu.HBM)
            for x in (right_side, texel_weight, seam_flags)
        ],
        sems=(9,), far_in=3,
    )
    from_mate, from_other = swapped_edges(to_mate, to_other)
    polar = lax.ppermute(
        polar, "lon", [(i, (i + half_turn) % (2 * half_turn)) for i in range(2 * half_turn)]
    )
    corner_near_own = corner_near
    corner_far = swapped_with(corner_far, half_turn - 1)
    corner_near = swapped_with(corner_near, half_turn + 1)
    s, d, inverse, d1, i1, d2 = call(
        bulk_kernel,
        [quarters] * 3 + [quarters1, quarters1, quarters1[1:]],
        [temp, temp, (tiles, 8, LANES), quarters[1:]],
        right_side, texel_weight, seam_flags, corner_near_own,
    )

    def level_scratch(tiles, rows):
        return [(tiles + 1, rows, LANES)] * 6

    def halo_scratch(tiles):
        return [(4, tiles + 1, 8, LANES)] * 3

    pack1 = (2 * (tiles1 + 1) + tiles1 // 2 + 1, 8, LANES)
    r, s1, d1_virtual, d2_virtual, to_mate, to_other = call(
        fine_kernel,
        [quarters, (4, tiles1 + 1, rows1, LANES), (4, rows1, LANES), (rows1, LANES), pack1, pack1],
        level_scratch(tiles, rows + 8)
        + halo_scratch(tiles)
        + [(4, rows, LANES)] * 3
        + [(tiles + 1, rows, LANES), (BATCH, 2, rows, LANES)]
        + level_scratch(tiles1, rows1)
        + [(4, rows1, LANES)]
        + [(tiles1 + 1, rows1, LANES)] * 4,
        s, d, inverse, d1, i1, d2, from_other, from_mate, polar, corner_near, corner_far,
    )
    from_mate, from_other = swapped_edges(to_mate, to_other)
    (fine_residual,) = call(
        merge_kernel, [(columns, height)], [temp, (columns, height)], r,
        sems=(GROUPS,), far_out=1,
    )
    wide = (tiles1 + 1, rows1 + 8, LANES)
    solution_2, residual_2 = call(
        coarse_kernel,
        [(columns // 4, height // 4)] * 2,
        level_scratch(tiles1, rows1 + 8)
        + halo_scratch(tiles1)
        + [(4, rows1, LANES), (tiles1 + 1, 8, LANES), (4, tiles1 + 1, 8, LANES)]
        + [wide] * 5,
        s1, d1, i1, d1_virtual, d2, d2_virtual, from_other, from_mate,
    )
    return fine_residual, solution_2, residual_2


def solution(mesh):
    spec = P(("groups", "lon"), None)
    return jax.shard_map(
        body, mesh=mesh, in_specs=(spec,) * 3, out_specs=(spec,) * 3, check_vma=False
    )
```

```python
import jax
import jax.numpy as jnp
from jax import lax
from jax.experimental import pallas as pl
from jax.experimental.pallas import tpu as pltpu
from jax.sharding import PartitionSpec as P

TILE = 32
SEAM_SCALE = 0.1
LANES = 128
GROUPS = 4
BATCH = 4
F32 = jnp.float32
BF16 = jnp.bfloat16


def loop(count, body, carry=0, unroll=4):
    unroll = min(unroll, count)

    def steps(block, carry):
        for i in range(unroll):
            carry = body(block * unroll + i, carry)
        return carry

    whole = count // unroll
    carry = steps(0, carry) if whole == 1 else lax.fori_loop(0, whole, steps, carry)
    for t in range(whole * unroll, count):
        carry = body(t, carry)
    return carry


def before(t, tiles):
    return (tiles if t == 0 else t - 1) if isinstance(t, int) else jnp.where(t == 0, tiles, t - 1)


def after(t, tiles):
    return (0 if t == tiles else t + 1) if isinstance(t, int) else t + 1


def lane_ids(rows):
    return lax.broadcasted_iota(jnp.int32, (rows, LANES), 1)


def row_ids(rows):
    return lax.broadcasted_iota(jnp.int32, (rows, LANES), 0)


def roll_up(x):
    return pltpu.roll(x, 1, 1)


def roll_down(x):
    return pltpu.roll(x, LANES - 1, 1)


def roll_rows(x, by):
    by %= x.shape[0]
    return x if by == 0 else pltpu.roll(x, by, 0)


def roll_lanes(x, by):
    by %= LANES
    return x if by == 0 else pltpu.roll(x, by, 1)


def col_prev(x):
    return pltpu.roll(x, 1, 0)


def col_next(x):
    return pltpu.roll(x, x.shape[0] - 1, 0)


def inverse_of(x):
    y = pl.reciprocal(x, approx=True)
    return y * (2.0 - x * y)


def selector(shape, rule):
    a = lax.broadcasted_iota(jnp.int32, shape, 0)
    b = lax.broadcasted_iota(jnp.int32, shape, 1)
    return jnp.where(rule(a, b), 1.0, 0.0).astype(BF16)


def splitter():
    return selector((256, 256), lambda a, b: a == 2 * (b % LANES) + b // LANES)


def merger():
    return selector((256, 256), lambda a, b: b == 2 * (a % LANES) + a // LANES)


def virtual_splitter():
    return selector(
        (LANES, 256),
        lambda a, b: a // 2 + jnp.where(a >= 64, 64, 0) + LANES * (a % 2) == b,
    )


def moved(x, matrix, exact=None):
    rows = x.shape[0]
    high = x.astype(BF16)
    low = (x - high.astype(F32)).astype(BF16)
    terms = [high, low] if exact is None else [high, low, exact]
    out = jnp.dot(jnp.concatenate(terms, 0), matrix, preferred_element_type=F32)
    both = out[:rows] + out[rows : 2 * rows]
    return both if exact is None else (both, out[2 * rows :])


def quarters_of(parts, temp):
    count = parts.shape[0] // 2
    temp[0] = parts[:, :LANES]
    temp[1] = parts[:, LANES:]
    return [temp[pr, pl.ds(pc, count, 2), :] for pc in (0, 1) for pr in (0, 1)]


def reds(swapped):
    return (1, 2) if swapped else (0, 3)


def interleaved(group, offset):
    sub = row_ids(8)
    packed = roll_rows(group[0], offset)
    for q in range(1, 4):
        packed = jnp.where(sub // 2 == q, roll_rows(group[q], 2 * q + offset), packed)
    return packed


def edge_packs(source, diag, swapped):
    sub = row_ids(8)
    even, odd = reds(swapped)
    rows = source[0].shape[0]
    packs = []
    for here, first, second, row, step in (
        (slice(rows - 8, rows), even, odd, 6, 1),
        (slice(0, 8), odd, even, 1, -1),
    ):
        gs = [x[here] for x in source]
        gd = [x[here] for x in diag]
        near = gs[first] * inverse_of(gd[first])
        far = roll_rows(gs[second] * inverse_of(gd[second]), step)
        gs[first] = jnp.where(sub == row, near, gs[first])
        gd[first] = jnp.where(sub == row, far, gd[first])
        offset = 2 if row == 6 else 0
        packs.append((interleaved(gs, offset), interleaved(gd, offset)))
    return packs


def unpacked_halo(left, right, swapped):
    sub = row_ids(8)
    even, odd = reds(swapped)
    (al, bl), (ar, br) = left, right
    source, diag = [], []
    for q in range(4):
        s = jnp.where(
            sub >= 6,
            roll_rows(al, 6 - 2 * q),
            jnp.where(sub <= 1, roll_rows(ar, -2 * q), 0.0),
        )
        d = jnp.where(
            sub >= 6,
            roll_rows(bl, 6 - 2 * q),
            jnp.where(sub <= 1, roll_rows(br, -2 * q), 4.0),
        )
        if q == even:
            s = jnp.where(sub == 2, roll_rows(br, 1 - 2 * odd), s)
            d = jnp.where((sub == 2) | (sub == 6), 1.0, d)
        if q == odd:
            s = jnp.where(sub == 5, roll_rows(bl, 5 - 2 * even), s)
            d = jnp.where((sub == 5) | (sub == 1), 1.0, d)
        source.append(s)
        diag.append(d)
    return source, diag


def is_odd():
    return lax.rem(lax.axis_index("lon"), 2) == 1


def chosen(odd, a, b):
    return jnp.where(odd, a, b), jnp.where(odd, b, a)


def store_edges(t, packs, odd, to_mate, to_other):
    right, left = packs
    for i in (0, 1):
        to_mate[i, t], to_other[i, t] = chosen(odd, left[i], right[i])


def placed(rows):
    sub = row_ids(8)
    packed = roll_rows(rows[0][0], -rows[0][1])
    for i, (x, at) in enumerate(rows):
        if i:
            packed = jnp.where(sub == i, roll_rows(x, i - at), packed)
    return packed


def sides(swapped):
    even, odd = reds(swapped)
    return (even, even ^ 1, odd, odd ^ 1), (odd, odd ^ 1, even, even ^ 1)


def state_packs(source, diag, last, first_black, residual, partial, diag2, swapped):
    rows = source[0].shape[0]
    packs = []
    for (a, ab, b, bb), here, near, far, ends in zip(
        sides(swapped),
        (slice(rows - 8, rows), slice(0, 8)),
        (7, 0),
        (6, 1),
        ((4, 5, 6), (3, 2, 1)),
    ):
        s, d, v = ([x[here] for x in group] for group in (source, diag, last))
        part, d2 = partial[here], diag2[here]
        pack0 = [(x, near) for x in s + d]
        pack1 = [
            (first_black[ab][here], near),
            (s[bb] + v[a], far),
            (d[bb], far),
            (first_black[bb][here], far),
            (v[b], far),
            (s[b] - d[b] * v[b] + v[ab], far),
            (residual[a][here] - v[bb], far),
            (part * inverse_of(d2), ends[0]),
        ]
        pack2 = [(part, ends[1]), (part, ends[2]), (d2, ends[1]), (d2, ends[2])]
        packs.append((placed(pack0), placed(pack1), placed(pack2)))
    return packs


def fill_halo(t, from_mate, from_other, odd, swapped, hs, hd, hi):
    al, ar = chosen(odd, from_mate[0, t], from_other[0, t])
    bl, br = chosen(odd, from_mate[1, t], from_other[1, t])
    source, diag = unpacked_halo((al, bl), (ar, br), swapped)
    for q in range(4):
        hs[q, t] = source[q]
        hd[q, t] = diag[q]
        hi[q, t] = inverse_of(diag[q])


def loader(own, halo, virtual, tiles):
    def load(q, t):
        if isinstance(t, int) and t == tiles:
            return jnp.concatenate([virtual[q], halo[q, t]], 0)
        return jnp.concatenate([own[q, t], halo[q, t]], 0)

    return load


def polar_packs(tiles_of):
    lane = lane_ids(tiles_of[0][0].shape[0])
    packs = []
    for pc in (0, 1):
        parts = [*tiles_of[2 * pc], *tiles_of[2 * pc + 1]]
        packed = parts[0]
        for m in range(1, 4):
            mine = (lane + (16 - 32 * m) % LANES) % LANES < 32
            packed = jnp.where(mine, roll_lanes(parts[m], 32 * m), packed)
        packs.append(packed)
    return packs


def polar_unpacked(x, q):
    lane = lane_ids(x.shape[1])
    used = (lane < 16) | (lane >= LANES - 16)
    m = 2 * (q % 2)
    return (
        jnp.where(used, roll_lanes(x[q // 2], 32 * m), 0.0),
        jnp.where(used, roll_lanes(x[q // 2], 32 * (m + 1)), 4.0),
    )


def seam_scales(flags, chunks):
    flag_cols, flag_lats = flags.shape
    flags = jnp.concatenate(
        [flags.astype(F32), jnp.zeros((8 - flag_cols, flag_lats), F32)], 0
    )
    lat = lax.broadcasted_iota(jnp.int32, (8, flag_lats), 1)
    stacked = jnp.concatenate([jnp.where(lat // 8 == c, flags, 0.0) for c in chunks], 0)
    spread = selector((flag_lats, LANES), lambda a, b: a % 8 == b // (TILE // 2))
    spread_flags = jnp.dot(stacked.astype(BF16), spread, preferred_element_type=F32)
    scale = jnp.where(spread_flags > 0.5, SEAM_SCALE, 1.0)
    return scale.reshape(len(chunks), 8, LANES)


def seam_rows(scales, flag_cols, rows):
    size = (rows // flag_cols, LANES)
    return jnp.concatenate(
        [jnp.broadcast_to(scales[i : i + 1], size) for i in range(flag_cols)], 0
    )


def edge_kernel(
    right_ref, weight_ref, flag_ref,
    to_mate, to_other, polar_ref, corner_near, corner_far,
    edge_s, edge_w, end_s, end_w, flags, temp_s, temp_w, temp_p, temp_q, scale_ref, sems,
):
    columns, height = right_ref.shape
    rows, tiles = columns // 2, height // 256
    pairs = [(flag_ref, flags)]
    for i, (src, dst, size) in enumerate(
        ((right_ref, edge_s, 8), (weight_ref, edge_w, 16))
    ):
        pairs.append((src.at[pl.ds(0, size)], dst.at[pl.ds(0, size)]))
        pairs.append((src.at[pl.ds(columns - size, size)], dst.at[pl.ds(size, size)]))
    for src, dst in ((right_ref, end_s), (weight_ref, end_w)):
        for end, start in enumerate((0, height - 256)):
            pairs.append((src.at[:, pl.ds(start, 256)], dst.at[end]))
    copies = [
        pltpu.make_async_copy(src, dst, sems.at[i]) for i, (src, dst) in enumerate(pairs)
    ]
    for copy in copies:
        copy.start()
    odd = is_odd()
    matrix = splitter()
    flag_cols = flag_ref.shape[0]
    copies[0].wait()
    scale_ref[...] = seam_scales(flags[...], range(tiles))
    for copy in copies[1:5]:
        copy.wait()
    sub = row_ids(8)
    lanes = [slice(c * 256, (c + 1) * 256) for c in range(tiles)]
    source, weight = moved(
        jnp.concatenate([edge_s[:, w] for w in lanes], 0),
        matrix,
        jnp.concatenate([edge_w[:, w] for w in lanes], 0),
    )
    weight = weight.reshape(tiles, 32, 256)
    weight = jnp.concatenate([weight[:, :8], weight[:, 24:]], 1).reshape(tiles * 16, 256)
    source = quarters_of(source, temp_s)
    weight = quarters_of(weight, temp_w)
    for c in range(tiles):
        here = slice(c * 8, (c + 1) * 8)
        scales = scale_ref[c]
        scale = jnp.where(sub < 4, scales[:1], scales[flag_cols - 1 : flag_cols])
        diag = [4.0 + w[here] * scale for w in weight]
        store_edges(
            c, edge_packs([x[here] for x in source], diag, False), odd, to_mate, to_other
        )

    for copy in copies[5:]:
        copy.wait()
    mirror = selector((LANES, LANES), lambda a, b: a + b == LANES - 1)
    lane = lane_ids(rows)
    source, weight = moved(
        jnp.concatenate([end_s[0], end_s[1]], 0),
        matrix,
        jnp.concatenate([end_w[0], end_w[1]], 0),
    )
    found = []
    for end, c in enumerate((0, tiles - 1)):
        here = slice(end * columns, (end + 1) * columns)
        scale = seam_rows(scale_ref[c], flag_cols, rows)
        found.append(
            (
                quarters_of(source[here], temp_p.at[end]),
                [4.0 + w * scale for w in quarters_of(weight[here], temp_q.at[end])],
            )
        )
    ends = [
        [jnp.where(lane >= 64, found[1][i][q ^ 1], found[0][i][q ^ 1]) for i in (0, 1)]
        for q in range(4)
    ]
    both = moved(jnp.concatenate(polar_packs(ends), 0), mirror)
    for pc in (0, 1):
        pack = both[pc * rows : (pc + 1) * rows]
        polar_ref[pc] = pack
        corner_near[pc], corner_far[pc] = chosen(odd, pack[:8], pack[rows - 8 :])


def bulk_kernel(
    right_ref, weight_ref, flag_ref, edges_first,
    s_ref, d_ref, i_ref, d1_ref, i1_ref, d2_ref,
    temp_s, temp_d, scale_ref, e_ref,
):
    tiles, rows = s_ref.shape[1], s_ref.shape[2]
    columns = 2 * rows
    matrix = splitter()
    scale_ref[...] = seam_scales(flag_ref[...], range(tiles))
    for start in range(0, tiles, BATCH):
        lanes = [slice((start + i) * 256, (start + i + 1) * 256) for i in range(BATCH)]
        source, weight = moved(
            jnp.concatenate([right_ref[:, w] for w in lanes], 0),
            matrix,
            jnp.concatenate([weight_ref[:, w] for w in lanes], 0),
        )
        for i in range(BATCH):
            c = start + i
            here = slice(i * columns, (i + 1) * columns)
            scale = seam_rows(scale_ref[c], flag_ref.shape[0], rows)
            for q, value in enumerate(quarters_of(source[here], temp_s.at[i])):
                s_ref[q, c] = value
            screen = [w * scale for w in quarters_of(weight[here], temp_d.at[i])]
            e_ref[c] = (screen[0] + screen[1]) + (screen[2] + screen[3])
            for q in range(4):
                diag = 4.0 + screen[q]
                d_ref[q, c] = diag
                i_ref[q, c] = inverse_of(diag)

    def use(c, screen):
        for q in range(4):
            d1_ref[q, c] = 4.0 + screen[q]
            i1_ref[q, c] = inverse_of(4.0 + screen[q])
        d2_ref[c] = 4.0 + ((screen[0] + screen[1]) + (screen[2] + screen[3]))

    split_tiles(lambda t: e_ref[t], tiles // 2, rows, matrix, temp_s, use)


def split_tiles(load, tiles, rows, matrix, temp, use):
    for start in range(0, tiles, BATCH):
        wide = [
            jnp.concatenate([load(2 * c), load(2 * c + 1)], 1)
            for c in range(start, start + BATCH)
        ]
        out = moved(jnp.concatenate(wide, 0), matrix)
        for i in range(BATCH):
            use(start + i, quarters_of(out[i * rows : (i + 1) * rows], temp.at[i, :, :rows]))


def half_sweep(v, load_s, load_i, tiles, red, unroll):
    rows = v[0].shape[1]
    lane = lane_ids(rows)
    y, z, qa, qb = (1, 2, 0, 3) if red else (3, 0, 2, 1)
    col_a, col_b = (col_prev, col_next) if red else (col_next, col_prev)

    def beside_virtual(q):
        ns, we = q ^ 1, q ^ 2
        here = v[ns][tiles]
        if q % 2 == 0:
            lat = jnp.where(lane == 0, roll_up(v[ns][tiles - 1]), roll_up(here))
        else:
            lat = jnp.where(lane == LANES - 1, roll_down(v[ns][0]), roll_down(here))
        cols = v[we][tiles]
        return (here + lat) + (cols + (col_prev if q < 2 else col_next)(cols))

    held = [
        (q, (load_s(q, tiles) + beside_virtual(q)) * load_i(q, tiles)) for q in (y, z)
    ]

    def body(t, carry):
        y_before, z_here = carry
        vy, vz = v[y][t], v[z][t]
        y_here = roll_up(vy)
        z_after = roll_down(v[z][t + 1])
        lat_a = vy + jnp.where(lane == 0, y_before, y_here)
        lat_b = vz + jnp.where(lane == LANES - 1, z_after, z_here)
        v[qa][t] = (load_s(qa, t) + (lat_a + (vz + col_a(vz)))) * load_i(qa, t)
        v[qb][t] = (load_s(qb, t) + (lat_b + (vy + col_b(vy)))) * load_i(qb, t)
        return y_here, z_after

    loop(tiles, body, (roll_up(v[y][tiles]), roll_down(v[z][0])), unroll)
    for q, value in held:
        v[q][tiles] = value


def smooth(v, load_s, load_i, tiles, unroll, after_sweep=None):
    zeros = jnp.zeros(v[0].shape[1:], F32)

    def first(t, _):
        for q in (0, 3):
            v[q][t] = load_s(q, t) * load_i(q, t)
        return 0

    loop(tiles, first, 0, unroll)
    for q in (1, 2):
        v[q][0] = zeros
        v[q][tiles - 1] = zeros
        v[q][tiles] = load_s(q, tiles) * load_i(q, tiles)
        v[3 * (q - 1)][tiles] = zeros
    for sweep, red in enumerate((False, True, False)):
        half_sweep(v, load_s, load_i, tiles, red, unroll)
        if after_sweep is not None:
            after_sweep(sweep)


def residuals(v, load_s, load_d, tiles, c0, c1, keep, unroll, valid=None):
    lane = lane_ids(v[0].shape[1])

    def body(t, carry):
        up1, up3, down0, down2 = carry
        x = [v[q][t] for q in range(4)]
        here1, here3 = roll_up(x[1]), roll_up(x[3])
        next0, next2 = (roll_down(v[q][after(t, tiles)]) for q in (0, 2))
        beside = [
            (x[1] + jnp.where(lane == 0, up1, here1)) + (x[2] + col_prev(x[2])),
            (x[0] + jnp.where(lane == LANES - 1, next0, down0)) + (x[3] + col_prev(x[3])),
            (x[3] + jnp.where(lane == 0, up3, here3)) + (x[0] + col_next(x[0])),
            (x[2] + jnp.where(lane == LANES - 1, next2, down2)) + (x[1] + col_next(x[1])),
        ]
        r = [load_s(q, t) - (load_d(q, t) * x[q] - beside[q]) for q in range(4)]
        keep(t, r)
        if valid is not None:
            virtual = isinstance(t, int) and t == tiles
            r = [jnp.where(valid(q, virtual), r[q], 0.0) for q in range(4)]
        c0[t] = (col_prev(r[2]) + col_next(r[0])) + 3.0 * (r[0] + r[2])
        c1[t] = (col_prev(r[3]) + col_next(r[1])) + 3.0 * (r[1] + r[3])
        return here1, here3, next0, next2

    start = (
        roll_up(v[1][tiles]), roll_up(v[3][tiles]), roll_down(v[0][0]), roll_down(v[2][0])
    )
    body(tiles, loop(tiles, body, start, unroll))


def restrict(c0, c1, tiles, rows, use, unroll):
    lane = lane_ids(rows)

    def body(t, carry):
        up, down = carry
        here, other = c0[t, :rows], c1[t, :rows]
        up_here = roll_up(other)
        down_next = roll_down(c0[after(t, tiles), :rows])
        north = jnp.where(lane == 0, up, up_here)
        south = jnp.where(lane == LANES - 1, down_next, down)
        use(t, ((north + south) + 3.0 * (here + other)) * (1.0 / 16.0))
        return up_here, down_next

    start = roll_up(c1[tiles, :rows]), roll_down(c0[0, :rows])
    body(tiles, loop(tiles, body, start, unroll))


def fine_kernel(
    s_ref, d_ref, i_ref, d1_ref, i1_ref, d2_ref,
    from_other, from_mate, polar_ref, corner_near, corner_far,
    r_ref, s1_ref, d1_virtual, d2_virtual, s2_ref, to_mate, to_other,
    v0, v1, v2, v3, c0, c1, hs, hd, hi, ps, pd, pi, n1, temp,
    w0, w1, w2, w3, e0, e1, pi1, black_even, black_odd, red_even, red_odd,
):
    v = [v0, v1, v2, v3]
    tiles, rows = s_ref.shape[1], s_ref.shape[2]
    sub = row_ids(8)
    odd = is_odd()

    def halo(t, _):
        fill_halo(t, from_mate, from_other, odd, False, hs, hd, hi)
        return 0

    loop(tiles, halo, 0, 8)
    total = -16.0
    for q in range(4):
        own_s, own_d = polar_unpacked(polar_ref, q)
        near_s, near_d = polar_unpacked(corner_near, q)
        far_s, far_d = polar_unpacked(corner_far, q)
        left_s, right_s = chosen(odd, near_s, far_s)
        left_d, right_d = chosen(odd, near_d, far_d)
        total = total + own_d
        ps[q] = own_s
        pd[q] = own_d
        pi[q] = inverse_of(own_d)
        source = jnp.where(sub >= 5, left_s, jnp.where(sub <= 2, right_s, 0.0))
        diag = jnp.where(sub >= 5, left_d, jnp.where(sub <= 2, right_d, 4.0))
        hs[q, tiles] = source
        hd[q, tiles] = diag
        hi[q, tiles] = inverse_of(diag)

    load_s = loader(s_ref, hs, ps, tiles)
    smooth(v, load_s, loader(i_ref, hi, pi, tiles), tiles, 32)

    def keep(t, r):
        if not (isinstance(t, int) and t == tiles):
            for q in range(4):
                r_ref[q, t] = r[q][:rows]

    residuals(v, load_s, loader(d_ref, hd, pd, tiles), tiles, c0, c1, keep, 16)

    def coarse(t, value):
        n1[t] = value

    restrict(c0, c1, tiles, rows, coarse, 16)

    def use(c, source):
        for q in range(4):
            s1_ref[q, c] = source[q]

    tiles1 = tiles // 2
    split_tiles(lambda t: n1[t], tiles1, rows, splitter(), temp, use)
    out = moved(jnp.concatenate([n1[tiles], total], 0), virtual_splitter())
    source = quarters_of(out[:rows], temp.at[0])
    screen = quarters_of(out[rows:], temp.at[1])
    for q in range(4):
        s1_ref[q, tiles1] = source[q]
        d1_virtual[q] = 4.0 + screen[q]
        pi1[q] = inverse_of(4.0 + screen[q])
    d2_virtual[...] = 4.0 + ((screen[0] + screen[1]) + (screen[2] + screen[3]))

    def own(main, virtual):
        return lambda q, t: virtual[q] if isinstance(t, int) and t == tiles1 else main[q, t]

    w = [w0, w1, w2, w3]
    rows1 = rows // 2
    row = row_ids(rows1)
    load_s, load_d = own(s1_ref, s1_ref.at[:, tiles1]), own(d1_ref, d1_virtual)

    def after_sweep(sweep):
        if sweep == 0:
            for t in range(tiles1 + 1):
                even, odd_red = reds(t == tiles1)
                black_even[t] = w[even ^ 1][t]
                black_odd[t] = w[odd_red ^ 1][t]

    smooth(w, load_s, own(i1_ref, pi1), tiles1, 16, after_sweep)

    def valid(q, virtual):
        even, odd_red = reds(virtual)
        first = 1 if q == odd_red ^ 1 else 2
        last = rows1 - 2 if q == even ^ 1 else rows1 - 3
        return (row >= first) & (row <= last)

    def keep_red(t, r):
        even, odd_red = reds(isinstance(t, int) and t == tiles1)
        red_even[t] = r[even]
        red_odd[t] = r[odd_red]

    residuals(w, load_s, load_d, tiles1, e0, e1, keep_red, 16, valid)
    shared = {}

    def edges(t, partial):
        virtual = t == tiles1
        even, odd_red = reds(virtual)
        s2_ref[t] = partial
        packs = state_packs(
            [s1_ref[q, t] for q in range(4)],
            [load_d(q, t) for q in range(4)],
            [w[q][t] for q in range(4)],
            {even ^ 1: black_even[t], odd_red ^ 1: black_odd[t]},
            {even: red_even[t], odd_red: red_odd[t]},
            partial,
            d2_virtual[...] if virtual else d2_ref[t],
            virtual,
        )
        right, left = packs
        count = tiles1 + 1
        for i in (0, 1):
            to_mate[i * count + t], to_other[i * count + t] = chosen(odd, left[i], right[i])
        pair = chosen(odd, left[2], right[2])
        if t % 2 == 0:
            shared[0] = pair
        if t % 2 == 1 or virtual:
            if t % 2 == 1:
                pair = [
                    jnp.where(sub < 4, x, roll_rows(y, 4)) for x, y in zip(shared[0], pair)
                ]
            to_mate[2 * count + t // 2], to_other[2 * count + t // 2] = pair

    restrict(e0, e1, tiles1, rows1, edges, 16)


def merge_kernel(r_ref, out_ref, temp, out_buf, sems):
    tiles = r_ref.shape[1]
    rows = r_ref.shape[2]
    matrix = merger()
    chunk = out_ref.shape[1] // GROUPS
    copies = []
    for group in range(GROUPS):
        for batch in range(tiles // GROUPS // BATCH):
            start = group * (tiles // GROUPS) + batch * BATCH
            both = []
            for i in range(BATCH):
                for pr in (0, 1):
                    for pc in (0, 1):
                        temp[i, pr, pl.ds(pc, rows, 2), :] = r_ref[2 * pc + pr, start + i]
                both.append(jnp.concatenate([temp[i, 0], temp[i, 1]], 1))
            out = moved(jnp.concatenate(both, 0), matrix)
            for i in range(BATCH):
                where = slice((start + i) * 256, (start + i + 1) * 256)
                out_buf[:, where] = out[2 * rows * i : 2 * rows * (i + 1)]
        part = pl.ds(group * chunk, chunk)
        copy = pltpu.make_async_copy(out_buf.at[:, part], out_ref.at[:, part], sems.at[group])
        copy.start()
        copies.append(copy)
    for copy in copies:
        copy.wait()


def coarse_kernel(
    s_ref, d_ref, i_ref, d_virtual, d2_ref, d2_virtual, s2_ref, from_other, from_mate,
    solution_ref, residual_ref,
    v0, v1, v2, v3, c0, c1, hs, hd, hi, part, fixes, s, d, inv, va, vb,
):
    v = [v0, v1, v2, v3]
    tiles, own = d_ref.shape[1], d_ref.shape[2]
    rows = own + 8
    count = tiles + 1
    sub = row_ids(8)
    odd_band = is_odd()
    def rim(x):
        return jnp.where(sub < 4, x[:8], x[own - 8 :])

    for t in range(count):
        places = t, count + t, 2 * count + t // 2
        packs = [chosen(odd_band, from_mate[i], from_other[i]) for i in places]
        source = [jnp.zeros((8, LANES), F32)] * 4
        diag = [jnp.full((8, LANES), 4.0, F32)] * 4
        inverse = [jnp.zeros((8, LANES), F32)] * 4
        fixed = [jnp.zeros((8, LANES), F32)] * 4
        more = jnp.zeros((8, LANES), F32)
        total = jnp.ones((8, LANES), F32)
        third = 4 * (t % 2)
        for side, (a, ab, b, bb) in enumerate(sides(t == tiles)):
            near, far, step = (7, 6, -1) if side == 0 else (0, 1, 1)
            pack0, pack1, pack2 = (pair[side] for pair in packs)

            def put(group, q, at, pack, row):
                group[q] = jnp.where(sub == at, roll_rows(pack, at - row), group[q])

            for q in range(4):
                put(source, q, near, pack0, q)
                put(diag, q, near, pack0, 4 + q)
            put(source, bb, far, pack1, 1)
            put(diag, bb, far, pack1, 2)
            put(source, b, far, pack1, 5)
            diag[b] = jnp.where(sub == far, 0.0, diag[b])
            put(source, a, far, pack1, 6)
            put(fixed, ab, near, pack1, 0)
            put(fixed, bb, far, pack1, 3)
            put(fixed, b, far, pack1, 4)
            for at, pack, row in (
                (far + 2 * step, pack1, 7), (far + step, pack2, third), (far, pack2, third + 1)
            ):
                more = jnp.where(sub == at, roll_rows(pack, at - row), more)
            for at, row in ((far + step, third + 2), (far, third + 3)):
                total = jnp.where(sub == at, roll_rows(pack2, at - row), total)
            for q in range(4):
                known = (sub == near) | (sub == far) if q == bb else sub == near
                inverse[q] = jnp.where(known, inverse_of(diag[q]), inverse[q])
        for q in range(4):
            own_d = rim(d_virtual[q] if t == tiles else d_ref[q, t])
            own_i = inverse_of(own_d) if t == tiles else rim(i_ref[q, t])
            hs[q, t] = jnp.concatenate([source[q], rim(s_ref[q, t])], 0)
            hd[q, t] = jnp.concatenate([diag[q], own_d], 0)
            hi[q, t] = jnp.concatenate([inverse[q], own_i], 0)
            fixes[q, t] = fixed[q]
        part[t] = more
        near_total = (diag[0] + diag[1]) + (diag[2] + diag[3]) - 12.0
        total = jnp.where((sub == 0) | (sub == 7), near_total, total)
        here = d2_virtual[...] if t == tiles else d2_ref[t]
        d[t] = jnp.concatenate([here, total], 0)
    def after_sweep(sweep):
        if sweep == 2:
            return
        for t in range(count):
            (a, ab, b, bb), (_, _, other_b, other_bb) = sides(t == tiles)
            todo = {}
            if sweep == 0:
                todo = {ab: (sub == 7) | (sub == 1), bb: (sub == 6) | (sub == 0)}
            else:
                todo = {b: sub == 6, other_b: sub == 1}
            for q, mask in todo.items():
                v[q][t, :8] = jnp.where(mask, fixes[q, t], v[q][t, :8])

    def of(ref):
        return lambda q, t: ref[q, t]

    smooth(v, of(hs), of(hi), tiles, 16, after_sweep)
    row = row_ids(16)

    def valid(q, virtual):
        even, odd_red = reds(virtual)
        after_band = 0 if q == odd_red ^ 1 else 1
        before_band = 7 if q == even ^ 1 else 6
        first = 8 if q == odd_red ^ 1 else 9
        last = 15 if q == even ^ 1 else 14
        return (row <= after_band) | ((row >= before_band) & (row <= first)) | (row >= last)

    residuals(v, of(hs), of(hd), tiles, c0, c1, lambda t, r: None, 16, valid)

    lane, row = lane_ids(rows), row_ids(rows)
    even = (lane + row) % 2 == 0
    odd = jnp.logical_not(even)

    def start(t, value):
        ends = value[8:]
        source = jnp.concatenate(
            [
                s2_ref[t, :8] + jnp.where(sub < 4, ends, 0.0),
                s2_ref[t, own - 8 :] + jnp.where(sub >= 4, ends, 0.0),
                value[:8] + part[t],
            ],
            0,
        )
        inverse = inverse_of(d[t])
        s[t] = source
        inv[t] = inverse
        virtual = isinstance(t, int) and t == tiles
        va[t] = jnp.where(odd if virtual else even, source * inverse, 0.0)

    restrict(c0, c1, tiles, 16, start, 16)

    def scan(v, use):
        up, down = roll_up(v[tiles]), roll_down(v[0])
        for t in range(tiles + 1):
            x = v[t]
            up_here, down_next = roll_up(x), roll_down(v[after(t, tiles)])
            north = jnp.where(lane == 0, up, up_here)
            south = jnp.where(lane == LANES - 1, down_next, down)
            use(t, x, (col_prev(x) + col_next(x)) + (north + south))
            up, down = up_here, down_next

    for old, new, mask, other in ((va, vb, odd, even), (vb, va, even, odd), (va, vb, odd, even)):

        def relax(t, x, beside):
            update = other if t == tiles else mask
            new[t] = jnp.where(update, (s[t] + beside) * inv[t], x)

        scan(old, relax)

    def finish(t, x, beside):
        if t < tiles:
            where = slice(t * LANES, (t + 1) * LANES)
            solution_ref[:, where] = x[:own]
            residual_ref[:, where] = (s[t] - (d[t] * x - beside))[:own]

    scan(vb, finish)


VMEM = pl.BlockSpec(memory_space=pltpu.VMEM)
HBM = pl.BlockSpec(memory_space=pltpu.HBM)


def call(kernel, out_shapes, scratch, *args, sems=None, far_in=0, far_out=0):
    scratch = [pltpu.VMEM(x, F32) if isinstance(x, tuple) else x for x in scratch]
    if sems is not None:
        scratch.append(pltpu.SemaphoreType.DMA(sems))
    return pl.pallas_call(
        kernel,
        out_shape=[jax.ShapeDtypeStruct(shape, F32) for shape in out_shapes],
        in_specs=[HBM] * far_in + [VMEM] * (len(args) - far_in),
        out_specs=[HBM] * far_out + [VMEM] * (len(out_shapes) - far_out),
        scratch_shapes=scratch,
        compiler_params=pltpu.CompilerParams(vmem_limit_bytes=40 * 2**20),
    )(*args)


def swapped_with(x, by):
    count = lax.axis_size("lon")
    pairs = [(i, (i + by) % count) for i in range(0, count, 2)]
    return lax.ppermute(x, "lon", pairs + [(b, a) for a, b in pairs])


def swapped_edges(to_mate, to_other):
    from_mate = swapped_with(to_mate, 1)
    return from_mate, swapped_with(to_other, -1)


def body(right_side, texel_weight, seam_flags):
    columns, height = right_side.shape
    half_turn = lax.axis_size("lon") // 2
    tiles, rows = height // 256, columns // 2
    tiles1, rows1 = tiles // 2, rows // 2
    temp = (BATCH, 2, columns, LANES)
    quarters = (4, tiles, rows, LANES)
    quarters1 = (4, tiles1, rows1, LANES)
    pack = (2, tiles, 8, LANES)
    corner = (2, 8, LANES)
    split = (2, 16 * tiles, LANES)
    to_mate, to_other, polar, corner_near, corner_far = call(
        edge_kernel,
        [pack, pack, (2, rows, LANES), corner, corner],
        [(16, height), pltpu.VMEM((32, height), BF16)]
        + [(2, columns, 256), pltpu.VMEM((2, columns, 256), BF16)]
        + [pltpu.VMEM(seam_flags.shape, jnp.int32), split, split]
        + [(2, 2, columns, LANES)] * 2
        + [(tiles, 8, LANES)],
        *[
            pltpu.with_memory_space_constraint(x, pltpu.HBM)
            for x in (right_side, texel_weight, seam_flags)
        ],
        sems=(9,), far_in=3,
    )
    from_mate, from_other = swapped_edges(to_mate, to_other)
    polar = lax.ppermute(
        polar, "lon", [(i, (i + half_turn) % (2 * half_turn)) for i in range(2 * half_turn)]
    )
    corner_near_own = corner_near
    corner_far = swapped_with(corner_far, half_turn - 1)
    corner_near = swapped_with(corner_near, half_turn + 1)
    s, d, inverse, d1, i1, d2 = call(
        bulk_kernel,
        [quarters] * 3 + [quarters1, quarters1, quarters1[1:]],
        [temp, temp, (tiles, 8, LANES), quarters[1:]],
        right_side, texel_weight, seam_flags, corner_near_own,
    )

    def level_scratch(tiles, rows):
        return [(tiles + 1, rows, LANES)] * 6

    def halo_scratch(tiles):
        return [(4, tiles + 1, 8, LANES)] * 3

    pack1 = (2 * (tiles1 + 1) + tiles1 // 2 + 1, 8, LANES)
    r, s1, d1_virtual, d2_virtual, s2_own, to_mate, to_other = call(
        fine_kernel,
        [quarters, (4, tiles1 + 1, rows1, LANES), (4, rows1, LANES), (rows1, LANES)]
        + [(tiles1 + 1, rows1, LANES), pack1, pack1],
        level_scratch(tiles, rows + 8)
        + halo_scratch(tiles)
        + [(4, rows, LANES)] * 3
        + [(tiles + 1, rows, LANES), (BATCH, 2, rows, LANES)]
        + level_scratch(tiles1, rows1)
        + [(4, rows1, LANES)]
        + [(tiles1 + 1, rows1, LANES)] * 4,
        s, d, inverse, d1, i1, d2, from_other, from_mate, polar, corner_near, corner_far,
    )
    from_mate, from_other = swapped_edges(to_mate, to_other)
    (fine_residual,) = call(
        merge_kernel, [(columns, height)], [temp, (columns, height)], r,
        sems=(GROUPS,), far_out=1,
    )
    wide = (tiles1 + 1, rows1 + 8, LANES)
    solution_2, residual_2 = call(
        coarse_kernel,
        [(columns // 4, height // 4)] * 2,
        level_scratch(tiles1, 16)
        + [(4, tiles1 + 1, 16, LANES)] * 3
        + [(tiles1 + 1, 8, LANES), (4, tiles1 + 1, 8, LANES)]
        + [wide] * 5,
        s1, d1, i1, d1_virtual, d2, d2_virtual, s2_own, from_other, from_mate,
    )
    return fine_residual, solution_2, residual_2


def solution(mesh):
    spec = P(("groups", "lon"), None)
    return jax.shard_map(
        body, mesh=mesh, in_specs=(spec,) * 3, out_specs=(spec,) * 3, check_vma=False
    )
```

```python
import jax
import jax.numpy as jnp
from jax import lax
from jax.experimental import pallas as pl
from jax.experimental.pallas import tpu as pltpu
from jax.sharding import PartitionSpec as P

TILE = 32
SEAM_SCALE = 0.1
LANES = 128
GROUPS = 4
BATCH = 4
F32 = jnp.float32
BF16 = jnp.bfloat16


def loop(count, body, carry=0, unroll=4):
    unroll = min(unroll, count)

    def steps(block, carry):
        for i in range(unroll):
            carry = body(block * unroll + i, carry)
        return carry

    whole = count // unroll
    carry = steps(0, carry) if whole == 1 else lax.fori_loop(0, whole, steps, carry)
    for t in range(whole * unroll, count):
        carry = body(t, carry)
    return carry


def before(t, tiles):
    return (tiles if t == 0 else t - 1) if isinstance(t, int) else jnp.where(t == 0, tiles, t - 1)


def after(t, tiles):
    return (0 if t == tiles else t + 1) if isinstance(t, int) else t + 1


def lane_ids(rows):
    return lax.broadcasted_iota(jnp.int32, (rows, LANES), 1)


def row_ids(rows):
    return lax.broadcasted_iota(jnp.int32, (rows, LANES), 0)


def roll_up(x):
    return pltpu.roll(x, 1, 1)


def roll_down(x):
    return pltpu.roll(x, LANES - 1, 1)


def roll_rows(x, by):
    by %= x.shape[0]
    return x if by == 0 else pltpu.roll(x, by, 0)


def roll_lanes(x, by):
    by %= LANES
    return x if by == 0 else pltpu.roll(x, by, 1)


def col_prev(x):
    return pltpu.roll(x, 1, 0)


def col_next(x):
    return pltpu.roll(x, x.shape[0] - 1, 0)


def inverse_of(x):
    return 1.0 / x


def selector(shape, rule):
    a = lax.broadcasted_iota(jnp.int32, shape, 0)
    b = lax.broadcasted_iota(jnp.int32, shape, 1)
    return jnp.where(rule(a, b), 1.0, 0.0).astype(BF16)


def splitter():
    return selector((256, 256), lambda a, b: a == 2 * (b % LANES) + b // LANES)


def merger():
    return selector((256, 256), lambda a, b: b == 2 * (a % LANES) + a // LANES)


def virtual_splitter():
    return selector(
        (LANES, 256),
        lambda a, b: a // 2 + jnp.where(a >= 64, 64, 0) + LANES * (a % 2) == b,
    )


def moved(x, matrix, exact=None):
    rows = x.shape[0]
    high = x.astype(BF16)
    low = (x - high.astype(F32)).astype(BF16)
    terms = [high, low] if exact is None else [high, low, exact]
    out = jnp.dot(jnp.concatenate(terms, 0), matrix, preferred_element_type=F32)
    both = out[:rows] + out[rows : 2 * rows]
    return both if exact is None else (both, out[2 * rows :])


def quarters_of(parts, temp):
    count = parts.shape[0] // 2
    temp[0] = parts[:, :LANES]
    temp[1] = parts[:, LANES:]
    return [temp[pr, pl.ds(pc, count, 2), :] for pc in (0, 1) for pr in (0, 1)]


def reds(swapped):
    return (1, 2) if swapped else (0, 3)


def interleaved(group, offset):
    sub = row_ids(8)
    packed = roll_rows(group[0], offset)
    for q in range(1, 4):
        packed = jnp.where(sub // 2 == q, roll_rows(group[q], 2 * q + offset), packed)
    return packed


def edge_packs(source, diag, swapped):
    sub = row_ids(8)
    even, odd = reds(swapped)
    rows = source[0].shape[0]
    packs = []
    for here, first, second, row, step in (
        (slice(rows - 8, rows), even, odd, 6, 1),
        (slice(0, 8), odd, even, 1, -1),
    ):
        gs = [x[here] for x in source]
        gd = [x[here] for x in diag]
        near = gs[first] * inverse_of(gd[first])
        far = roll_rows(gs[second] * inverse_of(gd[second]), step)
        gs[first] = jnp.where(sub == row, near, gs[first])
        gd[first] = jnp.where(sub == row, far, gd[first])
        offset = 2 if row == 6 else 0
        packs.append((interleaved(gs, offset), interleaved(gd, offset)))
    return packs


def unpacked_halo(left, right, swapped):
    sub = row_ids(8)
    even, odd = reds(swapped)
    (al, bl), (ar, br) = left, right
    source, diag = [], []
    for q in range(4):
        s = jnp.where(
            sub >= 6,
            roll_rows(al, 6 - 2 * q),
            jnp.where(sub <= 1, roll_rows(ar, -2 * q), 0.0),
        )
        d = jnp.where(
            sub >= 6,
            roll_rows(bl, 6 - 2 * q),
            jnp.where(sub <= 1, roll_rows(br, -2 * q), 4.0),
        )
        if q == even:
            s = jnp.where(sub == 2, roll_rows(br, 1 - 2 * odd), s)
            d = jnp.where((sub == 2) | (sub == 6), 1.0, d)
        if q == odd:
            s = jnp.where(sub == 5, roll_rows(bl, 5 - 2 * even), s)
            d = jnp.where((sub == 5) | (sub == 1), 1.0, d)
        source.append(s)
        diag.append(d)
    return source, diag


def is_odd():
    return lax.rem(lax.axis_index("lon"), 2) == 1


def chosen(odd, a, b):
    return jnp.where(odd, a, b), jnp.where(odd, b, a)


def store_edges(t, packs, odd, to_mate, to_other):
    right, left = packs
    for i in (0, 1):
        to_mate[i, t], to_other[i, t] = chosen(odd, left[i], right[i])


def placed(rows):
    sub = row_ids(8)
    packed = roll_rows(rows[0][0], -rows[0][1])
    for i, (x, at) in enumerate(rows):
        if i:
            packed = jnp.where(sub == i, roll_rows(x, i - at), packed)
    return packed


def sides(swapped):
    even, odd = reds(swapped)
    return (even, even ^ 1, odd, odd ^ 1), (odd, odd ^ 1, even, even ^ 1)


def state_packs(source, diag, last, first_black, residual, partial, diag2, swapped):
    rows = source[0].shape[0]
    packs = []
    for (a, ab, b, bb), here, near, far, ends in zip(
        sides(swapped),
        (slice(rows - 8, rows), slice(0, 8)),
        (7, 0),
        (6, 1),
        ((4, 5, 6), (3, 2, 1)),
    ):
        s, d, v = ([x[here] for x in group] for group in (source, diag, last))
        part, d2 = partial[here], diag2[here]
        pack0 = [(x, near) for x in s + d]
        pack1 = [
            (first_black[ab][here], near),
            (s[bb] + v[a], far),
            (d[bb], far),
            (first_black[bb][here], far),
            (v[b], far),
            (s[b] - d[b] * v[b] + v[ab], far),
            (residual[a][here] - v[bb], far),
            (part * inverse_of(d2), ends[0]),
        ]
        pack2 = [(part, ends[1]), (part, ends[2]), (d2, ends[1]), (d2, ends[2])]
        packs.append((placed(pack0), placed(pack1), placed(pack2)))
    return packs


def fill_halo(t, from_mate, from_other, odd, swapped, hs, hd, hi):
    al, ar = chosen(odd, from_mate[0, t], from_other[0, t])
    bl, br = chosen(odd, from_mate[1, t], from_other[1, t])
    source, diag = unpacked_halo((al, bl), (ar, br), swapped)
    for q in range(4):
        hs[q, t] = source[q]
        hd[q, t] = diag[q]
        hi[q, t] = inverse_of(diag[q])


def loader(own, halo, virtual, tiles):
    def load(q, t):
        if isinstance(t, int) and t == tiles:
            return jnp.concatenate([virtual[q], halo[q, t]], 0)
        return jnp.concatenate([own[q, t], halo[q, t]], 0)

    return load


def polar_packs(tiles_of):
    lane = lane_ids(tiles_of[0][0].shape[0])
    packs = []
    for pc in (0, 1):
        parts = [*tiles_of[2 * pc], *tiles_of[2 * pc + 1]]
        packed = parts[0]
        for m in range(1, 4):
            mine = (lane + (16 - 32 * m) % LANES) % LANES < 32
            packed = jnp.where(mine, roll_lanes(parts[m], 32 * m), packed)
        packs.append(packed)
    return packs


def polar_unpacked(x, q):
    lane = lane_ids(x.shape[1])
    used = (lane < 16) | (lane >= LANES - 16)
    m = 2 * (q % 2)
    return (
        jnp.where(used, roll_lanes(x[q // 2], 32 * m), 0.0),
        jnp.where(used, roll_lanes(x[q // 2], 32 * (m + 1)), 4.0),
    )


def seam_scales(flags, chunks):
    flag_cols, flag_lats = flags.shape
    flags = jnp.concatenate(
        [flags.astype(F32), jnp.zeros((8 - flag_cols, flag_lats), F32)], 0
    )
    lat = lax.broadcasted_iota(jnp.int32, (8, flag_lats), 1)
    stacked = jnp.concatenate([jnp.where(lat // 8 == c, flags, 0.0) for c in chunks], 0)
    spread = selector((flag_lats, LANES), lambda a, b: a % 8 == b // (TILE // 2))
    spread_flags = jnp.dot(stacked.astype(BF16), spread, preferred_element_type=F32)
    scale = jnp.where(spread_flags > 0.5, SEAM_SCALE, 1.0)
    return scale.reshape(len(chunks), 8, LANES)


def seam_rows(scales, flag_cols, rows):
    size = (rows // flag_cols, LANES)
    return jnp.concatenate(
        [jnp.broadcast_to(scales[i : i + 1], size) for i in range(flag_cols)], 0
    )


def edge_kernel(
    right_ref, weight_ref, flag_ref,
    to_mate, to_other, corner_ref,
    edge_s, edge_w, flags, temp_s, temp_w, scale_ref, sems,
):
    columns, height = right_ref.shape
    tiles = height // 256
    pairs = [(flag_ref, flags)]
    for i, (src, dst, size) in enumerate(
        ((right_ref, edge_s, 8), (weight_ref, edge_w, 16))
    ):
        pairs.append((src.at[pl.ds(0, size)], dst.at[pl.ds(0, size)]))
        pairs.append((src.at[pl.ds(columns - size, size)], dst.at[pl.ds(size, size)]))
    copies = [
        pltpu.make_async_copy(src, dst, sems.at[i]) for i, (src, dst) in enumerate(pairs)
    ]
    for copy in copies:
        copy.start()
    odd = is_odd()
    matrix = splitter()
    flag_cols = flag_ref.shape[0]
    copies[0].wait()
    scale_ref[...] = seam_scales(flags[...], range(tiles))
    for copy in copies[1:]:
        copy.wait()
    sub = row_ids(8)
    lanes = [slice(c * 256, (c + 1) * 256) for c in range(tiles)]
    source, weight = moved(
        jnp.concatenate([edge_s[:, w] for w in lanes], 0),
        matrix,
        jnp.concatenate([edge_w[:, w] for w in lanes], 0),
    )
    weight = weight.reshape(tiles, 32, 256)
    weight = jnp.concatenate([weight[:, :8], weight[:, 24:]], 1).reshape(tiles * 16, 256)
    source = quarters_of(source, temp_s)
    weight = quarters_of(weight, temp_w)
    found = []
    for c in range(tiles):
        here = slice(c * 8, (c + 1) * 8)
        scales = scale_ref[c]
        scale = jnp.where(sub < 4, scales[:1], scales[flag_cols - 1 : flag_cols])
        pair = [x[here] for x in source], [4.0 + w[here] * scale for w in weight]
        store_edges(c, edge_packs(*pair, False), odd, to_mate, to_other)
        if c in (0, tiles - 1):
            found.append(pair)
    both = mirrored_ends(*found)
    for pc in (0, 1):
        corner = both[8 * pc : 8 * (pc + 1)]
        corner_ref[pc] = corner


def mirrored_ends(first, last):
    mirror = selector((LANES, LANES), lambda a, b: a + b == LANES - 1)
    lane = lane_ids(first[0][0].shape[0])
    ends = [
        [jnp.where(lane >= 64, last[i][q ^ 1], first[i][q ^ 1]) for i in (0, 1)]
        for q in range(4)
    ]
    return moved(jnp.concatenate(polar_packs(ends), 0), mirror)


def polar_kernel(right_ref, weight_ref, flag_ref, edges_first, polar_ref, temp_s, temp_w):
    columns, height = right_ref.shape
    rows, tiles = columns // 2, height // 256
    scales = seam_scales(flag_ref[...], (0, tiles - 1))
    lanes = slice(0, 256), slice(height - 256, height)
    source, weight = moved(
        jnp.concatenate([right_ref[:, w] for w in lanes], 0),
        splitter(),
        jnp.concatenate([weight_ref[:, w] for w in lanes], 0),
    )
    found = []
    for end in (0, 1):
        here = slice(end * columns, (end + 1) * columns)
        scale = seam_rows(scales[end], flag_ref.shape[0], rows)
        found.append(
            (
                quarters_of(source[here], temp_s.at[end]),
                [4.0 + w * scale for w in quarters_of(weight[here], temp_w.at[end])],
            )
        )
    both = mirrored_ends(*found)
    for pc in (0, 1):
        polar_ref[pc] = both[pc * rows : (pc + 1) * rows]


def bulk_kernel(
    right_ref, weight_ref, flag_ref, polar_first,
    s_ref, d_ref, i_ref, d1_ref, i1_ref, d2_ref,
    temp_s, temp_d, scale_ref, e_ref,
):
    tiles, rows = s_ref.shape[1], s_ref.shape[2]
    columns = 2 * rows
    matrix = splitter()
    scale_ref[...] = seam_scales(flag_ref[...], range(tiles))
    for start in range(0, tiles, BATCH):
        lanes = [slice((start + i) * 256, (start + i + 1) * 256) for i in range(BATCH)]
        source, weight = moved(
            jnp.concatenate([right_ref[:, w] for w in lanes], 0),
            matrix,
            jnp.concatenate([weight_ref[:, w] for w in lanes], 0),
        )
        for i in range(BATCH):
            c = start + i
            here = slice(i * columns, (i + 1) * columns)
            scale = seam_rows(scale_ref[c], flag_ref.shape[0], rows)
            for q, value in enumerate(quarters_of(source[here], temp_s.at[i])):
                s_ref[q, c] = value
            screen = [w * scale for w in quarters_of(weight[here], temp_d.at[i])]
            e_ref[c] = (screen[0] + screen[1]) + (screen[2] + screen[3])
            for q in range(4):
                diag = 4.0 + screen[q]
                d_ref[q, c] = diag
                i_ref[q, c] = inverse_of(diag)

    def use(c, screen):
        for q in range(4):
            d1_ref[q, c] = 4.0 + screen[q]
            i1_ref[q, c] = inverse_of(4.0 + screen[q])
        d2_ref[c] = 4.0 + ((screen[0] + screen[1]) + (screen[2] + screen[3]))

    split_tiles(lambda t: e_ref[t], tiles // 2, rows, matrix, temp_s, use)


def split_tiles(load, tiles, rows, matrix, temp, use):
    for start in range(0, tiles, BATCH):
        wide = [
            jnp.concatenate([load(2 * c), load(2 * c + 1)], 1)
            for c in range(start, start + BATCH)
        ]
        out = moved(jnp.concatenate(wide, 0), matrix)
        for i in range(BATCH):
            use(start + i, quarters_of(out[i * rows : (i + 1) * rows], temp.at[i, :, :rows]))


def half_sweep(v, load_s, load_i, tiles, red, unroll, left=None):
    rows = v[0].shape[1]
    lane = lane_ids(rows)
    y, z, qa, qb = (1, 2, 0, 3) if red else (3, 0, 2, 1)
    col_a, col_b = (col_prev, col_next) if red else (col_next, col_prev)

    def beside_virtual(q):
        ns, we = q ^ 1, q ^ 2
        here = v[ns][tiles]
        if q % 2 == 0:
            lat = jnp.where(lane == 0, roll_up(v[ns][tiles - 1]), roll_up(here))
        else:
            lat = jnp.where(lane == LANES - 1, roll_down(v[ns][0]), roll_down(here))
        cols = v[we][tiles]
        return (here + lat) + (cols + (col_prev if q < 2 else col_next)(cols))

    held = [
        (q, (load_s(q, tiles) + beside_virtual(q)) * load_i(q, tiles)) for q in (y, z)
    ]

    def body(t, carry):
        y_before, z_here = carry
        vy, vz = v[y][t], v[z][t]
        y_here = roll_up(vy)
        z_after = roll_down(v[z][t + 1])
        lat_a = vy + jnp.where(lane == 0, y_before, y_here)
        lat_b = vz + jnp.where(lane == LANES - 1, z_after, z_here)
        all_a = load_s(qa, t) + (lat_a + (vz + col_a(vz)))
        all_b = load_s(qb, t) + (lat_b + (vy + col_b(vy)))
        new_a, new_b = all_a * load_i(qa, t), all_b * load_i(qb, t)
        v[qa][t], v[qb][t] = new_a, new_b
        if left is not None:
            load_d, rest = left
            rest[qa][t] = all_a - load_d(qa, t) * new_a
            rest[qb][t] = all_b - load_d(qb, t) * new_b
        return y_here, z_after

    loop(tiles, body, (roll_up(v[y][tiles]), roll_down(v[z][0])), unroll)
    for q, value in held:
        v[q][tiles] = value


def smooth(v, load_s, load_i, tiles, unroll, left, after_sweep=None):
    zeros = jnp.zeros(v[0].shape[1:], F32)

    def first(t, _):
        for q in (0, 3):
            v[q][t] = load_s(q, t) * load_i(q, t)
        return 0

    loop(tiles, first, 0, unroll)
    for q in (1, 2):
        v[q][0] = zeros
        v[q][tiles - 1] = zeros
        v[q][tiles] = load_s(q, tiles) * load_i(q, tiles)
        v[3 * (q - 1)][tiles] = zeros
    for sweep, red in enumerate((False, True, False)):
        half_sweep(v, load_s, load_i, tiles, red, unroll, left if sweep == 2 else None)
        if after_sweep is not None:
            after_sweep(sweep)


def residuals(v, load_s, left, tiles, c0, c1, keep, unroll, valid=None):
    lane = lane_ids(v[0].shape[1])
    load_d, rest = left

    def use(t, r):
        keep(t, r)
        if valid is not None:
            virtual = isinstance(t, int) and t == tiles
            r = [jnp.where(valid(q, virtual), r[q], 0.0) for q in range(4)]
        c0[t] = (col_prev(r[2]) + col_next(r[0])) + 3.0 * (r[0] + r[2])
        c1[t] = (col_prev(r[3]) + col_next(r[1])) + 3.0 * (r[1] + r[3])

    def north(q, t):
        return jnp.where(lane == 0, roll_up(v[q][before(t, tiles)]), roll_up(v[q][t]))

    def south(q, t):
        return jnp.where(
            lane == LANES - 1, roll_down(v[q][after(t, tiles)]), roll_down(v[q][t])
        )

    def full(t):
        x = [v[q][t] for q in range(4)]
        beside = [
            (x[1] + north(1, t)) + (x[2] + col_prev(x[2])),
            (x[0] + south(0, t)) + (x[3] + col_prev(x[3])),
            (x[3] + north(3, t)) + (x[0] + col_next(x[0])),
            (x[2] + south(2, t)) + (x[1] + col_next(x[1])),
        ]
        use(t, [load_s(q, t) - (load_d(q, t) * x[q] - beside[q]) for q in range(4)])

    def body(i, carry):
        t = i + 1
        up, down = carry
        x = [v[q][t] for q in range(4)]
        up_here, down_next = roll_up(x[1]), roll_down(v[2][t + 1])
        beside0 = (x[1] + jnp.where(lane == 0, up, up_here)) + (x[2] + col_prev(x[2]))
        beside3 = (x[2] + jnp.where(lane == LANES - 1, down_next, down)) + (
            x[1] + col_next(x[1])
        )
        r0 = load_s(0, t) - (load_d(0, t) * x[0] - beside0)
        r3 = load_s(3, t) - (load_d(3, t) * x[3] - beside3)
        use(t, [r0, rest[1][t], rest[2][t], r3])
        return up_here, down_next

    full(0)
    loop(tiles - 2, body, (roll_up(v[1][0]), roll_down(v[2][1])), unroll)
    full(tiles - 1)
    full(tiles)


def restrict(c0, c1, tiles, rows, use, unroll):
    lane = lane_ids(rows)

    def body(t, carry):
        up, down = carry
        here, other = c0[t, :rows], c1[t, :rows]
        up_here = roll_up(other)
        down_next = roll_down(c0[after(t, tiles), :rows])
        north = jnp.where(lane == 0, up, up_here)
        south = jnp.where(lane == LANES - 1, down_next, down)
        use(t, ((north + south) + 3.0 * (here + other)) * (1.0 / 16.0))
        return up_here, down_next

    start = roll_up(c1[tiles, :rows]), roll_down(c0[0, :rows])
    body(tiles, loop(tiles, body, start, unroll))


def fine_kernel(
    s_ref, d_ref, i_ref, d1_ref, i1_ref, d2_ref,
    from_other, from_mate, polar_ref, corner_near, corner_far,
    r_ref, s1_ref, d1_virtual, d2_virtual, s2_ref, to_mate, to_other,
    v0, v1, v2, v3, c0, c1, hs, hd, hi, ps, pd, pi, n1, temp,
    w0, w1, w2, w3, e0, e1, pi1, black_even, black_odd, red_even, red_odd,
    rest1, rest2, part1, part2,
):
    v = [v0, v1, v2, v3]
    tiles, rows = s_ref.shape[1], s_ref.shape[2]
    sub = row_ids(8)
    odd = is_odd()

    def halo(t, _):
        fill_halo(t, from_mate, from_other, odd, False, hs, hd, hi)
        return 0

    loop(tiles, halo, 0, 8)
    total = -16.0
    for q in range(4):
        own_s, own_d = polar_unpacked(polar_ref, q)
        near_s, near_d = polar_unpacked(corner_near, q)
        far_s, far_d = polar_unpacked(corner_far, q)
        left_s, right_s = chosen(odd, near_s, far_s)
        left_d, right_d = chosen(odd, near_d, far_d)
        total = total + own_d
        ps[q] = own_s
        pd[q] = own_d
        pi[q] = inverse_of(own_d)
        source = jnp.where(sub >= 5, left_s, jnp.where(sub <= 2, right_s, 0.0))
        diag = jnp.where(sub >= 5, left_d, jnp.where(sub <= 2, right_d, 4.0))
        hs[q, tiles] = source
        hd[q, tiles] = diag
        hi[q, tiles] = inverse_of(diag)

    load_s = loader(s_ref, hs, ps, tiles)
    left = loader(d_ref, hd, pd, tiles), {1: rest1, 2: rest2}
    smooth(v, load_s, loader(i_ref, hi, pi, tiles), tiles, 32, left)

    def keep(t, r):
        if not (isinstance(t, int) and t == tiles):
            for q in range(4):
                r_ref[q, t] = r[q][:rows]

    residuals(v, load_s, left, tiles, c0, c1, keep, 15)

    def coarse(t, value):
        n1[t] = value

    restrict(c0, c1, tiles, rows, coarse, 16)

    def use(c, source):
        for q in range(4):
            s1_ref[q, c] = source[q]

    tiles1 = tiles // 2
    split_tiles(lambda t: n1[t], tiles1, rows, splitter(), temp, use)
    out = moved(jnp.concatenate([n1[tiles], total], 0), virtual_splitter())
    source = quarters_of(out[:rows], temp.at[0])
    screen = quarters_of(out[rows:], temp.at[1])
    for q in range(4):
        s1_ref[q, tiles1] = source[q]
        d1_virtual[q] = 4.0 + screen[q]
        pi1[q] = inverse_of(4.0 + screen[q])
    d2_virtual[...] = 4.0 + ((screen[0] + screen[1]) + (screen[2] + screen[3]))

    def own(main, virtual):
        return lambda q, t: virtual[q] if isinstance(t, int) and t == tiles1 else main[q, t]

    w = [w0, w1, w2, w3]
    rows1 = rows // 2
    row = row_ids(rows1)
    load_s, load_d = own(s1_ref, s1_ref.at[:, tiles1]), own(d1_ref, d1_virtual)

    def after_sweep(sweep):
        if sweep == 0:
            for t in range(tiles1 + 1):
                even, odd_red = reds(t == tiles1)
                black_even[t] = w[even ^ 1][t]
                black_odd[t] = w[odd_red ^ 1][t]

    left = load_d, {1: part1, 2: part2}
    smooth(w, load_s, own(i1_ref, pi1), tiles1, 16, left, after_sweep)

    def valid(q, virtual):
        even, odd_red = reds(virtual)
        first = 1 if q == odd_red ^ 1 else 2
        last = rows1 - 2 if q == even ^ 1 else rows1 - 3
        return (row >= first) & (row <= last)

    def keep_red(t, r):
        even, odd_red = reds(isinstance(t, int) and t == tiles1)
        red_even[t] = r[even]
        red_odd[t] = r[odd_red]

    residuals(w, load_s, left, tiles1, e0, e1, keep_red, 16, valid)
    shared = {}

    def edges(t, partial):
        virtual = t == tiles1
        even, odd_red = reds(virtual)
        s2_ref[t] = partial
        packs = state_packs(
            [s1_ref[q, t] for q in range(4)],
            [load_d(q, t) for q in range(4)],
            [w[q][t] for q in range(4)],
            {even ^ 1: black_even[t], odd_red ^ 1: black_odd[t]},
            {even: red_even[t], odd_red: red_odd[t]},
            partial,
            d2_virtual[...] if virtual else d2_ref[t],
            virtual,
        )
        right, left = packs
        count = tiles1 + 1
        for i in (0, 1):
            to_mate[i * count + t], to_other[i * count + t] = chosen(odd, left[i], right[i])
        pair = chosen(odd, left[2], right[2])
        if t % 2 == 0:
            shared[0] = pair
        if t % 2 == 1 or virtual:
            if t % 2 == 1:
                pair = [
                    jnp.where(sub < 4, x, roll_rows(y, 4)) for x, y in zip(shared[0], pair)
                ]
            to_mate[2 * count + t // 2], to_other[2 * count + t // 2] = pair

    restrict(e0, e1, tiles1, rows1, edges, 16)


def merge_kernel(r_ref, out_ref, temp, out_buf, sems):
    tiles = r_ref.shape[1]
    rows = r_ref.shape[2]
    matrix = merger()
    chunk = out_ref.shape[1] // GROUPS
    copies = []
    for group in range(GROUPS):
        for batch in range(tiles // GROUPS // BATCH):
            start = group * (tiles // GROUPS) + batch * BATCH
            both = []
            for i in range(BATCH):
                for pr in (0, 1):
                    for pc in (0, 1):
                        temp[i, pr, pl.ds(pc, rows, 2), :] = r_ref[2 * pc + pr, start + i]
                both.append(jnp.concatenate([temp[i, 0], temp[i, 1]], 1))
            out = moved(jnp.concatenate(both, 0), matrix)
            for i in range(BATCH):
                where = slice((start + i) * 256, (start + i + 1) * 256)
                out_buf[:, where] = out[2 * rows * i : 2 * rows * (i + 1)]
        part = pl.ds(group * chunk, chunk)
        copy = pltpu.make_async_copy(out_buf.at[:, part], out_ref.at[:, part], sems.at[group])
        copy.start()
        copies.append(copy)
    for copy in copies:
        copy.wait()


def coarse_kernel(
    s_ref, d_ref, i_ref, d_virtual, d2_ref, d2_virtual, s2_ref, from_other, from_mate,
    solution_ref, residual_ref,
    v0, v1, v2, v3, c0, c1, hs, hd, hi, part, fixes, rest1, rest2, s, d, inv, va, vb,
):
    v = [v0, v1, v2, v3]
    tiles, own = d_ref.shape[1], d_ref.shape[2]
    rows = own + 8
    count = tiles + 1
    sub = row_ids(8)
    odd_band = is_odd()
    def rim(x):
        return jnp.where(sub < 4, x[:8], x[own - 8 :])

    for t in range(count):
        places = t, count + t, 2 * count + t // 2
        packs = [chosen(odd_band, from_mate[i], from_other[i]) for i in places]
        source = [jnp.zeros((8, LANES), F32)] * 4
        diag = [jnp.full((8, LANES), 4.0, F32)] * 4
        inverse = [jnp.zeros((8, LANES), F32)] * 4
        fixed = [jnp.zeros((8, LANES), F32)] * 4
        more = jnp.zeros((8, LANES), F32)
        total = jnp.ones((8, LANES), F32)
        third = 4 * (t % 2)
        for side, (a, ab, b, bb) in enumerate(sides(t == tiles)):
            near, far, step = (7, 6, -1) if side == 0 else (0, 1, 1)
            pack0, pack1, pack2 = (pair[side] for pair in packs)

            def put(group, q, at, pack, row):
                group[q] = jnp.where(sub == at, roll_rows(pack, at - row), group[q])

            for q in range(4):
                put(source, q, near, pack0, q)
                put(diag, q, near, pack0, 4 + q)
            put(source, bb, far, pack1, 1)
            put(diag, bb, far, pack1, 2)
            put(source, b, far, pack1, 5)
            diag[b] = jnp.where(sub == far, 0.0, diag[b])
            put(source, a, far, pack1, 6)
            put(fixed, ab, near, pack1, 0)
            put(fixed, bb, far, pack1, 3)
            put(fixed, b, far, pack1, 4)
            for at, pack, row in (
                (far + 2 * step, pack1, 7), (far + step, pack2, third), (far, pack2, third + 1)
            ):
                more = jnp.where(sub == at, roll_rows(pack, at - row), more)
            for at, row in ((far + step, third + 2), (far, third + 3)):
                total = jnp.where(sub == at, roll_rows(pack2, at - row), total)
            for q in range(4):
                known = (sub == near) | (sub == far) if q == bb else sub == near
                inverse[q] = jnp.where(known, inverse_of(diag[q]), inverse[q])
        for q in range(4):
            own_d = rim(d_virtual[q] if t == tiles else d_ref[q, t])
            own_i = inverse_of(own_d) if t == tiles else rim(i_ref[q, t])
            hs[q, t] = jnp.concatenate([source[q], rim(s_ref[q, t])], 0)
            hd[q, t] = jnp.concatenate([diag[q], own_d], 0)
            hi[q, t] = jnp.concatenate([inverse[q], own_i], 0)
            fixes[q, t] = fixed[q]
        part[t] = more
        near_total = (diag[0] + diag[1]) + (diag[2] + diag[3]) - 12.0
        total = jnp.where((sub == 0) | (sub == 7), near_total, total)
        here = d2_virtual[...] if t == tiles else d2_ref[t]
        d[t] = jnp.concatenate([here, total], 0)
    def after_sweep(sweep):
        if sweep == 2:
            return
        for t in range(count):
            (a, ab, b, bb), (_, _, other_b, other_bb) = sides(t == tiles)
            todo = {}
            if sweep == 0:
                todo = {ab: (sub == 7) | (sub == 1), bb: (sub == 6) | (sub == 0)}
            else:
                todo = {b: sub == 6, other_b: sub == 1}
            for q, mask in todo.items():
                v[q][t, :8] = jnp.where(mask, fixes[q, t], v[q][t, :8])

    def of(ref):
        return lambda q, t: ref[q, t]

    left = of(hd), {1: rest1, 2: rest2}
    smooth(v, of(hs), of(hi), tiles, 16, left, after_sweep)
    row = row_ids(16)

    def valid(q, virtual):
        even, odd_red = reds(virtual)
        after_band = 0 if q == odd_red ^ 1 else 1
        before_band = 7 if q == even ^ 1 else 6
        first = 8 if q == odd_red ^ 1 else 9
        last = 15 if q == even ^ 1 else 14
        return (row <= after_band) | ((row >= before_band) & (row <= first)) | (row >= last)

    residuals(v, of(hs), left, tiles, c0, c1, lambda t, r: None, 16, valid)

    lane, row = lane_ids(rows), row_ids(rows)
    even = (lane + row) % 2 == 0
    odd = jnp.logical_not(even)

    def start(t, value):
        ends = value[8:]
        source = jnp.concatenate(
            [
                s2_ref[t, :8] + jnp.where(sub < 4, ends, 0.0),
                s2_ref[t, own - 8 :] + jnp.where(sub >= 4, ends, 0.0),
                value[:8] + part[t],
            ],
            0,
        )
        inverse = inverse_of(d[t])
        s[t] = source
        inv[t] = inverse
        virtual = isinstance(t, int) and t == tiles
        va[t] = jnp.where(odd if virtual else even, source * inverse, 0.0)

    restrict(c0, c1, tiles, 16, start, 16)

    def scan(v, use):
        up, down = roll_up(v[tiles]), roll_down(v[0])
        for t in range(tiles + 1):
            x = v[t]
            up_here, down_next = roll_up(x), roll_down(v[after(t, tiles)])
            north = jnp.where(lane == 0, up, up_here)
            south = jnp.where(lane == LANES - 1, down_next, down)
            use(t, x, (col_prev(x) + col_next(x)) + (north + south))
            up, down = up_here, down_next

    for old, new, mask, other in ((va, vb, odd, even), (vb, va, even, odd), (va, vb, odd, even)):

        def relax(t, x, beside):
            update = other if t == tiles else mask
            new[t] = jnp.where(update, (s[t] + beside) * inv[t], x)

        scan(old, relax)

    def finish(t, x, beside):
        if t < tiles:
            where = slice(t * LANES, (t + 1) * LANES)
            solution_ref[:, where] = x[:own]
            residual_ref[:, where] = (s[t] - (d[t] * x - beside))[:own]

    scan(vb, finish)


VMEM = pl.BlockSpec(memory_space=pltpu.VMEM)
HBM = pl.BlockSpec(memory_space=pltpu.HBM)


def call(kernel, out_shapes, scratch, *args, sems=None, far_in=0, far_out=0):
    scratch = [pltpu.VMEM(x, F32) if isinstance(x, tuple) else x for x in scratch]
    if sems is not None:
        scratch.append(pltpu.SemaphoreType.DMA(sems))
    return pl.pallas_call(
        kernel,
        out_shape=[jax.ShapeDtypeStruct(shape, F32) for shape in out_shapes],
        in_specs=[HBM] * far_in + [VMEM] * (len(args) - far_in),
        out_specs=[HBM] * far_out + [VMEM] * (len(out_shapes) - far_out),
        scratch_shapes=scratch,
        compiler_params=pltpu.CompilerParams(vmem_limit_bytes=40 * 2**20),
    )(*args)


def swapped_with(x, by):
    count = lax.axis_size("lon")
    pairs = [(i, (i + by) % count) for i in range(0, count, 2)]
    return lax.ppermute(x, "lon", pairs + [(b, a) for a, b in pairs])


def swapped_edges(to_mate, to_other):
    from_mate = swapped_with(to_mate, 1)
    return from_mate, swapped_with(to_other, -1)


def body(right_side, texel_weight, seam_flags):
    columns, height = right_side.shape
    half_turn = lax.axis_size("lon") // 2
    tiles, rows = height // 256, columns // 2
    tiles1, rows1 = tiles // 2, rows // 2
    temp = (BATCH, 2, columns, LANES)
    quarters = (4, tiles, rows, LANES)
    quarters1 = (4, tiles1, rows1, LANES)
    split = (2, 16 * tiles, LANES)
    to_mate, to_other, corner = call(
        edge_kernel,
        [(2, tiles, 8, LANES), (2, tiles, 8, LANES), (2, 8, LANES)],
        [(16, height), pltpu.VMEM((32, height), BF16)]
        + [pltpu.VMEM(seam_flags.shape, jnp.int32), split, split, (tiles, 8, LANES)],
        *[
            pltpu.with_memory_space_constraint(x, pltpu.HBM)
            for x in (right_side, texel_weight, seam_flags)
        ],
        sems=(5,), far_in=3,
    )
    from_mate, from_other = swapped_edges(to_mate, to_other)
    corner_far = swapped_with(corner, half_turn - 1)
    corner_near = swapped_with(corner, half_turn + 1)
    ends = (2, 2, columns, LANES)
    (polar_own,) = call(
        polar_kernel, [(2, rows, LANES)], [ends, ends],
        right_side, texel_weight, seam_flags, corner,
    )
    polar = lax.ppermute(
        polar_own, "lon", [(i, (i + half_turn) % (2 * half_turn)) for i in range(2 * half_turn)]
    )
    s, d, inverse, d1, i1, d2 = call(
        bulk_kernel,
        [quarters] * 3 + [quarters1, quarters1, quarters1[1:]],
        [temp, temp, (tiles, 8, LANES), quarters[1:]],
        right_side, texel_weight, seam_flags, polar_own,
    )

    def level_scratch(tiles, rows):
        return [(tiles + 1, rows, LANES)] * 6

    def halo_scratch(tiles):
        return [(4, tiles + 1, 8, LANES)] * 3

    pack1 = (2 * (tiles1 + 1) + tiles1 // 2 + 1, 8, LANES)
    r, s1, d1_virtual, d2_virtual, s2_own, to_mate, to_other = call(
        fine_kernel,
        [quarters, (4, tiles1 + 1, rows1, LANES), (4, rows1, LANES), (rows1, LANES)]
        + [(tiles1 + 1, rows1, LANES), pack1, pack1],
        level_scratch(tiles, rows + 8)
        + halo_scratch(tiles)
        + [(4, rows, LANES)] * 3
        + [(tiles + 1, rows, LANES), (BATCH, 2, rows, LANES)]
        + level_scratch(tiles1, rows1)
        + [(4, rows1, LANES)]
        + [(tiles1 + 1, rows1, LANES)] * 4
        + [(tiles, rows + 8, LANES)] * 2
        + [(tiles1, rows1, LANES)] * 2,
        s, d, inverse, d1, i1, d2, from_other, from_mate, polar, corner_near, corner_far,
    )
    from_mate, from_other = swapped_edges(to_mate, to_other)
    (fine_residual,) = call(
        merge_kernel, [(columns, height)], [temp, (columns, height)], r,
        sems=(GROUPS,), far_out=1,
    )
    wide = (tiles1 + 1, rows1 + 8, LANES)
    solution_2, residual_2 = call(
        coarse_kernel,
        [(columns // 4, height // 4)] * 2,
        level_scratch(tiles1, 16)
        + [(4, tiles1 + 1, 16, LANES)] * 3
        + [(tiles1 + 1, 8, LANES), (4, tiles1 + 1, 8, LANES)]
        + [(tiles1, 16, LANES)] * 2
        + [wide] * 5,
        s1, d1, i1, d1_virtual, d2, d2_virtual, s2_own, from_other, from_mate,
    )
    return fine_residual, solution_2, residual_2


def solution(mesh):
    spec = P(("groups", "lon"), None)
    return jax.shard_map(
        body, mesh=mesh, in_specs=(spec,) * 3, out_specs=(spec,) * 3, check_vma=False
    )
```

```python
import jax
import jax.numpy as jnp
from jax import lax
from jax.experimental import pallas as pl
from jax.experimental.pallas import tpu as pltpu
from jax.sharding import PartitionSpec as P

TILE = 32
SEAM_SCALE = 0.1
LANES = 128
GROUPS = 4
BATCH = 4
F32 = jnp.float32
BF16 = jnp.bfloat16


def loop(count, body, carry=0, unroll=4):
    unroll = min(unroll, count)

    def steps(block, carry):
        for i in range(unroll):
            carry = body(block * unroll + i, carry)
        return carry

    whole = count // unroll
    carry = steps(0, carry) if whole == 1 else lax.fori_loop(0, whole, steps, carry)
    for t in range(whole * unroll, count):
        carry = body(t, carry)
    return carry


def before(t, tiles):
    return (tiles if t == 0 else t - 1) if isinstance(t, int) else jnp.where(t == 0, tiles, t - 1)


def after(t, tiles):
    return (0 if t == tiles else t + 1) if isinstance(t, int) else t + 1


def lane_ids(rows):
    return lax.broadcasted_iota(jnp.int32, (rows, LANES), 1)


def row_ids(rows):
    return lax.broadcasted_iota(jnp.int32, (rows, LANES), 0)


def roll_up(x):
    return pltpu.roll(x, 1, 1)


def roll_down(x):
    return pltpu.roll(x, LANES - 1, 1)


def roll_rows(x, by):
    by %= x.shape[0]
    return x if by == 0 else pltpu.roll(x, by, 0)


def roll_lanes(x, by):
    by %= LANES
    return x if by == 0 else pltpu.roll(x, by, 1)


def col_prev(x):
    return pltpu.roll(x, 1, 0)


def col_next(x):
    return pltpu.roll(x, x.shape[0] - 1, 0)


def inverse_of(x):
    return 1.0 / x


def selector(shape, rule):
    a = lax.broadcasted_iota(jnp.int32, shape, 0)
    b = lax.broadcasted_iota(jnp.int32, shape, 1)
    return jnp.where(rule(a, b), 1.0, 0.0).astype(BF16)


def splitter():
    return selector((256, 256), lambda a, b: a == 2 * (b % LANES) + b // LANES)


def merger():
    return selector((256, 256), lambda a, b: b == 2 * (a % LANES) + a // LANES)


def virtual_splitter():
    return selector(
        (LANES, 256),
        lambda a, b: a // 2 + jnp.where(a >= 64, 64, 0) + LANES * (a % 2) == b,
    )


def moved(x, matrix, exact=None):
    rows = x.shape[0]
    high = x.astype(BF16)
    low = (x - high.astype(F32)).astype(BF16)
    terms = [high, low] if exact is None else [high, low, exact]
    out = jnp.dot(jnp.concatenate(terms, 0), matrix, preferred_element_type=F32)
    both = out[:rows] + out[rows : 2 * rows]
    return both if exact is None else (both, out[2 * rows :])


def quarters_of(parts, temp):
    count = parts.shape[0] // 2
    temp[0] = parts[:, :LANES]
    temp[1] = parts[:, LANES:]
    return [temp[pr, pl.ds(pc, count, 2), :] for pc in (0, 1) for pr in (0, 1)]


def reds(swapped):
    return (1, 2) if swapped else (0, 3)


def interleaved(group, offset):
    sub = row_ids(8)
    packed = roll_rows(group[0], offset)
    for q in range(1, 4):
        packed = jnp.where(sub // 2 == q, roll_rows(group[q], 2 * q + offset), packed)
    return packed


def edge_packs(source, diag, swapped):
    sub = row_ids(8)
    even, odd = reds(swapped)
    rows = source[0].shape[0]
    packs = []
    for here, first, second, row, step in (
        (slice(rows - 8, rows), even, odd, 6, 1),
        (slice(0, 8), odd, even, 1, -1),
    ):
        gs = [x[here] for x in source]
        gd = [x[here] for x in diag]
        near = gs[first] * inverse_of(gd[first])
        far = roll_rows(gs[second] * inverse_of(gd[second]), step)
        gs[first] = jnp.where(sub == row, near, gs[first])
        gd[first] = jnp.where(sub == row, far, gd[first])
        offset = 2 if row == 6 else 0
        packs.append((interleaved(gs, offset), interleaved(gd, offset)))
    return packs


def unpacked_halo(left, right, swapped):
    sub = row_ids(8)
    even, odd = reds(swapped)
    (al, bl), (ar, br) = left, right
    source, diag = [], []
    for q in range(4):
        s = jnp.where(
            sub >= 6,
            roll_rows(al, 6 - 2 * q),
            jnp.where(sub <= 1, roll_rows(ar, -2 * q), 0.0),
        )
        d = jnp.where(
            sub >= 6,
            roll_rows(bl, 6 - 2 * q),
            jnp.where(sub <= 1, roll_rows(br, -2 * q), 4.0),
        )
        if q == even:
            s = jnp.where(sub == 2, roll_rows(br, 1 - 2 * odd), s)
            d = jnp.where((sub == 2) | (sub == 6), 1.0, d)
        if q == odd:
            s = jnp.where(sub == 5, roll_rows(bl, 5 - 2 * even), s)
            d = jnp.where((sub == 5) | (sub == 1), 1.0, d)
        source.append(s)
        diag.append(d)
    return source, diag


def is_odd():
    return lax.rem(lax.axis_index("lon"), 2) == 1


def chosen(odd, a, b):
    return jnp.where(odd, a, b), jnp.where(odd, b, a)


def store_edges(t, packs, odd, to_mate, to_other):
    right, left = packs
    for i in (0, 1):
        to_mate[i, t], to_other[i, t] = chosen(odd, left[i], right[i])


def placed(rows):
    sub = row_ids(8)
    packed = roll_rows(rows[0][0], -rows[0][1])
    for i, (x, at) in enumerate(rows):
        if i:
            packed = jnp.where(sub == i, roll_rows(x, i - at), packed)
    return packed


def sides(swapped):
    even, odd = reds(swapped)
    return (even, even ^ 1, odd, odd ^ 1), (odd, odd ^ 1, even, even ^ 1)


def state_packs(source, diag, last, first_black, residual, partial, diag2, swapped):
    rows = source[0].shape[0]
    packs = []
    for (a, ab, b, bb), here, near, far, ends in zip(
        sides(swapped),
        (slice(rows - 8, rows), slice(0, 8)),
        (7, 0),
        (6, 1),
        ((4, 5, 6), (3, 2, 1)),
    ):
        s, d, v = ([x[here] for x in group] for group in (source, diag, last))
        part, d2 = partial[here], diag2[here]
        pack0 = [(x, near) for x in s + d]
        pack1 = [
            (first_black[ab][here], near),
            (s[bb] + v[a], far),
            (d[bb], far),
            (first_black[bb][here], far),
            (v[b], far),
            (s[b] - d[b] * v[b] + v[ab], far),
            (residual[a][here] - v[bb], far),
            (part * inverse_of(d2), ends[0]),
        ]
        pack2 = [(part, ends[1]), (part, ends[2]), (d2, ends[1]), (d2, ends[2])]
        packs.append((placed(pack0), placed(pack1), placed(pack2)))
    return packs


def fill_halo(t, from_mate, from_other, odd, swapped, hs, hd, hi):
    al, ar = chosen(odd, from_mate[0, t], from_other[0, t])
    bl, br = chosen(odd, from_mate[1, t], from_other[1, t])
    source, diag = unpacked_halo((al, bl), (ar, br), swapped)
    for q in range(4):
        hs[q, t] = source[q]
        hd[q, t] = diag[q]
        hi[q, t] = inverse_of(diag[q])


def loader(own, halo, virtual, tiles):
    def load(q, t):
        if isinstance(t, int) and t == tiles:
            return jnp.concatenate([virtual[q], halo[q, t]], 0)
        return jnp.concatenate([own[q, t], halo[q, t]], 0)

    return load


def polar_packs(tiles_of):
    lane = lane_ids(tiles_of[0][0].shape[0])
    packs = []
    for pc in (0, 1):
        parts = [*tiles_of[2 * pc], *tiles_of[2 * pc + 1]]
        packed = parts[0]
        for m in range(1, 4):
            mine = (lane + (16 - 32 * m) % LANES) % LANES < 32
            packed = jnp.where(mine, roll_lanes(parts[m], 32 * m), packed)
        packs.append(packed)
    return packs


def polar_unpacked(x, q):
    lane = lane_ids(x.shape[1])
    used = (lane < 16) | (lane >= LANES - 16)
    m = 2 * (q % 2)
    return (
        jnp.where(used, roll_lanes(x[q // 2], 32 * m), 0.0),
        jnp.where(used, roll_lanes(x[q // 2], 32 * (m + 1)), 4.0),
    )


def seam_scales(flags, chunks):
    flag_cols, flag_lats = flags.shape
    flags = jnp.concatenate(
        [flags.astype(F32), jnp.zeros((8 - flag_cols, flag_lats), F32)], 0
    )
    lat = lax.broadcasted_iota(jnp.int32, (8, flag_lats), 1)
    stacked = jnp.concatenate([jnp.where(lat // 8 == c, flags, 0.0) for c in chunks], 0)
    spread = selector((flag_lats, LANES), lambda a, b: a % 8 == b // (TILE // 2))
    spread_flags = jnp.dot(stacked.astype(BF16), spread, preferred_element_type=F32)
    scale = jnp.where(spread_flags > 0.5, SEAM_SCALE, 1.0)
    return scale.reshape(len(chunks), 8, LANES)


def seam_rows(scales, flag_cols, rows):
    size = (rows // flag_cols, LANES)
    return jnp.concatenate(
        [jnp.broadcast_to(scales[i : i + 1], size) for i in range(flag_cols)], 0
    )


def edge_kernel(
    right_ref, weight_ref, flag_ref,
    to_mate, to_other, corner_ref,
    edge_s, edge_w, flags, temp_s, temp_w, scale_ref, sems,
):
    columns, height = right_ref.shape
    tiles = height // 256
    pairs = [(flag_ref, flags)]
    for i, (src, dst, size) in enumerate(
        ((right_ref, edge_s, 8), (weight_ref, edge_w, 16))
    ):
        pairs.append((src.at[pl.ds(0, size)], dst.at[pl.ds(0, size)]))
        pairs.append((src.at[pl.ds(columns - size, size)], dst.at[pl.ds(size, size)]))
    copies = [
        pltpu.make_async_copy(src, dst, sems.at[i]) for i, (src, dst) in enumerate(pairs)
    ]
    for copy in copies:
        copy.start()
    odd = is_odd()
    matrix = splitter()
    flag_cols = flag_ref.shape[0]
    copies[0].wait()
    scale_ref[...] = seam_scales(flags[...], range(tiles))
    for copy in copies[1:]:
        copy.wait()
    sub = row_ids(8)
    lanes = [slice(c * 256, (c + 1) * 256) for c in range(tiles)]
    source, weight = moved(
        jnp.concatenate([edge_s[:, w] for w in lanes], 0),
        matrix,
        jnp.concatenate([edge_w[:, w] for w in lanes], 0),
    )
    weight = weight.reshape(tiles, 32, 256)
    weight = jnp.concatenate([weight[:, :8], weight[:, 24:]], 1).reshape(tiles * 16, 256)
    source = quarters_of(source, temp_s)
    weight = quarters_of(weight, temp_w)
    found = []
    for c in range(tiles):
        here = slice(c * 8, (c + 1) * 8)
        scales = scale_ref[c]
        scale = jnp.where(sub < 4, scales[:1], scales[flag_cols - 1 : flag_cols])
        pair = [x[here] for x in source], [4.0 + w[here] * scale for w in weight]
        store_edges(c, edge_packs(*pair, False), odd, to_mate, to_other)
        if c in (0, tiles - 1):
            found.append(pair)
    both = mirrored_ends(*found)
    for pc in (0, 1):
        corner = both[8 * pc : 8 * (pc + 1)]
        corner_ref[pc] = corner


def mirrored_ends(first, last):
    mirror = selector((LANES, LANES), lambda a, b: a + b == LANES - 1)
    lane = lane_ids(first[0][0].shape[0])
    ends = [
        [jnp.where(lane >= 64, last[i][q ^ 1], first[i][q ^ 1]) for i in (0, 1)]
        for q in range(4)
    ]
    return moved(jnp.concatenate(polar_packs(ends), 0), mirror)


def polar_kernel(right_ref, weight_ref, flag_ref, edges_first, polar_ref, temp_s, temp_w):
    columns, height = right_ref.shape
    rows, tiles = columns // 2, height // 256
    scales = seam_scales(flag_ref[...], (0, tiles - 1))
    lanes = slice(0, 256), slice(height - 256, height)
    source, weight = moved(
        jnp.concatenate([right_ref[:, w] for w in lanes], 0),
        splitter(),
        jnp.concatenate([weight_ref[:, w] for w in lanes], 0),
    )
    found = []
    for end in (0, 1):
        here = slice(end * columns, (end + 1) * columns)
        scale = seam_rows(scales[end], flag_ref.shape[0], rows)
        found.append(
            (
                quarters_of(source[here], temp_s.at[end]),
                [4.0 + w * scale for w in quarters_of(weight[here], temp_w.at[end])],
            )
        )
    both = mirrored_ends(*found)
    for pc in (0, 1):
        polar_ref[pc] = both[pc * rows : (pc + 1) * rows]


def bulk_kernel(
    right_ref, weight_ref, flag_ref, polar_first,
    s_ref, d_ref, i_ref, d1_ref, i1_ref, d2_ref,
    temp, scale_ref, e_ref, split_temp,
):
    tiles, columns = s_ref.shape[1], s_ref.shape[2]
    rows = columns // 2
    matrix = splitter()
    scale_ref[...] = seam_scales(flag_ref[...], range(tiles))
    for start in range(0, tiles, BATCH):
        lanes = [slice((start + i) * 256, (start + i + 1) * 256) for i in range(BATCH)]
        source, weight = moved(
            jnp.concatenate([right_ref[:, w] for w in lanes], 0),
            matrix,
            jnp.concatenate([weight_ref[:, w] for w in lanes], 0),
        )
        for i in range(BATCH):
            c = start + i
            here = slice(i * columns, (i + 1) * columns)
            scale = seam_rows(scale_ref[c], flag_ref.shape[0], columns)
            screens = []
            for pr in (0, 1):
                half = slice(pr * LANES, (pr + 1) * LANES)
                screen = weight[here, half] * scale
                diag = 4.0 + screen
                s_ref[pr, c] = source[here, half]
                d_ref[pr, c] = diag
                i_ref[pr, c] = 1.0 / diag
                screens.append(screen)
            temp[i] = screens[0] + screens[1]
            e_ref[c] = temp[i, pl.ds(0, rows, 2), :] + temp[i, pl.ds(1, rows, 2), :]

    def use(c, screen):
        for q in range(4):
            d1_ref[q, c] = 4.0 + screen[q]
            i1_ref[q, c] = inverse_of(4.0 + screen[q])
        d2_ref[c] = 4.0 + ((screen[0] + screen[1]) + (screen[2] + screen[3]))

    split_tiles(lambda t: e_ref[t], tiles // 2, rows, matrix, split_temp, use)


def split_tiles(load, tiles, rows, matrix, temp, use):
    for start in range(0, tiles, BATCH):
        wide = [
            jnp.concatenate([load(2 * c), load(2 * c + 1)], 1)
            for c in range(start, start + BATCH)
        ]
        out = moved(jnp.concatenate(wide, 0), matrix)
        for i in range(BATCH):
            use(start + i, quarters_of(out[i * rows : (i + 1) * rows], temp.at[i, :, :rows]))


def half_sweep(v, load_s, load_i, tiles, red, unroll, left=None):
    rows = v[0].shape[1]
    lane = lane_ids(rows)
    y, z, qa, qb = (1, 2, 0, 3) if red else (3, 0, 2, 1)
    col_a, col_b = (col_prev, col_next) if red else (col_next, col_prev)

    def beside_virtual(q):
        ns, we = q ^ 1, q ^ 2
        here = v[ns][tiles]
        if q % 2 == 0:
            lat = jnp.where(lane == 0, roll_up(v[ns][tiles - 1]), roll_up(here))
        else:
            lat = jnp.where(lane == LANES - 1, roll_down(v[ns][0]), roll_down(here))
        cols = v[we][tiles]
        return (here + lat) + (cols + (col_prev if q < 2 else col_next)(cols))

    held = [
        (q, (load_s(q, tiles) + beside_virtual(q)) * load_i(q, tiles)) for q in (y, z)
    ]

    def body(t, carry):
        y_before, z_here = carry
        vy, vz = v[y][t], v[z][t]
        y_here = roll_up(vy)
        z_after = roll_down(v[z][t + 1])
        lat_a = vy + jnp.where(lane == 0, y_before, y_here)
        lat_b = vz + jnp.where(lane == LANES - 1, z_after, z_here)
        all_a = load_s(qa, t) + (lat_a + (vz + col_a(vz)))
        all_b = load_s(qb, t) + (lat_b + (vy + col_b(vy)))
        new_a, new_b = all_a * load_i(qa, t), all_b * load_i(qb, t)
        v[qa][t], v[qb][t] = new_a, new_b
        if left is not None:
            load_d, rest = left
            rest[qa][t] = all_a - load_d(qa, t) * new_a
            rest[qb][t] = all_b - load_d(qb, t) * new_b
        return y_here, z_after

    loop(tiles, body, (roll_up(v[y][tiles]), roll_down(v[z][0])), unroll)
    for q, value in held:
        v[q][tiles] = value


def smooth(v, load_s, load_i, tiles, unroll, left, after_sweep=None):
    zeros = jnp.zeros(v[0].shape[1:], F32)

    def first(t, _):
        for q in (0, 3):
            v[q][t] = load_s(q, t) * load_i(q, t)
        return 0

    loop(tiles, first, 0, unroll)
    for q in (1, 2):
        v[q][0] = zeros
        v[q][tiles - 1] = zeros
        v[q][tiles] = load_s(q, tiles) * load_i(q, tiles)
        v[3 * (q - 1)][tiles] = zeros
    for sweep, red in enumerate((False, True, False)):
        half_sweep(v, load_s, load_i, tiles, red, unroll, left if sweep == 2 else None)
        if after_sweep is not None:
            after_sweep(sweep)


def residuals(v, load_s, left, tiles, c0, c1, keep, unroll, valid=None):
    lane = lane_ids(v[0].shape[1])
    load_d, rest = left

    def use(t, r):
        keep(t, r)
        if valid is not None:
            virtual = isinstance(t, int) and t == tiles
            r = [jnp.where(valid(q, virtual), r[q], 0.0) for q in range(4)]
        c0[t] = (col_prev(r[2]) + col_next(r[0])) + 3.0 * (r[0] + r[2])
        c1[t] = (col_prev(r[3]) + col_next(r[1])) + 3.0 * (r[1] + r[3])

    def north(q, t):
        return jnp.where(lane == 0, roll_up(v[q][before(t, tiles)]), roll_up(v[q][t]))

    def south(q, t):
        return jnp.where(
            lane == LANES - 1, roll_down(v[q][after(t, tiles)]), roll_down(v[q][t])
        )

    def full(t):
        x = [v[q][t] for q in range(4)]
        beside = [
            (x[1] + north(1, t)) + (x[2] + col_prev(x[2])),
            (x[0] + south(0, t)) + (x[3] + col_prev(x[3])),
            (x[3] + north(3, t)) + (x[0] + col_next(x[0])),
            (x[2] + south(2, t)) + (x[1] + col_next(x[1])),
        ]
        use(t, [load_s(q, t) - (load_d(q, t) * x[q] - beside[q]) for q in range(4)])

    def body(i, carry):
        t = i + 1
        up, down = carry
        x = [v[q][t] for q in range(4)]
        up_here, down_next = roll_up(x[1]), roll_down(v[2][t + 1])
        beside0 = (x[1] + jnp.where(lane == 0, up, up_here)) + (x[2] + col_prev(x[2]))
        beside3 = (x[2] + jnp.where(lane == LANES - 1, down_next, down)) + (
            x[1] + col_next(x[1])
        )
        r0 = load_s(0, t) - (load_d(0, t) * x[0] - beside0)
        r3 = load_s(3, t) - (load_d(3, t) * x[3] - beside3)
        use(t, [r0, rest[1][t], rest[2][t], r3])
        return up_here, down_next

    full(0)
    loop(tiles - 2, body, (roll_up(v[1][0]), roll_down(v[2][1])), unroll)
    full(tiles - 1)
    full(tiles)


def restrict(c0, c1, tiles, rows, use, unroll):
    lane = lane_ids(rows)

    def body(t, carry):
        up, down = carry
        here, other = c0[t, :rows], c1[t, :rows]
        up_here = roll_up(other)
        down_next = roll_down(c0[after(t, tiles), :rows])
        north = jnp.where(lane == 0, up, up_here)
        south = jnp.where(lane == LANES - 1, down_next, down)
        use(t, ((north + south) + 3.0 * (here + other)) * (1.0 / 16.0))
        return up_here, down_next

    start = roll_up(c1[tiles, :rows]), roll_down(c0[0, :rows])
    body(tiles, loop(tiles, body, start, unroll))


class Fine:
    def __init__(self, own, halo, virtual, tiles, columns):
        self.own, self.halo, self.virtual = own, halo, virtual
        self.tiles, self.columns = tiles, columns

    def part(self, parity, t, start):
        return self.own[parity][t, pl.ds(8 + start, self.columns // 2, 2), :]

    def rows(self, q, t):
        return self.part(q % 2, t, q // 2)

    def whole(self, q, t):
        if t == self.tiles:
            return self.virtual[q][...]
        return jnp.concatenate([self.rows(q, t), self.halo[q][t]], 0)

    def ends(self, q, t):
        if t == self.tiles:
            whole = self.virtual[q][...]
            return whole[: self.columns // 2], whole[self.columns // 2 :]
        return self.rows(q, t), self.halo[q][t]

    def line(self, parity, t, column):
        row = self.own[parity][t, 8 + column : 9 + column]
        return jnp.broadcast_to(row, (8, LANES))

    def put(self, q, t, own, halo):
        pr, pc = q % 2, q // 2
        self.own[pr][t, pl.ds(8 + pc, self.columns // 2, 2), :] = own
        self.halo[q][t] = halo
        if pc == 1:
            self.own[pr][t, 7:8] = halo[7:8]
        else:
            at = 8 + self.columns
            self.own[pr][t, at : at + 1] = halo[0:1]

    def beside_columns(self, q, t, halo):
        sub = row_ids(8)
        pr, pc = q % 2, q // 2
        own = self.part(pr, t, pc - 1) + self.part(pr, t, pc + 1)
        if pc == 0:
            other = jnp.where(sub == 0, self.line(pr, t, self.columns - 1), col_prev(halo))
        else:
            other = jnp.where(sub == 7, self.line(pr, t, 0), col_next(halo))
        return own, halo + other


def fine_sweep(v, load_s, load_i, whole_s, whole_i, red, left):
    tiles = v.tiles
    y, z, qa, qb = (1, 2, 0, 3) if red else (3, 0, 2, 1)

    def lane_sum(parts, rolled, edge, lane_at):
        return [
            x + jnp.where(lane_ids(x.shape[0]) == lane_at, e, r)
            for x, r, e in zip(parts, rolled, edge)
        ]

    def beside_virtual(q):
        here, cols = v.whole(q ^ 1, tiles), v.whole(q ^ 2, tiles)
        lane = lane_ids(here.shape[0])
        if q % 2 == 0:
            lat = jnp.where(lane == 0, roll_up(v.whole(q ^ 1, tiles - 1)), roll_up(here))
        else:
            lat = jnp.where(lane == LANES - 1, roll_down(v.whole(q ^ 1, 0)), roll_down(here))
        return (here + lat) + (cols + (col_prev if q < 2 else col_next)(cols))

    held = [
        (q, (whole_s(q, tiles) + beside_virtual(q)) * whole_i(q, tiles)) for q in (y, z)
    ]
    y_before = [roll_up(x) for x in v.ends(y, tiles)]
    z_here = [roll_down(x) for x in v.ends(z, 0)]
    for t in range(tiles):
        vy, vz = v.ends(y, t), v.ends(z, t)
        y_here = [roll_up(x) for x in vy]
        z_after = [roll_down(x) for x in v.ends(z, t + 1)]
        lat_a = lane_sum(vy, y_here, y_before, 0)
        lat_b = lane_sum(vz, z_here, z_after, LANES - 1)
        new = []
        for q, lat, halo in ((qa, lat_a, vz[1]), (qb, lat_b, vy[1])):
            cols = v.beside_columns(q, t, halo)
            total = [x + (l + c) for x, l, c in zip(load_s(q, t), lat, cols)]
            value = [x * i for x, i in zip(total, load_i(q, t))]
            new.append((q, value))
            if left is not None:
                load_d, rest = left
                rest.put(q, t, *[x - d * u for x, d, u in zip(total, load_d(q, t), value)])
        for q, value in new:
            v.put(q, t, *value)
        y_before, z_here = y_here, z_after
    for q, value in held:
        v.virtual[q][...] = value


def fine_residuals(v, load_s, load_d, whole_s, whole_d, rest, c0, c1):
    tiles = v.tiles
    rows = v.columns // 2

    def columns_summed(t):
        for pr, ref in ((0, c0), (1, c1)):
            outer = rest.part(pr, t, -1) + rest.part(pr, t, 2)
            inner = rest.part(pr, t, 0) + rest.part(pr, t, 1)
            ref[t] = outer + 3.0 * inner

    def full(t):
        x = [v.whole(q, t) for q in range(4)]
        lane = lane_ids(x[0].shape[0])

        def north(q):
            return jnp.where(lane == 0, roll_up(v.whole(q, before(t, tiles))), roll_up(x[q]))

        def south(q):
            return jnp.where(
                lane == LANES - 1, roll_down(v.whole(q, after(t, tiles))), roll_down(x[q])
            )

        beside = [
            (x[1] + north(1)) + (x[2] + col_prev(x[2])),
            (x[0] + south(0)) + (x[3] + col_prev(x[3])),
            (x[3] + north(3)) + (x[0] + col_next(x[0])),
            (x[2] + south(2)) + (x[1] + col_next(x[1])),
        ]
        r = [whole_s(q, t) - (whole_d(q, t) * x[q] - beside[q]) for q in range(4)]
        if t == tiles:
            c0[t] = ((col_prev(r[2]) + col_next(r[0])) + 3.0 * (r[0] + r[2]))[:rows]
            c1[t] = ((col_prev(r[3]) + col_next(r[1])) + 3.0 * (r[1] + r[3]))[:rows]
        else:
            for q in range(4):
                rest.put(q, t, r[q][:rows], r[q][rows:])
            columns_summed(t)

    full(0)
    up = [roll_up(x) for x in v.ends(1, 0)]
    down = [roll_down(x) for x in v.ends(2, 1)]
    for t in range(1, tiles - 1):
        x = [v.ends(q, t) for q in range(4)]
        up_here = [roll_up(part) for part in x[1]]
        down_next = [roll_down(part) for part in v.ends(2, t + 1)]
        for q, ns, near, edge, lane_at in (
            (0, 1, up_here, up, 0), (3, 2, down, down_next, LANES - 1)
        ):
            cols = v.beside_columns(q, t, x[q ^ 2][1])
            r = []
            for i, (s, d) in enumerate(zip(load_s(q, t), load_d(q, t))):
                lane = lane_ids(s.shape[0])
                beside = x[ns][i] + jnp.where(lane == lane_at, edge[i], near[i]) + cols[i]
                r.append(s - (d * x[q][i] - beside))
            rest.put(q, t, *r)
        columns_summed(t)
        up, down = up_here, down_next
    full(tiles - 1)
    full(tiles)


def fine_kernel(
    s_ref, d_ref, i_ref, d1_ref, i1_ref, d2_ref,
    from_other, from_mate, polar_ref, corner_near, corner_far,
    r_ref, s1_ref, d1_virtual, d2_virtual, s2_ref, to_mate, to_other,
    v_ref, hv, pv, hr, c0, c1, hs, hd, hi, ps, pd, pi, n1, temp,
    w0, w1, w2, w3, e0, e1, pi1, black_even, black_odd, red_even, red_odd,
    part1, part2,
):
    tiles, columns = s_ref.shape[1], s_ref.shape[2]
    rows = columns // 2
    sub = row_ids(8)
    odd = is_odd()

    def halo(t, _):
        fill_halo(t, from_mate, from_other, odd, False, hs, hd, hi)
        return 0

    loop(tiles, halo, 0, 8)
    total = -16.0
    for q in range(4):
        own_s, own_d = polar_unpacked(polar_ref, q)
        near_s, near_d = polar_unpacked(corner_near, q)
        far_s, far_d = polar_unpacked(corner_far, q)
        left_s, right_s = chosen(odd, near_s, far_s)
        left_d, right_d = chosen(odd, near_d, far_d)
        total = total + own_d
        ps[q] = own_s
        pd[q] = own_d
        pi[q] = inverse_of(own_d)
        source = jnp.where(sub >= 5, left_s, jnp.where(sub <= 2, right_s, 0.0))
        diag = jnp.where(sub >= 5, left_d, jnp.where(sub <= 2, right_d, 4.0))
        hs[q, tiles] = source
        hd[q, tiles] = diag
        hi[q, tiles] = inverse_of(diag)

    def loaders(ref, halo, virtual):
        def split(q, t):
            return ref[q % 2, t, pl.ds(q // 2, rows, 2), :], halo[q, t]

        def whole(q, t):
            if t == tiles:
                return jnp.concatenate([virtual[q], halo[q, t]], 0)
            return jnp.concatenate(split(q, t), 0)

        return split, whole

    load_s, whole_s = loaders(s_ref, hs, ps)
    load_d, whole_d = loaders(d_ref, hd, pd)
    load_i, whole_i = loaders(i_ref, hi, pi)

    def held(own_ref, halo_ref):
        return Fine(
            [own_ref.at[p] for p in (0, 1)],
            [halo_ref.at[q] for q in range(4)],
            [pv.at[q] for q in range(4)],
            tiles,
            columns,
        )

    v, rest = held(v_ref, hv), held(r_ref, hr)
    for t in range(tiles):
        for q in (0, 3):
            v.put(q, t, *[x * i for x, i in zip(load_s(q, t), load_i(q, t))])
    for q in (1, 2):
        for t in (0, tiles - 1):
            v.put(q, t, jnp.zeros((rows, LANES), F32), jnp.zeros((8, LANES), F32))
        pv[q] = whole_s(q, tiles) * whole_i(q, tiles)
        pv[3 * (q - 1)] = jnp.zeros((rows + 8, LANES), F32)
    for red, left in ((False, None), (True, None), (False, (load_d, rest))):
        fine_sweep(v, load_s, load_i, whole_s, whole_i, red, left)
    fine_residuals(v, load_s, load_d, whole_s, whole_d, rest, c0, c1)

    def coarse(t, value):
        n1[t] = value

    restrict(c0, c1, tiles, rows, coarse, tiles)

    def use(c, source):
        for q in range(4):
            s1_ref[q, c] = source[q]

    tiles1 = tiles // 2
    split_tiles(lambda t: n1[t], tiles1, rows, splitter(), temp, use)
    out = moved(jnp.concatenate([n1[tiles], total], 0), virtual_splitter())
    source = quarters_of(out[:rows], temp.at[0])
    screen = quarters_of(out[rows:], temp.at[1])
    for q in range(4):
        s1_ref[q, tiles1] = source[q]
        d1_virtual[q] = 4.0 + screen[q]
        pi1[q] = inverse_of(4.0 + screen[q])
    d2_virtual[...] = 4.0 + ((screen[0] + screen[1]) + (screen[2] + screen[3]))

    def own(main, virtual):
        return lambda q, t: virtual[q] if isinstance(t, int) and t == tiles1 else main[q, t]

    w = [w0, w1, w2, w3]
    rows1 = rows // 2
    row = row_ids(rows1)
    load_s, load_d = own(s1_ref, s1_ref.at[:, tiles1]), own(d1_ref, d1_virtual)

    def after_sweep(sweep):
        if sweep == 0:
            for t in range(tiles1 + 1):
                even, odd_red = reds(t == tiles1)
                black_even[t] = w[even ^ 1][t]
                black_odd[t] = w[odd_red ^ 1][t]

    left = load_d, {1: part1, 2: part2}
    smooth(w, load_s, own(i1_ref, pi1), tiles1, 16, left, after_sweep)

    def valid(q, virtual):
        even, odd_red = reds(virtual)
        first = 1 if q == odd_red ^ 1 else 2
        last = rows1 - 2 if q == even ^ 1 else rows1 - 3
        return (row >= first) & (row <= last)

    def keep_red(t, r):
        even, odd_red = reds(isinstance(t, int) and t == tiles1)
        red_even[t] = r[even]
        red_odd[t] = r[odd_red]

    residuals(w, load_s, left, tiles1, e0, e1, keep_red, 16, valid)
    shared = {}

    def edges(t, partial):
        virtual = t == tiles1
        even, odd_red = reds(virtual)
        s2_ref[t] = partial
        packs = state_packs(
            [s1_ref[q, t] for q in range(4)],
            [load_d(q, t) for q in range(4)],
            [w[q][t] for q in range(4)],
            {even ^ 1: black_even[t], odd_red ^ 1: black_odd[t]},
            {even: red_even[t], odd_red: red_odd[t]},
            partial,
            d2_virtual[...] if virtual else d2_ref[t],
            virtual,
        )
        right, left = packs
        count = tiles1 + 1
        for i in (0, 1):
            to_mate[i * count + t], to_other[i * count + t] = chosen(odd, left[i], right[i])
        pair = chosen(odd, left[2], right[2])
        if t % 2 == 0:
            shared[0] = pair
        if t % 2 == 1 or virtual:
            if t % 2 == 1:
                pair = [
                    jnp.where(sub < 4, x, roll_rows(y, 4)) for x, y in zip(shared[0], pair)
                ]
            to_mate[2 * count + t // 2], to_other[2 * count + t // 2] = pair

    restrict(e0, e1, tiles1, rows1, edges, 16)


def merge_kernel(r_ref, out_ref, out_buf, sems):
    tiles = r_ref.shape[1]
    columns = out_ref.shape[0]
    matrix = merger()
    chunk = out_ref.shape[1] // GROUPS
    copies = []
    for group in range(GROUPS):
        for batch in range(tiles // GROUPS // BATCH):
            start = group * (tiles // GROUPS) + batch * BATCH
            own = slice(8, 8 + columns)
            both = [
                jnp.concatenate([r_ref[0, start + i, own], r_ref[1, start + i, own]], 1)
                for i in range(BATCH)
            ]
            out = moved(jnp.concatenate(both, 0), matrix)
            for i in range(BATCH):
                where = slice((start + i) * 256, (start + i + 1) * 256)
                out_buf[:, where] = out[columns * i : columns * (i + 1)]
        part = pl.ds(group * chunk, chunk)
        copy = pltpu.make_async_copy(out_buf.at[:, part], out_ref.at[:, part], sems.at[group])
        copy.start()
        copies.append(copy)
    for copy in copies:
        copy.wait()


def coarse_kernel(
    s_ref, d_ref, i_ref, d_virtual, d2_ref, d2_virtual, s2_ref, from_other, from_mate,
    solution_ref, residual_ref,
    v0, v1, v2, v3, c0, c1, hs, hd, hi, part, fixes, rest1, rest2, s, d, inv, va, vb,
):
    v = [v0, v1, v2, v3]
    tiles, own = d_ref.shape[1], d_ref.shape[2]
    rows = own + 8
    count = tiles + 1
    sub = row_ids(8)
    odd_band = is_odd()
    def rim(x):
        return jnp.where(sub < 4, x[:8], x[own - 8 :])

    for t in range(count):
        places = t, count + t, 2 * count + t // 2
        packs = [chosen(odd_band, from_mate[i], from_other[i]) for i in places]
        source = [jnp.zeros((8, LANES), F32)] * 4
        diag = [jnp.full((8, LANES), 4.0, F32)] * 4
        inverse = [jnp.zeros((8, LANES), F32)] * 4
        fixed = [jnp.zeros((8, LANES), F32)] * 4
        more = jnp.zeros((8, LANES), F32)
        total = jnp.ones((8, LANES), F32)
        third = 4 * (t % 2)
        for side, (a, ab, b, bb) in enumerate(sides(t == tiles)):
            near, far, step = (7, 6, -1) if side == 0 else (0, 1, 1)
            pack0, pack1, pack2 = (pair[side] for pair in packs)

            def put(group, q, at, pack, row):
                group[q] = jnp.where(sub == at, roll_rows(pack, at - row), group[q])

            for q in range(4):
                put(source, q, near, pack0, q)
                put(diag, q, near, pack0, 4 + q)
            put(source, bb, far, pack1, 1)
            put(diag, bb, far, pack1, 2)
            put(source, b, far, pack1, 5)
            diag[b] = jnp.where(sub == far, 0.0, diag[b])
            put(source, a, far, pack1, 6)
            put(fixed, ab, near, pack1, 0)
            put(fixed, bb, far, pack1, 3)
            put(fixed, b, far, pack1, 4)
            for at, pack, row in (
                (far + 2 * step, pack1, 7), (far + step, pack2, third), (far, pack2, third + 1)
            ):
                more = jnp.where(sub == at, roll_rows(pack, at - row), more)
            for at, row in ((far + step, third + 2), (far, third + 3)):
                total = jnp.where(sub == at, roll_rows(pack2, at - row), total)
            for q in range(4):
                known = (sub == near) | (sub == far) if q == bb else sub == near
                inverse[q] = jnp.where(known, inverse_of(diag[q]), inverse[q])
        for q in range(4):
            own_d = rim(d_virtual[q] if t == tiles else d_ref[q, t])
            own_i = inverse_of(own_d) if t == tiles else rim(i_ref[q, t])
            hs[q, t] = jnp.concatenate([source[q], rim(s_ref[q, t])], 0)
            hd[q, t] = jnp.concatenate([diag[q], own_d], 0)
            hi[q, t] = jnp.concatenate([inverse[q], own_i], 0)
            fixes[q, t] = fixed[q]
        part[t] = more
        near_total = (diag[0] + diag[1]) + (diag[2] + diag[3]) - 12.0
        total = jnp.where((sub == 0) | (sub == 7), near_total, total)
        here = d2_virtual[...] if t == tiles else d2_ref[t]
        d[t] = jnp.concatenate([here, total], 0)
    def after_sweep(sweep):
        if sweep == 2:
            return
        for t in range(count):
            (a, ab, b, bb), (_, _, other_b, other_bb) = sides(t == tiles)
            todo = {}
            if sweep == 0:
                todo = {ab: (sub == 7) | (sub == 1), bb: (sub == 6) | (sub == 0)}
            else:
                todo = {b: sub == 6, other_b: sub == 1}
            for q, mask in todo.items():
                v[q][t, :8] = jnp.where(mask, fixes[q, t], v[q][t, :8])

    def of(ref):
        return lambda q, t: ref[q, t]

    left = of(hd), {1: rest1, 2: rest2}
    smooth(v, of(hs), of(hi), tiles, 16, left, after_sweep)
    row = row_ids(16)

    def valid(q, virtual):
        even, odd_red = reds(virtual)
        after_band = 0 if q == odd_red ^ 1 else 1
        before_band = 7 if q == even ^ 1 else 6
        first = 8 if q == odd_red ^ 1 else 9
        last = 15 if q == even ^ 1 else 14
        return (row <= after_band) | ((row >= before_band) & (row <= first)) | (row >= last)

    residuals(v, of(hs), left, tiles, c0, c1, lambda t, r: None, 16, valid)

    lane, row = lane_ids(rows), row_ids(rows)
    even = (lane + row) % 2 == 0
    odd = jnp.logical_not(even)

    def start(t, value):
        ends = value[8:]
        source = jnp.concatenate(
            [
                s2_ref[t, :8] + jnp.where(sub < 4, ends, 0.0),
                s2_ref[t, own - 8 :] + jnp.where(sub >= 4, ends, 0.0),
                value[:8] + part[t],
            ],
            0,
        )
        inverse = inverse_of(d[t])
        s[t] = source
        inv[t] = inverse
        virtual = isinstance(t, int) and t == tiles
        va[t] = jnp.where(odd if virtual else even, source * inverse, 0.0)

    restrict(c0, c1, tiles, 16, start, 16)

    def scan(v, use):
        up, down = roll_up(v[tiles]), roll_down(v[0])
        for t in range(tiles + 1):
            x = v[t]
            up_here, down_next = roll_up(x), roll_down(v[after(t, tiles)])
            north = jnp.where(lane == 0, up, up_here)
            south = jnp.where(lane == LANES - 1, down_next, down)
            use(t, x, (col_prev(x) + col_next(x)) + (north + south))
            up, down = up_here, down_next

    for old, new, mask, other in ((va, vb, odd, even), (vb, va, even, odd), (va, vb, odd, even)):

        def relax(t, x, beside):
            update = other if t == tiles else mask
            new[t] = jnp.where(update, (s[t] + beside) * inv[t], x)

        scan(old, relax)

    def finish(t, x, beside):
        if t < tiles:
            where = slice(t * LANES, (t + 1) * LANES)
            solution_ref[:, where] = x[:own]
            residual_ref[:, where] = (s[t] - (d[t] * x - beside))[:own]

    scan(vb, finish)


VMEM = pl.BlockSpec(memory_space=pltpu.VMEM)
HBM = pl.BlockSpec(memory_space=pltpu.HBM)


def call(kernel, out_shapes, scratch, *args, sems=None, far_in=0, far_out=0):
    scratch = [pltpu.VMEM(x, F32) if isinstance(x, tuple) else x for x in scratch]
    if sems is not None:
        scratch.append(pltpu.SemaphoreType.DMA(sems))
    return pl.pallas_call(
        kernel,
        out_shape=[jax.ShapeDtypeStruct(shape, F32) for shape in out_shapes],
        in_specs=[HBM] * far_in + [VMEM] * (len(args) - far_in),
        out_specs=[HBM] * far_out + [VMEM] * (len(out_shapes) - far_out),
        scratch_shapes=scratch,
        compiler_params=pltpu.CompilerParams(vmem_limit_bytes=40 * 2**20),
    )(*args)


def swapped_with(x, by):
    count = lax.axis_size("lon")
    pairs = [(i, (i + by) % count) for i in range(0, count, 2)]
    return lax.ppermute(x, "lon", pairs + [(b, a) for a, b in pairs])


def swapped_edges(to_mate, to_other):
    from_mate = swapped_with(to_mate, 1)
    return from_mate, swapped_with(to_other, -1)


def body(right_side, texel_weight, seam_flags):
    columns, height = right_side.shape
    half_turn = lax.axis_size("lon") // 2
    tiles, rows = height // 256, columns // 2
    tiles1, rows1 = tiles // 2, rows // 2
    temp = (BATCH, 2, columns, LANES)
    natural = (2, tiles, columns, LANES)
    padded = (2, tiles, columns + 16, LANES)
    quarters1 = (4, tiles1, rows1, LANES)
    split = (2, 16 * tiles, LANES)
    to_mate, to_other, corner = call(
        edge_kernel,
        [(2, tiles, 8, LANES), (2, tiles, 8, LANES), (2, 8, LANES)],
        [(16, height), pltpu.VMEM((32, height), BF16)]
        + [pltpu.VMEM(seam_flags.shape, jnp.int32), split, split, (tiles, 8, LANES)],
        *[
            pltpu.with_memory_space_constraint(x, pltpu.HBM)
            for x in (right_side, texel_weight, seam_flags)
        ],
        sems=(5,), far_in=3,
    )
    from_mate, from_other = swapped_edges(to_mate, to_other)
    corner_far = swapped_with(corner, half_turn - 1)
    corner_near = swapped_with(corner, half_turn + 1)
    ends = (2, 2, columns, LANES)
    (polar_own,) = call(
        polar_kernel, [(2, rows, LANES)], [ends, ends],
        right_side, texel_weight, seam_flags, corner,
    )
    polar = lax.ppermute(
        polar_own, "lon", [(i, (i + half_turn) % (2 * half_turn)) for i in range(2 * half_turn)]
    )
    s, d, inverse, d1, i1, d2 = call(
        bulk_kernel,
        [natural] * 3 + [quarters1, quarters1, quarters1[1:]],
        [(BATCH, columns, LANES), (tiles, 8, LANES), (tiles, rows, LANES), (BATCH, 2, rows, LANES)],
        right_side, texel_weight, seam_flags, polar_own,
    )

    def level_scratch(tiles, rows):
        return [(tiles + 1, rows, LANES)] * 6

    def halo_scratch(tiles):
        return [(4, tiles + 1, 8, LANES)] * 3

    pack1 = (2 * (tiles1 + 1) + tiles1 // 2 + 1, 8, LANES)
    r, s1, d1_virtual, d2_virtual, s2_own, to_mate, to_other = call(
        fine_kernel,
        [padded, (4, tiles1 + 1, rows1, LANES), (4, rows1, LANES), (rows1, LANES)]
        + [(tiles1 + 1, rows1, LANES), pack1, pack1],
        [padded, (4, tiles, 8, LANES), (4, rows + 8, LANES), (4, tiles, 8, LANES)]
        + [(tiles + 1, rows, LANES)] * 2
        + halo_scratch(tiles)
        + [(4, rows, LANES)] * 3
        + [(tiles + 1, rows, LANES), (BATCH, 2, rows, LANES)]
        + level_scratch(tiles1, rows1)
        + [(4, rows1, LANES)]
        + [(tiles1 + 1, rows1, LANES)] * 4
        + [(tiles1, rows1, LANES)] * 2,
        s, d, inverse, d1, i1, d2, from_other, from_mate, polar, corner_near, corner_far,
    )
    from_mate, from_other = swapped_edges(to_mate, to_other)
    (fine_residual,) = call(
        merge_kernel, [(columns, height)], [(columns, height)], r,
        sems=(GROUPS,), far_out=1,
    )
    wide = (tiles1 + 1, rows1 + 8, LANES)
    solution_2, residual_2 = call(
        coarse_kernel,
        [(columns // 4, height // 4)] * 2,
        level_scratch(tiles1, 16)
        + [(4, tiles1 + 1, 16, LANES)] * 3
        + [(tiles1 + 1, 8, LANES), (4, tiles1 + 1, 8, LANES)]
        + [(tiles1, 16, LANES)] * 2
        + [wide] * 5,
        s1, d1, i1, d1_virtual, d2, d2_virtual, s2_own, from_other, from_mate,
    )
    return fine_residual, solution_2, residual_2


def solution(mesh):
    spec = P(("groups", "lon"), None)
    return jax.shard_map(
        body, mesh=mesh, in_specs=(spec,) * 3, out_specs=(spec,) * 3, check_vma=False
    )
```

```python
import jax
import jax.numpy as jnp
from jax import lax
from jax.experimental import pallas as pl
from jax.experimental.pallas import tpu as pltpu
from jax.sharding import PartitionSpec as P

TILE = 32
SEAM_SCALE = 0.1
LANES = 128
GROUPS = 4
BATCH = 4
F32 = jnp.float32
BF16 = jnp.bfloat16


def loop(count, body, carry=0, unroll=4):
    unroll = min(unroll, count)

    def steps(block, carry):
        for i in range(unroll):
            carry = body(block * unroll + i, carry)
        return carry

    whole = count // unroll
    carry = steps(0, carry) if whole == 1 else lax.fori_loop(0, whole, steps, carry)
    for t in range(whole * unroll, count):
        carry = body(t, carry)
    return carry


def before(t, tiles):
    return (tiles if t == 0 else t - 1) if isinstance(t, int) else jnp.where(t == 0, tiles, t - 1)


def after(t, tiles):
    return (0 if t == tiles else t + 1) if isinstance(t, int) else t + 1


def lane_ids(rows):
    return lax.broadcasted_iota(jnp.int32, (rows, LANES), 1)


def row_ids(rows):
    return lax.broadcasted_iota(jnp.int32, (rows, LANES), 0)


def roll_up(x):
    return pltpu.roll(x, 1, 1)


def roll_down(x):
    return pltpu.roll(x, LANES - 1, 1)


def roll_rows(x, by):
    by %= x.shape[0]
    return x if by == 0 else pltpu.roll(x, by, 0)


def roll_lanes(x, by):
    by %= LANES
    return x if by == 0 else pltpu.roll(x, by, 1)


def col_prev(x):
    return pltpu.roll(x, 1, 0)


def col_next(x):
    return pltpu.roll(x, x.shape[0] - 1, 0)


def inverse_of(x):
    return 1.0 / x


def selector(shape, rule):
    a = lax.broadcasted_iota(jnp.int32, shape, 0)
    b = lax.broadcasted_iota(jnp.int32, shape, 1)
    return jnp.where(rule(a, b), 1.0, 0.0).astype(BF16)


def splitter():
    return selector((256, 256), lambda a, b: a == 2 * (b % LANES) + b // LANES)


def merger():
    return selector((256, 256), lambda a, b: b == 2 * (a % LANES) + a // LANES)


def virtual_splitter():
    return selector(
        (LANES, 256),
        lambda a, b: a // 2 + jnp.where(a >= 64, 64, 0) + LANES * (a % 2) == b,
    )


def moved(x, matrix, exact=None):
    rows = x.shape[0]
    high = x.astype(BF16)
    low = (x - high.astype(F32)).astype(BF16)
    terms = [high, low] if exact is None else [high, low, exact]
    out = jnp.dot(jnp.concatenate(terms, 0), matrix, preferred_element_type=F32)
    both = out[:rows] + out[rows : 2 * rows]
    return both if exact is None else (both, out[2 * rows :])


def quarters_of(parts, temp):
    count = parts.shape[0] // 2
    temp[0] = parts[:, :LANES]
    temp[1] = parts[:, LANES:]
    return [temp[pr, pl.ds(pc, count, 2), :] for pc in (0, 1) for pr in (0, 1)]


def reds(swapped):
    return (1, 2) if swapped else (0, 3)


def interleaved(group, offset):
    sub = row_ids(8)
    packed = roll_rows(group[0], offset)
    for q in range(1, 4):
        packed = jnp.where(sub // 2 == q, roll_rows(group[q], 2 * q + offset), packed)
    return packed


def edge_packs(source, diag, swapped):
    sub = row_ids(8)
    even, odd = reds(swapped)
    rows = source[0].shape[0]
    packs = []
    for here, first, second, row, step in (
        (slice(rows - 8, rows), even, odd, 6, 1),
        (slice(0, 8), odd, even, 1, -1),
    ):
        gs = [x[here] for x in source]
        gd = [x[here] for x in diag]
        near = gs[first] * inverse_of(gd[first])
        far = roll_rows(gs[second] * inverse_of(gd[second]), step)
        gs[first] = jnp.where(sub == row, near, gs[first])
        gd[first] = jnp.where(sub == row, far, gd[first])
        offset = 2 if row == 6 else 0
        packs.append((interleaved(gs, offset), interleaved(gd, offset)))
    return packs


def unpacked_halo(left, right, swapped):
    sub = row_ids(8)
    even, odd = reds(swapped)
    (al, bl), (ar, br) = left, right
    source, diag = [], []
    for q in range(4):
        s = jnp.where(
            sub >= 6,
            roll_rows(al, 6 - 2 * q),
            jnp.where(sub <= 1, roll_rows(ar, -2 * q), 0.0),
        )
        d = jnp.where(
            sub >= 6,
            roll_rows(bl, 6 - 2 * q),
            jnp.where(sub <= 1, roll_rows(br, -2 * q), 4.0),
        )
        if q == even:
            s = jnp.where(sub == 2, roll_rows(br, 1 - 2 * odd), s)
            d = jnp.where((sub == 2) | (sub == 6), 1.0, d)
        if q == odd:
            s = jnp.where(sub == 5, roll_rows(bl, 5 - 2 * even), s)
            d = jnp.where((sub == 5) | (sub == 1), 1.0, d)
        source.append(s)
        diag.append(d)
    return source, diag


def is_odd():
    return lax.rem(lax.axis_index("lon"), 2) == 1


def chosen(odd, a, b):
    return jnp.where(odd, a, b), jnp.where(odd, b, a)


def store_edges(t, packs, odd, to_mate, to_other):
    right, left = packs
    for i in (0, 1):
        to_mate[i, t], to_other[i, t] = chosen(odd, left[i], right[i])


def sides(swapped):
    even, odd = reds(swapped)
    return (even, even ^ 1, odd, odd ^ 1), (odd, odd ^ 1, even, even ^ 1)


def paired(groups, shift):
    sub = row_ids(8)
    packed = roll_rows(groups[0], shift)
    for g in (1, 2, 3):
        packed = jnp.where(sub // 2 == g, roll_rows(groups[g], 2 * g + shift), packed)
    return packed


def state_packs(source, diag, last, first_black, residual, partial, diag2, swapped):
    sub = row_ids(8)
    rows = source[0].shape[0]
    packs = []
    for (a, ab, b, bb), here, near, far, step in zip(
        sides(swapped), (slice(rows - 8, rows), slice(0, 8)), (7, 0), (6, 1), (-1, 1)
    ):
        s, d, v = ([x[here] for x in group] for group in (source, diag, last))
        part, d2 = partial[here], diag2[here]
        beside = [
            s[bb] + v[a],
            d[bb],
            first_black[bb][here],
            v[b],
            s[b] - d[b] * v[b] + v[ab],
            residual[a][here] - v[bb],
            part,
            roll_rows(d2, -step),
        ]
        groups = [jnp.where(sub == far, y, x) for x, y in zip(s + d, beside)]
        shift = 2 if near == 7 else 0
        more = jnp.where(sub == far, d2, first_black[ab][here])
        more = jnp.where(sub == far + step, part, more)
        more = jnp.where(sub == far + 2 * step, part * inverse_of(d2), more)
        packs.append((paired(groups[:4], shift), paired(groups[4:], shift), more))
    return packs


def fill_halo(t, from_mate, from_other, odd, swapped, hs, hd, hi):
    al, ar = chosen(odd, from_mate[0, t], from_other[0, t])
    bl, br = chosen(odd, from_mate[1, t], from_other[1, t])
    source, diag = unpacked_halo((al, bl), (ar, br), swapped)
    for q in range(4):
        hs[q, t] = source[q]
        hd[q, t] = diag[q]
        hi[q, t] = inverse_of(diag[q])


def loader(own, halo, virtual, tiles):
    def load(q, t):
        if isinstance(t, int) and t == tiles:
            return jnp.concatenate([virtual[q], halo[q, t]], 0)
        return jnp.concatenate([own[q, t], halo[q, t]], 0)

    return load


def polar_packs(tiles_of):
    lane = lane_ids(tiles_of[0][0].shape[0])
    packs = []
    for pc in (0, 1):
        parts = [*tiles_of[2 * pc], *tiles_of[2 * pc + 1]]
        packed = parts[0]
        for m in range(1, 4):
            mine = (lane + (16 - 32 * m) % LANES) % LANES < 32
            packed = jnp.where(mine, roll_lanes(parts[m], 32 * m), packed)
        packs.append(packed)
    return packs


def polar_unpacked(x, q):
    lane = lane_ids(x.shape[1])
    used = (lane < 16) | (lane >= LANES - 16)
    m = 2 * (q % 2)
    return (
        jnp.where(used, roll_lanes(x[q // 2], 32 * m), 0.0),
        jnp.where(used, roll_lanes(x[q // 2], 32 * (m + 1)), 4.0),
    )


def seam_scales(flags, chunks):
    flag_cols, flag_lats = flags.shape
    flags = jnp.concatenate(
        [flags.astype(F32), jnp.zeros((8 - flag_cols, flag_lats), F32)], 0
    )
    lat = lax.broadcasted_iota(jnp.int32, (8, flag_lats), 1)
    stacked = jnp.concatenate([jnp.where(lat // 8 == c, flags, 0.0) for c in chunks], 0)
    spread = selector((flag_lats, LANES), lambda a, b: a % 8 == b // (TILE // 2))
    spread_flags = jnp.dot(stacked.astype(BF16), spread, preferred_element_type=F32)
    scale = jnp.where(spread_flags > 0.5, SEAM_SCALE, 1.0)
    return scale.reshape(len(chunks), 8, LANES)


def seam_rows(scales, flag_cols, rows):
    size = (rows // flag_cols, LANES)
    return jnp.concatenate(
        [jnp.broadcast_to(scales[i : i + 1], size) for i in range(flag_cols)], 0
    )


def edge_kernel(
    right_ref, weight_ref, flag_ref,
    to_mate, to_other, corner_ref,
    edge_s, edge_w, flags, temp_s, temp_w, scale_ref, sems,
):
    columns, height = right_ref.shape
    tiles = height // 256
    pairs = [(flag_ref, flags)]
    for i, (src, dst, size) in enumerate(
        ((right_ref, edge_s, 8), (weight_ref, edge_w, 16))
    ):
        pairs.append((src.at[pl.ds(0, size)], dst.at[pl.ds(0, size)]))
        pairs.append((src.at[pl.ds(columns - size, size)], dst.at[pl.ds(size, size)]))
    copies = [
        pltpu.make_async_copy(src, dst, sems.at[i]) for i, (src, dst) in enumerate(pairs)
    ]
    for copy in copies:
        copy.start()
    odd = is_odd()
    matrix = splitter()
    flag_cols = flag_ref.shape[0]
    copies[0].wait()
    scale_ref[...] = seam_scales(flags[...], range(tiles))
    for copy in copies[1:]:
        copy.wait()
    sub = row_ids(8)
    lanes = [slice(c * 256, (c + 1) * 256) for c in range(tiles)]
    source, weight = moved(
        jnp.concatenate([edge_s[:, w] for w in lanes], 0),
        matrix,
        jnp.concatenate([edge_w[:, w] for w in lanes], 0),
    )
    weight = weight.reshape(tiles, 32, 256)
    weight = jnp.concatenate([weight[:, :8], weight[:, 24:]], 1).reshape(tiles * 16, 256)
    source = quarters_of(source, temp_s)
    weight = quarters_of(weight, temp_w)
    found = []
    for c in range(tiles):
        here = slice(c * 8, (c + 1) * 8)
        scales = scale_ref[c]
        scale = jnp.where(sub < 4, scales[:1], scales[flag_cols - 1 : flag_cols])
        pair = [x[here] for x in source], [4.0 + w[here] * scale for w in weight]
        store_edges(c, edge_packs(*pair, False), odd, to_mate, to_other)
        if c in (0, tiles - 1):
            found.append(pair)
    both = mirrored_ends(*found)
    for pc in (0, 1):
        corner = both[8 * pc : 8 * (pc + 1)]
        corner_ref[pc] = corner


def mirrored_ends(first, last):
    mirror = selector((LANES, LANES), lambda a, b: a + b == LANES - 1)
    lane = lane_ids(first[0][0].shape[0])
    ends = [
        [jnp.where(lane >= 64, last[i][q ^ 1], first[i][q ^ 1]) for i in (0, 1)]
        for q in range(4)
    ]
    return moved(jnp.concatenate(polar_packs(ends), 0), mirror)


def polar_kernel(right_ref, weight_ref, flag_ref, edges_first, polar_ref, temp_s, temp_w):
    columns, height = right_ref.shape
    rows, tiles = columns // 2, height // 256
    scales = seam_scales(flag_ref[...], (0, tiles - 1))
    lanes = slice(0, 256), slice(height - 256, height)
    source, weight = moved(
        jnp.concatenate([right_ref[:, w] for w in lanes], 0),
        splitter(),
        jnp.concatenate([weight_ref[:, w] for w in lanes], 0),
    )
    found = []
    for end in (0, 1):
        here = slice(end * columns, (end + 1) * columns)
        scale = seam_rows(scales[end], flag_ref.shape[0], rows)
        found.append(
            (
                quarters_of(source[here], temp_s.at[end]),
                [4.0 + w * scale for w in quarters_of(weight[here], temp_w.at[end])],
            )
        )
    both = mirrored_ends(*found)
    for pc in (0, 1):
        polar_ref[pc] = both[pc * rows : (pc + 1) * rows]


def bulk_kernel(
    right_ref, weight_ref, flag_ref, polar_first,
    s_ref, d_ref, i_ref, d1_ref, i1_ref, d2_ref,
    temp, scale_ref, e_ref, split_temp,
):
    tiles, columns = s_ref.shape[1], s_ref.shape[2]
    rows = columns // 2
    matrix = splitter()
    scale_ref[...] = seam_scales(flag_ref[...], range(tiles))
    for start in range(0, tiles, BATCH):
        lanes = [slice((start + i) * 256, (start + i + 1) * 256) for i in range(BATCH)]
        source, weight = moved(
            jnp.concatenate([right_ref[:, w] for w in lanes], 0),
            matrix,
            jnp.concatenate([weight_ref[:, w] for w in lanes], 0),
        )
        for i in range(BATCH):
            c = start + i
            here = slice(i * columns, (i + 1) * columns)
            scale = seam_rows(scale_ref[c], flag_ref.shape[0], columns)
            screens = []
            for pr in (0, 1):
                half = slice(pr * LANES, (pr + 1) * LANES)
                screen = weight[here, half] * scale
                diag = 4.0 + screen
                s_ref[pr, c] = source[here, half]
                d_ref[pr, c] = diag
                i_ref[pr, c] = 1.0 / diag
                screens.append(screen)
            temp[i] = screens[0] + screens[1]
            e_ref[c] = temp[i, pl.ds(0, rows, 2), :] + temp[i, pl.ds(1, rows, 2), :]

    def use(c, screen):
        for q in range(4):
            d1_ref[q, c] = 4.0 + screen[q]
            i1_ref[q, c] = inverse_of(4.0 + screen[q])
        d2_ref[c] = 4.0 + ((screen[0] + screen[1]) + (screen[2] + screen[3]))

    split_tiles(lambda t: e_ref[t], tiles // 2, rows, matrix, split_temp, use)


def split_tiles(load, tiles, rows, matrix, temp, use):
    for start in range(0, tiles, BATCH):
        wide = [
            jnp.concatenate([load(2 * c), load(2 * c + 1)], 1)
            for c in range(start, start + BATCH)
        ]
        out = moved(jnp.concatenate(wide, 0), matrix)
        for i in range(BATCH):
            use(start + i, quarters_of(out[i * rows : (i + 1) * rows], temp.at[i, :, :rows]))


class Ring:
    def __init__(self, own, virtual, tiles, rows):
        self.own, self.virtual, self.tiles, self.rows = own, virtual, tiles, rows

    def part(self, parity, t, start):
        return self.own[parity, t, pl.ds(8 + start, self.rows, 2), :]

    def whole(self, q, t):
        return self.virtual[q] if t == self.tiles else self.part(q % 2, t, q // 2)

    def put(self, q, t, x):
        if t == self.tiles:
            self.virtual[q] = x
            return
        pr, pc = q % 2, q // 2
        self.own[pr, t, pl.ds(8 + pc, self.rows, 2), :] = x
        if pc == 1:
            self.own[pr, t, 7:8] = x[self.rows - 1 :]
        else:
            end = 8 + 2 * self.rows
            self.own[pr, t, end : end + 1] = x[:1]

    def beside_columns(self, q, t):
        pr, pc = q % 2, q // 2
        if t == self.tiles:
            x = self.virtual[q ^ 2]
            return x + (col_next if pc else col_prev)(x)
        return self.part(pr, t, pc - 1) + self.part(pr, t, pc + 1)

    def beside(self, q, t):
        x = self.whole(q ^ 1, t)
        lane = lane_ids(self.rows)
        if q % 2 == 0:
            other = roll_up(self.whole(q ^ 1, before(t, self.tiles)))
            lat = jnp.where(lane == 0, other, roll_up(x))
        else:
            other = roll_down(self.whole(q ^ 1, after(t, self.tiles)))
            lat = jnp.where(lane == LANES - 1, other, roll_down(x))
        return (x + lat) + self.beside_columns(q, t)


def ring_sweep(v, load_s, load_i, red, left):
    tiles = v.tiles
    lane = lane_ids(v.rows)
    y, z, qa, qb = (1, 2, 0, 3) if red else (3, 0, 2, 1)
    held = [(q, (load_s(q, tiles) + v.beside(q, tiles)) * load_i(q, tiles)) for q in (y, z)]
    y_before, vz = roll_up(v.whole(y, tiles)), v.whole(z, 0)
    z_here = roll_down(vz)
    for t in range(tiles):
        vy, z_next = v.whole(y, t), v.whole(z, t + 1)
        y_here, z_after = roll_up(vy), roll_down(z_next)
        lat_a = vy + jnp.where(lane == 0, y_before, y_here)
        lat_b = vz + jnp.where(lane == LANES - 1, z_after, z_here)
        new = []
        for q, lat in ((qa, lat_a), (qb, lat_b)):
            total = load_s(q, t) + (lat + v.beside_columns(q, t))
            value = total * load_i(q, t)
            new.append((q, value))
            if left is not None:
                load_d, rest = left
                rest.put(q, t, total - load_d(q, t) * value)
        for q, value in new:
            v.put(q, t, value)
        y_before, z_here, vz = y_here, z_after, z_next
    for q, value in held:
        v.put(q, tiles, value)


def ring_smooth(v, load_s, load_i, load_d, rest, after_sweep):
    tiles = v.tiles
    zeros = jnp.zeros((v.rows, LANES), F32)
    for t in range(tiles + 1):
        reds_here = (1, 2) if t == tiles else (0, 3)
        for q in reds_here:
            v.put(q, t, load_s(q, t) * load_i(q, t))
        if t in (0, tiles - 1, tiles):
            for q in reds_here:
                v.put(q ^ 1, t, zeros)
    for sweep, red in enumerate((False, True, False)):
        ring_sweep(v, load_s, load_i, red, (load_d, rest) if sweep == 2 else None)
        after_sweep(sweep)


def ring_residuals(v, load_s, load_d, rest, c0, c1, keep, valid):
    tiles = v.tiles
    lane = lane_ids(v.rows)

    def use(t, r):
        keep(t, r)
        r = [jnp.where(valid(q, t == tiles), r[q], 0.0) for q in range(4)]
        if t == tiles:
            c0[t] = (col_prev(r[2]) + col_next(r[0])) + 3.0 * (r[0] + r[2])
            c1[t] = (col_prev(r[3]) + col_next(r[1])) + 3.0 * (r[1] + r[3])
            return
        for q in range(4):
            rest.put(q, t, r[q])
        for pr, ref in ((0, c0), (1, c1)):
            outer = rest.part(pr, t, -1) + rest.part(pr, t, 2)
            ref[t] = outer + 3.0 * (rest.part(pr, t, 0) + rest.part(pr, t, 1))

    def residual(q, t, beside):
        return load_s(q, t) - (load_d(q, t) * v.whole(q, t) - beside)

    def full(t):
        use(t, [residual(q, t, v.beside(q, t)) for q in range(4)])

    full(0)
    up, x2 = roll_up(v.whole(1, 0)), v.whole(2, 1)
    down = roll_down(x2)
    for t in range(1, tiles - 1):
        x1, next2 = v.whole(1, t), v.whole(2, t + 1)
        up_here, down_next = roll_up(x1), roll_down(next2)
        lat0 = x1 + jnp.where(lane == 0, up, up_here)
        lat3 = x2 + jnp.where(lane == LANES - 1, down_next, down)
        r0 = residual(0, t, lat0 + v.beside_columns(0, t))
        r3 = residual(3, t, lat3 + v.beside_columns(3, t))
        use(t, [r0, rest.whole(1, t), rest.whole(2, t), r3])
        up, down, x2 = up_here, down_next, next2
    full(tiles - 1)
    full(tiles)


def restrict(c0, c1, tiles, rows, use, unroll):
    lane = lane_ids(rows)

    def body(t, carry):
        up, down = carry
        here, other = c0[t, :rows], c1[t, :rows]
        up_here = roll_up(other)
        down_next = roll_down(c0[after(t, tiles), :rows])
        north = jnp.where(lane == 0, up, up_here)
        south = jnp.where(lane == LANES - 1, down_next, down)
        use(t, ((north + south) + 3.0 * (here + other)) * (1.0 / 16.0))
        return up_here, down_next

    start = roll_up(c1[tiles, :rows]), roll_down(c0[0, :rows])
    body(tiles, loop(tiles, body, start, unroll))


class Fine:
    def __init__(self, own, halo, virtual, tiles, columns):
        self.own, self.halo, self.virtual = own, halo, virtual
        self.tiles, self.columns = tiles, columns

    def part(self, parity, t, start):
        return self.own[parity][t, pl.ds(8 + start, self.columns // 2, 2), :]

    def rows(self, q, t):
        return self.part(q % 2, t, q // 2)

    def whole(self, q, t):
        if t == self.tiles:
            return self.virtual[q][...]
        return jnp.concatenate([self.rows(q, t), self.halo[q][t]], 0)

    def ends(self, q, t):
        if t == self.tiles:
            whole = self.virtual[q][...]
            return whole[: self.columns // 2], whole[self.columns // 2 :]
        return self.rows(q, t), self.halo[q][t]

    def line(self, parity, t, column):
        row = self.own[parity][t, 8 + column : 9 + column]
        return jnp.broadcast_to(row, (8, LANES))

    def put(self, q, t, own, halo):
        pr, pc = q % 2, q // 2
        self.own[pr][t, pl.ds(8 + pc, self.columns // 2, 2), :] = own
        self.halo[q][t] = halo
        if pc == 1:
            self.own[pr][t, 7:8] = halo[7:8]
        else:
            at = 8 + self.columns
            self.own[pr][t, at : at + 1] = halo[0:1]

    def beside_columns(self, q, t, halo):
        sub = row_ids(8)
        pr, pc = q % 2, q // 2
        own = self.part(pr, t, pc - 1) + self.part(pr, t, pc + 1)
        if pc == 0:
            other = jnp.where(sub == 0, self.line(pr, t, self.columns - 1), col_prev(halo))
        else:
            other = jnp.where(sub == 7, self.line(pr, t, 0), col_next(halo))
        return own, halo + other


def fine_sweep(v, load_s, load_i, whole_s, whole_i, red, left):
    tiles = v.tiles
    y, z, qa, qb = (1, 2, 0, 3) if red else (3, 0, 2, 1)

    def lane_sum(parts, rolled, edge, lane_at):
        return [
            x + jnp.where(lane_ids(x.shape[0]) == lane_at, e, r)
            for x, r, e in zip(parts, rolled, edge)
        ]

    def beside_virtual(q):
        here, cols = v.whole(q ^ 1, tiles), v.whole(q ^ 2, tiles)
        lane = lane_ids(here.shape[0])
        if q % 2 == 0:
            lat = jnp.where(lane == 0, roll_up(v.whole(q ^ 1, tiles - 1)), roll_up(here))
        else:
            lat = jnp.where(lane == LANES - 1, roll_down(v.whole(q ^ 1, 0)), roll_down(here))
        return (here + lat) + (cols + (col_prev if q < 2 else col_next)(cols))

    held = [
        (q, (whole_s(q, tiles) + beside_virtual(q)) * whole_i(q, tiles)) for q in (y, z)
    ]
    y_before = [roll_up(x) for x in v.ends(y, tiles)]
    z_here = [roll_down(x) for x in v.ends(z, 0)]
    for t in range(tiles):
        vy, vz = v.ends(y, t), v.ends(z, t)
        y_here = [roll_up(x) for x in vy]
        z_after = [roll_down(x) for x in v.ends(z, t + 1)]
        lat_a = lane_sum(vy, y_here, y_before, 0)
        lat_b = lane_sum(vz, z_here, z_after, LANES - 1)
        new = []
        for q, lat, halo in ((qa, lat_a, vz[1]), (qb, lat_b, vy[1])):
            cols = v.beside_columns(q, t, halo)
            total = [x + (l + c) for x, l, c in zip(load_s(q, t), lat, cols)]
            value = [x * i for x, i in zip(total, load_i(q, t))]
            new.append((q, value))
            if left is not None:
                load_d, rest = left
                rest.put(q, t, *[x - d * u for x, d, u in zip(total, load_d(q, t), value)])
        for q, value in new:
            v.put(q, t, *value)
        y_before, z_here = y_here, z_after
    for q, value in held:
        v.virtual[q][...] = value


def fine_residuals(v, load_s, load_d, whole_s, whole_d, rest, c0, c1):
    tiles = v.tiles
    rows = v.columns // 2

    def columns_summed(t):
        for pr, ref in ((0, c0), (1, c1)):
            outer = rest.part(pr, t, -1) + rest.part(pr, t, 2)
            inner = rest.part(pr, t, 0) + rest.part(pr, t, 1)
            ref[t] = outer + 3.0 * inner

    def full(t):
        x = [v.whole(q, t) for q in range(4)]
        lane = lane_ids(x[0].shape[0])

        def north(q):
            return jnp.where(lane == 0, roll_up(v.whole(q, before(t, tiles))), roll_up(x[q]))

        def south(q):
            return jnp.where(
                lane == LANES - 1, roll_down(v.whole(q, after(t, tiles))), roll_down(x[q])
            )

        beside = [
            (x[1] + north(1)) + (x[2] + col_prev(x[2])),
            (x[0] + south(0)) + (x[3] + col_prev(x[3])),
            (x[3] + north(3)) + (x[0] + col_next(x[0])),
            (x[2] + south(2)) + (x[1] + col_next(x[1])),
        ]
        r = [whole_s(q, t) - (whole_d(q, t) * x[q] - beside[q]) for q in range(4)]
        if t == tiles:
            c0[t] = ((col_prev(r[2]) + col_next(r[0])) + 3.0 * (r[0] + r[2]))[:rows]
            c1[t] = ((col_prev(r[3]) + col_next(r[1])) + 3.0 * (r[1] + r[3]))[:rows]
        else:
            for q in range(4):
                rest.put(q, t, r[q][:rows], r[q][rows:])
            columns_summed(t)

    full(0)
    up = [roll_up(x) for x in v.ends(1, 0)]
    down = [roll_down(x) for x in v.ends(2, 1)]
    for t in range(1, tiles - 1):
        x = [v.ends(q, t) for q in range(4)]
        up_here = [roll_up(part) for part in x[1]]
        down_next = [roll_down(part) for part in v.ends(2, t + 1)]
        for q, ns, near, edge, lane_at in (
            (0, 1, up_here, up, 0), (3, 2, down, down_next, LANES - 1)
        ):
            cols = v.beside_columns(q, t, x[q ^ 2][1])
            r = []
            for i, (s, d) in enumerate(zip(load_s(q, t), load_d(q, t))):
                lane = lane_ids(s.shape[0])
                beside = x[ns][i] + jnp.where(lane == lane_at, edge[i], near[i]) + cols[i]
                r.append(s - (d * x[q][i] - beside))
            rest.put(q, t, *r)
        columns_summed(t)
        up, down = up_here, down_next
    full(tiles - 1)
    full(tiles)


def fine_kernel(
    s_ref, d_ref, i_ref, d1_ref, i1_ref, d2_ref,
    from_other, from_mate, polar_ref, corner_near, corner_far,
    r_ref, s1_ref, d1_virtual, d2_virtual, s2_ref, to_mate, to_other,
    v_ref, hv, pv, hr, c0, c1, hs, hd, hi, ps, pd, pi, n1, temp,
    w_ref, wv, rest1, e0, e1, pi1, black_even, black_odd, red_even, red_odd,
):
    tiles, columns = s_ref.shape[1], s_ref.shape[2]
    rows = columns // 2
    sub = row_ids(8)
    odd = is_odd()

    def halo(t, _):
        fill_halo(t, from_mate, from_other, odd, False, hs, hd, hi)
        return 0

    loop(tiles, halo, 0, 8)
    total = -16.0
    for q in range(4):
        own_s, own_d = polar_unpacked(polar_ref, q)
        near_s, near_d = polar_unpacked(corner_near, q)
        far_s, far_d = polar_unpacked(corner_far, q)
        left_s, right_s = chosen(odd, near_s, far_s)
        left_d, right_d = chosen(odd, near_d, far_d)
        total = total + own_d
        ps[q] = own_s
        pd[q] = own_d
        pi[q] = inverse_of(own_d)
        source = jnp.where(sub >= 5, left_s, jnp.where(sub <= 2, right_s, 0.0))
        diag = jnp.where(sub >= 5, left_d, jnp.where(sub <= 2, right_d, 4.0))
        hs[q, tiles] = source
        hd[q, tiles] = diag
        hi[q, tiles] = inverse_of(diag)

    def loaders(ref, halo, virtual):
        def split(q, t):
            return ref[q % 2, t, pl.ds(q // 2, rows, 2), :], halo[q, t]

        def whole(q, t):
            if t == tiles:
                return jnp.concatenate([virtual[q], halo[q, t]], 0)
            return jnp.concatenate(split(q, t), 0)

        return split, whole

    load_s, whole_s = loaders(s_ref, hs, ps)
    load_d, whole_d = loaders(d_ref, hd, pd)
    load_i, whole_i = loaders(i_ref, hi, pi)

    def held(own_ref, halo_ref):
        return Fine(
            [own_ref.at[p] for p in (0, 1)],
            [halo_ref.at[q] for q in range(4)],
            [pv.at[q] for q in range(4)],
            tiles,
            columns,
        )

    v, rest = held(v_ref, hv), held(r_ref, hr)
    for t in range(tiles):
        for q in (0, 3):
            v.put(q, t, *[x * i for x, i in zip(load_s(q, t), load_i(q, t))])
    for q in (1, 2):
        for t in (0, tiles - 1):
            v.put(q, t, jnp.zeros((rows, LANES), F32), jnp.zeros((8, LANES), F32))
        pv[q] = whole_s(q, tiles) * whole_i(q, tiles)
        pv[3 * (q - 1)] = jnp.zeros((rows + 8, LANES), F32)
    for red, left in ((False, None), (True, None), (False, (load_d, rest))):
        fine_sweep(v, load_s, load_i, whole_s, whole_i, red, left)
    fine_residuals(v, load_s, load_d, whole_s, whole_d, rest, c0, c1)

    def coarse(t, value):
        n1[t] = value

    restrict(c0, c1, tiles, rows, coarse, tiles)

    def use(c, source):
        for q in range(4):
            s1_ref[q, c] = source[q]

    tiles1 = tiles // 2
    split_tiles(lambda t: n1[t], tiles1, rows, splitter(), temp, use)
    out = moved(jnp.concatenate([n1[tiles], total], 0), virtual_splitter())
    source = quarters_of(out[:rows], temp.at[0])
    screen = quarters_of(out[rows:], temp.at[1])
    for q in range(4):
        s1_ref[q, tiles1] = source[q]
        d1_virtual[q] = 4.0 + screen[q]
        pi1[q] = inverse_of(4.0 + screen[q])
    d2_virtual[...] = 4.0 + ((screen[0] + screen[1]) + (screen[2] + screen[3]))

    def own(main, virtual):
        return lambda q, t: virtual[q] if isinstance(t, int) and t == tiles1 else main[q, t]

    rows1 = rows // 2
    w, rest1 = Ring(w_ref, wv, tiles1, rows1), Ring(rest1, wv, tiles1, rows1)
    row = row_ids(rows1)
    load_s, load_d = own(s1_ref, s1_ref.at[:, tiles1]), own(d1_ref, d1_virtual)

    def after_sweep(sweep):
        if sweep == 0:
            for t in range(tiles1 + 1):
                even, odd_red = reds(t == tiles1)
                black_even[t] = w.whole(even ^ 1, t)
                black_odd[t] = w.whole(odd_red ^ 1, t)

    ring_smooth(w, load_s, own(i1_ref, pi1), load_d, rest1, after_sweep)

    def valid(q, virtual):
        even, odd_red = reds(virtual)
        first = 1 if q == odd_red ^ 1 else 2
        last = rows1 - 2 if q == even ^ 1 else rows1 - 3
        return (row >= first) & (row <= last)

    def keep_red(t, r):
        even, odd_red = reds(isinstance(t, int) and t == tiles1)
        red_even[t] = r[even]
        red_odd[t] = r[odd_red]

    ring_residuals(w, load_s, load_d, rest1, e0, e1, keep_red, valid)
    shared = {}

    def edges(t, partial):
        virtual = t == tiles1
        even, odd_red = reds(virtual)
        s2_ref[t] = partial
        packs = state_packs(
            [s1_ref[q, t] for q in range(4)],
            [load_d(q, t) for q in range(4)],
            [w.whole(q, t) for q in range(4)],
            {even ^ 1: black_even[t], odd_red ^ 1: black_odd[t]},
            {even: red_even[t], odd_red: red_odd[t]},
            partial,
            d2_virtual[...] if virtual else d2_ref[t],
            virtual,
        )
        right, left = packs
        count = tiles1 + 1
        for i in (0, 1):
            to_mate[i * count + t], to_other[i * count + t] = chosen(odd, left[i], right[i])
        if t % 2 == 0:
            pair = chosen(odd, left[2], roll_rows(right[2], 4))
            shared[0] = pair
        else:
            pair = chosen(odd, roll_rows(left[2], 4), right[2])
            pair = [jnp.where(sub < 4, x, y) for x, y in zip(shared[0], pair)]
        if t % 2 == 1 or virtual:
            to_mate[2 * count + t // 2], to_other[2 * count + t // 2] = pair

    restrict(e0, e1, tiles1, rows1, edges, 16)


def merge_kernel(r_ref, out_ref, out_buf, sems):
    tiles = r_ref.shape[1]
    columns = out_ref.shape[0]
    matrix = merger()
    chunk = out_ref.shape[1] // GROUPS
    copies = []
    for group in range(GROUPS):
        for batch in range(tiles // GROUPS // BATCH):
            start = group * (tiles // GROUPS) + batch * BATCH
            own = slice(8, 8 + columns)
            both = [
                jnp.concatenate([r_ref[0, start + i, own], r_ref[1, start + i, own]], 1)
                for i in range(BATCH)
            ]
            out = moved(jnp.concatenate(both, 0), matrix)
            for i in range(BATCH):
                where = slice((start + i) * 256, (start + i + 1) * 256)
                out_buf[:, where] = out[columns * i : columns * (i + 1)]
        part = pl.ds(group * chunk, chunk)
        copy = pltpu.make_async_copy(out_buf.at[:, part], out_ref.at[:, part], sems.at[group])
        copy.start()
        copies.append(copy)
    for copy in copies:
        copy.wait()


def coarse_kernel(
    s_ref, d_ref, i_ref, d_virtual, d2_ref, d2_virtual, s2_ref, from_other, from_mate,
    solution_ref, residual_ref,
    v_ref, vv, rest, c0, c1, hs, hd, hi, part, fixes, s, d, inv, va, vb,
):
    tiles, own = d_ref.shape[1], d_ref.shape[2]
    v, rest = Ring(v_ref, vv, tiles, 16), Ring(rest, vv, tiles, 16)
    rows = own + 8
    count = tiles + 1
    sub = row_ids(8)
    odd_band = is_odd()
    def rim(x):
        return jnp.where(sub < 4, x[:8], x[own - 8 :])

    for t in range(count):
        places = t, count + t, 2 * count + t // 2
        packs = [chosen(odd_band, from_mate[i], from_other[i]) for i in places]
        source = [jnp.zeros((8, LANES), F32)] * 4
        diag = [jnp.full((8, LANES), 4.0, F32)] * 4
        inverse = [jnp.zeros((8, LANES), F32)] * 4
        fixed = [jnp.zeros((8, LANES), F32)] * 4
        more = jnp.zeros((8, LANES), F32)
        total = jnp.ones((8, LANES), F32)
        for side, (a, ab, b, bb) in enumerate(sides(t == tiles)):
            near, far, step = (7, 6, -1) if side == 0 else (0, 1, 1)
            first = 6 if side == 0 else 0
            pack0, pack1, pack2 = (pair[side] for pair in packs)
            groups = [
                roll_rows(pack, first - 2 * g) for pack in (pack0, pack1) for g in range(4)
            ]
            pack2 = roll_rows(pack2, 4 * (t % 2) + (4 if side == 0 else 0))

            def put(group, q, at, x):
                group[q] = jnp.where(sub == at, x, group[q])

            for q in range(4):
                put(source, q, near, groups[q])
                put(diag, q, near, groups[4 + q])
            put(source, bb, far, groups[0])
            put(diag, bb, far, groups[1])
            put(fixed, bb, far, groups[2])
            put(fixed, b, far, groups[3])
            put(source, b, far, groups[4])
            put(diag, b, far, 0.0)
            put(source, a, far, groups[5])
            put(fixed, ab, near, pack2)
            more = jnp.where(sub == far, groups[6], more)
            more = jnp.where((sub == far + step) | (sub == far + 2 * step), pack2, more)
            total = jnp.where(sub == far, pack2, total)
            total = jnp.where(sub == far + step, roll_rows(groups[7], step), total)
            for q in range(4):
                known = (sub == near) | (sub == far) if q == bb else sub == near
                inverse[q] = jnp.where(known, inverse_of(diag[q]), inverse[q])
        for q in range(4):
            own_d = rim(d_virtual[q] if t == tiles else d_ref[q, t])
            own_i = inverse_of(own_d) if t == tiles else rim(i_ref[q, t])
            hs[q, t] = jnp.concatenate([source[q], rim(s_ref[q, t])], 0)
            hd[q, t] = jnp.concatenate([diag[q], own_d], 0)
            hi[q, t] = jnp.concatenate([inverse[q], own_i], 0)
            fixes[q, t] = fixed[q]
        part[t] = more
        near_total = (diag[0] + diag[1]) + (diag[2] + diag[3]) - 12.0
        total = jnp.where((sub == 0) | (sub == 7), near_total, total)
        here = d2_virtual[...] if t == tiles else d2_ref[t]
        d[t] = jnp.concatenate([here, total], 0)

    def after_sweep(sweep):
        if sweep == 2:
            return
        for t in range(count):
            (a, ab, b, bb), (_, _, other_b, other_bb) = sides(t == tiles)
            todo = {}
            if sweep == 0:
                todo = {ab: (sub == 7) | (sub == 1), bb: (sub == 6) | (sub == 0)}
            else:
                todo = {b: sub == 6, other_b: sub == 1}
            for q, mask in todo.items():
                if t == tiles:
                    vv[q, :8] = jnp.where(mask, fixes[q, t], vv[q, :8])
                else:
                    place = pl.ds(8 + q // 2, 8, 2)
                    x = v_ref[q % 2, t, place, :]
                    v_ref[q % 2, t, place, :] = jnp.where(mask, fixes[q, t], x)

    def of(ref):
        return lambda q, t: ref[q, t]

    ring_smooth(v, of(hs), of(hi), of(hd), rest, after_sweep)
    row = row_ids(16)

    def valid(q, virtual):
        even, odd_red = reds(virtual)
        after_band = 0 if q == odd_red ^ 1 else 1
        before_band = 7 if q == even ^ 1 else 6
        first = 8 if q == odd_red ^ 1 else 9
        last = 15 if q == even ^ 1 else 14
        return (row <= after_band) | ((row >= before_band) & (row <= first)) | (row >= last)

    ring_residuals(v, of(hs), of(hd), rest, c0, c1, lambda t, r: None, valid)

    lane, row = lane_ids(rows), row_ids(rows)
    even = (lane + row) % 2 == 0
    odd = jnp.logical_not(even)

    def start(t, value):
        ends = value[8:]
        source = jnp.concatenate(
            [
                s2_ref[t, :8] + jnp.where(sub < 4, ends, 0.0),
                s2_ref[t, own - 8 :] + jnp.where(sub >= 4, ends, 0.0),
                value[:8] + part[t],
            ],
            0,
        )
        inverse = inverse_of(d[t])
        s[t] = source
        inv[t] = inverse
        virtual = isinstance(t, int) and t == tiles
        va[t] = jnp.where(odd if virtual else even, source * inverse, 0.0)

    restrict(c0, c1, tiles, 16, start, 16)

    def scan(v, use):
        up, down = roll_up(v[tiles]), roll_down(v[0])
        for t in range(tiles + 1):
            x = v[t]
            up_here, down_next = roll_up(x), roll_down(v[after(t, tiles)])
            north = jnp.where(lane == 0, up, up_here)
            south = jnp.where(lane == LANES - 1, down_next, down)
            use(t, x, (col_prev(x) + col_next(x)) + (north + south))
            up, down = up_here, down_next

    for old, new, mask, other in ((va, vb, odd, even), (vb, va, even, odd), (va, vb, odd, even)):

        def relax(t, x, beside):
            update = other if t == tiles else mask
            new[t] = jnp.where(update, (s[t] + beside) * inv[t], x)

        scan(old, relax)

    def finish(t, x, beside):
        if t < tiles:
            where = slice(t * LANES, (t + 1) * LANES)
            solution_ref[:, where] = x[:own]
            residual_ref[:, where] = (s[t] - (d[t] * x - beside))[:own]

    scan(vb, finish)


VMEM = pl.BlockSpec(memory_space=pltpu.VMEM)
HBM = pl.BlockSpec(memory_space=pltpu.HBM)


def call(kernel, out_shapes, scratch, *args, sems=None, far_in=0, far_out=0):
    scratch = [pltpu.VMEM(x, F32) if isinstance(x, tuple) else x for x in scratch]
    if sems is not None:
        scratch.append(pltpu.SemaphoreType.DMA(sems))
    return pl.pallas_call(
        kernel,
        out_shape=[jax.ShapeDtypeStruct(shape, F32) for shape in out_shapes],
        in_specs=[HBM] * far_in + [VMEM] * (len(args) - far_in),
        out_specs=[HBM] * far_out + [VMEM] * (len(out_shapes) - far_out),
        scratch_shapes=scratch,
        compiler_params=pltpu.CompilerParams(vmem_limit_bytes=40 * 2**20),
    )(*args)


def swapped_with(x, by):
    count = lax.axis_size("lon")
    pairs = [(i, (i + by) % count) for i in range(0, count, 2)]
    return lax.ppermute(x, "lon", pairs + [(b, a) for a, b in pairs])


def swapped_edges(to_mate, to_other):
    from_mate = swapped_with(to_mate, 1)
    return from_mate, swapped_with(to_other, -1)


def body(right_side, texel_weight, seam_flags):
    columns, height = right_side.shape
    half_turn = lax.axis_size("lon") // 2
    tiles, rows = height // 256, columns // 2
    tiles1, rows1 = tiles // 2, rows // 2
    temp = (BATCH, 2, columns, LANES)
    natural = (2, tiles, columns, LANES)
    padded = (2, tiles, columns + 16, LANES)
    quarters1 = (4, tiles1, rows1, LANES)
    split = (2, 16 * tiles, LANES)
    to_mate, to_other, corner = call(
        edge_kernel,
        [(2, tiles, 8, LANES), (2, tiles, 8, LANES), (2, 8, LANES)],
        [(16, height), pltpu.VMEM((32, height), BF16)]
        + [pltpu.VMEM(seam_flags.shape, jnp.int32), split, split, (tiles, 8, LANES)],
        *[
            pltpu.with_memory_space_constraint(x, pltpu.HBM)
            for x in (right_side, texel_weight, seam_flags)
        ],
        sems=(5,), far_in=3,
    )
    from_mate, from_other = swapped_edges(to_mate, to_other)
    corner_far = swapped_with(corner, half_turn - 1)
    corner_near = swapped_with(corner, half_turn + 1)
    ends = (2, 2, columns, LANES)
    (polar_own,) = call(
        polar_kernel, [(2, rows, LANES)], [ends, ends],
        right_side, texel_weight, seam_flags, corner,
    )
    polar = lax.ppermute(
        polar_own, "lon", [(i, (i + half_turn) % (2 * half_turn)) for i in range(2 * half_turn)]
    )
    s, d, inverse, d1, i1, d2 = call(
        bulk_kernel,
        [natural] * 3 + [quarters1, quarters1, quarters1[1:]],
        [(BATCH, columns, LANES), (tiles, 8, LANES), (tiles, rows, LANES), (BATCH, 2, rows, LANES)],
        right_side, texel_weight, seam_flags, polar_own,
    )

    ring = [(2, tiles1, 2 * rows1 + 16, LANES), (4, rows1, LANES)]
    ring += [ring[0], (tiles1 + 1, rows1, LANES), (tiles1 + 1, rows1, LANES)]

    def halo_scratch(tiles):
        return [(4, tiles + 1, 8, LANES)] * 3

    pack1 = (2 * (tiles1 + 1) + tiles1 // 2 + 1, 8, LANES)
    r, s1, d1_virtual, d2_virtual, s2_own, to_mate, to_other = call(
        fine_kernel,
        [padded, (4, tiles1 + 1, rows1, LANES), (4, rows1, LANES), (rows1, LANES)]
        + [(tiles1 + 1, rows1, LANES), pack1, pack1],
        [padded, (4, tiles, 8, LANES), (4, rows + 8, LANES), (4, tiles, 8, LANES)]
        + [(tiles + 1, rows, LANES)] * 2
        + halo_scratch(tiles)
        + [(4, rows, LANES)] * 3
        + [(tiles + 1, rows, LANES), (BATCH, 2, rows, LANES)]
        + ring
        + [(4, rows1, LANES)]
        + [(tiles1 + 1, rows1, LANES)] * 4,
        s, d, inverse, d1, i1, d2, from_other, from_mate, polar, corner_near, corner_far,
    )
    from_mate, from_other = swapped_edges(to_mate, to_other)
    (fine_residual,) = call(
        merge_kernel, [(columns, height)], [(columns, height)], r,
        sems=(GROUPS,), far_out=1,
    )
    wide = (tiles1 + 1, rows1 + 8, LANES)
    solution_2, residual_2 = call(
        coarse_kernel,
        [(columns // 4, height // 4)] * 2,
        ring
        + [(4, tiles1 + 1, 16, LANES)] * 3
        + [(tiles1 + 1, 8, LANES), (4, tiles1 + 1, 8, LANES)]
        + [wide] * 5,
        s1, d1, i1, d1_virtual, d2, d2_virtual, s2_own, from_other, from_mate,
    )
    return fine_residual, solution_2, residual_2


def solution(mesh):
    spec = P(("groups", "lon"), None)
    return jax.shard_map(
        body, mesh=mesh, in_specs=(spec,) * 3, out_specs=(spec,) * 3, check_vma=False
    )
```

```python
import jax
import jax.numpy as jnp
from jax import lax
from jax.experimental import pallas as pl
from jax.experimental.pallas import tpu as pltpu
from jax.sharding import PartitionSpec as P

TILE = 32
SEAM_SCALE = 0.1
LANES = 128
GROUPS = 4
BATCH = 4
F32 = jnp.float32
BF16 = jnp.bfloat16


def loop(count, body, carry=0, unroll=4):
    unroll = min(unroll, count)

    def steps(block, carry):
        for i in range(unroll):
            carry = body(block * unroll + i, carry)
        return carry

    whole = count // unroll
    carry = steps(0, carry) if whole == 1 else lax.fori_loop(0, whole, steps, carry)
    for t in range(whole * unroll, count):
        carry = body(t, carry)
    return carry


def before(t, tiles):
    return (tiles if t == 0 else t - 1) if isinstance(t, int) else jnp.where(t == 0, tiles, t - 1)


def after(t, tiles):
    return (0 if t == tiles else t + 1) if isinstance(t, int) else t + 1


def lane_ids(rows):
    return lax.broadcasted_iota(jnp.int32, (rows, LANES), 1)


def row_ids(rows):
    return lax.broadcasted_iota(jnp.int32, (rows, LANES), 0)


def roll_up(x):
    return pltpu.roll(x, 1, 1)


def roll_down(x):
    return pltpu.roll(x, LANES - 1, 1)


def roll_rows(x, by):
    by %= x.shape[0]
    return x if by == 0 else pltpu.roll(x, by, 0)


def roll_lanes(x, by):
    by %= LANES
    return x if by == 0 else pltpu.roll(x, by, 1)


def col_prev(x):
    return pltpu.roll(x, 1, 0)


def col_next(x):
    return pltpu.roll(x, x.shape[0] - 1, 0)


def inverse_of(x):
    return 1.0 / x


def selector(shape, rule):
    a = lax.broadcasted_iota(jnp.int32, shape, 0)
    b = lax.broadcasted_iota(jnp.int32, shape, 1)
    return jnp.where(rule(a, b), 1.0, 0.0).astype(BF16)


def splitter():
    return selector((256, 256), lambda a, b: a == 2 * (b % LANES) + b // LANES)


def merger():
    return selector((256, 256), lambda a, b: b == 2 * (a % LANES) + a // LANES)


def virtual_splitter():
    return selector(
        (LANES, 256),
        lambda a, b: a // 2 + jnp.where(a >= 64, 64, 0) + LANES * (a % 2) == b,
    )


def moved(x, matrix, exact=None):
    rows = x.shape[0]
    high = x.astype(BF16)
    low = (x - high.astype(F32)).astype(BF16)
    terms = [high, low] if exact is None else [high, low, exact]
    out = jnp.dot(jnp.concatenate(terms, 0), matrix, preferred_element_type=F32)
    both = out[:rows] + out[rows : 2 * rows]
    return both if exact is None else (both, out[2 * rows :])


def quarters_of(parts, temp):
    count = parts.shape[0] // 2
    temp[0] = parts[:, :LANES]
    temp[1] = parts[:, LANES:]
    return [temp[pr, pl.ds(pc, count, 2), :] for pc in (0, 1) for pr in (0, 1)]


def reds(swapped):
    return (1, 2) if swapped else (0, 3)


def interleaved(group, offset):
    sub = row_ids(8)
    packed = roll_rows(group[0], offset)
    for q in range(1, 4):
        packed = jnp.where(sub // 2 == q, roll_rows(group[q], 2 * q + offset), packed)
    return packed


def edge_packs(source, diag, swapped):
    sub = row_ids(8)
    even, odd = reds(swapped)
    rows = source[0].shape[0]
    packs = []
    for here, first, second, row, step in (
        (slice(rows - 8, rows), even, odd, 6, 1),
        (slice(0, 8), odd, even, 1, -1),
    ):
        gs = [x[here] for x in source]
        gd = [x[here] for x in diag]
        near = gs[first] * inverse_of(gd[first])
        far = roll_rows(gs[second] * inverse_of(gd[second]), step)
        gs[first] = jnp.where(sub == row, near, gs[first])
        gd[first] = jnp.where(sub == row, far, gd[first])
        offset = 2 if row == 6 else 0
        packs.append((interleaved(gs, offset), interleaved(gd, offset)))
    return packs


def unpacked_halo(left, right, swapped):
    sub = row_ids(8)
    even, odd = reds(swapped)
    (al, bl), (ar, br) = left, right
    source, diag = [], []
    for q in range(4):
        s = jnp.where(
            sub >= 6,
            roll_rows(al, 6 - 2 * q),
            jnp.where(sub <= 1, roll_rows(ar, -2 * q), 0.0),
        )
        d = jnp.where(
            sub >= 6,
            roll_rows(bl, 6 - 2 * q),
            jnp.where(sub <= 1, roll_rows(br, -2 * q), 4.0),
        )
        if q == even:
            s = jnp.where(sub == 2, roll_rows(br, 1 - 2 * odd), s)
            d = jnp.where((sub == 2) | (sub == 6), 1.0, d)
        if q == odd:
            s = jnp.where(sub == 5, roll_rows(bl, 5 - 2 * even), s)
            d = jnp.where((sub == 5) | (sub == 1), 1.0, d)
        source.append(s)
        diag.append(d)
    return source, diag


def is_odd():
    return lax.rem(lax.axis_index("lon"), 2) == 1


def chosen(odd, a, b):
    return jnp.where(odd, a, b), jnp.where(odd, b, a)


def store_edges(t, packs, odd, to_mate, to_other):
    right, left = packs
    for i in (0, 1):
        to_mate[i, t], to_other[i, t] = chosen(odd, left[i], right[i])


def sides(swapped):
    even, odd = reds(swapped)
    return (even, even ^ 1, odd, odd ^ 1), (odd, odd ^ 1, even, even ^ 1)


def paired(groups, shift):
    sub = row_ids(8)
    packed = roll_rows(groups[0], shift)
    for g in (1, 2, 3):
        packed = jnp.where(sub // 2 == g, roll_rows(groups[g], 2 * g + shift), packed)
    return packed


def state_packs(source, diag, last, first_black, residual, partial, diag2, swapped):
    sub = row_ids(8)
    rows = source[0].shape[0]
    packs = []
    for (a, ab, b, bb), here, near, far, step in zip(
        sides(swapped), (slice(rows - 8, rows), slice(0, 8)), (7, 0), (6, 1), (-1, 1)
    ):
        s, d, v = ([x[here] for x in group] for group in (source, diag, last))
        part, d2 = partial[here], diag2[here]
        beside = [
            s[bb] + v[a],
            d[bb],
            first_black[bb][here],
            v[b],
            s[b] - d[b] * v[b] + v[ab],
            residual[a][here] - v[bb],
            part,
            roll_rows(d2, -step),
        ]
        groups = [jnp.where(sub == far, y, x) for x, y in zip(s + d, beside)]
        shift = 2 if near == 7 else 0
        more = jnp.where(sub == far, d2, first_black[ab][here])
        more = jnp.where(sub == far + step, part, more)
        more = jnp.where(sub == far + 2 * step, part * inverse_of(d2), more)
        packs.append((paired(groups[:4], shift), paired(groups[4:], shift), more))
    return packs


def fill_halo(t, from_mate, from_other, odd, swapped, hs, hd, hi):
    al, ar = chosen(odd, from_mate[0, t], from_other[0, t])
    bl, br = chosen(odd, from_mate[1, t], from_other[1, t])
    source, diag = unpacked_halo((al, bl), (ar, br), swapped)
    for q in range(4):
        hs[q, t] = source[q]
        hd[q, t] = diag[q]
        hi[q, t] = inverse_of(diag[q])


def loader(own, halo, virtual, tiles):
    def load(q, t):
        if isinstance(t, int) and t == tiles:
            return jnp.concatenate([virtual[q], halo[q, t]], 0)
        return jnp.concatenate([own[q, t], halo[q, t]], 0)

    return load


def polar_packs(tiles_of):
    lane = lane_ids(tiles_of[0][0].shape[0])
    packs = []
    for pc in (0, 1):
        parts = [*tiles_of[2 * pc], *tiles_of[2 * pc + 1]]
        packed = parts[0]
        for m in range(1, 4):
            mine = (lane + (16 - 32 * m) % LANES) % LANES < 32
            packed = jnp.where(mine, roll_lanes(parts[m], 32 * m), packed)
        packs.append(packed)
    return packs


def polar_unpacked(x, q):
    lane = lane_ids(x.shape[1])
    used = (lane < 16) | (lane >= LANES - 16)
    m = 2 * (q % 2)
    return (
        jnp.where(used, roll_lanes(x[q // 2], 32 * m), 0.0),
        jnp.where(used, roll_lanes(x[q // 2], 32 * (m + 1)), 4.0),
    )


def seam_scales(flags, chunks):
    flag_cols, flag_lats = flags.shape
    flags = jnp.concatenate(
        [flags.astype(F32), jnp.zeros((8 - flag_cols, flag_lats), F32)], 0
    )
    lat = lax.broadcasted_iota(jnp.int32, (8, flag_lats), 1)
    stacked = jnp.concatenate([jnp.where(lat // 8 == c, flags, 0.0) for c in chunks], 0)
    spread = selector((flag_lats, LANES), lambda a, b: a % 8 == b // (TILE // 2))
    spread_flags = jnp.dot(stacked.astype(BF16), spread, preferred_element_type=F32)
    scale = jnp.where(spread_flags > 0.5, SEAM_SCALE, 1.0)
    return scale.reshape(len(chunks), 8, LANES)


def seam_rows(scales, flag_cols, rows):
    size = (rows // flag_cols, LANES)
    return jnp.concatenate(
        [jnp.broadcast_to(scales[i : i + 1], size) for i in range(flag_cols)], 0
    )


def edge_kernel(
    right_ref, weight_ref, flag_ref,
    to_mate, to_other, corner_ref,
    edge_s, edge_w, flags, temp_s, temp_w, scale_ref, sems,
):
    columns, height = right_ref.shape
    tiles = height // 256
    pairs = [(flag_ref, flags)]
    for i, (src, dst, size) in enumerate(
        ((right_ref, edge_s, 8), (weight_ref, edge_w, 16))
    ):
        pairs.append((src.at[pl.ds(0, size)], dst.at[pl.ds(0, size)]))
        pairs.append((src.at[pl.ds(columns - size, size)], dst.at[pl.ds(size, size)]))
    copies = [
        pltpu.make_async_copy(src, dst, sems.at[i]) for i, (src, dst) in enumerate(pairs)
    ]
    for copy in copies:
        copy.start()
    odd = is_odd()
    matrix = splitter()
    flag_cols = flag_ref.shape[0]
    copies[0].wait()
    scale_ref[...] = seam_scales(flags[...], range(tiles))
    for copy in copies[1:]:
        copy.wait()
    sub = row_ids(8)
    lanes = [slice(c * 256, (c + 1) * 256) for c in range(tiles)]
    source, weight = moved(
        jnp.concatenate([edge_s[:, w] for w in lanes], 0),
        matrix,
        jnp.concatenate([edge_w[:, w] for w in lanes], 0),
    )
    weight = weight.reshape(tiles, 32, 256)
    weight = jnp.concatenate([weight[:, :8], weight[:, 24:]], 1).reshape(tiles * 16, 256)
    source = quarters_of(source, temp_s)
    weight = quarters_of(weight, temp_w)
    found = []
    for c in range(tiles):
        here = slice(c * 8, (c + 1) * 8)
        scales = scale_ref[c]
        scale = jnp.where(sub < 4, scales[:1], scales[flag_cols - 1 : flag_cols])
        pair = [x[here] for x in source], [4.0 + w[here] * scale for w in weight]
        store_edges(c, edge_packs(*pair, False), odd, to_mate, to_other)
        if c in (0, tiles - 1):
            found.append(pair)
    both = mirrored_ends(*found)
    for pc in (0, 1):
        corner = both[8 * pc : 8 * (pc + 1)]
        corner_ref[pc] = corner


def mirrored_ends(first, last):
    mirror = selector((LANES, LANES), lambda a, b: a + b == LANES - 1)
    lane = lane_ids(first[0][0].shape[0])
    ends = [
        [jnp.where(lane >= 64, last[i][q ^ 1], first[i][q ^ 1]) for i in (0, 1)]
        for q in range(4)
    ]
    return moved(jnp.concatenate(polar_packs(ends), 0), mirror)


def polar_kernel(right_ref, weight_ref, flag_ref, edges_first, polar_ref, temp_s, temp_w):
    columns, height = right_ref.shape
    rows, tiles = columns // 2, height // 256
    scales = seam_scales(flag_ref[...], (0, tiles - 1))
    lanes = slice(0, 256), slice(height - 256, height)
    source, weight = moved(
        jnp.concatenate([right_ref[:, w] for w in lanes], 0),
        splitter(),
        jnp.concatenate([weight_ref[:, w] for w in lanes], 0),
    )
    found = []
    for end in (0, 1):
        here = slice(end * columns, (end + 1) * columns)
        scale = seam_rows(scales[end], flag_ref.shape[0], rows)
        found.append(
            (
                quarters_of(source[here], temp_s.at[end]),
                [4.0 + w * scale for w in quarters_of(weight[here], temp_w.at[end])],
            )
        )
    both = mirrored_ends(*found)
    for pc in (0, 1):
        polar_ref[pc] = both[pc * rows : (pc + 1) * rows]


def bulk_kernel(
    right_ref, weight_ref, flag_ref, polar_first,
    s_ref, d_ref, i_ref, d1_ref, i1_ref, d2_ref,
    temp, scale_ref, e_ref, split_temp,
):
    tiles, columns = s_ref.shape[1], s_ref.shape[2]
    rows = columns // 2
    matrix = splitter()
    scale_ref[...] = seam_scales(flag_ref[...], range(tiles))
    for start in range(0, tiles, BATCH):
        lanes = [slice((start + i) * 256, (start + i + 1) * 256) for i in range(BATCH)]
        source, weight = moved(
            jnp.concatenate([right_ref[:, w] for w in lanes], 0),
            matrix,
            jnp.concatenate([weight_ref[:, w] for w in lanes], 0),
        )
        for i in range(BATCH):
            c = start + i
            here = slice(i * columns, (i + 1) * columns)
            scale = seam_rows(scale_ref[c], flag_ref.shape[0], columns)
            screens = []
            for pr in (0, 1):
                half = slice(pr * LANES, (pr + 1) * LANES)
                screen = weight[here, half] * scale
                diag = 4.0 + screen
                s_ref[pr, c] = source[here, half]
                d_ref[pr, c] = diag
                i_ref[pr, c] = 1.0 / diag
                screens.append(screen)
            temp[i] = screens[0] + screens[1]
            e_ref[c] = temp[i, pl.ds(0, rows, 2), :] + temp[i, pl.ds(1, rows, 2), :]

    def use(c, screen):
        for q in range(4):
            d1_ref[q, c] = 4.0 + screen[q]
            i1_ref[q, c] = inverse_of(4.0 + screen[q])
        d2_ref[c] = 4.0 + ((screen[0] + screen[1]) + (screen[2] + screen[3]))

    split_tiles(lambda t: e_ref[t], tiles // 2, rows, matrix, split_temp, use)


def split_tiles(load, tiles, rows, matrix, temp, use):
    for start in range(0, tiles, BATCH):
        wide = [
            jnp.concatenate([load(2 * c), load(2 * c + 1)], 1)
            for c in range(start, start + BATCH)
        ]
        out = moved(jnp.concatenate(wide, 0), matrix)
        for i in range(BATCH):
            use(start + i, quarters_of(out[i * rows : (i + 1) * rows], temp.at[i, :, :rows]))


def half_sweep(v, load_s, load_i, tiles, red, unroll, left=None):
    rows = v[0].shape[1]
    lane = lane_ids(rows)
    y, z, qa, qb = (1, 2, 0, 3) if red else (3, 0, 2, 1)
    col_a, col_b = (col_prev, col_next) if red else (col_next, col_prev)

    def beside_virtual(q):
        ns, we = q ^ 1, q ^ 2
        here = v[ns][tiles]
        if q % 2 == 0:
            lat = jnp.where(lane == 0, roll_up(v[ns][tiles - 1]), roll_up(here))
        else:
            lat = jnp.where(lane == LANES - 1, roll_down(v[ns][0]), roll_down(here))
        cols = v[we][tiles]
        return (here + lat) + (cols + (col_prev if q < 2 else col_next)(cols))

    held = [
        (q, (load_s(q, tiles) + beside_virtual(q)) * load_i(q, tiles)) for q in (y, z)
    ]

    def body(t, carry):
        y_before, z_here = carry
        vy, vz = v[y][t], v[z][t]
        y_here = roll_up(vy)
        z_after = roll_down(v[z][t + 1])
        lat_a = vy + jnp.where(lane == 0, y_before, y_here)
        lat_b = vz + jnp.where(lane == LANES - 1, z_after, z_here)
        all_a = load_s(qa, t) + (lat_a + (vz + col_a(vz)))
        all_b = load_s(qb, t) + (lat_b + (vy + col_b(vy)))
        new_a, new_b = all_a * load_i(qa, t), all_b * load_i(qb, t)
        v[qa][t], v[qb][t] = new_a, new_b
        if left is not None:
            load_d, rest = left
            rest[qa][t] = all_a - load_d(qa, t) * new_a
            rest[qb][t] = all_b - load_d(qb, t) * new_b
        return y_here, z_after

    loop(tiles, body, (roll_up(v[y][tiles]), roll_down(v[z][0])), unroll)
    for q, value in held:
        v[q][tiles] = value


def smooth(v, load_s, load_i, tiles, unroll, left, after_sweep=None):
    zeros = jnp.zeros(v[0].shape[1:], F32)

    def first(t, _):
        for q in (0, 3):
            v[q][t] = load_s(q, t) * load_i(q, t)
        return 0

    loop(tiles, first, 0, unroll)
    for q in (1, 2):
        v[q][0] = zeros
        v[q][tiles - 1] = zeros
        v[q][tiles] = load_s(q, tiles) * load_i(q, tiles)
        v[3 * (q - 1)][tiles] = zeros
    for sweep, red in enumerate((False, True, False)):
        half_sweep(v, load_s, load_i, tiles, red, unroll, left if sweep == 2 else None)
        if after_sweep is not None:
            after_sweep(sweep)


def residuals(v, load_s, left, tiles, c0, c1, keep, unroll, valid=None):
    lane = lane_ids(v[0].shape[1])
    load_d, rest = left

    def use(t, r):
        keep(t, r)
        if valid is not None:
            virtual = isinstance(t, int) and t == tiles
            r = [jnp.where(valid(q, virtual), r[q], 0.0) for q in range(4)]
        c0[t] = (col_prev(r[2]) + col_next(r[0])) + 3.0 * (r[0] + r[2])
        c1[t] = (col_prev(r[3]) + col_next(r[1])) + 3.0 * (r[1] + r[3])

    def north(q, t):
        return jnp.where(lane == 0, roll_up(v[q][before(t, tiles)]), roll_up(v[q][t]))

    def south(q, t):
        return jnp.where(
            lane == LANES - 1, roll_down(v[q][after(t, tiles)]), roll_down(v[q][t])
        )

    def full(t):
        x = [v[q][t] for q in range(4)]
        beside = [
            (x[1] + north(1, t)) + (x[2] + col_prev(x[2])),
            (x[0] + south(0, t)) + (x[3] + col_prev(x[3])),
            (x[3] + north(3, t)) + (x[0] + col_next(x[0])),
            (x[2] + south(2, t)) + (x[1] + col_next(x[1])),
        ]
        use(t, [load_s(q, t) - (load_d(q, t) * x[q] - beside[q]) for q in range(4)])

    def body(i, carry):
        t = i + 1
        up, down = carry
        x = [v[q][t] for q in range(4)]
        up_here, down_next = roll_up(x[1]), roll_down(v[2][t + 1])
        beside0 = (x[1] + jnp.where(lane == 0, up, up_here)) + (x[2] + col_prev(x[2]))
        beside3 = (x[2] + jnp.where(lane == LANES - 1, down_next, down)) + (
            x[1] + col_next(x[1])
        )
        r0 = load_s(0, t) - (load_d(0, t) * x[0] - beside0)
        r3 = load_s(3, t) - (load_d(3, t) * x[3] - beside3)
        use(t, [r0, rest[1][t], rest[2][t], r3])
        return up_here, down_next

    full(0)
    loop(tiles - 2, body, (roll_up(v[1][0]), roll_down(v[2][1])), unroll)
    full(tiles - 1)
    full(tiles)


def restrict(c0, c1, tiles, rows, use, unroll):
    lane = lane_ids(rows)

    def body(t, carry):
        up, down = carry
        here, other = c0[t, :rows], c1[t, :rows]
        up_here = roll_up(other)
        down_next = roll_down(c0[after(t, tiles), :rows])
        north = jnp.where(lane == 0, up, up_here)
        south = jnp.where(lane == LANES - 1, down_next, down)
        use(t, ((north + south) + 3.0 * (here + other)) * (1.0 / 16.0))
        return up_here, down_next

    start = roll_up(c1[tiles, :rows]), roll_down(c0[0, :rows])
    body(tiles, loop(tiles, body, start, unroll))


class Fine:
    def __init__(self, own, halo, virtual, tiles, columns):
        self.own, self.halo, self.virtual = own, halo, virtual
        self.tiles, self.columns = tiles, columns

    def part(self, parity, t, start):
        return self.own[parity][t, pl.ds(8 + start, self.columns // 2, 2), :]

    def rows(self, q, t):
        return self.part(q % 2, t, q // 2)

    def whole(self, q, t):
        if t == self.tiles:
            return self.virtual[q][...]
        return jnp.concatenate([self.rows(q, t), self.halo[q][t]], 0)

    def ends(self, q, t):
        if t == self.tiles:
            whole = self.virtual[q][...]
            return whole[: self.columns // 2], whole[self.columns // 2 :]
        return self.rows(q, t), self.halo[q][t]

    def line(self, parity, t, column):
        row = self.own[parity][t, 8 + column : 9 + column]
        return jnp.broadcast_to(row, (8, LANES))

    def put(self, q, t, own, halo):
        pr, pc = q % 2, q // 2
        self.own[pr][t, pl.ds(8 + pc, self.columns // 2, 2), :] = own
        self.halo[q][t] = halo
        if pc == 1:
            self.own[pr][t, 7:8] = halo[7:8]
        else:
            at = 8 + self.columns
            self.own[pr][t, at : at + 1] = halo[0:1]

    def beside_columns(self, q, t, halo):
        sub = row_ids(8)
        pr, pc = q % 2, q // 2
        own = self.part(pr, t, pc - 1) + self.part(pr, t, pc + 1)
        if pc == 0:
            other = jnp.where(sub == 0, self.line(pr, t, self.columns - 1), col_prev(halo))
        else:
            other = jnp.where(sub == 7, self.line(pr, t, 0), col_next(halo))
        return own, halo + other


def fine_sweep(v, load_s, load_i, whole_s, whole_i, red, left):
    tiles = v.tiles
    y, z, qa, qb = (1, 2, 0, 3) if red else (3, 0, 2, 1)

    def lane_sum(parts, rolled, edge, lane_at):
        return [
            x + jnp.where(lane_ids(x.shape[0]) == lane_at, e, r)
            for x, r, e in zip(parts, rolled, edge)
        ]

    def beside_virtual(q):
        here, cols = v.whole(q ^ 1, tiles), v.whole(q ^ 2, tiles)
        lane = lane_ids(here.shape[0])
        if q % 2 == 0:
            lat = jnp.where(lane == 0, roll_up(v.whole(q ^ 1, tiles - 1)), roll_up(here))
        else:
            lat = jnp.where(lane == LANES - 1, roll_down(v.whole(q ^ 1, 0)), roll_down(here))
        return (here + lat) + (cols + (col_prev if q < 2 else col_next)(cols))

    held = [
        (q, (whole_s(q, tiles) + beside_virtual(q)) * whole_i(q, tiles)) for q in (y, z)
    ]
    y_before = [roll_up(x) for x in v.ends(y, tiles)]
    z_here = [roll_down(x) for x in v.ends(z, 0)]
    for t in range(tiles):
        vy, vz = v.ends(y, t), v.ends(z, t)
        y_here = [roll_up(x) for x in vy]
        z_after = [roll_down(x) for x in v.ends(z, t + 1)]
        lat_a = lane_sum(vy, y_here, y_before, 0)
        lat_b = lane_sum(vz, z_here, z_after, LANES - 1)
        new = []
        for q, lat, halo in ((qa, lat_a, vz[1]), (qb, lat_b, vy[1])):
            cols = v.beside_columns(q, t, halo)
            total = [x + (l + c) for x, l, c in zip(load_s(q, t), lat, cols)]
            value = [x * i for x, i in zip(total, load_i(q, t))]
            new.append((q, value))
            if left is not None:
                load_d, rest = left
                rest.put(q, t, *[x - d * u for x, d, u in zip(total, load_d(q, t), value)])
        for q, value in new:
            v.put(q, t, *value)
        y_before, z_here = y_here, z_after
    for q, value in held:
        v.virtual[q][...] = value


def fine_residuals(v, load_s, load_d, whole_s, whole_d, rest, c0, c1):
    tiles = v.tiles
    rows = v.columns // 2

    def columns_summed(t):
        for pr, ref in ((0, c0), (1, c1)):
            outer = rest.part(pr, t, -1) + rest.part(pr, t, 2)
            inner = rest.part(pr, t, 0) + rest.part(pr, t, 1)
            ref[t] = outer + 3.0 * inner

    def full(t):
        x = [v.whole(q, t) for q in range(4)]
        lane = lane_ids(x[0].shape[0])

        def north(q):
            return jnp.where(lane == 0, roll_up(v.whole(q, before(t, tiles))), roll_up(x[q]))

        def south(q):
            return jnp.where(
                lane == LANES - 1, roll_down(v.whole(q, after(t, tiles))), roll_down(x[q])
            )

        beside = [
            (x[1] + north(1)) + (x[2] + col_prev(x[2])),
            (x[0] + south(0)) + (x[3] + col_prev(x[3])),
            (x[3] + north(3)) + (x[0] + col_next(x[0])),
            (x[2] + south(2)) + (x[1] + col_next(x[1])),
        ]
        r = [whole_s(q, t) - (whole_d(q, t) * x[q] - beside[q]) for q in range(4)]
        if t == tiles:
            c0[t] = ((col_prev(r[2]) + col_next(r[0])) + 3.0 * (r[0] + r[2]))[:rows]
            c1[t] = ((col_prev(r[3]) + col_next(r[1])) + 3.0 * (r[1] + r[3]))[:rows]
        else:
            for q in range(4):
                rest.put(q, t, r[q][:rows], r[q][rows:])
            columns_summed(t)

    full(0)
    up = [roll_up(x) for x in v.ends(1, 0)]
    down = [roll_down(x) for x in v.ends(2, 1)]
    for t in range(1, tiles - 1):
        x = [v.ends(q, t) for q in range(4)]
        up_here = [roll_up(part) for part in x[1]]
        down_next = [roll_down(part) for part in v.ends(2, t + 1)]
        for q, ns, near, edge, lane_at in (
            (0, 1, up_here, up, 0), (3, 2, down, down_next, LANES - 1)
        ):
            cols = v.beside_columns(q, t, x[q ^ 2][1])
            r = []
            for i, (s, d) in enumerate(zip(load_s(q, t), load_d(q, t))):
                lane = lane_ids(s.shape[0])
                beside = x[ns][i] + jnp.where(lane == lane_at, edge[i], near[i]) + cols[i]
                r.append(s - (d * x[q][i] - beside))
            rest.put(q, t, *r)
        columns_summed(t)
        up, down = up_here, down_next
    full(tiles - 1)
    full(tiles)


def fine_kernel(
    s_ref, d_ref, i_ref, d1_ref, i1_ref, d2_ref,
    from_other, from_mate, polar_ref, corner_near, corner_far,
    r_ref, s1_ref, d1_virtual, d2_virtual, s2_ref, to_mate, to_other,
    v_ref, hv, pv, hr, c0, c1, hs, hd, hi, ps, pd, pi, n1, temp,
    w0, w1, w2, w3, e0, e1, pi1, black_even, black_odd, red_even, red_odd,
    part1, part2,
):
    tiles, columns = s_ref.shape[1], s_ref.shape[2]
    rows = columns // 2
    sub = row_ids(8)
    odd = is_odd()

    def halo(t, _):
        fill_halo(t, from_mate, from_other, odd, False, hs, hd, hi)
        return 0

    loop(tiles, halo, 0, 8)
    total = -16.0
    for q in range(4):
        own_s, own_d = polar_unpacked(polar_ref, q)
        near_s, near_d = polar_unpacked(corner_near, q)
        far_s, far_d = polar_unpacked(corner_far, q)
        left_s, right_s = chosen(odd, near_s, far_s)
        left_d, right_d = chosen(odd, near_d, far_d)
        total = total + own_d
        ps[q] = own_s
        pd[q] = own_d
        pi[q] = inverse_of(own_d)
        source = jnp.where(sub >= 5, left_s, jnp.where(sub <= 2, right_s, 0.0))
        diag = jnp.where(sub >= 5, left_d, jnp.where(sub <= 2, right_d, 4.0))
        hs[q, tiles] = source
        hd[q, tiles] = diag
        hi[q, tiles] = inverse_of(diag)

    def loaders(ref, halo, virtual):
        def split(q, t):
            return ref[q % 2, t, pl.ds(q // 2, rows, 2), :], halo[q, t]

        def whole(q, t):
            if t == tiles:
                return jnp.concatenate([virtual[q], halo[q, t]], 0)
            return jnp.concatenate(split(q, t), 0)

        return split, whole

    load_s, whole_s = loaders(s_ref, hs, ps)
    load_d, whole_d = loaders(d_ref, hd, pd)
    load_i, whole_i = loaders(i_ref, hi, pi)

    def held(own_ref, halo_ref):
        return Fine(
            [own_ref.at[p] for p in (0, 1)],
            [halo_ref.at[q] for q in range(4)],
            [pv.at[q] for q in range(4)],
            tiles,
            columns,
        )

    v, rest = held(v_ref, hv), held(r_ref, hr)
    for t in range(tiles):
        for q in (0, 3):
            v.put(q, t, *[x * i for x, i in zip(load_s(q, t), load_i(q, t))])
    for q in (1, 2):
        for t in (0, tiles - 1):
            v.put(q, t, jnp.zeros((rows, LANES), F32), jnp.zeros((8, LANES), F32))
        pv[q] = whole_s(q, tiles) * whole_i(q, tiles)
        pv[3 * (q - 1)] = jnp.zeros((rows + 8, LANES), F32)
    for red, left in ((False, None), (True, None), (False, (load_d, rest))):
        fine_sweep(v, load_s, load_i, whole_s, whole_i, red, left)
    fine_residuals(v, load_s, load_d, whole_s, whole_d, rest, c0, c1)

    def coarse(t, value):
        n1[t] = value

    restrict(c0, c1, tiles, rows, coarse, tiles)

    def use(c, source):
        for q in range(4):
            s1_ref[q, c] = source[q]

    tiles1 = tiles // 2
    split_tiles(lambda t: n1[t], tiles1, rows, splitter(), temp, use)
    out = moved(jnp.concatenate([n1[tiles], total], 0), virtual_splitter())
    source = quarters_of(out[:rows], temp.at[0])
    screen = quarters_of(out[rows:], temp.at[1])
    for q in range(4):
        s1_ref[q, tiles1] = source[q]
        d1_virtual[q] = 4.0 + screen[q]
        pi1[q] = inverse_of(4.0 + screen[q])
    d2_virtual[...] = 4.0 + ((screen[0] + screen[1]) + (screen[2] + screen[3]))

    def own(main, virtual):
        return lambda q, t: virtual[q] if isinstance(t, int) and t == tiles1 else main[q, t]

    w = [w0, w1, w2, w3]
    rows1 = rows // 2
    row = row_ids(rows1)
    load_s, load_d = own(s1_ref, s1_ref.at[:, tiles1]), own(d1_ref, d1_virtual)

    def after_sweep(sweep):
        if sweep == 0:
            for t in range(tiles1 + 1):
                even, odd_red = reds(t == tiles1)
                black_even[t] = w[even ^ 1][t]
                black_odd[t] = w[odd_red ^ 1][t]

    left = load_d, {1: part1, 2: part2}
    smooth(w, load_s, own(i1_ref, pi1), tiles1, 16, left, after_sweep)

    def valid(q, virtual):
        even, odd_red = reds(virtual)
        first = 1 if q == odd_red ^ 1 else 2
        last = rows1 - 2 if q == even ^ 1 else rows1 - 3
        return (row >= first) & (row <= last)

    def keep_red(t, r):
        even, odd_red = reds(isinstance(t, int) and t == tiles1)
        red_even[t] = r[even]
        red_odd[t] = r[odd_red]

    residuals(w, load_s, left, tiles1, e0, e1, keep_red, 16, valid)
    shared = {}

    def edges(t, partial):
        virtual = t == tiles1
        even, odd_red = reds(virtual)
        s2_ref[t] = partial
        packs = state_packs(
            [s1_ref[q, t] for q in range(4)],
            [load_d(q, t) for q in range(4)],
            [w[q][t] for q in range(4)],
            {even ^ 1: black_even[t], odd_red ^ 1: black_odd[t]},
            {even: red_even[t], odd_red: red_odd[t]},
            partial,
            d2_virtual[...] if virtual else d2_ref[t],
            virtual,
        )
        right, left = packs
        count = tiles1 + 1
        for i in (0, 1):
            to_mate[i * count + t], to_other[i * count + t] = chosen(odd, left[i], right[i])
        if t % 2 == 0:
            pair = chosen(odd, left[2], roll_rows(right[2], 4))
            shared[0] = pair
        else:
            pair = chosen(odd, roll_rows(left[2], 4), right[2])
            pair = [jnp.where(sub < 4, x, y) for x, y in zip(shared[0], pair)]
        if t % 2 == 1 or virtual:
            to_mate[2 * count + t // 2], to_other[2 * count + t // 2] = pair

    restrict(e0, e1, tiles1, rows1, edges, 16)


def merge_kernel(r_ref, out_ref, out_buf, sems):
    tiles = r_ref.shape[1]
    columns = out_ref.shape[0]
    matrix = merger()
    chunk = out_ref.shape[1] // GROUPS
    copies = []
    for group in range(GROUPS):
        for batch in range(tiles // GROUPS // BATCH):
            start = group * (tiles // GROUPS) + batch * BATCH
            own = slice(8, 8 + columns)
            both = [
                jnp.concatenate([r_ref[0, start + i, own], r_ref[1, start + i, own]], 1)
                for i in range(BATCH)
            ]
            out = moved(jnp.concatenate(both, 0), matrix)
            for i in range(BATCH):
                where = slice((start + i) * 256, (start + i + 1) * 256)
                out_buf[:, where] = out[columns * i : columns * (i + 1)]
        part = pl.ds(group * chunk, chunk)
        copy = pltpu.make_async_copy(out_buf.at[:, part], out_ref.at[:, part], sems.at[group])
        copy.start()
        copies.append(copy)
    for copy in copies:
        copy.wait()


def coarse_kernel(
    s_ref, d_ref, i_ref, d_virtual, d2_ref, d2_virtual, s2_ref, from_other, from_mate,
    solution_ref, residual_ref,
    v0, v1, v2, v3, c0, c1, hs, hd, hi, part, fixes, rest1, rest2, s, d, inv, va, vb,
):
    v = [v0, v1, v2, v3]
    tiles, own = d_ref.shape[1], d_ref.shape[2]
    rows = own + 8
    count = tiles + 1
    sub = row_ids(8)
    odd_band = is_odd()
    def rim(x):
        return jnp.where(sub < 4, x[:8], x[own - 8 :])

    for t in range(count):
        places = t, count + t, 2 * count + t // 2
        packs = [chosen(odd_band, from_mate[i], from_other[i]) for i in places]
        source = [jnp.zeros((8, LANES), F32)] * 4
        diag = [jnp.full((8, LANES), 4.0, F32)] * 4
        inverse = [jnp.zeros((8, LANES), F32)] * 4
        fixed = [jnp.zeros((8, LANES), F32)] * 4
        more = jnp.zeros((8, LANES), F32)
        total = jnp.ones((8, LANES), F32)
        for side, (a, ab, b, bb) in enumerate(sides(t == tiles)):
            near, far, step = (7, 6, -1) if side == 0 else (0, 1, 1)
            first = 6 if side == 0 else 0
            pack0, pack1, pack2 = (pair[side] for pair in packs)
            groups = [
                roll_rows(pack, first - 2 * g) for pack in (pack0, pack1) for g in range(4)
            ]
            pack2 = roll_rows(pack2, 4 * (t % 2) + (4 if side == 0 else 0))

            def put(group, q, at, x):
                group[q] = jnp.where(sub == at, x, group[q])

            for q in range(4):
                put(source, q, near, groups[q])
                put(diag, q, near, groups[4 + q])
            put(source, bb, far, groups[0])
            put(diag, bb, far, groups[1])
            put(fixed, bb, far, groups[2])
            put(fixed, b, far, groups[3])
            put(source, b, far, groups[4])
            put(diag, b, far, 0.0)
            put(source, a, far, groups[5])
            put(fixed, ab, near, pack2)
            more = jnp.where(sub == far, groups[6], more)
            more = jnp.where((sub == far + step) | (sub == far + 2 * step), pack2, more)
            total = jnp.where(sub == far, pack2, total)
            total = jnp.where(sub == far + step, roll_rows(groups[7], step), total)
            for q in range(4):
                known = (sub == near) | (sub == far) if q == bb else sub == near
                inverse[q] = jnp.where(known, inverse_of(diag[q]), inverse[q])
        for q in range(4):
            own_d = rim(d_virtual[q] if t == tiles else d_ref[q, t])
            own_i = inverse_of(own_d) if t == tiles else rim(i_ref[q, t])
            hs[q, t] = jnp.concatenate([source[q], rim(s_ref[q, t])], 0)
            hd[q, t] = jnp.concatenate([diag[q], own_d], 0)
            hi[q, t] = jnp.concatenate([inverse[q], own_i], 0)
            fixes[q, t] = fixed[q]
        part[t] = more
        near_total = (diag[0] + diag[1]) + (diag[2] + diag[3]) - 12.0
        total = jnp.where((sub == 0) | (sub == 7), near_total, total)
        here = d2_virtual[...] if t == tiles else d2_ref[t]
        d[t] = jnp.concatenate([here, total], 0)
    def after_sweep(sweep):
        if sweep == 2:
            return
        for t in range(count):
            (a, ab, b, bb), (_, _, other_b, other_bb) = sides(t == tiles)
            todo = {}
            if sweep == 0:
                todo = {ab: (sub == 7) | (sub == 1), bb: (sub == 6) | (sub == 0)}
            else:
                todo = {b: sub == 6, other_b: sub == 1}
            for q, mask in todo.items():
                v[q][t, :8] = jnp.where(mask, fixes[q, t], v[q][t, :8])

    def of(ref):
        return lambda q, t: ref[q, t]

    left = of(hd), {1: rest1, 2: rest2}
    smooth(v, of(hs), of(hi), tiles, 16, left, after_sweep)
    row = row_ids(16)

    def valid(q, virtual):
        even, odd_red = reds(virtual)
        after_band = 0 if q == odd_red ^ 1 else 1
        before_band = 7 if q == even ^ 1 else 6
        first = 8 if q == odd_red ^ 1 else 9
        last = 15 if q == even ^ 1 else 14
        return (row <= after_band) | ((row >= before_band) & (row <= first)) | (row >= last)

    residuals(v, of(hs), left, tiles, c0, c1, lambda t, r: None, 16, valid)

    lane, row = lane_ids(rows), row_ids(rows)
    even = (lane + row) % 2 == 0
    odd = jnp.logical_not(even)

    def start(t, value):
        ends = value[8:]
        source = jnp.concatenate(
            [
                s2_ref[t, :8] + jnp.where(sub < 4, ends, 0.0),
                s2_ref[t, own - 8 :] + jnp.where(sub >= 4, ends, 0.0),
                value[:8] + part[t],
            ],
            0,
        )
        inverse = inverse_of(d[t])
        s[t] = source
        inv[t] = inverse
        virtual = isinstance(t, int) and t == tiles
        va[t] = jnp.where(odd if virtual else even, source * inverse, 0.0)

    restrict(c0, c1, tiles, 16, start, 16)

    def scan(v, use):
        up, down = roll_up(v[tiles]), roll_down(v[0])
        for t in range(tiles + 1):
            x = v[t]
            up_here, down_next = roll_up(x), roll_down(v[after(t, tiles)])
            north = jnp.where(lane == 0, up, up_here)
            south = jnp.where(lane == LANES - 1, down_next, down)
            use(t, x, (col_prev(x) + col_next(x)) + (north + south))
            up, down = up_here, down_next

    for old, new, mask, other in ((va, vb, odd, even), (vb, va, even, odd), (va, vb, odd, even)):

        def relax(t, x, beside):
            update = other if t == tiles else mask
            new[t] = jnp.where(update, (s[t] + beside) * inv[t], x)

        scan(old, relax)

    def finish(t, x, beside):
        if t < tiles:
            where = slice(t * LANES, (t + 1) * LANES)
            solution_ref[:, where] = x[:own]
            residual_ref[:, where] = (s[t] - (d[t] * x - beside))[:own]

    scan(vb, finish)


VMEM = pl.BlockSpec(memory_space=pltpu.VMEM)
HBM = pl.BlockSpec(memory_space=pltpu.HBM)


def call(kernel, out_shapes, scratch, *args, sems=None, far_in=0, far_out=0):
    scratch = [pltpu.VMEM(x, F32) if isinstance(x, tuple) else x for x in scratch]
    if sems is not None:
        scratch.append(pltpu.SemaphoreType.DMA(sems))
    return pl.pallas_call(
        kernel,
        out_shape=[jax.ShapeDtypeStruct(shape, F32) for shape in out_shapes],
        in_specs=[HBM] * far_in + [VMEM] * (len(args) - far_in),
        out_specs=[HBM] * far_out + [VMEM] * (len(out_shapes) - far_out),
        scratch_shapes=scratch,
        compiler_params=pltpu.CompilerParams(vmem_limit_bytes=40 * 2**20),
    )(*args)


def swapped_with(x, by):
    count = lax.axis_size("lon")
    pairs = [(i, (i + by) % count) for i in range(0, count, 2)]
    return lax.ppermute(x, "lon", pairs + [(b, a) for a, b in pairs])


def swapped_edges(to_mate, to_other):
    from_mate = swapped_with(to_mate, 1)
    return from_mate, swapped_with(to_other, -1)


def body(right_side, texel_weight, seam_flags):
    columns, height = right_side.shape
    half_turn = lax.axis_size("lon") // 2
    tiles, rows = height // 256, columns // 2
    tiles1, rows1 = tiles // 2, rows // 2
    temp = (BATCH, 2, columns, LANES)
    natural = (2, tiles, columns, LANES)
    padded = (2, tiles, columns + 16, LANES)
    quarters1 = (4, tiles1, rows1, LANES)
    split = (2, 16 * tiles, LANES)
    to_mate, to_other, corner = call(
        edge_kernel,
        [(2, tiles, 8, LANES), (2, tiles, 8, LANES), (2, 8, LANES)],
        [(16, height), pltpu.VMEM((32, height), BF16)]
        + [pltpu.VMEM(seam_flags.shape, jnp.int32), split, split, (tiles, 8, LANES)],
        *[
            pltpu.with_memory_space_constraint(x, pltpu.HBM)
            for x in (right_side, texel_weight, seam_flags)
        ],
        sems=(5,), far_in=3,
    )
    from_mate, from_other = swapped_edges(to_mate, to_other)
    corner_far = swapped_with(corner, half_turn - 1)
    corner_near = swapped_with(corner, half_turn + 1)
    ends = (2, 2, columns, LANES)
    (polar_own,) = call(
        polar_kernel, [(2, rows, LANES)], [ends, ends],
        right_side, texel_weight, seam_flags, corner,
    )
    polar = lax.ppermute(
        polar_own, "lon", [(i, (i + half_turn) % (2 * half_turn)) for i in range(2 * half_turn)]
    )
    s, d, inverse, d1, i1, d2 = call(
        bulk_kernel,
        [natural] * 3 + [quarters1, quarters1, quarters1[1:]],
        [(BATCH, columns, LANES), (tiles, 8, LANES), (tiles, rows, LANES), (BATCH, 2, rows, LANES)],
        right_side, texel_weight, seam_flags, polar_own,
    )

    def level_scratch(tiles, rows):
        return [(tiles + 1, rows, LANES)] * 6

    def halo_scratch(tiles):
        return [(4, tiles + 1, 8, LANES)] * 3

    pack1 = (2 * (tiles1 + 1) + tiles1 // 2 + 1, 8, LANES)
    r, s1, d1_virtual, d2_virtual, s2_own, to_mate, to_other = call(
        fine_kernel,
        [padded, (4, tiles1 + 1, rows1, LANES), (4, rows1, LANES), (rows1, LANES)]
        + [(tiles1 + 1, rows1, LANES), pack1, pack1],
        [padded, (4, tiles, 8, LANES), (4, rows + 8, LANES), (4, tiles, 8, LANES)]
        + [(tiles + 1, rows, LANES)] * 2
        + halo_scratch(tiles)
        + [(4, rows, LANES)] * 3
        + [(tiles + 1, rows, LANES), (BATCH, 2, rows, LANES)]
        + level_scratch(tiles1, rows1)
        + [(4, rows1, LANES)]
        + [(tiles1 + 1, rows1, LANES)] * 4
        + [(tiles1, rows1, LANES)] * 2,
        s, d, inverse, d1, i1, d2, from_other, from_mate, polar, corner_near, corner_far,
    )
    from_mate, from_other = swapped_edges(to_mate, to_other)
    (fine_residual,) = call(
        merge_kernel, [(columns, height)], [(columns, height)], r,
        sems=(GROUPS,), far_out=1,
    )
    wide = (tiles1 + 1, rows1 + 8, LANES)
    solution_2, residual_2 = call(
        coarse_kernel,
        [(columns // 4, height // 4)] * 2,
        level_scratch(tiles1, 16)
        + [(4, tiles1 + 1, 16, LANES)] * 3
        + [(tiles1 + 1, 8, LANES), (4, tiles1 + 1, 8, LANES)]
        + [(tiles1, 16, LANES)] * 2
        + [wide] * 5,
        s1, d1, i1, d1_virtual, d2, d2_virtual, s2_own, from_other, from_mate,
    )
    return fine_residual, solution_2, residual_2


def solution(mesh):
    spec = P(("groups", "lon"), None)
    return jax.shard_map(
        body, mesh=mesh, in_specs=(spec,) * 3, out_specs=(spec,) * 3, check_vma=False
    )
```

```python
import jax
import jax.numpy as jnp
from jax import lax
from jax.experimental import pallas as pl
from jax.experimental.pallas import tpu as pltpu
from jax.sharding import PartitionSpec as P

TILE = 32
SEAM_SCALE = 0.1
LANES = 128
GROUPS = 4
BATCH = 4
F32 = jnp.float32
BF16 = jnp.bfloat16


def loop(count, body, carry=0, unroll=4):
    unroll = min(unroll, count)

    def steps(block, carry):
        for i in range(unroll):
            carry = body(block * unroll + i, carry)
        return carry

    whole = count // unroll
    carry = steps(0, carry) if whole == 1 else lax.fori_loop(0, whole, steps, carry)
    for t in range(whole * unroll, count):
        carry = body(t, carry)
    return carry


def before(t, tiles):
    return (tiles if t == 0 else t - 1) if isinstance(t, int) else jnp.where(t == 0, tiles, t - 1)


def after(t, tiles):
    return (0 if t == tiles else t + 1) if isinstance(t, int) else t + 1


def lane_ids(rows):
    return lax.broadcasted_iota(jnp.int32, (rows, LANES), 1)


def row_ids(rows):
    return lax.broadcasted_iota(jnp.int32, (rows, LANES), 0)


def roll_up(x):
    return pltpu.roll(x, 1, 1)


def roll_down(x):
    return pltpu.roll(x, LANES - 1, 1)


def roll_rows(x, by):
    by %= x.shape[0]
    return x if by == 0 else pltpu.roll(x, by, 0)


def roll_lanes(x, by):
    by %= LANES
    return x if by == 0 else pltpu.roll(x, by, 1)


def col_prev(x):
    return pltpu.roll(x, 1, 0)


def col_next(x):
    return pltpu.roll(x, x.shape[0] - 1, 0)


def inverse_of(x):
    return 1.0 / x


def selector(shape, rule):
    a = lax.broadcasted_iota(jnp.int32, shape, 0)
    b = lax.broadcasted_iota(jnp.int32, shape, 1)
    return jnp.where(rule(a, b), 1.0, 0.0).astype(BF16)


def splitter():
    return selector((256, 256), lambda a, b: a == 2 * (b % LANES) + b // LANES)


def merger():
    return selector((256, 256), lambda a, b: b == 2 * (a % LANES) + a // LANES)


def virtual_splitter():
    return selector(
        (LANES, 256),
        lambda a, b: a // 2 + jnp.where(a >= 64, 64, 0) + LANES * (a % 2) == b,
    )


def moved(x, matrix, exact=None):
    rows = x.shape[0]
    high = x.astype(BF16)
    low = (x - high.astype(F32)).astype(BF16)
    terms = [high, low] if exact is None else [high, low, exact]
    out = jnp.dot(jnp.concatenate(terms, 0), matrix, preferred_element_type=F32)
    both = out[:rows] + out[rows : 2 * rows]
    return both if exact is None else (both, out[2 * rows :])


def quarters_of(parts, temp):
    count = parts.shape[0] // 2
    temp[0] = parts[:, :LANES]
    temp[1] = parts[:, LANES:]
    return [temp[pr, pl.ds(pc, count, 2), :] for pc in (0, 1) for pr in (0, 1)]


def reds(swapped):
    return (1, 2) if swapped else (0, 3)


def interleaved(group, offset):
    sub = row_ids(8)
    packed = roll_rows(group[0], offset)
    for q in range(1, 4):
        packed = jnp.where(sub // 2 == q, roll_rows(group[q], 2 * q + offset), packed)
    return packed


def edge_packs(source, diag, swapped):
    sub = row_ids(8)
    even, odd = reds(swapped)
    rows = source[0].shape[0]
    packs = []
    for here, first, second, row, step in (
        (slice(rows - 8, rows), even, odd, 6, 1),
        (slice(0, 8), odd, even, 1, -1),
    ):
        gs = [x[here] for x in source]
        gd = [x[here] for x in diag]
        near = gs[first] * inverse_of(gd[first])
        far = roll_rows(gs[second] * inverse_of(gd[second]), step)
        gs[first] = jnp.where(sub == row, near, gs[first])
        gd[first] = jnp.where(sub == row, far, gd[first])
        offset = 2 if row == 6 else 0
        packs.append((interleaved(gs, offset), interleaved(gd, offset)))
    return packs


def unpacked_halo(left, right, swapped):
    sub = row_ids(8)
    even, odd = reds(swapped)
    (al, bl), (ar, br) = left, right
    source, diag = [], []
    for q in range(4):
        s = jnp.where(
            sub >= 6,
            roll_rows(al, 6 - 2 * q),
            jnp.where(sub <= 1, roll_rows(ar, -2 * q), 0.0),
        )
        d = jnp.where(
            sub >= 6,
            roll_rows(bl, 6 - 2 * q),
            jnp.where(sub <= 1, roll_rows(br, -2 * q), 4.0),
        )
        if q == even:
            s = jnp.where(sub == 2, roll_rows(br, 1 - 2 * odd), s)
            d = jnp.where((sub == 2) | (sub == 6), 1.0, d)
        if q == odd:
            s = jnp.where(sub == 5, roll_rows(bl, 5 - 2 * even), s)
            d = jnp.where((sub == 5) | (sub == 1), 1.0, d)
        source.append(s)
        diag.append(d)
    return source, diag


def is_odd():
    return lax.rem(lax.axis_index("lon"), 2) == 1


def chosen(odd, a, b):
    return jnp.where(odd, a, b), jnp.where(odd, b, a)


def store_edges(t, packs, odd, to_mate, to_other):
    right, left = packs
    for i in (0, 1):
        to_mate[i, t], to_other[i, t] = chosen(odd, left[i], right[i])


def sides(swapped):
    even, odd = reds(swapped)
    return (even, even ^ 1, odd, odd ^ 1), (odd, odd ^ 1, even, even ^ 1)


def paired(groups, shift):
    sub = row_ids(8)
    packed = roll_rows(groups[0], shift)
    for g in (1, 2, 3):
        packed = jnp.where(sub // 2 == g, roll_rows(groups[g], 2 * g + shift), packed)
    return packed


def state_packs(source, diag, last, first_black, residual, partial, diag2, swapped):
    sub = row_ids(8)
    rows = source[0].shape[0]
    packs = []
    for (a, ab, b, bb), here, near, far, step in zip(
        sides(swapped), (slice(rows - 8, rows), slice(0, 8)), (7, 0), (6, 1), (-1, 1)
    ):
        s, d, v = ([x[here] for x in group] for group in (source, diag, last))
        part, d2 = partial[here], diag2[here]
        beside = [
            s[bb] + v[a],
            d[bb],
            first_black[bb][here],
            v[b],
            s[b] - d[b] * v[b] + v[ab],
            residual[a][here] - v[bb],
            part,
            roll_rows(d2, -step),
        ]
        groups = [jnp.where(sub == far, y, x) for x, y in zip(s + d, beside)]
        shift = 2 if near == 7 else 0
        more = jnp.where(sub == far, d2, first_black[ab][here])
        more = jnp.where(sub == far + step, part, more)
        more = jnp.where(sub == far + 2 * step, part * inverse_of(d2), more)
        packs.append((paired(groups[:4], shift), paired(groups[4:], shift), more))
    return packs


def fill_halo(t, from_mate, from_other, odd, swapped, hs, hd, hi):
    al, ar = chosen(odd, from_mate[0, t], from_other[0, t])
    bl, br = chosen(odd, from_mate[1, t], from_other[1, t])
    source, diag = unpacked_halo((al, bl), (ar, br), swapped)
    for q in range(4):
        hs[q, t] = source[q]
        hd[q, t] = diag[q]
        hi[q, t] = inverse_of(diag[q])


def loader(own, halo, virtual, tiles):
    def load(q, t):
        if isinstance(t, int) and t == tiles:
            return jnp.concatenate([virtual[q], halo[q, t]], 0)
        return jnp.concatenate([own[q, t], halo[q, t]], 0)

    return load


def polar_packs(tiles_of):
    lane = lane_ids(tiles_of[0][0].shape[0])
    packs = []
    for pc in (0, 1):
        parts = [*tiles_of[2 * pc], *tiles_of[2 * pc + 1]]
        packed = parts[0]
        for m in range(1, 4):
            mine = (lane + (16 - 32 * m) % LANES) % LANES < 32
            packed = jnp.where(mine, roll_lanes(parts[m], 32 * m), packed)
        packs.append(packed)
    return packs


def polar_unpacked(x, q):
    lane = lane_ids(x.shape[1])
    used = (lane < 16) | (lane >= LANES - 16)
    m = 2 * (q % 2)
    return (
        jnp.where(used, roll_lanes(x[q // 2], 32 * m), 0.0),
        jnp.where(used, roll_lanes(x[q // 2], 32 * (m + 1)), 4.0),
    )


def seam_scales(flags, chunks):
    flag_cols, flag_lats = flags.shape
    flags = jnp.concatenate(
        [flags.astype(F32), jnp.zeros((8 - flag_cols, flag_lats), F32)], 0
    )
    lat = lax.broadcasted_iota(jnp.int32, (8, flag_lats), 1)
    stacked = jnp.concatenate([jnp.where(lat // 8 == c, flags, 0.0) for c in chunks], 0)
    spread = selector((flag_lats, LANES), lambda a, b: a % 8 == b // (TILE // 2))
    spread_flags = jnp.dot(stacked.astype(BF16), spread, preferred_element_type=F32)
    scale = jnp.where(spread_flags > 0.5, SEAM_SCALE, 1.0)
    return scale.reshape(len(chunks), 8, LANES)


def seam_rows(scales, flag_cols, rows):
    size = (rows // flag_cols, LANES)
    return jnp.concatenate(
        [jnp.broadcast_to(scales[i : i + 1], size) for i in range(flag_cols)], 0
    )


def edge_kernel(
    right_ref, weight_ref, flag_ref,
    to_mate, to_other, corner_ref,
    edge_s, edge_w, flags, temp_s, temp_w, scale_ref, sems,
):
    columns, height = right_ref.shape
    tiles = height // 256
    half = height // 2
    pairs = [(flag_ref, flags)]
    for start in (0, half):
        part = pl.ds(start, half)
        for src, dst, size in ((right_ref, edge_s, 8), (weight_ref, edge_w, 16)):
            for at, to in ((0, 0), (columns - size, size)):
                pairs.append((src.at[pl.ds(at, size), part], dst.at[pl.ds(to, size), part]))
    copies = [
        pltpu.make_async_copy(src, dst, sems.at[i]) for i, (src, dst) in enumerate(pairs)
    ]
    for copy in copies:
        copy.start()
    odd = is_odd()
    matrix = splitter()
    flag_cols = flag_ref.shape[0]
    copies[0].wait()
    scale_ref[...] = seam_scales(flags[...], range(tiles))
    sub = row_ids(8)
    count = tiles // 2
    found = []
    for part in (0, 1):
        for copy in copies[1 + 4 * part : 5 + 4 * part]:
            copy.wait()
        chunks = range(part * count, (part + 1) * count)
        lanes = [slice(c * 256, (c + 1) * 256) for c in chunks]
        source, weight = moved(
            jnp.concatenate([edge_s[:, w] for w in lanes], 0),
            matrix,
            jnp.concatenate([edge_w[:, w] for w in lanes], 0),
        )
        weight = weight.reshape(count, 32, 256)
        weight = jnp.concatenate([weight[:, :8], weight[:, 24:]], 1).reshape(count * 16, 256)
        source = quarters_of(source, temp_s.at[part])
        weight = quarters_of(weight, temp_w.at[part])
        for i, c in enumerate(chunks):
            here = slice(i * 8, (i + 1) * 8)
            scales = scale_ref[c]
            scale = jnp.where(sub < 4, scales[:1], scales[flag_cols - 1 : flag_cols])
            pair = [x[here] for x in source], [4.0 + w[here] * scale for w in weight]
            store_edges(c, edge_packs(*pair, False), odd, to_mate, to_other)
            if c in (0, tiles - 1):
                found.append(pair)
    both = mirrored_ends(*found)
    for pc in (0, 1):
        corner = both[8 * pc : 8 * (pc + 1)]
        corner_ref[pc] = corner


def mirrored_ends(first, last):
    mirror = selector((LANES, LANES), lambda a, b: a + b == LANES - 1)
    lane = lane_ids(first[0][0].shape[0])
    ends = [
        [jnp.where(lane >= 64, last[i][q ^ 1], first[i][q ^ 1]) for i in (0, 1)]
        for q in range(4)
    ]
    return moved(jnp.concatenate(polar_packs(ends), 0), mirror)


def polar_kernel(right_ref, weight_ref, flag_ref, edges_first, polar_ref, temp_s, temp_w):
    columns, height = right_ref.shape
    rows, tiles = columns // 2, height // 256
    scales = seam_scales(flag_ref[...], (0, tiles - 1))
    lanes = slice(0, 256), slice(height - 256, height)
    source, weight = moved(
        jnp.concatenate([right_ref[:, w] for w in lanes], 0),
        splitter(),
        jnp.concatenate([weight_ref[:, w] for w in lanes], 0),
    )
    found = []
    for end in (0, 1):
        here = slice(end * columns, (end + 1) * columns)
        scale = seam_rows(scales[end], flag_ref.shape[0], rows)
        found.append(
            (
                quarters_of(source[here], temp_s.at[end]),
                [4.0 + w * scale for w in quarters_of(weight[here], temp_w.at[end])],
            )
        )
    both = mirrored_ends(*found)
    for pc in (0, 1):
        polar_ref[pc] = both[pc * rows : (pc + 1) * rows]


def bulk_kernel(
    right_ref, weight_ref, flag_ref, polar_first,
    s_ref, d_ref, i_ref, d1_ref, i1_ref, d2_ref,
    temp, scale_ref, e_ref, split_temp,
):
    tiles, columns = s_ref.shape[1], s_ref.shape[2]
    rows = columns // 2
    matrix = splitter()
    scale_ref[...] = seam_scales(flag_ref[...], range(tiles))
    for start in range(0, tiles, BATCH):
        lanes = [slice((start + i) * 256, (start + i + 1) * 256) for i in range(BATCH)]
        source, weight = moved(
            jnp.concatenate([right_ref[:, w] for w in lanes], 0),
            matrix,
            jnp.concatenate([weight_ref[:, w] for w in lanes], 0),
        )
        for i in range(BATCH):
            c = start + i
            here = slice(i * columns, (i + 1) * columns)
            scale = seam_rows(scale_ref[c], flag_ref.shape[0], columns)
            screens = []
            for pr in (0, 1):
                half = slice(pr * LANES, (pr + 1) * LANES)
                screen = weight[here, half] * scale
                diag = 4.0 + screen
                s_ref[pr, c] = source[here, half]
                d_ref[pr, c] = diag
                i_ref[pr, c] = 1.0 / diag
                screens.append(screen)
            temp[i] = screens[0] + screens[1]
            e_ref[c] = temp[i, pl.ds(0, rows, 2), :] + temp[i, pl.ds(1, rows, 2), :]

    def use(c, screen):
        for q in range(4):
            d1_ref[q, c] = 4.0 + screen[q]
            i1_ref[q, c] = inverse_of(4.0 + screen[q])
        d2_ref[c] = 4.0 + ((screen[0] + screen[1]) + (screen[2] + screen[3]))

    split_tiles(lambda t: e_ref[t], tiles // 2, rows, matrix, split_temp, use)


def split_tiles(load, tiles, rows, matrix, temp, use):
    for start in range(0, tiles, BATCH):
        wide = [
            jnp.concatenate([load(2 * c), load(2 * c + 1)], 1)
            for c in range(start, start + BATCH)
        ]
        out = moved(jnp.concatenate(wide, 0), matrix)
        for i in range(BATCH):
            use(start + i, quarters_of(out[i * rows : (i + 1) * rows], temp.at[i, :, :rows]))


def half_sweep(v, load_s, load_i, tiles, red, unroll, left=None):
    rows = v[0].shape[1]
    lane = lane_ids(rows)
    y, z, qa, qb = (1, 2, 0, 3) if red else (3, 0, 2, 1)
    col_a, col_b = (col_prev, col_next) if red else (col_next, col_prev)

    def beside_virtual(q):
        ns, we = q ^ 1, q ^ 2
        here = v[ns][tiles]
        if q % 2 == 0:
            lat = jnp.where(lane == 0, roll_up(v[ns][tiles - 1]), roll_up(here))
        else:
            lat = jnp.where(lane == LANES - 1, roll_down(v[ns][0]), roll_down(here))
        cols = v[we][tiles]
        return (here + lat) + (cols + (col_prev if q < 2 else col_next)(cols))

    held = [
        (q, (load_s(q, tiles) + beside_virtual(q)) * load_i(q, tiles)) for q in (y, z)
    ]

    def body(t, carry):
        y_before, z_here = carry
        vy, vz = v[y][t], v[z][t]
        y_here = roll_up(vy)
        z_after = roll_down(v[z][t + 1])
        lat_a = vy + jnp.where(lane == 0, y_before, y_here)
        lat_b = vz + jnp.where(lane == LANES - 1, z_after, z_here)
        all_a = load_s(qa, t) + (lat_a + (vz + col_a(vz)))
        all_b = load_s(qb, t) + (lat_b + (vy + col_b(vy)))
        new_a, new_b = all_a * load_i(qa, t), all_b * load_i(qb, t)
        v[qa][t], v[qb][t] = new_a, new_b
        if left is not None:
            load_d, rest = left
            rest[qa][t] = all_a - load_d(qa, t) * new_a
            rest[qb][t] = all_b - load_d(qb, t) * new_b
        return y_here, z_after

    loop(tiles, body, (roll_up(v[y][tiles]), roll_down(v[z][0])), unroll)
    for q, value in held:
        v[q][tiles] = value


def smooth(v, load_s, load_i, tiles, unroll, left, after_sweep=None):
    zeros = jnp.zeros(v[0].shape[1:], F32)

    def first(t, _):
        for q in (0, 3):
            v[q][t] = load_s(q, t) * load_i(q, t)
        return 0

    loop(tiles, first, 0, unroll)
    for q in (1, 2):
        v[q][0] = zeros
        v[q][tiles - 1] = zeros
        v[q][tiles] = load_s(q, tiles) * load_i(q, tiles)
        v[3 * (q - 1)][tiles] = zeros
    for sweep, red in enumerate((False, True, False)):
        half_sweep(v, load_s, load_i, tiles, red, unroll, left if sweep == 2 else None)
        if after_sweep is not None:
            after_sweep(sweep)


def residuals(v, load_s, left, tiles, c0, c1, keep, unroll, valid=None):
    lane = lane_ids(v[0].shape[1])
    load_d, rest = left

    def use(t, r):
        keep(t, r)
        if valid is not None:
            virtual = isinstance(t, int) and t == tiles
            r = [jnp.where(valid(q, virtual), r[q], 0.0) for q in range(4)]
        c0[t] = (col_prev(r[2]) + col_next(r[0])) + 3.0 * (r[0] + r[2])
        c1[t] = (col_prev(r[3]) + col_next(r[1])) + 3.0 * (r[1] + r[3])

    def north(q, t):
        return jnp.where(lane == 0, roll_up(v[q][before(t, tiles)]), roll_up(v[q][t]))

    def south(q, t):
        return jnp.where(
            lane == LANES - 1, roll_down(v[q][after(t, tiles)]), roll_down(v[q][t])
        )

    def full(t):
        x = [v[q][t] for q in range(4)]
        beside = [
            (x[1] + north(1, t)) + (x[2] + col_prev(x[2])),
            (x[0] + south(0, t)) + (x[3] + col_prev(x[3])),
            (x[3] + north(3, t)) + (x[0] + col_next(x[0])),
            (x[2] + south(2, t)) + (x[1] + col_next(x[1])),
        ]
        use(t, [load_s(q, t) - (load_d(q, t) * x[q] - beside[q]) for q in range(4)])

    def body(i, carry):
        t = i + 1
        up, down = carry
        x = [v[q][t] for q in range(4)]
        up_here, down_next = roll_up(x[1]), roll_down(v[2][t + 1])
        beside0 = (x[1] + jnp.where(lane == 0, up, up_here)) + (x[2] + col_prev(x[2]))
        beside3 = (x[2] + jnp.where(lane == LANES - 1, down_next, down)) + (
            x[1] + col_next(x[1])
        )
        r0 = load_s(0, t) - (load_d(0, t) * x[0] - beside0)
        r3 = load_s(3, t) - (load_d(3, t) * x[3] - beside3)
        use(t, [r0, rest[1][t], rest[2][t], r3])
        return up_here, down_next

    full(0)
    loop(tiles - 2, body, (roll_up(v[1][0]), roll_down(v[2][1])), unroll)
    full(tiles - 1)
    full(tiles)


def restrict(c0, c1, tiles, rows, use, unroll):
    lane = lane_ids(rows)

    def body(t, carry):
        up, down = carry
        here, other = c0[t, :rows], c1[t, :rows]
        up_here = roll_up(other)
        down_next = roll_down(c0[after(t, tiles), :rows])
        north = jnp.where(lane == 0, up, up_here)
        south = jnp.where(lane == LANES - 1, down_next, down)
        use(t, ((north + south) + 3.0 * (here + other)) * (1.0 / 16.0))
        return up_here, down_next

    start = roll_up(c1[tiles, :rows]), roll_down(c0[0, :rows])
    body(tiles, loop(tiles, body, start, unroll))


class Fine:
    def __init__(self, own, halo, virtual, tiles, columns):
        self.own, self.halo, self.virtual = own, halo, virtual
        self.tiles, self.columns = tiles, columns

    def part(self, parity, t, start):
        return self.own[parity][t, pl.ds(8 + start, self.columns // 2, 2), :]

    def rows(self, q, t):
        return self.part(q % 2, t, q // 2)

    def whole(self, q, t):
        if t == self.tiles:
            return self.virtual[q][...]
        return jnp.concatenate([self.rows(q, t), self.halo[q][t]], 0)

    def ends(self, q, t):
        if t == self.tiles:
            whole = self.virtual[q][...]
            return whole[: self.columns // 2], whole[self.columns // 2 :]
        return self.rows(q, t), self.halo[q][t]

    def line(self, parity, t, column):
        row = self.own[parity][t, 8 + column : 9 + column]
        return jnp.broadcast_to(row, (8, LANES))

    def put(self, q, t, own, halo):
        pr, pc = q % 2, q // 2
        self.own[pr][t, pl.ds(8 + pc, self.columns // 2, 2), :] = own
        self.halo[q][t] = halo
        if pc == 1:
            self.own[pr][t, 7:8] = halo[7:8]
        else:
            at = 8 + self.columns
            self.own[pr][t, at : at + 1] = halo[0:1]

    def beside_columns(self, q, t, halo):
        sub = row_ids(8)
        pr, pc = q % 2, q // 2
        own = self.part(pr, t, pc - 1) + self.part(pr, t, pc + 1)
        if pc == 0:
            other = jnp.where(sub == 0, self.line(pr, t, self.columns - 1), col_prev(halo))
        else:
            other = jnp.where(sub == 7, self.line(pr, t, 0), col_next(halo))
        return own, halo + other


def fine_sweep(v, load_s, load_i, whole_s, whole_i, red, left):
    tiles = v.tiles
    y, z, qa, qb = (1, 2, 0, 3) if red else (3, 0, 2, 1)

    def lane_sum(parts, rolled, edge, lane_at):
        return [
            x + jnp.where(lane_ids(x.shape[0]) == lane_at, e, r)
            for x, r, e in zip(parts, rolled, edge)
        ]

    def beside_virtual(q):
        here, cols = v.whole(q ^ 1, tiles), v.whole(q ^ 2, tiles)
        lane = lane_ids(here.shape[0])
        if q % 2 == 0:
            lat = jnp.where(lane == 0, roll_up(v.whole(q ^ 1, tiles - 1)), roll_up(here))
        else:
            lat = jnp.where(lane == LANES - 1, roll_down(v.whole(q ^ 1, 0)), roll_down(here))
        return (here + lat) + (cols + (col_prev if q < 2 else col_next)(cols))

    held = [
        (q, (whole_s(q, tiles) + beside_virtual(q)) * whole_i(q, tiles)) for q in (y, z)
    ]
    y_before = [roll_up(x) for x in v.ends(y, tiles)]
    z_here = [roll_down(x) for x in v.ends(z, 0)]
    for t in range(tiles):
        vy, vz = v.ends(y, t), v.ends(z, t)
        y_here = [roll_up(x) for x in vy]
        z_after = [roll_down(x) for x in v.ends(z, t + 1)]
        lat_a = lane_sum(vy, y_here, y_before, 0)
        lat_b = lane_sum(vz, z_here, z_after, LANES - 1)
        new = []
        for q, lat, halo in ((qa, lat_a, vz[1]), (qb, lat_b, vy[1])):
            cols = v.beside_columns(q, t, halo)
            total = [x + (l + c) for x, l, c in zip(load_s(q, t), lat, cols)]
            value = [x * i for x, i in zip(total, load_i(q, t))]
            new.append((q, value))
            if left is not None:
                load_d, rest = left
                rest.put(q, t, *[x - d * u for x, d, u in zip(total, load_d(q, t), value)])
        for q, value in new:
            v.put(q, t, *value)
        y_before, z_here = y_here, z_after
    for q, value in held:
        v.virtual[q][...] = value


def fine_residuals(v, load_s, load_d, whole_s, whole_d, rest, c0, c1):
    tiles = v.tiles
    rows = v.columns // 2

    def columns_summed(t):
        for pr, ref in ((0, c0), (1, c1)):
            outer = rest.part(pr, t, -1) + rest.part(pr, t, 2)
            inner = rest.part(pr, t, 0) + rest.part(pr, t, 1)
            ref[t] = outer + 3.0 * inner

    def full(t):
        x = [v.whole(q, t) for q in range(4)]
        lane = lane_ids(x[0].shape[0])

        def north(q):
            return jnp.where(lane == 0, roll_up(v.whole(q, before(t, tiles))), roll_up(x[q]))

        def south(q):
            return jnp.where(
                lane == LANES - 1, roll_down(v.whole(q, after(t, tiles))), roll_down(x[q])
            )

        beside = [
            (x[1] + north(1)) + (x[2] + col_prev(x[2])),
            (x[0] + south(0)) + (x[3] + col_prev(x[3])),
            (x[3] + north(3)) + (x[0] + col_next(x[0])),
            (x[2] + south(2)) + (x[1] + col_next(x[1])),
        ]
        r = [whole_s(q, t) - (whole_d(q, t) * x[q] - beside[q]) for q in range(4)]
        if t == tiles:
            c0[t] = ((col_prev(r[2]) + col_next(r[0])) + 3.0 * (r[0] + r[2]))[:rows]
            c1[t] = ((col_prev(r[3]) + col_next(r[1])) + 3.0 * (r[1] + r[3]))[:rows]
        else:
            for q in range(4):
                rest.put(q, t, r[q][:rows], r[q][rows:])
            columns_summed(t)

    full(0)
    up = [roll_up(x) for x in v.ends(1, 0)]
    down = [roll_down(x) for x in v.ends(2, 1)]
    for t in range(1, tiles - 1):
        x = [v.ends(q, t) for q in range(4)]
        up_here = [roll_up(part) for part in x[1]]
        down_next = [roll_down(part) for part in v.ends(2, t + 1)]
        for q, ns, near, edge, lane_at in (
            (0, 1, up_here, up, 0), (3, 2, down, down_next, LANES - 1)
        ):
            cols = v.beside_columns(q, t, x[q ^ 2][1])
            r = []
            for i, (s, d) in enumerate(zip(load_s(q, t), load_d(q, t))):
                lane = lane_ids(s.shape[0])
                beside = x[ns][i] + jnp.where(lane == lane_at, edge[i], near[i]) + cols[i]
                r.append(s - (d * x[q][i] - beside))
            rest.put(q, t, *r)
        columns_summed(t)
        up, down = up_here, down_next
    full(tiles - 1)
    full(tiles)


def fine_kernel(
    s_ref, d_ref, i_ref, d1_ref, i1_ref, d2_ref,
    from_other, from_mate, polar_ref, corner_near, corner_far,
    r_ref, s1_ref, d1_virtual, d2_virtual, s2_ref, to_mate, to_other,
    v_ref, hv, pv, hr, c0, c1, hs, hd, hi, ps, pd, pi, n1, temp,
    w0, w1, w2, w3, e0, e1, pi1, black_even, black_odd, red_even, red_odd,
    part1, part2,
):
    tiles, columns = s_ref.shape[1], s_ref.shape[2]
    rows = columns // 2
    sub = row_ids(8)
    odd = is_odd()

    def halo(t, _):
        fill_halo(t, from_mate, from_other, odd, False, hs, hd, hi)
        return 0

    loop(tiles, halo, 0, 8)
    total = -16.0
    for q in range(4):
        own_s, own_d = polar_unpacked(polar_ref, q)
        near_s, near_d = polar_unpacked(corner_near, q)
        far_s, far_d = polar_unpacked(corner_far, q)
        left_s, right_s = chosen(odd, near_s, far_s)
        left_d, right_d = chosen(odd, near_d, far_d)
        total = total + own_d
        ps[q] = own_s
        pd[q] = own_d
        pi[q] = inverse_of(own_d)
        source = jnp.where(sub >= 5, left_s, jnp.where(sub <= 2, right_s, 0.0))
        diag = jnp.where(sub >= 5, left_d, jnp.where(sub <= 2, right_d, 4.0))
        hs[q, tiles] = source
        hd[q, tiles] = diag
        hi[q, tiles] = inverse_of(diag)

    def loaders(ref, halo, virtual):
        def split(q, t):
            return ref[q % 2, t, pl.ds(q // 2, rows, 2), :], halo[q, t]

        def whole(q, t):
            if t == tiles:
                return jnp.concatenate([virtual[q], halo[q, t]], 0)
            return jnp.concatenate(split(q, t), 0)

        return split, whole

    load_s, whole_s = loaders(s_ref, hs, ps)
    load_d, whole_d = loaders(d_ref, hd, pd)
    load_i, whole_i = loaders(i_ref, hi, pi)

    def held(own_ref, halo_ref):
        return Fine(
            [own_ref.at[p] for p in (0, 1)],
            [halo_ref.at[q] for q in range(4)],
            [pv.at[q] for q in range(4)],
            tiles,
            columns,
        )

    v, rest = held(v_ref, hv), held(r_ref, hr)
    for t in range(tiles):
        for q in (0, 3):
            v.put(q, t, *[x * i for x, i in zip(load_s(q, t), load_i(q, t))])
    for q in (1, 2):
        for t in (0, tiles - 1):
            v.put(q, t, jnp.zeros((rows, LANES), F32), jnp.zeros((8, LANES), F32))
        pv[q] = whole_s(q, tiles) * whole_i(q, tiles)
        pv[3 * (q - 1)] = jnp.zeros((rows + 8, LANES), F32)
    for red, left in ((False, None), (True, None), (False, (load_d, rest))):
        fine_sweep(v, load_s, load_i, whole_s, whole_i, red, left)
    fine_residuals(v, load_s, load_d, whole_s, whole_d, rest, c0, c1)

    def coarse(t, value):
        n1[t] = value

    restrict(c0, c1, tiles, rows, coarse, tiles)

    def use(c, source):
        for q in range(4):
            s1_ref[q, c] = source[q]

    tiles1 = tiles // 2
    split_tiles(lambda t: n1[t], tiles1, rows, splitter(), temp, use)
    out = moved(jnp.concatenate([n1[tiles], total], 0), virtual_splitter())
    source = quarters_of(out[:rows], temp.at[0])
    screen = quarters_of(out[rows:], temp.at[1])
    for q in range(4):
        s1_ref[q, tiles1] = source[q]
        d1_virtual[q] = 4.0 + screen[q]
        pi1[q] = inverse_of(4.0 + screen[q])
    d2_virtual[...] = 4.0 + ((screen[0] + screen[1]) + (screen[2] + screen[3]))

    def own(main, virtual):
        return lambda q, t: virtual[q] if isinstance(t, int) and t == tiles1 else main[q, t]

    w = [w0, w1, w2, w3]
    rows1 = rows // 2
    row = row_ids(rows1)
    load_s, load_d = own(s1_ref, s1_ref.at[:, tiles1]), own(d1_ref, d1_virtual)

    def after_sweep(sweep):
        if sweep == 0:
            for t in range(tiles1 + 1):
                even, odd_red = reds(t == tiles1)
                black_even[t] = w[even ^ 1][t]
                black_odd[t] = w[odd_red ^ 1][t]

    left = load_d, {1: part1, 2: part2}
    smooth(w, load_s, own(i1_ref, pi1), tiles1, 16, left, after_sweep)

    def valid(q, virtual):
        even, odd_red = reds(virtual)
        first = 1 if q == odd_red ^ 1 else 2
        last = rows1 - 2 if q == even ^ 1 else rows1 - 3
        return (row >= first) & (row <= last)

    def keep_red(t, r):
        even, odd_red = reds(isinstance(t, int) and t == tiles1)
        red_even[t] = r[even]
        red_odd[t] = r[odd_red]

    residuals(w, load_s, left, tiles1, e0, e1, keep_red, 16, valid)
    shared = {}

    def edges(t, partial):
        virtual = t == tiles1
        even, odd_red = reds(virtual)
        s2_ref[t] = partial
        packs = state_packs(
            [s1_ref[q, t] for q in range(4)],
            [load_d(q, t) for q in range(4)],
            [w[q][t] for q in range(4)],
            {even ^ 1: black_even[t], odd_red ^ 1: black_odd[t]},
            {even: red_even[t], odd_red: red_odd[t]},
            partial,
            d2_virtual[...] if virtual else d2_ref[t],
            virtual,
        )
        right, left = packs
        count = tiles1 + 1
        for i in (0, 1):
            to_mate[i * count + t], to_other[i * count + t] = chosen(odd, left[i], right[i])
        if t % 2 == 0:
            pair = chosen(odd, left[2], roll_rows(right[2], 4))
            shared[0] = pair
        else:
            pair = chosen(odd, roll_rows(left[2], 4), right[2])
            pair = [jnp.where(sub < 4, x, y) for x, y in zip(shared[0], pair)]
        if t % 2 == 1 or virtual:
            to_mate[2 * count + t // 2], to_other[2 * count + t // 2] = pair

    restrict(e0, e1, tiles1, rows1, edges, 16)


def merge_kernel(r_ref, out_ref, out_buf, sems):
    tiles = r_ref.shape[1]
    columns = out_ref.shape[0]
    matrix = merger()
    chunk = out_ref.shape[1] // GROUPS
    copies = []
    for group in range(GROUPS):
        for batch in range(tiles // GROUPS // BATCH):
            start = group * (tiles // GROUPS) + batch * BATCH
            own = slice(8, 8 + columns)
            both = [
                jnp.concatenate([r_ref[0, start + i, own], r_ref[1, start + i, own]], 1)
                for i in range(BATCH)
            ]
            out = moved(jnp.concatenate(both, 0), matrix)
            for i in range(BATCH):
                where = slice((start + i) * 256, (start + i + 1) * 256)
                out_buf[:, where] = out[columns * i : columns * (i + 1)]
        part = pl.ds(group * chunk, chunk)
        copy = pltpu.make_async_copy(out_buf.at[:, part], out_ref.at[:, part], sems.at[group])
        copy.start()
        copies.append(copy)
    for copy in copies:
        copy.wait()


def coarse_kernel(
    s_ref, d_ref, i_ref, d_virtual, d2_ref, d2_virtual, s2_ref, from_other, from_mate,
    solution_ref, residual_ref,
    v0, v1, v2, v3, c0, c1, hs, hd, hi, part, fixes, rest1, rest2, s, d, inv, va, vb,
    solution_buf, residual_buf, sems,
):
    v = [v0, v1, v2, v3]
    tiles, own = d_ref.shape[1], d_ref.shape[2]
    rows = own + 8
    count = tiles + 1
    sub = row_ids(8)
    odd_band = is_odd()
    def rim(x):
        return jnp.where(sub < 4, x[:8], x[own - 8 :])

    for t in range(count):
        places = t, count + t, 2 * count + t // 2
        packs = [chosen(odd_band, from_mate[i], from_other[i]) for i in places]
        source = [jnp.zeros((8, LANES), F32)] * 4
        diag = [jnp.full((8, LANES), 4.0, F32)] * 4
        inverse = [jnp.zeros((8, LANES), F32)] * 4
        fixed = [jnp.zeros((8, LANES), F32)] * 4
        more = jnp.zeros((8, LANES), F32)
        total = jnp.ones((8, LANES), F32)
        for side, (a, ab, b, bb) in enumerate(sides(t == tiles)):
            near, far, step = (7, 6, -1) if side == 0 else (0, 1, 1)
            first = 6 if side == 0 else 0
            pack0, pack1, pack2 = (pair[side] for pair in packs)
            groups = [
                roll_rows(pack, first - 2 * g) for pack in (pack0, pack1) for g in range(4)
            ]
            pack2 = roll_rows(pack2, 4 * (t % 2) + (4 if side == 0 else 0))

            def put(group, q, at, x):
                group[q] = jnp.where(sub == at, x, group[q])

            for q in range(4):
                put(source, q, near, groups[q])
                put(diag, q, near, groups[4 + q])
            put(source, bb, far, groups[0])
            put(diag, bb, far, groups[1])
            put(fixed, bb, far, groups[2])
            put(fixed, b, far, groups[3])
            put(source, b, far, groups[4])
            put(diag, b, far, 0.0)
            put(source, a, far, groups[5])
            put(fixed, ab, near, pack2)
            more = jnp.where(sub == far, groups[6], more)
            more = jnp.where((sub == far + step) | (sub == far + 2 * step), pack2, more)
            total = jnp.where(sub == far, pack2, total)
            total = jnp.where(sub == far + step, roll_rows(groups[7], step), total)
            for q in range(4):
                known = (sub == near) | (sub == far) if q == bb else sub == near
                inverse[q] = jnp.where(known, inverse_of(diag[q]), inverse[q])
        for q in range(4):
            own_d = rim(d_virtual[q] if t == tiles else d_ref[q, t])
            own_i = inverse_of(own_d) if t == tiles else rim(i_ref[q, t])
            hs[q, t] = jnp.concatenate([source[q], rim(s_ref[q, t])], 0)
            hd[q, t] = jnp.concatenate([diag[q], own_d], 0)
            hi[q, t] = jnp.concatenate([inverse[q], own_i], 0)
            fixes[q, t] = fixed[q]
        part[t] = more
        near_total = (diag[0] + diag[1]) + (diag[2] + diag[3]) - 12.0
        total = jnp.where((sub == 0) | (sub == 7), near_total, total)
        here = d2_virtual[...] if t == tiles else d2_ref[t]
        d[t] = jnp.concatenate([here, total], 0)
    def after_sweep(sweep):
        if sweep == 2:
            return
        for t in range(count):
            (a, ab, b, bb), (_, _, other_b, other_bb) = sides(t == tiles)
            todo = {}
            if sweep == 0:
                todo = {ab: (sub == 7) | (sub == 1), bb: (sub == 6) | (sub == 0)}
            else:
                todo = {b: sub == 6, other_b: sub == 1}
            for q, mask in todo.items():
                v[q][t, :8] = jnp.where(mask, fixes[q, t], v[q][t, :8])

    def of(ref):
        return lambda q, t: ref[q, t]

    left = of(hd), {1: rest1, 2: rest2}
    smooth(v, of(hs), of(hi), tiles, 16, left, after_sweep)
    row = row_ids(16)

    def valid(q, virtual):
        even, odd_red = reds(virtual)
        after_band = 0 if q == odd_red ^ 1 else 1
        before_band = 7 if q == even ^ 1 else 6
        first = 8 if q == odd_red ^ 1 else 9
        last = 15 if q == even ^ 1 else 14
        return (row <= after_band) | ((row >= before_band) & (row <= first)) | (row >= last)

    residuals(v, of(hs), left, tiles, c0, c1, lambda t, r: None, 16, valid)

    lane, row = lane_ids(rows), row_ids(rows)
    even = (lane + row) % 2 == 0
    odd = jnp.logical_not(even)

    def start(t, value):
        ends = value[8:]
        source = jnp.concatenate(
            [
                s2_ref[t, :8] + jnp.where(sub < 4, ends, 0.0),
                s2_ref[t, own - 8 :] + jnp.where(sub >= 4, ends, 0.0),
                value[:8] + part[t],
            ],
            0,
        )
        inverse = inverse_of(d[t])
        s[t] = source
        inv[t] = inverse
        virtual = isinstance(t, int) and t == tiles
        va[t] = jnp.where(odd if virtual else even, source * inverse, 0.0)

    restrict(c0, c1, tiles, 16, start, 16)

    def scan(v, use):
        up, down = roll_up(v[tiles]), roll_down(v[0])
        for t in range(tiles + 1):
            x = v[t]
            up_here, down_next = roll_up(x), roll_down(v[after(t, tiles)])
            north = jnp.where(lane == 0, up, up_here)
            south = jnp.where(lane == LANES - 1, down_next, down)
            use(t, x, (col_prev(x) + col_next(x)) + (north + south))
            up, down = up_here, down_next

    for old, new, mask, other in ((va, vb, odd, even), (vb, va, even, odd), (va, vb, odd, even)):

        def relax(t, x, beside):
            update = other if t == tiles else mask
            new[t] = jnp.where(update, (s[t] + beside) * inv[t], x)

        scan(old, relax)

    for t in range(tiles):
        solution_buf[:, t * LANES : (t + 1) * LANES] = vb[t, :own]
    copies = [
        pltpu.make_async_copy(src, dst, sems.at[i])
        for i, (src, dst) in enumerate(
            ((solution_buf, solution_ref), (residual_buf, residual_ref))
        )
    ]
    copies[0].start()

    def finish(t, x, beside):
        if t < tiles:
            where = slice(t * LANES, (t + 1) * LANES)
            residual_buf[:, where] = (s[t] - (d[t] * x - beside))[:own]

    scan(vb, finish)
    copies[1].start()
    for copy in copies:
        copy.wait()


VMEM = pl.BlockSpec(memory_space=pltpu.VMEM)
HBM = pl.BlockSpec(memory_space=pltpu.HBM)


def call(kernel, out_shapes, scratch, *args, sems=None, far_in=0, far_out=0):
    scratch = [pltpu.VMEM(x, F32) if isinstance(x, tuple) else x for x in scratch]
    if sems is not None:
        scratch.append(pltpu.SemaphoreType.DMA(sems))
    return pl.pallas_call(
        kernel,
        out_shape=[jax.ShapeDtypeStruct(shape, F32) for shape in out_shapes],
        in_specs=[HBM] * far_in + [VMEM] * (len(args) - far_in),
        out_specs=[HBM] * far_out + [VMEM] * (len(out_shapes) - far_out),
        scratch_shapes=scratch,
        compiler_params=pltpu.CompilerParams(vmem_limit_bytes=40 * 2**20),
    )(*args)


def swapped_with(x, by):
    count = lax.axis_size("lon")
    pairs = [(i, (i + by) % count) for i in range(0, count, 2)]
    return lax.ppermute(x, "lon", pairs + [(b, a) for a, b in pairs])


def swapped_edges(to_mate, to_other):
    from_mate = swapped_with(to_mate, 1)
    return from_mate, swapped_with(to_other, -1)


def body(right_side, texel_weight, seam_flags):
    columns, height = right_side.shape
    half_turn = lax.axis_size("lon") // 2
    tiles, rows = height // 256, columns // 2
    tiles1, rows1 = tiles // 2, rows // 2
    temp = (BATCH, 2, columns, LANES)
    natural = (2, tiles, columns, LANES)
    padded = (2, tiles, columns + 16, LANES)
    quarters1 = (4, tiles1, rows1, LANES)
    split = (2, 2, 8 * tiles, LANES)
    to_mate, to_other, corner = call(
        edge_kernel,
        [(2, tiles, 8, LANES), (2, tiles, 8, LANES), (2, 8, LANES)],
        [(16, height), pltpu.VMEM((32, height), BF16)]
        + [pltpu.VMEM(seam_flags.shape, jnp.int32), split, split, (tiles, 8, LANES)],
        *[
            pltpu.with_memory_space_constraint(x, pltpu.HBM)
            for x in (right_side, texel_weight, seam_flags)
        ],
        sems=(9,), far_in=3,
    )
    from_mate, from_other = swapped_edges(to_mate, to_other)
    corner_far = swapped_with(corner, half_turn - 1)
    corner_near = swapped_with(corner, half_turn + 1)
    ends = (2, 2, columns, LANES)
    (polar_own,) = call(
        polar_kernel, [(2, rows, LANES)], [ends, ends],
        right_side, texel_weight, seam_flags, corner,
    )
    polar = lax.ppermute(
        polar_own, "lon", [(i, (i + half_turn) % (2 * half_turn)) for i in range(2 * half_turn)]
    )
    s, d, inverse, d1, i1, d2 = call(
        bulk_kernel,
        [natural] * 3 + [quarters1, quarters1, quarters1[1:]],
        [(BATCH, columns, LANES), (tiles, 8, LANES), (tiles, rows, LANES), (BATCH, 2, rows, LANES)],
        right_side, texel_weight, seam_flags, polar_own,
    )

    def level_scratch(tiles, rows):
        return [(tiles + 1, rows, LANES)] * 6

    def halo_scratch(tiles):
        return [(4, tiles + 1, 8, LANES)] * 3

    pack1 = (2 * (tiles1 + 1) + tiles1 // 2 + 1, 8, LANES)
    r, s1, d1_virtual, d2_virtual, s2_own, to_mate, to_other = call(
        fine_kernel,
        [padded, (4, tiles1 + 1, rows1, LANES), (4, rows1, LANES), (rows1, LANES)]
        + [(tiles1 + 1, rows1, LANES), pack1, pack1],
        [padded, (4, tiles, 8, LANES), (4, rows + 8, LANES), (4, tiles, 8, LANES)]
        + [(tiles + 1, rows, LANES)] * 2
        + halo_scratch(tiles)
        + [(4, rows, LANES)] * 3
        + [(tiles + 1, rows, LANES), (BATCH, 2, rows, LANES)]
        + level_scratch(tiles1, rows1)
        + [(4, rows1, LANES)]
        + [(tiles1 + 1, rows1, LANES)] * 4
        + [(tiles1, rows1, LANES)] * 2,
        s, d, inverse, d1, i1, d2, from_other, from_mate, polar, corner_near, corner_far,
    )
    from_mate, from_other = swapped_edges(to_mate, to_other)
    (fine_residual,) = call(
        merge_kernel, [(columns, height)], [(columns, height)], r,
        sems=(GROUPS,), far_out=1,
    )
    wide = (tiles1 + 1, rows1 + 8, LANES)
    solution_2, residual_2 = call(
        coarse_kernel,
        [(columns // 4, height // 4)] * 2,
        level_scratch(tiles1, 16)
        + [(4, tiles1 + 1, 16, LANES)] * 3
        + [(tiles1 + 1, 8, LANES), (4, tiles1 + 1, 8, LANES)]
        + [(tiles1, 16, LANES)] * 2
        + [wide] * 5
        + [(columns // 4, height // 4)] * 2,
        s1, d1, i1, d1_virtual, d2, d2_virtual, s2_own, from_other, from_mate,
        sems=(2,), far_out=2,
    )
    return fine_residual, solution_2, residual_2


def solution(mesh):
    spec = P(("groups", "lon"), None)
    return jax.shard_map(
        body, mesh=mesh, in_specs=(spec,) * 3, out_specs=(spec,) * 3, check_vma=False
    )
```

```python
import jax
import jax.numpy as jnp
from jax import lax
from jax.experimental import pallas as pl
from jax.experimental.pallas import tpu as pltpu
from jax.sharding import PartitionSpec as P

TILE = 32
SEAM_SCALE = 0.1
LANES = 128
GROUPS = 4
BATCH = 4
F32 = jnp.float32
BF16 = jnp.bfloat16


def loop(count, body, carry=0, unroll=4):
    unroll = min(unroll, count)

    def steps(block, carry):
        for i in range(unroll):
            carry = body(block * unroll + i, carry)
        return carry

    whole = count // unroll
    carry = steps(0, carry) if whole == 1 else lax.fori_loop(0, whole, steps, carry)
    for t in range(whole * unroll, count):
        carry = body(t, carry)
    return carry


def before(t, tiles):
    return (tiles if t == 0 else t - 1) if isinstance(t, int) else jnp.where(t == 0, tiles, t - 1)


def after(t, tiles):
    return (0 if t == tiles else t + 1) if isinstance(t, int) else t + 1


def lane_ids(rows):
    return lax.broadcasted_iota(jnp.int32, (rows, LANES), 1)


def row_ids(rows):
    return lax.broadcasted_iota(jnp.int32, (rows, LANES), 0)


def roll_up(x):
    return pltpu.roll(x, 1, 1)


def roll_down(x):
    return pltpu.roll(x, LANES - 1, 1)


def roll_rows(x, by):
    by %= x.shape[0]
    return x if by == 0 else pltpu.roll(x, by, 0)


def roll_lanes(x, by):
    by %= LANES
    return x if by == 0 else pltpu.roll(x, by, 1)


def col_prev(x):
    return pltpu.roll(x, 1, 0)


def col_next(x):
    return pltpu.roll(x, x.shape[0] - 1, 0)


def inverse_of(x):
    return 1.0 / x


def selector(shape, rule):
    a = lax.broadcasted_iota(jnp.int32, shape, 0)
    b = lax.broadcasted_iota(jnp.int32, shape, 1)
    return jnp.where(rule(a, b), 1.0, 0.0).astype(BF16)


def splitter():
    return selector((256, 256), lambda a, b: a == 2 * (b % LANES) + b // LANES)


def merger():
    return selector((256, 256), lambda a, b: b == 2 * (a % LANES) + a // LANES)


def virtual_splitter():
    return selector(
        (LANES, 256),
        lambda a, b: a // 2 + jnp.where(a >= 64, 64, 0) + LANES * (a % 2) == b,
    )


def moved(x, matrix, exact=None):
    rows = x.shape[0]
    high = x.astype(BF16)
    low = (x - high.astype(F32)).astype(BF16)
    terms = [high, low] if exact is None else [high, low, exact]
    out = jnp.dot(jnp.concatenate(terms, 0), matrix, preferred_element_type=F32)
    both = out[:rows] + out[rows : 2 * rows]
    return both if exact is None else (both, out[2 * rows :])


def quarters_of(parts, temp):
    count = parts.shape[0] // 2
    temp[0] = parts[:, :LANES]
    temp[1] = parts[:, LANES:]
    return [temp[pr, pl.ds(pc, count, 2), :] for pc in (0, 1) for pr in (0, 1)]


def reds(swapped):
    return (1, 2) if swapped else (0, 3)


def interleaved(group, offset):
    sub = row_ids(8)
    packed = roll_rows(group[0], offset)
    for q in range(1, 4):
        packed = jnp.where(sub // 2 == q, roll_rows(group[q], 2 * q + offset), packed)
    return packed


def edge_packs(source, diag, swapped):
    sub = row_ids(8)
    even, odd = reds(swapped)
    rows = source[0].shape[0]
    packs = []
    for here, first, second, row, step in (
        (slice(rows - 8, rows), even, odd, 6, 1),
        (slice(0, 8), odd, even, 1, -1),
    ):
        gs = [x[here] for x in source]
        gd = [x[here] for x in diag]
        near = gs[first] * inverse_of(gd[first])
        far = roll_rows(gs[second] * inverse_of(gd[second]), step)
        gs[first] = jnp.where(sub == row, near, gs[first])
        gd[first] = jnp.where(sub == row, far, gd[first])
        offset = 2 if row == 6 else 0
        packs.append((interleaved(gs, offset), interleaved(gd, offset)))
    return packs


def unpacked_halo(left, right, swapped):
    sub = row_ids(8)
    even, odd = reds(swapped)
    (al, bl), (ar, br) = left, right
    source, diag = [], []
    for q in range(4):
        s = jnp.where(
            sub >= 6,
            roll_rows(al, 6 - 2 * q),
            jnp.where(sub <= 1, roll_rows(ar, -2 * q), 0.0),
        )
        d = jnp.where(
            sub >= 6,
            roll_rows(bl, 6 - 2 * q),
            jnp.where(sub <= 1, roll_rows(br, -2 * q), 4.0),
        )
        if q == even:
            s = jnp.where(sub == 2, roll_rows(br, 1 - 2 * odd), s)
            d = jnp.where((sub == 2) | (sub == 6), 1.0, d)
        if q == odd:
            s = jnp.where(sub == 5, roll_rows(bl, 5 - 2 * even), s)
            d = jnp.where((sub == 5) | (sub == 1), 1.0, d)
        source.append(s)
        diag.append(d)
    return source, diag


def is_odd():
    return lax.rem(lax.axis_index("lon"), 2) == 1


def chosen(odd, a, b):
    return jnp.where(odd, a, b), jnp.where(odd, b, a)


def store_edges(t, packs, odd, to_mate, to_other):
    right, left = packs
    for i in (0, 1):
        to_mate[i, t], to_other[i, t] = chosen(odd, left[i], right[i])


def sides(swapped):
    even, odd = reds(swapped)
    return (even, even ^ 1, odd, odd ^ 1), (odd, odd ^ 1, even, even ^ 1)


def paired(groups, shift):
    sub = row_ids(8)
    packed = roll_rows(groups[0], shift)
    for g in (1, 2, 3):
        packed = jnp.where(sub // 2 == g, roll_rows(groups[g], 2 * g + shift), packed)
    return packed


def state_packs(source, diag, last, first_black, residual, partial, diag2, swapped):
    sub = row_ids(8)
    rows = source[0].shape[0]
    packs = []
    for (a, ab, b, bb), here, near, far, step in zip(
        sides(swapped), (slice(rows - 8, rows), slice(0, 8)), (7, 0), (6, 1), (-1, 1)
    ):
        s, d, v = ([x[here] for x in group] for group in (source, diag, last))
        part, d2 = partial[here], diag2[here]
        beside = [
            s[bb] + v[a],
            d[bb],
            first_black[bb][here],
            v[b],
            s[b] - d[b] * v[b] + v[ab],
            residual[a][here] - v[bb],
            part,
            roll_rows(d2, -step),
        ]
        groups = [jnp.where(sub == far, y, x) for x, y in zip(s + d, beside)]
        shift = 2 if near == 7 else 0
        more = jnp.where(sub == far, d2, first_black[ab][here])
        more = jnp.where(sub == far + step, part, more)
        more = jnp.where(sub == far + 2 * step, part * inverse_of(d2), more)
        packs.append((paired(groups[:4], shift), paired(groups[4:], shift), more))
    return packs


def fill_halo(t, from_mate, from_other, odd, swapped, hs, hd, hi):
    al, ar = chosen(odd, from_mate[0, t], from_other[0, t])
    bl, br = chosen(odd, from_mate[1, t], from_other[1, t])
    source, diag = unpacked_halo((al, bl), (ar, br), swapped)
    for q in range(4):
        hs[q, t] = source[q]
        hd[q, t] = diag[q]
        hi[q, t] = inverse_of(diag[q])


def loader(own, halo, virtual, tiles):
    def load(q, t):
        if isinstance(t, int) and t == tiles:
            return jnp.concatenate([virtual[q], halo[q, t]], 0)
        return jnp.concatenate([own[q, t], halo[q, t]], 0)

    return load


def polar_packs(tiles_of):
    lane = lane_ids(tiles_of[0][0].shape[0])
    packs = []
    for pc in (0, 1):
        parts = [*tiles_of[2 * pc], *tiles_of[2 * pc + 1]]
        packed = parts[0]
        for m in range(1, 4):
            mine = (lane + (16 - 32 * m) % LANES) % LANES < 32
            packed = jnp.where(mine, roll_lanes(parts[m], 32 * m), packed)
        packs.append(packed)
    return packs


def polar_unpacked(x, q):
    lane = lane_ids(x.shape[1])
    used = (lane < 16) | (lane >= LANES - 16)
    m = 2 * (q % 2)
    return (
        jnp.where(used, roll_lanes(x[q // 2], 32 * m), 0.0),
        jnp.where(used, roll_lanes(x[q // 2], 32 * (m + 1)), 4.0),
    )


def seam_scales(flags, chunks):
    flag_cols, flag_lats = flags.shape
    flags = jnp.concatenate(
        [flags.astype(F32), jnp.zeros((8 - flag_cols, flag_lats), F32)], 0
    )
    lat = lax.broadcasted_iota(jnp.int32, (8, flag_lats), 1)
    stacked = jnp.concatenate([jnp.where(lat // 8 == c, flags, 0.0) for c in chunks], 0)
    spread = selector((flag_lats, LANES), lambda a, b: a % 8 == b // (TILE // 2))
    spread_flags = jnp.dot(stacked.astype(BF16), spread, preferred_element_type=F32)
    scale = jnp.where(spread_flags > 0.5, SEAM_SCALE, 1.0)
    return scale.reshape(len(chunks), 8, LANES)


def seam_rows(scales, flag_cols, rows):
    size = (rows // flag_cols, LANES)
    return jnp.concatenate(
        [jnp.broadcast_to(scales[i : i + 1], size) for i in range(flag_cols)], 0
    )


def edge_kernel(
    right_ref, weight_ref, flag_ref,
    right_here, weight_here, to_mate, to_other, corner_ref,
    flags, temp_s, temp_w, scale_ref, sems,
):
    columns, height = right_ref.shape
    tiles = height // 256
    pairs = [(flag_ref, flags)]
    inputs = (right_ref, right_here, 8), (weight_ref, weight_here, 16)
    for src, dst, size in inputs:
        for start in (0, columns - size):
            part = pl.ds(start, size)
            pairs.append((src.at[part], dst.at[part]))
    for src, dst, size in inputs:
        part = pl.ds(size, columns - 2 * size)
        pairs.append((src.at[part], dst.at[part]))
    copies = [
        pltpu.make_async_copy(src, dst, sems.at[i]) for i, (src, dst) in enumerate(pairs)
    ]
    for copy in copies:
        copy.start()
    odd = is_odd()
    matrix = splitter()
    flag_cols = flag_ref.shape[0]
    copies[0].wait()
    scale_ref[...] = seam_scales(flags[...], range(tiles))
    for copy in copies[1:5]:
        copy.wait()
    sub = row_ids(8)
    lanes = [slice(c * 256, (c + 1) * 256) for c in range(tiles)]

    def ends(size):
        return slice(0, size), slice(columns - size, columns)

    source, weight = moved(
        jnp.concatenate([right_here[at, w] for w in lanes for at in ends(8)], 0),
        matrix,
        jnp.concatenate([weight_here[at, w] for w in lanes for at in ends(16)], 0),
    )
    weight = weight.reshape(tiles, 32, 256)
    weight = jnp.concatenate([weight[:, :8], weight[:, 24:]], 1).reshape(tiles * 16, 256)
    source = quarters_of(source, temp_s)
    weight = quarters_of(weight, temp_w)
    found = []
    for c in range(tiles):
        here = slice(c * 8, (c + 1) * 8)
        scales = scale_ref[c]
        scale = jnp.where(sub < 4, scales[:1], scales[flag_cols - 1 : flag_cols])
        pair = [x[here] for x in source], [4.0 + w[here] * scale for w in weight]
        store_edges(c, edge_packs(*pair, False), odd, to_mate, to_other)
        if c in (0, tiles - 1):
            found.append(pair)
    both = mirrored_ends(*found)
    for pc in (0, 1):
        corner_ref[pc] = both[8 * pc : 8 * (pc + 1)]
    for copy in copies[5:]:
        copy.wait()


def mirrored_ends(first, last):
    mirror = selector((LANES, LANES), lambda a, b: a + b == LANES - 1)
    lane = lane_ids(first[0][0].shape[0])
    ends = [
        [jnp.where(lane >= 64, last[i][q ^ 1], first[i][q ^ 1]) for i in (0, 1)]
        for q in range(4)
    ]
    return moved(jnp.concatenate(polar_packs(ends), 0), mirror)


def polar_kernel(right_ref, weight_ref, flag_ref, edges_first, polar_ref, temp_s, temp_w):
    columns, height = right_ref.shape
    rows, tiles = columns // 2, height // 256
    scales = seam_scales(flag_ref[...], (0, tiles - 1))
    lanes = slice(0, 256), slice(height - 256, height)
    source, weight = moved(
        jnp.concatenate([right_ref[:, w] for w in lanes], 0),
        splitter(),
        jnp.concatenate([weight_ref[:, w] for w in lanes], 0),
    )
    found = []
    for end in (0, 1):
        here = slice(end * columns, (end + 1) * columns)
        scale = seam_rows(scales[end], flag_ref.shape[0], rows)
        found.append(
            (
                quarters_of(source[here], temp_s.at[end]),
                [4.0 + w * scale for w in quarters_of(weight[here], temp_w.at[end])],
            )
        )
    both = mirrored_ends(*found)
    for pc in (0, 1):
        polar_ref[pc] = both[pc * rows : (pc + 1) * rows]


def bulk_kernel(
    right_ref, weight_ref, flag_ref, polar_first,
    s_ref, d_ref, i_ref, d1_ref, i1_ref, d2_ref,
    temp, scale_ref, e_ref, split_temp,
):
    tiles, columns = s_ref.shape[1], s_ref.shape[2]
    rows = columns // 2
    matrix = splitter()
    scale_ref[...] = seam_scales(flag_ref[...], range(tiles))
    for start in range(0, tiles, BATCH):
        lanes = [slice((start + i) * 256, (start + i + 1) * 256) for i in range(BATCH)]
        source, weight = moved(
            jnp.concatenate([right_ref[:, w] for w in lanes], 0),
            matrix,
            jnp.concatenate([weight_ref[:, w] for w in lanes], 0),
        )
        for i in range(BATCH):
            c = start + i
            here = slice(i * columns, (i + 1) * columns)
            scale = seam_rows(scale_ref[c], flag_ref.shape[0], columns)
            screens = []
            for pr in (0, 1):
                half = slice(pr * LANES, (pr + 1) * LANES)
                screen = weight[here, half] * scale
                diag = 4.0 + screen
                s_ref[pr, c] = source[here, half]
                d_ref[pr, c] = diag
                i_ref[pr, c] = 1.0 / diag
                screens.append(screen)
            temp[i] = screens[0] + screens[1]
            e_ref[c] = temp[i, pl.ds(0, rows, 2), :] + temp[i, pl.ds(1, rows, 2), :]

    def use(c, screen):
        for q in range(4):
            d1_ref[q, c] = 4.0 + screen[q]
            i1_ref[q, c] = inverse_of(4.0 + screen[q])
        d2_ref[c] = 4.0 + ((screen[0] + screen[1]) + (screen[2] + screen[3]))

    split_tiles(lambda t: e_ref[t], tiles // 2, rows, matrix, split_temp, use)


def split_tiles(load, tiles, rows, matrix, temp, use):
    for start in range(0, tiles, BATCH):
        wide = [
            jnp.concatenate([load(2 * c), load(2 * c + 1)], 1)
            for c in range(start, start + BATCH)
        ]
        out = moved(jnp.concatenate(wide, 0), matrix)
        for i in range(BATCH):
            use(start + i, quarters_of(out[i * rows : (i + 1) * rows], temp.at[i, :, :rows]))


def half_sweep(v, load_s, load_i, tiles, red, unroll, left=None):
    rows = v[0].shape[1]
    lane = lane_ids(rows)
    y, z, qa, qb = (1, 2, 0, 3) if red else (3, 0, 2, 1)
    col_a, col_b = (col_prev, col_next) if red else (col_next, col_prev)

    def beside_virtual(q):
        ns, we = q ^ 1, q ^ 2
        here = v[ns][tiles]
        if q % 2 == 0:
            lat = jnp.where(lane == 0, roll_up(v[ns][tiles - 1]), roll_up(here))
        else:
            lat = jnp.where(lane == LANES - 1, roll_down(v[ns][0]), roll_down(here))
        cols = v[we][tiles]
        return (here + lat) + (cols + (col_prev if q < 2 else col_next)(cols))

    held = [
        (q, (load_s(q, tiles) + beside_virtual(q)) * load_i(q, tiles)) for q in (y, z)
    ]

    def body(t, carry):
        y_before, z_here = carry
        vy, vz = v[y][t], v[z][t]
        y_here = roll_up(vy)
        z_after = roll_down(v[z][t + 1])
        lat_a = vy + jnp.where(lane == 0, y_before, y_here)
        lat_b = vz + jnp.where(lane == LANES - 1, z_after, z_here)
        all_a = load_s(qa, t) + (lat_a + (vz + col_a(vz)))
        all_b = load_s(qb, t) + (lat_b + (vy + col_b(vy)))
        new_a, new_b = all_a * load_i(qa, t), all_b * load_i(qb, t)
        v[qa][t], v[qb][t] = new_a, new_b
        if left is not None:
            load_d, rest = left
            rest[qa][t] = all_a - load_d(qa, t) * new_a
            rest[qb][t] = all_b - load_d(qb, t) * new_b
        return y_here, z_after

    loop(tiles, body, (roll_up(v[y][tiles]), roll_down(v[z][0])), unroll)
    for q, value in held:
        v[q][tiles] = value


def smooth(v, load_s, load_i, tiles, unroll, left, after_sweep=None):
    zeros = jnp.zeros(v[0].shape[1:], F32)

    def first(t, _):
        for q in (0, 3):
            v[q][t] = load_s(q, t) * load_i(q, t)
        return 0

    loop(tiles, first, 0, unroll)
    for q in (1, 2):
        v[q][0] = zeros
        v[q][tiles - 1] = zeros
        v[q][tiles] = load_s(q, tiles) * load_i(q, tiles)
        v[3 * (q - 1)][tiles] = zeros
    for sweep, red in enumerate((False, True, False)):
        half_sweep(v, load_s, load_i, tiles, red, unroll, left if sweep == 2 else None)
        if after_sweep is not None:
            after_sweep(sweep)


def residuals(v, load_s, left, tiles, c0, c1, keep, unroll, valid=None):
    lane = lane_ids(v[0].shape[1])
    load_d, rest = left

    def use(t, r):
        keep(t, r)
        if valid is not None:
            virtual = isinstance(t, int) and t == tiles
            r = [jnp.where(valid(q, virtual), r[q], 0.0) for q in range(4)]
        c0[t] = (col_prev(r[2]) + col_next(r[0])) + 3.0 * (r[0] + r[2])
        c1[t] = (col_prev(r[3]) + col_next(r[1])) + 3.0 * (r[1] + r[3])

    def north(q, t):
        return jnp.where(lane == 0, roll_up(v[q][before(t, tiles)]), roll_up(v[q][t]))

    def south(q, t):
        return jnp.where(
            lane == LANES - 1, roll_down(v[q][after(t, tiles)]), roll_down(v[q][t])
        )

    def full(t):
        x = [v[q][t] for q in range(4)]
        beside = [
            (x[1] + north(1, t)) + (x[2] + col_prev(x[2])),
            (x[0] + south(0, t)) + (x[3] + col_prev(x[3])),
            (x[3] + north(3, t)) + (x[0] + col_next(x[0])),
            (x[2] + south(2, t)) + (x[1] + col_next(x[1])),
        ]
        use(t, [load_s(q, t) - (load_d(q, t) * x[q] - beside[q]) for q in range(4)])

    def body(i, carry):
        t = i + 1
        up, down = carry
        x = [v[q][t] for q in range(4)]
        up_here, down_next = roll_up(x[1]), roll_down(v[2][t + 1])
        beside0 = (x[1] + jnp.where(lane == 0, up, up_here)) + (x[2] + col_prev(x[2]))
        beside3 = (x[2] + jnp.where(lane == LANES - 1, down_next, down)) + (
            x[1] + col_next(x[1])
        )
        r0 = load_s(0, t) - (load_d(0, t) * x[0] - beside0)
        r3 = load_s(3, t) - (load_d(3, t) * x[3] - beside3)
        use(t, [r0, rest[1][t], rest[2][t], r3])
        return up_here, down_next

    full(0)
    loop(tiles - 2, body, (roll_up(v[1][0]), roll_down(v[2][1])), unroll)
    full(tiles - 1)
    full(tiles)


def restrict(c0, c1, tiles, rows, use, unroll):
    lane = lane_ids(rows)

    def body(t, carry):
        up, down = carry
        here, other = c0[t, :rows], c1[t, :rows]
        up_here = roll_up(other)
        down_next = roll_down(c0[after(t, tiles), :rows])
        north = jnp.where(lane == 0, up, up_here)
        south = jnp.where(lane == LANES - 1, down_next, down)
        use(t, ((north + south) + 3.0 * (here + other)) * (1.0 / 16.0))
        return up_here, down_next

    start = roll_up(c1[tiles, :rows]), roll_down(c0[0, :rows])
    body(tiles, loop(tiles, body, start, unroll))


class Fine:
    def __init__(self, own, halo, virtual, tiles, columns):
        self.own, self.halo, self.virtual = own, halo, virtual
        self.tiles, self.columns = tiles, columns

    def part(self, parity, t, start):
        return self.own[parity][t, pl.ds(8 + start, self.columns // 2, 2), :]

    def rows(self, q, t):
        return self.part(q % 2, t, q // 2)

    def whole(self, q, t):
        if t == self.tiles:
            return self.virtual[q][...]
        return jnp.concatenate([self.rows(q, t), self.halo[q][t]], 0)

    def ends(self, q, t):
        if t == self.tiles:
            whole = self.virtual[q][...]
            return whole[: self.columns // 2], whole[self.columns // 2 :]
        return self.rows(q, t), self.halo[q][t]

    def line(self, parity, t, column):
        row = self.own[parity][t, 8 + column : 9 + column]
        return jnp.broadcast_to(row, (8, LANES))

    def put(self, q, t, own, halo):
        pr, pc = q % 2, q // 2
        self.own[pr][t, pl.ds(8 + pc, self.columns // 2, 2), :] = own
        self.halo[q][t] = halo
        if pc == 1:
            self.own[pr][t, 7:8] = halo[7:8]
        else:
            at = 8 + self.columns
            self.own[pr][t, at : at + 1] = halo[0:1]

    def beside_columns(self, q, t, halo):
        sub = row_ids(8)
        pr, pc = q % 2, q // 2
        own = self.part(pr, t, pc - 1) + self.part(pr, t, pc + 1)
        if pc == 0:
            other = jnp.where(sub == 0, self.line(pr, t, self.columns - 1), col_prev(halo))
        else:
            other = jnp.where(sub == 7, self.line(pr, t, 0), col_next(halo))
        return own, halo + other


def fine_sweep(v, load_s, load_i, whole_s, whole_i, red, left):
    tiles = v.tiles
    y, z, qa, qb = (1, 2, 0, 3) if red else (3, 0, 2, 1)

    def lane_sum(parts, rolled, edge, lane_at):
        return [
            x + jnp.where(lane_ids(x.shape[0]) == lane_at, e, r)
            for x, r, e in zip(parts, rolled, edge)
        ]

    def beside_virtual(q):
        here, cols = v.whole(q ^ 1, tiles), v.whole(q ^ 2, tiles)
        lane = lane_ids(here.shape[0])
        if q % 2 == 0:
            lat = jnp.where(lane == 0, roll_up(v.whole(q ^ 1, tiles - 1)), roll_up(here))
        else:
            lat = jnp.where(lane == LANES - 1, roll_down(v.whole(q ^ 1, 0)), roll_down(here))
        return (here + lat) + (cols + (col_prev if q < 2 else col_next)(cols))

    held = [
        (q, (whole_s(q, tiles) + beside_virtual(q)) * whole_i(q, tiles)) for q in (y, z)
    ]
    y_before = [roll_up(x) for x in v.ends(y, tiles)]
    z_here = [roll_down(x) for x in v.ends(z, 0)]
    for t in range(tiles):
        vy, vz = v.ends(y, t), v.ends(z, t)
        y_here = [roll_up(x) for x in vy]
        z_after = [roll_down(x) for x in v.ends(z, t + 1)]
        lat_a = lane_sum(vy, y_here, y_before, 0)
        lat_b = lane_sum(vz, z_here, z_after, LANES - 1)
        new = []
        for q, lat, halo in ((qa, lat_a, vz[1]), (qb, lat_b, vy[1])):
            cols = v.beside_columns(q, t, halo)
            total = [x + (l + c) for x, l, c in zip(load_s(q, t), lat, cols)]
            value = [x * i for x, i in zip(total, load_i(q, t))]
            new.append((q, value))
            if left is not None:
                load_d, rest = left
                rest.put(q, t, *[x - d * u for x, d, u in zip(total, load_d(q, t), value)])
        for q, value in new:
            v.put(q, t, *value)
        y_before, z_here = y_here, z_after
    for q, value in held:
        v.virtual[q][...] = value


def fine_residuals(v, load_s, load_d, whole_s, whole_d, rest, c0, c1):
    tiles = v.tiles
    rows = v.columns // 2

    def columns_summed(t):
        for pr, ref in ((0, c0), (1, c1)):
            outer = rest.part(pr, t, -1) + rest.part(pr, t, 2)
            inner = rest.part(pr, t, 0) + rest.part(pr, t, 1)
            ref[t] = outer + 3.0 * inner

    def full(t):
        x = [v.whole(q, t) for q in range(4)]
        lane = lane_ids(x[0].shape[0])

        def north(q):
            return jnp.where(lane == 0, roll_up(v.whole(q, before(t, tiles))), roll_up(x[q]))

        def south(q):
            return jnp.where(
                lane == LANES - 1, roll_down(v.whole(q, after(t, tiles))), roll_down(x[q])
            )

        beside = [
            (x[1] + north(1)) + (x[2] + col_prev(x[2])),
            (x[0] + south(0)) + (x[3] + col_prev(x[3])),
            (x[3] + north(3)) + (x[0] + col_next(x[0])),
            (x[2] + south(2)) + (x[1] + col_next(x[1])),
        ]
        r = [whole_s(q, t) - (whole_d(q, t) * x[q] - beside[q]) for q in range(4)]
        if t == tiles:
            c0[t] = ((col_prev(r[2]) + col_next(r[0])) + 3.0 * (r[0] + r[2]))[:rows]
            c1[t] = ((col_prev(r[3]) + col_next(r[1])) + 3.0 * (r[1] + r[3]))[:rows]
        else:
            for q in range(4):
                rest.put(q, t, r[q][:rows], r[q][rows:])
            columns_summed(t)

    full(0)
    up = [roll_up(x) for x in v.ends(1, 0)]
    down = [roll_down(x) for x in v.ends(2, 1)]
    for t in range(1, tiles - 1):
        x = [v.ends(q, t) for q in range(4)]
        up_here = [roll_up(part) for part in x[1]]
        down_next = [roll_down(part) for part in v.ends(2, t + 1)]
        for q, ns, near, edge, lane_at in (
            (0, 1, up_here, up, 0), (3, 2, down, down_next, LANES - 1)
        ):
            cols = v.beside_columns(q, t, x[q ^ 2][1])
            r = []
            for i, (s, d) in enumerate(zip(load_s(q, t), load_d(q, t))):
                lane = lane_ids(s.shape[0])
                beside = x[ns][i] + jnp.where(lane == lane_at, edge[i], near[i]) + cols[i]
                r.append(s - (d * x[q][i] - beside))
            rest.put(q, t, *r)
        columns_summed(t)
        up, down = up_here, down_next
    full(tiles - 1)
    full(tiles)


def fine_kernel(
    s_ref, d_ref, i_ref, d1_ref, i1_ref, d2_ref,
    from_other, from_mate, polar_ref, corner_near, corner_far,
    r_ref, s1_ref, d1_virtual, d2_virtual, s2_ref, to_mate, to_other,
    v_ref, hv, pv, hr, c0, c1, hs, hd, hi, ps, pd, pi, n1, temp,
    w0, w1, w2, w3, e0, e1, pi1, black_even, black_odd, red_even, red_odd,
    part1, part2,
):
    tiles, columns = s_ref.shape[1], s_ref.shape[2]
    rows = columns // 2
    sub = row_ids(8)
    odd = is_odd()

    def halo(t, _):
        fill_halo(t, from_mate, from_other, odd, False, hs, hd, hi)
        return 0

    loop(tiles, halo, 0, 8)
    total = -16.0
    for q in range(4):
        own_s, own_d = polar_unpacked(polar_ref, q)
        near_s, near_d = polar_unpacked(corner_near, q)
        far_s, far_d = polar_unpacked(corner_far, q)
        left_s, right_s = chosen(odd, near_s, far_s)
        left_d, right_d = chosen(odd, near_d, far_d)
        total = total + own_d
        ps[q] = own_s
        pd[q] = own_d
        pi[q] = inverse_of(own_d)
        source = jnp.where(sub >= 5, left_s, jnp.where(sub <= 2, right_s, 0.0))
        diag = jnp.where(sub >= 5, left_d, jnp.where(sub <= 2, right_d, 4.0))
        hs[q, tiles] = source
        hd[q, tiles] = diag
        hi[q, tiles] = inverse_of(diag)

    def loaders(ref, halo, virtual):
        def split(q, t):
            return ref[q % 2, t, pl.ds(q // 2, rows, 2), :], halo[q, t]

        def whole(q, t):
            if t == tiles:
                return jnp.concatenate([virtual[q], halo[q, t]], 0)
            return jnp.concatenate(split(q, t), 0)

        return split, whole

    load_s, whole_s = loaders(s_ref, hs, ps)
    load_d, whole_d = loaders(d_ref, hd, pd)
    load_i, whole_i = loaders(i_ref, hi, pi)

    def held(own_ref, halo_ref):
        return Fine(
            [own_ref.at[p] for p in (0, 1)],
            [halo_ref.at[q] for q in range(4)],
            [pv.at[q] for q in range(4)],
            tiles,
            columns,
        )

    v, rest = held(v_ref, hv), held(r_ref, hr)
    for t in range(tiles):
        for q in (0, 3):
            v.put(q, t, *[x * i for x, i in zip(load_s(q, t), load_i(q, t))])
    for q in (1, 2):
        for t in (0, tiles - 1):
            v.put(q, t, jnp.zeros((rows, LANES), F32), jnp.zeros((8, LANES), F32))
        pv[q] = whole_s(q, tiles) * whole_i(q, tiles)
        pv[3 * (q - 1)] = jnp.zeros((rows + 8, LANES), F32)
    for red, left in ((False, None), (True, None), (False, (load_d, rest))):
        fine_sweep(v, load_s, load_i, whole_s, whole_i, red, left)
    fine_residuals(v, load_s, load_d, whole_s, whole_d, rest, c0, c1)

    def coarse(t, value):
        n1[t] = value

    restrict(c0, c1, tiles, rows, coarse, tiles)

    def use(c, source):
        for q in range(4):
            s1_ref[q, c] = source[q]

    tiles1 = tiles // 2
    split_tiles(lambda t: n1[t], tiles1, rows, splitter(), temp, use)
    out = moved(jnp.concatenate([n1[tiles], total], 0), virtual_splitter())
    source = quarters_of(out[:rows], temp.at[0])
    screen = quarters_of(out[rows:], temp.at[1])
    for q in range(4):
        s1_ref[q, tiles1] = source[q]
        d1_virtual[q] = 4.0 + screen[q]
        pi1[q] = inverse_of(4.0 + screen[q])
    d2_virtual[...] = 4.0 + ((screen[0] + screen[1]) + (screen[2] + screen[3]))

    def own(main, virtual):
        return lambda q, t: virtual[q] if isinstance(t, int) and t == tiles1 else main[q, t]

    w = [w0, w1, w2, w3]
    rows1 = rows // 2
    row = row_ids(rows1)
    load_s, load_d = own(s1_ref, s1_ref.at[:, tiles1]), own(d1_ref, d1_virtual)

    def after_sweep(sweep):
        if sweep == 0:
            for t in range(tiles1 + 1):
                even, odd_red = reds(t == tiles1)
                black_even[t] = w[even ^ 1][t]
                black_odd[t] = w[odd_red ^ 1][t]

    left = load_d, {1: part1, 2: part2}
    smooth(w, load_s, own(i1_ref, pi1), tiles1, 16, left, after_sweep)

    def valid(q, virtual):
        even, odd_red = reds(virtual)
        first = 1 if q == odd_red ^ 1 else 2
        last = rows1 - 2 if q == even ^ 1 else rows1 - 3
        return (row >= first) & (row <= last)

    def keep_red(t, r):
        even, odd_red = reds(isinstance(t, int) and t == tiles1)
        red_even[t] = r[even]
        red_odd[t] = r[odd_red]

    residuals(w, load_s, left, tiles1, e0, e1, keep_red, 16, valid)
    shared = {}

    def edges(t, partial):
        virtual = t == tiles1
        even, odd_red = reds(virtual)
        s2_ref[t] = partial
        packs = state_packs(
            [s1_ref[q, t] for q in range(4)],
            [load_d(q, t) for q in range(4)],
            [w[q][t] for q in range(4)],
            {even ^ 1: black_even[t], odd_red ^ 1: black_odd[t]},
            {even: red_even[t], odd_red: red_odd[t]},
            partial,
            d2_virtual[...] if virtual else d2_ref[t],
            virtual,
        )
        right, left = packs
        count = tiles1 + 1
        for i in (0, 1):
            to_mate[i * count + t], to_other[i * count + t] = chosen(odd, left[i], right[i])
        if t % 2 == 0:
            pair = chosen(odd, left[2], roll_rows(right[2], 4))
            shared[0] = pair
        else:
            pair = chosen(odd, roll_rows(left[2], 4), right[2])
            pair = [jnp.where(sub < 4, x, y) for x, y in zip(shared[0], pair)]
        if t % 2 == 1 or virtual:
            to_mate[2 * count + t // 2], to_other[2 * count + t // 2] = pair

    restrict(e0, e1, tiles1, rows1, edges, 16)


def merge_kernel(r_ref, out_ref, out_buf, sems):
    tiles = r_ref.shape[1]
    columns = out_ref.shape[0]
    matrix = merger()
    chunk = out_ref.shape[1] // GROUPS
    copies = []
    for group in range(GROUPS):
        for batch in range(tiles // GROUPS // BATCH):
            start = group * (tiles // GROUPS) + batch * BATCH
            own = slice(8, 8 + columns)
            both = [
                jnp.concatenate([r_ref[0, start + i, own], r_ref[1, start + i, own]], 1)
                for i in range(BATCH)
            ]
            out = moved(jnp.concatenate(both, 0), matrix)
            for i in range(BATCH):
                where = slice((start + i) * 256, (start + i + 1) * 256)
                out_buf[:, where] = out[columns * i : columns * (i + 1)]
        part = pl.ds(group * chunk, chunk)
        copy = pltpu.make_async_copy(out_buf.at[:, part], out_ref.at[:, part], sems.at[group])
        copy.start()
        copies.append(copy)
    for copy in copies:
        copy.wait()


def coarse_kernel(
    s_ref, d_ref, i_ref, d_virtual, d2_ref, d2_virtual, s2_ref, from_other, from_mate,
    solution_ref, residual_ref,
    v0, v1, v2, v3, c0, c1, hs, hd, hi, part, fixes, rest1, rest2, s, d, inv, va, vb,
):
    v = [v0, v1, v2, v3]
    tiles, own = d_ref.shape[1], d_ref.shape[2]
    rows = own + 8
    count = tiles + 1
    sub = row_ids(8)
    odd_band = is_odd()
    def rim(x):
        return jnp.where(sub < 4, x[:8], x[own - 8 :])

    for t in range(count):
        places = t, count + t, 2 * count + t // 2
        packs = [chosen(odd_band, from_mate[i], from_other[i]) for i in places]
        source = [jnp.zeros((8, LANES), F32)] * 4
        diag = [jnp.full((8, LANES), 4.0, F32)] * 4
        inverse = [jnp.zeros((8, LANES), F32)] * 4
        fixed = [jnp.zeros((8, LANES), F32)] * 4
        more = jnp.zeros((8, LANES), F32)
        total = jnp.ones((8, LANES), F32)
        for side, (a, ab, b, bb) in enumerate(sides(t == tiles)):
            near, far, step = (7, 6, -1) if side == 0 else (0, 1, 1)
            first = 6 if side == 0 else 0
            pack0, pack1, pack2 = (pair[side] for pair in packs)
            groups = [
                roll_rows(pack, first - 2 * g) for pack in (pack0, pack1) for g in range(4)
            ]
            pack2 = roll_rows(pack2, 4 * (t % 2) + (4 if side == 0 else 0))

            def put(group, q, at, x):
                group[q] = jnp.where(sub == at, x, group[q])

            for q in range(4):
                put(source, q, near, groups[q])
                put(diag, q, near, groups[4 + q])
            put(source, bb, far, groups[0])
            put(diag, bb, far, groups[1])
            put(fixed, bb, far, groups[2])
            put(fixed, b, far, groups[3])
            put(source, b, far, groups[4])
            put(diag, b, far, 0.0)
            put(source, a, far, groups[5])
            put(fixed, ab, near, pack2)
            more = jnp.where(sub == far, groups[6], more)
            more = jnp.where((sub == far + step) | (sub == far + 2 * step), pack2, more)
            total = jnp.where(sub == far, pack2, total)
            total = jnp.where(sub == far + step, roll_rows(groups[7], step), total)
            for q in range(4):
                known = (sub == near) | (sub == far) if q == bb else sub == near
                inverse[q] = jnp.where(known, inverse_of(diag[q]), inverse[q])
        for q in range(4):
            own_d = rim(d_virtual[q] if t == tiles else d_ref[q, t])
            own_i = inverse_of(own_d) if t == tiles else rim(i_ref[q, t])
            hs[q, t] = jnp.concatenate([source[q], rim(s_ref[q, t])], 0)
            hd[q, t] = jnp.concatenate([diag[q], own_d], 0)
            hi[q, t] = jnp.concatenate([inverse[q], own_i], 0)
            fixes[q, t] = fixed[q]
        part[t] = more
        near_total = (diag[0] + diag[1]) + (diag[2] + diag[3]) - 12.0
        total = jnp.where((sub == 0) | (sub == 7), near_total, total)
        here = d2_virtual[...] if t == tiles else d2_ref[t]
        d[t] = jnp.concatenate([here, total], 0)
    def after_sweep(sweep):
        if sweep == 2:
            return
        for t in range(count):
            (a, ab, b, bb), (_, _, other_b, other_bb) = sides(t == tiles)
            todo = {}
            if sweep == 0:
                todo = {ab: (sub == 7) | (sub == 1), bb: (sub == 6) | (sub == 0)}
            else:
                todo = {b: sub == 6, other_b: sub == 1}
            for q, mask in todo.items():
                v[q][t, :8] = jnp.where(mask, fixes[q, t], v[q][t, :8])

    def of(ref):
        return lambda q, t: ref[q, t]

    left = of(hd), {1: rest1, 2: rest2}
    smooth(v, of(hs), of(hi), tiles, 16, left, after_sweep)
    row = row_ids(16)

    def valid(q, virtual):
        even, odd_red = reds(virtual)
        after_band = 0 if q == odd_red ^ 1 else 1
        before_band = 7 if q == even ^ 1 else 6
        first = 8 if q == odd_red ^ 1 else 9
        last = 15 if q == even ^ 1 else 14
        return (row <= after_band) | ((row >= before_band) & (row <= first)) | (row >= last)

    residuals(v, of(hs), left, tiles, c0, c1, lambda t, r: None, 16, valid)

    lane, row = lane_ids(rows), row_ids(rows)
    even = (lane + row) % 2 == 0
    odd = jnp.logical_not(even)

    def start(t, value):
        ends = value[8:]
        source = jnp.concatenate(
            [
                s2_ref[t, :8] + jnp.where(sub < 4, ends, 0.0),
                s2_ref[t, own - 8 :] + jnp.where(sub >= 4, ends, 0.0),
                value[:8] + part[t],
            ],
            0,
        )
        inverse = inverse_of(d[t])
        s[t] = source
        inv[t] = inverse
        virtual = isinstance(t, int) and t == tiles
        va[t] = jnp.where(odd if virtual else even, source * inverse, 0.0)

    restrict(c0, c1, tiles, 16, start, 16)

    def scan(v, use):
        up, down = roll_up(v[tiles]), roll_down(v[0])
        for t in range(tiles + 1):
            x = v[t]
            up_here, down_next = roll_up(x), roll_down(v[after(t, tiles)])
            north = jnp.where(lane == 0, up, up_here)
            south = jnp.where(lane == LANES - 1, down_next, down)
            use(t, x, (col_prev(x) + col_next(x)) + (north + south))
            up, down = up_here, down_next

    for old, new, mask, other in ((va, vb, odd, even), (vb, va, even, odd), (va, vb, odd, even)):

        def relax(t, x, beside):
            update = other if t == tiles else mask
            new[t] = jnp.where(update, (s[t] + beside) * inv[t], x)

        scan(old, relax)

    def finish(t, x, beside):
        if t < tiles:
            where = slice(t * LANES, (t + 1) * LANES)
            solution_ref[:, where] = x[:own]
            residual_ref[:, where] = (s[t] - (d[t] * x - beside))[:own]

    scan(vb, finish)


VMEM = pl.BlockSpec(memory_space=pltpu.VMEM)
HBM = pl.BlockSpec(memory_space=pltpu.HBM)


def call(kernel, out_shapes, scratch, *args, sems=None, far_in=0, far_out=0):
    scratch = [pltpu.VMEM(x, F32) if isinstance(x, tuple) else x for x in scratch]
    if sems is not None:
        scratch.append(pltpu.SemaphoreType.DMA(sems))
    return pl.pallas_call(
        kernel,
        out_shape=[
            jax.ShapeDtypeStruct(x, F32) if isinstance(x, tuple) else x for x in out_shapes
        ],
        in_specs=[HBM] * far_in + [VMEM] * (len(args) - far_in),
        out_specs=[HBM] * far_out + [VMEM] * (len(out_shapes) - far_out),
        scratch_shapes=scratch,
        compiler_params=pltpu.CompilerParams(vmem_limit_bytes=40 * 2**20),
    )(*args)


def swapped_with(x, by):
    count = lax.axis_size("lon")
    pairs = [(i, (i + by) % count) for i in range(0, count, 2)]
    return lax.ppermute(x, "lon", pairs + [(b, a) for a, b in pairs])


def swapped_edges(to_mate, to_other):
    from_mate = swapped_with(to_mate, 1)
    return from_mate, swapped_with(to_other, -1)


def body(right_side, texel_weight, seam_flags):
    columns, height = right_side.shape
    half_turn = lax.axis_size("lon") // 2
    tiles, rows = height // 256, columns // 2
    tiles1, rows1 = tiles // 2, rows // 2
    temp = (BATCH, 2, columns, LANES)
    natural = (2, tiles, columns, LANES)
    padded = (2, tiles, columns + 16, LANES)
    quarters1 = (4, tiles1, rows1, LANES)
    split = (2, 16 * tiles, LANES)
    right_here, weight_here, to_mate, to_other, corner = call(
        edge_kernel,
        [(columns, height), jax.ShapeDtypeStruct((columns, height), BF16)]
        + [(2, tiles, 8, LANES), (2, tiles, 8, LANES), (2, 8, LANES)],
        [pltpu.VMEM(seam_flags.shape, jnp.int32), split, split, (tiles, 8, LANES)],
        *[
            pltpu.with_memory_space_constraint(x, pltpu.HBM)
            for x in (right_side, texel_weight, seam_flags)
        ],
        sems=(7,), far_in=3,
    )
    from_mate, from_other = swapped_edges(to_mate, to_other)
    corner_far = swapped_with(corner, half_turn - 1)
    corner_near = swapped_with(corner, half_turn + 1)
    ends = (2, 2, columns, LANES)
    (polar_own,) = call(
        polar_kernel, [(2, rows, LANES)], [ends, ends],
        right_here, weight_here, seam_flags, corner,
    )
    polar = lax.ppermute(
        polar_own, "lon", [(i, (i + half_turn) % (2 * half_turn)) for i in range(2 * half_turn)]
    )
    s, d, inverse, d1, i1, d2 = call(
        bulk_kernel,
        [natural] * 3 + [quarters1, quarters1, quarters1[1:]],
        [(BATCH, columns, LANES), (tiles, 8, LANES), (tiles, rows, LANES), (BATCH, 2, rows, LANES)],
        right_here, weight_here, seam_flags, polar_own,
    )

    def level_scratch(tiles, rows):
        return [(tiles + 1, rows, LANES)] * 6

    def halo_scratch(tiles):
        return [(4, tiles + 1, 8, LANES)] * 3

    pack1 = (2 * (tiles1 + 1) + tiles1 // 2 + 1, 8, LANES)
    r, s1, d1_virtual, d2_virtual, s2_own, to_mate, to_other = call(
        fine_kernel,
        [padded, (4, tiles1 + 1, rows1, LANES), (4, rows1, LANES), (rows1, LANES)]
        + [(tiles1 + 1, rows1, LANES), pack1, pack1],
        [padded, (4, tiles, 8, LANES), (4, rows + 8, LANES), (4, tiles, 8, LANES)]
        + [(tiles + 1, rows, LANES)] * 2
        + halo_scratch(tiles)
        + [(4, rows, LANES)] * 3
        + [(tiles + 1, rows, LANES), (BATCH, 2, rows, LANES)]
        + level_scratch(tiles1, rows1)
        + [(4, rows1, LANES)]
        + [(tiles1 + 1, rows1, LANES)] * 4
        + [(tiles1, rows1, LANES)] * 2,
        s, d, inverse, d1, i1, d2, from_other, from_mate, polar, corner_near, corner_far,
    )
    from_mate, from_other = swapped_edges(to_mate, to_other)
    (fine_residual,) = call(
        merge_kernel, [(columns, height)], [(columns, height)], r,
        sems=(GROUPS,), far_out=1,
    )
    wide = (tiles1 + 1, rows1 + 8, LANES)
    solution_2, residual_2 = call(
        coarse_kernel,
        [(columns // 4, height // 4)] * 2,
        level_scratch(tiles1, 16)
        + [(4, tiles1 + 1, 16, LANES)] * 3
        + [(tiles1 + 1, 8, LANES), (4, tiles1 + 1, 8, LANES)]
        + [(tiles1, 16, LANES)] * 2
        + [wide] * 5,
        s1, d1, i1, d1_virtual, d2, d2_virtual, s2_own, from_other, from_mate,
    )
    return fine_residual, solution_2, residual_2


def solution(mesh):
    spec = P(("groups", "lon"), None)
    return jax.shard_map(
        body, mesh=mesh, in_specs=(spec,) * 3, out_specs=(spec,) * 3, check_vma=False
    )
```

```python
import jax
import jax.numpy as jnp
from jax import lax
from jax.experimental import pallas as pl
from jax.experimental.pallas import tpu as pltpu
from jax.sharding import PartitionSpec as P

TILE = 32
SEAM_SCALE = 0.1
LANES = 128
GROUPS = 4
BATCH = 4
F32 = jnp.float32
BF16 = jnp.bfloat16


def loop(count, body, carry=0, unroll=4):
    unroll = min(unroll, count)

    def steps(block, carry):
        for i in range(unroll):
            carry = body(block * unroll + i, carry)
        return carry

    whole = count // unroll
    carry = steps(0, carry) if whole == 1 else lax.fori_loop(0, whole, steps, carry)
    for t in range(whole * unroll, count):
        carry = body(t, carry)
    return carry


def before(t, tiles):
    return (tiles if t == 0 else t - 1) if isinstance(t, int) else jnp.where(t == 0, tiles, t - 1)


def after(t, tiles):
    return (0 if t == tiles else t + 1) if isinstance(t, int) else t + 1


def lane_ids(rows):
    return lax.broadcasted_iota(jnp.int32, (rows, LANES), 1)


def row_ids(rows):
    return lax.broadcasted_iota(jnp.int32, (rows, LANES), 0)


def roll_up(x):
    return pltpu.roll(x, 1, 1)


def roll_down(x):
    return pltpu.roll(x, LANES - 1, 1)


def roll_rows(x, by):
    by %= x.shape[0]
    return x if by == 0 else pltpu.roll(x, by, 0)


def roll_lanes(x, by):
    by %= LANES
    return x if by == 0 else pltpu.roll(x, by, 1)


def col_prev(x):
    return pltpu.roll(x, 1, 0)


def col_next(x):
    return pltpu.roll(x, x.shape[0] - 1, 0)


def inverse_of(x):
    return 1.0 / x


def selector(shape, rule):
    a = lax.broadcasted_iota(jnp.int32, shape, 0)
    b = lax.broadcasted_iota(jnp.int32, shape, 1)
    return jnp.where(rule(a, b), 1.0, 0.0).astype(BF16)


def splitter():
    return selector((256, 256), lambda a, b: a == 2 * (b % LANES) + b // LANES)


def merger():
    return selector((256, 256), lambda a, b: b == 2 * (a % LANES) + a // LANES)


def virtual_splitter():
    return selector(
        (LANES, 256),
        lambda a, b: a // 2 + jnp.where(a >= 64, 64, 0) + LANES * (a % 2) == b,
    )


def moved(x, matrix, exact=None):
    rows = x.shape[0]
    high = x.astype(BF16)
    low = (x - high.astype(F32)).astype(BF16)
    terms = [high, low] if exact is None else [high, low, exact]
    out = jnp.dot(jnp.concatenate(terms, 0), matrix, preferred_element_type=F32)
    both = out[:rows] + out[rows : 2 * rows]
    return both if exact is None else (both, out[2 * rows :])


def quarters_of(parts, temp):
    count = parts.shape[0] // 2
    temp[0] = parts[:, :LANES]
    temp[1] = parts[:, LANES:]
    return [temp[pr, pl.ds(pc, count, 2), :] for pc in (0, 1) for pr in (0, 1)]


def reds(swapped):
    return (1, 2) if swapped else (0, 3)


def interleaved(group, offset):
    sub = row_ids(8)
    packed = roll_rows(group[0], offset)
    for q in range(1, 4):
        packed = jnp.where(sub // 2 == q, roll_rows(group[q], 2 * q + offset), packed)
    return packed


def edge_packs(source, diag, swapped):
    sub = row_ids(8)
    even, odd = reds(swapped)
    rows = source[0].shape[0]
    packs = []
    for here, first, second, row, step in (
        (slice(rows - 8, rows), even, odd, 6, 1),
        (slice(0, 8), odd, even, 1, -1),
    ):
        gs = [x[here] for x in source]
        gd = [x[here] for x in diag]
        near = gs[first] * inverse_of(gd[first])
        far = roll_rows(gs[second] * inverse_of(gd[second]), step)
        gs[first] = jnp.where(sub == row, near, gs[first])
        gd[first] = jnp.where(sub == row, far, gd[first])
        offset = 2 if row == 6 else 0
        packs.append((interleaved(gs, offset), interleaved(gd, offset)))
    return packs


def unpacked_halo(left, right, swapped):
    sub = row_ids(8)
    even, odd = reds(swapped)
    (al, bl), (ar, br) = left, right
    source, diag = [], []
    for q in range(4):
        s = jnp.where(
            sub >= 6,
            roll_rows(al, 6 - 2 * q),
            jnp.where(sub <= 1, roll_rows(ar, -2 * q), 0.0),
        )
        d = jnp.where(
            sub >= 6,
            roll_rows(bl, 6 - 2 * q),
            jnp.where(sub <= 1, roll_rows(br, -2 * q), 4.0),
        )
        if q == even:
            s = jnp.where(sub == 2, roll_rows(br, 1 - 2 * odd), s)
            d = jnp.where((sub == 2) | (sub == 6), 1.0, d)
        if q == odd:
            s = jnp.where(sub == 5, roll_rows(bl, 5 - 2 * even), s)
            d = jnp.where((sub == 5) | (sub == 1), 1.0, d)
        source.append(s)
        diag.append(d)
    return source, diag


def is_odd():
    return lax.rem(lax.axis_index("lon"), 2) == 1


def chosen(odd, a, b):
    return jnp.where(odd, a, b), jnp.where(odd, b, a)


def store_edges(t, packs, odd, to_mate, to_other):
    right, left = packs
    for i in (0, 1):
        to_mate[i, t], to_other[i, t] = chosen(odd, left[i], right[i])


def sides(swapped):
    even, odd = reds(swapped)
    return (even, even ^ 1, odd, odd ^ 1), (odd, odd ^ 1, even, even ^ 1)


def paired(groups, shift):
    sub = row_ids(8)
    packed = roll_rows(groups[0], shift)
    for g in (1, 2, 3):
        packed = jnp.where(sub // 2 == g, roll_rows(groups[g], 2 * g + shift), packed)
    return packed


def state_packs(source, diag, last, first_black, residual, partial, diag2, swapped):
    sub = row_ids(8)
    rows = source[0].shape[0]
    packs = []
    for (a, ab, b, bb), here, near, far, step in zip(
        sides(swapped), (slice(rows - 8, rows), slice(0, 8)), (7, 0), (6, 1), (-1, 1)
    ):
        s, d, v = ([x[here] for x in group] for group in (source, diag, last))
        part, d2 = partial[here], diag2[here]
        beside = [
            s[bb] + v[a],
            d[bb],
            first_black[bb][here],
            v[b],
            s[b] - d[b] * v[b] + v[ab],
            residual[a][here] - v[bb],
            part,
            roll_rows(d2, -step),
        ]
        groups = [jnp.where(sub == far, y, x) for x, y in zip(s + d, beside)]
        shift = 2 if near == 7 else 0
        more = jnp.where(sub == far, d2, first_black[ab][here])
        more = jnp.where(sub == far + step, part, more)
        more = jnp.where(sub == far + 2 * step, part * inverse_of(d2), more)
        packs.append((paired(groups[:4], shift), paired(groups[4:], shift), more))
    return packs


def fill_halo(t, from_mate, from_other, odd, swapped, hs, hd, hi):
    al, ar = chosen(odd, from_mate[0, t], from_other[0, t])
    bl, br = chosen(odd, from_mate[1, t], from_other[1, t])
    source, diag = unpacked_halo((al, bl), (ar, br), swapped)
    for q in range(4):
        hs[q, t] = source[q]
        hd[q, t] = diag[q]
        hi[q, t] = inverse_of(diag[q])


def loader(own, halo, virtual, tiles):
    def load(q, t):
        if isinstance(t, int) and t == tiles:
            return jnp.concatenate([virtual[q], halo[q, t]], 0)
        return jnp.concatenate([own[q, t], halo[q, t]], 0)

    return load


def polar_packs(tiles_of):
    lane = lane_ids(tiles_of[0][0].shape[0])
    packs = []
    for pc in (0, 1):
        parts = [*tiles_of[2 * pc], *tiles_of[2 * pc + 1]]
        packed = parts[0]
        for m in range(1, 4):
            mine = (lane + (16 - 32 * m) % LANES) % LANES < 32
            packed = jnp.where(mine, roll_lanes(parts[m], 32 * m), packed)
        packs.append(packed)
    return packs


def polar_unpacked(x, q):
    lane = lane_ids(x.shape[1])
    used = (lane < 16) | (lane >= LANES - 16)
    m = 2 * (q % 2)
    return (
        jnp.where(used, roll_lanes(x[q // 2], 32 * m), 0.0),
        jnp.where(used, roll_lanes(x[q // 2], 32 * (m + 1)), 4.0),
    )


def seam_scales(flags, chunks):
    flag_cols, flag_lats = flags.shape
    flags = jnp.concatenate(
        [flags.astype(F32), jnp.zeros((8 - flag_cols, flag_lats), F32)], 0
    )
    lat = lax.broadcasted_iota(jnp.int32, (8, flag_lats), 1)
    stacked = jnp.concatenate([jnp.where(lat // 8 == c, flags, 0.0) for c in chunks], 0)
    spread = selector((flag_lats, LANES), lambda a, b: a % 8 == b // (TILE // 2))
    spread_flags = jnp.dot(stacked.astype(BF16), spread, preferred_element_type=F32)
    scale = jnp.where(spread_flags > 0.5, SEAM_SCALE, 1.0)
    return scale.reshape(len(chunks), 8, LANES)


def seam_rows(scales, flag_cols, rows):
    size = (rows // flag_cols, LANES)
    return jnp.concatenate(
        [jnp.broadcast_to(scales[i : i + 1], size) for i in range(flag_cols)], 0
    )


def edge_kernel(
    right_ref, weight_ref, flag_ref,
    right_here, weight_here, to_mate, to_other, corner_ref,
    flags, temp_s, temp_w, scale_ref, sems,
):
    columns, height = right_ref.shape
    tiles = height // 256
    pairs = [(flag_ref, flags)]
    inputs = (right_ref, right_here, 8), (weight_ref, weight_here, 16)
    for src, dst, size in inputs:
        for start in (0, columns - size):
            part = pl.ds(start, size)
            pairs.append((src.at[part], dst.at[part]))
    for src, dst, size in inputs:
        part = pl.ds(size, columns - 2 * size)
        pairs.append((src.at[part], dst.at[part]))
    copies = [
        pltpu.make_async_copy(src, dst, sems.at[i]) for i, (src, dst) in enumerate(pairs)
    ]
    for copy in copies:
        copy.start()
    odd = is_odd()
    matrix = splitter()
    flag_cols = flag_ref.shape[0]
    copies[0].wait()
    scale_ref[...] = seam_scales(flags[...], range(tiles))
    for copy in copies[1:5]:
        copy.wait()
    sub = row_ids(8)
    lanes = [slice(c * 256, (c + 1) * 256) for c in range(tiles)]

    def ends(size):
        return slice(0, size), slice(columns - size, columns)

    source, weight = moved(
        jnp.concatenate([right_here[at, w] for w in lanes for at in ends(8)], 0),
        matrix,
        jnp.concatenate([weight_here[at, w] for w in lanes for at in ends(16)], 0),
    )
    weight = weight.reshape(tiles, 32, 256)
    weight = jnp.concatenate([weight[:, :8], weight[:, 24:]], 1).reshape(tiles * 16, 256)
    source = quarters_of(source, temp_s)
    weight = quarters_of(weight, temp_w)
    found = []
    for c in range(tiles):
        here = slice(c * 8, (c + 1) * 8)
        scales = scale_ref[c]
        scale = jnp.where(sub < 4, scales[:1], scales[flag_cols - 1 : flag_cols])
        pair = [x[here] for x in source], [4.0 + w[here] * scale for w in weight]
        store_edges(c, edge_packs(*pair, False), odd, to_mate, to_other)
        if c in (0, tiles - 1):
            found.append(pair)
    both = mirrored_ends(*found)
    for pc in (0, 1):
        corner_ref[pc] = both[8 * pc : 8 * (pc + 1)]
    for copy in copies[5:]:
        copy.wait()


def mirrored_ends(first, last):
    mirror = selector((LANES, LANES), lambda a, b: a + b == LANES - 1)
    lane = lane_ids(first[0][0].shape[0])
    ends = [
        [jnp.where(lane >= 64, last[i][q ^ 1], first[i][q ^ 1]) for i in (0, 1)]
        for q in range(4)
    ]
    return moved(jnp.concatenate(polar_packs(ends), 0), mirror)


def polar_kernel(right_ref, weight_ref, flag_ref, edges_first, polar_ref, temp_s, temp_w):
    columns, height = right_ref.shape
    rows, tiles = columns // 2, height // 256
    scales = seam_scales(flag_ref[...], (0, tiles - 1))
    lanes = slice(0, 256), slice(height - 256, height)
    source, weight = moved(
        jnp.concatenate([right_ref[:, w] for w in lanes], 0),
        splitter(),
        jnp.concatenate([weight_ref[:, w] for w in lanes], 0),
    )
    found = []
    for end in (0, 1):
        here = slice(end * columns, (end + 1) * columns)
        scale = seam_rows(scales[end], flag_ref.shape[0], rows)
        found.append(
            (
                quarters_of(source[here], temp_s.at[end]),
                [4.0 + w * scale for w in quarters_of(weight[here], temp_w.at[end])],
            )
        )
    both = mirrored_ends(*found)
    for pc in (0, 1):
        polar_ref[pc] = both[pc * rows : (pc + 1) * rows]


def bulk_kernel(
    right_ref, weight_ref, flag_ref, polar_first,
    s_ref, d_ref, i_ref, d1_ref, i1_ref, d2_ref,
    temp, scale_ref, e_ref, split_temp,
):
    tiles, columns = s_ref.shape[1], s_ref.shape[2]
    rows = columns // 2
    matrix = splitter()
    scale_ref[...] = seam_scales(flag_ref[...], range(tiles))
    for start in range(0, tiles, BATCH):
        lanes = [slice((start + i) * 256, (start + i + 1) * 256) for i in range(BATCH)]
        source, weight = moved(
            jnp.concatenate([right_ref[:, w] for w in lanes], 0),
            matrix,
            jnp.concatenate([weight_ref[:, w] for w in lanes], 0),
        )
        for i in range(BATCH):
            c = start + i
            here = slice(i * columns, (i + 1) * columns)
            scale = seam_rows(scale_ref[c], flag_ref.shape[0], columns)
            screens = []
            for pr in (0, 1):
                half = slice(pr * LANES, (pr + 1) * LANES)
                screen = weight[here, half] * scale
                diag = 4.0 + screen
                s_ref[pr, c] = source[here, half]
                d_ref[pr, c] = diag
                i_ref[pr, c] = 1.0 / diag
                screens.append(screen)
            temp[i] = screens[0] + screens[1]
            e_ref[c] = temp[i, pl.ds(0, rows, 2), :] + temp[i, pl.ds(1, rows, 2), :]

    def use(c, screen):
        for q in range(4):
            d1_ref[q, c] = 4.0 + screen[q]
            i1_ref[q, c] = inverse_of(4.0 + screen[q])
        d2_ref[c] = 4.0 + ((screen[0] + screen[1]) + (screen[2] + screen[3]))

    split_tiles(lambda t: e_ref[t], tiles // 2, rows, matrix, split_temp, use)


def split_tiles(load, tiles, rows, matrix, temp, use):
    for start in range(0, tiles, BATCH):
        wide = [
            jnp.concatenate([load(2 * c), load(2 * c + 1)], 1)
            for c in range(start, start + BATCH)
        ]
        out = moved(jnp.concatenate(wide, 0), matrix)
        for i in range(BATCH):
            use(start + i, quarters_of(out[i * rows : (i + 1) * rows], temp.at[i, :, :rows]))


def half_sweep(v, load_s, load_i, tiles, red, unroll, left=None):
    rows = v[0].shape[1]
    lane = lane_ids(rows)
    y, z, qa, qb = (1, 2, 0, 3) if red else (3, 0, 2, 1)
    col_a, col_b = (col_prev, col_next) if red else (col_next, col_prev)

    def beside_virtual(q):
        ns, we = q ^ 1, q ^ 2
        here = v[ns][tiles]
        if q % 2 == 0:
            lat = jnp.where(lane == 0, roll_up(v[ns][tiles - 1]), roll_up(here))
        else:
            lat = jnp.where(lane == LANES - 1, roll_down(v[ns][0]), roll_down(here))
        cols = v[we][tiles]
        return (here + lat) + (cols + (col_prev if q < 2 else col_next)(cols))

    held = [
        (q, (load_s(q, tiles) + beside_virtual(q)) * load_i(q, tiles)) for q in (y, z)
    ]

    def body(t, carry):
        y_before, z_here = carry
        vy, vz = v[y][t], v[z][t]
        y_here = roll_up(vy)
        z_after = roll_down(v[z][t + 1])
        lat_a = vy + jnp.where(lane == 0, y_before, y_here)
        lat_b = vz + jnp.where(lane == LANES - 1, z_after, z_here)
        all_a = load_s(qa, t) + (lat_a + (vz + col_a(vz)))
        all_b = load_s(qb, t) + (lat_b + (vy + col_b(vy)))
        new_a, new_b = all_a * load_i(qa, t), all_b * load_i(qb, t)
        v[qa][t], v[qb][t] = new_a, new_b
        if left is not None:
            load_d, rest = left
            rest[qa][t] = all_a - load_d(qa, t) * new_a
            rest[qb][t] = all_b - load_d(qb, t) * new_b
        return y_here, z_after

    loop(tiles, body, (roll_up(v[y][tiles]), roll_down(v[z][0])), unroll)
    for q, value in held:
        v[q][tiles] = value


def smooth(v, load_s, load_i, tiles, unroll, left, after_sweep=None):
    zeros = jnp.zeros(v[0].shape[1:], F32)

    def first(t, _):
        for q in (0, 3):
            v[q][t] = load_s(q, t) * load_i(q, t)
        return 0

    loop(tiles, first, 0, unroll)
    for q in (1, 2):
        v[q][0] = zeros
        v[q][tiles - 1] = zeros
        v[q][tiles] = load_s(q, tiles) * load_i(q, tiles)
        v[3 * (q - 1)][tiles] = zeros
    for sweep, red in enumerate((False, True, False)):
        half_sweep(v, load_s, load_i, tiles, red, unroll, left if sweep == 2 else None)
        if after_sweep is not None:
            after_sweep(sweep)


def residuals(v, load_s, left, tiles, c0, c1, keep, unroll, valid=None):
    lane = lane_ids(v[0].shape[1])
    load_d, rest = left

    def use(t, r):
        keep(t, r)
        if valid is not None:
            virtual = isinstance(t, int) and t == tiles
            r = [jnp.where(valid(q, virtual), r[q], 0.0) for q in range(4)]
        c0[t] = (col_prev(r[2]) + col_next(r[0])) + 3.0 * (r[0] + r[2])
        c1[t] = (col_prev(r[3]) + col_next(r[1])) + 3.0 * (r[1] + r[3])

    def north(q, t):
        return jnp.where(lane == 0, roll_up(v[q][before(t, tiles)]), roll_up(v[q][t]))

    def south(q, t):
        return jnp.where(
            lane == LANES - 1, roll_down(v[q][after(t, tiles)]), roll_down(v[q][t])
        )

    def full(t):
        x = [v[q][t] for q in range(4)]
        beside = [
            (x[1] + north(1, t)) + (x[2] + col_prev(x[2])),
            (x[0] + south(0, t)) + (x[3] + col_prev(x[3])),
            (x[3] + north(3, t)) + (x[0] + col_next(x[0])),
            (x[2] + south(2, t)) + (x[1] + col_next(x[1])),
        ]
        use(t, [load_s(q, t) - (load_d(q, t) * x[q] - beside[q]) for q in range(4)])

    def body(i, carry):
        t = i + 1
        up, down = carry
        x = [v[q][t] for q in range(4)]
        up_here, down_next = roll_up(x[1]), roll_down(v[2][t + 1])
        beside0 = (x[1] + jnp.where(lane == 0, up, up_here)) + (x[2] + col_prev(x[2]))
        beside3 = (x[2] + jnp.where(lane == LANES - 1, down_next, down)) + (
            x[1] + col_next(x[1])
        )
        r0 = load_s(0, t) - (load_d(0, t) * x[0] - beside0)
        r3 = load_s(3, t) - (load_d(3, t) * x[3] - beside3)
        use(t, [r0, rest[1][t], rest[2][t], r3])
        return up_here, down_next

    full(0)
    loop(tiles - 2, body, (roll_up(v[1][0]), roll_down(v[2][1])), unroll)
    full(tiles - 1)
    full(tiles)


def restrict(c0, c1, tiles, rows, use, unroll):
    lane = lane_ids(rows)

    def body(t, carry):
        up, down = carry
        here, other = c0[t, :rows], c1[t, :rows]
        up_here = roll_up(other)
        down_next = roll_down(c0[after(t, tiles), :rows])
        north = jnp.where(lane == 0, up, up_here)
        south = jnp.where(lane == LANES - 1, down_next, down)
        use(t, ((north + south) + 3.0 * (here + other)) * (1.0 / 16.0))
        return up_here, down_next

    start = roll_up(c1[tiles, :rows]), roll_down(c0[0, :rows])
    body(tiles, loop(tiles, body, start, unroll))


class Fine:
    def __init__(self, own, halo, virtual, tiles, columns):
        self.own, self.halo, self.virtual = own, halo, virtual
        self.tiles, self.columns = tiles, columns

    def part(self, parity, t, start):
        return self.own[parity][t, pl.ds(8 + start, self.columns // 2, 2), :]

    def rows(self, q, t):
        return self.part(q % 2, t, q // 2)

    def whole(self, q, t):
        if isinstance(t, int) and t == self.tiles:
            return self.virtual[q][...]
        return jnp.concatenate([self.rows(q, t), self.halo[q][t]], 0)

    def ends(self, q, t):
        if isinstance(t, int) and t == self.tiles:
            whole = self.virtual[q][...]
            return whole[: self.columns // 2], whole[self.columns // 2 :]
        return self.rows(q, t), self.halo[q][t]

    def line(self, parity, t, column):
        row = self.own[parity][t, 8 + column : 9 + column]
        return jnp.broadcast_to(row, (8, LANES))

    def put(self, q, t, own, halo):
        pr, pc = q % 2, q // 2
        self.own[pr][t, pl.ds(8 + pc, self.columns // 2, 2), :] = own
        self.halo[q][t] = halo
        if pc == 1:
            self.own[pr][t, 7:8] = halo[7:8]
        else:
            at = 8 + self.columns
            self.own[pr][t, at : at + 1] = halo[0:1]

    def beside_columns(self, q, t, halo):
        sub = row_ids(8)
        pr, pc = q % 2, q // 2
        own = self.part(pr, t, pc - 1) + self.part(pr, t, pc + 1)
        if pc == 0:
            other = jnp.where(sub == 0, self.line(pr, t, self.columns - 1), col_prev(halo))
        else:
            other = jnp.where(sub == 7, self.line(pr, t, 0), col_next(halo))
        return own, halo + other


def fine_sweep(v, load_s, load_i, whole_s, whole_i, red, left):
    tiles = v.tiles
    y, z, qa, qb = (1, 2, 0, 3) if red else (3, 0, 2, 1)

    def lane_sum(parts, rolled, edge, lane_at):
        return [
            x + jnp.where(lane_ids(x.shape[0]) == lane_at, e, r)
            for x, r, e in zip(parts, rolled, edge)
        ]

    def beside_virtual(q):
        here, cols = v.whole(q ^ 1, tiles), v.whole(q ^ 2, tiles)
        lane = lane_ids(here.shape[0])
        if q % 2 == 0:
            lat = jnp.where(lane == 0, roll_up(v.whole(q ^ 1, tiles - 1)), roll_up(here))
        else:
            lat = jnp.where(lane == LANES - 1, roll_down(v.whole(q ^ 1, 0)), roll_down(here))
        return (here + lat) + (cols + (col_prev if q < 2 else col_next)(cols))

    held = [
        (q, (whole_s(q, tiles) + beside_virtual(q)) * whole_i(q, tiles)) for q in (y, z)
    ]

    def body(t, carry):
        y_before, z_here = carry
        vy, vz = v.ends(y, t), v.ends(z, t)
        y_here = [roll_up(x) for x in vy]
        z_after = [roll_down(x) for x in v.ends(z, t + 1)]
        lat_a = lane_sum(vy, y_here, y_before, 0)
        lat_b = lane_sum(vz, z_here, z_after, LANES - 1)
        new = []
        for q, lat, halo in ((qa, lat_a, vz[1]), (qb, lat_b, vy[1])):
            cols = v.beside_columns(q, t, halo)
            total = [x + (l + c) for x, l, c in zip(load_s(q, t), lat, cols)]
            value = [x * i for x, i in zip(total, load_i(q, t))]
            new.append((q, value))
            if left is not None:
                load_d, rest = left
                rest.put(q, t, *[x - d * u for x, d, u in zip(total, load_d(q, t), value)])
        for q, value in new:
            v.put(q, t, *value)
        return y_here, z_after

    start = [roll_up(x) for x in v.ends(y, tiles)], [roll_down(x) for x in v.ends(z, 0)]
    body(tiles - 1, loop(tiles - 1, body, start, 10))
    for q, value in held:
        v.virtual[q][...] = value


def fine_residuals(v, load_s, load_d, whole_s, whole_d, rest, c0, c1):
    tiles = v.tiles
    rows = v.columns // 2

    def columns_summed(t):
        for pr, ref in ((0, c0), (1, c1)):
            outer = rest.part(pr, t, -1) + rest.part(pr, t, 2)
            inner = rest.part(pr, t, 0) + rest.part(pr, t, 1)
            ref[t] = outer + 3.0 * inner

    def full(t):
        x = [v.whole(q, t) for q in range(4)]
        lane = lane_ids(x[0].shape[0])

        def north(q):
            return jnp.where(lane == 0, roll_up(v.whole(q, before(t, tiles))), roll_up(x[q]))

        def south(q):
            return jnp.where(
                lane == LANES - 1, roll_down(v.whole(q, after(t, tiles))), roll_down(x[q])
            )

        beside = [
            (x[1] + north(1)) + (x[2] + col_prev(x[2])),
            (x[0] + south(0)) + (x[3] + col_prev(x[3])),
            (x[3] + north(3)) + (x[0] + col_next(x[0])),
            (x[2] + south(2)) + (x[1] + col_next(x[1])),
        ]
        r = [whole_s(q, t) - (whole_d(q, t) * x[q] - beside[q]) for q in range(4)]
        if t == tiles:
            c0[t] = ((col_prev(r[2]) + col_next(r[0])) + 3.0 * (r[0] + r[2]))[:rows]
            c1[t] = ((col_prev(r[3]) + col_next(r[1])) + 3.0 * (r[1] + r[3]))[:rows]
        else:
            for q in range(4):
                rest.put(q, t, r[q][:rows], r[q][rows:])
            columns_summed(t)

    full(0)

    def body(i, carry):
        t = i + 1
        up, down = carry
        x = [v.ends(q, t) for q in range(4)]
        up_here = [roll_up(part) for part in x[1]]
        down_next = [roll_down(part) for part in v.ends(2, t + 1)]
        for q, ns, near, edge, lane_at in (
            (0, 1, up_here, up, 0), (3, 2, down, down_next, LANES - 1)
        ):
            cols = v.beside_columns(q, t, x[q ^ 2][1])
            r = []
            for i, (s, d) in enumerate(zip(load_s(q, t), load_d(q, t))):
                lane = lane_ids(s.shape[0])
                beside = x[ns][i] + jnp.where(lane == lane_at, edge[i], near[i]) + cols[i]
                r.append(s - (d * x[q][i] - beside))
            rest.put(q, t, *r)
        columns_summed(t)
        return up_here, down_next

    start = [roll_up(x) for x in v.ends(1, 0)], [roll_down(x) for x in v.ends(2, 1)]
    loop(tiles - 2, body, start, 10)
    full(tiles - 1)
    full(tiles)


def fine_kernel(
    s_ref, d_ref, i_ref, d1_ref, i1_ref, d2_ref,
    from_other, from_mate, polar_ref, corner_near, corner_far,
    r_ref, s1_ref, d1_virtual, d2_virtual, s2_ref, to_mate, to_other,
    v_ref, hv, pv, hr, c0, c1, hs, hd, hi, ps, pd, pi, n1, temp,
    w0, w1, w2, w3, e0, e1, pi1, black_even, black_odd, red_even, red_odd,
    part1, part2,
):
    tiles, columns = s_ref.shape[1], s_ref.shape[2]
    rows = columns // 2
    sub = row_ids(8)
    odd = is_odd()

    def halo(t, _):
        fill_halo(t, from_mate, from_other, odd, False, hs, hd, hi)
        return 0

    loop(tiles, halo, 0, 8)
    total = -16.0
    for q in range(4):
        own_s, own_d = polar_unpacked(polar_ref, q)
        near_s, near_d = polar_unpacked(corner_near, q)
        far_s, far_d = polar_unpacked(corner_far, q)
        left_s, right_s = chosen(odd, near_s, far_s)
        left_d, right_d = chosen(odd, near_d, far_d)
        total = total + own_d
        ps[q] = own_s
        pd[q] = own_d
        pi[q] = inverse_of(own_d)
        source = jnp.where(sub >= 5, left_s, jnp.where(sub <= 2, right_s, 0.0))
        diag = jnp.where(sub >= 5, left_d, jnp.where(sub <= 2, right_d, 4.0))
        hs[q, tiles] = source
        hd[q, tiles] = diag
        hi[q, tiles] = inverse_of(diag)

    def loaders(ref, halo, virtual):
        def split(q, t):
            return ref[q % 2, t, pl.ds(q // 2, rows, 2), :], halo[q, t]

        def whole(q, t):
            if t == tiles:
                return jnp.concatenate([virtual[q], halo[q, t]], 0)
            return jnp.concatenate(split(q, t), 0)

        return split, whole

    load_s, whole_s = loaders(s_ref, hs, ps)
    load_d, whole_d = loaders(d_ref, hd, pd)
    load_i, whole_i = loaders(i_ref, hi, pi)

    def held(own_ref, halo_ref):
        return Fine(
            [own_ref.at[p] for p in (0, 1)],
            [halo_ref.at[q] for q in range(4)],
            [pv.at[q] for q in range(4)],
            tiles,
            columns,
        )

    v, rest = held(v_ref, hv), held(r_ref, hr)

    def first(t, _):
        for q in (0, 3):
            v.put(q, t, *[x * i for x, i in zip(load_s(q, t), load_i(q, t))])
        return 0

    loop(tiles, first, 0, 8)
    for q in (1, 2):
        for t in (0, tiles - 1):
            v.put(q, t, jnp.zeros((rows, LANES), F32), jnp.zeros((8, LANES), F32))
        pv[q] = whole_s(q, tiles) * whole_i(q, tiles)
        pv[3 * (q - 1)] = jnp.zeros((rows + 8, LANES), F32)
    for red, left in ((False, None), (True, None), (False, (load_d, rest))):
        fine_sweep(v, load_s, load_i, whole_s, whole_i, red, left)
    fine_residuals(v, load_s, load_d, whole_s, whole_d, rest, c0, c1)

    def coarse(t, value):
        n1[t] = value

    restrict(c0, c1, tiles, rows, coarse, 8)

    def use(c, source):
        for q in range(4):
            s1_ref[q, c] = source[q]

    tiles1 = tiles // 2
    split_tiles(lambda t: n1[t], tiles1, rows, splitter(), temp, use)
    out = moved(jnp.concatenate([n1[tiles], total], 0), virtual_splitter())
    source = quarters_of(out[:rows], temp.at[0])
    screen = quarters_of(out[rows:], temp.at[1])
    for q in range(4):
        s1_ref[q, tiles1] = source[q]
        d1_virtual[q] = 4.0 + screen[q]
        pi1[q] = inverse_of(4.0 + screen[q])
    d2_virtual[...] = 4.0 + ((screen[0] + screen[1]) + (screen[2] + screen[3]))

    def own(main, virtual):
        return lambda q, t: virtual[q] if isinstance(t, int) and t == tiles1 else main[q, t]

    w = [w0, w1, w2, w3]
    rows1 = rows // 2
    row = row_ids(rows1)
    load_s, load_d = own(s1_ref, s1_ref.at[:, tiles1]), own(d1_ref, d1_virtual)

    def after_sweep(sweep):
        if sweep == 0:
            for t in range(tiles1 + 1):
                even, odd_red = reds(t == tiles1)
                black_even[t] = w[even ^ 1][t]
                black_odd[t] = w[odd_red ^ 1][t]

    left = load_d, {1: part1, 2: part2}
    smooth(w, load_s, own(i1_ref, pi1), tiles1, 16, left, after_sweep)

    def valid(q, virtual):
        even, odd_red = reds(virtual)
        first = 1 if q == odd_red ^ 1 else 2
        last = rows1 - 2 if q == even ^ 1 else rows1 - 3
        return (row >= first) & (row <= last)

    def keep_red(t, r):
        even, odd_red = reds(isinstance(t, int) and t == tiles1)
        red_even[t] = r[even]
        red_odd[t] = r[odd_red]

    residuals(w, load_s, left, tiles1, e0, e1, keep_red, 16, valid)
    shared = {}

    def edges(t, partial):
        virtual = t == tiles1
        even, odd_red = reds(virtual)
        s2_ref[t] = partial
        packs = state_packs(
            [s1_ref[q, t] for q in range(4)],
            [load_d(q, t) for q in range(4)],
            [w[q][t] for q in range(4)],
            {even ^ 1: black_even[t], odd_red ^ 1: black_odd[t]},
            {even: red_even[t], odd_red: red_odd[t]},
            partial,
            d2_virtual[...] if virtual else d2_ref[t],
            virtual,
        )
        right, left = packs
        count = tiles1 + 1
        for i in (0, 1):
            to_mate[i * count + t], to_other[i * count + t] = chosen(odd, left[i], right[i])
        if t % 2 == 0:
            pair = chosen(odd, left[2], roll_rows(right[2], 4))
            shared[0] = pair
        else:
            pair = chosen(odd, roll_rows(left[2], 4), right[2])
            pair = [jnp.where(sub < 4, x, y) for x, y in zip(shared[0], pair)]
        if t % 2 == 1 or virtual:
            to_mate[2 * count + t // 2], to_other[2 * count + t // 2] = pair

    restrict(e0, e1, tiles1, rows1, edges, 16)


def merge_kernel(r_ref, out_ref, out_buf, sems):
    tiles = r_ref.shape[1]
    columns = out_ref.shape[0]
    matrix = merger()
    chunk = out_ref.shape[1] // GROUPS
    copies = []
    for group in range(GROUPS):
        for batch in range(tiles // GROUPS // BATCH):
            start = group * (tiles // GROUPS) + batch * BATCH
            own = slice(8, 8 + columns)
            both = [
                jnp.concatenate([r_ref[0, start + i, own], r_ref[1, start + i, own]], 1)
                for i in range(BATCH)
            ]
            out = moved(jnp.concatenate(both, 0), matrix)
            for i in range(BATCH):
                where = slice((start + i) * 256, (start + i + 1) * 256)
                out_buf[:, where] = out[columns * i : columns * (i + 1)]
        part = pl.ds(group * chunk, chunk)
        copy = pltpu.make_async_copy(out_buf.at[:, part], out_ref.at[:, part], sems.at[group])
        copy.start()
        copies.append(copy)
    for copy in copies:
        copy.wait()


def coarse_kernel(
    s_ref, d_ref, i_ref, d_virtual, d2_ref, d2_virtual, s2_ref, from_other, from_mate,
    solution_ref, residual_ref,
    v0, v1, v2, v3, c0, c1, hs, hd, hi, part, fixes, rest1, rest2, s, d, inv, va, vb,
):
    v = [v0, v1, v2, v3]
    tiles, own = d_ref.shape[1], d_ref.shape[2]
    rows = own + 8
    count = tiles + 1
    sub = row_ids(8)
    odd_band = is_odd()
    def rim(x):
        return jnp.where(sub < 4, x[:8], x[own - 8 :])

    for t in range(count):
        places = t, count + t, 2 * count + t // 2
        packs = [chosen(odd_band, from_mate[i], from_other[i]) for i in places]
        source = [jnp.zeros((8, LANES), F32)] * 4
        diag = [jnp.full((8, LANES), 4.0, F32)] * 4
        inverse = [jnp.zeros((8, LANES), F32)] * 4
        fixed = [jnp.zeros((8, LANES), F32)] * 4
        more = jnp.zeros((8, LANES), F32)
        total = jnp.ones((8, LANES), F32)
        for side, (a, ab, b, bb) in enumerate(sides(t == tiles)):
            near, far, step = (7, 6, -1) if side == 0 else (0, 1, 1)
            first = 6 if side == 0 else 0
            pack0, pack1, pack2 = (pair[side] for pair in packs)
            groups = [
                roll_rows(pack, first - 2 * g) for pack in (pack0, pack1) for g in range(4)
            ]
            pack2 = roll_rows(pack2, 4 * (t % 2) + (4 if side == 0 else 0))

            def put(group, q, at, x):
                group[q] = jnp.where(sub == at, x, group[q])

            for q in range(4):
                put(source, q, near, groups[q])
                put(diag, q, near, groups[4 + q])
            put(source, bb, far, groups[0])
            put(diag, bb, far, groups[1])
            put(fixed, bb, far, groups[2])
            put(fixed, b, far, groups[3])
            put(source, b, far, groups[4])
            put(diag, b, far, 0.0)
            put(source, a, far, groups[5])
            put(fixed, ab, near, pack2)
            more = jnp.where(sub == far, groups[6], more)
            more = jnp.where((sub == far + step) | (sub == far + 2 * step), pack2, more)
            total = jnp.where(sub == far, pack2, total)
            total = jnp.where(sub == far + step, roll_rows(groups[7], step), total)
            for q in range(4):
                known = (sub == near) | (sub == far) if q == bb else sub == near
                inverse[q] = jnp.where(known, inverse_of(diag[q]), inverse[q])
        for q in range(4):
            own_d = rim(d_virtual[q] if t == tiles else d_ref[q, t])
            own_i = inverse_of(own_d) if t == tiles else rim(i_ref[q, t])
            hs[q, t] = jnp.concatenate([source[q], rim(s_ref[q, t])], 0)
            hd[q, t] = jnp.concatenate([diag[q], own_d], 0)
            hi[q, t] = jnp.concatenate([inverse[q], own_i], 0)
            fixes[q, t] = fixed[q]
        part[t] = more
        near_total = (diag[0] + diag[1]) + (diag[2] + diag[3]) - 12.0
        total = jnp.where((sub == 0) | (sub == 7), near_total, total)
        here = d2_virtual[...] if t == tiles else d2_ref[t]
        d[t] = jnp.concatenate([here, total], 0)
    def after_sweep(sweep):
        if sweep == 2:
            return
        for t in range(count):
            (a, ab, b, bb), (_, _, other_b, other_bb) = sides(t == tiles)
            todo = {}
            if sweep == 0:
                todo = {ab: (sub == 7) | (sub == 1), bb: (sub == 6) | (sub == 0)}
            else:
                todo = {b: sub == 6, other_b: sub == 1}
            for q, mask in todo.items():
                v[q][t, :8] = jnp.where(mask, fixes[q, t], v[q][t, :8])

    def of(ref):
        return lambda q, t: ref[q, t]

    left = of(hd), {1: rest1, 2: rest2}
    smooth(v, of(hs), of(hi), tiles, 16, left, after_sweep)
    row = row_ids(16)

    def valid(q, virtual):
        even, odd_red = reds(virtual)
        after_band = 0 if q == odd_red ^ 1 else 1
        before_band = 7 if q == even ^ 1 else 6
        first = 8 if q == odd_red ^ 1 else 9
        last = 15 if q == even ^ 1 else 14
        return (row <= after_band) | ((row >= before_band) & (row <= first)) | (row >= last)

    residuals(v, of(hs), left, tiles, c0, c1, lambda t, r: None, 16, valid)

    lane, row = lane_ids(rows), row_ids(rows)
    even = (lane + row) % 2 == 0
    odd = jnp.logical_not(even)

    def start(t, value):
        ends = value[8:]
        source = jnp.concatenate(
            [
                s2_ref[t, :8] + jnp.where(sub < 4, ends, 0.0),
                s2_ref[t, own - 8 :] + jnp.where(sub >= 4, ends, 0.0),
                value[:8] + part[t],
            ],
            0,
        )
        inverse = inverse_of(d[t])
        s[t] = source
        inv[t] = inverse
        virtual = isinstance(t, int) and t == tiles
        va[t] = jnp.where(odd if virtual else even, source * inverse, 0.0)

    restrict(c0, c1, tiles, 16, start, 16)

    def scan(v, use):
        up, down = roll_up(v[tiles]), roll_down(v[0])
        for t in range(tiles + 1):
            x = v[t]
            up_here, down_next = roll_up(x), roll_down(v[after(t, tiles)])
            north = jnp.where(lane == 0, up, up_here)
            south = jnp.where(lane == LANES - 1, down_next, down)
            use(t, x, (col_prev(x) + col_next(x)) + (north + south))
            up, down = up_here, down_next

    for old, new, mask, other in ((va, vb, odd, even), (vb, va, even, odd), (va, vb, odd, even)):

        def relax(t, x, beside):
            update = other if t == tiles else mask
            new[t] = jnp.where(update, (s[t] + beside) * inv[t], x)

        scan(old, relax)

    def finish(t, x, beside):
        if t < tiles:
            where = slice(t * LANES, (t + 1) * LANES)
            solution_ref[:, where] = x[:own]
            residual_ref[:, where] = (s[t] - (d[t] * x - beside))[:own]

    scan(vb, finish)


VMEM = pl.BlockSpec(memory_space=pltpu.VMEM)
HBM = pl.BlockSpec(memory_space=pltpu.HBM)


def call(kernel, out_shapes, scratch, *args, sems=None, far_in=0, far_out=0):
    scratch = [pltpu.VMEM(x, F32) if isinstance(x, tuple) else x for x in scratch]
    if sems is not None:
        scratch.append(pltpu.SemaphoreType.DMA(sems))
    return pl.pallas_call(
        kernel,
        out_shape=[
            jax.ShapeDtypeStruct(x, F32) if isinstance(x, tuple) else x for x in out_shapes
        ],
        in_specs=[HBM] * far_in + [VMEM] * (len(args) - far_in),
        out_specs=[HBM] * far_out + [VMEM] * (len(out_shapes) - far_out),
        scratch_shapes=scratch,
        compiler_params=pltpu.CompilerParams(vmem_limit_bytes=40 * 2**20),
    )(*args)


def swapped_with(x, by):
    count = lax.axis_size("lon")
    pairs = [(i, (i + by) % count) for i in range(0, count, 2)]
    return lax.ppermute(x, "lon", pairs + [(b, a) for a, b in pairs])


def swapped_edges(to_mate, to_other):
    from_mate = swapped_with(to_mate, 1)
    return from_mate, swapped_with(to_other, -1)


def body(right_side, texel_weight, seam_flags):
    columns, height = right_side.shape
    half_turn = lax.axis_size("lon") // 2
    tiles, rows = height // 256, columns // 2
    tiles1, rows1 = tiles // 2, rows // 2
    temp = (BATCH, 2, columns, LANES)
    natural = (2, tiles, columns, LANES)
    padded = (2, tiles, columns + 16, LANES)
    quarters1 = (4, tiles1, rows1, LANES)
    split = (2, 16 * tiles, LANES)
    right_here, weight_here, to_mate, to_other, corner = call(
        edge_kernel,
        [(columns, height), jax.ShapeDtypeStruct((columns, height), BF16)]
        + [(2, tiles, 8, LANES), (2, tiles, 8, LANES), (2, 8, LANES)],
        [pltpu.VMEM(seam_flags.shape, jnp.int32), split, split, (tiles, 8, LANES)],
        *[
            pltpu.with_memory_space_constraint(x, pltpu.HBM)
            for x in (right_side, texel_weight, seam_flags)
        ],
        sems=(7,), far_in=3,
    )
    from_mate, from_other = swapped_edges(to_mate, to_other)
    corner_far = swapped_with(corner, half_turn - 1)
    corner_near = swapped_with(corner, half_turn + 1)
    ends = (2, 2, columns, LANES)
    (polar_own,) = call(
        polar_kernel, [(2, rows, LANES)], [ends, ends],
        right_here, weight_here, seam_flags, corner,
    )
    polar = lax.ppermute(
        polar_own, "lon", [(i, (i + half_turn) % (2 * half_turn)) for i in range(2 * half_turn)]
    )
    s, d, inverse, d1, i1, d2 = call(
        bulk_kernel,
        [natural] * 3 + [quarters1, quarters1, quarters1[1:]],
        [(BATCH, columns, LANES), (tiles, 8, LANES), (tiles, rows, LANES), (BATCH, 2, rows, LANES)],
        right_here, weight_here, seam_flags, polar_own,
    )

    def level_scratch(tiles, rows):
        return [(tiles + 1, rows, LANES)] * 6

    def halo_scratch(tiles):
        return [(4, tiles + 1, 8, LANES)] * 3

    pack1 = (2 * (tiles1 + 1) + tiles1 // 2 + 1, 8, LANES)
    r, s1, d1_virtual, d2_virtual, s2_own, to_mate, to_other = call(
        fine_kernel,
        [padded, (4, tiles1 + 1, rows1, LANES), (4, rows1, LANES), (rows1, LANES)]
        + [(tiles1 + 1, rows1, LANES), pack1, pack1],
        [padded, (4, tiles, 8, LANES), (4, rows + 8, LANES), (4, tiles, 8, LANES)]
        + [(tiles + 1, rows, LANES)] * 2
        + halo_scratch(tiles)
        + [(4, rows, LANES)] * 3
        + [(tiles + 1, rows, LANES), (BATCH, 2, rows, LANES)]
        + level_scratch(tiles1, rows1)
        + [(4, rows1, LANES)]
        + [(tiles1 + 1, rows1, LANES)] * 4
        + [(tiles1, rows1, LANES)] * 2,
        s, d, inverse, d1, i1, d2, from_other, from_mate, polar, corner_near, corner_far,
    )
    from_mate, from_other = swapped_edges(to_mate, to_other)
    (fine_residual,) = call(
        merge_kernel, [(columns, height)], [(columns, height)], r,
        sems=(GROUPS,), far_out=1,
    )
    wide = (tiles1 + 1, rows1 + 8, LANES)
    solution_2, residual_2 = call(
        coarse_kernel,
        [(columns // 4, height // 4)] * 2,
        level_scratch(tiles1, 16)
        + [(4, tiles1 + 1, 16, LANES)] * 3
        + [(tiles1 + 1, 8, LANES), (4, tiles1 + 1, 8, LANES)]
        + [(tiles1, 16, LANES)] * 2
        + [wide] * 5,
        s1, d1, i1, d1_virtual, d2, d2_virtual, s2_own, from_other, from_mate,
    )
    return fine_residual, solution_2, residual_2


def solution(mesh):
    spec = P(("groups", "lon"), None)
    return jax.shard_map(
        body, mesh=mesh, in_specs=(spec,) * 3, out_specs=(spec,) * 3, check_vma=False
    )
```

```python
import jax
import jax.numpy as jnp
from jax import lax
from jax.experimental import pallas as pl
from jax.experimental.pallas import tpu as pltpu
from jax.sharding import PartitionSpec as P

TILE = 32
SEAM_SCALE = 0.1
LANES = 128
GROUPS = 4
BATCH = 4
F32 = jnp.float32
BF16 = jnp.bfloat16


def loop(count, body, carry=0, unroll=4):
    unroll = min(unroll, count)

    def steps(block, carry):
        for i in range(unroll):
            carry = body(block * unroll + i, carry)
        return carry

    whole = count // unroll
    carry = steps(0, carry) if whole == 1 else lax.fori_loop(0, whole, steps, carry)
    for t in range(whole * unroll, count):
        carry = body(t, carry)
    return carry


def before(t, tiles):
    return (tiles if t == 0 else t - 1) if isinstance(t, int) else jnp.where(t == 0, tiles, t - 1)


def after(t, tiles):
    return (0 if t == tiles else t + 1) if isinstance(t, int) else t + 1


def lane_ids(rows):
    return lax.broadcasted_iota(jnp.int32, (rows, LANES), 1)


def row_ids(rows):
    return lax.broadcasted_iota(jnp.int32, (rows, LANES), 0)


def roll_up(x):
    return pltpu.roll(x, 1, 1)


def roll_down(x):
    return pltpu.roll(x, LANES - 1, 1)


def roll_rows(x, by):
    by %= x.shape[0]
    return x if by == 0 else pltpu.roll(x, by, 0)


def roll_lanes(x, by):
    by %= LANES
    return x if by == 0 else pltpu.roll(x, by, 1)


def col_prev(x):
    return pltpu.roll(x, 1, 0)


def col_next(x):
    return pltpu.roll(x, x.shape[0] - 1, 0)


def inverse_of(x):
    return 1.0 / x


def selector(shape, rule):
    a = lax.broadcasted_iota(jnp.int32, shape, 0)
    b = lax.broadcasted_iota(jnp.int32, shape, 1)
    return jnp.where(rule(a, b), 1.0, 0.0).astype(BF16)


def splitter():
    return selector((256, 256), lambda a, b: a == 2 * (b % LANES) + b // LANES)


def merger():
    return selector((256, 256), lambda a, b: b == 2 * (a % LANES) + a // LANES)


def virtual_splitter():
    return selector(
        (LANES, 256),
        lambda a, b: a // 2 + jnp.where(a >= 64, 64, 0) + LANES * (a % 2) == b,
    )


def moved(x, matrix, exact=None):
    rows = x.shape[0]
    high = x.astype(BF16)
    low = (x - high.astype(F32)).astype(BF16)
    terms = [high, low] if exact is None else [high, low, exact]
    out = jnp.dot(jnp.concatenate(terms, 0), matrix, preferred_element_type=F32)
    both = out[:rows] + out[rows : 2 * rows]
    return both if exact is None else (both, out[2 * rows :])


def quarters_of(parts, temp):
    count = parts.shape[0] // 2
    temp[0] = parts[:, :LANES]
    temp[1] = parts[:, LANES:]
    return [temp[pr, pl.ds(pc, count, 2), :] for pc in (0, 1) for pr in (0, 1)]


def reds(swapped):
    return (1, 2) if swapped else (0, 3)


def interleaved(group, offset):
    sub = row_ids(8)
    packed = roll_rows(group[0], offset)
    for q in range(1, 4):
        packed = jnp.where(sub // 2 == q, roll_rows(group[q], 2 * q + offset), packed)
    return packed


def edge_packs(source, diag, swapped):
    sub = row_ids(8)
    even, odd = reds(swapped)
    rows = source[0].shape[0]
    packs = []
    for here, first, second, row, step in (
        (slice(rows - 8, rows), even, odd, 6, 1),
        (slice(0, 8), odd, even, 1, -1),
    ):
        gs = [x[here] for x in source]
        gd = [x[here] for x in diag]
        near = gs[first] * inverse_of(gd[first])
        far = roll_rows(gs[second] * inverse_of(gd[second]), step)
        gs[first] = jnp.where(sub == row, near, gs[first])
        gd[first] = jnp.where(sub == row, far, gd[first])
        offset = 2 if row == 6 else 0
        packs.append((interleaved(gs, offset), interleaved(gd, offset)))
    return packs


def unpacked_halo(left, right, swapped):
    sub = row_ids(8)
    even, odd = reds(swapped)
    (al, bl), (ar, br) = left, right
    source, diag = [], []
    for q in range(4):
        s = jnp.where(
            sub >= 6,
            roll_rows(al, 6 - 2 * q),
            jnp.where(sub <= 1, roll_rows(ar, -2 * q), 0.0),
        )
        d = jnp.where(
            sub >= 6,
            roll_rows(bl, 6 - 2 * q),
            jnp.where(sub <= 1, roll_rows(br, -2 * q), 4.0),
        )
        if q == even:
            s = jnp.where(sub == 2, roll_rows(br, 1 - 2 * odd), s)
            d = jnp.where((sub == 2) | (sub == 6), 1.0, d)
        if q == odd:
            s = jnp.where(sub == 5, roll_rows(bl, 5 - 2 * even), s)
            d = jnp.where((sub == 5) | (sub == 1), 1.0, d)
        source.append(s)
        diag.append(d)
    return source, diag


def is_odd():
    return lax.rem(lax.axis_index("lon"), 2) == 1


def chosen(odd, a, b):
    return jnp.where(odd, a, b), jnp.where(odd, b, a)


def store_edges(t, packs, odd, to_mate, to_other):
    right, left = packs
    for i in (0, 1):
        to_mate[i, t], to_other[i, t] = chosen(odd, left[i], right[i])


def sides(swapped):
    even, odd = reds(swapped)
    return (even, even ^ 1, odd, odd ^ 1), (odd, odd ^ 1, even, even ^ 1)


def paired(groups, shift):
    sub = row_ids(8)
    packed = roll_rows(groups[0], shift)
    for g in (1, 2, 3):
        packed = jnp.where(sub // 2 == g, roll_rows(groups[g], 2 * g + shift), packed)
    return packed


def state_packs(source, diag, last, first_black, residual, partial, diag2, swapped):
    sub = row_ids(8)
    rows = source[0].shape[0]
    packs = []
    for (a, ab, b, bb), here, near, far, step in zip(
        sides(swapped), (slice(rows - 8, rows), slice(0, 8)), (7, 0), (6, 1), (-1, 1)
    ):
        s, d, v = ([x[here] for x in group] for group in (source, diag, last))
        part, d2 = partial[here], diag2[here]
        beside = [
            s[bb] + v[a],
            d[bb],
            first_black[bb][here],
            v[b],
            s[b] - d[b] * v[b] + v[ab],
            residual[a][here] - v[bb],
            part,
            roll_rows(d2, -step),
        ]
        groups = [jnp.where(sub == far, y, x) for x, y in zip(s + d, beside)]
        shift = 2 if near == 7 else 0
        more = jnp.where(sub == far, d2, first_black[ab][here])
        more = jnp.where(sub == far + step, part, more)
        more = jnp.where(sub == far + 2 * step, part * inverse_of(d2), more)
        packs.append((paired(groups[:4], shift), paired(groups[4:], shift), more))
    return packs


def fill_halo(t, from_mate, from_other, odd, swapped, hs, hd, hi):
    al, ar = chosen(odd, from_mate[0, t], from_other[0, t])
    bl, br = chosen(odd, from_mate[1, t], from_other[1, t])
    source, diag = unpacked_halo((al, bl), (ar, br), swapped)
    for q in range(4):
        hs[q, t] = source[q]
        hd[q, t] = diag[q]
        hi[q, t] = inverse_of(diag[q])


def loader(own, halo, virtual, tiles):
    def load(q, t):
        if isinstance(t, int) and t == tiles:
            return jnp.concatenate([virtual[q], halo[q, t]], 0)
        return jnp.concatenate([own[q, t], halo[q, t]], 0)

    return load


def polar_packs(tiles_of):
    lane = lane_ids(tiles_of[0][0].shape[0])
    packs = []
    for pc in (0, 1):
        parts = [*tiles_of[2 * pc], *tiles_of[2 * pc + 1]]
        packed = parts[0]
        for m in range(1, 4):
            mine = (lane + (16 - 32 * m) % LANES) % LANES < 32
            packed = jnp.where(mine, roll_lanes(parts[m], 32 * m), packed)
        packs.append(packed)
    return packs


def polar_unpacked(x, q):
    lane = lane_ids(x.shape[1])
    used = (lane < 16) | (lane >= LANES - 16)
    m = 2 * (q % 2)
    return (
        jnp.where(used, roll_lanes(x[q // 2], 32 * m), 0.0),
        jnp.where(used, roll_lanes(x[q // 2], 32 * (m + 1)), 4.0),
    )


def seam_scales(flags, chunks):
    flag_cols, flag_lats = flags.shape
    flags = jnp.concatenate(
        [flags.astype(F32), jnp.zeros((8 - flag_cols, flag_lats), F32)], 0
    )
    lat = lax.broadcasted_iota(jnp.int32, (8, flag_lats), 1)
    stacked = jnp.concatenate([jnp.where(lat // 8 == c, flags, 0.0) for c in chunks], 0)
    spread = selector((flag_lats, LANES), lambda a, b: a % 8 == b // (TILE // 2))
    spread_flags = jnp.dot(stacked.astype(BF16), spread, preferred_element_type=F32)
    scale = jnp.where(spread_flags > 0.5, SEAM_SCALE, 1.0)
    return scale.reshape(len(chunks), 8, LANES)


def seam_rows(scales, flag_cols, rows):
    size = (rows // flag_cols, LANES)
    return jnp.concatenate(
        [jnp.broadcast_to(scales[i : i + 1], size) for i in range(flag_cols)], 0
    )


def edge_kernel(
    right_ref, weight_ref, flag_ref,
    right_here, weight_here, to_mate, to_other, corner_ref,
    flags, temp_s, temp_w, scale_ref, sems,
):
    columns, height = right_ref.shape
    tiles = height // 256
    pairs = [(flag_ref, flags)]
    inputs = (right_ref, right_here, 8), (weight_ref, weight_here, 16)
    for src, dst, size in inputs:
        for start in (0, columns - size):
            part = pl.ds(start, size)
            pairs.append((src.at[part], dst.at[part]))
    for src, dst, size in inputs:
        part = pl.ds(size, columns - 2 * size)
        pairs.append((src.at[part], dst.at[part]))
    copies = [
        pltpu.make_async_copy(src, dst, sems.at[i]) for i, (src, dst) in enumerate(pairs)
    ]
    for copy in copies:
        copy.start()
    odd = is_odd()
    matrix = splitter()
    flag_cols = flag_ref.shape[0]
    copies[0].wait()
    scale_ref[...] = seam_scales(flags[...], range(tiles))
    for copy in copies[1:5]:
        copy.wait()
    sub = row_ids(8)
    def ends(size):
        return slice(0, size), slice(columns - size, columns)

    count = tiles // 4
    found = []
    for batch in range(4):
        chunks = range(batch * count, (batch + 1) * count)
        lanes = [slice(c * 256, (c + 1) * 256) for c in chunks]
        source, weight = moved(
            jnp.concatenate([right_here[at, w] for w in lanes for at in ends(8)], 0),
            matrix,
            jnp.concatenate([weight_here[at, w] for w in lanes for at in ends(16)], 0),
        )
        weight = weight.reshape(count, 32, 256)
        weight = jnp.concatenate([weight[:, :8], weight[:, 24:]], 1).reshape(count * 16, 256)
        source = quarters_of(source, temp_s.at[batch])
        weight = quarters_of(weight, temp_w.at[batch])
        for i, c in enumerate(chunks):
            here = slice(i * 8, (i + 1) * 8)
            scales = scale_ref[c]
            scale = jnp.where(sub < 4, scales[:1], scales[flag_cols - 1 : flag_cols])
            pair = [x[here] for x in source], [4.0 + w[here] * scale for w in weight]
            store_edges(c, edge_packs(*pair, False), odd, to_mate, to_other)
            if c in (0, tiles - 1):
                found.append(pair)
    both = mirrored_ends(*found)
    for pc in (0, 1):
        corner_ref[pc] = both[8 * pc : 8 * (pc + 1)]
    for copy in copies[5:]:
        copy.wait()


def mirrored_ends(first, last):
    mirror = selector((LANES, LANES), lambda a, b: a + b == LANES - 1)
    lane = lane_ids(first[0][0].shape[0])
    ends = [
        [jnp.where(lane >= 64, last[i][q ^ 1], first[i][q ^ 1]) for i in (0, 1)]
        for q in range(4)
    ]
    return moved(jnp.concatenate(polar_packs(ends), 0), mirror)


def polar_kernel(right_ref, weight_ref, flag_ref, edges_first, polar_ref, temp_s, temp_w):
    columns, height = right_ref.shape
    rows, tiles = columns // 2, height // 256
    scales = seam_scales(flag_ref[...], (0, tiles - 1))
    lanes = slice(0, 256), slice(height - 256, height)
    source, weight = moved(
        jnp.concatenate([right_ref[:, w] for w in lanes], 0),
        splitter(),
        jnp.concatenate([weight_ref[:, w] for w in lanes], 0),
    )
    found = []
    for end in (0, 1):
        here = slice(end * columns, (end + 1) * columns)
        scale = seam_rows(scales[end], flag_ref.shape[0], rows)
        found.append(
            (
                quarters_of(source[here], temp_s.at[end]),
                [4.0 + w * scale for w in quarters_of(weight[here], temp_w.at[end])],
            )
        )
    both = mirrored_ends(*found)
    for pc in (0, 1):
        polar_ref[pc] = both[pc * rows : (pc + 1) * rows]


def bulk_kernel(
    right_ref, weight_ref, flag_ref, polar_first,
    s_ref, d_ref, i_ref, d1_ref, i1_ref, d2_ref,
    temp, scale_ref, e_ref, split_temp,
):
    tiles, columns = s_ref.shape[1], s_ref.shape[2]
    rows = columns // 2
    matrix = splitter()
    scale_ref[...] = seam_scales(flag_ref[...], range(tiles))
    for start in range(0, tiles, BATCH):
        lanes = [slice((start + i) * 256, (start + i + 1) * 256) for i in range(BATCH)]
        source, weight = moved(
            jnp.concatenate([right_ref[:, w] for w in lanes], 0),
            matrix,
            jnp.concatenate([weight_ref[:, w] for w in lanes], 0),
        )
        for i in range(BATCH):
            c = start + i
            here = slice(i * columns, (i + 1) * columns)
            scale = seam_rows(scale_ref[c], flag_ref.shape[0], columns)
            screens = []
            for pr in (0, 1):
                half = slice(pr * LANES, (pr + 1) * LANES)
                screen = weight[here, half] * scale
                diag = 4.0 + screen
                s_ref[pr, c] = source[here, half]
                d_ref[pr, c] = diag
                i_ref[pr, c] = 1.0 / diag
                screens.append(screen)
            temp[i] = screens[0] + screens[1]
            e_ref[c] = temp[i, pl.ds(0, rows, 2), :] + temp[i, pl.ds(1, rows, 2), :]

    def use(c, screen):
        for q in range(4):
            d1_ref[q, c] = 4.0 + screen[q]
            i1_ref[q, c] = inverse_of(4.0 + screen[q])
        d2_ref[c] = 4.0 + ((screen[0] + screen[1]) + (screen[2] + screen[3]))

    split_tiles(lambda t: e_ref[t], tiles // 2, rows, matrix, split_temp, use)


def split_tiles(load, tiles, rows, matrix, temp, use):
    for start in range(0, tiles, BATCH):
        wide = [
            jnp.concatenate([load(2 * c), load(2 * c + 1)], 1)
            for c in range(start, start + BATCH)
        ]
        out = moved(jnp.concatenate(wide, 0), matrix)
        for i in range(BATCH):
            use(start + i, quarters_of(out[i * rows : (i + 1) * rows], temp.at[i, :, :rows]))


def half_sweep(v, load_s, load_i, tiles, red, unroll, left=None):
    rows = v[0].shape[1]
    lane = lane_ids(rows)
    y, z, qa, qb = (1, 2, 0, 3) if red else (3, 0, 2, 1)
    col_a, col_b = (col_prev, col_next) if red else (col_next, col_prev)

    def beside_virtual(q):
        ns, we = q ^ 1, q ^ 2
        here = v[ns][tiles]
        if q % 2 == 0:
            lat = jnp.where(lane == 0, roll_up(v[ns][tiles - 1]), roll_up(here))
        else:
            lat = jnp.where(lane == LANES - 1, roll_down(v[ns][0]), roll_down(here))
        cols = v[we][tiles]
        return (here + lat) + (cols + (col_prev if q < 2 else col_next)(cols))

    held = [
        (q, (load_s(q, tiles) + beside_virtual(q)) * load_i(q, tiles)) for q in (y, z)
    ]

    def body(t, carry):
        y_before, z_here = carry
        vy, vz = v[y][t], v[z][t]
        y_here = roll_up(vy)
        z_after = roll_down(v[z][t + 1])
        lat_a = vy + jnp.where(lane == 0, y_before, y_here)
        lat_b = vz + jnp.where(lane == LANES - 1, z_after, z_here)
        all_a = load_s(qa, t) + (lat_a + (vz + col_a(vz)))
        all_b = load_s(qb, t) + (lat_b + (vy + col_b(vy)))
        new_a, new_b = all_a * load_i(qa, t), all_b * load_i(qb, t)
        v[qa][t], v[qb][t] = new_a, new_b
        if left is not None:
            load_d, rest = left
            rest[qa][t] = all_a - load_d(qa, t) * new_a
            rest[qb][t] = all_b - load_d(qb, t) * new_b
        return y_here, z_after

    loop(tiles, body, (roll_up(v[y][tiles]), roll_down(v[z][0])), unroll)
    for q, value in held:
        v[q][tiles] = value


def smooth(v, load_s, load_i, tiles, unroll, left, after_sweep=None):
    zeros = jnp.zeros(v[0].shape[1:], F32)

    def first(t, _):
        for q in (0, 3):
            v[q][t] = load_s(q, t) * load_i(q, t)
        return 0

    loop(tiles, first, 0, unroll)
    for q in (1, 2):
        v[q][0] = zeros
        v[q][tiles - 1] = zeros
        v[q][tiles] = load_s(q, tiles) * load_i(q, tiles)
        v[3 * (q - 1)][tiles] = zeros
    for sweep, red in enumerate((False, True, False)):
        half_sweep(v, load_s, load_i, tiles, red, unroll, left if sweep == 2 else None)
        if after_sweep is not None:
            after_sweep(sweep)


def residuals(v, load_s, left, tiles, c0, c1, keep, unroll, valid=None):
    lane = lane_ids(v[0].shape[1])
    load_d, rest = left

    def use(t, r):
        keep(t, r)
        if valid is not None:
            virtual = isinstance(t, int) and t == tiles
            r = [jnp.where(valid(q, virtual), r[q], 0.0) for q in range(4)]
        c0[t] = (col_prev(r[2]) + col_next(r[0])) + 3.0 * (r[0] + r[2])
        c1[t] = (col_prev(r[3]) + col_next(r[1])) + 3.0 * (r[1] + r[3])

    def north(q, t):
        return jnp.where(lane == 0, roll_up(v[q][before(t, tiles)]), roll_up(v[q][t]))

    def south(q, t):
        return jnp.where(
            lane == LANES - 1, roll_down(v[q][after(t, tiles)]), roll_down(v[q][t])
        )

    def full(t):
        x = [v[q][t] for q in range(4)]
        beside = [
            (x[1] + north(1, t)) + (x[2] + col_prev(x[2])),
            (x[0] + south(0, t)) + (x[3] + col_prev(x[3])),
            (x[3] + north(3, t)) + (x[0] + col_next(x[0])),
            (x[2] + south(2, t)) + (x[1] + col_next(x[1])),
        ]
        use(t, [load_s(q, t) - (load_d(q, t) * x[q] - beside[q]) for q in range(4)])

    def body(i, carry):
        t = i + 1
        up, down = carry
        x = [v[q][t] for q in range(4)]
        up_here, down_next = roll_up(x[1]), roll_down(v[2][t + 1])
        beside0 = (x[1] + jnp.where(lane == 0, up, up_here)) + (x[2] + col_prev(x[2]))
        beside3 = (x[2] + jnp.where(lane == LANES - 1, down_next, down)) + (
            x[1] + col_next(x[1])
        )
        r0 = load_s(0, t) - (load_d(0, t) * x[0] - beside0)
        r3 = load_s(3, t) - (load_d(3, t) * x[3] - beside3)
        use(t, [r0, rest[1][t], rest[2][t], r3])
        return up_here, down_next

    full(0)
    loop(tiles - 2, body, (roll_up(v[1][0]), roll_down(v[2][1])), unroll)
    full(tiles - 1)
    full(tiles)


def restrict(c0, c1, tiles, rows, use, unroll):
    lane = lane_ids(rows)

    def body(t, carry):
        up, down = carry
        here, other = c0[t, :rows], c1[t, :rows]
        up_here = roll_up(other)
        down_next = roll_down(c0[after(t, tiles), :rows])
        north = jnp.where(lane == 0, up, up_here)
        south = jnp.where(lane == LANES - 1, down_next, down)
        use(t, ((north + south) + 3.0 * (here + other)) * (1.0 / 16.0))
        return up_here, down_next

    start = roll_up(c1[tiles, :rows]), roll_down(c0[0, :rows])
    body(tiles, loop(tiles, body, start, unroll))


class Fine:
    def __init__(self, own, halo, virtual, tiles, columns):
        self.own, self.halo, self.virtual = own, halo, virtual
        self.tiles, self.columns = tiles, columns

    def part(self, parity, t, start):
        return self.own[parity][t, pl.ds(8 + start, self.columns // 2, 2), :]

    def rows(self, q, t):
        return self.part(q % 2, t, q // 2)

    def whole(self, q, t):
        if t == self.tiles:
            return self.virtual[q][...]
        return jnp.concatenate([self.rows(q, t), self.halo[q][t]], 0)

    def ends(self, q, t):
        if t == self.tiles:
            whole = self.virtual[q][...]
            return whole[: self.columns // 2], whole[self.columns // 2 :]
        return self.rows(q, t), self.halo[q][t]

    def line(self, parity, t, column):
        row = self.own[parity][t, 8 + column : 9 + column]
        return jnp.broadcast_to(row, (8, LANES))

    def put(self, q, t, own, halo):
        pr, pc = q % 2, q // 2
        self.own[pr][t, pl.ds(8 + pc, self.columns // 2, 2), :] = own
        self.halo[q][t] = halo
        if pc == 1:
            self.own[pr][t, 7:8] = halo[7:8]
        else:
            at = 8 + self.columns
            self.own[pr][t, at : at + 1] = halo[0:1]

    def beside_columns(self, q, t, halo):
        sub = row_ids(8)
        pr, pc = q % 2, q // 2
        own = self.part(pr, t, pc - 1) + self.part(pr, t, pc + 1)
        if pc == 0:
            other = jnp.where(sub == 0, self.line(pr, t, self.columns - 1), col_prev(halo))
        else:
            other = jnp.where(sub == 7, self.line(pr, t, 0), col_next(halo))
        return own, halo + other


def fine_sweep(v, load_s, load_i, whole_s, whole_i, red, left):
    tiles = v.tiles
    y, z, qa, qb = (1, 2, 0, 3) if red else (3, 0, 2, 1)

    def lane_sum(parts, rolled, edge, lane_at):
        return [
            x + jnp.where(lane_ids(x.shape[0]) == lane_at, e, r)
            for x, r, e in zip(parts, rolled, edge)
        ]

    def beside_virtual(q):
        here, cols = v.whole(q ^ 1, tiles), v.whole(q ^ 2, tiles)
        lane = lane_ids(here.shape[0])
        if q % 2 == 0:
            lat = jnp.where(lane == 0, roll_up(v.whole(q ^ 1, tiles - 1)), roll_up(here))
        else:
            lat = jnp.where(lane == LANES - 1, roll_down(v.whole(q ^ 1, 0)), roll_down(here))
        return (here + lat) + (cols + (col_prev if q < 2 else col_next)(cols))

    held = [
        (q, (whole_s(q, tiles) + beside_virtual(q)) * whole_i(q, tiles)) for q in (y, z)
    ]
    y_before = [roll_up(x) for x in v.ends(y, tiles)]
    z_here = [roll_down(x) for x in v.ends(z, 0)]
    for t in range(tiles):
        vy, vz = v.ends(y, t), v.ends(z, t)
        y_here = [roll_up(x) for x in vy]
        z_after = [roll_down(x) for x in v.ends(z, t + 1)]
        lat_a = lane_sum(vy, y_here, y_before, 0)
        lat_b = lane_sum(vz, z_here, z_after, LANES - 1)
        new = []
        for q, lat, halo in ((qa, lat_a, vz[1]), (qb, lat_b, vy[1])):
            cols = v.beside_columns(q, t, halo)
            total = [x + (l + c) for x, l, c in zip(load_s(q, t), lat, cols)]
            value = [x * i for x, i in zip(total, load_i(q, t))]
            new.append((q, value))
            if left is not None:
                load_d, rest = left
                rest.put(q, t, *[x - d * u for x, d, u in zip(total, load_d(q, t), value)])
        for q, value in new:
            v.put(q, t, *value)
        y_before, z_here = y_here, z_after
    for q, value in held:
        v.virtual[q][...] = value


def fine_residuals(v, load_s, load_d, whole_s, whole_d, rest, c0, c1):
    tiles = v.tiles
    rows = v.columns // 2

    def columns_summed(t):
        for pr, ref in ((0, c0), (1, c1)):
            outer = rest.part(pr, t, -1) + rest.part(pr, t, 2)
            inner = rest.part(pr, t, 0) + rest.part(pr, t, 1)
            ref[t] = outer + 3.0 * inner

    def full(t):
        x = [v.whole(q, t) for q in range(4)]
        lane = lane_ids(x[0].shape[0])

        def north(q):
            return jnp.where(lane == 0, roll_up(v.whole(q, before(t, tiles))), roll_up(x[q]))

        def south(q):
            return jnp.where(
                lane == LANES - 1, roll_down(v.whole(q, after(t, tiles))), roll_down(x[q])
            )

        beside = [
            (x[1] + north(1)) + (x[2] + col_prev(x[2])),
            (x[0] + south(0)) + (x[3] + col_prev(x[3])),
            (x[3] + north(3)) + (x[0] + col_next(x[0])),
            (x[2] + south(2)) + (x[1] + col_next(x[1])),
        ]
        r = [whole_s(q, t) - (whole_d(q, t) * x[q] - beside[q]) for q in range(4)]
        if t == tiles:
            c0[t] = ((col_prev(r[2]) + col_next(r[0])) + 3.0 * (r[0] + r[2]))[:rows]
            c1[t] = ((col_prev(r[3]) + col_next(r[1])) + 3.0 * (r[1] + r[3]))[:rows]
        else:
            for q in range(4):
                rest.put(q, t, r[q][:rows], r[q][rows:])
            columns_summed(t)

    full(0)
    up = [roll_up(x) for x in v.ends(1, 0)]
    down = [roll_down(x) for x in v.ends(2, 1)]
    for t in range(1, tiles - 1):
        x = [v.ends(q, t) for q in range(4)]
        up_here = [roll_up(part) for part in x[1]]
        down_next = [roll_down(part) for part in v.ends(2, t + 1)]
        for q, ns, near, edge, lane_at in (
            (0, 1, up_here, up, 0), (3, 2, down, down_next, LANES - 1)
        ):
            cols = v.beside_columns(q, t, x[q ^ 2][1])
            r = []
            for i, (s, d) in enumerate(zip(load_s(q, t), load_d(q, t))):
                lane = lane_ids(s.shape[0])
                beside = x[ns][i] + jnp.where(lane == lane_at, edge[i], near[i]) + cols[i]
                r.append(s - (d * x[q][i] - beside))
            rest.put(q, t, *r)
        columns_summed(t)
        up, down = up_here, down_next
    full(tiles - 1)
    full(tiles)


def fine_kernel(
    s_ref, d_ref, i_ref, d1_ref, i1_ref, d2_ref,
    from_other, from_mate, polar_ref, corner_near, corner_far,
    r_ref, s1_ref, d1_virtual, d2_virtual, s2_ref, to_mate, to_other,
    v_ref, hv, pv, hr, c0, c1, hs, hd, hi, ps, pd, pi, n1, temp,
    w0, w1, w2, w3, e0, e1, pi1, black_even, black_odd, red_even, red_odd,
    part1, part2,
):
    tiles, columns = s_ref.shape[1], s_ref.shape[2]
    rows = columns // 2
    sub = row_ids(8)
    odd = is_odd()

    def halo(t, _):
        fill_halo(t, from_mate, from_other, odd, False, hs, hd, hi)
        return 0

    loop(tiles, halo, 0, tiles)
    total = -16.0
    for q in range(4):
        own_s, own_d = polar_unpacked(polar_ref, q)
        near_s, near_d = polar_unpacked(corner_near, q)
        far_s, far_d = polar_unpacked(corner_far, q)
        left_s, right_s = chosen(odd, near_s, far_s)
        left_d, right_d = chosen(odd, near_d, far_d)
        total = total + own_d
        ps[q] = own_s
        pd[q] = own_d
        pi[q] = inverse_of(own_d)
        source = jnp.where(sub >= 5, left_s, jnp.where(sub <= 2, right_s, 0.0))
        diag = jnp.where(sub >= 5, left_d, jnp.where(sub <= 2, right_d, 4.0))
        hs[q, tiles] = source
        hd[q, tiles] = diag
        hi[q, tiles] = inverse_of(diag)

    def loaders(ref, halo, virtual):
        def split(q, t):
            return ref[q % 2, t, pl.ds(q // 2, rows, 2), :], halo[q, t]

        def whole(q, t):
            if t == tiles:
                return jnp.concatenate([virtual[q], halo[q, t]], 0)
            return jnp.concatenate(split(q, t), 0)

        return split, whole

    load_s, whole_s = loaders(s_ref, hs, ps)
    load_d, whole_d = loaders(d_ref, hd, pd)
    load_i, whole_i = loaders(i_ref, hi, pi)

    def held(own_ref, halo_ref):
        return Fine(
            [own_ref.at[p] for p in (0, 1)],
            [halo_ref.at[q] for q in range(4)],
            [pv.at[q] for q in range(4)],
            tiles,
            columns,
        )

    v, rest = held(v_ref, hv), held(r_ref, hr)
    for t in range(tiles):
        for q in (0, 3):
            v.put(q, t, *[x * i for x, i in zip(load_s(q, t), load_i(q, t))])
    for q in (1, 2):
        for t in (0, tiles - 1):
            v.put(q, t, jnp.zeros((rows, LANES), F32), jnp.zeros((8, LANES), F32))
        pv[q] = whole_s(q, tiles) * whole_i(q, tiles)
        pv[3 * (q - 1)] = jnp.zeros((rows + 8, LANES), F32)
    for red, left in ((False, None), (True, None), (False, (load_d, rest))):
        fine_sweep(v, load_s, load_i, whole_s, whole_i, red, left)
    fine_residuals(v, load_s, load_d, whole_s, whole_d, rest, c0, c1)

    def coarse(t, value):
        n1[t] = value

    restrict(c0, c1, tiles, rows, coarse, tiles)

    def use(c, source):
        for q in range(4):
            s1_ref[q, c] = source[q]

    tiles1 = tiles // 2
    split_tiles(lambda t: n1[t], tiles1, rows, splitter(), temp, use)
    out = moved(jnp.concatenate([n1[tiles], total], 0), virtual_splitter())
    source = quarters_of(out[:rows], temp.at[0])
    screen = quarters_of(out[rows:], temp.at[1])
    for q in range(4):
        s1_ref[q, tiles1] = source[q]
        d1_virtual[q] = 4.0 + screen[q]
        pi1[q] = inverse_of(4.0 + screen[q])
    d2_virtual[...] = 4.0 + ((screen[0] + screen[1]) + (screen[2] + screen[3]))

    def own(main, virtual):
        return lambda q, t: virtual[q] if isinstance(t, int) and t == tiles1 else main[q, t]

    w = [w0, w1, w2, w3]
    rows1 = rows // 2
    row = row_ids(rows1)
    load_s, load_d = own(s1_ref, s1_ref.at[:, tiles1]), own(d1_ref, d1_virtual)

    def after_sweep(sweep):
        if sweep == 0:
            for t in range(tiles1 + 1):
                even, odd_red = reds(t == tiles1)
                black_even[t] = w[even ^ 1][t]
                black_odd[t] = w[odd_red ^ 1][t]

    left = load_d, {1: part1, 2: part2}
    smooth(w, load_s, own(i1_ref, pi1), tiles1, 16, left, after_sweep)

    def valid(q, virtual):
        even, odd_red = reds(virtual)
        first = 1 if q == odd_red ^ 1 else 2
        last = rows1 - 2 if q == even ^ 1 else rows1 - 3
        return (row >= first) & (row <= last)

    def keep_red(t, r):
        even, odd_red = reds(isinstance(t, int) and t == tiles1)
        red_even[t] = r[even]
        red_odd[t] = r[odd_red]

    residuals(w, load_s, left, tiles1, e0, e1, keep_red, 16, valid)
    shared = {}

    def edges(t, partial):
        virtual = t == tiles1
        even, odd_red = reds(virtual)
        s2_ref[t] = partial
        packs = state_packs(
            [s1_ref[q, t] for q in range(4)],
            [load_d(q, t) for q in range(4)],
            [w[q][t] for q in range(4)],
            {even ^ 1: black_even[t], odd_red ^ 1: black_odd[t]},
            {even: red_even[t], odd_red: red_odd[t]},
            partial,
            d2_virtual[...] if virtual else d2_ref[t],
            virtual,
        )
        right, left = packs
        count = tiles1 + 1
        for i in (0, 1):
            to_mate[i * count + t], to_other[i * count + t] = chosen(odd, left[i], right[i])
        if t % 2 == 0:
            pair = chosen(odd, left[2], roll_rows(right[2], 4))
            shared[0] = pair
        else:
            pair = chosen(odd, roll_rows(left[2], 4), right[2])
            pair = [jnp.where(sub < 4, x, y) for x, y in zip(shared[0], pair)]
        if t % 2 == 1 or virtual:
            to_mate[2 * count + t // 2], to_other[2 * count + t // 2] = pair

    restrict(e0, e1, tiles1, rows1, edges, 16)


def merge_kernel(r_ref, out_ref, out_buf, sems):
    tiles = r_ref.shape[1]
    columns = out_ref.shape[0]
    matrix = merger()
    chunk = out_ref.shape[1] // GROUPS
    copies = []
    for group in range(GROUPS):
        for batch in range(tiles // GROUPS // BATCH):
            start = group * (tiles // GROUPS) + batch * BATCH
            own = slice(8, 8 + columns)
            both = [
                jnp.concatenate([r_ref[0, start + i, own], r_ref[1, start + i, own]], 1)
                for i in range(BATCH)
            ]
            out = moved(jnp.concatenate(both, 0), matrix)
            for i in range(BATCH):
                where = slice((start + i) * 256, (start + i + 1) * 256)
                out_buf[:, where] = out[columns * i : columns * (i + 1)]
        part = pl.ds(group * chunk, chunk)
        copy = pltpu.make_async_copy(out_buf.at[:, part], out_ref.at[:, part], sems.at[group])
        copy.start()
        copies.append(copy)
    for copy in copies:
        copy.wait()


def coarse_kernel(
    s_ref, d_ref, i_ref, d_virtual, d2_ref, d2_virtual, s2_ref, from_other, from_mate,
    solution_ref, residual_ref,
    v0, v1, v2, v3, c0, c1, hs, hd, hi, part, fixes, rest1, rest2, s, d, inv, va, vb,
):
    v = [v0, v1, v2, v3]
    tiles, own = d_ref.shape[1], d_ref.shape[2]
    rows = own + 8
    count = tiles + 1
    sub = row_ids(8)
    odd_band = is_odd()
    def rim(x):
        return jnp.where(sub < 4, x[:8], x[own - 8 :])

    for t in range(count):
        places = t, count + t, 2 * count + t // 2
        packs = [chosen(odd_band, from_mate[i], from_other[i]) for i in places]
        source = [jnp.zeros((8, LANES), F32)] * 4
        diag = [jnp.full((8, LANES), 4.0, F32)] * 4
        inverse = [jnp.zeros((8, LANES), F32)] * 4
        fixed = [jnp.zeros((8, LANES), F32)] * 4
        more = jnp.zeros((8, LANES), F32)
        total = jnp.ones((8, LANES), F32)
        for side, (a, ab, b, bb) in enumerate(sides(t == tiles)):
            near, far, step = (7, 6, -1) if side == 0 else (0, 1, 1)
            first = 6 if side == 0 else 0
            pack0, pack1, pack2 = (pair[side] for pair in packs)
            groups = [
                roll_rows(pack, first - 2 * g) for pack in (pack0, pack1) for g in range(4)
            ]
            pack2 = roll_rows(pack2, 4 * (t % 2) + (4 if side == 0 else 0))

            def put(group, q, at, x):
                group[q] = jnp.where(sub == at, x, group[q])

            for q in range(4):
                put(source, q, near, groups[q])
                put(diag, q, near, groups[4 + q])
            put(source, bb, far, groups[0])
            put(diag, bb, far, groups[1])
            put(fixed, bb, far, groups[2])
            put(fixed, b, far, groups[3])
            put(source, b, far, groups[4])
            put(diag, b, far, 0.0)
            put(source, a, far, groups[5])
            put(fixed, ab, near, pack2)
            more = jnp.where(sub == far, groups[6], more)
            more = jnp.where((sub == far + step) | (sub == far + 2 * step), pack2, more)
            total = jnp.where(sub == far, pack2, total)
            total = jnp.where(sub == far + step, roll_rows(groups[7], step), total)
            for q in range(4):
                known = (sub == near) | (sub == far) if q == bb else sub == near
                inverse[q] = jnp.where(known, inverse_of(diag[q]), inverse[q])
        for q in range(4):
            own_d = rim(d_virtual[q] if t == tiles else d_ref[q, t])
            own_i = inverse_of(own_d) if t == tiles else rim(i_ref[q, t])
            hs[q, t] = jnp.concatenate([source[q], rim(s_ref[q, t])], 0)
            hd[q, t] = jnp.concatenate([diag[q], own_d], 0)
            hi[q, t] = jnp.concatenate([inverse[q], own_i], 0)
            fixes[q, t] = fixed[q]
        part[t] = more
        near_total = (diag[0] + diag[1]) + (diag[2] + diag[3]) - 12.0
        total = jnp.where((sub == 0) | (sub == 7), near_total, total)
        here = d2_virtual[...] if t == tiles else d2_ref[t]
        d[t] = jnp.concatenate([here, total], 0)
    def after_sweep(sweep):
        if sweep == 2:
            return
        for t in range(count):
            (a, ab, b, bb), (_, _, other_b, other_bb) = sides(t == tiles)
            todo = {}
            if sweep == 0:
                todo = {ab: (sub == 7) | (sub == 1), bb: (sub == 6) | (sub == 0)}
            else:
                todo = {b: sub == 6, other_b: sub == 1}
            for q, mask in todo.items():
                v[q][t, :8] = jnp.where(mask, fixes[q, t], v[q][t, :8])

    def of(ref):
        return lambda q, t: ref[q, t]

    left = of(hd), {1: rest1, 2: rest2}
    smooth(v, of(hs), of(hi), tiles, 16, left, after_sweep)
    row = row_ids(16)

    def valid(q, virtual):
        even, odd_red = reds(virtual)
        after_band = 0 if q == odd_red ^ 1 else 1
        before_band = 7 if q == even ^ 1 else 6
        first = 8 if q == odd_red ^ 1 else 9
        last = 15 if q == even ^ 1 else 14
        return (row <= after_band) | ((row >= before_band) & (row <= first)) | (row >= last)

    residuals(v, of(hs), left, tiles, c0, c1, lambda t, r: None, 16, valid)

    lane, row = lane_ids(rows), row_ids(rows)
    even = (lane + row) % 2 == 0
    odd = jnp.logical_not(even)

    def start(t, value):
        ends = value[8:]
        source = jnp.concatenate(
            [
                s2_ref[t, :8] + jnp.where(sub < 4, ends, 0.0),
                s2_ref[t, own - 8 :] + jnp.where(sub >= 4, ends, 0.0),
                value[:8] + part[t],
            ],
            0,
        )
        inverse = inverse_of(d[t])
        s[t] = source
        inv[t] = inverse
        virtual = isinstance(t, int) and t == tiles
        va[t] = jnp.where(odd if virtual else even, source * inverse, 0.0)

    restrict(c0, c1, tiles, 16, start, 16)

    def scan(v, use):
        up, down = roll_up(v[tiles]), roll_down(v[0])
        for t in range(tiles + 1):
            x = v[t]
            up_here, down_next = roll_up(x), roll_down(v[after(t, tiles)])
            north = jnp.where(lane == 0, up, up_here)
            south = jnp.where(lane == LANES - 1, down_next, down)
            use(t, x, (col_prev(x) + col_next(x)) + (north + south))
            up, down = up_here, down_next

    for old, new, mask, other in ((va, vb, odd, even), (vb, va, even, odd), (va, vb, odd, even)):

        def relax(t, x, beside):
            update = other if t == tiles else mask
            new[t] = jnp.where(update, (s[t] + beside) * inv[t], x)

        scan(old, relax)

    def finish(t, x, beside):
        if t < tiles:
            where = slice(t * LANES, (t + 1) * LANES)
            solution_ref[:, where] = x[:own]
            residual_ref[:, where] = (s[t] - (d[t] * x - beside))[:own]

    scan(vb, finish)


VMEM = pl.BlockSpec(memory_space=pltpu.VMEM)
HBM = pl.BlockSpec(memory_space=pltpu.HBM)


def call(kernel, out_shapes, scratch, *args, sems=None, far_in=0, far_out=0):
    scratch = [pltpu.VMEM(x, F32) if isinstance(x, tuple) else x for x in scratch]
    if sems is not None:
        scratch.append(pltpu.SemaphoreType.DMA(sems))
    return pl.pallas_call(
        kernel,
        out_shape=[
            jax.ShapeDtypeStruct(x, F32) if isinstance(x, tuple) else x for x in out_shapes
        ],
        in_specs=[HBM] * far_in + [VMEM] * (len(args) - far_in),
        out_specs=[HBM] * far_out + [VMEM] * (len(out_shapes) - far_out),
        scratch_shapes=scratch,
        compiler_params=pltpu.CompilerParams(vmem_limit_bytes=40 * 2**20),
    )(*args)


def swapped_with(x, by):
    count = lax.axis_size("lon")
    pairs = [(i, (i + by) % count) for i in range(0, count, 2)]
    return lax.ppermute(x, "lon", pairs + [(b, a) for a, b in pairs])


def swapped_edges(to_mate, to_other):
    from_mate = swapped_with(to_mate, 1)
    return from_mate, swapped_with(to_other, -1)


def body(right_side, texel_weight, seam_flags):
    columns, height = right_side.shape
    half_turn = lax.axis_size("lon") // 2
    tiles, rows = height // 256, columns // 2
    tiles1, rows1 = tiles // 2, rows // 2
    temp = (BATCH, 2, columns, LANES)
    natural = (2, tiles, columns, LANES)
    padded = (2, tiles, columns + 16, LANES)
    quarters1 = (4, tiles1, rows1, LANES)
    split = (4, 2, 4 * tiles, LANES)
    right_here, weight_here, to_mate, to_other, corner = call(
        edge_kernel,
        [(columns, height), jax.ShapeDtypeStruct((columns, height), BF16)]
        + [(2, tiles, 8, LANES), (2, tiles, 8, LANES), (2, 8, LANES)],
        [pltpu.VMEM(seam_flags.shape, jnp.int32), split, split, (tiles, 8, LANES)],
        *[
            pltpu.with_memory_space_constraint(x, pltpu.HBM)
            for x in (right_side, texel_weight, seam_flags)
        ],
        sems=(7,), far_in=3,
    )
    from_mate, from_other = swapped_edges(to_mate, to_other)
    corner_far = swapped_with(corner, half_turn - 1)
    corner_near = swapped_with(corner, half_turn + 1)
    ends = (2, 2, columns, LANES)
    (polar_own,) = call(
        polar_kernel, [(2, rows, LANES)], [ends, ends],
        right_here, weight_here, seam_flags, corner,
    )
    polar = lax.ppermute(
        polar_own, "lon", [(i, (i + half_turn) % (2 * half_turn)) for i in range(2 * half_turn)]
    )
    s, d, inverse, d1, i1, d2 = call(
        bulk_kernel,
        [natural] * 3 + [quarters1, quarters1, quarters1[1:]],
        [(BATCH, columns, LANES), (tiles, 8, LANES), (tiles, rows, LANES), (BATCH, 2, rows, LANES)],
        right_here, weight_here, seam_flags, polar_own,
    )

    def level_scratch(tiles, rows):
        return [(tiles + 1, rows, LANES)] * 6

    def halo_scratch(tiles):
        return [(4, tiles + 1, 8, LANES)] * 3

    pack1 = (2 * (tiles1 + 1) + tiles1 // 2 + 1, 8, LANES)
    r, s1, d1_virtual, d2_virtual, s2_own, to_mate, to_other = call(
        fine_kernel,
        [padded, (4, tiles1 + 1, rows1, LANES), (4, rows1, LANES), (rows1, LANES)]
        + [(tiles1 + 1, rows1, LANES), pack1, pack1],
        [padded, (4, tiles, 8, LANES), (4, rows + 8, LANES), (4, tiles, 8, LANES)]
        + [(tiles + 1, rows, LANES)] * 2
        + halo_scratch(tiles)
        + [(4, rows, LANES)] * 3
        + [(tiles + 1, rows, LANES), (BATCH, 2, rows, LANES)]
        + level_scratch(tiles1, rows1)
        + [(4, rows1, LANES)]
        + [(tiles1 + 1, rows1, LANES)] * 4
        + [(tiles1, rows1, LANES)] * 2,
        s, d, inverse, d1, i1, d2, from_other, from_mate, polar, corner_near, corner_far,
    )
    from_mate, from_other = swapped_edges(to_mate, to_other)
    (fine_residual,) = call(
        merge_kernel, [(columns, height)], [(columns, height)], r,
        sems=(GROUPS,), far_out=1,
    )
    wide = (tiles1 + 1, rows1 + 8, LANES)
    solution_2, residual_2 = call(
        coarse_kernel,
        [(columns // 4, height // 4)] * 2,
        level_scratch(tiles1, 16)
        + [(4, tiles1 + 1, 16, LANES)] * 3
        + [(tiles1 + 1, 8, LANES), (4, tiles1 + 1, 8, LANES)]
        + [(tiles1, 16, LANES)] * 2
        + [wide] * 5,
        s1, d1, i1, d1_virtual, d2, d2_virtual, s2_own, from_other, from_mate,
    )
    return fine_residual, solution_2, residual_2


def solution(mesh):
    spec = P(("groups", "lon"), None)
    return jax.shard_map(
        body, mesh=mesh, in_specs=(spec,) * 3, out_specs=(spec,) * 3, check_vma=False
    )
```

```python
import jax
import jax.numpy as jnp
from jax import lax
from jax.experimental import pallas as pl
from jax.experimental.pallas import tpu as pltpu
from jax.sharding import PartitionSpec as P

TILE = 32
SEAM_SCALE = 0.1
LANES = 128
GROUPS = 4
BATCH = 4
F32 = jnp.float32
BF16 = jnp.bfloat16


def loop(count, body, carry=0, unroll=4):
    unroll = min(unroll, count)

    def steps(block, carry):
        for i in range(unroll):
            carry = body(block * unroll + i, carry)
        return carry

    whole = count // unroll
    carry = steps(0, carry) if whole == 1 else lax.fori_loop(0, whole, steps, carry)
    for t in range(whole * unroll, count):
        carry = body(t, carry)
    return carry


def before(t, tiles):
    return (tiles if t == 0 else t - 1) if isinstance(t, int) else jnp.where(t == 0, tiles, t - 1)


def after(t, tiles):
    return (0 if t == tiles else t + 1) if isinstance(t, int) else t + 1


def lane_ids(rows):
    return lax.broadcasted_iota(jnp.int32, (rows, LANES), 1)


def row_ids(rows):
    return lax.broadcasted_iota(jnp.int32, (rows, LANES), 0)


def roll_up(x):
    return pltpu.roll(x, 1, 1)


def roll_down(x):
    return pltpu.roll(x, LANES - 1, 1)


def roll_rows(x, by):
    by %= x.shape[0]
    return x if by == 0 else pltpu.roll(x, by, 0)


def roll_lanes(x, by):
    by %= LANES
    return x if by == 0 else pltpu.roll(x, by, 1)


def col_prev(x):
    return pltpu.roll(x, 1, 0)


def col_next(x):
    return pltpu.roll(x, x.shape[0] - 1, 0)


def inverse_of(x):
    return 1.0 / x


def selector(shape, rule):
    a = lax.broadcasted_iota(jnp.int32, shape, 0)
    b = lax.broadcasted_iota(jnp.int32, shape, 1)
    return jnp.where(rule(a, b), 1.0, 0.0).astype(BF16)


def splitter():
    return selector((256, 256), lambda a, b: a == 2 * (b % LANES) + b // LANES)


def merger():
    return selector((256, 256), lambda a, b: b == 2 * (a % LANES) + a // LANES)


def virtual_splitter():
    return selector(
        (LANES, 256),
        lambda a, b: a // 2 + jnp.where(a >= 64, 64, 0) + LANES * (a % 2) == b,
    )


def moved(x, matrix, exact=None):
    rows = x.shape[0]
    high = x.astype(BF16)
    low = (x - high.astype(F32)).astype(BF16)
    terms = [high, low] if exact is None else [high, low, exact]
    out = jnp.dot(jnp.concatenate(terms, 0), matrix, preferred_element_type=F32)
    both = out[:rows] + out[rows : 2 * rows]
    return both if exact is None else (both, out[2 * rows :])


def quarters_of(parts, temp):
    count = parts.shape[0] // 2
    temp[0] = parts[:, :LANES]
    temp[1] = parts[:, LANES:]
    return [temp[pr, pl.ds(pc, count, 2), :] for pc in (0, 1) for pr in (0, 1)]


def reds(swapped):
    return (1, 2) if swapped else (0, 3)


def interleaved(group, offset):
    sub = row_ids(8)
    packed = roll_rows(group[0], offset)
    for q in range(1, 4):
        packed = jnp.where(sub // 2 == q, roll_rows(group[q], 2 * q + offset), packed)
    return packed


def edge_packs(source, diag, swapped):
    sub = row_ids(8)
    even, odd = reds(swapped)
    rows = source[0].shape[0]
    packs = []
    for here, first, second, row, step in (
        (slice(rows - 8, rows), even, odd, 6, 1),
        (slice(0, 8), odd, even, 1, -1),
    ):
        gs = [x[here] for x in source]
        gd = [x[here] for x in diag]
        near = gs[first] * inverse_of(gd[first])
        far = roll_rows(gs[second] * inverse_of(gd[second]), step)
        gs[first] = jnp.where(sub == row, near, gs[first])
        gd[first] = jnp.where(sub == row, far, gd[first])
        offset = 2 if row == 6 else 0
        packs.append((interleaved(gs, offset), interleaved(gd, offset)))
    return packs


def unpacked_halo(left, right, swapped):
    sub = row_ids(8)
    even, odd = reds(swapped)
    (al, bl), (ar, br) = left, right
    source, diag = [], []
    for q in range(4):
        s = jnp.where(
            sub >= 6,
            roll_rows(al, 6 - 2 * q),
            jnp.where(sub <= 1, roll_rows(ar, -2 * q), 0.0),
        )
        d = jnp.where(
            sub >= 6,
            roll_rows(bl, 6 - 2 * q),
            jnp.where(sub <= 1, roll_rows(br, -2 * q), 4.0),
        )
        if q == even:
            s = jnp.where(sub == 2, roll_rows(br, 1 - 2 * odd), s)
            d = jnp.where((sub == 2) | (sub == 6), 1.0, d)
        if q == odd:
            s = jnp.where(sub == 5, roll_rows(bl, 5 - 2 * even), s)
            d = jnp.where((sub == 5) | (sub == 1), 1.0, d)
        source.append(s)
        diag.append(d)
    return source, diag


def is_odd():
    return lax.rem(lax.axis_index("lon"), 2) == 1


def chosen(odd, a, b):
    return jnp.where(odd, a, b), jnp.where(odd, b, a)


def store_edges(t, packs, odd, to_mate, to_other):
    right, left = packs
    for i in (0, 1):
        to_mate[i, t], to_other[i, t] = chosen(odd, left[i], right[i])


def sides(swapped):
    even, odd = reds(swapped)
    return (even, even ^ 1, odd, odd ^ 1), (odd, odd ^ 1, even, even ^ 1)


def paired(groups, shift):
    sub = row_ids(8)
    packed = roll_rows(groups[0], shift)
    for g in (1, 2, 3):
        packed = jnp.where(sub // 2 == g, roll_rows(groups[g], 2 * g + shift), packed)
    return packed


def state_packs(source, diag, last, first_black, residual, partial, diag2, swapped):
    sub = row_ids(8)
    rows = source[0].shape[0]
    packs = []
    for (a, ab, b, bb), here, near, far, step in zip(
        sides(swapped), (slice(rows - 8, rows), slice(0, 8)), (7, 0), (6, 1), (-1, 1)
    ):
        s, d, v = ([x[here] for x in group] for group in (source, diag, last))
        part, d2 = partial[here], diag2[here]
        beside = [
            s[bb] + v[a],
            d[bb],
            first_black[bb][here],
            v[b],
            s[b] - d[b] * v[b] + v[ab],
            residual[a][here] - v[bb],
            part,
            roll_rows(d2, -step),
        ]
        groups = [jnp.where(sub == far, y, x) for x, y in zip(s + d, beside)]
        shift = 2 if near == 7 else 0
        more = jnp.where(sub == far, d2, first_black[ab][here])
        more = jnp.where(sub == far + step, part, more)
        more = jnp.where(sub == far + 2 * step, part * inverse_of(d2), more)
        packs.append((paired(groups[:4], shift), paired(groups[4:], shift), more))
    return packs


def fill_halo(t, from_mate, from_other, odd, swapped, hs, hd, hi):
    al, ar = chosen(odd, from_mate[0, t], from_other[0, t])
    bl, br = chosen(odd, from_mate[1, t], from_other[1, t])
    source, diag = unpacked_halo((al, bl), (ar, br), swapped)
    for q in range(4):
        hs[q, t] = source[q]
        hd[q, t] = diag[q]
        hi[q, t] = inverse_of(diag[q])


def loader(own, halo, virtual, tiles):
    def load(q, t):
        if isinstance(t, int) and t == tiles:
            return jnp.concatenate([virtual[q], halo[q, t]], 0)
        return jnp.concatenate([own[q, t], halo[q, t]], 0)

    return load


def polar_packs(tiles_of):
    lane = lane_ids(tiles_of[0][0].shape[0])
    packs = []
    for pc in (0, 1):
        parts = [*tiles_of[2 * pc], *tiles_of[2 * pc + 1]]
        packed = parts[0]
        for m in range(1, 4):
            mine = (lane + (16 - 32 * m) % LANES) % LANES < 32
            packed = jnp.where(mine, roll_lanes(parts[m], 32 * m), packed)
        packs.append(packed)
    return packs


def polar_unpacked(x, q):
    lane = lane_ids(x.shape[1])
    used = (lane < 16) | (lane >= LANES - 16)
    m = 2 * (q % 2)
    return (
        jnp.where(used, roll_lanes(x[q // 2], 32 * m), 0.0),
        jnp.where(used, roll_lanes(x[q // 2], 32 * (m + 1)), 4.0),
    )


def seam_scales(flags, chunks):
    flag_cols, flag_lats = flags.shape
    flags = jnp.concatenate(
        [flags.astype(F32), jnp.zeros((8 - flag_cols, flag_lats), F32)], 0
    )
    lat = lax.broadcasted_iota(jnp.int32, (8, flag_lats), 1)
    stacked = jnp.concatenate([jnp.where(lat // 8 == c, flags, 0.0) for c in chunks], 0)
    spread = selector((flag_lats, LANES), lambda a, b: a % 8 == b // (TILE // 2))
    spread_flags = jnp.dot(stacked.astype(BF16), spread, preferred_element_type=F32)
    scale = jnp.where(spread_flags > 0.5, SEAM_SCALE, 1.0)
    return scale.reshape(len(chunks), 8, LANES)


def seam_rows(scales, flag_cols, rows):
    size = (rows // flag_cols, LANES)
    return jnp.concatenate(
        [jnp.broadcast_to(scales[i : i + 1], size) for i in range(flag_cols)], 0
    )


def edge_kernel(
    right_ref, weight_ref, flag_ref,
    right_here, weight_here, scale_ref, to_mate, to_other, corner_ref,
    flags, temp_s, temp_w, sems,
):
    columns, height = right_ref.shape
    tiles = height // 256
    pairs = [(flag_ref, flags)]
    inputs = (right_ref, right_here, 8), (weight_ref, weight_here, 16)
    for src, dst, size in inputs:
        for start in (0, columns - size):
            part = pl.ds(start, size)
            pairs.append((src.at[part], dst.at[part]))
    for src, dst, size in inputs:
        part = pl.ds(size, columns - 2 * size)
        pairs.append((src.at[part], dst.at[part]))
    copies = [
        pltpu.make_async_copy(src, dst, sems.at[i]) for i, (src, dst) in enumerate(pairs)
    ]
    for copy in copies:
        copy.start()
    odd = is_odd()
    matrix = splitter()
    flag_cols = flag_ref.shape[0]
    copies[0].wait()
    scale_ref[...] = seam_scales(flags[...], range(tiles))
    for copy in copies[1:5]:
        copy.wait()
    sub = row_ids(8)
    def ends(size):
        return slice(0, size), slice(columns - size, columns)

    count = tiles // 4
    found = []
    for batch in range(4):
        chunks = range(batch * count, (batch + 1) * count)
        lanes = [slice(c * 256, (c + 1) * 256) for c in chunks]
        source, weight = moved(
            jnp.concatenate([right_here[at, w] for w in lanes for at in ends(8)], 0),
            matrix,
            jnp.concatenate([weight_here[at, w] for w in lanes for at in ends(16)], 0),
        )
        weight = weight.reshape(count, 32, 256)
        weight = jnp.concatenate([weight[:, :8], weight[:, 24:]], 1).reshape(count * 16, 256)
        source = quarters_of(source, temp_s.at[batch])
        weight = quarters_of(weight, temp_w.at[batch])
        for i, c in enumerate(chunks):
            here = slice(i * 8, (i + 1) * 8)
            scales = scale_ref[c]
            scale = jnp.where(sub < 4, scales[:1], scales[flag_cols - 1 : flag_cols])
            pair = [x[here] for x in source], [4.0 + w[here] * scale for w in weight]
            store_edges(c, edge_packs(*pair, False), odd, to_mate, to_other)
            if c in (0, tiles - 1):
                found.append(pair)
    both = mirrored_ends(*found)
    for pc in (0, 1):
        corner_ref[pc] = both[8 * pc : 8 * (pc + 1)]
    for copy in copies[5:]:
        copy.wait()


def mirrored_ends(first, last):
    mirror = selector((LANES, LANES), lambda a, b: a + b == LANES - 1)
    lane = lane_ids(first[0][0].shape[0])
    ends = [
        [jnp.where(lane >= 64, last[i][q ^ 1], first[i][q ^ 1]) for i in (0, 1)]
        for q in range(4)
    ]
    return moved(jnp.concatenate(polar_packs(ends), 0), mirror)


def polar_kernel(right_ref, weight_ref, scale_ref, edges_first, polar_ref, temp_s, temp_w):
    columns, height = right_ref.shape
    rows, tiles = columns // 2, height // 256
    flag_cols = columns // TILE
    lanes = slice(0, 256), slice(height - 256, height)
    source, weight = moved(
        jnp.concatenate([right_ref[:, w] for w in lanes], 0),
        splitter(),
        jnp.concatenate([weight_ref[:, w] for w in lanes], 0),
    )
    found = []
    for end in (0, 1):
        here = slice(end * columns, (end + 1) * columns)
        scale = seam_rows(scale_ref[end * (tiles - 1)], flag_cols, rows)
        found.append(
            (
                quarters_of(source[here], temp_s.at[end]),
                [4.0 + w * scale for w in quarters_of(weight[here], temp_w.at[end])],
            )
        )
    both = mirrored_ends(*found)
    for pc in (0, 1):
        polar_ref[pc] = both[pc * rows : (pc + 1) * rows]


def bulk_kernel(
    right_ref, weight_ref, scale_ref, polar_first,
    s_ref, d_ref, i_ref, d1_ref, i1_ref, d2_ref,
    temp, e_ref, split_temp,
):
    tiles, columns = s_ref.shape[1], s_ref.shape[2]
    rows = columns // 2
    matrix = splitter()
    for start in range(0, tiles, BATCH):
        lanes = [slice((start + i) * 256, (start + i + 1) * 256) for i in range(BATCH)]
        source, weight = moved(
            jnp.concatenate([right_ref[:, w] for w in lanes], 0),
            matrix,
            jnp.concatenate([weight_ref[:, w] for w in lanes], 0),
        )
        for i in range(BATCH):
            c = start + i
            here = slice(i * columns, (i + 1) * columns)
            scale = seam_rows(scale_ref[c], columns // TILE, columns)
            screens = []
            for pr in (0, 1):
                half = slice(pr * LANES, (pr + 1) * LANES)
                screen = weight[here, half] * scale
                diag = 4.0 + screen
                s_ref[pr, c] = source[here, half]
                d_ref[pr, c] = diag
                i_ref[pr, c] = 1.0 / diag
                screens.append(screen)
            temp[i] = screens[0] + screens[1]
            e_ref[c] = temp[i, pl.ds(0, rows, 2), :] + temp[i, pl.ds(1, rows, 2), :]

    def use(c, screen):
        for q in range(4):
            d1_ref[q, c] = 4.0 + screen[q]
            i1_ref[q, c] = inverse_of(4.0 + screen[q])
        d2_ref[c] = 4.0 + ((screen[0] + screen[1]) + (screen[2] + screen[3]))

    split_tiles(lambda t: e_ref[t], tiles // 2, rows, matrix, split_temp, use)


def split_tiles(load, tiles, rows, matrix, temp, use):
    for start in range(0, tiles, BATCH):
        wide = [
            jnp.concatenate([load(2 * c), load(2 * c + 1)], 1)
            for c in range(start, start + BATCH)
        ]
        out = moved(jnp.concatenate(wide, 0), matrix)
        for i in range(BATCH):
            use(start + i, quarters_of(out[i * rows : (i + 1) * rows], temp.at[i, :, :rows]))


def half_sweep(v, load_s, load_i, tiles, red, unroll, left=None):
    rows = v[0].shape[1]
    lane = lane_ids(rows)
    y, z, qa, qb = (1, 2, 0, 3) if red else (3, 0, 2, 1)
    col_a, col_b = (col_prev, col_next) if red else (col_next, col_prev)

    def beside_virtual(q):
        ns, we = q ^ 1, q ^ 2
        here = v[ns][tiles]
        if q % 2 == 0:
            lat = jnp.where(lane == 0, roll_up(v[ns][tiles - 1]), roll_up(here))
        else:
            lat = jnp.where(lane == LANES - 1, roll_down(v[ns][0]), roll_down(here))
        cols = v[we][tiles]
        return (here + lat) + (cols + (col_prev if q < 2 else col_next)(cols))

    held = [
        (q, (load_s(q, tiles) + beside_virtual(q)) * load_i(q, tiles)) for q in (y, z)
    ]

    def body(t, carry):
        y_before, z_here = carry
        vy, vz = v[y][t], v[z][t]
        y_here = roll_up(vy)
        z_after = roll_down(v[z][t + 1])
        lat_a = vy + jnp.where(lane == 0, y_before, y_here)
        lat_b = vz + jnp.where(lane == LANES - 1, z_after, z_here)
        all_a = load_s(qa, t) + (lat_a + (vz + col_a(vz)))
        all_b = load_s(qb, t) + (lat_b + (vy + col_b(vy)))
        new_a, new_b = all_a * load_i(qa, t), all_b * load_i(qb, t)
        v[qa][t], v[qb][t] = new_a, new_b
        if left is not None:
            load_d, rest = left
            rest[qa][t] = all_a - load_d(qa, t) * new_a
            rest[qb][t] = all_b - load_d(qb, t) * new_b
        return y_here, z_after

    loop(tiles, body, (roll_up(v[y][tiles]), roll_down(v[z][0])), unroll)
    for q, value in held:
        v[q][tiles] = value


def smooth(v, load_s, load_i, tiles, unroll, left, after_sweep=None):
    zeros = jnp.zeros(v[0].shape[1:], F32)

    def first(t, _):
        for q in (0, 3):
            v[q][t] = load_s(q, t) * load_i(q, t)
        return 0

    loop(tiles, first, 0, unroll)
    for q in (1, 2):
        v[q][0] = zeros
        v[q][tiles - 1] = zeros
        v[q][tiles] = load_s(q, tiles) * load_i(q, tiles)
        v[3 * (q - 1)][tiles] = zeros
    for sweep, red in enumerate((False, True, False)):
        half_sweep(v, load_s, load_i, tiles, red, unroll, left if sweep == 2 else None)
        if after_sweep is not None:
            after_sweep(sweep)


def residuals(v, load_s, left, tiles, c0, c1, keep, unroll, valid=None):
    lane = lane_ids(v[0].shape[1])
    load_d, rest = left

    def use(t, r):
        keep(t, r)
        if valid is not None:
            virtual = isinstance(t, int) and t == tiles
            r = [jnp.where(valid(q, virtual), r[q], 0.0) for q in range(4)]
        c0[t] = (col_prev(r[2]) + col_next(r[0])) + 3.0 * (r[0] + r[2])
        c1[t] = (col_prev(r[3]) + col_next(r[1])) + 3.0 * (r[1] + r[3])

    def north(q, t):
        return jnp.where(lane == 0, roll_up(v[q][before(t, tiles)]), roll_up(v[q][t]))

    def south(q, t):
        return jnp.where(
            lane == LANES - 1, roll_down(v[q][after(t, tiles)]), roll_down(v[q][t])
        )

    def full(t):
        x = [v[q][t] for q in range(4)]
        beside = [
            (x[1] + north(1, t)) + (x[2] + col_prev(x[2])),
            (x[0] + south(0, t)) + (x[3] + col_prev(x[3])),
            (x[3] + north(3, t)) + (x[0] + col_next(x[0])),
            (x[2] + south(2, t)) + (x[1] + col_next(x[1])),
        ]
        use(t, [load_s(q, t) - (load_d(q, t) * x[q] - beside[q]) for q in range(4)])

    def body(i, carry):
        t = i + 1
        up, down = carry
        x = [v[q][t] for q in range(4)]
        up_here, down_next = roll_up(x[1]), roll_down(v[2][t + 1])
        beside0 = (x[1] + jnp.where(lane == 0, up, up_here)) + (x[2] + col_prev(x[2]))
        beside3 = (x[2] + jnp.where(lane == LANES - 1, down_next, down)) + (
            x[1] + col_next(x[1])
        )
        r0 = load_s(0, t) - (load_d(0, t) * x[0] - beside0)
        r3 = load_s(3, t) - (load_d(3, t) * x[3] - beside3)
        use(t, [r0, rest[1][t], rest[2][t], r3])
        return up_here, down_next

    full(0)
    loop(tiles - 2, body, (roll_up(v[1][0]), roll_down(v[2][1])), unroll)
    full(tiles - 1)
    full(tiles)


def restrict(c0, c1, tiles, rows, use, unroll):
    lane = lane_ids(rows)

    def body(t, carry):
        up, down = carry
        here, other = c0[t, :rows], c1[t, :rows]
        up_here = roll_up(other)
        down_next = roll_down(c0[after(t, tiles), :rows])
        north = jnp.where(lane == 0, up, up_here)
        south = jnp.where(lane == LANES - 1, down_next, down)
        use(t, ((north + south) + 3.0 * (here + other)) * (1.0 / 16.0))
        return up_here, down_next

    start = roll_up(c1[tiles, :rows]), roll_down(c0[0, :rows])
    body(tiles, loop(tiles, body, start, unroll))


class Fine:
    def __init__(self, own, halo, virtual, tiles, columns):
        self.own, self.halo, self.virtual = own, halo, virtual
        self.tiles, self.columns = tiles, columns

    def part(self, parity, t, start):
        return self.own[parity][t, pl.ds(8 + start, self.columns // 2, 2), :]

    def rows(self, q, t):
        return self.part(q % 2, t, q // 2)

    def whole(self, q, t):
        if t == self.tiles:
            return self.virtual[q][...]
        return jnp.concatenate([self.rows(q, t), self.halo[q][t]], 0)

    def ends(self, q, t):
        if t == self.tiles:
            whole = self.virtual[q][...]
            return whole[: self.columns // 2], whole[self.columns // 2 :]
        return self.rows(q, t), self.halo[q][t]

    def line(self, parity, t, column):
        row = self.own[parity][t, 8 + column : 9 + column]
        return jnp.broadcast_to(row, (8, LANES))

    def put(self, q, t, own, halo):
        pr, pc = q % 2, q // 2
        self.own[pr][t, pl.ds(8 + pc, self.columns // 2, 2), :] = own
        self.halo[q][t] = halo
        if pc == 1:
            self.own[pr][t, 7:8] = halo[7:8]
        else:
            at = 8 + self.columns
            self.own[pr][t, at : at + 1] = halo[0:1]

    def beside_columns(self, q, t, halo):
        sub = row_ids(8)
        pr, pc = q % 2, q // 2
        own = self.part(pr, t, pc - 1) + self.part(pr, t, pc + 1)
        if pc == 0:
            other = jnp.where(sub == 0, self.line(pr, t, self.columns - 1), col_prev(halo))
        else:
            other = jnp.where(sub == 7, self.line(pr, t, 0), col_next(halo))
        return own, halo + other


def fine_sweep(v, load_s, load_i, whole_s, whole_i, red, left):
    tiles = v.tiles
    y, z, qa, qb = (1, 2, 0, 3) if red else (3, 0, 2, 1)

    def lane_sum(parts, rolled, edge, lane_at):
        return [
            x + jnp.where(lane_ids(x.shape[0]) == lane_at, e, r)
            for x, r, e in zip(parts, rolled, edge)
        ]

    def beside_virtual(q):
        here, cols = v.whole(q ^ 1, tiles), v.whole(q ^ 2, tiles)
        lane = lane_ids(here.shape[0])
        if q % 2 == 0:
            lat = jnp.where(lane == 0, roll_up(v.whole(q ^ 1, tiles - 1)), roll_up(here))
        else:
            lat = jnp.where(lane == LANES - 1, roll_down(v.whole(q ^ 1, 0)), roll_down(here))
        return (here + lat) + (cols + (col_prev if q < 2 else col_next)(cols))

    held = [
        (q, (whole_s(q, tiles) + beside_virtual(q)) * whole_i(q, tiles)) for q in (y, z)
    ]
    y_before = [roll_up(x) for x in v.ends(y, tiles)]
    z_here = [roll_down(x) for x in v.ends(z, 0)]
    for t in range(tiles):
        vy, vz = v.ends(y, t), v.ends(z, t)
        y_here = [roll_up(x) for x in vy]
        z_after = [roll_down(x) for x in v.ends(z, t + 1)]
        lat_a = lane_sum(vy, y_here, y_before, 0)
        lat_b = lane_sum(vz, z_here, z_after, LANES - 1)
        new = []
        for q, lat, halo in ((qa, lat_a, vz[1]), (qb, lat_b, vy[1])):
            cols = v.beside_columns(q, t, halo)
            total = [x + (l + c) for x, l, c in zip(load_s(q, t), lat, cols)]
            value = [x * i for x, i in zip(total, load_i(q, t))]
            new.append((q, value))
            if left is not None:
                load_d, rest = left
                rest.put(q, t, *[x - d * u for x, d, u in zip(total, load_d(q, t), value)])
        for q, value in new:
            v.put(q, t, *value)
        y_before, z_here = y_here, z_after
    for q, value in held:
        v.virtual[q][...] = value


def fine_residuals(v, load_s, load_d, whole_s, whole_d, rest, c0, c1):
    tiles = v.tiles
    rows = v.columns // 2

    def columns_summed(t):
        for pr, ref in ((0, c0), (1, c1)):
            outer = rest.part(pr, t, -1) + rest.part(pr, t, 2)
            inner = rest.part(pr, t, 0) + rest.part(pr, t, 1)
            ref[t] = outer + 3.0 * inner

    def full(t):
        x = [v.whole(q, t) for q in range(4)]
        lane = lane_ids(x[0].shape[0])

        def north(q):
            return jnp.where(lane == 0, roll_up(v.whole(q, before(t, tiles))), roll_up(x[q]))

        def south(q):
            return jnp.where(
                lane == LANES - 1, roll_down(v.whole(q, after(t, tiles))), roll_down(x[q])
            )

        beside = [
            (x[1] + north(1)) + (x[2] + col_prev(x[2])),
            (x[0] + south(0)) + (x[3] + col_prev(x[3])),
            (x[3] + north(3)) + (x[0] + col_next(x[0])),
            (x[2] + south(2)) + (x[1] + col_next(x[1])),
        ]
        r = [whole_s(q, t) - (whole_d(q, t) * x[q] - beside[q]) for q in range(4)]
        if t == tiles:
            c0[t] = ((col_prev(r[2]) + col_next(r[0])) + 3.0 * (r[0] + r[2]))[:rows]
            c1[t] = ((col_prev(r[3]) + col_next(r[1])) + 3.0 * (r[1] + r[3]))[:rows]
        else:
            for q in range(4):
                rest.put(q, t, r[q][:rows], r[q][rows:])
            columns_summed(t)

    full(0)
    up = [roll_up(x) for x in v.ends(1, 0)]
    down = [roll_down(x) for x in v.ends(2, 1)]
    for t in range(1, tiles - 1):
        x = [v.ends(q, t) for q in range(4)]
        up_here = [roll_up(part) for part in x[1]]
        down_next = [roll_down(part) for part in v.ends(2, t + 1)]
        for q, ns, near, edge, lane_at in (
            (0, 1, up_here, up, 0), (3, 2, down, down_next, LANES - 1)
        ):
            cols = v.beside_columns(q, t, x[q ^ 2][1])
            r = []
            for i, (s, d) in enumerate(zip(load_s(q, t), load_d(q, t))):
                lane = lane_ids(s.shape[0])
                beside = x[ns][i] + jnp.where(lane == lane_at, edge[i], near[i]) + cols[i]
                r.append(s - (d * x[q][i] - beside))
            rest.put(q, t, *r)
        columns_summed(t)
        up, down = up_here, down_next
    full(tiles - 1)
    full(tiles)


def fine_kernel(
    s_ref, d_ref, i_ref, d1_ref, i1_ref, d2_ref,
    from_other, from_mate, polar_ref, corner_near, corner_far,
    r_ref, s1_ref, d1_virtual, d2_virtual, s2_ref, to_mate, to_other,
    v_ref, hv, pv, hr, c0, c1, hs, hd, hi, ps, pd, pi, n1, temp,
    w0, w1, w2, w3, e0, e1, pi1, black_even, black_odd, red_even, red_odd,
    part1, part2,
):
    tiles, columns = s_ref.shape[1], s_ref.shape[2]
    rows = columns // 2
    sub = row_ids(8)
    odd = is_odd()

    def halo(t, _):
        fill_halo(t, from_mate, from_other, odd, False, hs, hd, hi)
        return 0

    loop(tiles, halo, 0, tiles)
    total = -16.0
    for q in range(4):
        own_s, own_d = polar_unpacked(polar_ref, q)
        near_s, near_d = polar_unpacked(corner_near, q)
        far_s, far_d = polar_unpacked(corner_far, q)
        left_s, right_s = chosen(odd, near_s, far_s)
        left_d, right_d = chosen(odd, near_d, far_d)
        total = total + own_d
        ps[q] = own_s
        pd[q] = own_d
        pi[q] = inverse_of(own_d)
        source = jnp.where(sub >= 5, left_s, jnp.where(sub <= 2, right_s, 0.0))
        diag = jnp.where(sub >= 5, left_d, jnp.where(sub <= 2, right_d, 4.0))
        hs[q, tiles] = source
        hd[q, tiles] = diag
        hi[q, tiles] = inverse_of(diag)

    def loaders(ref, halo, virtual):
        def split(q, t):
            return ref[q % 2, t, pl.ds(q // 2, rows, 2), :], halo[q, t]

        def whole(q, t):
            if t == tiles:
                return jnp.concatenate([virtual[q], halo[q, t]], 0)
            return jnp.concatenate(split(q, t), 0)

        return split, whole

    load_s, whole_s = loaders(s_ref, hs, ps)
    load_d, whole_d = loaders(d_ref, hd, pd)
    load_i, whole_i = loaders(i_ref, hi, pi)

    def held(own_ref, halo_ref):
        return Fine(
            [own_ref.at[p] for p in (0, 1)],
            [halo_ref.at[q] for q in range(4)],
            [pv.at[q] for q in range(4)],
            tiles,
            columns,
        )

    v, rest = held(v_ref, hv), held(r_ref, hr)
    for t in range(tiles):
        for q in (0, 3):
            v.put(q, t, *[x * i for x, i in zip(load_s(q, t), load_i(q, t))])
    for q in (1, 2):
        for t in (0, tiles - 1):
            v.put(q, t, jnp.zeros((rows, LANES), F32), jnp.zeros((8, LANES), F32))
        pv[q] = whole_s(q, tiles) * whole_i(q, tiles)
        pv[3 * (q - 1)] = jnp.zeros((rows + 8, LANES), F32)
    for red, left in ((False, None), (True, None), (False, (load_d, rest))):
        fine_sweep(v, load_s, load_i, whole_s, whole_i, red, left)
    fine_residuals(v, load_s, load_d, whole_s, whole_d, rest, c0, c1)

    def coarse(t, value):
        n1[t] = value

    restrict(c0, c1, tiles, rows, coarse, tiles)

    def use(c, source):
        for q in range(4):
            s1_ref[q, c] = source[q]

    tiles1 = tiles // 2
    split_tiles(lambda t: n1[t], tiles1, rows, splitter(), temp, use)
    out = moved(jnp.concatenate([n1[tiles], total], 0), virtual_splitter())
    source = quarters_of(out[:rows], temp.at[0])
    screen = quarters_of(out[rows:], temp.at[1])
    for q in range(4):
        s1_ref[q, tiles1] = source[q]
        d1_virtual[q] = 4.0 + screen[q]
        pi1[q] = inverse_of(4.0 + screen[q])
    d2_virtual[...] = 4.0 + ((screen[0] + screen[1]) + (screen[2] + screen[3]))

    def own(main, virtual):
        return lambda q, t: virtual[q] if isinstance(t, int) and t == tiles1 else main[q, t]

    w = [w0, w1, w2, w3]
    rows1 = rows // 2
    row = row_ids(rows1)
    load_s, load_d = own(s1_ref, s1_ref.at[:, tiles1]), own(d1_ref, d1_virtual)

    def after_sweep(sweep):
        if sweep == 0:
            for t in range(tiles1 + 1):
                even, odd_red = reds(t == tiles1)
                black_even[t] = w[even ^ 1][t]
                black_odd[t] = w[odd_red ^ 1][t]

    left = load_d, {1: part1, 2: part2}
    smooth(w, load_s, own(i1_ref, pi1), tiles1, 16, left, after_sweep)

    def valid(q, virtual):
        even, odd_red = reds(virtual)
        first = 1 if q == odd_red ^ 1 else 2
        last = rows1 - 2 if q == even ^ 1 else rows1 - 3
        return (row >= first) & (row <= last)

    def keep_red(t, r):
        even, odd_red = reds(isinstance(t, int) and t == tiles1)
        red_even[t] = r[even]
        red_odd[t] = r[odd_red]

    residuals(w, load_s, left, tiles1, e0, e1, keep_red, 16, valid)
    shared = {}

    def edges(t, partial):
        virtual = t == tiles1
        even, odd_red = reds(virtual)
        s2_ref[t] = partial
        packs = state_packs(
            [s1_ref[q, t] for q in range(4)],
            [load_d(q, t) for q in range(4)],
            [w[q][t] for q in range(4)],
            {even ^ 1: black_even[t], odd_red ^ 1: black_odd[t]},
            {even: red_even[t], odd_red: red_odd[t]},
            partial,
            d2_virtual[...] if virtual else d2_ref[t],
            virtual,
        )
        right, left = packs
        count = tiles1 + 1
        for i in (0, 1):
            to_mate[i * count + t], to_other[i * count + t] = chosen(odd, left[i], right[i])
        if t % 2 == 0:
            pair = chosen(odd, left[2], roll_rows(right[2], 4))
            shared[0] = pair
        else:
            pair = chosen(odd, roll_rows(left[2], 4), right[2])
            pair = [jnp.where(sub < 4, x, y) for x, y in zip(shared[0], pair)]
        if t % 2 == 1 or virtual:
            to_mate[2 * count + t // 2], to_other[2 * count + t // 2] = pair

    restrict(e0, e1, tiles1, rows1, edges, 16)


def merge_kernel(
    r_ref, s_ref, d_ref, i_ref, d_virtual, d2_ref, d2_virtual,
    out_ref, rim_s, rim_d, rim_i, inverse2,
    out_buf, sems,
):
    tiles = r_ref.shape[1]
    columns = out_ref.shape[0]
    matrix = merger()
    chunk = out_ref.shape[1] // GROUPS
    copies = []
    for group in range(GROUPS):
        for batch in range(tiles // GROUPS // BATCH):
            start = group * (tiles // GROUPS) + batch * BATCH
            own = slice(8, 8 + columns)
            both = [
                jnp.concatenate([r_ref[0, start + i, own], r_ref[1, start + i, own]], 1)
                for i in range(BATCH)
            ]
            out = moved(jnp.concatenate(both, 0), matrix)
            for i in range(BATCH):
                where = slice((start + i) * 256, (start + i + 1) * 256)
                out_buf[:, where] = out[columns * i : columns * (i + 1)]
        part = pl.ds(group * chunk, chunk)
        copy = pltpu.make_async_copy(out_buf.at[:, part], out_ref.at[:, part], sems.at[group])
        copy.start()
        copies.append(copy)

    sub = row_ids(8)
    tiles1, own = d_ref.shape[1], d_ref.shape[2]

    def rim(x):
        return jnp.where(sub < 4, x[:8], x[own - 8 :])

    for t in range(tiles1 + 1):
        for q in range(4):
            rim_s[q, t] = rim(s_ref[q, t])
            if t == tiles1:
                rim_d[q, t] = rim(d_virtual[q])
                rim_i[q, t] = inverse_of(rim(d_virtual[q]))
            else:
                rim_d[q, t] = rim(d_ref[q, t])
                rim_i[q, t] = rim(i_ref[q, t])
        inverse2[t] = inverse_of(d2_virtual[...] if t == tiles1 else d2_ref[t])
    for copy in copies:
        copy.wait()


def coarse_kernel(
    rim_s, rim_d, rim_i, inverse2, d2_ref, d2_virtual, s2_ref, from_other, from_mate,
    solution_ref, residual_ref,
    v0, v1, v2, v3, c0, c1, hs, hd, hi, part, fixes, rest1, rest2, s, d, inv, va, vb,
):
    v = [v0, v1, v2, v3]
    tiles, own = d2_ref.shape[:2]
    rows = own + 8
    count = tiles + 1
    sub = row_ids(8)
    odd_band = is_odd()
    for t in range(count):
        places = t, count + t, 2 * count + t // 2
        packs = [chosen(odd_band, from_mate[i], from_other[i]) for i in places]
        source = [jnp.zeros((8, LANES), F32)] * 4
        diag = [jnp.full((8, LANES), 4.0, F32)] * 4
        inverse = [jnp.zeros((8, LANES), F32)] * 4
        fixed = [jnp.zeros((8, LANES), F32)] * 4
        more = jnp.zeros((8, LANES), F32)
        total = jnp.ones((8, LANES), F32)
        for side, (a, ab, b, bb) in enumerate(sides(t == tiles)):
            near, far, step = (7, 6, -1) if side == 0 else (0, 1, 1)
            first = 6 if side == 0 else 0
            pack0, pack1, pack2 = (pair[side] for pair in packs)
            groups = [
                roll_rows(pack, first - 2 * g) for pack in (pack0, pack1) for g in range(4)
            ]
            pack2 = roll_rows(pack2, 4 * (t % 2) + (4 if side == 0 else 0))

            def put(group, q, at, x):
                group[q] = jnp.where(sub == at, x, group[q])

            for q in range(4):
                put(source, q, near, groups[q])
                put(diag, q, near, groups[4 + q])
            put(source, bb, far, groups[0])
            put(diag, bb, far, groups[1])
            put(fixed, bb, far, groups[2])
            put(fixed, b, far, groups[3])
            put(source, b, far, groups[4])
            put(diag, b, far, 0.0)
            put(source, a, far, groups[5])
            put(fixed, ab, near, pack2)
            more = jnp.where(sub == far, groups[6], more)
            more = jnp.where((sub == far + step) | (sub == far + 2 * step), pack2, more)
            total = jnp.where(sub == far, pack2, total)
            total = jnp.where(sub == far + step, roll_rows(groups[7], step), total)
            for q in range(4):
                known = (sub == near) | (sub == far) if q == bb else sub == near
                inverse[q] = jnp.where(known, inverse_of(diag[q]), inverse[q])
        for q in range(4):
            hs[q, t] = source[q]
            hd[q, t] = diag[q]
            hi[q, t] = inverse[q]
            fixes[q, t] = fixed[q]
        part[t] = more
        near_total = (diag[0] + diag[1]) + (diag[2] + diag[3]) - 12.0
        total = jnp.where((sub == 0) | (sub == 7), near_total, total)
        here = d2_virtual[...] if t == tiles else d2_ref[t]
        d[t] = jnp.concatenate([here, total], 0)
        inv[t] = jnp.concatenate([inverse2[t], inverse_of(total)], 0)
    def after_sweep(sweep):
        if sweep == 2:
            return
        for t in range(count):
            (a, ab, b, bb), (_, _, other_b, other_bb) = sides(t == tiles)
            todo = {}
            if sweep == 0:
                todo = {ab: (sub == 7) | (sub == 1), bb: (sub == 6) | (sub == 0)}
            else:
                todo = {b: sub == 6, other_b: sub == 1}
            for q, mask in todo.items():
                v[q][t, :8] = jnp.where(mask, fixes[q, t], v[q][t, :8])

    def of(halo, own_rows):
        return lambda q, t: jnp.concatenate([halo[q, t], own_rows[q, t]], 0)

    load_s = of(hs, rim_s)
    left = of(hd, rim_d), {1: rest1, 2: rest2}
    smooth(v, load_s, of(hi, rim_i), tiles, 16, left, after_sweep)
    row = row_ids(16)

    def valid(q, virtual):
        even, odd_red = reds(virtual)
        after_band = 0 if q == odd_red ^ 1 else 1
        before_band = 7 if q == even ^ 1 else 6
        first = 8 if q == odd_red ^ 1 else 9
        last = 15 if q == even ^ 1 else 14
        return (row <= after_band) | ((row >= before_band) & (row <= first)) | (row >= last)

    residuals(v, load_s, left, tiles, c0, c1, lambda t, r: None, 16, valid)

    lane, row = lane_ids(rows), row_ids(rows)
    even = (lane + row) % 2 == 0
    odd = jnp.logical_not(even)

    def start(t, value):
        ends = value[8:]
        source = jnp.concatenate(
            [
                s2_ref[t, :8] + jnp.where(sub < 4, ends, 0.0),
                s2_ref[t, own - 8 :] + jnp.where(sub >= 4, ends, 0.0),
                value[:8] + part[t],
            ],
            0,
        )
        s[t] = source
        virtual = isinstance(t, int) and t == tiles
        va[t] = jnp.where(odd if virtual else even, source * inv[t], 0.0)

    restrict(c0, c1, tiles, 16, start, 16)

    def scan(v, use):
        up, down = roll_up(v[tiles]), roll_down(v[0])
        for t in range(tiles + 1):
            x = v[t]
            up_here, down_next = roll_up(x), roll_down(v[after(t, tiles)])
            north = jnp.where(lane == 0, up, up_here)
            south = jnp.where(lane == LANES - 1, down_next, down)
            use(t, x, (col_prev(x) + col_next(x)) + (north + south))
            up, down = up_here, down_next

    for old, new, mask, other in ((va, vb, odd, even), (vb, va, even, odd), (va, vb, odd, even)):

        def relax(t, x, beside):
            update = other if t == tiles else mask
            new[t] = jnp.where(update, (s[t] + beside) * inv[t], x)

        scan(old, relax)

    def finish(t, x, beside):
        if t < tiles:
            where = slice(t * LANES, (t + 1) * LANES)
            solution_ref[:, where] = x[:own]
            residual_ref[:, where] = (s[t] - (d[t] * x - beside))[:own]

    scan(vb, finish)


VMEM = pl.BlockSpec(memory_space=pltpu.VMEM)
HBM = pl.BlockSpec(memory_space=pltpu.HBM)


def call(kernel, out_shapes, scratch, *args, sems=None, far_in=0, far_out=0):
    scratch = [pltpu.VMEM(x, F32) if isinstance(x, tuple) else x for x in scratch]
    if sems is not None:
        scratch.append(pltpu.SemaphoreType.DMA(sems))
    return pl.pallas_call(
        kernel,
        out_shape=[
            jax.ShapeDtypeStruct(x, F32) if isinstance(x, tuple) else x for x in out_shapes
        ],
        in_specs=[HBM] * far_in + [VMEM] * (len(args) - far_in),
        out_specs=[HBM] * far_out + [VMEM] * (len(out_shapes) - far_out),
        scratch_shapes=scratch,
        compiler_params=pltpu.CompilerParams(vmem_limit_bytes=40 * 2**20),
    )(*args)


def swapped_with(x, by):
    count = lax.axis_size("lon")
    pairs = [(i, (i + by) % count) for i in range(0, count, 2)]
    return lax.ppermute(x, "lon", pairs + [(b, a) for a, b in pairs])


def swapped_edges(to_mate, to_other):
    from_mate = swapped_with(to_mate, 1)
    return from_mate, swapped_with(to_other, -1)


def body(right_side, texel_weight, seam_flags):
    columns, height = right_side.shape
    half_turn = lax.axis_size("lon") // 2
    tiles, rows = height // 256, columns // 2
    tiles1, rows1 = tiles // 2, rows // 2
    temp = (BATCH, 2, columns, LANES)
    natural = (2, tiles, columns, LANES)
    padded = (2, tiles, columns + 16, LANES)
    quarters1 = (4, tiles1, rows1, LANES)
    split = (4, 2, 4 * tiles, LANES)
    right_here, weight_here, scales, to_mate, to_other, corner = call(
        edge_kernel,
        [(columns, height), jax.ShapeDtypeStruct((columns, height), BF16)]
        + [(tiles, 8, LANES), (2, tiles, 8, LANES), (2, tiles, 8, LANES), (2, 8, LANES)],
        [pltpu.VMEM(seam_flags.shape, jnp.int32), split, split],
        *[
            pltpu.with_memory_space_constraint(x, pltpu.HBM)
            for x in (right_side, texel_weight, seam_flags)
        ],
        sems=(7,), far_in=3,
    )
    from_mate, from_other = swapped_edges(to_mate, to_other)
    corner_far = swapped_with(corner, half_turn - 1)
    corner_near = swapped_with(corner, half_turn + 1)
    ends = (2, 2, columns, LANES)
    (polar_own,) = call(
        polar_kernel, [(2, rows, LANES)], [ends, ends],
        right_here, weight_here, scales, corner,
    )
    polar = lax.ppermute(
        polar_own, "lon", [(i, (i + half_turn) % (2 * half_turn)) for i in range(2 * half_turn)]
    )
    s, d, inverse, d1, i1, d2 = call(
        bulk_kernel,
        [natural] * 3 + [quarters1, quarters1, quarters1[1:]],
        [(BATCH, columns, LANES), (tiles, rows, LANES), (BATCH, 2, rows, LANES)],
        right_here, weight_here, scales, polar_own,
    )

    def level_scratch(tiles, rows):
        return [(tiles + 1, rows, LANES)] * 6

    def halo_scratch(tiles):
        return [(4, tiles + 1, 8, LANES)] * 3

    pack1 = (2 * (tiles1 + 1) + tiles1 // 2 + 1, 8, LANES)
    r, s1, d1_virtual, d2_virtual, s2_own, to_mate, to_other = call(
        fine_kernel,
        [padded, (4, tiles1 + 1, rows1, LANES), (4, rows1, LANES), (rows1, LANES)]
        + [(tiles1 + 1, rows1, LANES), pack1, pack1],
        [padded, (4, tiles, 8, LANES), (4, rows + 8, LANES), (4, tiles, 8, LANES)]
        + [(tiles + 1, rows, LANES)] * 2
        + halo_scratch(tiles)
        + [(4, rows, LANES)] * 3
        + [(tiles + 1, rows, LANES), (BATCH, 2, rows, LANES)]
        + level_scratch(tiles1, rows1)
        + [(4, rows1, LANES)]
        + [(tiles1 + 1, rows1, LANES)] * 4
        + [(tiles1, rows1, LANES)] * 2,
        s, d, inverse, d1, i1, d2, from_other, from_mate, polar, corner_near, corner_far,
    )
    from_mate, from_other = swapped_edges(to_mate, to_other)
    rim = (4, tiles1 + 1, 8, LANES)
    fine_residual, rim_s, rim_d, rim_i, inverse2 = call(
        merge_kernel,
        [(columns, height), rim, rim, rim, (tiles1 + 1, rows1, LANES)],
        [(columns, height)],
        r, s1, d1, i1, d1_virtual, d2, d2_virtual,
        sems=(GROUPS,), far_out=1,
    )
    wide = (tiles1 + 1, rows1 + 8, LANES)
    solution_2, residual_2 = call(
        coarse_kernel,
        [(columns // 4, height // 4)] * 2,
        level_scratch(tiles1, 16)
        + [(4, tiles1 + 1, 8, LANES)] * 3
        + [(tiles1 + 1, 8, LANES), (4, tiles1 + 1, 8, LANES)]
        + [(tiles1, 16, LANES)] * 2
        + [wide] * 5,
        rim_s, rim_d, rim_i, inverse2, d2, d2_virtual, s2_own, from_other, from_mate,
    )
    return fine_residual, solution_2, residual_2


def solution(mesh):
    spec = P(("groups", "lon"), None)
    return jax.shard_map(
        body, mesh=mesh, in_specs=(spec,) * 3, out_specs=(spec,) * 3, check_vma=False
    )
```

```python
import jax
import jax.numpy as jnp
from jax import lax
from jax.experimental import pallas as pl
from jax.experimental.pallas import tpu as pltpu
from jax.sharding import PartitionSpec as P

TILE = 32
SEAM_SCALE = 0.1
LANES = 128
GROUPS = 4
BATCH = 4
F32 = jnp.float32
BF16 = jnp.bfloat16


def loop(count, body, carry=0, unroll=4):
    unroll = min(unroll, count)

    def steps(block, carry):
        for i in range(unroll):
            carry = body(block * unroll + i, carry)
        return carry

    whole = count // unroll
    carry = steps(0, carry) if whole == 1 else lax.fori_loop(0, whole, steps, carry)
    for t in range(whole * unroll, count):
        carry = body(t, carry)
    return carry


def before(t, tiles):
    return (tiles if t == 0 else t - 1) if isinstance(t, int) else jnp.where(t == 0, tiles, t - 1)


def after(t, tiles):
    return (0 if t == tiles else t + 1) if isinstance(t, int) else t + 1


def lane_ids(rows):
    return lax.broadcasted_iota(jnp.int32, (rows, LANES), 1)


def row_ids(rows):
    return lax.broadcasted_iota(jnp.int32, (rows, LANES), 0)


def roll_up(x):
    return pltpu.roll(x, 1, 1)


def roll_down(x):
    return pltpu.roll(x, LANES - 1, 1)


def roll_rows(x, by):
    by %= x.shape[0]
    return x if by == 0 else pltpu.roll(x, by, 0)


def roll_lanes(x, by):
    by %= LANES
    return x if by == 0 else pltpu.roll(x, by, 1)


def col_prev(x):
    return pltpu.roll(x, 1, 0)


def col_next(x):
    return pltpu.roll(x, x.shape[0] - 1, 0)


def inverse_of(x):
    return 1.0 / x


def selector(shape, rule):
    a = lax.broadcasted_iota(jnp.int32, shape, 0)
    b = lax.broadcasted_iota(jnp.int32, shape, 1)
    return jnp.where(rule(a, b), 1.0, 0.0).astype(BF16)


def splitter():
    return selector((256, 256), lambda a, b: a == 2 * (b % LANES) + b // LANES)


def merger():
    return selector((256, 256), lambda a, b: b == 2 * (a % LANES) + a // LANES)


def virtual_splitter():
    return selector(
        (LANES, 256),
        lambda a, b: a // 2 + jnp.where(a >= 64, 64, 0) + LANES * (a % 2) == b,
    )


def moved(x, matrix, exact=None):
    rows = x.shape[0]
    high = x.astype(BF16)
    low = (x - high.astype(F32)).astype(BF16)
    terms = [high, low] if exact is None else [high, low, exact]
    out = jnp.dot(jnp.concatenate(terms, 0), matrix, preferred_element_type=F32)
    both = out[:rows] + out[rows : 2 * rows]
    return both if exact is None else (both, out[2 * rows :])


def quarters_of(parts, temp):
    count = parts.shape[0] // 2
    temp[0] = parts[:, :LANES]
    temp[1] = parts[:, LANES:]
    return [temp[pr, pl.ds(pc, count, 2), :] for pc in (0, 1) for pr in (0, 1)]


def reds(swapped):
    return (1, 2) if swapped else (0, 3)


def interleaved(group, offset):
    sub = row_ids(8)
    packed = roll_rows(group[0], offset)
    for q in range(1, 4):
        packed = jnp.where(sub // 2 == q, roll_rows(group[q], 2 * q + offset), packed)
    return packed


def edge_packs(source, diag, swapped):
    sub = row_ids(8)
    even, odd = reds(swapped)
    rows = source[0].shape[0]
    packs = []
    for here, first, second, row, step in (
        (slice(rows - 8, rows), even, odd, 6, 1),
        (slice(0, 8), odd, even, 1, -1),
    ):
        gs = [x[here] for x in source]
        gd = [x[here] for x in diag]
        near = gs[first] * inverse_of(gd[first])
        far = roll_rows(gs[second] * inverse_of(gd[second]), step)
        gs[first] = jnp.where(sub == row, near, gs[first])
        gd[first] = jnp.where(sub == row, far, gd[first])
        offset = 2 if row == 6 else 0
        packs.append((interleaved(gs, offset), interleaved(gd, offset)))
    return packs


def unpacked_halo(left, right, swapped):
    sub = row_ids(8)
    even, odd = reds(swapped)
    (al, bl), (ar, br) = left, right
    source, diag = [], []
    for q in range(4):
        s = jnp.where(
            sub >= 6,
            roll_rows(al, 6 - 2 * q),
            jnp.where(sub <= 1, roll_rows(ar, -2 * q), 0.0),
        )
        d = jnp.where(
            sub >= 6,
            roll_rows(bl, 6 - 2 * q),
            jnp.where(sub <= 1, roll_rows(br, -2 * q), 4.0),
        )
        if q == even:
            s = jnp.where(sub == 2, roll_rows(br, 1 - 2 * odd), s)
            d = jnp.where((sub == 2) | (sub == 6), 1.0, d)
        if q == odd:
            s = jnp.where(sub == 5, roll_rows(bl, 5 - 2 * even), s)
            d = jnp.where((sub == 5) | (sub == 1), 1.0, d)
        source.append(s)
        diag.append(d)
    return source, diag


def is_odd():
    return lax.rem(lax.axis_index("lon"), 2) == 1


def chosen(odd, a, b):
    return jnp.where(odd, a, b), jnp.where(odd, b, a)


def store_edges(t, packs, odd, to_mate, to_other):
    right, left = packs
    for i in (0, 1):
        to_mate[i, t], to_other[i, t] = chosen(odd, left[i], right[i])


def sides(swapped):
    even, odd = reds(swapped)
    return (even, even ^ 1, odd, odd ^ 1), (odd, odd ^ 1, even, even ^ 1)


def paired(groups, shift):
    sub = row_ids(8)
    packed = roll_rows(groups[0], shift)
    for g in (1, 2, 3):
        packed = jnp.where(sub // 2 == g, roll_rows(groups[g], 2 * g + shift), packed)
    return packed


def state_packs(source, diag, last, first_black, residual, partial, diag2, swapped):
    sub = row_ids(8)
    rows = source[0].shape[0]
    packs = []
    for (a, ab, b, bb), here, near, far, step in zip(
        sides(swapped), (slice(rows - 8, rows), slice(0, 8)), (7, 0), (6, 1), (-1, 1)
    ):
        s, d, v = ([x[here] for x in group] for group in (source, diag, last))
        part, d2 = partial[here], diag2[here]
        beside = [
            s[bb] + v[a],
            d[bb],
            first_black[bb][here],
            v[b],
            s[b] - d[b] * v[b] + v[ab],
            residual[a][here] - v[bb],
            part,
            roll_rows(d2, -step),
        ]
        groups = [jnp.where(sub == far, y, x) for x, y in zip(s + d, beside)]
        shift = 2 if near == 7 else 0
        more = jnp.where(sub == far, d2, first_black[ab][here])
        more = jnp.where(sub == far + step, part, more)
        more = jnp.where(sub == far + 2 * step, part * inverse_of(d2), more)
        packs.append((paired(groups[:4], shift), paired(groups[4:], shift), more))
    return packs


def fill_halo(t, from_mate, from_other, odd, swapped, hs, hd, hi):
    al, ar = chosen(odd, from_mate[0, t], from_other[0, t])
    bl, br = chosen(odd, from_mate[1, t], from_other[1, t])
    source, diag = unpacked_halo((al, bl), (ar, br), swapped)
    for q in range(4):
        hs[q, t] = source[q]
        hd[q, t] = diag[q]
        hi[q, t] = inverse_of(diag[q])


def loader(own, halo, virtual, tiles):
    def load(q, t):
        if isinstance(t, int) and t == tiles:
            return jnp.concatenate([virtual[q], halo[q, t]], 0)
        return jnp.concatenate([own[q, t], halo[q, t]], 0)

    return load


def polar_packs(tiles_of):
    lane = lane_ids(tiles_of[0][0].shape[0])
    packs = []
    for pc in (0, 1):
        parts = [*tiles_of[2 * pc], *tiles_of[2 * pc + 1]]
        packed = parts[0]
        for m in range(1, 4):
            mine = (lane + (16 - 32 * m) % LANES) % LANES < 32
            packed = jnp.where(mine, roll_lanes(parts[m], 32 * m), packed)
        packs.append(packed)
    return packs


def polar_unpacked(x, q):
    lane = lane_ids(x.shape[1])
    used = (lane < 16) | (lane >= LANES - 16)
    m = 2 * (q % 2)
    return (
        jnp.where(used, roll_lanes(x[q // 2], 32 * m), 0.0),
        jnp.where(used, roll_lanes(x[q // 2], 32 * (m + 1)), 4.0),
    )


def seam_scales(flags, chunks):
    flag_cols, flag_lats = flags.shape
    flags = jnp.concatenate(
        [flags.astype(F32), jnp.zeros((8 - flag_cols, flag_lats), F32)], 0
    )
    lat = lax.broadcasted_iota(jnp.int32, (8, flag_lats), 1)
    stacked = jnp.concatenate([jnp.where(lat // 8 == c, flags, 0.0) for c in chunks], 0)
    spread = selector((flag_lats, LANES), lambda a, b: a % 8 == b // (TILE // 2))
    spread_flags = jnp.dot(stacked.astype(BF16), spread, preferred_element_type=F32)
    scale = jnp.where(spread_flags > 0.5, SEAM_SCALE, 1.0)
    return scale.reshape(len(chunks), 8, LANES)


def seam_rows(scales, flag_cols, rows):
    size = (rows // flag_cols, LANES)
    return jnp.concatenate(
        [jnp.broadcast_to(scales[i : i + 1], size) for i in range(flag_cols)], 0
    )


def edge_kernel(
    right_ref, weight_ref, flag_ref,
    right_here, weight_here, scale_ref, to_mate, to_other, corner_ref,
    flags, temp_s, temp_w, sems,
):
    columns, height = right_ref.shape
    tiles = height // 256
    pairs = [(flag_ref, flags)]
    inputs = (right_ref, right_here, 8), (weight_ref, weight_here, 16)
    for src, dst, size in inputs:
        for start in (0, columns - size):
            part = pl.ds(start, size)
            pairs.append((src.at[part], dst.at[part]))
    for src, dst, size in inputs:
        part = pl.ds(size, columns - 2 * size)
        pairs.append((src.at[part], dst.at[part]))
    copies = [
        pltpu.make_async_copy(src, dst, sems.at[i]) for i, (src, dst) in enumerate(pairs)
    ]
    for copy in copies:
        copy.start()
    odd = is_odd()
    matrix = splitter()
    flag_cols = flag_ref.shape[0]
    copies[0].wait()
    scale_ref[...] = seam_scales(flags[...], range(tiles))
    for copy in copies[1:5]:
        copy.wait()
    sub = row_ids(8)
    def ends(size):
        return slice(0, size), slice(columns - size, columns)

    count = tiles // 4
    found = []
    for batch in range(4):
        chunks = range(batch * count, (batch + 1) * count)
        lanes = [slice(c * 256, (c + 1) * 256) for c in chunks]
        source, weight = moved(
            jnp.concatenate([right_here[at, w] for w in lanes for at in ends(8)], 0),
            matrix,
            jnp.concatenate([weight_here[at, w] for w in lanes for at in ends(16)], 0),
        )
        weight = weight.reshape(count, 32, 256)
        weight = jnp.concatenate([weight[:, :8], weight[:, 24:]], 1).reshape(count * 16, 256)
        source = quarters_of(source, temp_s.at[batch])
        weight = quarters_of(weight, temp_w.at[batch])
        for i, c in enumerate(chunks):
            here = slice(i * 8, (i + 1) * 8)
            scales = scale_ref[c]
            scale = jnp.where(sub < 4, scales[:1], scales[flag_cols - 1 : flag_cols])
            pair = [x[here] for x in source], [4.0 + w[here] * scale for w in weight]
            store_edges(c, edge_packs(*pair, False), odd, to_mate, to_other)
            if c in (0, tiles - 1):
                found.append(pair)
    both = mirrored_ends(*found)
    for pc in (0, 1):
        corner_ref[pc] = both[8 * pc : 8 * (pc + 1)]
    for copy in copies[5:]:
        copy.wait()


def mirrored_ends(first, last):
    mirror = selector((LANES, LANES), lambda a, b: a + b == LANES - 1)
    lane = lane_ids(first[0][0].shape[0])
    ends = [
        [jnp.where(lane >= 64, last[i][q ^ 1], first[i][q ^ 1]) for i in (0, 1)]
        for q in range(4)
    ]
    return moved(jnp.concatenate(polar_packs(ends), 0), mirror)


def polar_kernel(right_ref, weight_ref, scale_ref, edges_first, polar_ref, temp_s, temp_w):
    columns, height = right_ref.shape
    rows, tiles = columns // 2, height // 256
    flag_cols = columns // TILE
    lanes = slice(0, 256), slice(height - 256, height)
    source, weight = moved(
        jnp.concatenate([right_ref[:, w] for w in lanes], 0),
        splitter(),
        jnp.concatenate([weight_ref[:, w] for w in lanes], 0),
    )
    found = []
    for end in (0, 1):
        here = slice(end * columns, (end + 1) * columns)
        scale = seam_rows(scale_ref[end * (tiles - 1)], flag_cols, rows)
        found.append(
            (
                quarters_of(source[here], temp_s.at[end]),
                [4.0 + w * scale for w in quarters_of(weight[here], temp_w.at[end])],
            )
        )
    both = mirrored_ends(*found)
    for pc in (0, 1):
        polar_ref[pc] = both[pc * rows : (pc + 1) * rows]


def bulk_kernel(
    right_ref, weight_ref, scale_ref, polar_first,
    s_ref, d_ref, i_ref, d1_ref, i1_ref, d2_ref,
    temp, e_ref, split_temp,
):
    tiles, columns = s_ref.shape[1], s_ref.shape[2]
    rows = columns // 2
    matrix = splitter()
    for start in range(0, tiles, BATCH):
        lanes = [slice((start + i) * 256, (start + i + 1) * 256) for i in range(BATCH)]
        source, weight = moved(
            jnp.concatenate([right_ref[:, w] for w in lanes], 0),
            matrix,
            jnp.concatenate([weight_ref[:, w] for w in lanes], 0),
        )
        for i in range(BATCH):
            c = start + i
            here = slice(i * columns, (i + 1) * columns)
            scale = seam_rows(scale_ref[c], columns // TILE, columns)
            screens = []
            for pr in (0, 1):
                half = slice(pr * LANES, (pr + 1) * LANES)
                screen = weight[here, half] * scale
                diag = 4.0 + screen
                s_ref[pr, c] = source[here, half]
                d_ref[pr, c] = diag
                i_ref[pr, c] = 1.0 / diag
                screens.append(screen)
            temp[i] = screens[0] + screens[1]
            e_ref[c] = temp[i, pl.ds(0, rows, 2), :] + temp[i, pl.ds(1, rows, 2), :]

    def use(c, screen):
        for q in range(4):
            d1_ref[q, c] = 4.0 + screen[q]
            i1_ref[q, c] = inverse_of(4.0 + screen[q])
        d2_ref[c] = 4.0 + ((screen[0] + screen[1]) + (screen[2] + screen[3]))

    split_tiles(lambda t: e_ref[t], tiles // 2, rows, matrix, split_temp, use)


def split_tiles(load, tiles, rows, matrix, temp, use):
    for start in range(0, tiles, BATCH):
        wide = [
            jnp.concatenate([load(2 * c), load(2 * c + 1)], 1)
            for c in range(start, start + BATCH)
        ]
        out = moved(jnp.concatenate(wide, 0), matrix)
        for i in range(BATCH):
            use(start + i, quarters_of(out[i * rows : (i + 1) * rows], temp.at[i, :, :rows]))


def half_sweep(v, load_s, load_i, tiles, red, unroll, left=None):
    rows = v[0].shape[1]
    lane = lane_ids(rows)
    y, z, qa, qb = (1, 2, 0, 3) if red else (3, 0, 2, 1)
    col_a, col_b = (col_prev, col_next) if red else (col_next, col_prev)

    def beside_virtual(q):
        ns, we = q ^ 1, q ^ 2
        here = v[ns][tiles]
        if q % 2 == 0:
            lat = jnp.where(lane == 0, roll_up(v[ns][tiles - 1]), roll_up(here))
        else:
            lat = jnp.where(lane == LANES - 1, roll_down(v[ns][0]), roll_down(here))
        cols = v[we][tiles]
        return (here + lat) + (cols + (col_prev if q < 2 else col_next)(cols))

    held = [
        (q, (load_s(q, tiles) + beside_virtual(q)) * load_i(q, tiles)) for q in (y, z)
    ]

    def body(t, carry):
        y_before, z_here = carry
        vy, vz = v[y][t], v[z][t]
        y_here = roll_up(vy)
        z_after = roll_down(v[z][t + 1])
        lat_a = vy + jnp.where(lane == 0, y_before, y_here)
        lat_b = vz + jnp.where(lane == LANES - 1, z_after, z_here)
        all_a = load_s(qa, t) + (lat_a + (vz + col_a(vz)))
        all_b = load_s(qb, t) + (lat_b + (vy + col_b(vy)))
        new_a, new_b = all_a * load_i(qa, t), all_b * load_i(qb, t)
        v[qa][t], v[qb][t] = new_a, new_b
        if left is not None:
            load_d, rest = left
            rest[qa][t] = all_a - load_d(qa, t) * new_a
            rest[qb][t] = all_b - load_d(qb, t) * new_b
        return y_here, z_after

    loop(tiles, body, (roll_up(v[y][tiles]), roll_down(v[z][0])), unroll)
    for q, value in held:
        v[q][tiles] = value


def smooth(v, load_s, load_i, tiles, unroll, left, after_sweep=None):
    zeros = jnp.zeros(v[0].shape[1:], F32)

    def first(t, _):
        for q in (0, 3):
            v[q][t] = load_s(q, t) * load_i(q, t)
        return 0

    loop(tiles, first, 0, unroll)
    for q in (1, 2):
        v[q][0] = zeros
        v[q][tiles - 1] = zeros
        v[q][tiles] = load_s(q, tiles) * load_i(q, tiles)
        v[3 * (q - 1)][tiles] = zeros
    for sweep, red in enumerate((False, True, False)):
        half_sweep(v, load_s, load_i, tiles, red, unroll, left if sweep == 2 else None)
        if after_sweep is not None:
            after_sweep(sweep)


def residuals(v, load_s, left, tiles, c0, c1, keep, unroll, valid=None):
    lane = lane_ids(v[0].shape[1])
    load_d, rest = left

    def use(t, r):
        keep(t, r)
        if valid is not None:
            virtual = isinstance(t, int) and t == tiles
            r = [jnp.where(valid(q, virtual), r[q], 0.0) for q in range(4)]
        c0[t] = (col_prev(r[2]) + col_next(r[0])) + 3.0 * (r[0] + r[2])
        c1[t] = (col_prev(r[3]) + col_next(r[1])) + 3.0 * (r[1] + r[3])

    def north(q, t):
        return jnp.where(lane == 0, roll_up(v[q][before(t, tiles)]), roll_up(v[q][t]))

    def south(q, t):
        return jnp.where(
            lane == LANES - 1, roll_down(v[q][after(t, tiles)]), roll_down(v[q][t])
        )

    def full(t):
        x = [v[q][t] for q in range(4)]
        beside = [
            (x[1] + north(1, t)) + (x[2] + col_prev(x[2])),
            (x[0] + south(0, t)) + (x[3] + col_prev(x[3])),
            (x[3] + north(3, t)) + (x[0] + col_next(x[0])),
            (x[2] + south(2, t)) + (x[1] + col_next(x[1])),
        ]
        use(t, [load_s(q, t) - (load_d(q, t) * x[q] - beside[q]) for q in range(4)])

    def body(i, carry):
        t = i + 1
        up, down = carry
        x = [v[q][t] for q in range(4)]
        up_here, down_next = roll_up(x[1]), roll_down(v[2][t + 1])
        beside0 = (x[1] + jnp.where(lane == 0, up, up_here)) + (x[2] + col_prev(x[2]))
        beside3 = (x[2] + jnp.where(lane == LANES - 1, down_next, down)) + (
            x[1] + col_next(x[1])
        )
        r0 = load_s(0, t) - (load_d(0, t) * x[0] - beside0)
        r3 = load_s(3, t) - (load_d(3, t) * x[3] - beside3)
        use(t, [r0, rest[1][t], rest[2][t], r3])
        return up_here, down_next

    full(0)
    loop(tiles - 2, body, (roll_up(v[1][0]), roll_down(v[2][1])), unroll)
    full(tiles - 1)
    full(tiles)


def restrict(c0, c1, tiles, rows, use, unroll):
    lane = lane_ids(rows)

    def body(t, carry):
        up, down = carry
        here, other = c0[t, :rows], c1[t, :rows]
        up_here = roll_up(other)
        down_next = roll_down(c0[after(t, tiles), :rows])
        north = jnp.where(lane == 0, up, up_here)
        south = jnp.where(lane == LANES - 1, down_next, down)
        use(t, ((north + south) + 3.0 * (here + other)) * (1.0 / 16.0))
        return up_here, down_next

    start = roll_up(c1[tiles, :rows]), roll_down(c0[0, :rows])
    body(tiles, loop(tiles, body, start, unroll))


class Fine:
    def __init__(self, own, halo, virtual, tiles, columns):
        self.own, self.halo, self.virtual = own, halo, virtual
        self.tiles, self.columns = tiles, columns

    def part(self, parity, t, start):
        return self.own[parity][t, pl.ds(8 + start, self.columns // 2, 2), :]

    def rows(self, q, t):
        return self.part(q % 2, t, q // 2)

    def whole(self, q, t):
        if t == self.tiles:
            return self.virtual[q][...]
        return jnp.concatenate([self.rows(q, t), self.halo[q][t]], 0)

    def ends(self, q, t):
        if t == self.tiles:
            whole = self.virtual[q][...]
            return whole[: self.columns // 2], whole[self.columns // 2 :]
        return self.rows(q, t), self.halo[q][t]

    def line(self, parity, t, column):
        row = self.own[parity][t, 8 + column : 9 + column]
        return jnp.broadcast_to(row, (8, LANES))

    def put(self, q, t, own, halo):
        pr, pc = q % 2, q // 2
        self.own[pr][t, pl.ds(8 + pc, self.columns // 2, 2), :] = own
        self.halo[q][t] = halo
        if pc == 1:
            self.own[pr][t, 7:8] = halo[7:8]
        else:
            at = 8 + self.columns
            self.own[pr][t, at : at + 1] = halo[0:1]

    def beside_columns(self, q, t, near):
        sub = row_ids(8)
        pr, pc = q % 2, q // 2
        rows, halo = near
        own = rows + self.part(pr, t, 2 if pc else -1)
        if pc == 0:
            other = jnp.where(sub == 0, self.line(pr, t, self.columns - 1), col_prev(halo))
        else:
            other = jnp.where(sub == 7, self.line(pr, t, 0), col_next(halo))
        return own, halo + other


def fine_sweep(v, load_s, load_i, whole_s, whole_i, red, left):
    tiles = v.tiles
    y, z, qa, qb = (1, 2, 0, 3) if red else (3, 0, 2, 1)

    def lane_sum(parts, rolled, edge, lane_at):
        return [
            x + jnp.where(lane_ids(x.shape[0]) == lane_at, e, r)
            for x, r, e in zip(parts, rolled, edge)
        ]

    def beside_virtual(q):
        here, cols = v.whole(q ^ 1, tiles), v.whole(q ^ 2, tiles)
        lane = lane_ids(here.shape[0])
        if q % 2 == 0:
            lat = jnp.where(lane == 0, roll_up(v.whole(q ^ 1, tiles - 1)), roll_up(here))
        else:
            lat = jnp.where(lane == LANES - 1, roll_down(v.whole(q ^ 1, 0)), roll_down(here))
        return (here + lat) + (cols + (col_prev if q < 2 else col_next)(cols))

    held = [
        (q, (whole_s(q, tiles) + beside_virtual(q)) * whole_i(q, tiles)) for q in (y, z)
    ]
    y_before = [roll_up(x) for x in v.ends(y, tiles)]
    vz = v.ends(z, 0)
    z_here = [roll_down(x) for x in vz]
    for t in range(tiles):
        vy, z_next = v.ends(y, t), v.ends(z, t + 1)
        y_here = [roll_up(x) for x in vy]
        z_after = [roll_down(x) for x in z_next]
        lat_a = lane_sum(vy, y_here, y_before, 0)
        lat_b = lane_sum(vz, z_here, z_after, LANES - 1)
        new = []
        for q, lat, near in ((qa, lat_a, vz), (qb, lat_b, vy)):
            cols = v.beside_columns(q, t, near)
            total = [x + (l + c) for x, l, c in zip(load_s(q, t), lat, cols)]
            value = [x * i for x, i in zip(total, load_i(q, t))]
            new.append((q, value))
            if left is not None and 0 < t < tiles - 1:
                load_d, rest = left
                rest.put(q, t, *[x - d * u for x, d, u in zip(total, load_d(q, t), value)])
        for q, value in new:
            v.put(q, t, *value)
        y_before, z_here, vz = y_here, z_after, z_next
    for q, value in held:
        v.virtual[q][...] = value


def fine_residuals(v, load_s, load_d, whole_s, whole_d, rest, c0, c1):
    tiles = v.tiles
    rows = v.columns // 2

    def columns_summed(t):
        for pr, ref in ((0, c0), (1, c1)):
            outer = rest.part(pr, t, -1) + rest.part(pr, t, 2)
            inner = rest.part(pr, t, 0) + rest.part(pr, t, 1)
            ref[t] = outer + 3.0 * inner

    def full(t):
        x = [v.whole(q, t) for q in range(4)]
        lane = lane_ids(x[0].shape[0])

        def north(q):
            return jnp.where(lane == 0, roll_up(v.whole(q, before(t, tiles))), roll_up(x[q]))

        def south(q):
            return jnp.where(
                lane == LANES - 1, roll_down(v.whole(q, after(t, tiles))), roll_down(x[q])
            )

        beside = [
            (x[1] + north(1)) + (x[2] + col_prev(x[2])),
            (x[0] + south(0)) + (x[3] + col_prev(x[3])),
            (x[3] + north(3)) + (x[0] + col_next(x[0])),
            (x[2] + south(2)) + (x[1] + col_next(x[1])),
        ]
        r = [whole_s(q, t) - (whole_d(q, t) * x[q] - beside[q]) for q in range(4)]
        if t == tiles:
            c0[t] = ((col_prev(r[2]) + col_next(r[0])) + 3.0 * (r[0] + r[2]))[:rows]
            c1[t] = ((col_prev(r[3]) + col_next(r[1])) + 3.0 * (r[1] + r[3]))[:rows]
        else:
            for q in range(4):
                rest.put(q, t, r[q][:rows], r[q][rows:])
            columns_summed(t)

    full(0)
    up = [roll_up(x) for x in v.ends(1, 0)]
    x2 = v.ends(2, 1)
    down = [roll_down(x) for x in x2]
    for t in range(1, tiles - 1):
        x = [v.ends(0, t), v.ends(1, t), x2, v.ends(3, t)]
        x2 = v.ends(2, t + 1)
        up_here = [roll_up(part) for part in x[1]]
        down_next = [roll_down(part) for part in x2]
        for q, ns, near, edge, lane_at in (
            (0, 1, up_here, up, 0), (3, 2, down, down_next, LANES - 1)
        ):
            cols = v.beside_columns(q, t, x[q ^ 2])
            r = []
            for i, (s, d) in enumerate(zip(load_s(q, t), load_d(q, t))):
                lane = lane_ids(s.shape[0])
                beside = x[ns][i] + jnp.where(lane == lane_at, edge[i], near[i]) + cols[i]
                r.append(s - (d * x[q][i] - beside))
            rest.put(q, t, *r)
        columns_summed(t)
        up, down = up_here, down_next
    full(tiles - 1)
    full(tiles)


def fine_kernel(
    s_ref, d_ref, i_ref, d1_ref, i1_ref, d2_ref,
    from_other, from_mate, polar_ref, corner_near, corner_far,
    r_ref, s1_ref, d1_virtual, d2_virtual, s2_ref, to_mate, to_other,
    v_ref, hv, pv, hr, c0, c1, hs, hd, hi, ps, pd, pi, n1, temp,
    w0, w1, w2, w3, e0, e1, pi1, black_even, black_odd, red_even, red_odd,
    part1, part2,
):
    tiles, columns = s_ref.shape[1], s_ref.shape[2]
    rows = columns // 2
    sub = row_ids(8)
    odd = is_odd()

    def halo(t, _):
        fill_halo(t, from_mate, from_other, odd, False, hs, hd, hi)
        return 0

    loop(tiles, halo, 0, tiles)
    total = -16.0
    for q in range(4):
        own_s, own_d = polar_unpacked(polar_ref, q)
        near_s, near_d = polar_unpacked(corner_near, q)
        far_s, far_d = polar_unpacked(corner_far, q)
        left_s, right_s = chosen(odd, near_s, far_s)
        left_d, right_d = chosen(odd, near_d, far_d)
        total = total + own_d
        ps[q] = own_s
        pd[q] = own_d
        pi[q] = inverse_of(own_d)
        source = jnp.where(sub >= 5, left_s, jnp.where(sub <= 2, right_s, 0.0))
        diag = jnp.where(sub >= 5, left_d, jnp.where(sub <= 2, right_d, 4.0))
        hs[q, tiles] = source
        hd[q, tiles] = diag
        hi[q, tiles] = inverse_of(diag)

    def loaders(ref, halo, virtual):
        def split(q, t):
            return ref[q % 2, t, pl.ds(q // 2, rows, 2), :], halo[q, t]

        def whole(q, t):
            if t == tiles:
                return jnp.concatenate([virtual[q], halo[q, t]], 0)
            return jnp.concatenate(split(q, t), 0)

        return split, whole

    load_s, whole_s = loaders(s_ref, hs, ps)
    load_d, whole_d = loaders(d_ref, hd, pd)
    load_i, whole_i = loaders(i_ref, hi, pi)

    def held(own_ref, halo_ref):
        return Fine(
            [own_ref.at[p] for p in (0, 1)],
            [halo_ref.at[q] for q in range(4)],
            [pv.at[q] for q in range(4)],
            tiles,
            columns,
        )

    v, rest = held(v_ref, hv), held(r_ref, hr)
    for t in range(tiles):
        for q in (0, 3):
            v.put(q, t, *[x * i for x, i in zip(load_s(q, t), load_i(q, t))])
    for q in (1, 2):
        for t in (0, tiles - 1):
            v.put(q, t, jnp.zeros((rows, LANES), F32), jnp.zeros((8, LANES), F32))
        pv[q] = whole_s(q, tiles) * whole_i(q, tiles)
        pv[3 * (q - 1)] = jnp.zeros((rows + 8, LANES), F32)
    for red, left in ((False, None), (True, None), (False, (load_d, rest))):
        fine_sweep(v, load_s, load_i, whole_s, whole_i, red, left)
    fine_residuals(v, load_s, load_d, whole_s, whole_d, rest, c0, c1)

    def coarse(t, value):
        n1[t] = value

    restrict(c0, c1, tiles, rows, coarse, tiles)

    def use(c, source):
        for q in range(4):
            s1_ref[q, c] = source[q]

    tiles1 = tiles // 2
    split_tiles(lambda t: n1[t], tiles1, rows, splitter(), temp, use)
    out = moved(jnp.concatenate([n1[tiles], total], 0), virtual_splitter())
    source = quarters_of(out[:rows], temp.at[0])
    screen = quarters_of(out[rows:], temp.at[1])
    for q in range(4):
        s1_ref[q, tiles1] = source[q]
        d1_virtual[q] = 4.0 + screen[q]
        pi1[q] = inverse_of(4.0 + screen[q])
    d2_virtual[...] = 4.0 + ((screen[0] + screen[1]) + (screen[2] + screen[3]))

    def own(main, virtual):
        return lambda q, t: virtual[q] if isinstance(t, int) and t == tiles1 else main[q, t]

    w = [w0, w1, w2, w3]
    rows1 = rows // 2
    row = row_ids(rows1)
    load_s, load_d = own(s1_ref, s1_ref.at[:, tiles1]), own(d1_ref, d1_virtual)

    def after_sweep(sweep):
        if sweep == 0:
            for t in range(tiles1 + 1):
                even, odd_red = reds(t == tiles1)
                black_even[t] = w[even ^ 1][t]
                black_odd[t] = w[odd_red ^ 1][t]

    left = load_d, {1: part1, 2: part2}
    smooth(w, load_s, own(i1_ref, pi1), tiles1, 16, left, after_sweep)

    def valid(q, virtual):
        even, odd_red = reds(virtual)
        first = 1 if q == odd_red ^ 1 else 2
        last = rows1 - 2 if q == even ^ 1 else rows1 - 3
        return (row >= first) & (row <= last)

    def keep_red(t, r):
        even, odd_red = reds(isinstance(t, int) and t == tiles1)
        red_even[t] = r[even]
        red_odd[t] = r[odd_red]

    residuals(w, load_s, left, tiles1, e0, e1, keep_red, 16, valid)
    shared = {}

    def edges(t, partial):
        virtual = t == tiles1
        even, odd_red = reds(virtual)
        s2_ref[t] = partial
        packs = state_packs(
            [s1_ref[q, t] for q in range(4)],
            [load_d(q, t) for q in range(4)],
            [w[q][t] for q in range(4)],
            {even ^ 1: black_even[t], odd_red ^ 1: black_odd[t]},
            {even: red_even[t], odd_red: red_odd[t]},
            partial,
            d2_virtual[...] if virtual else d2_ref[t],
            virtual,
        )
        right, left = packs
        count = tiles1 + 1
        for i in (0, 1):
            to_mate[i * count + t], to_other[i * count + t] = chosen(odd, left[i], right[i])
        if t % 2 == 0:
            pair = chosen(odd, left[2], roll_rows(right[2], 4))
            shared[0] = pair
        else:
            pair = chosen(odd, roll_rows(left[2], 4), right[2])
            pair = [jnp.where(sub < 4, x, y) for x, y in zip(shared[0], pair)]
        if t % 2 == 1 or virtual:
            to_mate[2 * count + t // 2], to_other[2 * count + t // 2] = pair

    restrict(e0, e1, tiles1, rows1, edges, 16)


def merge_kernel(
    r_ref, s_ref, d_ref, i_ref, d_virtual, d2_ref, d2_virtual,
    out_ref, rim_s, rim_d, rim_i, inverse2,
    out_buf, sems,
):
    tiles = r_ref.shape[1]
    columns = out_ref.shape[0]
    matrix = merger()
    chunk = out_ref.shape[1] // GROUPS
    copies = []
    for group in range(GROUPS):
        for batch in range(tiles // GROUPS // BATCH):
            start = group * (tiles // GROUPS) + batch * BATCH
            own = slice(8, 8 + columns)
            both = [
                jnp.concatenate([r_ref[0, start + i, own], r_ref[1, start + i, own]], 1)
                for i in range(BATCH)
            ]
            out = moved(jnp.concatenate(both, 0), matrix)
            for i in range(BATCH):
                where = slice((start + i) * 256, (start + i + 1) * 256)
                out_buf[:, where] = out[columns * i : columns * (i + 1)]
        part = pl.ds(group * chunk, chunk)
        copy = pltpu.make_async_copy(out_buf.at[:, part], out_ref.at[:, part], sems.at[group])
        copy.start()
        copies.append(copy)

    sub = row_ids(8)
    tiles1, own = d_ref.shape[1], d_ref.shape[2]

    def rim(x):
        return jnp.where(sub < 4, x[:8], x[own - 8 :])

    for t in range(tiles1 + 1):
        for q in range(4):
            rim_s[q, t] = rim(s_ref[q, t])
            if t == tiles1:
                rim_d[q, t] = rim(d_virtual[q])
                rim_i[q, t] = inverse_of(rim(d_virtual[q]))
            else:
                rim_d[q, t] = rim(d_ref[q, t])
                rim_i[q, t] = rim(i_ref[q, t])
        inverse2[t] = inverse_of(d2_virtual[...] if t == tiles1 else d2_ref[t])
    for copy in copies:
        copy.wait()


def coarse_kernel(
    rim_s, rim_d, rim_i, inverse2, d2_ref, d2_virtual, s2_ref, from_other, from_mate,
    solution_ref, residual_ref,
    v0, v1, v2, v3, c0, c1, hs, hd, hi, part, fixes, rest1, rest2, s, d, inv, va, vb,
):
    v = [v0, v1, v2, v3]
    tiles, own = d2_ref.shape[:2]
    rows = own + 8
    count = tiles + 1
    sub = row_ids(8)
    odd_band = is_odd()
    for t in range(count):
        places = t, count + t, 2 * count + t // 2
        packs = [chosen(odd_band, from_mate[i], from_other[i]) for i in places]
        source = [jnp.zeros((8, LANES), F32)] * 4
        diag = [jnp.full((8, LANES), 4.0, F32)] * 4
        inverse = [jnp.zeros((8, LANES), F32)] * 4
        fixed = [jnp.zeros((8, LANES), F32)] * 4
        more = jnp.zeros((8, LANES), F32)
        total = jnp.ones((8, LANES), F32)
        for side, (a, ab, b, bb) in enumerate(sides(t == tiles)):
            near, far, step = (7, 6, -1) if side == 0 else (0, 1, 1)
            first = 6 if side == 0 else 0
            pack0, pack1, pack2 = (pair[side] for pair in packs)
            groups = [
                roll_rows(pack, first - 2 * g) for pack in (pack0, pack1) for g in range(4)
            ]
            pack2 = roll_rows(pack2, 4 * (t % 2) + (4 if side == 0 else 0))

            def put(group, q, at, x):
                group[q] = jnp.where(sub == at, x, group[q])

            for q in range(4):
                put(source, q, near, groups[q])
                put(diag, q, near, groups[4 + q])
            put(source, bb, far, groups[0])
            put(diag, bb, far, groups[1])
            put(fixed, bb, far, groups[2])
            put(fixed, b, far, groups[3])
            put(source, b, far, groups[4])
            put(diag, b, far, 0.0)
            put(source, a, far, groups[5])
            put(fixed, ab, near, pack2)
            more = jnp.where(sub == far, groups[6], more)
            more = jnp.where((sub == far + step) | (sub == far + 2 * step), pack2, more)
            total = jnp.where(sub == far, pack2, total)
            total = jnp.where(sub == far + step, roll_rows(groups[7], step), total)
            for q in range(4):
                known = (sub == near) | (sub == far) if q == bb else sub == near
                inverse[q] = jnp.where(known, inverse_of(diag[q]), inverse[q])
        for q in range(4):
            hs[q, t] = source[q]
            hd[q, t] = diag[q]
            hi[q, t] = inverse[q]
            fixes[q, t] = fixed[q]
        part[t] = more
        near_total = (diag[0] + diag[1]) + (diag[2] + diag[3]) - 12.0
        total = jnp.where((sub == 0) | (sub == 7), near_total, total)
        here = d2_virtual[...] if t == tiles else d2_ref[t]
        d[t] = jnp.concatenate([here, total], 0)
        inv[t] = jnp.concatenate([inverse2[t], inverse_of(total)], 0)
    def after_sweep(sweep):
        if sweep == 2:
            return
        for t in range(count):
            (a, ab, b, bb), (_, _, other_b, other_bb) = sides(t == tiles)
            todo = {}
            if sweep == 0:
                todo = {ab: (sub == 7) | (sub == 1), bb: (sub == 6) | (sub == 0)}
            else:
                todo = {b: sub == 6, other_b: sub == 1}
            for q, mask in todo.items():
                v[q][t, :8] = jnp.where(mask, fixes[q, t], v[q][t, :8])

    def of(halo, own_rows):
        return lambda q, t: jnp.concatenate([halo[q, t], own_rows[q, t]], 0)

    load_s = of(hs, rim_s)
    left = of(hd, rim_d), {1: rest1, 2: rest2}
    smooth(v, load_s, of(hi, rim_i), tiles, 16, left, after_sweep)
    row = row_ids(16)

    def valid(q, virtual):
        even, odd_red = reds(virtual)
        after_band = 0 if q == odd_red ^ 1 else 1
        before_band = 7 if q == even ^ 1 else 6
        first = 8 if q == odd_red ^ 1 else 9
        last = 15 if q == even ^ 1 else 14
        return (row <= after_band) | ((row >= before_band) & (row <= first)) | (row >= last)

    residuals(v, load_s, left, tiles, c0, c1, lambda t, r: None, 16, valid)

    lane, row = lane_ids(rows), row_ids(rows)
    even = (lane + row) % 2 == 0
    odd = jnp.logical_not(even)

    def start(t, value):
        ends = value[8:]
        source = jnp.concatenate(
            [
                s2_ref[t, :8] + jnp.where(sub < 4, ends, 0.0),
                s2_ref[t, own - 8 :] + jnp.where(sub >= 4, ends, 0.0),
                value[:8] + part[t],
            ],
            0,
        )
        s[t] = source
        virtual = isinstance(t, int) and t == tiles
        va[t] = jnp.where(odd if virtual else even, source * inv[t], 0.0)

    restrict(c0, c1, tiles, 16, start, 16)

    def scan(v, use):
        up, down = roll_up(v[tiles]), roll_down(v[0])
        for t in range(tiles + 1):
            x = v[t]
            up_here, down_next = roll_up(x), roll_down(v[after(t, tiles)])
            north = jnp.where(lane == 0, up, up_here)
            south = jnp.where(lane == LANES - 1, down_next, down)
            use(t, x, (col_prev(x) + col_next(x)) + (north + south))
            up, down = up_here, down_next

    for old, new, mask, other in ((va, vb, odd, even), (vb, va, even, odd), (va, vb, odd, even)):

        def relax(t, x, beside):
            update = other if t == tiles else mask
            new[t] = jnp.where(update, (s[t] + beside) * inv[t], x)

        scan(old, relax)

    def finish(t, x, beside):
        if t < tiles:
            where = slice(t * LANES, (t + 1) * LANES)
            solution_ref[:, where] = x[:own]
            residual_ref[:, where] = (s[t] - (d[t] * x - beside))[:own]

    scan(vb, finish)


VMEM = pl.BlockSpec(memory_space=pltpu.VMEM)
HBM = pl.BlockSpec(memory_space=pltpu.HBM)


def call(kernel, out_shapes, scratch, *args, sems=None, far_in=0, far_out=0):
    scratch = [pltpu.VMEM(x, F32) if isinstance(x, tuple) else x for x in scratch]
    if sems is not None:
        scratch.append(pltpu.SemaphoreType.DMA(sems))
    return pl.pallas_call(
        kernel,
        out_shape=[
            jax.ShapeDtypeStruct(x, F32) if isinstance(x, tuple) else x for x in out_shapes
        ],
        in_specs=[HBM] * far_in + [VMEM] * (len(args) - far_in),
        out_specs=[HBM] * far_out + [VMEM] * (len(out_shapes) - far_out),
        scratch_shapes=scratch,
        compiler_params=pltpu.CompilerParams(vmem_limit_bytes=40 * 2**20),
    )(*args)


def swapped_with(x, by):
    count = lax.axis_size("lon")
    pairs = [(i, (i + by) % count) for i in range(0, count, 2)]
    return lax.ppermute(x, "lon", pairs + [(b, a) for a, b in pairs])


def swapped_edges(to_mate, to_other):
    from_mate = swapped_with(to_mate, 1)
    return from_mate, swapped_with(to_other, -1)


def body(right_side, texel_weight, seam_flags):
    columns, height = right_side.shape
    half_turn = lax.axis_size("lon") // 2
    tiles, rows = height // 256, columns // 2
    tiles1, rows1 = tiles // 2, rows // 2
    temp = (BATCH, 2, columns, LANES)
    natural = (2, tiles, columns, LANES)
    padded = (2, tiles, columns + 16, LANES)
    quarters1 = (4, tiles1, rows1, LANES)
    split = (4, 2, 4 * tiles, LANES)
    right_here, weight_here, scales, to_mate, to_other, corner = call(
        edge_kernel,
        [(columns, height), jax.ShapeDtypeStruct((columns, height), BF16)]
        + [(tiles, 8, LANES), (2, tiles, 8, LANES), (2, tiles, 8, LANES), (2, 8, LANES)],
        [pltpu.VMEM(seam_flags.shape, jnp.int32), split, split],
        *[
            pltpu.with_memory_space_constraint(x, pltpu.HBM)
            for x in (right_side, texel_weight, seam_flags)
        ],
        sems=(7,), far_in=3,
    )
    from_mate, from_other = swapped_edges(to_mate, to_other)
    corner_far = swapped_with(corner, half_turn - 1)
    corner_near = swapped_with(corner, half_turn + 1)
    ends = (2, 2, columns, LANES)
    (polar_own,) = call(
        polar_kernel, [(2, rows, LANES)], [ends, ends],
        right_here, weight_here, scales, corner,
    )
    polar = lax.ppermute(
        polar_own, "lon", [(i, (i + half_turn) % (2 * half_turn)) for i in range(2 * half_turn)]
    )
    s, d, inverse, d1, i1, d2 = call(
        bulk_kernel,
        [natural] * 3 + [quarters1, quarters1, quarters1[1:]],
        [(BATCH, columns, LANES), (tiles, rows, LANES), (BATCH, 2, rows, LANES)],
        right_here, weight_here, scales, polar_own,
    )

    def level_scratch(tiles, rows):
        return [(tiles + 1, rows, LANES)] * 6

    def halo_scratch(tiles):
        return [(4, tiles + 1, 8, LANES)] * 3

    pack1 = (2 * (tiles1 + 1) + tiles1 // 2 + 1, 8, LANES)
    r, s1, d1_virtual, d2_virtual, s2_own, to_mate, to_other = call(
        fine_kernel,
        [padded, (4, tiles1 + 1, rows1, LANES), (4, rows1, LANES), (rows1, LANES)]
        + [(tiles1 + 1, rows1, LANES), pack1, pack1],
        [padded, (4, tiles, 8, LANES), (4, rows + 8, LANES), (4, tiles, 8, LANES)]
        + [(tiles + 1, rows, LANES)] * 2
        + halo_scratch(tiles)
        + [(4, rows, LANES)] * 3
        + [(tiles + 1, rows, LANES), (BATCH, 2, rows, LANES)]
        + level_scratch(tiles1, rows1)
        + [(4, rows1, LANES)]
        + [(tiles1 + 1, rows1, LANES)] * 4
        + [(tiles1, rows1, LANES)] * 2,
        s, d, inverse, d1, i1, d2, from_other, from_mate, polar, corner_near, corner_far,
    )
    from_mate, from_other = swapped_edges(to_mate, to_other)
    rim = (4, tiles1 + 1, 8, LANES)
    fine_residual, rim_s, rim_d, rim_i, inverse2 = call(
        merge_kernel,
        [(columns, height), rim, rim, rim, (tiles1 + 1, rows1, LANES)],
        [(columns, height)],
        r, s1, d1, i1, d1_virtual, d2, d2_virtual,
        sems=(GROUPS,), far_out=1,
    )
    wide = (tiles1 + 1, rows1 + 8, LANES)
    solution_2, residual_2 = call(
        coarse_kernel,
        [(columns // 4, height // 4)] * 2,
        level_scratch(tiles1, 16)
        + [(4, tiles1 + 1, 8, LANES)] * 3
        + [(tiles1 + 1, 8, LANES), (4, tiles1 + 1, 8, LANES)]
        + [(tiles1, 16, LANES)] * 2
        + [wide] * 5,
        rim_s, rim_d, rim_i, inverse2, d2, d2_virtual, s2_own, from_other, from_mate,
    )
    return fine_residual, solution_2, residual_2


def solution(mesh):
    spec = P(("groups", "lon"), None)
    return jax.shard_map(
        body, mesh=mesh, in_specs=(spec,) * 3, out_specs=(spec,) * 3, check_vma=False
    )
```

```python
import jax
import jax.numpy as jnp
from jax import lax
from jax.experimental import pallas as pl
from jax.experimental.pallas import tpu as pltpu
from jax.sharding import PartitionSpec as P

TILE = 32
SEAM_SCALE = 0.1
LANES = 128
GROUPS = 4
BATCH = 4
F32 = jnp.float32
BF16 = jnp.bfloat16


def loop(count, body, carry=0, unroll=4):
    unroll = min(unroll, count)

    def steps(block, carry):
        for i in range(unroll):
            carry = body(block * unroll + i, carry)
        return carry

    whole = count // unroll
    carry = steps(0, carry) if whole == 1 else lax.fori_loop(0, whole, steps, carry)
    for t in range(whole * unroll, count):
        carry = body(t, carry)
    return carry


def before(t, tiles):
    return (tiles if t == 0 else t - 1) if isinstance(t, int) else jnp.where(t == 0, tiles, t - 1)


def after(t, tiles):
    return (0 if t == tiles else t + 1) if isinstance(t, int) else t + 1


def lane_ids(rows):
    return lax.broadcasted_iota(jnp.int32, (rows, LANES), 1)


def row_ids(rows):
    return lax.broadcasted_iota(jnp.int32, (rows, LANES), 0)


def roll_up(x):
    return pltpu.roll(x, 1, 1)


def roll_down(x):
    return pltpu.roll(x, LANES - 1, 1)


def roll_rows(x, by):
    by %= x.shape[0]
    return x if by == 0 else pltpu.roll(x, by, 0)


def roll_lanes(x, by):
    by %= LANES
    return x if by == 0 else pltpu.roll(x, by, 1)


def col_prev(x):
    return pltpu.roll(x, 1, 0)


def col_next(x):
    return pltpu.roll(x, x.shape[0] - 1, 0)


def inverse_of(x):
    return 1.0 / x


def selector(shape, rule):
    a = lax.broadcasted_iota(jnp.int32, shape, 0)
    b = lax.broadcasted_iota(jnp.int32, shape, 1)
    return jnp.where(rule(a, b), 1.0, 0.0).astype(BF16)


def splitter():
    return selector((256, 256), lambda a, b: a == 2 * (b % LANES) + b // LANES)


def merger():
    return selector((256, 256), lambda a, b: b == 2 * (a % LANES) + a // LANES)


def virtual_splitter():
    return selector(
        (LANES, 256),
        lambda a, b: a // 2 + jnp.where(a >= 64, 64, 0) + LANES * (a % 2) == b,
    )


def moved(x, matrix, exact=None):
    rows = x.shape[0]
    high = x.astype(BF16)
    low = (x - high.astype(F32)).astype(BF16)
    terms = [high, low] if exact is None else [high, low, exact]
    out = jnp.dot(jnp.concatenate(terms, 0), matrix, preferred_element_type=F32)
    both = out[:rows] + out[rows : 2 * rows]
    return both if exact is None else (both, out[2 * rows :])


def quarters_of(parts, temp):
    count = parts.shape[0] // 2
    temp[0] = parts[:, :LANES]
    temp[1] = parts[:, LANES:]
    return [temp[pr, pl.ds(pc, count, 2), :] for pc in (0, 1) for pr in (0, 1)]


def reds(swapped):
    return (1, 2) if swapped else (0, 3)


def interleaved(group, offset):
    sub = row_ids(8)
    packed = roll_rows(group[0], offset)
    for q in range(1, 4):
        packed = jnp.where(sub // 2 == q, roll_rows(group[q], 2 * q + offset), packed)
    return packed


def edge_packs(source, diag, swapped):
    sub = row_ids(8)
    even, odd = reds(swapped)
    rows = source[0].shape[0]
    packs = []
    for here, first, second, row, step in (
        (slice(rows - 8, rows), even, odd, 6, 1),
        (slice(0, 8), odd, even, 1, -1),
    ):
        gs = [x[here] for x in source]
        gd = [x[here] for x in diag]
        near = gs[first] * inverse_of(gd[first])
        far = roll_rows(gs[second] * inverse_of(gd[second]), step)
        gs[first] = jnp.where(sub == row, near, gs[first])
        gd[first] = jnp.where(sub == row, far, gd[first])
        offset = 2 if row == 6 else 0
        packs.append((interleaved(gs, offset), interleaved(gd, offset)))
    return packs


def unpacked_halo(left, right, swapped):
    sub = row_ids(8)
    even, odd = reds(swapped)
    (al, bl), (ar, br) = left, right
    source, diag = [], []
    for q in range(4):
        s = jnp.where(
            sub >= 6,
            roll_rows(al, 6 - 2 * q),
            jnp.where(sub <= 1, roll_rows(ar, -2 * q), 0.0),
        )
        d = jnp.where(
            sub >= 6,
            roll_rows(bl, 6 - 2 * q),
            jnp.where(sub <= 1, roll_rows(br, -2 * q), 4.0),
        )
        if q == even:
            s = jnp.where(sub == 2, roll_rows(br, 1 - 2 * odd), s)
            d = jnp.where((sub == 2) | (sub == 6), 1.0, d)
        if q == odd:
            s = jnp.where(sub == 5, roll_rows(bl, 5 - 2 * even), s)
            d = jnp.where((sub == 5) | (sub == 1), 1.0, d)
        source.append(s)
        diag.append(d)
    return source, diag


def is_odd():
    return lax.rem(lax.axis_index("lon"), 2) == 1


def chosen(odd, a, b):
    return jnp.where(odd, a, b), jnp.where(odd, b, a)


def store_edges(t, packs, odd, to_mate, to_other):
    right, left = packs
    for i in (0, 1):
        to_mate[i, t], to_other[i, t] = chosen(odd, left[i], right[i])


def sides(swapped):
    even, odd = reds(swapped)
    return (even, even ^ 1, odd, odd ^ 1), (odd, odd ^ 1, even, even ^ 1)


def paired(groups, shift):
    sub = row_ids(8)
    packed = roll_rows(groups[0], shift)
    for g in (1, 2, 3):
        packed = jnp.where(sub // 2 == g, roll_rows(groups[g], 2 * g + shift), packed)
    return packed


def state_packs(source, diag, last, first_black, residual, partial, diag2, swapped):
    sub = row_ids(8)
    rows = source[0].shape[0]
    packs = []
    for (a, ab, b, bb), here, near, far, step in zip(
        sides(swapped), (slice(rows - 8, rows), slice(0, 8)), (7, 0), (6, 1), (-1, 1)
    ):
        s, d, v = ([x[here] for x in group] for group in (source, diag, last))
        part, d2 = partial[here], diag2[here]
        beside = [
            s[bb] + v[a],
            d[bb],
            first_black[bb][here],
            v[b],
            s[b] - d[b] * v[b] + v[ab],
            residual[a][here] - v[bb],
            part,
            roll_rows(d2, -step),
        ]
        groups = [jnp.where(sub == far, y, x) for x, y in zip(s + d, beside)]
        shift = 2 if near == 7 else 0
        more = jnp.where(sub == far, d2, first_black[ab][here])
        more = jnp.where(sub == far + step, part, more)
        more = jnp.where(sub == far + 2 * step, part * inverse_of(d2), more)
        packs.append((paired(groups[:4], shift), paired(groups[4:], shift), more))
    return packs


def fill_halo(t, from_mate, from_other, odd, swapped, hs, hd, hi):
    al, ar = chosen(odd, from_mate[0, t], from_other[0, t])
    bl, br = chosen(odd, from_mate[1, t], from_other[1, t])
    source, diag = unpacked_halo((al, bl), (ar, br), swapped)
    for q in range(4):
        hs[q, t] = source[q]
        hd[q, t] = diag[q]
        hi[q, t] = inverse_of(diag[q])


def loader(own, halo, virtual, tiles):
    def load(q, t):
        if isinstance(t, int) and t == tiles:
            return jnp.concatenate([virtual[q], halo[q, t]], 0)
        return jnp.concatenate([own[q, t], halo[q, t]], 0)

    return load


def polar_packs(tiles_of):
    lane = lane_ids(tiles_of[0][0].shape[0])
    packs = []
    for pc in (0, 1):
        parts = [*tiles_of[2 * pc], *tiles_of[2 * pc + 1]]
        packed = parts[0]
        for m in range(1, 4):
            mine = (lane + (16 - 32 * m) % LANES) % LANES < 32
            packed = jnp.where(mine, roll_lanes(parts[m], 32 * m), packed)
        packs.append(packed)
    return packs


def polar_unpacked(x, q):
    lane = lane_ids(x.shape[1])
    used = (lane < 16) | (lane >= LANES - 16)
    m = 2 * (q % 2)
    return (
        jnp.where(used, roll_lanes(x[q // 2], 32 * m), 0.0),
        jnp.where(used, roll_lanes(x[q // 2], 32 * (m + 1)), 4.0),
    )


def seam_scales(flags, chunks):
    flag_cols, flag_lats = flags.shape
    flags = jnp.concatenate(
        [flags.astype(F32), jnp.zeros((8 - flag_cols, flag_lats), F32)], 0
    )
    lat = lax.broadcasted_iota(jnp.int32, (8, flag_lats), 1)
    stacked = jnp.concatenate([jnp.where(lat // 8 == c, flags, 0.0) for c in chunks], 0)
    spread = selector((flag_lats, LANES), lambda a, b: a % 8 == b // (TILE // 2))
    spread_flags = jnp.dot(stacked.astype(BF16), spread, preferred_element_type=F32)
    scale = jnp.where(spread_flags > 0.5, SEAM_SCALE, 1.0)
    return scale.reshape(len(chunks), 8, LANES)


def seam_rows(scales, flag_cols, rows):
    size = (rows // flag_cols, LANES)
    return jnp.concatenate(
        [jnp.broadcast_to(scales[i : i + 1], size) for i in range(flag_cols)], 0
    )


def edge_kernel(
    right_ref, weight_ref, flag_ref,
    right_here, weight_here, scale_ref, to_mate, to_other, corner_ref,
    flags, temp_s, temp_w, sems,
):
    columns, height = right_ref.shape
    tiles = height // 256
    pairs = [(flag_ref, flags)]
    inputs = (right_ref, right_here, 8), (weight_ref, weight_here, 16)
    for src, dst, size in inputs:
        for start in (0, columns - size):
            part = pl.ds(start, size)
            pairs.append((src.at[part], dst.at[part]))
    for src, dst, size in inputs:
        part = pl.ds(size, columns - 2 * size)
        pairs.append((src.at[part], dst.at[part]))
    copies = [
        pltpu.make_async_copy(src, dst, sems.at[i]) for i, (src, dst) in enumerate(pairs)
    ]
    for copy in copies:
        copy.start()
    odd = is_odd()
    matrix = splitter()
    flag_cols = flag_ref.shape[0]
    copies[0].wait()
    scale_ref[...] = seam_scales(flags[...], range(tiles))
    for copy in copies[1:5]:
        copy.wait()
    sub = row_ids(8)
    def ends(size):
        return slice(0, size), slice(columns - size, columns)

    count = tiles // 4
    found = []
    for batch in range(4):
        chunks = range(batch * count, (batch + 1) * count)
        lanes = [slice(c * 256, (c + 1) * 256) for c in chunks]
        source, weight = moved(
            jnp.concatenate([right_here[at, w] for w in lanes for at in ends(8)], 0),
            matrix,
            jnp.concatenate([weight_here[at, w] for w in lanes for at in ends(16)], 0),
        )
        weight = weight.reshape(count, 32, 256)
        weight = jnp.concatenate([weight[:, :8], weight[:, 24:]], 1).reshape(count * 16, 256)
        source = quarters_of(source, temp_s.at[batch])
        weight = quarters_of(weight, temp_w.at[batch])
        for i, c in enumerate(chunks):
            here = slice(i * 8, (i + 1) * 8)
            scales = scale_ref[c]
            scale = jnp.where(sub < 4, scales[:1], scales[flag_cols - 1 : flag_cols])
            pair = [x[here] for x in source], [4.0 + w[here] * scale for w in weight]
            store_edges(c, edge_packs(*pair, False), odd, to_mate, to_other)
            if c in (0, tiles - 1):
                found.append(pair)
    both = mirrored_ends(*found)
    for pc in (0, 1):
        corner_ref[pc] = both[8 * pc : 8 * (pc + 1)]
    for copy in copies[5:]:
        copy.wait()


def mirrored_ends(first, last):
    mirror = selector((LANES, LANES), lambda a, b: a + b == LANES - 1)
    lane = lane_ids(first[0][0].shape[0])
    ends = [
        [jnp.where(lane >= 64, last[i][q ^ 1], first[i][q ^ 1]) for i in (0, 1)]
        for q in range(4)
    ]
    return moved(jnp.concatenate(polar_packs(ends), 0), mirror)


def polar_kernel(right_ref, weight_ref, scale_ref, edges_first, polar_ref, temp_s, temp_w):
    columns, height = right_ref.shape
    rows, tiles = columns // 2, height // 256
    flag_cols = columns // TILE
    lanes = slice(0, 256), slice(height - 256, height)
    source, weight = moved(
        jnp.concatenate([right_ref[:, w] for w in lanes], 0),
        splitter(),
        jnp.concatenate([weight_ref[:, w] for w in lanes], 0),
    )
    found = []
    for end in (0, 1):
        here = slice(end * columns, (end + 1) * columns)
        scale = seam_rows(scale_ref[end * (tiles - 1)], flag_cols, rows)
        found.append(
            (
                quarters_of(source[here], temp_s.at[end]),
                [4.0 + w * scale for w in quarters_of(weight[here], temp_w.at[end])],
            )
        )
    both = mirrored_ends(*found)
    for pc in (0, 1):
        polar_ref[pc] = both[pc * rows : (pc + 1) * rows]


def bulk_kernel(
    right_ref, weight_ref, scale_ref, polar_first,
    s_ref, d_ref, i_ref, d1_ref, i1_ref, d2_ref,
    temp, e_ref, split_temp,
):
    tiles, columns = s_ref.shape[1], s_ref.shape[2]
    rows = columns // 2
    matrix = splitter()
    for start in range(0, tiles, BATCH):
        lanes = [slice((start + i) * 256, (start + i + 1) * 256) for i in range(BATCH)]
        source, weight = moved(
            jnp.concatenate([right_ref[:, w] for w in lanes], 0),
            matrix,
            jnp.concatenate([weight_ref[:, w] for w in lanes], 0),
        )
        for i in range(BATCH):
            c = start + i
            here = slice(i * columns, (i + 1) * columns)
            scale = seam_rows(scale_ref[c], columns // TILE, columns)
            screens = []
            for pr in (0, 1):
                half = slice(pr * LANES, (pr + 1) * LANES)
                screen = weight[here, half] * scale
                diag = 4.0 + screen
                s_ref[pr, c] = source[here, half]
                d_ref[pr, c] = diag
                i_ref[pr, c] = 1.0 / diag
                screens.append(screen)
            temp[i] = screens[0] + screens[1]
            e_ref[c] = temp[i, pl.ds(0, rows, 2), :] + temp[i, pl.ds(1, rows, 2), :]

    def use(c, screen):
        for q in range(4):
            d1_ref[q, c] = 4.0 + screen[q]
            i1_ref[q, c] = inverse_of(4.0 + screen[q])
        d2_ref[c] = 4.0 + ((screen[0] + screen[1]) + (screen[2] + screen[3]))

    split_tiles(lambda t: e_ref[t], tiles // 2, rows, matrix, split_temp, use)


def split_tiles(load, tiles, rows, matrix, temp, use):
    for start in range(0, tiles, BATCH):
        wide = [
            jnp.concatenate([load(2 * c), load(2 * c + 1)], 1)
            for c in range(start, start + BATCH)
        ]
        out = moved(jnp.concatenate(wide, 0), matrix)
        for i in range(BATCH):
            use(start + i, quarters_of(out[i * rows : (i + 1) * rows], temp.at[i, :, :rows]))


def half_sweep(v, load_s, load_i, tiles, red, unroll, left=None):
    rows = v[0].shape[1]
    lane = lane_ids(rows)
    y, z, qa, qb = (1, 2, 0, 3) if red else (3, 0, 2, 1)
    col_a, col_b = (col_prev, col_next) if red else (col_next, col_prev)

    def beside_virtual(q):
        ns, we = q ^ 1, q ^ 2
        here = v[ns][tiles]
        if q % 2 == 0:
            lat = jnp.where(lane == 0, roll_up(v[ns][tiles - 1]), roll_up(here))
        else:
            lat = jnp.where(lane == LANES - 1, roll_down(v[ns][0]), roll_down(here))
        cols = v[we][tiles]
        return (here + lat) + (cols + (col_prev if q < 2 else col_next)(cols))

    held = [
        (q, (load_s(q, tiles) + beside_virtual(q)) * load_i(q, tiles)) for q in (y, z)
    ]

    def body(t, carry):
        y_before, z_here, vz = carry
        vy, z_next = v[y][t], v[z][t + 1]
        y_here = roll_up(vy)
        z_after = roll_down(z_next)
        lat_a = vy + jnp.where(lane == 0, y_before, y_here)
        lat_b = vz + jnp.where(lane == LANES - 1, z_after, z_here)
        all_a = load_s(qa, t) + (lat_a + (vz + col_a(vz)))
        all_b = load_s(qb, t) + (lat_b + (vy + col_b(vy)))
        new_a, new_b = all_a * load_i(qa, t), all_b * load_i(qb, t)
        v[qa][t], v[qb][t] = new_a, new_b
        if left is not None:
            load_d, rest = left
            rest[qa][t] = all_a - load_d(qa, t) * new_a
            rest[qb][t] = all_b - load_d(qb, t) * new_b
        return y_here, z_after, z_next

    first = v[z][0]
    loop(tiles, body, (roll_up(v[y][tiles]), roll_down(first), first), unroll)
    for q, value in held:
        v[q][tiles] = value


def smooth(v, load_s, load_i, tiles, unroll, left, after_sweep=None):
    zeros = jnp.zeros(v[0].shape[1:], F32)

    def first(t, _):
        for q in (0, 3):
            v[q][t] = load_s(q, t) * load_i(q, t)
        return 0

    loop(tiles, first, 0, unroll)
    for q in (1, 2):
        v[q][0] = zeros
        v[q][tiles - 1] = zeros
        v[q][tiles] = load_s(q, tiles) * load_i(q, tiles)
        v[3 * (q - 1)][tiles] = zeros
    for sweep, red in enumerate((False, True, False)):
        half_sweep(v, load_s, load_i, tiles, red, unroll, left if sweep == 2 else None)
        if after_sweep is not None:
            after_sweep(sweep)


def residuals(v, load_s, left, tiles, c0, c1, keep, unroll, valid=None):
    lane = lane_ids(v[0].shape[1])
    load_d, rest = left

    def use(t, r):
        keep(t, r)
        if valid is not None:
            virtual = isinstance(t, int) and t == tiles
            r = [jnp.where(valid(q, virtual), r[q], 0.0) for q in range(4)]
        c0[t] = (col_prev(r[2]) + col_next(r[0])) + 3.0 * (r[0] + r[2])
        c1[t] = (col_prev(r[3]) + col_next(r[1])) + 3.0 * (r[1] + r[3])

    def north(q, t):
        return jnp.where(lane == 0, roll_up(v[q][before(t, tiles)]), roll_up(v[q][t]))

    def south(q, t):
        return jnp.where(
            lane == LANES - 1, roll_down(v[q][after(t, tiles)]), roll_down(v[q][t])
        )

    def full(t):
        x = [v[q][t] for q in range(4)]
        beside = [
            (x[1] + north(1, t)) + (x[2] + col_prev(x[2])),
            (x[0] + south(0, t)) + (x[3] + col_prev(x[3])),
            (x[3] + north(3, t)) + (x[0] + col_next(x[0])),
            (x[2] + south(2, t)) + (x[1] + col_next(x[1])),
        ]
        use(t, [load_s(q, t) - (load_d(q, t) * x[q] - beside[q]) for q in range(4)])

    def body(i, carry):
        t = i + 1
        up, down, x2 = carry
        x = [v[0][t], v[1][t], x2, v[3][t]]
        next2 = v[2][t + 1]
        up_here, down_next = roll_up(x[1]), roll_down(next2)
        beside0 = (x[1] + jnp.where(lane == 0, up, up_here)) + (x[2] + col_prev(x[2]))
        beside3 = (x[2] + jnp.where(lane == LANES - 1, down_next, down)) + (
            x[1] + col_next(x[1])
        )
        r0 = load_s(0, t) - (load_d(0, t) * x[0] - beside0)
        r3 = load_s(3, t) - (load_d(3, t) * x[3] - beside3)
        use(t, [r0, rest[1][t], rest[2][t], r3])
        return up_here, down_next, next2

    full(0)
    first = v[2][1]
    loop(tiles - 2, body, (roll_up(v[1][0]), roll_down(first), first), unroll)
    full(tiles - 1)
    full(tiles)


def restrict(c0, c1, tiles, rows, use, unroll):
    lane = lane_ids(rows)

    def body(t, carry):
        up, down = carry
        here, other = c0[t, :rows], c1[t, :rows]
        up_here = roll_up(other)
        down_next = roll_down(c0[after(t, tiles), :rows])
        north = jnp.where(lane == 0, up, up_here)
        south = jnp.where(lane == LANES - 1, down_next, down)
        use(t, ((north + south) + 3.0 * (here + other)) * (1.0 / 16.0))
        return up_here, down_next

    start = roll_up(c1[tiles, :rows]), roll_down(c0[0, :rows])
    body(tiles, loop(tiles, body, start, unroll))


class Fine:
    def __init__(self, own, halo, virtual, tiles, columns):
        self.own, self.halo, self.virtual = own, halo, virtual
        self.tiles, self.columns = tiles, columns

    def part(self, parity, t, start):
        return self.own[parity][t, pl.ds(8 + start, self.columns // 2, 2), :]

    def rows(self, q, t):
        return self.part(q % 2, t, q // 2)

    def whole(self, q, t):
        if t == self.tiles:
            return self.virtual[q][...]
        return jnp.concatenate([self.rows(q, t), self.halo[q][t]], 0)

    def ends(self, q, t):
        if t == self.tiles:
            whole = self.virtual[q][...]
            return whole[: self.columns // 2], whole[self.columns // 2 :]
        return self.rows(q, t), self.halo[q][t]

    def line(self, parity, t, column):
        row = self.own[parity][t, 8 + column : 9 + column]
        return jnp.broadcast_to(row, (8, LANES))

    def put(self, q, t, own, halo):
        pr, pc = q % 2, q // 2
        self.own[pr][t, pl.ds(8 + pc, self.columns // 2, 2), :] = own
        self.halo[q][t] = halo
        if pc == 1:
            self.own[pr][t, 7:8] = halo[7:8]
        else:
            at = 8 + self.columns
            self.own[pr][t, at : at + 1] = halo[0:1]

    def beside_columns(self, q, t, near):
        sub = row_ids(8)
        pr, pc = q % 2, q // 2
        rows, halo = near
        own = rows + self.part(pr, t, 2 if pc else -1)
        if pc == 0:
            other = jnp.where(sub == 0, self.line(pr, t, self.columns - 1), col_prev(halo))
        else:
            other = jnp.where(sub == 7, self.line(pr, t, 0), col_next(halo))
        return own, halo + other


def fine_sweep(v, load_s, load_i, whole_s, whole_i, red, left):
    tiles = v.tiles
    y, z, qa, qb = (1, 2, 0, 3) if red else (3, 0, 2, 1)

    def lane_sum(parts, rolled, edge, lane_at):
        return [
            x + jnp.where(lane_ids(x.shape[0]) == lane_at, e, r)
            for x, r, e in zip(parts, rolled, edge)
        ]

    def beside_virtual(q):
        here, cols = v.whole(q ^ 1, tiles), v.whole(q ^ 2, tiles)
        lane = lane_ids(here.shape[0])
        if q % 2 == 0:
            lat = jnp.where(lane == 0, roll_up(v.whole(q ^ 1, tiles - 1)), roll_up(here))
        else:
            lat = jnp.where(lane == LANES - 1, roll_down(v.whole(q ^ 1, 0)), roll_down(here))
        return (here + lat) + (cols + (col_prev if q < 2 else col_next)(cols))

    held = [
        (q, (whole_s(q, tiles) + beside_virtual(q)) * whole_i(q, tiles)) for q in (y, z)
    ]
    y_before = [roll_up(x) for x in v.ends(y, tiles)]
    vz = v.ends(z, 0)
    z_here = [roll_down(x) for x in vz]
    for t in range(tiles):
        vy, z_next = v.ends(y, t), v.ends(z, t + 1)
        y_here = [roll_up(x) for x in vy]
        z_after = [roll_down(x) for x in z_next]
        lat_a = lane_sum(vy, y_here, y_before, 0)
        lat_b = lane_sum(vz, z_here, z_after, LANES - 1)
        new = []
        for q, lat, near in ((qa, lat_a, vz), (qb, lat_b, vy)):
            cols = v.beside_columns(q, t, near)
            total = [x + (l + c) for x, l, c in zip(load_s(q, t), lat, cols)]
            value = [x * i for x, i in zip(total, load_i(q, t))]
            new.append((q, value))
            if left is not None and 0 < t < tiles - 1:
                load_d, rest = left
                rest.put(q, t, *[x - d * u for x, d, u in zip(total, load_d(q, t), value)])
        for q, value in new:
            v.put(q, t, *value)
        y_before, z_here, vz = y_here, z_after, z_next
    for q, value in held:
        v.virtual[q][...] = value


def fine_residuals(v, load_s, load_d, whole_s, whole_d, rest, c0, c1):
    tiles = v.tiles
    rows = v.columns // 2

    def columns_summed(t):
        for pr, ref in ((0, c0), (1, c1)):
            outer = rest.part(pr, t, -1) + rest.part(pr, t, 2)
            inner = rest.part(pr, t, 0) + rest.part(pr, t, 1)
            ref[t] = outer + 3.0 * inner

    def full(t):
        x = [v.whole(q, t) for q in range(4)]
        lane = lane_ids(x[0].shape[0])

        def north(q):
            return jnp.where(lane == 0, roll_up(v.whole(q, before(t, tiles))), roll_up(x[q]))

        def south(q):
            return jnp.where(
                lane == LANES - 1, roll_down(v.whole(q, after(t, tiles))), roll_down(x[q])
            )

        beside = [
            (x[1] + north(1)) + (x[2] + col_prev(x[2])),
            (x[0] + south(0)) + (x[3] + col_prev(x[3])),
            (x[3] + north(3)) + (x[0] + col_next(x[0])),
            (x[2] + south(2)) + (x[1] + col_next(x[1])),
        ]
        r = [whole_s(q, t) - (whole_d(q, t) * x[q] - beside[q]) for q in range(4)]
        if t == tiles:
            c0[t] = ((col_prev(r[2]) + col_next(r[0])) + 3.0 * (r[0] + r[2]))[:rows]
            c1[t] = ((col_prev(r[3]) + col_next(r[1])) + 3.0 * (r[1] + r[3]))[:rows]
        else:
            for q in range(4):
                rest.put(q, t, r[q][:rows], r[q][rows:])
            columns_summed(t)

    full(0)
    up = [roll_up(x) for x in v.ends(1, 0)]
    x2 = v.ends(2, 1)
    down = [roll_down(x) for x in x2]
    for t in range(1, tiles - 1):
        x = [v.ends(0, t), v.ends(1, t), x2, v.ends(3, t)]
        x2 = v.ends(2, t + 1)
        up_here = [roll_up(part) for part in x[1]]
        down_next = [roll_down(part) for part in x2]
        for q, ns, near, edge, lane_at in (
            (0, 1, up_here, up, 0), (3, 2, down, down_next, LANES - 1)
        ):
            cols = v.beside_columns(q, t, x[q ^ 2])
            r = []
            for i, (s, d) in enumerate(zip(load_s(q, t), load_d(q, t))):
                lane = lane_ids(s.shape[0])
                beside = x[ns][i] + jnp.where(lane == lane_at, edge[i], near[i]) + cols[i]
                r.append(s - (d * x[q][i] - beside))
            rest.put(q, t, *r)
        columns_summed(t)
        up, down = up_here, down_next
    full(tiles - 1)
    full(tiles)


def fine_kernel(
    s_ref, d_ref, i_ref, d1_ref, i1_ref, d2_ref,
    from_other, from_mate, polar_ref, corner_near, corner_far,
    r_ref, s1_ref, d1_virtual, d2_virtual, s2_ref, to_mate, to_other,
    v_ref, hv, pv, hr, c0, c1, hs, hd, hi, ps, pd, pi, n1, temp,
    w0, w1, w2, w3, e0, e1, pi1, black_even, black_odd, red_even, red_odd,
    part1, part2,
):
    tiles, columns = s_ref.shape[1], s_ref.shape[2]
    rows = columns // 2
    sub = row_ids(8)
    odd = is_odd()

    def halo(t, _):
        fill_halo(t, from_mate, from_other, odd, False, hs, hd, hi)
        return 0

    loop(tiles, halo, 0, tiles)
    total = -16.0
    for q in range(4):
        own_s, own_d = polar_unpacked(polar_ref, q)
        near_s, near_d = polar_unpacked(corner_near, q)
        far_s, far_d = polar_unpacked(corner_far, q)
        left_s, right_s = chosen(odd, near_s, far_s)
        left_d, right_d = chosen(odd, near_d, far_d)
        total = total + own_d
        ps[q] = own_s
        pd[q] = own_d
        pi[q] = inverse_of(own_d)
        source = jnp.where(sub >= 5, left_s, jnp.where(sub <= 2, right_s, 0.0))
        diag = jnp.where(sub >= 5, left_d, jnp.where(sub <= 2, right_d, 4.0))
        hs[q, tiles] = source
        hd[q, tiles] = diag
        hi[q, tiles] = inverse_of(diag)

    def loaders(ref, halo, virtual):
        def split(q, t):
            return ref[q % 2, t, pl.ds(q // 2, rows, 2), :], halo[q, t]

        def whole(q, t):
            if t == tiles:
                return jnp.concatenate([virtual[q], halo[q, t]], 0)
            return jnp.concatenate(split(q, t), 0)

        return split, whole

    load_s, whole_s = loaders(s_ref, hs, ps)
    load_d, whole_d = loaders(d_ref, hd, pd)
    load_i, whole_i = loaders(i_ref, hi, pi)

    def held(own_ref, halo_ref):
        return Fine(
            [own_ref.at[p] for p in (0, 1)],
            [halo_ref.at[q] for q in range(4)],
            [pv.at[q] for q in range(4)],
            tiles,
            columns,
        )

    v, rest = held(v_ref, hv), held(r_ref, hr)
    for t in range(tiles):
        for q in (0, 3):
            v.put(q, t, *[x * i for x, i in zip(load_s(q, t), load_i(q, t))])
    for q in (1, 2):
        for t in (0, tiles - 1):
            v.put(q, t, jnp.zeros((rows, LANES), F32), jnp.zeros((8, LANES), F32))
        pv[q] = whole_s(q, tiles) * whole_i(q, tiles)
        pv[3 * (q - 1)] = jnp.zeros((rows + 8, LANES), F32)
    for red, left in ((False, None), (True, None), (False, (load_d, rest))):
        fine_sweep(v, load_s, load_i, whole_s, whole_i, red, left)
    fine_residuals(v, load_s, load_d, whole_s, whole_d, rest, c0, c1)

    def coarse(t, value):
        n1[t] = value

    restrict(c0, c1, tiles, rows, coarse, tiles)

    def use(c, source):
        for q in range(4):
            s1_ref[q, c] = source[q]

    tiles1 = tiles // 2
    split_tiles(lambda t: n1[t], tiles1, rows, splitter(), temp, use)
    out = moved(jnp.concatenate([n1[tiles], total], 0), virtual_splitter())
    source = quarters_of(out[:rows], temp.at[0])
    screen = quarters_of(out[rows:], temp.at[1])
    for q in range(4):
        s1_ref[q, tiles1] = source[q]
        d1_virtual[q] = 4.0 + screen[q]
        pi1[q] = inverse_of(4.0 + screen[q])
    d2_virtual[...] = 4.0 + ((screen[0] + screen[1]) + (screen[2] + screen[3]))

    def own(main, virtual):
        return lambda q, t: virtual[q] if isinstance(t, int) and t == tiles1 else main[q, t]

    w = [w0, w1, w2, w3]
    rows1 = rows // 2
    row = row_ids(rows1)
    load_s, load_d = own(s1_ref, s1_ref.at[:, tiles1]), own(d1_ref, d1_virtual)

    def after_sweep(sweep):
        if sweep == 0:
            for t in range(tiles1 + 1):
                even, odd_red = reds(t == tiles1)
                black_even[t] = w[even ^ 1][t]
                black_odd[t] = w[odd_red ^ 1][t]

    left = load_d, {1: part1, 2: part2}
    smooth(w, load_s, own(i1_ref, pi1), tiles1, 16, left, after_sweep)

    def valid(q, virtual):
        even, odd_red = reds(virtual)
        first = 1 if q == odd_red ^ 1 else 2
        last = rows1 - 2 if q == even ^ 1 else rows1 - 3
        return (row >= first) & (row <= last)

    def keep_red(t, r):
        even, odd_red = reds(isinstance(t, int) and t == tiles1)
        red_even[t] = r[even]
        red_odd[t] = r[odd_red]

    residuals(w, load_s, left, tiles1, e0, e1, keep_red, 16, valid)
    shared = {}

    def edges(t, partial):
        virtual = t == tiles1
        even, odd_red = reds(virtual)
        s2_ref[t] = partial
        packs = state_packs(
            [s1_ref[q, t] for q in range(4)],
            [load_d(q, t) for q in range(4)],
            [w[q][t] for q in range(4)],
            {even ^ 1: black_even[t], odd_red ^ 1: black_odd[t]},
            {even: red_even[t], odd_red: red_odd[t]},
            partial,
            d2_virtual[...] if virtual else d2_ref[t],
            virtual,
        )
        right, left = packs
        count = tiles1 + 1
        for i in (0, 1):
            to_mate[i * count + t], to_other[i * count + t] = chosen(odd, left[i], right[i])
        if t % 2 == 0:
            pair = chosen(odd, left[2], roll_rows(right[2], 4))
            shared[0] = pair
        else:
            pair = chosen(odd, roll_rows(left[2], 4), right[2])
            pair = [jnp.where(sub < 4, x, y) for x, y in zip(shared[0], pair)]
        if t % 2 == 1 or virtual:
            to_mate[2 * count + t // 2], to_other[2 * count + t // 2] = pair

    restrict(e0, e1, tiles1, rows1, edges, 16)


def merge_kernel(
    r_ref, s_ref, d_ref, i_ref, d_virtual, d2_ref, d2_virtual,
    out_ref, rim_s, rim_d, rim_i, inverse2,
    out_buf, sems,
):
    tiles = r_ref.shape[1]
    columns = out_ref.shape[0]
    matrix = merger()
    chunk = out_ref.shape[1] // GROUPS
    copies = []
    for group in range(GROUPS):
        for batch in range(tiles // GROUPS // BATCH):
            start = group * (tiles // GROUPS) + batch * BATCH
            own = slice(8, 8 + columns)
            both = [
                jnp.concatenate([r_ref[0, start + i, own], r_ref[1, start + i, own]], 1)
                for i in range(BATCH)
            ]
            out = moved(jnp.concatenate(both, 0), matrix)
            for i in range(BATCH):
                where = slice((start + i) * 256, (start + i + 1) * 256)
                out_buf[:, where] = out[columns * i : columns * (i + 1)]
        part = pl.ds(group * chunk, chunk)
        copy = pltpu.make_async_copy(out_buf.at[:, part], out_ref.at[:, part], sems.at[group])
        copy.start()
        copies.append(copy)

    sub = row_ids(8)
    tiles1, own = d_ref.shape[1], d_ref.shape[2]

    def rim(x):
        return jnp.where(sub < 4, x[:8], x[own - 8 :])

    for t in range(tiles1 + 1):
        for q in range(4):
            rim_s[q, t] = rim(s_ref[q, t])
            if t == tiles1:
                rim_d[q, t] = rim(d_virtual[q])
                rim_i[q, t] = inverse_of(rim(d_virtual[q]))
            else:
                rim_d[q, t] = rim(d_ref[q, t])
                rim_i[q, t] = rim(i_ref[q, t])
        inverse2[t] = inverse_of(d2_virtual[...] if t == tiles1 else d2_ref[t])
    for copy in copies:
        copy.wait()


def coarse_kernel(
    rim_s, rim_d, rim_i, inverse2, d2_ref, d2_virtual, s2_ref, from_other, from_mate,
    solution_ref, residual_ref,
    v0, v1, v2, v3, c0, c1, hs, hd, hi, part, fixes, rest1, rest2, s, d, inv, va, vb,
):
    v = [v0, v1, v2, v3]
    tiles, own = d2_ref.shape[:2]
    rows = own + 8
    count = tiles + 1
    sub = row_ids(8)
    odd_band = is_odd()
    for t in range(count):
        places = t, count + t, 2 * count + t // 2
        packs = [chosen(odd_band, from_mate[i], from_other[i]) for i in places]
        source = [jnp.zeros((8, LANES), F32)] * 4
        diag = [jnp.full((8, LANES), 4.0, F32)] * 4
        inverse = [jnp.zeros((8, LANES), F32)] * 4
        fixed = [jnp.zeros((8, LANES), F32)] * 4
        more = jnp.zeros((8, LANES), F32)
        total = jnp.ones((8, LANES), F32)
        for side, (a, ab, b, bb) in enumerate(sides(t == tiles)):
            near, far, step = (7, 6, -1) if side == 0 else (0, 1, 1)
            first = 6 if side == 0 else 0
            pack0, pack1, pack2 = (pair[side] for pair in packs)
            groups = [
                roll_rows(pack, first - 2 * g) for pack in (pack0, pack1) for g in range(4)
            ]
            pack2 = roll_rows(pack2, 4 * (t % 2) + (4 if side == 0 else 0))

            def put(group, q, at, x):
                group[q] = jnp.where(sub == at, x, group[q])

            for q in range(4):
                put(source, q, near, groups[q])
                put(diag, q, near, groups[4 + q])
            put(source, bb, far, groups[0])
            put(diag, bb, far, groups[1])
            put(fixed, bb, far, groups[2])
            put(fixed, b, far, groups[3])
            put(source, b, far, groups[4])
            put(diag, b, far, 0.0)
            put(source, a, far, groups[5])
            put(fixed, ab, near, pack2)
            more = jnp.where(sub == far, groups[6], more)
            more = jnp.where((sub == far + step) | (sub == far + 2 * step), pack2, more)
            total = jnp.where(sub == far, pack2, total)
            total = jnp.where(sub == far + step, roll_rows(groups[7], step), total)
            for q in range(4):
                known = (sub == near) | (sub == far) if q == bb else sub == near
                inverse[q] = jnp.where(known, inverse_of(diag[q]), inverse[q])
        for q in range(4):
            hs[q, t] = source[q]
            hd[q, t] = diag[q]
            hi[q, t] = inverse[q]
            fixes[q, t] = fixed[q]
        part[t] = more
        near_total = (diag[0] + diag[1]) + (diag[2] + diag[3]) - 12.0
        total = jnp.where((sub == 0) | (sub == 7), near_total, total)
        here = d2_virtual[...] if t == tiles else d2_ref[t]
        d[t] = jnp.concatenate([here, total], 0)
        inv[t] = jnp.concatenate([inverse2[t], inverse_of(total)], 0)
    def after_sweep(sweep):
        if sweep == 2:
            return
        for t in range(count):
            (a, ab, b, bb), (_, _, other_b, other_bb) = sides(t == tiles)
            todo = {}
            if sweep == 0:
                todo = {ab: (sub == 7) | (sub == 1), bb: (sub == 6) | (sub == 0)}
            else:
                todo = {b: sub == 6, other_b: sub == 1}
            for q, mask in todo.items():
                v[q][t, :8] = jnp.where(mask, fixes[q, t], v[q][t, :8])

    def of(halo, own_rows):
        return lambda q, t: jnp.concatenate([halo[q, t], own_rows[q, t]], 0)

    load_s = of(hs, rim_s)
    left = of(hd, rim_d), {1: rest1, 2: rest2}
    smooth(v, load_s, of(hi, rim_i), tiles, 16, left, after_sweep)
    row = row_ids(16)

    def valid(q, virtual):
        even, odd_red = reds(virtual)
        after_band = 0 if q == odd_red ^ 1 else 1
        before_band = 7 if q == even ^ 1 else 6
        first = 8 if q == odd_red ^ 1 else 9
        last = 15 if q == even ^ 1 else 14
        return (row <= after_band) | ((row >= before_band) & (row <= first)) | (row >= last)

    residuals(v, load_s, left, tiles, c0, c1, lambda t, r: None, 16, valid)

    lane, row = lane_ids(rows), row_ids(rows)
    even = (lane + row) % 2 == 0
    odd = jnp.logical_not(even)

    def start(t, value):
        ends = value[8:]
        source = jnp.concatenate(
            [
                s2_ref[t, :8] + jnp.where(sub < 4, ends, 0.0),
                s2_ref[t, own - 8 :] + jnp.where(sub >= 4, ends, 0.0),
                value[:8] + part[t],
            ],
            0,
        )
        s[t] = source
        virtual = isinstance(t, int) and t == tiles
        va[t] = jnp.where(odd if virtual else even, source * inv[t], 0.0)

    restrict(c0, c1, tiles, 16, start, 16)

    def scan(v, use):
        up, down = roll_up(v[tiles]), roll_down(v[0])
        for t in range(tiles + 1):
            x = v[t]
            up_here, down_next = roll_up(x), roll_down(v[after(t, tiles)])
            north = jnp.where(lane == 0, up, up_here)
            south = jnp.where(lane == LANES - 1, down_next, down)
            use(t, x, (col_prev(x) + col_next(x)) + (north + south))
            up, down = up_here, down_next

    for old, new, mask, other in ((va, vb, odd, even), (vb, va, even, odd), (va, vb, odd, even)):

        def relax(t, x, beside):
            update = other if t == tiles else mask
            new[t] = jnp.where(update, (s[t] + beside) * inv[t], x)

        scan(old, relax)

    def finish(t, x, beside):
        if t < tiles:
            where = slice(t * LANES, (t + 1) * LANES)
            solution_ref[:, where] = x[:own]
            residual_ref[:, where] = (s[t] - (d[t] * x - beside))[:own]

    scan(vb, finish)


VMEM = pl.BlockSpec(memory_space=pltpu.VMEM)
HBM = pl.BlockSpec(memory_space=pltpu.HBM)


def call(kernel, out_shapes, scratch, *args, sems=None, far_in=0, far_out=0):
    scratch = [pltpu.VMEM(x, F32) if isinstance(x, tuple) else x for x in scratch]
    if sems is not None:
        scratch.append(pltpu.SemaphoreType.DMA(sems))
    return pl.pallas_call(
        kernel,
        out_shape=[
            jax.ShapeDtypeStruct(x, F32) if isinstance(x, tuple) else x for x in out_shapes
        ],
        in_specs=[HBM] * far_in + [VMEM] * (len(args) - far_in),
        out_specs=[HBM] * far_out + [VMEM] * (len(out_shapes) - far_out),
        scratch_shapes=scratch,
        compiler_params=pltpu.CompilerParams(vmem_limit_bytes=40 * 2**20),
    )(*args)


def swapped_with(x, by):
    count = lax.axis_size("lon")
    pairs = [(i, (i + by) % count) for i in range(0, count, 2)]
    return lax.ppermute(x, "lon", pairs + [(b, a) for a, b in pairs])


def swapped_edges(to_mate, to_other):
    from_mate = swapped_with(to_mate, 1)
    return from_mate, swapped_with(to_other, -1)


def body(right_side, texel_weight, seam_flags):
    columns, height = right_side.shape
    half_turn = lax.axis_size("lon") // 2
    tiles, rows = height // 256, columns // 2
    tiles1, rows1 = tiles // 2, rows // 2
    temp = (BATCH, 2, columns, LANES)
    natural = (2, tiles, columns, LANES)
    padded = (2, tiles, columns + 16, LANES)
    quarters1 = (4, tiles1, rows1, LANES)
    split = (4, 2, 4 * tiles, LANES)
    right_here, weight_here, scales, to_mate, to_other, corner = call(
        edge_kernel,
        [(columns, height), jax.ShapeDtypeStruct((columns, height), BF16)]
        + [(tiles, 8, LANES), (2, tiles, 8, LANES), (2, tiles, 8, LANES), (2, 8, LANES)],
        [pltpu.VMEM(seam_flags.shape, jnp.int32), split, split],
        *[
            pltpu.with_memory_space_constraint(x, pltpu.HBM)
            for x in (right_side, texel_weight, seam_flags)
        ],
        sems=(7,), far_in=3,
    )
    from_mate, from_other = swapped_edges(to_mate, to_other)
    corner_far = swapped_with(corner, half_turn - 1)
    corner_near = swapped_with(corner, half_turn + 1)
    ends = (2, 2, columns, LANES)
    (polar_own,) = call(
        polar_kernel, [(2, rows, LANES)], [ends, ends],
        right_here, weight_here, scales, corner,
    )
    polar = lax.ppermute(
        polar_own, "lon", [(i, (i + half_turn) % (2 * half_turn)) for i in range(2 * half_turn)]
    )
    s, d, inverse, d1, i1, d2 = call(
        bulk_kernel,
        [natural] * 3 + [quarters1, quarters1, quarters1[1:]],
        [(BATCH, columns, LANES), (tiles, rows, LANES), (BATCH, 2, rows, LANES)],
        right_here, weight_here, scales, polar_own,
    )

    def level_scratch(tiles, rows):
        return [(tiles + 1, rows, LANES)] * 6

    def halo_scratch(tiles):
        return [(4, tiles + 1, 8, LANES)] * 3

    pack1 = (2 * (tiles1 + 1) + tiles1 // 2 + 1, 8, LANES)
    r, s1, d1_virtual, d2_virtual, s2_own, to_mate, to_other = call(
        fine_kernel,
        [padded, (4, tiles1 + 1, rows1, LANES), (4, rows1, LANES), (rows1, LANES)]
        + [(tiles1 + 1, rows1, LANES), pack1, pack1],
        [padded, (4, tiles, 8, LANES), (4, rows + 8, LANES), (4, tiles, 8, LANES)]
        + [(tiles + 1, rows, LANES)] * 2
        + halo_scratch(tiles)
        + [(4, rows, LANES)] * 3
        + [(tiles + 1, rows, LANES), (BATCH, 2, rows, LANES)]
        + level_scratch(tiles1, rows1)
        + [(4, rows1, LANES)]
        + [(tiles1 + 1, rows1, LANES)] * 4
        + [(tiles1, rows1, LANES)] * 2,
        s, d, inverse, d1, i1, d2, from_other, from_mate, polar, corner_near, corner_far,
    )
    from_mate, from_other = swapped_edges(to_mate, to_other)
    rim = (4, tiles1 + 1, 8, LANES)
    fine_residual, rim_s, rim_d, rim_i, inverse2 = call(
        merge_kernel,
        [(columns, height), rim, rim, rim, (tiles1 + 1, rows1, LANES)],
        [(columns, height)],
        r, s1, d1, i1, d1_virtual, d2, d2_virtual,
        sems=(GROUPS,), far_out=1,
    )
    wide = (tiles1 + 1, rows1 + 8, LANES)
    solution_2, residual_2 = call(
        coarse_kernel,
        [(columns // 4, height // 4)] * 2,
        level_scratch(tiles1, 16)
        + [(4, tiles1 + 1, 8, LANES)] * 3
        + [(tiles1 + 1, 8, LANES), (4, tiles1 + 1, 8, LANES)]
        + [(tiles1, 16, LANES)] * 2
        + [wide] * 5,
        rim_s, rim_d, rim_i, inverse2, d2, d2_virtual, s2_own, from_other, from_mate,
    )
    return fine_residual, solution_2, residual_2


def solution(mesh):
    spec = P(("groups", "lon"), None)
    return jax.shard_map(
        body, mesh=mesh, in_specs=(spec,) * 3, out_specs=(spec,) * 3, check_vma=False
    )
```
